32 devices in a mesh: dp: 16 (over z, y, x), pair: 2 (over core).
Axes of the slice: x: 2, y: 2, z: 4, core: 2. Of those that a mesh axis runs over, the one named last changes fastest.
Arguments:
- tokens: bfloat16 [4096, 2, 1024], P(('dp', 'pair')), may hold values from -6 to 6
- norm_attn: bfloat16 [2, 1024], P(None, ('dp', 'pair')), may hold values from 0.099609375 to 1.8984375
- w_qkv: bfloat16 [2, 1024, 3072], P(None, ('dp', 'pair')), may hold values from -0.1875 to 0.1875
- w_out: bfloat16 [2, 1024, 1024], P(None, ('dp', 'pair')), may hold values from -0.375 to 0.375
- norm_ff: bfloat16 [2, 1024], P(None, ('dp', 'pair')), may hold values from 0.099609375 to 1.8984375
- w_gate_up: bfloat16 [2, 1024, 8192], P(None, ('dp', 'pair')), may hold values from -0.1875 to 0.1875
- w_down: bfloat16 [2, 4096, 1024], P(None, ('dp', 'pair')), may hold values from -0.125 to 0.125
- cotangent: bfloat16 [4096, 2, 1024], P(('dp', 'pair')), may hold values from -6 to 6
- valid_frames: int32 [32], P(('dp', 'pair')), may hold values from 32 to 128, as said below
- item_lengths: int32 [4], replicated, may hold values from 512 to 1536, as said below
Outputs:
- output: bfloat16 [4096, 2, 1024], P(('dp', 'pair'))
- grad_tokens: float32 [4096, 2, 1024], P(('dp', 'pair'))
- grad_norm_attn: float32 [2, 1024], P(None, ('dp', 'pair'))
- grad_w_qkv: float32 [2, 1024, 3072], P(None, ('dp', 'pair'))
- grad_w_out: float32 [2, 1024, 1024], P(None, ('dp', 'pair'))
- grad_norm_ff: float32 [2, 1024], P(None, ('dp', 'pair'))
- grad_w_gate_up: float32 [2, 1024, 8192], P(None, ('dp', 'pair'))
- grad_w_down: float32 [2, 4096, 1024], P(None, ('dp', 'pair'))
The draws below stay inside these ranges and needn't reach their ends.
Inputs may be any that keep to these rules, and one draw needn't show every extreme that they name: `valid_frames`: entry j counts the slots, from the first, of device j's 128 frame slots that hold data; some device is full in every draw. `item_lengths`: the items tile all 4096 slots in order, padding slots included, so the lengths sum to 4096; some item has exactly 1536 slots.
All inputs are finite; a program needn't handle non-finite values.
Results may differ from the reference program's by a relative error of at most 0.0095.
Values may be sent and summed in bfloat16 or wider, within the bound.
A program may use at most 448 MiB of HBM per device.

```python
import math
import jax
import jax.numpy as jnp
from jax import lax

D = 1024
HEAD_DIM = 64
FF = 4096
POS = 2
SETS = 2
FRAMES_DEV = 128
FRAMES = 4096
ITEMS = 4
ITEM_MEAN = 1024


def draw_valid_frames(key, part):
    device_count = FRAMES // FRAMES_DEV
    first_key = jax.random.fold_in(key, 11)
    second_key = jax.random.fold_in(key, 12)
    counts = jax.random.randint(first_key, (device_count,), FRAMES_DEV // 4, FRAMES_DEV + 1)
    full_at = jax.random.randint(second_key, (), 0, device_count)
    counts = jnp.where(jnp.arange(device_count) == full_at, FRAMES_DEV, counts)
    return counts.astype(jnp.int32)


def draw_item_lengths(key, part):
    pair_count = ITEMS // 2
    first_key = jax.random.fold_in(key, 21)
    second_key = jax.random.fold_in(key, 22)
    offsets = jax.random.randint(first_key, (pair_count,), 0, ITEM_MEAN // 2 + 1)
    offsets = jnp.where(jnp.arange(pair_count) == 0, ITEM_MEAN // 2, offsets)
    paired = jnp.stack([ITEM_MEAN + offsets, ITEM_MEAN - offsets], axis=1).reshape(ITEMS)
    order = jax.random.permutation(second_key, ITEMS)
    return paired[order].astype(jnp.int32)


def steps_of(own_key, shape, split, smallest, largest):
    def one(dim, blocks):
        heights = jax.random.uniform(jax.random.fold_in(jax.random.fold_in(own_key, 6), dim), (blocks,), jnp.float32, smallest / len(split), largest / len(split))
        return jnp.repeat(jnp.exp(heights), shape[dim] // blocks).reshape((-1,) + (1,) * (len(shape) - dim - 1))

    level = one(*split[0])
    for cut in split[1:]:
        level = level * one(*cut)
    return level


def scatter_about(stream_key, dims, scale, reach, split=(), kind=jnp.bfloat16):
    drawn = jax.random.normal(stream_key, dims, jnp.float32) * scale
    if len(split) > 0:
        drawn = steps_of(stream_key, dims, split, -0.22, 0.18) * drawn
    return jnp.clip(drawn, min=-reach, max=reach).astype(kind)


def setup_inputs(seed: int = 0) -> dict:
    key_of = jax.random.split(jax.random.key(seed), 11)
    tokens = scatter_about(key_of[0], (FRAMES, POS, D), 1.0, 6.0, ((0, 32),))
    norm_attn = jnp.clip(1.0 + 0.18 * jax.random.normal(key_of[1], (SETS, D), jnp.float32), 0.099609375, 1.8984375).astype(jnp.bfloat16)
    w_qkv = scatter_about(key_of[2], (SETS, D, 3 * D), D ** -0.5, 0.1875, ((1, 32),))
    w_out = scatter_about(key_of[3], (SETS, D, D), (D // 4) ** -0.5, 0.375, ((1, 32),))
    norm_ff = jnp.clip(1.0 + 0.18 * jax.random.normal(key_of[4], (SETS, D), jnp.float32), 0.099609375, 1.8984375).astype(jnp.bfloat16)
    w_gate_up = scatter_about(key_of[5], (SETS, D, 2 * FF), D ** -0.5, 0.1875, ((1, 32),))
    w_down = scatter_about(key_of[6], (SETS, FF, D), (FF // 2) ** -0.5, 0.125, ((1, 32),))
    cotangent = scatter_about(key_of[7], (FRAMES, POS, D), 1.0, 6.0, ((0, 32),))
    valid_frames = draw_valid_frames(jax.random.fold_in(key_of[10], 71), 0)
    item_lengths = draw_item_lengths(jax.random.fold_in(key_of[10], 71), 0)
    return dict(tokens=tokens, norm_attn=norm_attn, w_qkv=w_qkv, w_out=w_out, norm_ff=norm_ff, w_gate_up=w_gate_up, w_down=w_down, cotangent=cotangent, valid_frames=valid_frames, item_lengths=item_lengths)


@jax.custom_vjp
def low(v):
    return lax.optimization_barrier(v.astype(jnp.bfloat16)).astype(jnp.float32)

@jax.custom_vjp
def low_back(v):
    return v

def low_keep(v):
    return (low(v), None)

def low_pass(kept, grad):
    return (grad,)

def back_keep(v):
    return (v, None)

def back_low(kept, grad):
    return (low(grad),)
low.defvjp(low_keep, low_pass)
low_back.defvjp(back_keep, back_low)

def per_set(activations, weight):
    frame_count = activations.shape[0]
    by_set = activations.reshape(frame_count, SETS, POS // SETS, activations.shape[-1])
    product = jnp.einsum('fspk,ske->fspe', by_set, weight, precision=lax.Precision.HIGHEST)
    return product.reshape(frame_count, POS, weight.shape[-1])

def spread_gain(gain_row):
    return jnp.repeat(gain_row, POS // SETS, axis=0)

def normed(values):
    return values * lax.rsqrt(lax.optimization_barrier(jnp.mean(values * values, axis=-1, keepdims=True)) + 1e-05)

def layer_block(resid_in, norm_attn, w_qkv, w_out, norm_ff, w_gate_up, w_down):
    frame_count = resid_in.shape[0]
    head_count = D // HEAD_DIM
    attn_in = low(normed(resid_in) * spread_gain(norm_attn))
    qkv_rows = low(low_back(per_set(attn_in, w_qkv)))
    queries = qkv_rows[..., :D].reshape(frame_count, POS, head_count, HEAD_DIM)
    key_heads = qkv_rows[..., D:2 * D].reshape(frame_count, POS, head_count, HEAD_DIM)
    value_heads = qkv_rows[..., 2 * D:].reshape(frame_count, POS, head_count, HEAD_DIM)
    scores = low_back(jnp.einsum('fphd,fqhd->fhpq', queries, key_heads, precision=lax.Precision.HIGHEST) * (1.0 / math.sqrt(HEAD_DIM)))
    causal = jnp.arange(POS)[:, None] >= jnp.arange(POS)[None, :]
    scores = jnp.where(causal, scores, -1e+30)
    attn_probs = low(jax.nn.softmax(scores, axis=-1))
    context = jnp.einsum('fhpq,fqhd->fphd', attn_probs, value_heads, precision=lax.Precision.HIGHEST)
    context = low(low_back(context.reshape(frame_count, POS, D)))
    resid_mid = resid_in + low_back(per_set(context, w_out))
    ff_in = low(normed(resid_mid) * spread_gain(norm_ff))
    gate_up = low_back(per_set(ff_in, w_gate_up))
    hidden = low(jax.nn.silu(gate_up[..., :FF]) * gate_up[..., FF:])
    return resid_mid + low_back(per_set(hidden, w_down))

def reference(tokens, norm_attn, w_qkv, w_out, norm_ff, w_gate_up, w_down, cotangent, valid_frames, item_lengths):
    block_frames = math.gcd(FRAMES, max(4096 // POS, 1))
    block_count = FRAMES // block_frames
    weight_list = tuple((w.astype(jnp.float32) for w in (norm_attn, w_qkv, w_out, norm_ff, w_gate_up, w_down)))
    token_blocks = tokens.astype(jnp.float32).reshape(block_count, block_frames, POS, D)

    def forward(blocks, gain_one, qkv_weight, out_weight, gain_two, gate_up_weight, down_weight):

        def block_step(one_block):
            return layer_block(one_block, gain_one, qkv_weight, out_weight, gain_two, gate_up_weight, down_weight)
        return lax.map(jax.checkpoint(block_step), blocks)
    result, pullback = jax.vjp(forward, token_blocks, *weight_list)
    frame_ids = jnp.arange(FRAMES, dtype=jnp.int32)
    owner_ids = frame_ids // FRAMES_DEV
    is_valid = frame_ids % FRAMES_DEV < valid_frames[owner_ids]
    item_ends = jnp.cumsum(item_lengths).astype(jnp.int32)
    item_starts = item_ends - item_lengths
    in_item = (frame_ids[:, None] >= item_starts[None, :]) & (frame_ids[:, None] < item_ends[None, :])
    item_share = ITEM_MEAN / item_lengths.astype(jnp.float32)
    frame_weight = lax.optimization_barrier(jnp.sum(jnp.where(in_item, item_share[None, :], 0.0), axis=1))
    frame_weight = jnp.where(is_valid, frame_weight, 0.0)
    cot_blocks = (cotangent.astype(jnp.float32) * frame_weight[:, None, None]).reshape(block_count, block_frames, POS, D)
    gradients = pullback(cot_blocks)
    output = result.reshape(FRAMES, POS, D).astype(jnp.bfloat16)
    grad_tokens = gradients[0].reshape(FRAMES, POS, D).astype(jnp.float32)
    return (output, grad_tokens, gradients[1], gradients[2], gradients[3], gradients[4], gradients[5], gradients[6])
```

```python
import functools
import math

import jax
import jax.numpy as jnp
from jax import lax
from jax.experimental import pallas as pl
from jax.experimental.pallas import tpu as pltpu
from jax.sharding import PartitionSpec as P

HEAD_DIM = 64


def per_pos(activations, weight):
    return jnp.einsum("fgk,gke->fge", activations, weight, preferred_element_type=jnp.float32)


def per_pos_back(gradients, weight):
    return jnp.einsum("fge,gke->fgk", gradients, weight, preferred_element_type=jnp.float32)


def pos_grad(activations, gradients):
    return jnp.einsum("fgk,fge->kge", activations, gradients, preferred_element_type=jnp.float32)


def gain_grad(normed_rows, gradients):
    return jnp.transpose(jnp.sum(normed_rows * gradients, axis=0))


def back_layout(share):
    return jnp.swapaxes(share, 0, 1)


def normed(values):
    inverse = lax.rsqrt(jnp.mean(values * values, axis=-1, keepdims=True) + 1e-05)
    return (values * inverse, inverse)


def norm_back(normed_rows, inverse, gradients):
    return inverse * (
        gradients - normed_rows * jnp.mean(gradients * normed_rows, axis=-1, keepdims=True)
    )


def gather_ff_fwd(norm_ff, w_gate_up, w_down, start, group):
    return (
        lax.all_gather(norm_ff[start : start + group], ("dp", "pair"), axis=1, tiled=True),
        lax.all_gather(w_gate_up[start : start + group], ("dp", "pair"), axis=1, tiled=True),
        lax.all_gather(w_down[start : start + group], ("dp", "pair"), axis=1, tiled=True),
    )


def gather_ff_back(norm_ff, w_gate_up, w_down, start, group):
    return (
        lax.all_gather(norm_ff[start : start + group], ("dp", "pair"), axis=1, tiled=True),
        lax.all_gather(w_gate_up[start : start + group], ("dp", "pair"), axis=1, tiled=True),
        lax.all_gather(w_down[start : start + group], ("dp", "pair"), axis=1, tiled=True),
    )


def local(
    tokens,
    norm_attn,
    w_qkv,
    w_out,
    norm_ff,
    w_gate_up,
    w_down,
    cotangent,
    valid_frames,
    item_lengths,
):
    frame_count, positions, model_width = tokens.shape
    head_count = model_width // HEAD_DIM
    ff_units = w_gate_up.shape[2] // 2
    score_scale = 1.0 / math.sqrt(HEAD_DIM)
    causal = jnp.arange(positions)[:, None] >= jnp.arange(positions)[None, :]
    head_shape = (frame_count, positions, head_count, HEAD_DIM)
    group = 1
    gains_attn, qkv_full, out_full = (
        lax.all_gather(norm_attn, ("dp", "pair"), axis=1, tiled=True),
        lax.all_gather(w_qkv, ("dp", "pair"), axis=1, tiled=True),
        lax.all_gather(w_out, ("dp", "pair"), axis=1, tiled=True),
    )
    resid_in = tokens.astype(jnp.float32)
    normed_one, inverse_one = normed(resid_in)
    attn_in = (normed_one * gains_attn.astype(jnp.float32)[None]).astype(jnp.bfloat16)
    qkv_rows = per_pos(attn_in, qkv_full).astype(jnp.bfloat16)
    queries = qkv_rows[..., :model_width].reshape(head_shape)
    key_heads = qkv_rows[..., model_width : 2 * model_width].reshape(head_shape)
    value_heads = qkv_rows[..., 2 * model_width :].reshape(head_shape)
    scores = (
        jnp.einsum("fphd,fqhd->fhpq", queries, key_heads, preferred_element_type=jnp.float32)
        * score_scale
    )
    scores = jnp.where(causal, scores, -1e30)
    row_max = jnp.max(scores, axis=-1, keepdims=True)
    attn_probs = jnp.exp(scores - row_max)
    attn_probs = attn_probs / jnp.sum(attn_probs, axis=-1, keepdims=True)
    probs_low = attn_probs.astype(jnp.bfloat16)
    context = jnp.einsum(
        "fhpq,fqhd->fphd", probs_low, value_heads, preferred_element_type=jnp.float32
    )
    context = context.astype(jnp.bfloat16).reshape(frame_count, positions, model_width)
    resid_mid = resid_in + per_pos(context, out_full)
    kept_parts = []
    out_parts = []
    for start in range(0, positions, group):
        gains_ff, gate_up_full, down_full = gather_ff_fwd(norm_ff, w_gate_up, w_down, start, group)
        mid_part = resid_mid[:, start : start + group]
        normed_two, inverse_two = normed(mid_part)
        ff_in = (normed_two * gains_ff.astype(jnp.float32)[None]).astype(jnp.bfloat16)
        gate_up = per_pos(ff_in, gate_up_full)
        gate_part = gate_up[..., :ff_units]
        up_part = gate_up[..., ff_units:]
        sigmoid_gate = jax.nn.sigmoid(gate_part)
        silu_gate = gate_part * sigmoid_gate
        hidden = (silu_gate * up_part).astype(jnp.bfloat16)
        out_parts.append(mid_part + per_pos(hidden, down_full))
        kept_parts.append(
            (normed_two, inverse_two, ff_in, gate_part, up_part, sigmoid_gate, silu_gate, hidden)
        )
    output = jnp.concatenate(out_parts, axis=1).astype(jnp.bfloat16)
    device_index = lax.axis_index(("dp", "pair"))
    local_ids = jnp.arange(frame_count, dtype=jnp.int32)
    frame_ids = device_index * frame_count + local_ids
    item_ends = jnp.cumsum(item_lengths)
    item_starts = item_ends - item_lengths
    in_item = (frame_ids[:, None] >= item_starts[None, :]) & (
        frame_ids[:, None] < item_ends[None, :]
    )
    item_share = 8 * frame_count / item_lengths.astype(jnp.float32)
    frame_weight = jnp.sum(jnp.where(in_item, item_share[None, :], 0.0), axis=1)
    frame_weight = jnp.where(local_ids < valid_frames[0], frame_weight, 0.0)
    grad_out = cotangent.astype(jnp.float32) * frame_weight[:, None, None]
    mid_grads = []
    share_norm_ff_parts = []
    share_gate_up_parts = []
    share_down_parts = []
    for index, start in enumerate(range(0, positions, group)):
        normed_two, inverse_two, ff_in, gate_part, up_part, sigmoid_gate, silu_gate, hidden = (
            kept_parts[index]
        )
        gains_ff, gate_up_full, down_full = gather_ff_back(norm_ff, w_gate_up, w_down, start, group)
        grad_part = grad_out[:, start : start + group]
        grad_low = grad_part.astype(jnp.bfloat16)
        grad_down = pos_grad(hidden, grad_low)
        d_hidden = per_pos_back(grad_low, down_full)
        d_gate = d_hidden * up_part * sigmoid_gate * (1.0 + gate_part * (1.0 - sigmoid_gate))
        d_up = d_hidden * silu_gate
        d_gate_up = jnp.concatenate([d_gate, d_up], axis=-1).astype(jnp.bfloat16)
        grad_gate_up = pos_grad(ff_in, d_gate_up)
        d_ff_in = per_pos_back(d_gate_up, gate_up_full)
        grad_norm_ff = gain_grad(normed_two, d_ff_in)
        mid_grads.append(
            grad_part
            + norm_back(normed_two, inverse_two, d_ff_in * gains_ff.astype(jnp.float32)[None])
        )
        share_a, share_b, share_c = (
            lax.psum_scatter(grad_norm_ff, ("dp", "pair"), scatter_dimension=0, tiled=True),
            lax.psum_scatter(grad_gate_up, ("dp", "pair"), scatter_dimension=0, tiled=True),
            lax.psum_scatter(grad_down, ("dp", "pair"), scatter_dimension=0, tiled=True),
        )
        share_norm_ff_parts.append(jnp.transpose(share_a))
        share_gate_up_parts.append(back_layout(share_b))
        share_down_parts.append(back_layout(share_c))
    d_mid = jnp.concatenate(mid_grads, axis=1)
    gains_attn, qkv_full, out_full = (
        lax.all_gather(norm_attn, ("dp", "pair"), axis=1, tiled=True),
        lax.all_gather(w_qkv, ("dp", "pair"), axis=1, tiled=True),
        lax.all_gather(w_out, ("dp", "pair"), axis=1, tiled=True),
    )
    d_mid_low = d_mid.astype(jnp.bfloat16)
    grad_out_proj = pos_grad(context, d_mid_low)
    d_context = per_pos_back(d_mid_low, out_full).astype(jnp.bfloat16).reshape(head_shape)
    d_probs = jnp.einsum(
        "fphd,fqhd->fhpq", d_context, value_heads, preferred_element_type=jnp.float32
    )
    d_values = jnp.einsum(
        "fhpq,fphd->fqhd", probs_low, d_context, preferred_element_type=jnp.float32
    )
    d_scores = attn_probs * (d_probs - jnp.sum(attn_probs * d_probs, axis=-1, keepdims=True))
    d_scores = d_scores.astype(jnp.bfloat16)
    d_queries = (
        jnp.einsum("fhpq,fqhd->fphd", d_scores, key_heads, preferred_element_type=jnp.float32)
        * score_scale
    )
    d_keys = (
        jnp.einsum("fhpq,fphd->fqhd", d_scores, queries, preferred_element_type=jnp.float32)
        * score_scale
    )
    row_shape = (frame_count, positions, model_width)
    d_qkv = jnp.concatenate(
        [d_queries.reshape(row_shape), d_keys.reshape(row_shape), d_values.reshape(row_shape)],
        axis=-1,
    ).astype(jnp.bfloat16)
    grad_qkv = pos_grad(attn_in, d_qkv)
    d_attn_in = per_pos_back(d_qkv, qkv_full)
    grad_norm_attn = gain_grad(normed_one, d_attn_in)
    grad_tokens = d_mid + norm_back(
        normed_one, inverse_one, d_attn_in * gains_attn.astype(jnp.float32)[None]
    )
    share_norm_attn, share_qkv, share_out = (
        lax.psum_scatter(grad_norm_attn, ("dp", "pair"), scatter_dimension=0, tiled=True),
        lax.psum_scatter(grad_qkv, ("dp", "pair"), scatter_dimension=0, tiled=True),
        lax.psum_scatter(grad_out_proj, ("dp", "pair"), scatter_dimension=0, tiled=True),
    )
    share_norm_attn = jnp.transpose(share_norm_attn)
    share_qkv = back_layout(share_qkv)
    share_out = back_layout(share_out)
    share_norm_ff = jnp.concatenate(share_norm_ff_parts, axis=0)
    share_gate_up = jnp.concatenate(share_gate_up_parts, axis=0)
    share_down = jnp.concatenate(share_down_parts, axis=0)
    return (
        output,
        grad_tokens,
        share_norm_attn,
        share_qkv,
        share_out,
        share_norm_ff,
        share_gate_up,
        share_down,
    )


MESH_ID = pl.DeviceIdType.MESH
BF16 = jnp.bfloat16
F32 = jnp.float32


def here():
    dp = lax.axis_index("dp")
    core = lax.axis_index("pair")
    return lax.div(dp, 4), lax.rem(lax.div(dp, 2), 2), lax.rem(dp, 2), core


def flip(value, bit):
    return 1 - value if bit else value


def push(src, dst, send_sem, recv_sem, to):
    return pltpu.make_async_remote_copy(
        src_ref=src,
        dst_ref=dst,
        send_sem=send_sem,
        recv_sem=recv_sem,
        device_id=to,
        device_id_type=MESH_ID,
    )


def arrived(dst, recv_sem, to):
    push(dst, dst, recv_sem, recv_sem, to).wait_recv()


def greet_all(z, y, x, core):
    barrier = pltpu.get_barrier_semaphore()
    me = 2 * (z * 4 + y * 2 + x) + core

    def one(step, carry):
        other = lax.rem(me + step, 32)
        pl.semaphore_signal(
            barrier, inc=1, device_id=(lax.div(other, 2), lax.rem(other, 2)), device_id_type=MESH_ID
        )
        return carry

    lax.fori_loop(1, 32, one, 0)
    pl.semaphore_wait(barrier, 31)


def greet(peers):
    barrier = pltpu.get_barrier_semaphore()
    for to in peers:
        pl.semaphore_signal(barrier, inc=1, device_id=to, device_id_type=MESH_ID)
    pl.semaphore_wait(barrier, len(peers))


def maybe(condition, do):
    if condition is None:
        do()
    else:
        pl.when(condition)(do)


OFFSETS = [
    (dz, dy, dx) for dz in (0, -1, 1, -2, 2, -3, 3) for dy in (0, 1) for dx in (0, 1)
]
ORDERS = ("zxy", "zyx", "xyz", "yxz")


def hops(offset):
    return abs(offset[0]) + offset[1] + offset[2]


def arrival_axis(order, offset):
    part = dict(z=offset[0], y=offset[1], x=offset[2])
    last = None
    for axis in order:
        if part[axis] != 0:
            last = axis
    return last


def onward(order, offset):
    directions = []
    last = arrival_axis(order, offset)
    start = 0
    if last is not None:
        start = order.index(last) + 1
        if last == "z":
            directions.append("u" if offset[0] < 0 else "d")
    for axis in order[start:]:
        directions.extend(["u", "d"] if axis == "z" else [axis])
    return directions


def came_from(order, offset):
    last = arrival_axis(order, offset)
    if last == "z":
        return "d" if offset[0] < 0 else "u"
    return last


def offset_exists(offset, z):
    if offset[0] < 0:
        return z >= -offset[0]
    if offset[0] > 0:
        return z <= 3 - offset[0]
    return None


def direction_exists(direction, z):
    return {"u": z < 3, "d": z > 0}.get(direction)


DIRECTIONS = ("x", "y", "u", "d", "s")


def neighbour(direction, z, y, x, core):
    if direction == "x":
        return (z * 4 + y * 2 + 1 - x, core)
    if direction == "y":
        return (z * 4 + (1 - y) * 2 + x, core)
    if direction == "u":
        return (z * 4 + 4 + y * 2 + x, core)
    if direction == "d":
        return (z * 4 - 4 + y * 2 + x, core)
    return (z * 4 + y * 2 + x, 1 - core)


def chip_of(offset, z, y, x):
    return (z + offset[0]) * 4 + flip(y, offset[1]) * 2 + flip(x, offset[2])


def gather_attn_kernel(
    gains_ref,
    qkv_ref,
    out_ref,
    gains_full,
    qkv_full,
    out_full,
    plane_sem,
    sibling_sem,
    send_sem,
    local_sem,
    gains_send,
    gains_recv,
):
    z, y, x, core = here()
    me = 2 * (z * 4 + y * 2 + x) + core
    greet_all(z, y, x, core)
    pieces = [
        (qkv_ref, qkv_full, 0, "zxy"),
        (qkv_ref, qkv_full, 1, "zyx"),
        (out_ref, out_full, 0, "xyz"),
        (out_ref, out_full, 1, "yxz"),
    ]

    def rows(piece, device):
        source, full, index, _ = pieces[piece]
        height = source.shape[1]
        return full.at[index, pl.ds(pl.multiple_of(device * height, height), height), :]

    pending = []

    def send(piece, offset, direction):
        source, full, index, _ = pieces[piece]
        chip = chip_of(offset, z, y, x)
        block = rows(piece, 2 * chip + core)
        src = source.at[index] if hops(offset) == 0 else block
        recv = sibling_sem if direction == "s" else plane_sem
        return push(
            src,
            block,
            send_sem.at[piece, chip, DIRECTIONS.index(direction)],
            recv.at[piece, chip],
            neighbour(direction, z, y, x, core),
        )

    def handle(piece, offset, finish):
        order = pieces[piece][3]

        def go():
            chip = chip_of(offset, z, y, x)
            if hops(offset) > 0 and not finish:
                arrived(
                    rows(piece, 2 * chip + core),
                    plane_sem.at[piece, chip],
                    neighbour("s", z, y, x, core),
                )
            for direction in onward(order, offset) + ["s"]:
                copy = send(piece, offset, direction)
                maybe(
                    direction_exists(direction, z), copy.wait_send if finish else copy.start
                )

        maybe(offset_exists(offset, z), go)

    events = sorted(
        ((hops(offset), rank, piece, offset) for piece in range(4) for rank, offset in enumerate(OFFSETS)),
        key=lambda event: event[:3],
    )
    for _, _, piece, offset in events:
        if hops(offset) == 0:
            handle(piece, offset, False)

    def gains_copy(step):
        other = lax.rem(me + step, 32)
        return push(
            gains_ref,
            gains_full.at[me],
            gains_send.at[step],
            gains_recv.at[me],
            (lax.div(other, 2), lax.rem(other, 2)),
        )

    def gains_start(step, carry):
        gains_copy(step).start()
        return carry

    lax.fori_loop(1, 32, gains_start, 0)
    own = [
        pltpu.make_async_copy(source.at[index], rows(piece, me), local_sem.at[piece])
        for piece, (source, full, index, _) in enumerate(pieces)
    ]
    own.append(pltpu.make_async_copy(gains_ref, gains_full.at[me], local_sem.at[4]))
    for copy in own:
        copy.start()
    for _, _, piece, offset in events:
        if hops(offset) > 0:
            handle(piece, offset, False)
    for _, _, piece, offset in events:
        handle(piece, offset, True)

    def sibling_wait(chip, carry):
        for piece in range(4):
            arrived(
                rows(piece, 2 * chip + 1 - core),
                sibling_sem.at[piece, chip],
                neighbour("s", z, y, x, core),
            )
        return carry

    lax.fori_loop(0, 16, sibling_wait, 0)

    def gains_wait(step, carry):
        other = lax.rem(me + step, 32)
        gains_copy(step).wait_send()
        arrived(gains_full.at[other], gains_recv.at[other], neighbour("s", z, y, x, core))
        return carry

    lax.fori_loop(1, 32, gains_wait, 0)
    for copy in own:
        copy.wait()


def gather_attn(gains, w_qkv, w_out):
    sets, height, qkv_width = w_qkv.shape
    out_width = w_out.shape[2]
    dma = pltpu.SemaphoreType.DMA
    return pl.pallas_call(
        gather_attn_kernel,
        out_shape=(
            jax.ShapeDtypeStruct((32,) + gains.shape, BF16),
            jax.ShapeDtypeStruct((sets, 32 * height, qkv_width), BF16),
            jax.ShapeDtypeStruct((sets, 32 * height, out_width), BF16),
        ),
        in_specs=[pl.BlockSpec(memory_space=pl.ANY)] * 3,
        out_specs=(pl.BlockSpec(memory_space=pl.ANY),) * 3,
        scratch_shapes=[
            dma((4, 16)),
            dma((4, 16)),
            dma((4, 16, 5)),
            dma((5,)),
            dma((32,)),
            dma((32,)),
        ],
        compiler_params=pltpu.CompilerParams(collective_id=0, has_side_effects=True),
        name="gather_attn",
    )(gains, w_qkv, w_out)


RANK_STEPS = sorted(
    ((dl, dx, dc) for dl in (0, 1) for dx in (0, 1) for dc in (0, 1)), key=lambda step: (sum(step), step)
)


def group_place(z, y, x, core):
    zh, zl = lax.div(z, 2), lax.rem(z, 2)

    def member(step):
        return ((2 * zh + flip(zl, step[0])) * 4 + y * 2 + flip(x, step[1]), flip(core, step[2]))

    def rank(step):
        return 4 * flip(zl, step[0]) + 2 * flip(x, step[1]) + flip(core, step[2])

    def device(step, dzh=0, dy=0):
        return 16 * flip(zh, dzh) + 4 * flip(y, dy) + 8 * flip(zl, step[0]) + 2 * flip(x, step[1]) + flip(core, step[2])

    far = ((2 * (1 - zh) + zl) * 4 + y * 2 + x, core)
    across = (z * 4 + (1 - y) * 2 + x, core)
    return zh, zl, member, rank, device, far, across


def gather_ff_kernel(
    gate_up_ref,
    down_ref,
    rows_ref,
    grads_ref,
    gate_up_full,
    down_full,
    rows_full,
    grads_full,
    rank_send,
    rank_recv,
    far_send,
    far_recv,
    across_send,
    across_recv,
    act_send,
    act_recv,
    local_sem,
):
    z, y, x, core = here()
    zh, zl, member, rank, device, far, across = group_place(z, y, x, core)
    own_step = (0, 0, 0)
    others = RANK_STEPS[1:]
    greet([member(step) for step in others] + [far, across])
    height = gate_up_ref.shape[2]
    down_height = down_ref.shape[1]
    act_height = rows_ref.shape[1]
    sends = []

    def start(copy):
        copy.start()
        sends.append(copy)

    def weight_rows(number):
        return gate_up_full.at[:, pl.ds(pl.multiple_of(number * height, height), height), :]

    def down_rows(dzh, dy):
        number = 2 * flip(zh, dzh) + flip(y, dy)
        return down_full.at[:, pl.ds(pl.multiple_of(number * down_height, down_height), down_height), :]

    def act_rows(full, step):
        return full.at[:, pl.ds(pl.multiple_of(rank(step) * act_height, act_height), act_height), :]

    acts = [(rows_ref, rows_full), (grads_ref, grads_full)]

    def send_act(which, step, source, hop):
        to = member(tuple(1 if axis == hop else 0 for axis in range(3)))
        landed = tuple(bit ^ (1 if axis == hop else 0) for axis, bit in enumerate(step))
        start(
            push(
                source,
                act_rows(acts[which][1], step),
                act_send.at[which, 4 * step[0] + 2 * step[1] + step[2], hop],
                act_recv.at[which, 4 * landed[0] + 2 * landed[1] + landed[2]],
                to,
            )
        )

    def wait_act(which, step):
        arrived(
            act_rows(acts[which][1], step),
            act_recv.at[which, 4 * step[0] + 2 * step[1] + step[2]],
            across,
        )

    mine = gate_up_ref.at[rank(own_step)]
    for slot, step in enumerate(RANK_STEPS):
        if step != own_step:
            start(
                push(
                    gate_up_ref.at[rank(step)],
                    weight_rows(device(own_step)),
                    rank_send.at[slot],
                    rank_recv.at[slot],
                    member(step),
                )
            )
    start(push(mine, weight_rows(device(own_step)), far_send.at[0], far_recv.at[0], far))
    start(push(mine, weight_rows(device(own_step)), across_send.at[0, 0], across_recv.at[0, 0], across))
    start(push(down_ref, down_rows(0, 0), far_send.at[8], far_recv.at[8], far))
    start(push(down_ref, down_rows(0, 0), across_send.at[0, 8], across_recv.at[0, 8], across))
    for which in (0, 1):
        for hop in (0, 1, 2):
            send_act(which, own_step, acts[which][0], hop)
    local = [
        pltpu.make_async_copy(mine, weight_rows(device(own_step)), local_sem.at[0]),
        pltpu.make_async_copy(down_ref, down_rows(0, 0), local_sem.at[1]),
        pltpu.make_async_copy(rows_ref, act_rows(rows_full, own_step), local_sem.at[2]),
        pltpu.make_async_copy(grads_ref, act_rows(grads_full, own_step), local_sem.at[3]),
    ]
    for copy in local:
        copy.start()
    for slot, step in enumerate(RANK_STEPS):
        if step == own_step:
            continue
        block = weight_rows(device(step))
        arrived(block, rank_recv.at[slot], member(step))
        start(push(block, block, far_send.at[slot], far_recv.at[slot], far))
        start(push(block, block, across_send.at[0, slot], across_recv.at[0, slot], across))
    for slot, step in enumerate(RANK_STEPS):
        block = weight_rows(device(step, 1, 0))
        arrived(block, far_recv.at[slot], far)
        start(push(block, block, across_send.at[1, slot], across_recv.at[1, slot], across))
    block = down_rows(1, 0)
    arrived(block, far_recv.at[8], far)
    start(push(block, block, across_send.at[1, 8], across_recv.at[1, 8], across))
    for which in (0, 1):
        step = (1, 0, 0)
        wait_act(which, step)
        block = act_rows(acts[which][1], step)
        send_act(which, step, block, 1)
        send_act(which, step, block, 2)
    for which in (0, 1):
        for step in ((0, 1, 0), (1, 1, 0)):
            wait_act(which, step)
            send_act(which, step, act_rows(acts[which][1], step), 2)
    for which in (0, 1):
        for step in ((0, 0, 1), (1, 0, 1), (0, 1, 1), (1, 1, 1)):
            wait_act(which, step)
    for dzh in (0, 1):
        for slot, step in enumerate(RANK_STEPS):
            arrived(weight_rows(device(step, dzh, 1)), across_recv.at[dzh, slot], across)
        arrived(down_rows(dzh, 1), across_recv.at[dzh, 8], across)
    for copy in sends:
        copy.wait_send()
    for copy in local:
        copy.wait()


def gather_ff(gate_up_parts, w_down, rows, grads):
    ranks, sets, height, width = gate_up_parts.shape
    dma = pltpu.SemaphoreType.DMA
    return pl.pallas_call(
        gather_ff_kernel,
        out_shape=(
            jax.ShapeDtypeStruct((sets, 32 * height, width), BF16),
            jax.ShapeDtypeStruct((sets, 4 * w_down.shape[1], w_down.shape[2]), BF16),
            jax.ShapeDtypeStruct((sets, ranks * rows.shape[1], rows.shape[2]), BF16),
            jax.ShapeDtypeStruct((sets, ranks * grads.shape[1], grads.shape[2]), BF16),
        ),
        in_specs=[pl.BlockSpec(memory_space=pl.ANY)] * 4,
        out_specs=(pl.BlockSpec(memory_space=pl.ANY),) * 4,
        scratch_shapes=[
            dma((8,)),
            dma((8,)),
            dma((9,)),
            dma((9,)),
            dma((2, 9)),
            dma((2, 9)),
            dma((2, 8, 3)),
            dma((2, 8)),
            dma((4,)),
        ],
        compiler_params=pltpu.CompilerParams(collective_id=1, has_side_effects=True),
        name="gather_ff",
    )(gate_up_parts, w_down, rows, grads)


def add_into(target, sources, rows=16, columns=1024):
    height, width = target.shape
    across = width // columns

    def one(step, carry):
        top = pl.multiple_of(lax.div(step, across) * rows, rows)
        left = pl.multiple_of(lax.rem(step, across) * columns, columns)
        spot = (pl.ds(top, rows), pl.ds(left, columns))
        total = sources[0][spot].astype(F32)
        for source in sources[1:]:
            total = total + source[spot].astype(F32)
        target[spot] = total.astype(target.dtype)
        return carry

    lax.fori_loop(0, (height // rows) * across, one, 0)


def scatter_ff_kernel(
    out_ref,
    back_ref,
    gate_up_ref,
    down_ref,
    out_sum,
    back_sum,
    gate_up_sum,
    down_sum,
    core_buf,
    x_buf,
    z_buf,
    across_gate,
    across_down,
    far_gate,
    far_down,
    rank_buf,
    core_send,
    core_recv,
    x_send,
    x_recv,
    z_send,
    z_recv,
    across_send,
    across_recv,
    far_send,
    far_recv,
    rank_send,
    rank_recv,
):
    z, y, x, core = here()
    zh, zl, member, rank, device, far, across = group_place(z, y, x, core)
    own_step = (0, 0, 0)
    others = RANK_STEPS[1:]
    greet([member(step) for step in others] + [far, across])
    sets = out_ref.shape[0]
    act_height = out_sum.shape[1]
    height = gate_up_sum.shape[2]
    down_height = down_sum.shape[1]
    sends = []

    def start(copy):
        copy.start()
        sends.append(copy)

    def run_rows(dzh, dy, low):
        number = 16 * flip(zh, dzh) + 4 * flip(y, dy) + 8 * low
        return pl.ds(pl.multiple_of(number * height, 4 * height), 4 * height)

    def down_rows(dzh, dy):
        number = 2 * flip(zh, dzh) + flip(y, dy)
        return pl.ds(pl.multiple_of(number * down_height, down_height), down_height)

    def act_rows(step):
        return pl.ds(pl.multiple_of(rank(step) * act_height, act_height), act_height)

    for turn, dzh in enumerate((1, 0)):
        for s in range(sets):
            for low in (0, 1):
                start(
                    push(
                        gate_up_ref.at[s, run_rows(dzh, 1, low)],
                        across_gate.at[turn, s, low],
                        across_send.at[turn, s, low],
                        across_recv.at[turn, s, low],
                        across,
                    )
                )
            start(
                push(
                    down_ref.at[s, down_rows(dzh, 1)],
                    across_down.at[turn, s],
                    across_send.at[turn, s, 2],
                    across_recv.at[turn, s, 2],
                    across,
                )
            )
    acts = [back_ref, out_ref]
    act_sums = [back_sum, out_sum]
    sibling = member((0, 0, 1))
    plan = [(1, 1), (0, 1), (1, 0), (0, 0)]
    for which in (0, 1):
        for dl, dx in plan:
            start(
                push(
                    acts[which].at[:, act_rows((dl, dx, 1))],
                    core_buf.at[which, dl, dx],
                    core_send.at[which, dl, dx],
                    core_recv.at[which, dl, dx],
                    sibling,
                )
            )

    def core_add(which, dl, dx):
        block = core_buf.at[which, dl, dx]
        arrived(block, core_recv.at[which, dl, dx], sibling)
        for s in range(sets):
            add_into(block.at[s], [block.at[s], acts[which].at[s, act_rows((dl, dx, 0))]])

    for which in (0, 1):
        for dl in (1, 0):
            core_add(which, dl, 1)
            start(
                push(
                    core_buf.at[which, dl, 1],
                    x_buf.at[which, dl],
                    x_send.at[which, dl],
                    x_recv.at[which, dl],
                    member((0, 1, 0)),
                )
            )
    for s in range(sets):
        for low in (0, 1):
            block = across_gate.at[0, s, low]
            arrived(block, across_recv.at[0, s, low], across)
            add_into(block, [block, gate_up_ref.at[s, run_rows(1, 0, low)]])
            start(push(block, far_gate.at[s, low], far_send.at[s, low], far_recv.at[s, low], far))
        block = across_down.at[0, s]
        arrived(block, across_recv.at[0, s, 2], across)
        add_into(block, [block, down_ref.at[s, down_rows(1, 0)]])
        start(push(block, far_down.at[s], far_send.at[s, 2], far_recv.at[s, 2], far))
    for which in (0, 1):
        core_add(which, 1, 0)
        arrived(x_buf.at[which, 1], x_recv.at[which, 1], member((0, 1, 0)))
        for s in range(sets):
            block = x_buf.at[which, 1, s]
            add_into(block, [block, core_buf.at[which, 1, 0, s]])
        start(
            push(
                x_buf.at[which, 1],
                z_buf.at[which],
                z_send.at[which],
                z_recv.at[which],
                member((1, 0, 0)),
            )
        )
    for which in (0, 1):
        core_add(which, 0, 0)
        arrived(x_buf.at[which, 0], x_recv.at[which, 0], member((0, 1, 0)))
        arrived(z_buf.at[which], z_recv.at[which], member((1, 0, 0)))
        for s in range(sets):
            add_into(
                act_sums[which].at[s],
                [core_buf.at[which, 0, 0, s], x_buf.at[which, 0, s], z_buf.at[which, s]],
            )
    for s in range(sets):
        for low in (0, 1):
            block = across_gate.at[1, s, low]
            arrived(block, across_recv.at[1, s, low], across)
            arrived(far_gate.at[s, low], far_recv.at[s, low], far)
            add_into(block, [block, far_gate.at[s, low], gate_up_ref.at[s, run_rows(0, 0, low)]])
        arrived(across_down.at[1, s], across_recv.at[1, s, 2], across)
        arrived(far_down.at[s], far_recv.at[s, 2], far)
        add_into(
            down_sum.at[s],
            [across_down.at[1, s], far_down.at[s], down_ref.at[s, down_rows(0, 0)]],
        )

    def share(step, s):
        number = 2 * flip(x, step[1]) + flip(core, step[2])
        return across_gate.at[1, s, flip(zl, step[0]), pl.ds(pl.multiple_of(number * height, height), height)]

    for slot, step in enumerate(RANK_STEPS):
        if step != own_step:
            for s in range(sets):
                start(
                    push(
                        share(step, s),
                        rank_buf.at[slot, s],
                        rank_send.at[slot, s],
                        rank_recv.at[slot, s],
                        member(step),
                    )
                )
    for slot, step in enumerate(RANK_STEPS):
        for s in range(sets):
            if step == own_step:
                add_into(gate_up_sum.at[rank(step), s], [share(step, s)])
            else:
                arrived(rank_buf.at[slot, s], rank_recv.at[slot, s], member(step))
                add_into(gate_up_sum.at[rank(step), s], [rank_buf.at[slot, s]])
    for copy in sends:
        copy.wait_send()


def scatter_ff(out_part, back_part, gate_up_grad, down_grad):
    sets, rows, model = out_part.shape
    width = gate_up_grad.shape[2]
    act_height = rows // 8
    height = gate_up_grad.shape[1] // 32
    down_height = down_grad.shape[1] // 4
    dma = pltpu.SemaphoreType.DMA
    vmem = pl.BlockSpec(memory_space=pltpu.VMEM)
    return pl.pallas_call(
        scatter_ff_kernel,
        out_shape=(
            jax.ShapeDtypeStruct((sets, act_height, model), F32),
            jax.ShapeDtypeStruct((sets, act_height, model), F32),
            jax.ShapeDtypeStruct((8, sets, height, width), F32),
            jax.ShapeDtypeStruct((sets, down_height, model), F32),
        ),
        in_specs=[vmem] * 4,
        out_specs=(vmem,) * 4,
        scratch_shapes=[
            pltpu.VMEM((2, 2, 2, sets, act_height, model), BF16),
            pltpu.VMEM((2, 2, sets, act_height, model), BF16),
            pltpu.VMEM((2, sets, act_height, model), BF16),
            pltpu.VMEM((2, sets, 2, 4 * height, width), BF16),
            pltpu.VMEM((2, sets, down_height, model), BF16),
            pltpu.VMEM((sets, 2, 4 * height, width), BF16),
            pltpu.VMEM((sets, down_height, model), BF16),
            pltpu.VMEM((8, sets, height, width), BF16),
            dma((2, 2, 2)),
            dma((2, 2, 2)),
            dma((2, 2)),
            dma((2, 2)),
            dma((2,)),
            dma((2,)),
            dma((2, sets, 3)),
            dma((2, sets, 3)),
            dma((sets, 3)),
            dma((sets, 3)),
            dma((8, sets)),
            dma((8, sets)),
        ],
        compiler_params=pltpu.CompilerParams(
            collective_id=2, has_side_effects=True, vmem_limit_bytes=60 * 2**20
        ),
        name="scatter_ff",
    )(out_part, back_part, gate_up_grad, down_grad)


def slot_index(order, direction, offset, z, y, x):
    axis = {"u": "z", "d": "z"}.get(direction, direction)
    index, count = 0, 1
    values = dict(z=z + offset[0], y=flip(y, offset[1]), x=flip(x, offset[2]))
    sizes = dict(z=4, y=2, x=2)
    for earlier in order[: order.index(axis)]:
        index = index * sizes[earlier] + values[earlier]
        count *= sizes[earlier]
    if axis == "z":
        index = index * 4 + values["z"]
        count *= 4
    return index, count


def slot_base(order):
    base, total = {}, 0
    for direction in ("x", "y", "u", "d"):
        base[direction] = total
        total += slot_index(order, direction, (0, 0, 0), 0, 0, 0)[1]
    return base, total


def scatter_attn_kernel(
    gains_ref,
    qkv_ref,
    out_ref,
    gains_sum,
    qkv_sum,
    out_sum,
    core_qkv,
    core_out,
    slots_0,
    slots_1,
    slots_2,
    slots_3,
    gains_buf,
    core_send,
    core_recv,
    tree_send,
    tree_recv,
    gains_send,
    gains_recv,
):
    z, y, x, core = here()
    me = 2 * (z * 4 + y * 2 + x) + core
    greet_all(z, y, x, core)
    height = qkv_sum.shape[1]
    pieces = [
        (qkv_ref, qkv_sum, core_qkv, 0, "zxy", slots_0),
        (qkv_ref, qkv_sum, core_qkv, 1, "zyx", slots_1),
        (out_ref, out_sum, core_out, 0, "xyz", slots_2),
        (out_ref, out_sum, core_out, 1, "yxz", slots_3),
    ]
    sibling = neighbour("s", z, y, x, core)
    events = sorted(
        ((-hops(offset), rank, piece, offset) for piece in range(4) for rank, offset in enumerate(OFFSETS)),
        key=lambda event: event[:3],
    )

    def own_rows(piece, chip, of_core):
        source, _, _, index, _, _ = pieces[piece]
        return source.at[index, pl.ds(pl.multiple_of((2 * chip + of_core) * height, height), height), :]

    def core_copy(piece, offset):
        chip = chip_of(offset, z, y, x)
        _, _, buf, index, _, _ = pieces[piece]
        return push(
            own_rows(piece, chip, 1 - core),
            buf.at[index, chip],
            core_send.at[piece, chip],
            core_recv.at[piece, chip],
            sibling,
        )

    def tree_copy(piece, offset):
        _, _, buf, index, order, slots = pieces[piece]
        chip = chip_of(offset, z, y, x)
        toward = came_from(order, offset)
        seen = {"x": "x", "y": "y", "u": "d", "d": "u"}[toward]
        base, _ = slot_base(order)
        index_there, _ = slot_index(order, seen, offset, z, y, x)
        place = base[seen] + index_there
        return push(
            buf.at[index, chip],
            slots.at[place],
            tree_send.at[piece, chip],
            tree_recv.at[piece, place],
            neighbour(toward, z, y, x, core),
        )

    def gains_copy(step):
        other = lax.rem(me + step, 32)
        return push(
            gains_ref.at[other],
            gains_buf.at[me],
            gains_send.at[step],
            gains_recv.at[me],
            (lax.div(other, 2), lax.rem(other, 2)),
        )

    for _, _, piece, offset in events:
        maybe(offset_exists(offset, z), core_copy(piece, offset).start)

    def gains_start(step, carry):
        gains_copy(step).start()
        return carry

    lax.fori_loop(1, 32, gains_start, 0)

    def handle(piece, offset):
        _, result, buf, index, order, slots = pieces[piece]
        base, _ = slot_base(order)

        def go():
            chip = chip_of(offset, z, y, x)
            block = buf.at[index, chip]
            arrived(block, core_recv.at[piece, chip], sibling)
            sure, unsure = [], []
            for direction in onward(order, offset):
                local, _ = slot_index(order, direction, offset, z, y, x)
                place = base[direction] + local
                (sure if direction in "xy" else unsure).append((direction, place))
            terms = [block, own_rows(piece, chip, core)]
            for direction, place in sure:
                arrived(slots.at[place], tree_recv.at[piece, place], sibling)
                terms.append(slots.at[place])
            last = hops(offset) == 0
            target = result.at[index] if last else block
            add_into(target, terms)
            for direction, place in unsure:

                def more(place=place):
                    arrived(slots.at[place], tree_recv.at[piece, place], sibling)
                    add_into(target, [target, slots.at[place]])

                maybe(direction_exists(direction, z), more)
            if not last:
                tree_copy(piece, offset).start()

        maybe(offset_exists(offset, z), go)

    for _, _, piece, offset in events:
        handle(piece, offset)

    gains_sum[...] = gains_ref[me]

    def gains_wait(step, carry):
        other = lax.rem(me + step, 32)
        gains_copy(step).wait_send()
        arrived(gains_buf.at[other], gains_recv.at[other], sibling)
        gains_sum[...] += gains_buf[other]
        return carry

    lax.fori_loop(1, 32, gains_wait, 0)
    for _, _, piece, offset in events:

        def finish(piece=piece, offset=offset):
            core_copy(piece, offset).wait_send()
            if hops(offset) > 0:
                tree_copy(piece, offset).wait_send()

        maybe(offset_exists(offset, z), finish)


def scatter_attn(gain_parts, qkv_grad, out_grad):
    sets, rows, qkv_width = qkv_grad.shape
    out_width = out_grad.shape[2]
    height = rows // 32
    dma = pltpu.SemaphoreType.DMA
    vmem = pl.BlockSpec(memory_space=pltpu.VMEM)
    places = [slot_base(order)[1] for order in ORDERS]
    return pl.pallas_call(
        scatter_attn_kernel,
        out_shape=(
            jax.ShapeDtypeStruct(gain_parts.shape[1:], F32),
            jax.ShapeDtypeStruct((sets, height, qkv_width), F32),
            jax.ShapeDtypeStruct((sets, height, out_width), F32),
        ),
        in_specs=[vmem] * 3,
        out_specs=(vmem,) * 3,
        scratch_shapes=[
            pltpu.VMEM((sets, 16, height, qkv_width), BF16),
            pltpu.VMEM((sets, 16, height, out_width), BF16),
            pltpu.VMEM((places[0], height, qkv_width), BF16),
            pltpu.VMEM((places[1], height, qkv_width), BF16),
            pltpu.VMEM((places[2], height, out_width), BF16),
            pltpu.VMEM((places[3], height, out_width), BF16),
            pltpu.VMEM((32,) + gain_parts.shape[1:], F32),
            dma((4, 16)),
            dma((4, 16)),
            dma((4, 16)),
            dma((4, max(places))),
            dma((32,)),
            dma((32,)),
        ],
        compiler_params=pltpu.CompilerParams(
            collective_id=3, has_side_effects=True, vmem_limit_bytes=60 * 2**20
        ),
        name="scatter_attn",
    )(gain_parts, qkv_grad, out_grad)


def by_set(activations, weight):
    return jnp.einsum("sfk,ske->sfe", activations, weight, preferred_element_type=F32)


def by_set_back(gradients, weight):
    return jnp.einsum("sfe,ske->sfk", gradients, weight, preferred_element_type=F32)


def set_grad(activations, gradients):
    return jnp.einsum("sfk,sfe->ske", activations, gradients, preferred_element_type=F32)


def head_sums(product, spread):
    high = product.astype(BF16)
    low = (product - high.astype(F32)).astype(BF16)
    sums = jnp.dot(high, spread, preferred_element_type=F32)
    return sums + jnp.dot(low, spread, preferred_element_type=F32)


def over_heads(values, spread):
    return lax.dot_general(
        values, spread, (((1,), (1,)), ((), ())), preferred_element_type=F32
    )


def local_fast(
    tokens,
    norm_attn,
    w_qkv,
    w_out,
    norm_ff,
    w_gate_up,
    w_down,
    cotangent,
    valid_frames,
    item_lengths,
):
    frame_count, positions, model = tokens.shape
    head_count = model // HEAD_DIM
    ff_units = w_gate_up.shape[2] // 2
    score_scale = 1.0 / math.sqrt(HEAD_DIM)
    own_gain = norm_attn.shape[1]
    gains = jnp.zeros((16, 128), BF16)
    gains = gains.at[0:positions, :own_gain].set(norm_attn)
    gains = gains.at[positions : 2 * positions, :own_gain].set(norm_ff)
    gains_full, qkv_full, out_full = gather_attn(gains, w_qkv, w_out)
    gains_rows = jnp.swapaxes(gains_full[:, : 2 * positions, :own_gain], 0, 1)
    gains_rows = gains_rows.reshape(2 * positions, model).astype(F32)
    gain_one = gains_rows[:positions, None, :]
    gain_two = gains_rows[positions:, None, :]

    spread = (
        jnp.arange(model)[:, None] // HEAD_DIM == jnp.arange(128)[None, :]
    ).astype(BF16)

    device_index = lax.axis_index(("dp", "pair"))
    local_ids = jnp.arange(frame_count, dtype=jnp.int32)
    frame_ids = device_index * frame_count + local_ids
    item_ends = jnp.cumsum(item_lengths)
    item_starts = item_ends - item_lengths
    in_item = (frame_ids[:, None] >= item_starts[None, :]) & (
        frame_ids[:, None] < item_ends[None, :]
    )
    item_share = 8 * frame_count / item_lengths.astype(F32)
    frame_weight = jnp.sum(jnp.where(in_item, item_share[None, :], 0.0), axis=1)
    frame_weight = jnp.where(local_ids < valid_frames[0], frame_weight, 0.0)
    grad_out = jnp.swapaxes(cotangent, 0, 1).astype(F32) * frame_weight[None, :, None]
    grad_low = grad_out.astype(BF16)

    resid_in = jnp.swapaxes(tokens, 0, 1).astype(F32)
    normed_one, inverse_one = normed(resid_in)
    attn_in = (normed_one * gain_one).astype(BF16)
    qkv = by_set(attn_in, qkv_full).astype(BF16)
    queries = [qkv[p, :, :model].astype(F32) for p in range(positions)]
    keys = [qkv[p, :, model : 2 * model].astype(F32) for p in range(positions)]
    values = [qkv[p, :, 2 * model :].astype(F32) for p in range(positions)]
    probs = []
    contexts = []
    for p in range(positions):
        scores = [head_sums(queries[p] * keys[q], spread) * score_scale for q in range(p + 1)]
        top = functools.reduce(jnp.maximum, scores)
        powers = [jnp.exp(score - top) for score in scores]
        total = functools.reduce(jnp.add, powers)
        probs.append([power / total for power in powers])
        context = sum(
            over_heads(prob.astype(BF16), spread) * values[q] for q, prob in enumerate(probs[p])
        )
        contexts.append(context.astype(BF16))
    context = jnp.stack(contexts)
    resid_mid = resid_in + by_set(context, out_full)
    normed_two, inverse_two = normed(resid_mid)
    ff_in = (normed_two * gain_two).astype(BF16)

    unit = w_down.shape[1]
    parts = w_gate_up.reshape(positions, -1, 2, 2, 2, 2, 2, 2, unit)
    parts = parts.transpose(4, 6, 7, 0, 1, 2, 3, 5, 8)
    parts = parts.reshape(8, positions, w_gate_up.shape[1], 8 * unit)
    gate_up_full, down_full, ff_rows, grad_rows = gather_ff(parts, w_down, ff_in, grad_low)
    split = 4 * unit
    gate_up = by_set(ff_rows, gate_up_full)
    gate, up = gate_up[..., :split], gate_up[..., split:]
    sigmoid_gate = jax.nn.sigmoid(gate)
    silu_gate = gate * sigmoid_gate
    hidden = (silu_gate * up).astype(BF16)
    out_part = by_set(hidden, down_full).astype(BF16)
    d_hidden = by_set_back(grad_rows, down_full)
    d_gate = d_hidden * up * sigmoid_gate * (1.0 + gate * (1.0 - sigmoid_gate))
    d_up = d_hidden * silu_gate
    d_gate_up = jnp.concatenate([d_gate, d_up], axis=-1).astype(BF16)
    down_grad = set_grad(hidden, grad_rows).astype(BF16)
    gate_up_grad = set_grad(ff_rows, d_gate_up).astype(BF16)
    back_part = by_set_back(d_gate_up, gate_up_full).astype(BF16)
    out_sum, d_ff_in, gate_up_sum, down_sum = scatter_ff(
        out_part, back_part, gate_up_grad, down_grad
    )
    output = jnp.swapaxes((resid_mid + out_sum).astype(BF16), 0, 1)
    share_gate_up = gate_up_sum.reshape(2, 2, 2, positions, -1, 2, 2, 2, unit)
    share_gate_up = share_gate_up.transpose(3, 4, 5, 6, 0, 7, 1, 2, 8)
    share_gate_up = share_gate_up.reshape(w_gate_up.shape)

    grad_norm_ff = jnp.sum(normed_two * d_ff_in, axis=1)
    d_mid = grad_out + norm_back(normed_two, inverse_two, d_ff_in * gain_two)
    d_mid_low = d_mid.astype(BF16)
    out_grad = set_grad(context, d_mid_low).astype(BF16)
    d_context = by_set_back(d_mid_low, out_full).astype(BF16).astype(F32)
    d_queries = []
    d_keys = [0.0] * positions
    d_values = [0.0] * positions
    for p in range(positions):
        d_probs = [head_sums(d_context[p] * values[q], spread) for q in range(p + 1)]
        mean = functools.reduce(jnp.add, [prob * d for prob, d in zip(probs[p], d_probs)])
        d_query = 0.0
        for q in range(p + 1):
            d_score = (probs[p][q] * (d_probs[q] - mean)).astype(BF16)
            d_score = over_heads(d_score, spread)
            d_values[q] += over_heads(probs[p][q].astype(BF16), spread) * d_context[p]
            d_query += d_score * keys[q]
            d_keys[q] += d_score * queries[p]
        d_queries.append(d_query)
    d_qkv = jnp.stack(
        [
            jnp.concatenate(
                [d_queries[p] * score_scale, d_keys[p] * score_scale, d_values[p]], axis=-1
            )
            for p in range(positions)
        ]
    ).astype(BF16)
    qkv_grad = set_grad(attn_in, d_qkv).astype(BF16)
    d_attn_in = by_set_back(d_qkv, qkv_full)
    grad_norm_attn = jnp.sum(normed_one * d_attn_in, axis=1)
    grad_tokens = d_mid + norm_back(normed_one, inverse_one, d_attn_in * gain_one)
    grad_tokens = jnp.swapaxes(grad_tokens, 0, 1)
    gain_grads = jnp.concatenate([grad_norm_attn, grad_norm_ff], axis=0)
    gain_grads = jnp.swapaxes(gain_grads.reshape(2 * positions, 32, own_gain), 0, 1)
    gain_parts = jnp.zeros((32, 8, 128), F32).at[:, : 2 * positions, :own_gain].set(gain_grads)
    gains_sum, share_qkv, share_out = scatter_attn(gain_parts, qkv_grad, out_grad)
    return (
        output,
        grad_tokens,
        gains_sum[:positions, :own_gain],
        share_qkv,
        share_out,
        gains_sum[positions : 2 * positions, :own_gain],
        share_gate_up,
        down_sum,
    )


def solution(mesh):
    in_specs = (
        P(("dp", "pair"), None, None),
        P(None, ("dp", "pair")),
        P(None, ("dp", "pair"), None),
        P(None, ("dp", "pair"), None),
        P(None, ("dp", "pair")),
        P(None, ("dp", "pair"), None),
        P(None, ("dp", "pair"), None),
        P(("dp", "pair"), None, None),
        P(("dp", "pair")),
        P(),
    )
    out_specs = (
        P(("dp", "pair"), None, None),
        P(("dp", "pair"), None, None),
        P(None, ("dp", "pair")),
        P(None, ("dp", "pair"), None),
        P(None, ("dp", "pair"), None),
        P(None, ("dp", "pair")),
        P(None, ("dp", "pair"), None),
        P(None, ("dp", "pair"), None),
    )
    body = local_fast if mesh.shape["dp"] == 16 and mesh.shape["pair"] == 2 else local
    return jax.shard_map(body, mesh=mesh, in_specs=in_specs, out_specs=out_specs, check_vma=False)
```

```python
import functools
import math

import jax
import jax.numpy as jnp
from jax import lax
from jax.experimental import pallas as pl
from jax.experimental.pallas import tpu as pltpu
from jax.sharding import PartitionSpec as P

HEAD_DIM = 64


def per_pos(activations, weight):
    return jnp.einsum("fgk,gke->fge", activations, weight, preferred_element_type=jnp.float32)


def per_pos_back(gradients, weight):
    return jnp.einsum("fge,gke->fgk", gradients, weight, preferred_element_type=jnp.float32)


def pos_grad(activations, gradients):
    return jnp.einsum("fgk,fge->kge", activations, gradients, preferred_element_type=jnp.float32)


def gain_grad(normed_rows, gradients):
    return jnp.transpose(jnp.sum(normed_rows * gradients, axis=0))


def back_layout(share):
    return jnp.swapaxes(share, 0, 1)


def normed(values):
    inverse = lax.rsqrt(jnp.mean(values * values, axis=-1, keepdims=True) + 1e-05)
    return (values * inverse, inverse)


def norm_back(normed_rows, inverse, gradients):
    return inverse * (
        gradients - normed_rows * jnp.mean(gradients * normed_rows, axis=-1, keepdims=True)
    )


def gather_ff_fwd(norm_ff, w_gate_up, w_down, start, group):
    return (
        lax.all_gather(norm_ff[start : start + group], ("dp", "pair"), axis=1, tiled=True),
        lax.all_gather(w_gate_up[start : start + group], ("dp", "pair"), axis=1, tiled=True),
        lax.all_gather(w_down[start : start + group], ("dp", "pair"), axis=1, tiled=True),
    )


def gather_ff_back(norm_ff, w_gate_up, w_down, start, group):
    return (
        lax.all_gather(norm_ff[start : start + group], ("dp", "pair"), axis=1, tiled=True),
        lax.all_gather(w_gate_up[start : start + group], ("dp", "pair"), axis=1, tiled=True),
        lax.all_gather(w_down[start : start + group], ("dp", "pair"), axis=1, tiled=True),
    )


def local(
    tokens,
    norm_attn,
    w_qkv,
    w_out,
    norm_ff,
    w_gate_up,
    w_down,
    cotangent,
    valid_frames,
    item_lengths,
):
    frame_count, positions, model_width = tokens.shape
    head_count = model_width // HEAD_DIM
    ff_units = w_gate_up.shape[2] // 2
    score_scale = 1.0 / math.sqrt(HEAD_DIM)
    causal = jnp.arange(positions)[:, None] >= jnp.arange(positions)[None, :]
    head_shape = (frame_count, positions, head_count, HEAD_DIM)
    group = 1
    gains_attn, qkv_full, out_full = (
        lax.all_gather(norm_attn, ("dp", "pair"), axis=1, tiled=True),
        lax.all_gather(w_qkv, ("dp", "pair"), axis=1, tiled=True),
        lax.all_gather(w_out, ("dp", "pair"), axis=1, tiled=True),
    )
    resid_in = tokens.astype(jnp.float32)
    normed_one, inverse_one = normed(resid_in)
    attn_in = (normed_one * gains_attn.astype(jnp.float32)[None]).astype(jnp.bfloat16)
    qkv_rows = per_pos(attn_in, qkv_full).astype(jnp.bfloat16)
    queries = qkv_rows[..., :model_width].reshape(head_shape)
    key_heads = qkv_rows[..., model_width : 2 * model_width].reshape(head_shape)
    value_heads = qkv_rows[..., 2 * model_width :].reshape(head_shape)
    scores = (
        jnp.einsum("fphd,fqhd->fhpq", queries, key_heads, preferred_element_type=jnp.float32)
        * score_scale
    )
    scores = jnp.where(causal, scores, -1e30)
    row_max = jnp.max(scores, axis=-1, keepdims=True)
    attn_probs = jnp.exp(scores - row_max)
    attn_probs = attn_probs / jnp.sum(attn_probs, axis=-1, keepdims=True)
    probs_low = attn_probs.astype(jnp.bfloat16)
    context = jnp.einsum(
        "fhpq,fqhd->fphd", probs_low, value_heads, preferred_element_type=jnp.float32
    )
    context = context.astype(jnp.bfloat16).reshape(frame_count, positions, model_width)
    resid_mid = resid_in + per_pos(context, out_full)
    kept_parts = []
    out_parts = []
    for start in range(0, positions, group):
        gains_ff, gate_up_full, down_full = gather_ff_fwd(norm_ff, w_gate_up, w_down, start, group)
        mid_part = resid_mid[:, start : start + group]
        normed_two, inverse_two = normed(mid_part)
        ff_in = (normed_two * gains_ff.astype(jnp.float32)[None]).astype(jnp.bfloat16)
        gate_up = per_pos(ff_in, gate_up_full)
        gate_part = gate_up[..., :ff_units]
        up_part = gate_up[..., ff_units:]
        sigmoid_gate = jax.nn.sigmoid(gate_part)
        silu_gate = gate_part * sigmoid_gate
        hidden = (silu_gate * up_part).astype(jnp.bfloat16)
        out_parts.append(mid_part + per_pos(hidden, down_full))
        kept_parts.append(
            (normed_two, inverse_two, ff_in, gate_part, up_part, sigmoid_gate, silu_gate, hidden)
        )
    output = jnp.concatenate(out_parts, axis=1).astype(jnp.bfloat16)
    device_index = lax.axis_index(("dp", "pair"))
    local_ids = jnp.arange(frame_count, dtype=jnp.int32)
    frame_ids = device_index * frame_count + local_ids
    item_ends = jnp.cumsum(item_lengths)
    item_starts = item_ends - item_lengths
    in_item = (frame_ids[:, None] >= item_starts[None, :]) & (
        frame_ids[:, None] < item_ends[None, :]
    )
    item_share = 8 * frame_count / item_lengths.astype(jnp.float32)
    frame_weight = jnp.sum(jnp.where(in_item, item_share[None, :], 0.0), axis=1)
    frame_weight = jnp.where(local_ids < valid_frames[0], frame_weight, 0.0)
    grad_out = cotangent.astype(jnp.float32) * frame_weight[:, None, None]
    mid_grads = []
    share_norm_ff_parts = []
    share_gate_up_parts = []
    share_down_parts = []
    for index, start in enumerate(range(0, positions, group)):
        normed_two, inverse_two, ff_in, gate_part, up_part, sigmoid_gate, silu_gate, hidden = (
            kept_parts[index]
        )
        gains_ff, gate_up_full, down_full = gather_ff_back(norm_ff, w_gate_up, w_down, start, group)
        grad_part = grad_out[:, start : start + group]
        grad_low = grad_part.astype(jnp.bfloat16)
        grad_down = pos_grad(hidden, grad_low)
        d_hidden = per_pos_back(grad_low, down_full)
        d_gate = d_hidden * up_part * sigmoid_gate * (1.0 + gate_part * (1.0 - sigmoid_gate))
        d_up = d_hidden * silu_gate
        d_gate_up = jnp.concatenate([d_gate, d_up], axis=-1).astype(jnp.bfloat16)
        grad_gate_up = pos_grad(ff_in, d_gate_up)
        d_ff_in = per_pos_back(d_gate_up, gate_up_full)
        grad_norm_ff = gain_grad(normed_two, d_ff_in)
        mid_grads.append(
            grad_part
            + norm_back(normed_two, inverse_two, d_ff_in * gains_ff.astype(jnp.float32)[None])
        )
        share_a, share_b, share_c = (
            lax.psum_scatter(grad_norm_ff, ("dp", "pair"), scatter_dimension=0, tiled=True),
            lax.psum_scatter(grad_gate_up, ("dp", "pair"), scatter_dimension=0, tiled=True),
            lax.psum_scatter(grad_down, ("dp", "pair"), scatter_dimension=0, tiled=True),
        )
        share_norm_ff_parts.append(jnp.transpose(share_a))
        share_gate_up_parts.append(back_layout(share_b))
        share_down_parts.append(back_layout(share_c))
    d_mid = jnp.concatenate(mid_grads, axis=1)
    gains_attn, qkv_full, out_full = (
        lax.all_gather(norm_attn, ("dp", "pair"), axis=1, tiled=True),
        lax.all_gather(w_qkv, ("dp", "pair"), axis=1, tiled=True),
        lax.all_gather(w_out, ("dp", "pair"), axis=1, tiled=True),
    )
    d_mid_low = d_mid.astype(jnp.bfloat16)
    grad_out_proj = pos_grad(context, d_mid_low)
    d_context = per_pos_back(d_mid_low, out_full).astype(jnp.bfloat16).reshape(head_shape)
    d_probs = jnp.einsum(
        "fphd,fqhd->fhpq", d_context, value_heads, preferred_element_type=jnp.float32
    )
    d_values = jnp.einsum(
        "fhpq,fphd->fqhd", probs_low, d_context, preferred_element_type=jnp.float32
    )
    d_scores = attn_probs * (d_probs - jnp.sum(attn_probs * d_probs, axis=-1, keepdims=True))
    d_scores = d_scores.astype(jnp.bfloat16)
    d_queries = (
        jnp.einsum("fhpq,fqhd->fphd", d_scores, key_heads, preferred_element_type=jnp.float32)
        * score_scale
    )
    d_keys = (
        jnp.einsum("fhpq,fphd->fqhd", d_scores, queries, preferred_element_type=jnp.float32)
        * score_scale
    )
    row_shape = (frame_count, positions, model_width)
    d_qkv = jnp.concatenate(
        [d_queries.reshape(row_shape), d_keys.reshape(row_shape), d_values.reshape(row_shape)],
        axis=-1,
    ).astype(jnp.bfloat16)
    grad_qkv = pos_grad(attn_in, d_qkv)
    d_attn_in = per_pos_back(d_qkv, qkv_full)
    grad_norm_attn = gain_grad(normed_one, d_attn_in)
    grad_tokens = d_mid + norm_back(
        normed_one, inverse_one, d_attn_in * gains_attn.astype(jnp.float32)[None]
    )
    share_norm_attn, share_qkv, share_out = (
        lax.psum_scatter(grad_norm_attn, ("dp", "pair"), scatter_dimension=0, tiled=True),
        lax.psum_scatter(grad_qkv, ("dp", "pair"), scatter_dimension=0, tiled=True),
        lax.psum_scatter(grad_out_proj, ("dp", "pair"), scatter_dimension=0, tiled=True),
    )
    share_norm_attn = jnp.transpose(share_norm_attn)
    share_qkv = back_layout(share_qkv)
    share_out = back_layout(share_out)
    share_norm_ff = jnp.concatenate(share_norm_ff_parts, axis=0)
    share_gate_up = jnp.concatenate(share_gate_up_parts, axis=0)
    share_down = jnp.concatenate(share_down_parts, axis=0)
    return (
        output,
        grad_tokens,
        share_norm_attn,
        share_qkv,
        share_out,
        share_norm_ff,
        share_gate_up,
        share_down,
    )


MESH_ID = pl.DeviceIdType.MESH
BF16 = jnp.bfloat16
F32 = jnp.float32


def here():
    dp = lax.axis_index("dp")
    core = lax.axis_index("pair")
    return lax.div(dp, 4), lax.rem(lax.div(dp, 2), 2), lax.rem(dp, 2), core


def flip(value, bit):
    return 1 - value if bit else value


def push(src, dst, send_sem, recv_sem, to):
    return pltpu.make_async_remote_copy(
        src_ref=src,
        dst_ref=dst,
        send_sem=send_sem,
        recv_sem=recv_sem,
        device_id=to,
        device_id_type=MESH_ID,
    )


def arrived(dst, recv_sem, to):
    push(dst, dst, recv_sem, recv_sem, to).wait_recv()


def greet_all(z, y, x, core):
    barrier = pltpu.get_barrier_semaphore()
    me = 2 * (z * 4 + y * 2 + x) + core

    def one(step, carry):
        other = lax.rem(me + step, 32)
        pl.semaphore_signal(
            barrier, inc=1, device_id=(lax.div(other, 2), lax.rem(other, 2)), device_id_type=MESH_ID
        )
        return carry

    lax.fori_loop(1, 32, one, 0)
    pl.semaphore_wait(barrier, 31)


def greet(peers):
    barrier = pltpu.get_barrier_semaphore()
    for to in peers:
        pl.semaphore_signal(barrier, inc=1, device_id=to, device_id_type=MESH_ID)
    pl.semaphore_wait(barrier, len(peers))


def maybe(condition, do):
    if condition is None:
        do()
    else:
        pl.when(condition)(do)


OFFSETS = [
    (dz, dy, dx) for dz in (0, -1, 1, -2, 2, -3, 3) for dy in (0, 1) for dx in (0, 1)
]
ORDERS = ("zxy", "zyx", "xyz", "yxz")


def hops(offset):
    return abs(offset[0]) + offset[1] + offset[2]


def arrival_axis(order, offset):
    part = dict(z=offset[0], y=offset[1], x=offset[2])
    last = None
    for axis in order:
        if part[axis] != 0:
            last = axis
    return last


def onward(order, offset):
    directions = []
    last = arrival_axis(order, offset)
    start = 0
    if last is not None:
        start = order.index(last) + 1
        if last == "z":
            directions.append("u" if offset[0] < 0 else "d")
    for axis in order[start:]:
        directions.extend(["u", "d"] if axis == "z" else [axis])
    return directions


def came_from(order, offset):
    last = arrival_axis(order, offset)
    if last == "z":
        return "d" if offset[0] < 0 else "u"
    return last


def offset_exists(offset, z):
    if offset[0] < 0:
        return z >= -offset[0]
    if offset[0] > 0:
        return z <= 3 - offset[0]
    return None


def direction_exists(direction, z):
    return {"u": z < 3, "d": z > 0}.get(direction)


DIRECTIONS = ("x", "y", "u", "d", "s")


def neighbour(direction, z, y, x, core):
    if direction == "x":
        return (z * 4 + y * 2 + 1 - x, core)
    if direction == "y":
        return (z * 4 + (1 - y) * 2 + x, core)
    if direction == "u":
        return (z * 4 + 4 + y * 2 + x, core)
    if direction == "d":
        return (z * 4 - 4 + y * 2 + x, core)
    return (z * 4 + y * 2 + x, 1 - core)


def chip_of(offset, z, y, x):
    return (z + offset[0]) * 4 + flip(y, offset[1]) * 2 + flip(x, offset[2])


RANK_STEPS = sorted(
    ((dl, dx, dc) for dl in (0, 1) for dx in (0, 1) for dc in (0, 1)), key=lambda step: (sum(step), step)
)


def group_place(z, y, x, core):
    zh, zl = lax.div(z, 2), lax.rem(z, 2)

    def member(step):
        return ((2 * zh + flip(zl, step[0])) * 4 + y * 2 + flip(x, step[1]), flip(core, step[2]))

    def rank(step):
        return 4 * flip(zl, step[0]) + 2 * flip(x, step[1]) + flip(core, step[2])

    def device(step, dzh=0, dy=0):
        return 16 * flip(zh, dzh) + 4 * flip(y, dy) + 8 * flip(zl, step[0]) + 2 * flip(x, step[1]) + flip(core, step[2])

    far = ((2 * (1 - zh) + zl) * 4 + y * 2 + x, core)
    across = (z * 4 + (1 - y) * 2 + x, core)
    return zh, zl, member, rank, device, far, across


def add_into(target, sources, rows=16, columns=1024):
    height, width = target.shape
    across = width // columns

    def one(step, carry):
        top = pl.multiple_of(lax.div(step, across) * rows, rows)
        left = pl.multiple_of(lax.rem(step, across) * columns, columns)
        spot = (pl.ds(top, rows), pl.ds(left, columns))
        total = sources[0][spot].astype(F32)
        for source in sources[1:]:
            total = total + source[spot].astype(F32)
        target[spot] = total.astype(target.dtype)
        return carry

    lax.fori_loop(0, (height // rows) * across, one, 0)


def scatter_ff_kernel(
    out_ref,
    back_ref,
    gate_up_ref,
    down_ref,
    out_sum,
    back_sum,
    gate_up_sum,
    down_sum,
    core_buf,
    x_buf,
    z_buf,
    across_gate,
    across_down,
    far_gate,
    far_down,
    rank_buf,
    core_send,
    core_recv,
    x_send,
    x_recv,
    z_send,
    z_recv,
    across_send,
    across_recv,
    far_send,
    far_recv,
    rank_send,
    rank_recv,
):
    z, y, x, core = here()
    zh, zl, member, rank, device, far, across = group_place(z, y, x, core)
    own_step = (0, 0, 0)
    others = RANK_STEPS[1:]
    greet([member(step) for step in others] + [far, across])
    sets = out_ref.shape[0]
    act_height = out_sum.shape[1]
    height = gate_up_sum.shape[2]
    down_height = down_sum.shape[1]
    sends = []

    def start(copy):
        copy.start()
        sends.append(copy)

    def run_rows(dzh, dy, low):
        number = 16 * flip(zh, dzh) + 4 * flip(y, dy) + 8 * low
        return pl.ds(pl.multiple_of(number * height, 4 * height), 4 * height)

    def down_rows(dzh, dy):
        number = 2 * flip(zh, dzh) + flip(y, dy)
        return pl.ds(pl.multiple_of(number * down_height, down_height), down_height)

    def act_rows(step):
        return pl.ds(pl.multiple_of(rank(step) * act_height, act_height), act_height)

    for turn, dzh in enumerate((1, 0)):
        for s in range(sets):
            for low in (0, 1):
                start(
                    push(
                        gate_up_ref.at[s, run_rows(dzh, 1, low)],
                        across_gate.at[turn, s, low],
                        across_send.at[turn, s, low],
                        across_recv.at[turn, s, low],
                        across,
                    )
                )
            start(
                push(
                    down_ref.at[s, down_rows(dzh, 1)],
                    across_down.at[turn, s],
                    across_send.at[turn, s, 2],
                    across_recv.at[turn, s, 2],
                    across,
                )
            )
    acts = [back_ref, out_ref]
    act_sums = [back_sum, out_sum]
    sibling = member((0, 0, 1))
    plan = [(1, 1), (0, 1), (1, 0), (0, 0)]
    for which in (0, 1):
        for dl, dx in plan:
            start(
                push(
                    acts[which].at[:, act_rows((dl, dx, 1))],
                    core_buf.at[which, dl, dx],
                    core_send.at[which, dl, dx],
                    core_recv.at[which, dl, dx],
                    sibling,
                )
            )

    def core_add(which, dl, dx):
        block = core_buf.at[which, dl, dx]
        arrived(block, core_recv.at[which, dl, dx], sibling)
        for s in range(sets):
            add_into(block.at[s], [block.at[s], acts[which].at[s, act_rows((dl, dx, 0))]])

    for which in (0, 1):
        for dl in (1, 0):
            core_add(which, dl, 1)
            start(
                push(
                    core_buf.at[which, dl, 1],
                    x_buf.at[which, dl],
                    x_send.at[which, dl],
                    x_recv.at[which, dl],
                    member((0, 1, 0)),
                )
            )
    for s in range(sets):
        for low in (0, 1):
            block = across_gate.at[0, s, low]
            arrived(block, across_recv.at[0, s, low], across)
            add_into(block, [block, gate_up_ref.at[s, run_rows(1, 0, low)]])
            start(push(block, far_gate.at[s, low], far_send.at[s, low], far_recv.at[s, low], far))
        block = across_down.at[0, s]
        arrived(block, across_recv.at[0, s, 2], across)
        add_into(block, [block, down_ref.at[s, down_rows(1, 0)]])
        start(push(block, far_down.at[s], far_send.at[s, 2], far_recv.at[s, 2], far))
    for which in (0, 1):
        core_add(which, 1, 0)
        arrived(x_buf.at[which, 1], x_recv.at[which, 1], member((0, 1, 0)))
        for s in range(sets):
            block = x_buf.at[which, 1, s]
            add_into(block, [block, core_buf.at[which, 1, 0, s]])
        start(
            push(
                x_buf.at[which, 1],
                z_buf.at[which],
                z_send.at[which],
                z_recv.at[which],
                member((1, 0, 0)),
            )
        )
    for which in (0, 1):
        core_add(which, 0, 0)
        arrived(x_buf.at[which, 0], x_recv.at[which, 0], member((0, 1, 0)))
        arrived(z_buf.at[which], z_recv.at[which], member((1, 0, 0)))
        for s in range(sets):
            add_into(
                act_sums[which].at[s],
                [core_buf.at[which, 0, 0, s], x_buf.at[which, 0, s], z_buf.at[which, s]],
            )
    for s in range(sets):
        for low in (0, 1):
            block = across_gate.at[1, s, low]
            arrived(block, across_recv.at[1, s, low], across)
            arrived(far_gate.at[s, low], far_recv.at[s, low], far)
            add_into(block, [block, far_gate.at[s, low], gate_up_ref.at[s, run_rows(0, 0, low)]])
        arrived(across_down.at[1, s], across_recv.at[1, s, 2], across)
        arrived(far_down.at[s], far_recv.at[s, 2], far)
        add_into(
            down_sum.at[s],
            [across_down.at[1, s], far_down.at[s], down_ref.at[s, down_rows(0, 0)]],
        )

    def share(step, s):
        number = 2 * flip(x, step[1]) + flip(core, step[2])
        return across_gate.at[1, s, flip(zl, step[0]), pl.ds(pl.multiple_of(number * height, height), height)]

    for slot, step in enumerate(RANK_STEPS):
        if step != own_step:
            for s in range(sets):
                start(
                    push(
                        share(step, s),
                        rank_buf.at[slot, s],
                        rank_send.at[slot, s],
                        rank_recv.at[slot, s],
                        member(step),
                    )
                )
    for slot, step in enumerate(RANK_STEPS):
        for s in range(sets):
            if step == own_step:
                add_into(gate_up_sum.at[rank(step), s], [share(step, s)])
            else:
                arrived(rank_buf.at[slot, s], rank_recv.at[slot, s], member(step))
                add_into(gate_up_sum.at[rank(step), s], [rank_buf.at[slot, s]])
    for copy in sends:
        copy.wait_send()


def scatter_ff(out_part, back_part, gate_up_grad, down_grad):
    sets, rows, model = out_part.shape
    width = gate_up_grad.shape[2]
    act_height = rows // 8
    height = gate_up_grad.shape[1] // 32
    down_height = down_grad.shape[1] // 4
    dma = pltpu.SemaphoreType.DMA
    vmem = pl.BlockSpec(memory_space=pltpu.VMEM)
    return pl.pallas_call(
        scatter_ff_kernel,
        out_shape=(
            jax.ShapeDtypeStruct((sets, act_height, model), F32),
            jax.ShapeDtypeStruct((sets, act_height, model), F32),
            jax.ShapeDtypeStruct((8, sets, height, width), F32),
            jax.ShapeDtypeStruct((sets, down_height, model), F32),
        ),
        in_specs=[vmem] * 4,
        out_specs=(vmem,) * 4,
        scratch_shapes=[
            pltpu.VMEM((2, 2, 2, sets, act_height, model), BF16),
            pltpu.VMEM((2, 2, sets, act_height, model), BF16),
            pltpu.VMEM((2, sets, act_height, model), BF16),
            pltpu.VMEM((2, sets, 2, 4 * height, width), BF16),
            pltpu.VMEM((2, sets, down_height, model), BF16),
            pltpu.VMEM((sets, 2, 4 * height, width), BF16),
            pltpu.VMEM((sets, down_height, model), BF16),
            pltpu.VMEM((8, sets, height, width), BF16),
            dma((2, 2, 2)),
            dma((2, 2, 2)),
            dma((2, 2)),
            dma((2, 2)),
            dma((2,)),
            dma((2,)),
            dma((2, sets, 3)),
            dma((2, sets, 3)),
            dma((sets, 3)),
            dma((sets, 3)),
            dma((8, sets)),
            dma((8, sets)),
        ],
        compiler_params=pltpu.CompilerParams(
            collective_id=2, has_side_effects=True, vmem_limit_bytes=60 * 2**20
        ),
        name="scatter_ff",
    )(out_part, back_part, gate_up_grad, down_grad)


def slot_index(order, direction, offset, z, y, x):
    axis = {"u": "z", "d": "z"}.get(direction, direction)
    index, count = 0, 1
    values = dict(z=z + offset[0], y=flip(y, offset[1]), x=flip(x, offset[2]))
    sizes = dict(z=4, y=2, x=2)
    for earlier in order[: order.index(axis)]:
        index = index * sizes[earlier] + values[earlier]
        count *= sizes[earlier]
    if axis == "z":
        index = index * 4 + values["z"]
        count *= 4
    return index, count


def slot_base(order):
    base, total = {}, 0
    for direction in ("x", "y", "u", "d"):
        base[direction] = total
        total += slot_index(order, direction, (0, 0, 0), 0, 0, 0)[1]
    return base, total


def scatter_attn_kernel(
    gains_ref,
    qkv_ref,
    out_ref,
    gains_sum,
    qkv_sum,
    out_sum,
    core_qkv,
    core_out,
    slots_0,
    slots_1,
    slots_2,
    slots_3,
    gains_buf,
    core_send,
    core_recv,
    tree_send,
    tree_recv,
    gains_send,
    gains_recv,
):
    z, y, x, core = here()
    me = 2 * (z * 4 + y * 2 + x) + core
    greet_all(z, y, x, core)
    height = qkv_sum.shape[1]
    pieces = [
        (qkv_ref, qkv_sum, core_qkv, 0, "zxy", slots_0),
        (qkv_ref, qkv_sum, core_qkv, 1, "zyx", slots_1),
        (out_ref, out_sum, core_out, 0, "xyz", slots_2),
        (out_ref, out_sum, core_out, 1, "yxz", slots_3),
    ]
    sibling = neighbour("s", z, y, x, core)
    events = sorted(
        ((-hops(offset), rank, piece, offset) for piece in range(4) for rank, offset in enumerate(OFFSETS)),
        key=lambda event: event[:3],
    )

    def own_rows(piece, chip, of_core):
        source, _, _, index, _, _ = pieces[piece]
        return source.at[index, pl.ds(pl.multiple_of((2 * chip + of_core) * height, height), height), :]

    def core_copy(piece, offset):
        chip = chip_of(offset, z, y, x)
        _, _, buf, index, _, _ = pieces[piece]
        return push(
            own_rows(piece, chip, 1 - core),
            buf.at[index, chip],
            core_send.at[piece, chip],
            core_recv.at[piece, chip],
            sibling,
        )

    def tree_copy(piece, offset):
        _, _, buf, index, order, slots = pieces[piece]
        chip = chip_of(offset, z, y, x)
        toward = came_from(order, offset)
        seen = {"x": "x", "y": "y", "u": "d", "d": "u"}[toward]
        base, _ = slot_base(order)
        index_there, _ = slot_index(order, seen, offset, z, y, x)
        place = base[seen] + index_there
        return push(
            buf.at[index, chip],
            slots.at[place],
            tree_send.at[piece, chip],
            tree_recv.at[piece, place],
            neighbour(toward, z, y, x, core),
        )

    def gains_copy(step):
        other = lax.rem(me + step, 32)
        return push(
            gains_ref.at[other],
            gains_buf.at[me],
            gains_send.at[step],
            gains_recv.at[me],
            (lax.div(other, 2), lax.rem(other, 2)),
        )

    for _, _, piece, offset in events:
        maybe(offset_exists(offset, z), core_copy(piece, offset).start)

    def gains_start(step, carry):
        gains_copy(step).start()
        return carry

    lax.fori_loop(1, 32, gains_start, 0)

    def handle(piece, offset):
        _, result, buf, index, order, slots = pieces[piece]
        base, _ = slot_base(order)

        def go():
            chip = chip_of(offset, z, y, x)
            block = buf.at[index, chip]
            arrived(block, core_recv.at[piece, chip], sibling)
            sure, unsure = [], []
            for direction in onward(order, offset):
                local, _ = slot_index(order, direction, offset, z, y, x)
                place = base[direction] + local
                (sure if direction in "xy" else unsure).append((direction, place))
            terms = [block, own_rows(piece, chip, core)]
            for direction, place in sure:
                arrived(slots.at[place], tree_recv.at[piece, place], sibling)
                terms.append(slots.at[place])
            last = hops(offset) == 0
            target = result.at[index] if last else block
            add_into(target, terms)
            for direction, place in unsure:

                def more(place=place):
                    arrived(slots.at[place], tree_recv.at[piece, place], sibling)
                    add_into(target, [target, slots.at[place]])

                maybe(direction_exists(direction, z), more)
            if not last:
                tree_copy(piece, offset).start()

        maybe(offset_exists(offset, z), go)

    for _, _, piece, offset in events:
        handle(piece, offset)

    gains_sum[...] = gains_ref[me]

    def gains_wait(step, carry):
        other = lax.rem(me + step, 32)
        gains_copy(step).wait_send()
        arrived(gains_buf.at[other], gains_recv.at[other], sibling)
        gains_sum[...] += gains_buf[other]
        return carry

    lax.fori_loop(1, 32, gains_wait, 0)
    for _, _, piece, offset in events:

        def finish(piece=piece, offset=offset):
            core_copy(piece, offset).wait_send()
            if hops(offset) > 0:
                tree_copy(piece, offset).wait_send()

        maybe(offset_exists(offset, z), finish)


def scatter_attn(gain_parts, qkv_grad, out_grad):
    sets, rows, qkv_width = qkv_grad.shape
    out_width = out_grad.shape[2]
    height = rows // 32
    dma = pltpu.SemaphoreType.DMA
    vmem = pl.BlockSpec(memory_space=pltpu.VMEM)
    places = [slot_base(order)[1] for order in ORDERS]
    return pl.pallas_call(
        scatter_attn_kernel,
        out_shape=(
            jax.ShapeDtypeStruct(gain_parts.shape[1:], F32),
            jax.ShapeDtypeStruct((sets, height, qkv_width), F32),
            jax.ShapeDtypeStruct((sets, height, out_width), F32),
        ),
        in_specs=[vmem] * 3,
        out_specs=(vmem,) * 3,
        scratch_shapes=[
            pltpu.VMEM((sets, 16, height, qkv_width), BF16),
            pltpu.VMEM((sets, 16, height, out_width), BF16),
            pltpu.VMEM((places[0], height, qkv_width), BF16),
            pltpu.VMEM((places[1], height, qkv_width), BF16),
            pltpu.VMEM((places[2], height, out_width), BF16),
            pltpu.VMEM((places[3], height, out_width), BF16),
            pltpu.VMEM((32,) + gain_parts.shape[1:], F32),
            dma((4, 16)),
            dma((4, 16)),
            dma((4, 16)),
            dma((4, max(places))),
            dma((32,)),
            dma((32,)),
        ],
        compiler_params=pltpu.CompilerParams(
            collective_id=3, has_side_effects=True, vmem_limit_bytes=60 * 2**20
        ),
        name="scatter_attn",
    )(gain_parts, qkv_grad, out_grad)


def row_loop(height, chunk, body):
    def one(step, carry):
        body(pl.ds(pl.multiple_of(step * chunk, chunk), chunk))
        return carry

    lax.fori_loop(0, height // chunk, one, 0)


def tile_loop(width, tile, body):
    def one(step, carry):
        body(pl.ds(pl.multiple_of(step * tile, tile), tile))
        return carry

    lax.fori_loop(0, width // tile, one, 0)


def make_spread(spread):
    height, width = spread.shape
    head = lax.broadcasted_iota(jnp.int32, (height, width), 0) // HEAD_DIM
    spread[...] = jnp.where(
        head == lax.broadcasted_iota(jnp.int32, (height, width), 1), 1.0, 0.0
    ).astype(BF16)


def pairs_of(positions):
    return [(p, q) for p in range(positions) for q in range(p + 1)]


def split_product(product):
    high = product.astype(BF16)
    return high, (product - high.astype(F32)).astype(BF16)


def sums_over_heads(halves, spread, index, height):
    return jnp.dot(
        halves[2 * index], spread[...], preferred_element_type=F32
    ) + jnp.dot(halves[2 * index + 1], spread[...], preferred_element_type=F32)


def to_heads(values, spread):
    return lax.dot_general(
        values, spread[...], (((1,), (1,)), ((), ())), preferred_element_type=F32
    ).astype(BF16)


def attention_probs(qkv, halves, spread, model):
    positions, height, _ = qkv.shape
    scale = 1.0 / math.sqrt(HEAD_DIM)
    pairs = pairs_of(positions)

    def products(rows):
        for index, (p, q) in enumerate(pairs):
            product = qkv[p, rows, :model].astype(F32) * qkv[q, rows, model : 2 * model].astype(F32)
            halves[2 * index, rows, :], halves[2 * index + 1, rows, :] = split_product(product)

    row_loop(height, 16, products)
    scores = [sums_over_heads(halves, spread, index, height) * scale for index in range(len(pairs))]
    probs = []
    for p in range(positions):
        own = [scores[index] for index, pair in enumerate(pairs) if pair[0] == p]
        top = functools.reduce(jnp.maximum, own)
        powers = [jnp.exp(score - top) for score in own]
        total = functools.reduce(jnp.add, powers)
        probs.extend([power / total for power in powers])
    return probs


def forward_kernel(
    gains_ref,
    tokens_ref,
    qkv_ref,
    out_ref,
    gate_up_ref,
    down_ref,
    grads_ref,
    gain_rows,
    qkv_rows,
    context,
    resid_mid,
    qkv_full,
    out_full,
    gate_up_full,
    down_full,
    rows_full,
    grads_full,
    qkv_buf,
    out_buf,
    gains_all,
    attn_in,
    ff_in,
    halves,
    spread,
    plane_sem,
    sibling_sem,
    send_sem,
    gains_send,
    gains_recv,
    rank_send,
    rank_recv,
    far_send,
    far_recv,
    across_send,
    across_recv,
    act_send,
    act_recv,
    local_sem,
    keep_sem,
):
    z, y, x, core = here()
    me = 2 * (z * 4 + y * 2 + x) + core
    zh, zl, member, rank, device, far, across = group_place(z, y, x, core)
    own_step = (0, 0, 0)
    positions, act_height, model = tokens_ref.shape
    height = gate_up_ref.shape[2]
    down_height = down_ref.shape[1]
    sibling = neighbour("s", z, y, x, core)
    greet_all(z, y, x, core)
    pieces = [
        (qkv_ref, qkv_buf, 0, "zxy"),
        (qkv_ref, qkv_buf, 1, "zyx"),
        (out_ref, out_buf, 0, "xyz"),
        (out_ref, out_buf, 1, "yxz"),
    ]

    def piece_rows(piece, number):
        _, full, index, _ = pieces[piece]
        return full.at[index, pl.ds(pl.multiple_of(number * height, height), height), :]

    def tree_send(piece, offset, direction):
        source, _, index, _ = pieces[piece]
        chip = chip_of(offset, z, y, x)
        block = piece_rows(piece, 2 * chip + core)
        recv = sibling_sem if direction == "s" else plane_sem
        return push(
            source.at[index] if hops(offset) == 0 else block,
            block,
            send_sem.at[piece, chip, DIRECTIONS.index(direction)],
            recv.at[piece, chip],
            neighbour(direction, z, y, x, core),
        )

    def tree_step(piece, offset, finish=False):
        order = pieces[piece][3]

        def go():
            chip = chip_of(offset, z, y, x)
            if hops(offset) > 0 and not finish:
                arrived(piece_rows(piece, 2 * chip + core), plane_sem.at[piece, chip], sibling)
            for direction in onward(order, offset) + ["s"]:
                copy = tree_send(piece, offset, direction)
                maybe(direction_exists(direction, z), copy.wait_send if finish else copy.start)

        maybe(offset_exists(offset, z), go)

    events = sorted(
        ((hops(offset), place, piece, offset) for piece in range(4) for place, offset in enumerate(OFFSETS)),
        key=lambda event: event[:3],
    )

    def tree_steps(distance):
        for hop, _, piece, offset in events:
            if hop == distance:
                tree_step(piece, offset)

    def gains_copy(step):
        other = lax.rem(me + step, 32)
        return push(
            gains_ref,
            gains_all.at[me],
            gains_send.at[step],
            gains_recv.at[me],
            (lax.div(other, 2), lax.rem(other, 2)),
        )

    def gains_start(step, carry):
        gains_copy(step).start()
        return carry

    def gains_wait(step, carry):
        other = lax.rem(me + step, 32)
        gains_copy(step).wait_send()
        arrived(gains_all.at[other], gains_recv.at[other], sibling)
        return carry

    sends = []

    def start(copy):
        copy.start()
        sends.append(copy)

    def weight_rows(number):
        return gate_up_full.at[:, pl.ds(pl.multiple_of(number * height, height), height), :]

    def down_rows(dzh, dy):
        number = 2 * flip(zh, dzh) + flip(y, dy)
        return down_full.at[:, pl.ds(pl.multiple_of(number * down_height, down_height), down_height), :]

    def act_rows(which, step):
        full = (rows_full, grads_full)[which]
        return full.at[:, pl.ds(pl.multiple_of(rank(step) * act_height, act_height), act_height), :]

    def send_act(which, step, source, hop):
        landed = tuple(bit ^ (1 if axis == hop else 0) for axis, bit in enumerate(step))
        start(
            push(
                source,
                act_rows(which, step),
                act_send.at[which, 4 * step[0] + 2 * step[1] + step[2], hop],
                act_recv.at[which, 4 * landed[0] + 2 * landed[1] + landed[2]],
                member(tuple(1 if axis == hop else 0 for axis in range(3))),
            )
        )

    def wait_act(which, step):
        arrived(
            act_rows(which, step), act_recv.at[which, 4 * step[0] + 2 * step[1] + step[2]], sibling
        )

    def act_own(which, source):
        for hop in (0, 1, 2):
            send_act(which, own_step, source, hop)

    def act_from_z(which):
        step = (1, 0, 0)
        wait_act(which, step)
        send_act(which, step, act_rows(which, step), 1)
        send_act(which, step, act_rows(which, step), 2)

    def act_from_x(which):
        for step in ((0, 1, 0), (1, 1, 0)):
            wait_act(which, step)
            send_act(which, step, act_rows(which, step), 2)

    def act_from_core(which):
        for step in ((0, 0, 1), (1, 0, 1), (0, 1, 1), (1, 1, 1)):
            wait_act(which, step)

    mine = gate_up_ref.at[rank(own_step)]

    def ff_own():
        for slot, step in enumerate(RANK_STEPS):
            if step != own_step:
                start(
                    push(
                        gate_up_ref.at[rank(step)],
                        weight_rows(device(own_step)),
                        rank_send.at[slot],
                        rank_recv.at[slot],
                        member(step),
                    )
                )
        start(push(mine, weight_rows(device(own_step)), far_send.at[0], far_recv.at[0], far))
        start(push(down_ref, down_rows(0, 0), far_send.at[8], far_recv.at[8], far))
        start(push(mine, weight_rows(device(own_step)), across_send.at[0, 0], across_recv.at[0, 0], across))
        start(push(down_ref, down_rows(0, 0), across_send.at[0, 8], across_recv.at[0, 8], across))

    def ff_from_rank(slots):
        for slot in slots:
            step = RANK_STEPS[slot]
            block = weight_rows(device(step))
            arrived(block, rank_recv.at[slot], sibling)
            start(push(block, block, far_send.at[slot], far_recv.at[slot], far))
            start(push(block, block, across_send.at[0, slot], across_recv.at[0, slot], across))

    def ff_from_far(slots):
        for slot in slots:
            block = down_rows(1, 0) if slot == 8 else weight_rows(device(RANK_STEPS[slot], 1, 0))
            arrived(block, far_recv.at[slot], sibling)
            start(push(block, block, across_send.at[1, slot], across_recv.at[1, slot], across))

    tree_steps(0)
    lax.fori_loop(1, 32, gains_start, 0)
    ff_own()
    act_own(1, grads_ref)
    local = [
        pltpu.make_async_copy(source.at[index], piece_rows(piece, me), local_sem.at[piece])
        for piece, (source, _, index, _) in enumerate(pieces)
    ]
    local.append(pltpu.make_async_copy(gains_ref, gains_all.at[me], local_sem.at[4]))
    local.append(pltpu.make_async_copy(mine, weight_rows(device(own_step)), local_sem.at[5]))
    local.append(pltpu.make_async_copy(down_ref, down_rows(0, 0), local_sem.at[6]))
    local.append(pltpu.make_async_copy(grads_ref, act_rows(1, own_step), local_sem.at[7]))
    for copy in local:
        copy.start()
    make_spread(spread)
    tree_steps(1)
    ff_from_rank((1, 2, 3, 4))
    lax.fori_loop(1, 32, gains_wait, 0)
    local[4].wait()
    for block in range(8):
        total = gains_all[4 * block].astype(F32)
        for part in range(1, 4):
            total = total + gains_all[4 * block + part].astype(F32)
        gain_rows[:, 128 * block : 128 * block + 128] = total

    def first_norm(rows):
        for p in range(positions):
            values = tokens_ref[p, rows, :].astype(F32)
            r, _ = normed(values)
            attn_in[p, rows, :] = (r * gain_rows[p : p + 1, :]).astype(BF16)

    row_loop(act_height, 16, first_norm)
    tree_steps(2)
    ff_from_rank((5, 6, 7))
    act_from_z(1)
    tree_steps(3)
    ff_from_far((0, 8, 1, 2))
    tree_steps(4)
    ff_from_far((3, 4, 5))
    act_from_x(1)
    tree_steps(5)
    ff_from_far((6, 7))

    def sibling_wait(chip, carry):
        for piece in range(4):
            arrived(piece_rows(piece, 2 * chip + 1 - core), sibling_sem.at[piece, chip], sibling)
        return carry

    lax.fori_loop(0, 16, sibling_wait, 0)
    for piece in range(4):
        local[piece].wait()
    keep = [
        pltpu.make_async_copy(qkv_buf, qkv_full, keep_sem.at[0]),
        pltpu.make_async_copy(out_buf, out_full, keep_sem.at[1]),
    ]
    for copy in keep:
        copy.start()

    for p in range(positions):

        def project(columns, p=p):
            qkv_rows[p, :, columns] = jnp.dot(
                attn_in[p], qkv_buf[p, :, columns], preferred_element_type=F32
            ).astype(BF16)

        tile_loop(3 * model, 512, project)
    pairs = pairs_of(positions)
    probs = attention_probs(qkv_rows, halves, spread, model)
    for index in range(len(pairs)):
        halves[2 * index] = to_heads(probs[index].astype(BF16), spread)

    def mix(rows):
        for p in range(positions):
            total = None
            for index, (own, q) in enumerate(pairs):
                if own == p:
                    term = halves[2 * index, rows, :].astype(F32) * qkv_rows[
                        q, rows, 2 * model :
                    ].astype(F32)
                    total = term if total is None else total + term
            context[p, rows, :] = total.astype(BF16)

    row_loop(act_height, 16, mix)
    for p in range(positions):

        def attend(columns, p=p):
            resid_mid[p, :, columns] = tokens_ref[p, :, columns].astype(F32) + jnp.dot(
                context[p], out_buf[p, :, columns], preferred_element_type=F32
            )

        tile_loop(model, 512, attend)

    def second_norm(rows):
        for p in range(positions):
            r, _ = normed(resid_mid[p, rows, :])
            ff_in[p, rows, :] = (r * gain_rows[positions + p : positions + p + 1, :]).astype(BF16)

    row_loop(act_height, 16, second_norm)
    act_own(0, ff_in)
    own_rows = pltpu.make_async_copy(ff_in, act_rows(0, own_step), local_sem.at[8])
    own_rows.start()
    act_from_z(0)
    act_from_x(0)
    act_from_core(1)
    for dzh in (0, 1):
        for slot, step in enumerate(RANK_STEPS):
            arrived(weight_rows(device(step, dzh, 1)), across_recv.at[dzh, slot], sibling)
        arrived(down_rows(dzh, 1), across_recv.at[dzh, 8], sibling)
    for _, _, piece, offset in events:
        tree_step(piece, offset, finish=True)
    act_from_core(0)
    for copy in sends:
        copy.wait_send()
    for copy in local[5:] + keep + [own_rows]:
        copy.wait()


def forward_gather(gains, tokens, w_qkv, w_out, gate_up_parts, w_down, grads):
    positions, act_height, model = tokens.shape
    _, height, qkv_width = w_qkv.shape
    ranks, _, _, width = gate_up_parts.shape
    dma = pltpu.SemaphoreType.DMA
    vmem = pl.BlockSpec(memory_space=pltpu.VMEM)
    anywhere = pl.BlockSpec(memory_space=pl.ANY)
    pair_count = len(pairs_of(positions))
    return pl.pallas_call(
        forward_kernel,
        out_shape=(
            jax.ShapeDtypeStruct((16, model), F32),
            jax.ShapeDtypeStruct((positions, act_height, 3 * model), BF16),
            jax.ShapeDtypeStruct((positions, act_height, model), BF16),
            jax.ShapeDtypeStruct((positions, act_height, model), F32),
            jax.ShapeDtypeStruct((positions, model, qkv_width), BF16),
            jax.ShapeDtypeStruct((positions, model, model), BF16),
            jax.ShapeDtypeStruct((positions, model, width), BF16),
            jax.ShapeDtypeStruct((positions, 4 * w_down.shape[1], model), BF16),
            jax.ShapeDtypeStruct((positions, ranks * act_height, model), BF16),
            jax.ShapeDtypeStruct((positions, ranks * act_height, model), BF16),
        ),
        in_specs=[anywhere, vmem] + [anywhere] * 5,
        out_specs=(vmem,) * 4 + (anywhere,) * 6,
        scratch_shapes=[
            pltpu.VMEM((positions, model, qkv_width), BF16),
            pltpu.VMEM((positions, model, model), BF16),
            pltpu.VMEM((32, 16, 128), BF16),
            pltpu.VMEM((positions, act_height, model), BF16),
            pltpu.VMEM((positions, act_height, model), BF16),
            pltpu.VMEM((2 * pair_count, act_height, model), BF16),
            pltpu.VMEM((model, 128), BF16),
            dma((4, 16)),
            dma((4, 16)),
            dma((4, 16, 5)),
            dma((32,)),
            dma((32,)),
            dma((8,)),
            dma((8,)),
            dma((9,)),
            dma((9,)),
            dma((2, 9)),
            dma((2, 9)),
            dma((2, 8, 3)),
            dma((2, 8)),
            dma((9,)),
            dma((2,)),
        ],
        compiler_params=pltpu.CompilerParams(
            collective_id=4, has_side_effects=True, vmem_limit_bytes=56 * 2**20
        ),
        name="forward_gather",
    )(gains, tokens, w_qkv, w_out, gate_up_parts, w_down, grads)


def by_set(activations, weight):
    return jnp.einsum("sfk,ske->sfe", activations, weight, preferred_element_type=F32)


def by_set_back(gradients, weight):
    return jnp.einsum("sfe,ske->sfk", gradients, weight, preferred_element_type=F32)


def set_grad(activations, gradients):
    return jnp.einsum("sfk,sfe->ske", activations, gradients, preferred_element_type=F32)


def head_sums(product, spread):
    high = product.astype(BF16)
    low = (product - high.astype(F32)).astype(BF16)
    sums = jnp.dot(high, spread, preferred_element_type=F32)
    return sums + jnp.dot(low, spread, preferred_element_type=F32)


def over_heads(values, spread):
    return lax.dot_general(
        values, spread, (((1,), (1,)), ((), ())), preferred_element_type=F32
    )


def local_fast(
    tokens,
    norm_attn,
    w_qkv,
    w_out,
    norm_ff,
    w_gate_up,
    w_down,
    cotangent,
    valid_frames,
    item_lengths,
):
    frame_count, positions, model = tokens.shape
    head_count = model // HEAD_DIM
    ff_units = w_gate_up.shape[2] // 2
    score_scale = 1.0 / math.sqrt(HEAD_DIM)
    own_gain = norm_attn.shape[1]
    spread = (
        jnp.arange(model)[:, None] // HEAD_DIM == jnp.arange(128)[None, :]
    ).astype(BF16)

    device_index = lax.axis_index(("dp", "pair"))
    local_ids = jnp.arange(frame_count, dtype=jnp.int32)
    frame_ids = device_index * frame_count + local_ids
    item_ends = jnp.cumsum(item_lengths)
    item_starts = item_ends - item_lengths
    in_item = (frame_ids[:, None] >= item_starts[None, :]) & (
        frame_ids[:, None] < item_ends[None, :]
    )
    item_share = 8 * frame_count / item_lengths.astype(F32)
    frame_weight = jnp.sum(jnp.where(in_item, item_share[None, :], 0.0), axis=1)
    frame_weight = jnp.where(local_ids < valid_frames[0], frame_weight, 0.0)
    grad_out = jnp.swapaxes(cotangent, 0, 1).astype(F32) * frame_weight[None, :, None]
    grad_low = grad_out.astype(BF16)

    unit_gains = jnp.concatenate([norm_attn, norm_ff], axis=0)
    lanes = jnp.arange(128, dtype=jnp.int32) // own_gain
    gains = jnp.where(lanes == lax.rem(device_index, 128 // own_gain), jnp.tile(unit_gains, (1, 128 // own_gain)), 0)
    gains = jnp.pad(gains, ((0, 16 - 2 * positions), (0, 0)))

    unit = w_down.shape[1]
    parts = w_gate_up.reshape(positions, -1, 2, 2, 2, 2, 2, 2, unit)
    parts = parts.transpose(4, 6, 7, 0, 1, 2, 3, 5, 8)
    parts = parts.reshape(8, positions, w_gate_up.shape[1], 8 * unit)
    tokens_low = jnp.swapaxes(tokens, 0, 1)
    (
        gains_rows,
        qkv,
        context,
        resid_mid,
        qkv_full,
        out_full,
        gate_up_full,
        down_full,
        ff_rows,
        grad_rows,
    ) = forward_gather(gains, tokens_low, w_qkv, w_out, parts, w_down, grad_low)
    gain_one = gains_rows[:positions, None, :]
    gain_two = gains_rows[positions : 2 * positions, None, :]
    normed_one, inverse_one = normed(tokens_low.astype(F32))
    attn_in = (normed_one * gain_one).astype(BF16)
    normed_two, inverse_two = normed(resid_mid)
    queries = [qkv[p, :, :model].astype(F32) for p in range(positions)]
    keys = [qkv[p, :, model : 2 * model].astype(F32) for p in range(positions)]
    values = [qkv[p, :, 2 * model :].astype(F32) for p in range(positions)]
    probs = []
    for p in range(positions):
        scores = [head_sums(queries[p] * keys[q], spread) * score_scale for q in range(p + 1)]
        top = functools.reduce(jnp.maximum, scores)
        powers = [jnp.exp(score - top) for score in scores]
        total = functools.reduce(jnp.add, powers)
        probs.append([power / total for power in powers])

    split = 4 * unit
    gate_up = by_set(ff_rows, gate_up_full)
    gate, up = gate_up[..., :split], gate_up[..., split:]
    sigmoid_gate = jax.nn.sigmoid(gate)
    silu_gate = gate * sigmoid_gate
    hidden = (silu_gate * up).astype(BF16)
    out_part = by_set(hidden, down_full).astype(BF16)
    d_hidden = by_set_back(grad_rows, down_full)
    d_gate = d_hidden * up * sigmoid_gate * (1.0 + gate * (1.0 - sigmoid_gate))
    d_up = d_hidden * silu_gate
    d_gate_up = jnp.concatenate([d_gate, d_up], axis=-1).astype(BF16)
    down_grad = set_grad(hidden, grad_rows).astype(BF16)
    gate_up_grad = set_grad(ff_rows, d_gate_up).astype(BF16)
    back_part = by_set_back(d_gate_up, gate_up_full).astype(BF16)
    out_sum, d_ff_in, gate_up_sum, down_sum = scatter_ff(
        out_part, back_part, gate_up_grad, down_grad
    )
    output = jnp.swapaxes((resid_mid + out_sum).astype(BF16), 0, 1)
    share_gate_up = gate_up_sum.reshape(2, 2, 2, positions, -1, 2, 2, 2, unit)
    share_gate_up = share_gate_up.transpose(3, 4, 5, 6, 0, 7, 1, 2, 8)
    share_gate_up = share_gate_up.reshape(w_gate_up.shape)

    grad_norm_ff = jnp.sum(normed_two * d_ff_in, axis=1)
    d_mid = grad_out + norm_back(normed_two, inverse_two, d_ff_in * gain_two)
    d_mid_low = d_mid.astype(BF16)
    out_grad = set_grad(context, d_mid_low).astype(BF16)
    d_context = by_set_back(d_mid_low, out_full).astype(BF16).astype(F32)
    d_queries = []
    d_keys = [0.0] * positions
    d_values = [0.0] * positions
    for p in range(positions):
        d_probs = [head_sums(d_context[p] * values[q], spread) for q in range(p + 1)]
        mean = functools.reduce(jnp.add, [prob * d for prob, d in zip(probs[p], d_probs)])
        d_query = 0.0
        for q in range(p + 1):
            d_score = (probs[p][q] * (d_probs[q] - mean)).astype(BF16)
            d_score = over_heads(d_score, spread)
            d_values[q] += over_heads(probs[p][q].astype(BF16), spread) * d_context[p]
            d_query += d_score * keys[q]
            d_keys[q] += d_score * queries[p]
        d_queries.append(d_query)
    d_qkv = jnp.stack(
        [
            jnp.concatenate(
                [d_queries[p] * score_scale, d_keys[p] * score_scale, d_values[p]], axis=-1
            )
            for p in range(positions)
        ]
    ).astype(BF16)
    qkv_grad = set_grad(attn_in, d_qkv).astype(BF16)
    d_attn_in = by_set_back(d_qkv, qkv_full)
    grad_norm_attn = jnp.sum(normed_one * d_attn_in, axis=1)
    grad_tokens = d_mid + norm_back(normed_one, inverse_one, d_attn_in * gain_one)
    grad_tokens = jnp.swapaxes(grad_tokens, 0, 1)
    gain_grads = jnp.concatenate([grad_norm_attn, grad_norm_ff], axis=0)
    gain_grads = jnp.swapaxes(gain_grads.reshape(2 * positions, 32, own_gain), 0, 1)
    gain_parts = jnp.zeros((32, 8, 128), F32).at[:, : 2 * positions, :own_gain].set(gain_grads)
    gains_sum, share_qkv, share_out = scatter_attn(gain_parts, qkv_grad, out_grad)
    return (
        output,
        grad_tokens,
        gains_sum[:positions, :own_gain],
        share_qkv,
        share_out,
        gains_sum[positions : 2 * positions, :own_gain],
        share_gate_up,
        down_sum,
    )


def solution(mesh):
    in_specs = (
        P(("dp", "pair"), None, None),
        P(None, ("dp", "pair")),
        P(None, ("dp", "pair"), None),
        P(None, ("dp", "pair"), None),
        P(None, ("dp", "pair")),
        P(None, ("dp", "pair"), None),
        P(None, ("dp", "pair"), None),
        P(("dp", "pair"), None, None),
        P(("dp", "pair")),
        P(),
    )
    out_specs = (
        P(("dp", "pair"), None, None),
        P(("dp", "pair"), None, None),
        P(None, ("dp", "pair")),
        P(None, ("dp", "pair"), None),
        P(None, ("dp", "pair"), None),
        P(None, ("dp", "pair")),
        P(None, ("dp", "pair"), None),
        P(None, ("dp", "pair"), None),
    )
    body = local_fast if mesh.shape["dp"] == 16 and mesh.shape["pair"] == 2 else local
    return jax.shard_map(body, mesh=mesh, in_specs=in_specs, out_specs=out_specs, check_vma=False)
```

```python
import functools
import math

import jax
import jax.numpy as jnp
from jax import lax
from jax.experimental import pallas as pl
from jax.experimental.pallas import tpu as pltpu
from jax.sharding import PartitionSpec as P

HEAD_DIM = 64


def per_pos(activations, weight):
    return jnp.einsum("fgk,gke->fge", activations, weight, preferred_element_type=jnp.float32)


def per_pos_back(gradients, weight):
    return jnp.einsum("fge,gke->fgk", gradients, weight, preferred_element_type=jnp.float32)


def pos_grad(activations, gradients):
    return jnp.einsum("fgk,fge->kge", activations, gradients, preferred_element_type=jnp.float32)


def gain_grad(normed_rows, gradients):
    return jnp.transpose(jnp.sum(normed_rows * gradients, axis=0))


def back_layout(share):
    return jnp.swapaxes(share, 0, 1)


def normed(values):
    inverse = lax.rsqrt(jnp.mean(values * values, axis=-1, keepdims=True) + 1e-05)
    return (values * inverse, inverse)


def norm_back(normed_rows, inverse, gradients):
    return inverse * (
        gradients - normed_rows * jnp.mean(gradients * normed_rows, axis=-1, keepdims=True)
    )


def gather_ff_fwd(norm_ff, w_gate_up, w_down, start, group):
    return (
        lax.all_gather(norm_ff[start : start + group], ("dp", "pair"), axis=1, tiled=True),
        lax.all_gather(w_gate_up[start : start + group], ("dp", "pair"), axis=1, tiled=True),
        lax.all_gather(w_down[start : start + group], ("dp", "pair"), axis=1, tiled=True),
    )


def gather_ff_back(norm_ff, w_gate_up, w_down, start, group):
    return (
        lax.all_gather(norm_ff[start : start + group], ("dp", "pair"), axis=1, tiled=True),
        lax.all_gather(w_gate_up[start : start + group], ("dp", "pair"), axis=1, tiled=True),
        lax.all_gather(w_down[start : start + group], ("dp", "pair"), axis=1, tiled=True),
    )


def local(
    tokens,
    norm_attn,
    w_qkv,
    w_out,
    norm_ff,
    w_gate_up,
    w_down,
    cotangent,
    valid_frames,
    item_lengths,
):
    frame_count, positions, model_width = tokens.shape
    head_count = model_width // HEAD_DIM
    ff_units = w_gate_up.shape[2] // 2
    score_scale = 1.0 / math.sqrt(HEAD_DIM)
    causal = jnp.arange(positions)[:, None] >= jnp.arange(positions)[None, :]
    head_shape = (frame_count, positions, head_count, HEAD_DIM)
    group = 1
    gains_attn, qkv_full, out_full = (
        lax.all_gather(norm_attn, ("dp", "pair"), axis=1, tiled=True),
        lax.all_gather(w_qkv, ("dp", "pair"), axis=1, tiled=True),
        lax.all_gather(w_out, ("dp", "pair"), axis=1, tiled=True),
    )
    resid_in = tokens.astype(jnp.float32)
    normed_one, inverse_one = normed(resid_in)
    attn_in = (normed_one * gains_attn.astype(jnp.float32)[None]).astype(jnp.bfloat16)
    qkv_rows = per_pos(attn_in, qkv_full).astype(jnp.bfloat16)
    queries = qkv_rows[..., :model_width].reshape(head_shape)
    key_heads = qkv_rows[..., model_width : 2 * model_width].reshape(head_shape)
    value_heads = qkv_rows[..., 2 * model_width :].reshape(head_shape)
    scores = (
        jnp.einsum("fphd,fqhd->fhpq", queries, key_heads, preferred_element_type=jnp.float32)
        * score_scale
    )
    scores = jnp.where(causal, scores, -1e30)
    row_max = jnp.max(scores, axis=-1, keepdims=True)
    attn_probs = jnp.exp(scores - row_max)
    attn_probs = attn_probs / jnp.sum(attn_probs, axis=-1, keepdims=True)
    probs_low = attn_probs.astype(jnp.bfloat16)
    context = jnp.einsum(
        "fhpq,fqhd->fphd", probs_low, value_heads, preferred_element_type=jnp.float32
    )
    context = context.astype(jnp.bfloat16).reshape(frame_count, positions, model_width)
    resid_mid = resid_in + per_pos(context, out_full)
    kept_parts = []
    out_parts = []
    for start in range(0, positions, group):
        gains_ff, gate_up_full, down_full = gather_ff_fwd(norm_ff, w_gate_up, w_down, start, group)
        mid_part = resid_mid[:, start : start + group]
        normed_two, inverse_two = normed(mid_part)
        ff_in = (normed_two * gains_ff.astype(jnp.float32)[None]).astype(jnp.bfloat16)
        gate_up = per_pos(ff_in, gate_up_full)
        gate_part = gate_up[..., :ff_units]
        up_part = gate_up[..., ff_units:]
        sigmoid_gate = jax.nn.sigmoid(gate_part)
        silu_gate = gate_part * sigmoid_gate
        hidden = (silu_gate * up_part).astype(jnp.bfloat16)
        out_parts.append(mid_part + per_pos(hidden, down_full))
        kept_parts.append(
            (normed_two, inverse_two, ff_in, gate_part, up_part, sigmoid_gate, silu_gate, hidden)
        )
    output = jnp.concatenate(out_parts, axis=1).astype(jnp.bfloat16)
    device_index = lax.axis_index(("dp", "pair"))
    local_ids = jnp.arange(frame_count, dtype=jnp.int32)
    frame_ids = device_index * frame_count + local_ids
    item_ends = jnp.cumsum(item_lengths)
    item_starts = item_ends - item_lengths
    in_item = (frame_ids[:, None] >= item_starts[None, :]) & (
        frame_ids[:, None] < item_ends[None, :]
    )
    item_share = 8 * frame_count / item_lengths.astype(jnp.float32)
    frame_weight = jnp.sum(jnp.where(in_item, item_share[None, :], 0.0), axis=1)
    frame_weight = jnp.where(local_ids < valid_frames[0], frame_weight, 0.0)
    grad_out = cotangent.astype(jnp.float32) * frame_weight[:, None, None]
    mid_grads = []
    share_norm_ff_parts = []
    share_gate_up_parts = []
    share_down_parts = []
    for index, start in enumerate(range(0, positions, group)):
        normed_two, inverse_two, ff_in, gate_part, up_part, sigmoid_gate, silu_gate, hidden = (
            kept_parts[index]
        )
        gains_ff, gate_up_full, down_full = gather_ff_back(norm_ff, w_gate_up, w_down, start, group)
        grad_part = grad_out[:, start : start + group]
        grad_low = grad_part.astype(jnp.bfloat16)
        grad_down = pos_grad(hidden, grad_low)
        d_hidden = per_pos_back(grad_low, down_full)
        d_gate = d_hidden * up_part * sigmoid_gate * (1.0 + gate_part * (1.0 - sigmoid_gate))
        d_up = d_hidden * silu_gate
        d_gate_up = jnp.concatenate([d_gate, d_up], axis=-1).astype(jnp.bfloat16)
        grad_gate_up = pos_grad(ff_in, d_gate_up)
        d_ff_in = per_pos_back(d_gate_up, gate_up_full)
        grad_norm_ff = gain_grad(normed_two, d_ff_in)
        mid_grads.append(
            grad_part
            + norm_back(normed_two, inverse_two, d_ff_in * gains_ff.astype(jnp.float32)[None])
        )
        share_a, share_b, share_c = (
            lax.psum_scatter(grad_norm_ff, ("dp", "pair"), scatter_dimension=0, tiled=True),
            lax.psum_scatter(grad_gate_up, ("dp", "pair"), scatter_dimension=0, tiled=True),
            lax.psum_scatter(grad_down, ("dp", "pair"), scatter_dimension=0, tiled=True),
        )
        share_norm_ff_parts.append(jnp.transpose(share_a))
        share_gate_up_parts.append(back_layout(share_b))
        share_down_parts.append(back_layout(share_c))
    d_mid = jnp.concatenate(mid_grads, axis=1)
    gains_attn, qkv_full, out_full = (
        lax.all_gather(norm_attn, ("dp", "pair"), axis=1, tiled=True),
        lax.all_gather(w_qkv, ("dp", "pair"), axis=1, tiled=True),
        lax.all_gather(w_out, ("dp", "pair"), axis=1, tiled=True),
    )
    d_mid_low = d_mid.astype(jnp.bfloat16)
    grad_out_proj = pos_grad(context, d_mid_low)
    d_context = per_pos_back(d_mid_low, out_full).astype(jnp.bfloat16).reshape(head_shape)
    d_probs = jnp.einsum(
        "fphd,fqhd->fhpq", d_context, value_heads, preferred_element_type=jnp.float32
    )
    d_values = jnp.einsum(
        "fhpq,fphd->fqhd", probs_low, d_context, preferred_element_type=jnp.float32
    )
    d_scores = attn_probs * (d_probs - jnp.sum(attn_probs * d_probs, axis=-1, keepdims=True))
    d_scores = d_scores.astype(jnp.bfloat16)
    d_queries = (
        jnp.einsum("fhpq,fqhd->fphd", d_scores, key_heads, preferred_element_type=jnp.float32)
        * score_scale
    )
    d_keys = (
        jnp.einsum("fhpq,fphd->fqhd", d_scores, queries, preferred_element_type=jnp.float32)
        * score_scale
    )
    row_shape = (frame_count, positions, model_width)
    d_qkv = jnp.concatenate(
        [d_queries.reshape(row_shape), d_keys.reshape(row_shape), d_values.reshape(row_shape)],
        axis=-1,
    ).astype(jnp.bfloat16)
    grad_qkv = pos_grad(attn_in, d_qkv)
    d_attn_in = per_pos_back(d_qkv, qkv_full)
    grad_norm_attn = gain_grad(normed_one, d_attn_in)
    grad_tokens = d_mid + norm_back(
        normed_one, inverse_one, d_attn_in * gains_attn.astype(jnp.float32)[None]
    )
    share_norm_attn, share_qkv, share_out = (
        lax.psum_scatter(grad_norm_attn, ("dp", "pair"), scatter_dimension=0, tiled=True),
        lax.psum_scatter(grad_qkv, ("dp", "pair"), scatter_dimension=0, tiled=True),
        lax.psum_scatter(grad_out_proj, ("dp", "pair"), scatter_dimension=0, tiled=True),
    )
    share_norm_attn = jnp.transpose(share_norm_attn)
    share_qkv = back_layout(share_qkv)
    share_out = back_layout(share_out)
    share_norm_ff = jnp.concatenate(share_norm_ff_parts, axis=0)
    share_gate_up = jnp.concatenate(share_gate_up_parts, axis=0)
    share_down = jnp.concatenate(share_down_parts, axis=0)
    return (
        output,
        grad_tokens,
        share_norm_attn,
        share_qkv,
        share_out,
        share_norm_ff,
        share_gate_up,
        share_down,
    )


MESH_ID = pl.DeviceIdType.MESH
BF16 = jnp.bfloat16
F32 = jnp.float32


def here():
    dp = lax.axis_index("dp")
    core = lax.axis_index("pair")
    return lax.div(dp, 4), lax.rem(lax.div(dp, 2), 2), lax.rem(dp, 2), core


def flip(value, bit):
    return 1 - value if bit else value


def push(src, dst, send_sem, recv_sem, to):
    return pltpu.make_async_remote_copy(
        src_ref=src,
        dst_ref=dst,
        send_sem=send_sem,
        recv_sem=recv_sem,
        device_id=to,
        device_id_type=MESH_ID,
    )


def arrived(dst, recv_sem, to):
    push(dst, dst, recv_sem, recv_sem, to).wait_recv()


def greet_all(z, y, x, core):
    barrier = pltpu.get_barrier_semaphore()
    me = 2 * (z * 4 + y * 2 + x) + core

    def one(step, carry):
        other = lax.rem(me + step, 32)
        pl.semaphore_signal(
            barrier, inc=1, device_id=(lax.div(other, 2), lax.rem(other, 2)), device_id_type=MESH_ID
        )
        return carry

    lax.fori_loop(1, 32, one, 0)
    pl.semaphore_wait(barrier, 31)


def greet(peers):
    barrier = pltpu.get_barrier_semaphore()
    for to in peers:
        pl.semaphore_signal(barrier, inc=1, device_id=to, device_id_type=MESH_ID)
    pl.semaphore_wait(barrier, len(peers))


def maybe(condition, do):
    if condition is None:
        do()
    else:
        pl.when(condition)(do)


OFFSETS = [
    (dz, dy, dx) for dz in (0, -1, 1, -2, 2, -3, 3) for dy in (0, 1) for dx in (0, 1)
]
ORDERS = ("zxy", "zyx", "xyz", "yxz")


def hops(offset):
    return abs(offset[0]) + offset[1] + offset[2]


def arrival_axis(order, offset):
    part = dict(z=offset[0], y=offset[1], x=offset[2])
    last = None
    for axis in order:
        if part[axis] != 0:
            last = axis
    return last


def onward(order, offset):
    directions = []
    last = arrival_axis(order, offset)
    start = 0
    if last is not None:
        start = order.index(last) + 1
        if last == "z":
            directions.append("u" if offset[0] < 0 else "d")
    for axis in order[start:]:
        directions.extend(["u", "d"] if axis == "z" else [axis])
    return directions


def came_from(order, offset):
    last = arrival_axis(order, offset)
    if last == "z":
        return "d" if offset[0] < 0 else "u"
    return last


def offset_exists(offset, z):
    if offset[0] < 0:
        return z >= -offset[0]
    if offset[0] > 0:
        return z <= 3 - offset[0]
    return None


def direction_exists(direction, z):
    return {"u": z < 3, "d": z > 0}.get(direction)


DIRECTIONS = ("x", "y", "u", "d", "s")


def neighbour(direction, z, y, x, core):
    if direction == "x":
        return (z * 4 + y * 2 + 1 - x, core)
    if direction == "y":
        return (z * 4 + (1 - y) * 2 + x, core)
    if direction == "u":
        return (z * 4 + 4 + y * 2 + x, core)
    if direction == "d":
        return (z * 4 - 4 + y * 2 + x, core)
    return (z * 4 + y * 2 + x, 1 - core)


def chip_of(offset, z, y, x):
    return (z + offset[0]) * 4 + flip(y, offset[1]) * 2 + flip(x, offset[2])


RANK_STEPS = sorted(
    ((dl, dx, dc) for dl in (0, 1) for dx in (0, 1) for dc in (0, 1)), key=lambda step: (sum(step), step)
)


def group_place(z, y, x, core):
    zh, zl = lax.div(z, 2), lax.rem(z, 2)

    def member(step):
        return ((2 * zh + flip(zl, step[0])) * 4 + y * 2 + flip(x, step[1]), flip(core, step[2]))

    def rank(step):
        return 4 * flip(zl, step[0]) + 2 * flip(x, step[1]) + flip(core, step[2])

    def device(step, dzh=0, dy=0):
        return 16 * flip(zh, dzh) + 4 * flip(y, dy) + 8 * flip(zl, step[0]) + 2 * flip(x, step[1]) + flip(core, step[2])

    far = ((2 * (1 - zh) + zl) * 4 + y * 2 + x, core)
    across = (z * 4 + (1 - y) * 2 + x, core)
    return zh, zl, member, rank, device, far, across


def add_into(target, sources, rows=16, columns=1024):
    height, width = target.shape
    across = width // columns

    def one(step, carry):
        top = pl.multiple_of(lax.div(step, across) * rows, rows)
        left = pl.multiple_of(lax.rem(step, across) * columns, columns)
        spot = (pl.ds(top, rows), pl.ds(left, columns))
        total = sources[0][spot].astype(F32)
        for source in sources[1:]:
            total = total + source[spot].astype(F32)
        target[spot] = total.astype(target.dtype)
        return carry

    lax.fori_loop(0, (height // rows) * across, one, 0)


def row_loop(height, chunk, body):
    def one(step, carry):
        body(pl.ds(pl.multiple_of(step * chunk, chunk), chunk))
        return carry

    lax.fori_loop(0, height // chunk, one, 0)


def tile_loop(width, tile, body):
    def one(step, carry):
        body(pl.ds(pl.multiple_of(step * tile, tile), tile))
        return carry

    lax.fori_loop(0, width // tile, one, 0)


def make_spread(spread):
    height, width = spread.shape
    head = lax.broadcasted_iota(jnp.int32, (height, width), 0) // HEAD_DIM
    spread[...] = jnp.where(
        head == lax.broadcasted_iota(jnp.int32, (height, width), 1), 1.0, 0.0
    ).astype(BF16)


def pairs_of(positions):
    return [(p, q) for p in range(positions) for q in range(p + 1)]


def split_product(product):
    high = product.astype(BF16)
    return high, (product - high.astype(F32)).astype(BF16)


def sums_over_heads(halves, spread, index, height):
    return jnp.dot(
        halves[2 * index], spread[...], preferred_element_type=F32
    ) + jnp.dot(halves[2 * index + 1], spread[...], preferred_element_type=F32)


def to_heads(values, spread):
    return lax.dot_general(
        values, spread[...], (((1,), (1,)), ((), ())), preferred_element_type=F32
    ).astype(BF16)


def attention_probs(qkv, halves, spread, model):
    positions, height, _ = qkv.shape
    scale = 1.0 / math.sqrt(HEAD_DIM)
    pairs = pairs_of(positions)

    def products(rows):
        for index, (p, q) in enumerate(pairs):
            product = qkv[p, rows, :model].astype(F32) * qkv[q, rows, model : 2 * model].astype(F32)
            halves[2 * index, rows, :], halves[2 * index + 1, rows, :] = split_product(product)

    row_loop(height, 16, products)
    scores = [sums_over_heads(halves, spread, index, height) * scale for index in range(len(pairs))]
    probs = []
    for p in range(positions):
        own = [scores[index] for index, pair in enumerate(pairs) if pair[0] == p]
        top = functools.reduce(jnp.maximum, own)
        powers = [jnp.exp(score - top) for score in own]
        total = functools.reduce(jnp.add, powers)
        probs.extend([power / total for power in powers])
    return probs


def forward_kernel(
    gains_ref,
    tokens_ref,
    qkv_ref,
    out_ref,
    gate_up_ref,
    down_ref,
    grads_ref,
    gain_rows,
    qkv_rows,
    context,
    resid_mid,
    qkv_full,
    out_full,
    gate_up_full,
    down_full,
    rows_full,
    grads_full,
    qkv_buf,
    out_buf,
    gains_all,
    attn_in,
    ff_in,
    halves,
    spread,
    plane_sem,
    sibling_sem,
    send_sem,
    gains_send,
    gains_recv,
    rank_send,
    rank_recv,
    far_send,
    far_recv,
    across_send,
    across_recv,
    act_send,
    act_recv,
    local_sem,
    keep_sem,
):
    z, y, x, core = here()
    me = 2 * (z * 4 + y * 2 + x) + core
    zh, zl, member, rank, device, far, across = group_place(z, y, x, core)
    own_step = (0, 0, 0)
    positions, act_height, model = tokens_ref.shape
    height = gate_up_ref.shape[2]
    down_height = down_ref.shape[1]
    sibling = neighbour("s", z, y, x, core)
    greet_all(z, y, x, core)
    pieces = [
        (qkv_ref, qkv_buf, 0, "zxy"),
        (qkv_ref, qkv_buf, 1, "zyx"),
        (out_ref, out_buf, 0, "xyz"),
        (out_ref, out_buf, 1, "yxz"),
    ]

    def piece_rows(piece, number):
        _, full, index, _ = pieces[piece]
        return full.at[index, pl.ds(pl.multiple_of(number * height, height), height), :]

    def tree_send(piece, offset, direction):
        source, _, index, _ = pieces[piece]
        chip = chip_of(offset, z, y, x)
        block = piece_rows(piece, 2 * chip + core)
        recv = sibling_sem if direction == "s" else plane_sem
        return push(
            source.at[index] if hops(offset) == 0 else block,
            block,
            send_sem.at[piece, chip, DIRECTIONS.index(direction)],
            recv.at[piece, chip],
            neighbour(direction, z, y, x, core),
        )

    def tree_step(piece, offset, finish=False):
        order = pieces[piece][3]

        def go():
            chip = chip_of(offset, z, y, x)
            if hops(offset) > 0 and not finish:
                arrived(piece_rows(piece, 2 * chip + core), plane_sem.at[piece, chip], sibling)
            for direction in onward(order, offset) + ["s"]:
                copy = tree_send(piece, offset, direction)
                maybe(direction_exists(direction, z), copy.wait_send if finish else copy.start)

        maybe(offset_exists(offset, z), go)

    events = sorted(
        ((hops(offset), place, piece, offset) for piece in range(4) for place, offset in enumerate(OFFSETS)),
        key=lambda event: event[:3],
    )

    def tree_steps(distance):
        for hop, _, piece, offset in events:
            if hop == distance:
                tree_step(piece, offset)

    def gains_copy(step):
        other = lax.rem(me + step, 32)
        return push(
            gains_ref,
            gains_all.at[me],
            gains_send.at[step],
            gains_recv.at[me],
            (lax.div(other, 2), lax.rem(other, 2)),
        )

    def gains_start(step, carry):
        gains_copy(step).start()
        return carry

    def gains_wait(step, carry):
        other = lax.rem(me + step, 32)
        gains_copy(step).wait_send()
        arrived(gains_all.at[other], gains_recv.at[other], sibling)
        return carry

    sends = []

    def start(copy):
        copy.start()
        sends.append(copy)

    def weight_rows(number):
        return gate_up_full.at[:, pl.ds(pl.multiple_of(number * height, height), height), :]

    def down_rows(dzh, dy):
        number = 2 * flip(zh, dzh) + flip(y, dy)
        return down_full.at[:, pl.ds(pl.multiple_of(number * down_height, down_height), down_height), :]

    def act_rows(which, step):
        full = (rows_full, grads_full)[which]
        return full.at[:, pl.ds(pl.multiple_of(rank(step) * act_height, act_height), act_height), :]

    def send_act(which, step, source, hop):
        landed = tuple(bit ^ (1 if axis == hop else 0) for axis, bit in enumerate(step))
        start(
            push(
                source,
                act_rows(which, step),
                act_send.at[which, 4 * step[0] + 2 * step[1] + step[2], hop],
                act_recv.at[which, 4 * landed[0] + 2 * landed[1] + landed[2]],
                member(tuple(1 if axis == hop else 0 for axis in range(3))),
            )
        )

    def wait_act(which, step):
        arrived(
            act_rows(which, step), act_recv.at[which, 4 * step[0] + 2 * step[1] + step[2]], sibling
        )

    def act_own(which, source):
        for hop in (0, 1, 2):
            send_act(which, own_step, source, hop)

    def act_from_z(which):
        step = (1, 0, 0)
        wait_act(which, step)
        send_act(which, step, act_rows(which, step), 1)
        send_act(which, step, act_rows(which, step), 2)

    def act_from_x(which):
        for step in ((0, 1, 0), (1, 1, 0)):
            wait_act(which, step)
            send_act(which, step, act_rows(which, step), 2)

    def act_from_core(which):
        for step in ((0, 0, 1), (1, 0, 1), (0, 1, 1), (1, 1, 1)):
            wait_act(which, step)

    mine = gate_up_ref.at[rank(own_step)]

    def ff_own():
        for slot, step in enumerate(RANK_STEPS):
            if step != own_step:
                start(
                    push(
                        gate_up_ref.at[rank(step)],
                        weight_rows(device(own_step)),
                        rank_send.at[slot],
                        rank_recv.at[slot],
                        member(step),
                    )
                )
        start(push(mine, weight_rows(device(own_step)), far_send.at[0], far_recv.at[0], far))
        start(push(down_ref, down_rows(0, 0), far_send.at[8], far_recv.at[8], far))
        start(push(mine, weight_rows(device(own_step)), across_send.at[0, 0], across_recv.at[0, 0], across))
        start(push(down_ref, down_rows(0, 0), across_send.at[0, 8], across_recv.at[0, 8], across))

    def ff_from_rank(slots):
        for slot in slots:
            step = RANK_STEPS[slot]
            block = weight_rows(device(step))
            arrived(block, rank_recv.at[slot], sibling)
            start(push(block, block, far_send.at[slot], far_recv.at[slot], far))
            start(push(block, block, across_send.at[0, slot], across_recv.at[0, slot], across))

    def ff_from_far(slots):
        for slot in slots:
            block = down_rows(1, 0) if slot == 8 else weight_rows(device(RANK_STEPS[slot], 1, 0))
            arrived(block, far_recv.at[slot], sibling)
            start(push(block, block, across_send.at[1, slot], across_recv.at[1, slot], across))

    tree_steps(0)
    lax.fori_loop(1, 32, gains_start, 0)
    ff_own()
    act_own(1, grads_ref)
    local = [
        pltpu.make_async_copy(source.at[index], piece_rows(piece, me), local_sem.at[piece])
        for piece, (source, _, index, _) in enumerate(pieces)
    ]
    local.append(pltpu.make_async_copy(gains_ref, gains_all.at[me], local_sem.at[4]))
    local.append(pltpu.make_async_copy(mine, weight_rows(device(own_step)), local_sem.at[5]))
    local.append(pltpu.make_async_copy(down_ref, down_rows(0, 0), local_sem.at[6]))
    local.append(pltpu.make_async_copy(grads_ref, act_rows(1, own_step), local_sem.at[7]))
    for copy in local:
        copy.start()
    make_spread(spread)
    tree_steps(1)
    ff_from_rank((1, 2, 3, 4))
    lax.fori_loop(1, 32, gains_wait, 0)
    local[4].wait()
    for block in range(8):
        total = gains_all[4 * block].astype(F32)
        for part in range(1, 4):
            total = total + gains_all[4 * block + part].astype(F32)
        gain_rows[:, 128 * block : 128 * block + 128] = total

    def first_norm(rows):
        for p in range(positions):
            values = tokens_ref[p, rows, :].astype(F32)
            r, _ = normed(values)
            attn_in[p, rows, :] = (r * gain_rows[p : p + 1, :]).astype(BF16)

    row_loop(act_height, 16, first_norm)
    tree_steps(2)
    ff_from_rank((5, 6, 7))
    act_from_z(1)
    tree_steps(3)
    ff_from_far((0, 8, 1, 2))
    tree_steps(4)
    ff_from_far((3, 4, 5))
    act_from_x(1)
    tree_steps(5)
    ff_from_far((6, 7))

    def sibling_wait(chip, carry):
        for piece in range(4):
            arrived(piece_rows(piece, 2 * chip + 1 - core), sibling_sem.at[piece, chip], sibling)
        return carry

    lax.fori_loop(0, 16, sibling_wait, 0)
    for piece in range(4):
        local[piece].wait()
    keep = [
        pltpu.make_async_copy(qkv_buf, qkv_full, keep_sem.at[0]),
        pltpu.make_async_copy(out_buf, out_full, keep_sem.at[1]),
    ]
    for copy in keep:
        copy.start()

    for p in range(positions):

        def project(columns, p=p):
            qkv_rows[p, :, columns] = jnp.dot(
                attn_in[p], qkv_buf[p, :, columns], preferred_element_type=F32
            ).astype(BF16)

        tile_loop(3 * model, 512, project)
    pairs = pairs_of(positions)
    probs = attention_probs(qkv_rows, halves, spread, model)
    for index in range(len(pairs)):
        halves[2 * index] = to_heads(probs[index].astype(BF16), spread)

    def mix(rows):
        for p in range(positions):
            total = None
            for index, (own, q) in enumerate(pairs):
                if own == p:
                    term = halves[2 * index, rows, :].astype(F32) * qkv_rows[
                        q, rows, 2 * model :
                    ].astype(F32)
                    total = term if total is None else total + term
            context[p, rows, :] = total.astype(BF16)

    row_loop(act_height, 16, mix)
    for p in range(positions):

        def attend(columns, p=p):
            resid_mid[p, :, columns] = tokens_ref[p, :, columns].astype(F32) + jnp.dot(
                context[p], out_buf[p, :, columns], preferred_element_type=F32
            )

        tile_loop(model, 512, attend)

    def second_norm(rows):
        for p in range(positions):
            r, _ = normed(resid_mid[p, rows, :])
            ff_in[p, rows, :] = (r * gain_rows[positions + p : positions + p + 1, :]).astype(BF16)

    row_loop(act_height, 16, second_norm)
    act_own(0, ff_in)
    own_rows = pltpu.make_async_copy(ff_in, act_rows(0, own_step), local_sem.at[8])
    own_rows.start()
    act_from_z(0)
    act_from_x(0)
    act_from_core(1)
    for dzh in (0, 1):
        for slot, step in enumerate(RANK_STEPS):
            arrived(weight_rows(device(step, dzh, 1)), across_recv.at[dzh, slot], sibling)
        arrived(down_rows(dzh, 1), across_recv.at[dzh, 8], sibling)
    for _, _, piece, offset in events:
        tree_step(piece, offset, finish=True)
    act_from_core(0)
    for copy in sends:
        copy.wait_send()
    for copy in local[5:] + keep + [own_rows]:
        copy.wait()


def forward_gather(gains, tokens, w_qkv, w_out, gate_up_parts, w_down, grads):
    positions, act_height, model = tokens.shape
    _, height, qkv_width = w_qkv.shape
    ranks, _, _, width = gate_up_parts.shape
    dma = pltpu.SemaphoreType.DMA
    vmem = pl.BlockSpec(memory_space=pltpu.VMEM)
    anywhere = pl.BlockSpec(memory_space=pl.ANY)
    pair_count = len(pairs_of(positions))
    return pl.pallas_call(
        forward_kernel,
        out_shape=(
            jax.ShapeDtypeStruct((16, model), F32),
            jax.ShapeDtypeStruct((positions, act_height, 3 * model), BF16),
            jax.ShapeDtypeStruct((positions, act_height, model), BF16),
            jax.ShapeDtypeStruct((positions, act_height, model), F32),
            jax.ShapeDtypeStruct((positions, model, qkv_width), BF16),
            jax.ShapeDtypeStruct((positions, model, model), BF16),
            jax.ShapeDtypeStruct((positions, model, width), BF16),
            jax.ShapeDtypeStruct((positions, 4 * w_down.shape[1], model), BF16),
            jax.ShapeDtypeStruct((positions, ranks * act_height, model), BF16),
            jax.ShapeDtypeStruct((positions, ranks * act_height, model), BF16),
        ),
        in_specs=[anywhere, vmem] + [anywhere] * 5,
        out_specs=(vmem,) * 4 + (anywhere,) * 6,
        scratch_shapes=[
            pltpu.VMEM((positions, model, qkv_width), BF16),
            pltpu.VMEM((positions, model, model), BF16),
            pltpu.VMEM((32, 16, 128), BF16),
            pltpu.VMEM((positions, act_height, model), BF16),
            pltpu.VMEM((positions, act_height, model), BF16),
            pltpu.VMEM((2 * pair_count, act_height, model), BF16),
            pltpu.VMEM((model, 128), BF16),
            dma((4, 16)),
            dma((4, 16)),
            dma((4, 16, 5)),
            dma((32,)),
            dma((32,)),
            dma((8,)),
            dma((8,)),
            dma((9,)),
            dma((9,)),
            dma((2, 9)),
            dma((2, 9)),
            dma((2, 8, 3)),
            dma((2, 8)),
            dma((9,)),
            dma((2,)),
        ],
        compiler_params=pltpu.CompilerParams(
            collective_id=4, has_side_effects=True, vmem_limit_bytes=56 * 2**20
        ),
        name="forward_gather",
    )(gains, tokens, w_qkv, w_out, gate_up_parts, w_down, grads)


def slot_index(order, direction, offset, z, y, x):
    axis = {"u": "z", "d": "z"}.get(direction, direction)
    index, count = 0, 1
    values = dict(z=z + offset[0], y=flip(y, offset[1]), x=flip(x, offset[2]))
    sizes = dict(z=4, y=2, x=2)
    for earlier in order[: order.index(axis)]:
        index = index * sizes[earlier] + values[earlier]
        count *= sizes[earlier]
    if axis == "z":
        index = index * 5 + (4 if direction == "d" and offset[0] == 0 else values["z"])
        count *= 5
    return index, count


def slot_base(order):
    base, total = {}, 0
    for axis, direction in (("x", "x"), ("y", "y"), ("z", "u")):
        base[axis] = total
        total += slot_index(order, direction, (0, 0, 0), 0, 0, 0)[1]
    base["u"] = base["d"] = base["z"]
    return base, total


def backward_kernel(
    tokens_ref,
    cot_ref,
    gain_rows,
    qkv_rows,
    context,
    resid_mid,
    qkv_full,
    out_full,
    out_ref,
    back_ref,
    gate_up_ref,
    down_ref,
    output,
    grad_tokens,
    gains_sum,
    qkv_sum,
    attn_out_sum,
    gate_up_sum,
    down_sum,
    act_own,
    core_buf,
    x_buf,
    z_buf,
    gate_own,
    down_own,
    across_gate,
    across_down,
    far_gate,
    far_down,
    qkv_grad,
    out_grad,
    slots_0,
    slots_1,
    slots_2,
    slots_3,
    qkv_tiles,
    out_tiles,
    turned,
    attn_turned,
    context_turned,
    d_qkv,
    d_mid_low,
    d_mid,
    d_context,
    d_rows,
    halves,
    probs_buf,
    spread,
    gain_acc,
    gains_part,
    gains_buf,
    core_send,
    core_recv,
    x_send,
    x_recv,
    z_send,
    z_recv,
    across_send,
    across_recv,
    far_send,
    far_recv,
    rank_send,
    rank_recv,
    swap_send,
    swap_recv,
    tree_send,
    tree_recv,
    gains_send,
    gains_recv,
    own_sem,
    part_sem,
    tile_sem,
):
    z, y, x, core = here()
    me = 2 * (z * 4 + y * 2 + x) + core
    zh, zl, member, rank, device, far, across = group_place(z, y, x, core)
    own_step = (0, 0, 0)
    positions, act_height, model = tokens_ref.shape
    sets = positions
    height = qkv_sum.shape[1]
    down_height = down_sum.shape[1]
    half = 16 * height
    sibling = member((0, 0, 1))
    scale = 1.0 / math.sqrt(HEAD_DIM)
    pairs = pairs_of(positions)
    greet_all(z, y, x, core)
    sends = []

    def start(copy):
        copy.start()
        sends.append(copy)

    def run_rows(dzh, dy, low):
        number = 16 * flip(zh, dzh) + 4 * flip(y, dy) + 8 * low
        return pl.ds(pl.multiple_of(number * height, 4 * height), 4 * height)

    def down_rows(dzh, dy):
        number = 2 * flip(zh, dzh) + flip(y, dy)
        return pl.ds(pl.multiple_of(number * down_height, down_height), down_height)

    def ff_across(turn):
        dzh = 1 - turn
        for s in range(sets):
            for low in (0, 1):
                start(
                    push(
                        gate_up_ref.at[s, run_rows(dzh, 1, low)],
                        across_gate.at[turn, s, low],
                        across_send.at[turn, s, low],
                        across_recv.at[turn, s, low],
                        across,
                    )
                )
            start(
                push(
                    down_ref.at[s, down_rows(dzh, 1)],
                    across_down.at[turn, s],
                    across_send.at[turn, s, 2],
                    across_recv.at[turn, s, 2],
                    across,
                )
            )

    part_copies = []
    for turn in (0, 1):
        for s in range(sets):
            for low in (0, 1):
                part_copies.append(
                    pltpu.make_async_copy(
                        gate_up_ref.at[s, run_rows(1 - turn, 0, low)],
                        gate_own.at[turn, s, low],
                        part_sem.at[turn, s, low],
                    )
                )
            part_copies.append(
                pltpu.make_async_copy(
                    down_ref.at[s, down_rows(1 - turn, 0)], down_own.at[turn, s], part_sem.at[turn, s, 2]
                )
            )

    def ff_first():
        for s in range(sets):
            for low in (0, 1):
                block = across_gate.at[0, s, low]
                arrived(block, across_recv.at[0, s, low], across)
                add_into(block, [block, gate_own.at[0, s, low]])
                start(push(block, far_gate.at[s, low], far_send.at[s, low], far_recv.at[s, low], far))
            block = across_down.at[0, s]
            arrived(block, across_recv.at[0, s, 2], across)
            add_into(block, [block, down_own.at[0, s]])
            start(push(block, far_down.at[s], far_send.at[s, 2], far_recv.at[s, 2], far))

    def share(step, s):
        number = 2 * flip(x, step[1]) + flip(core, step[2])
        return across_gate.at[
            1, s, flip(zl, step[0]), pl.ds(pl.multiple_of(number * height, height), height)
        ]

    def ff_second():
        for s in range(sets):
            for low in (0, 1):
                block = across_gate.at[1, s, low]
                arrived(block, across_recv.at[1, s, low], across)
                arrived(far_gate.at[s, low], far_recv.at[s, low], far)
                add_into(block, [block, far_gate.at[s, low], gate_own.at[1, s, low]])
            for slot, step in enumerate(RANK_STEPS):
                if step != own_step:
                    start(
                        push(
                            share(step, s),
                            gate_up_sum.at[rank(own_step), s],
                            rank_send.at[slot, s],
                            rank_recv.at[slot, s],
                            member(step),
                        )
                    )
            add_into(gate_up_sum.at[rank(own_step), s], [share(own_step, s)])
            arrived(across_down.at[1, s], across_recv.at[1, s, 2], across)
            arrived(far_down.at[s], far_recv.at[s, 2], far)
            add_into(down_sum.at[s], [across_down.at[1, s], far_down.at[s], down_own.at[1, s]])

    def ff_last():
        for slot, step in enumerate(RANK_STEPS):
            for s in range(sets):
                if step != own_step:
                    arrived(gate_up_sum.at[rank(step), s], rank_recv.at[slot, s], member(step))

    acts = [back_ref, out_ref]

    def act_rows(step):
        return pl.ds(pl.multiple_of(rank(step) * act_height, act_height), act_height)

    def act_core_sends(which):
        for dl, dx in ((1, 1), (0, 1), (1, 0), (0, 0)):
            start(
                push(
                    acts[which].at[:, act_rows((dl, dx, 1))],
                    core_buf.at[which, dl, dx],
                    core_send.at[which, dl, dx],
                    core_recv.at[which, dl, dx],
                    sibling,
                )
            )

    def act_load(which):
        return [
            pltpu.make_async_copy(
                acts[which].at[:, act_rows((dl, dx, 0))], act_own.at[dl, dx], own_sem.at[which, dl, dx]
            )
            for dl in (0, 1)
            for dx in (0, 1)
        ]

    def core_add(which, dl, dx):
        block = core_buf.at[which, dl, dx]
        arrived(block, core_recv.at[which, dl, dx], sibling)
        for s in range(sets):
            add_into(block.at[s], [block.at[s], act_own.at[dl, dx, s]])

    def act_first(which):
        for dl in (1, 0):
            core_add(which, dl, 1)
            start(
                push(
                    core_buf.at[which, dl, 1],
                    x_buf.at[which, dl],
                    x_send.at[which, dl],
                    x_recv.at[which, dl],
                    member((0, 1, 0)),
                )
            )
        core_add(which, 1, 0)
        core_add(which, 0, 0)

    def act_second(which):
        arrived(x_buf.at[which, 1], x_recv.at[which, 1], member((0, 1, 0)))
        for s in range(sets):
            block = x_buf.at[which, 1, s]
            add_into(block, [block, core_buf.at[which, 1, 0, s]])
        start(
            push(
                x_buf.at[which, 1], z_buf.at[which], z_send.at[which], z_recv.at[which], member((1, 0, 0))
            )
        )

    def act_third(which):
        arrived(x_buf.at[which, 0], x_recv.at[which, 0], member((0, 1, 0)))
        arrived(z_buf.at[which], z_recv.at[which], member((1, 0, 0)))

    pieces = [
        (qkv_grad, qkv_sum, 0, "zxy", slots_0),
        (qkv_grad, qkv_sum, 1, "zyx", slots_1),
        (out_grad, attn_out_sum, 0, "xyz", slots_2),
        (out_grad, attn_out_sum, 1, "yxz", slots_3),
    ]
    events = sorted(
        ((-hops(offset), place, piece, offset) for piece in range(4) for place, offset in enumerate(OFFSETS)),
        key=lambda event: event[:3],
    )

    def tree_block(piece, offset):
        source, _, index, _, _ = pieces[piece]
        chip = chip_of(offset, z, y, x)
        return source.at[index, pl.ds(pl.multiple_of(chip * height, height), height), :]

    def tree_copy(piece, offset):
        _, _, _, order, slots = pieces[piece]
        toward = came_from(order, offset)
        base, _ = slot_base(order)
        seen = {"x": "x", "y": "y", "u": "d", "d": "u"}[toward]
        nearer = offset
        if toward == "u":
            nearer = (offset[0] - 1, offset[1], offset[2])
        if toward == "d":
            nearer = (offset[0] + 1, offset[1], offset[2])
        there = {"u": z + 1, "d": z - 1}.get(toward, z)
        index_there, _ = slot_index(
            order, seen, nearer, there, y if toward != "y" else 1 - y, x if toward != "x" else 1 - x
        )
        if toward in "xy":
            index_there, _ = slot_index(order, seen, offset, z, y, x)
        place = base[seen] + index_there
        return push(
            tree_block(piece, offset),
            slots.at[place],
            tree_send.at[piece, chip_of(offset, z, y, x)],
            tree_recv.at[piece, place],
            neighbour(toward, z, y, x, core),
        )

    def tree_step(piece, offset):
        _, result, index, order, slots = pieces[piece]
        base, _ = slot_base(order)

        def go():
            block = tree_block(piece, offset)
            sure, unsure = [], []
            for direction in onward(order, offset):
                local, _ = slot_index(order, direction, offset, z, y, x)
                place = base[direction] + local
                (sure if direction in "xy" else unsure).append((direction, place))
            terms = [block]
            for _, place in sure:
                arrived(slots.at[place], tree_recv.at[piece, place], sibling)
                terms.append(slots.at[place])
            last = hops(offset) == 0
            target = result.at[index] if last else block
            if last or len(terms) > 1:
                add_into(target, terms)
            for direction, place in unsure:

                def more(place=place):
                    arrived(slots.at[place], tree_recv.at[piece, place], sibling)
                    add_into(target, [target, slots.at[place]])

                maybe(direction_exists(direction, z), more)
            if not last:
                tree_copy(piece, offset).start()

        maybe(offset_exists(offset, z), go)

    def tree_steps(which, distances):
        for hop, _, piece, offset in events:
            if piece in which and -hop in distances:
                tree_step(piece, offset)

    def gains_copy(step):
        other = lax.rem(me + step, 32)
        return push(
            gains_part.at[lax.div(other, 4)],
            gains_buf.at[me],
            gains_send.at[step],
            gains_recv.at[me],
            (lax.div(other, 2), lax.rem(other, 2)),
        )

    def gains_start(step, carry):
        gains_copy(step).start()
        return carry

    def gains_wait(step, carry):
        other = lax.rem(me + step, 32)
        gains_copy(step).wait_send()
        arrived(gains_buf.at[other], gains_recv.at[other], sibling)
        gains_sum[...] += gains_buf[other]
        return carry

    def swap_copy(index, source, target):
        return push(source, target, swap_send.at[index], swap_recv.at[index], sibling)

    def turn(source, target, slot):
        def one(block, p):
            flat = source(p, block)
            turned[slot, p, pl.ds(2 * block, 2)] = flat.T.astype(BF16).reshape(2, 2, height, act_height)

        for p in range(positions):
            for block in range(model // 128):
                one(block, p)
            target[p, :, :, :act_height] = turned[slot, p, :, core]

    qkv_tile = qkv_tiles.shape[1]
    tile_count = model // qkv_tile

    def qkv_load(number):
        p, tile = divmod(number, tile_count)
        return pltpu.make_async_copy(
            qkv_full.at[p, pl.ds(tile * qkv_tile, qkv_tile)],
            qkv_tiles.at[number % 2],
            tile_sem.at[number % 2],
        )

    out_loads = [
        pltpu.make_async_copy(out_full.at[p], out_tiles.at[p], tile_sem.at[2 + p]) for p in range(positions)
    ]

    act_core_sends(0)
    ff_across(0)
    ff_across(1)
    load_back = act_load(0)
    for copy in load_back + out_loads + part_copies:
        copy.start()
    act_core_sends(1)
    qkv_load(0).start()
    qkv_load(1).start()
    make_spread(spread)
    gain_acc[...] = jnp.zeros_like(gain_acc)
    for copy in load_back:
        copy.wait()
    act_first(0)
    load_out = act_load(1)
    for copy in load_out:
        copy.start()

    def context_block(p, block):
        return context[p, :, 128 * block : 128 * block + 128].astype(F32)

    def attn_norm(rows):
        for p in range(positions):
            r, _ = normed(tokens_ref[p, rows, :].astype(F32))
            d_rows[p, rows, :] = r * gain_rows[p : p + 1, :]

    row_loop(act_height, 16, attn_norm)
    turn(context_block, context_turned, 0)
    turn(
        lambda p, block: d_rows[p, :, 128 * block : 128 * block + 128], attn_turned, 1
    )
    swaps = []
    for p in range(positions):
        swaps.append(
            swap_copy(
                4 * p,
                turned.at[0, p, :, 1 - core],
                context_turned.at[p, :, :, pl.ds(act_height, act_height)],
            )
        )
        swaps.append(
            swap_copy(
                4 * p + 1,
                turned.at[1, p, :, 1 - core],
                attn_turned.at[p, :, :, pl.ds(act_height, act_height)],
            )
        )
        swaps[-1].start()
        swaps[-2].start()
    act_second(0)
    for copy in part_copies:
        copy.wait()
    ff_first()
    probs = attention_probs(qkv_rows, halves, spread, model)
    for index in range(len(pairs)):
        probs_buf[index] = probs[index]
    act_third(0)

    def mid_back(rows):
        for p in range(positions):
            d_ff_in = (
                core_buf[0, 0, 0, p, rows, :].astype(F32)
                + x_buf[0, 0, p, rows, :].astype(F32)
                + z_buf[0, p, rows, :].astype(F32)
            )
            r, inverse = normed(resid_mid[p, rows, :])
            gain_acc[positions + p] += r * d_ff_in
            total = cot_ref[p, rows, :] + norm_back(
                r, inverse, d_ff_in * gain_rows[positions + p : positions + p + 1, :]
            )
            d_mid[p, rows, :] = total
            d_mid_low[p, rows, :] = total.astype(BF16)

    row_loop(act_height, 16, mid_back)
    for p in range(positions):
        swaps.append(
            swap_copy(
                4 * p + 2,
                d_mid_low.at[p, pl.ds(0, act_height)],
                d_mid_low.at[p, pl.ds(act_height, act_height)],
            )
        )
        swaps[-1].start()
    for copy in out_loads:
        copy.wait()
    for p in range(positions):

        def context_back(columns, p=p):
            d_context[p, :, columns] = lax.dot_general(
                d_mid_low[p, :act_height, :],
                out_tiles[p, columns, :],
                (((1,), (1,)), ((), ())),
                preferred_element_type=F32,
            ).astype(BF16)

        tile_loop(model, 256, context_back)

    def context_products(rows):
        for index, (p, q) in enumerate(pairs):
            product = d_context[p, rows, :].astype(F32) * qkv_rows[q, rows, 2 * model :].astype(F32)
            halves[2 * index, rows, :], halves[2 * index + 1, rows, :] = split_product(product)

    row_loop(act_height, 16, context_products)
    d_probs = [sums_over_heads(halves, spread, index, act_height) for index in range(len(pairs))]
    for p in range(positions):
        own = [index for index, pair in enumerate(pairs) if pair[0] == p]
        mean = functools.reduce(jnp.add, [probs_buf[index] * d_probs[index] for index in own])
        for index in own:
            d_score = (probs_buf[index] * (d_probs[index] - mean)).astype(BF16)
            halves[2 * index] = to_heads(d_score, spread)
            halves[2 * index + 1] = to_heads(probs_buf[index].astype(BF16), spread)

    def qkv_back(rows):
        d_keys = [None] * positions
        d_values = [None] * positions

        def plus(total, term):
            return term if total is None else total + term

        for p in range(positions):
            d_query = None
            d_own = d_context[p, rows, :].astype(F32)
            query = qkv_rows[p, rows, :model].astype(F32)
            for index, (own, q) in enumerate(pairs):
                if own == p:
                    d_score = halves[2 * index, rows, :].astype(F32)
                    key = qkv_rows[q, rows, model : 2 * model].astype(F32)
                    d_query = plus(d_query, d_score * key)
                    d_keys[q] = plus(d_keys[q], d_score * query)
                    d_values[q] = plus(d_values[q], halves[2 * index + 1, rows, :].astype(F32) * d_own)
            d_qkv[p, rows, :model] = (d_query * scale).astype(BF16)
        for p in range(positions):
            d_qkv[p, rows, model : 2 * model] = (d_keys[p] * scale).astype(BF16)
            d_qkv[p, rows, 2 * model :] = d_values[p].astype(BF16)

    row_loop(act_height, 16, qkv_back)
    for p in range(positions):
        swaps.append(
            swap_copy(
                4 * p + 3,
                d_qkv.at[p, pl.ds(0, act_height)],
                d_qkv.at[p, pl.ds(act_height, act_height)],
            )
        )
        swaps[-1].start()

    def swap_wait(index, target):
        arrived(target, swap_recv.at[index], sibling)

    for p in range(positions):
        swap_wait(4 * p, context_turned.at[p, :, :, pl.ds(act_height, act_height)])
        swap_wait(4 * p + 2, d_mid_low.at[p, pl.ds(act_height, act_height)])

        def out_weights(columns, p=p):
            out_grad[p, :, columns] = jnp.dot(
                context_turned[p].reshape(half, 2 * act_height),
                d_mid_low[p, :, columns],
                preferred_element_type=F32,
            ).astype(BF16)

        tile_loop(model, 256, out_weights)
    tree_steps((2, 3), (5,))
    for copy in load_out:
        copy.wait()
    act_first(1)
    for p in range(positions):
        swap_wait(4 * p + 1, attn_turned.at[p, :, :, pl.ds(act_height, act_height)])
        swap_wait(4 * p + 3, d_qkv.at[p, pl.ds(act_height, act_height)])

        def qkv_weights(columns, p=p):
            qkv_grad[p, :, columns] = jnp.dot(
                attn_turned[p].reshape(half, 2 * act_height),
                d_qkv[p, :, columns],
                preferred_element_type=F32,
            ).astype(BF16)

        tile_loop(3 * model, 256, qkv_weights)
        tree_steps((p,), (5,))
    tree_steps((0, 1, 2, 3), (4,))
    act_second(1)
    ff_second()
    for number in range(positions * tile_count):
        p, tile = divmod(number, tile_count)
        qkv_load(number).wait()
        d_rows[p, :, tile * qkv_tile : (tile + 1) * qkv_tile] = lax.dot_general(
            d_qkv[p, :act_height, :],
            qkv_tiles[number % 2],
            (((1,), (1,)), ((), ())),
            preferred_element_type=F32,
        )
        if number + 2 < positions * tile_count:
            qkv_load(number + 2).start()
    tree_steps((0, 1, 2, 3), (3,))

    def attn_back(rows):
        for p in range(positions):
            r, inverse = normed(tokens_ref[p, rows, :].astype(F32))
            d_attn_in = d_rows[p, rows, :]
            gain_acc[p] += r * d_attn_in
            grad_tokens[p, rows, :] = d_mid[p, rows, :] + norm_back(
                r, inverse, d_attn_in * gain_rows[p : p + 1, :]
            )

    row_loop(act_height, 16, attn_back)
    gains_part[...] = jnp.zeros_like(gains_part)
    for index in range(2 * positions):
        sums = jnp.sum(gain_acc[index], axis=0, keepdims=True)
        for block in range(8):
            gains_part[block, index : index + 1, :] = sums[:, 128 * block : 128 * block + 128]
    lax.fori_loop(1, 32, gains_start, 0)
    tree_steps((0, 1, 2, 3), (2,))
    act_third(1)

    def finish_output(rows):
        for p in range(positions):
            total = (
                core_buf[1, 0, 0, p, rows, :].astype(F32)
                + x_buf[1, 0, p, rows, :].astype(F32)
                + z_buf[1, p, rows, :].astype(F32)
            )
            output[p, rows, :] = (resid_mid[p, rows, :] + total).astype(BF16)

    row_loop(act_height, 16, finish_output)
    tree_steps((0, 1, 2, 3), (1,))
    tree_steps((0, 1, 2, 3), (0,))
    ff_last()
    gains_sum[...] = gains_part[lax.div(me, 4)]
    lax.fori_loop(1, 32, gains_wait, 0)
    for _, _, piece, offset in events:
        if hops(offset) > 0:
            maybe(offset_exists(offset, z), tree_copy(piece, offset).wait_send)
    for copy in sends + swaps:
        copy.wait_send()


def backward_scatter(
    tokens,
    grads,
    gain_rows,
    qkv_rows,
    context,
    resid_mid,
    qkv_full,
    out_full,
    out_part,
    back_part,
    gate_up_grad,
    down_grad,
):
    sets, act_height, model = tokens.shape
    width = gate_up_grad.shape[2]
    height = model // 32
    down_height = down_grad.shape[1] // 4
    dma = pltpu.SemaphoreType.DMA
    vmem = pl.BlockSpec(memory_space=pltpu.VMEM)
    anywhere = pl.BlockSpec(memory_space=pl.ANY)
    places = [slot_base(order)[1] for order in ORDERS]
    pair_count = len(pairs_of(sets))
    act = (sets, act_height, model)
    return pl.pallas_call(
        backward_kernel,
        out_shape=(
            jax.ShapeDtypeStruct(act, BF16),
            jax.ShapeDtypeStruct(act, F32),
            jax.ShapeDtypeStruct((8, 128), F32),
            jax.ShapeDtypeStruct((sets, height, 3 * model), F32),
            jax.ShapeDtypeStruct((sets, height, model), F32),
            jax.ShapeDtypeStruct((8, sets, height, width), BF16),
            jax.ShapeDtypeStruct((sets, down_height, model), F32),
        ),
        in_specs=[vmem] * 6 + [anywhere] * 6,
        out_specs=(vmem,) * 7,
        scratch_shapes=[
            pltpu.VMEM((2, 2) + act, BF16),
            pltpu.VMEM((2, 2, 2) + act, BF16),
            pltpu.VMEM((2, 2) + act, BF16),
            pltpu.VMEM((2,) + act, BF16),
            pltpu.VMEM((2, sets, 2, 4 * height, width), BF16),
            pltpu.VMEM((2, sets, down_height, model), BF16),
            pltpu.VMEM((2, sets, 2, 4 * height, width), BF16),
            pltpu.VMEM((2, sets, down_height, model), BF16),
            pltpu.VMEM((sets, 2, 4 * height, width), BF16),
            pltpu.VMEM((sets, down_height, model), BF16),
            pltpu.VMEM((sets, 16 * height, 3 * model), BF16),
            pltpu.VMEM((sets, 16 * height, model), BF16),
            pltpu.VMEM((places[0], height, 3 * model), BF16),
            pltpu.VMEM((places[1], height, 3 * model), BF16),
            pltpu.VMEM((places[2], height, model), BF16),
            pltpu.VMEM((places[3], height, model), BF16),
            pltpu.VMEM((2, 128, 3 * model), BF16),
            pltpu.VMEM((sets, model, model), BF16),
            pltpu.VMEM((2, sets, 16, 2, height, act_height), BF16),
            pltpu.VMEM((sets, 16, height, 2 * act_height), BF16),
            pltpu.VMEM((sets, 16, height, 2 * act_height), BF16),
            pltpu.VMEM((sets, 2 * act_height, 3 * model), BF16),
            pltpu.VMEM((sets, 2 * act_height, model), BF16),
            pltpu.VMEM(act, F32),
            pltpu.VMEM(act, BF16),
            pltpu.VMEM(act, F32),
            pltpu.VMEM((2 * pair_count, act_height, model), BF16),
            pltpu.VMEM((pair_count, act_height, 128), F32),
            pltpu.VMEM((model, 128), BF16),
            pltpu.VMEM((2 * sets, 16, model), F32),
            pltpu.VMEM((8, 8, 128), F32),
            pltpu.VMEM((32, 8, 128), F32),
            dma((2, 2, 2)),
            dma((2, 2, 2)),
            dma((2, 2)),
            dma((2, 2)),
            dma((2,)),
            dma((2,)),
            dma((2, sets, 3)),
            dma((2, sets, 3)),
            dma((sets, 3)),
            dma((sets, 3)),
            dma((8, sets)),
            dma((8, sets)),
            dma((4 * sets,)),
            dma((4 * sets,)),
            dma((4, 16)),
            dma((4, max(places))),
            dma((32,)),
            dma((32,)),
            dma((2, 2, 2)),
            dma((2, sets, 3)),
            dma((2 + sets,)),
        ],
        compiler_params=pltpu.CompilerParams(
            collective_id=5, has_side_effects=True, vmem_limit_bytes=63 * 2**20
        ),
        name="backward_scatter",
    )(
        tokens,
        grads,
        gain_rows,
        qkv_rows,
        context,
        resid_mid,
        qkv_full,
        out_full,
        out_part,
        back_part,
        gate_up_grad,
        down_grad,
    )


def by_set(activations, weight):
    return jnp.einsum("sfk,ske->sfe", activations, weight, preferred_element_type=F32)


def by_set_back(gradients, weight):
    return jnp.einsum("sfe,ske->sfk", gradients, weight, preferred_element_type=F32)


def set_grad(activations, gradients):
    return jnp.einsum("sfk,sfe->ske", activations, gradients, preferred_element_type=F32)


def local_fast(
    tokens,
    norm_attn,
    w_qkv,
    w_out,
    norm_ff,
    w_gate_up,
    w_down,
    cotangent,
    valid_frames,
    item_lengths,
):
    frame_count, positions, model = tokens.shape
    own_gain = norm_attn.shape[1]
    device_index = lax.axis_index(("dp", "pair"))
    local_ids = jnp.arange(frame_count, dtype=jnp.int32)
    frame_ids = device_index * frame_count + local_ids
    item_ends = jnp.cumsum(item_lengths)
    item_starts = item_ends - item_lengths
    in_item = (frame_ids[:, None] >= item_starts[None, :]) & (
        frame_ids[:, None] < item_ends[None, :]
    )
    item_share = 8 * frame_count / item_lengths.astype(F32)
    frame_weight = jnp.sum(jnp.where(in_item, item_share[None, :], 0.0), axis=1)
    frame_weight = jnp.where(local_ids < valid_frames[0], frame_weight, 0.0)
    grad_out = jnp.swapaxes(cotangent, 0, 1).astype(F32) * frame_weight[None, :, None]
    grad_low = grad_out.astype(BF16)

    unit_gains = jnp.concatenate([norm_attn, norm_ff], axis=0)
    lanes = jnp.arange(128, dtype=jnp.int32) // own_gain
    gains = jnp.where(lanes == lax.rem(device_index, 128 // own_gain), jnp.tile(unit_gains, (1, 128 // own_gain)), 0)
    gains = jnp.pad(gains, ((0, 16 - 2 * positions), (0, 0)))

    unit = w_down.shape[1]
    parts = w_gate_up.reshape(positions, -1, 2, 2, 2, 2, 2, 2, unit)
    parts = parts.transpose(4, 6, 7, 0, 1, 2, 3, 5, 8)
    parts = parts.reshape(8, positions, w_gate_up.shape[1], 8 * unit)
    tokens_low = jnp.swapaxes(tokens, 0, 1)
    (
        gains_rows,
        qkv,
        context,
        resid_mid,
        qkv_full,
        out_full,
        gate_up_full,
        down_full,
        ff_rows,
        grad_rows,
    ) = forward_gather(gains, tokens_low, w_qkv, w_out, parts, w_down, grad_low)
    split = 4 * unit
    gate_up = by_set(ff_rows, gate_up_full)
    gate, up = gate_up[..., :split], gate_up[..., split:]
    sigmoid_gate = jax.nn.sigmoid(gate)
    silu_gate = gate * sigmoid_gate
    hidden = (silu_gate * up).astype(BF16)
    out_part = by_set(hidden, down_full).astype(BF16)
    d_hidden = by_set_back(grad_rows, down_full)
    d_gate = d_hidden * up * sigmoid_gate * (1.0 + gate * (1.0 - sigmoid_gate))
    d_up = d_hidden * silu_gate
    d_gate_up = jnp.concatenate([d_gate, d_up], axis=-1).astype(BF16)
    down_grad = set_grad(hidden, grad_rows).astype(BF16)
    gate_up_grad = set_grad(ff_rows, d_gate_up).astype(BF16)
    back_part = by_set_back(d_gate_up, gate_up_full).astype(BF16)
    output, grad_tokens, gains_sum, share_qkv, share_out, gate_up_sum, down_sum = backward_scatter(
        tokens_low,
        grad_out,
        gains_rows,
        qkv,
        context,
        resid_mid,
        qkv_full,
        out_full,
        out_part,
        back_part,
        gate_up_grad,
        down_grad,
    )
    output = jnp.swapaxes(output, 0, 1)
    grad_tokens = jnp.swapaxes(grad_tokens, 0, 1)
    share_gate_up = gate_up_sum.reshape(2, 2, 2, positions, -1, 2, 2, 2, unit)
    share_gate_up = share_gate_up.transpose(3, 4, 5, 6, 0, 7, 1, 2, 8)
    share_gate_up = share_gate_up.reshape(w_gate_up.shape).astype(F32)
    shift = lax.rem(device_index, 128 // own_gain) * own_gain
    gain_grads = lax.dynamic_slice(gains_sum, (0, shift), (2 * positions, own_gain))
    return (
        output,
        grad_tokens,
        gain_grads[:positions],
        share_qkv,
        share_out,
        gain_grads[positions:],
        share_gate_up,
        down_sum,
    )


def solution(mesh):
    in_specs = (
        P(("dp", "pair"), None, None),
        P(None, ("dp", "pair")),
        P(None, ("dp", "pair"), None),
        P(None, ("dp", "pair"), None),
        P(None, ("dp", "pair")),
        P(None, ("dp", "pair"), None),
        P(None, ("dp", "pair"), None),
        P(("dp", "pair"), None, None),
        P(("dp", "pair")),
        P(),
    )
    out_specs = (
        P(("dp", "pair"), None, None),
        P(("dp", "pair"), None, None),
        P(None, ("dp", "pair")),
        P(None, ("dp", "pair"), None),
        P(None, ("dp", "pair"), None),
        P(None, ("dp", "pair")),
        P(None, ("dp", "pair"), None),
        P(None, ("dp", "pair"), None),
    )
    body = local_fast if mesh.shape["dp"] == 16 and mesh.shape["pair"] == 2 else local
    return jax.shard_map(body, mesh=mesh, in_specs=in_specs, out_specs=out_specs, check_vma=False)
```

```python
import functools
import math

import jax
import jax.numpy as jnp
from jax import lax
from jax.experimental import pallas as pl
from jax.experimental.pallas import tpu as pltpu
from jax.sharding import PartitionSpec as P

HEAD_DIM = 64


def per_pos(activations, weight):
    return jnp.einsum("fgk,gke->fge", activations, weight, preferred_element_type=jnp.float32)


def per_pos_back(gradients, weight):
    return jnp.einsum("fge,gke->fgk", gradients, weight, preferred_element_type=jnp.float32)


def pos_grad(activations, gradients):
    return jnp.einsum("fgk,fge->kge", activations, gradients, preferred_element_type=jnp.float32)


def gain_grad(normed_rows, gradients):
    return jnp.transpose(jnp.sum(normed_rows * gradients, axis=0))


def back_layout(share):
    return jnp.swapaxes(share, 0, 1)


def normed(values):
    inverse = lax.rsqrt(jnp.mean(values * values, axis=-1, keepdims=True) + 1e-05)
    return (values * inverse, inverse)


def norm_back(normed_rows, inverse, gradients):
    return inverse * (
        gradients - normed_rows * jnp.mean(gradients * normed_rows, axis=-1, keepdims=True)
    )


def gather_ff_fwd(norm_ff, w_gate_up, w_down, start, group):
    return (
        lax.all_gather(norm_ff[start : start + group], ("dp", "pair"), axis=1, tiled=True),
        lax.all_gather(w_gate_up[start : start + group], ("dp", "pair"), axis=1, tiled=True),
        lax.all_gather(w_down[start : start + group], ("dp", "pair"), axis=1, tiled=True),
    )


def gather_ff_back(norm_ff, w_gate_up, w_down, start, group):
    return (
        lax.all_gather(norm_ff[start : start + group], ("dp", "pair"), axis=1, tiled=True),
        lax.all_gather(w_gate_up[start : start + group], ("dp", "pair"), axis=1, tiled=True),
        lax.all_gather(w_down[start : start + group], ("dp", "pair"), axis=1, tiled=True),
    )


def local(
    tokens,
    norm_attn,
    w_qkv,
    w_out,
    norm_ff,
    w_gate_up,
    w_down,
    cotangent,
    valid_frames,
    item_lengths,
):
    frame_count, positions, model_width = tokens.shape
    head_count = model_width // HEAD_DIM
    ff_units = w_gate_up.shape[2] // 2
    score_scale = 1.0 / math.sqrt(HEAD_DIM)
    causal = jnp.arange(positions)[:, None] >= jnp.arange(positions)[None, :]
    head_shape = (frame_count, positions, head_count, HEAD_DIM)
    group = 1
    gains_attn, qkv_full, out_full = (
        lax.all_gather(norm_attn, ("dp", "pair"), axis=1, tiled=True),
        lax.all_gather(w_qkv, ("dp", "pair"), axis=1, tiled=True),
        lax.all_gather(w_out, ("dp", "pair"), axis=1, tiled=True),
    )
    resid_in = tokens.astype(jnp.float32)
    normed_one, inverse_one = normed(resid_in)
    attn_in = (normed_one * gains_attn.astype(jnp.float32)[None]).astype(jnp.bfloat16)
    qkv_rows = per_pos(attn_in, qkv_full).astype(jnp.bfloat16)
    queries = qkv_rows[..., :model_width].reshape(head_shape)
    key_heads = qkv_rows[..., model_width : 2 * model_width].reshape(head_shape)
    value_heads = qkv_rows[..., 2 * model_width :].reshape(head_shape)
    scores = (
        jnp.einsum("fphd,fqhd->fhpq", queries, key_heads, preferred_element_type=jnp.float32)
        * score_scale
    )
    scores = jnp.where(causal, scores, -1e30)
    row_max = jnp.max(scores, axis=-1, keepdims=True)
    attn_probs = jnp.exp(scores - row_max)
    attn_probs = attn_probs / jnp.sum(attn_probs, axis=-1, keepdims=True)
    probs_low = attn_probs.astype(jnp.bfloat16)
    context = jnp.einsum(
        "fhpq,fqhd->fphd", probs_low, value_heads, preferred_element_type=jnp.float32
    )
    context = context.astype(jnp.bfloat16).reshape(frame_count, positions, model_width)
    resid_mid = resid_in + per_pos(context, out_full)
    kept_parts = []
    out_parts = []
    for start in range(0, positions, group):
        gains_ff, gate_up_full, down_full = gather_ff_fwd(norm_ff, w_gate_up, w_down, start, group)
        mid_part = resid_mid[:, start : start + group]
        normed_two, inverse_two = normed(mid_part)
        ff_in = (normed_two * gains_ff.astype(jnp.float32)[None]).astype(jnp.bfloat16)
        gate_up = per_pos(ff_in, gate_up_full)
        gate_part = gate_up[..., :ff_units]
        up_part = gate_up[..., ff_units:]
        sigmoid_gate = jax.nn.sigmoid(gate_part)
        silu_gate = gate_part * sigmoid_gate
        hidden = (silu_gate * up_part).astype(jnp.bfloat16)
        out_parts.append(mid_part + per_pos(hidden, down_full))
        kept_parts.append(
            (normed_two, inverse_two, ff_in, gate_part, up_part, sigmoid_gate, silu_gate, hidden)
        )
    output = jnp.concatenate(out_parts, axis=1).astype(jnp.bfloat16)
    device_index = lax.axis_index(("dp", "pair"))
    local_ids = jnp.arange(frame_count, dtype=jnp.int32)
    frame_ids = device_index * frame_count + local_ids
    item_ends = jnp.cumsum(item_lengths)
    item_starts = item_ends - item_lengths
    in_item = (frame_ids[:, None] >= item_starts[None, :]) & (
        frame_ids[:, None] < item_ends[None, :]
    )
    item_share = 8 * frame_count / item_lengths.astype(jnp.float32)
    frame_weight = jnp.sum(jnp.where(in_item, item_share[None, :], 0.0), axis=1)
    frame_weight = jnp.where(local_ids < valid_frames[0], frame_weight, 0.0)
    grad_out = cotangent.astype(jnp.float32) * frame_weight[:, None, None]
    mid_grads = []
    share_norm_ff_parts = []
    share_gate_up_parts = []
    share_down_parts = []
    for index, start in enumerate(range(0, positions, group)):
        normed_two, inverse_two, ff_in, gate_part, up_part, sigmoid_gate, silu_gate, hidden = (
            kept_parts[index]
        )
        gains_ff, gate_up_full, down_full = gather_ff_back(norm_ff, w_gate_up, w_down, start, group)
        grad_part = grad_out[:, start : start + group]
        grad_low = grad_part.astype(jnp.bfloat16)
        grad_down = pos_grad(hidden, grad_low)
        d_hidden = per_pos_back(grad_low, down_full)
        d_gate = d_hidden * up_part * sigmoid_gate * (1.0 + gate_part * (1.0 - sigmoid_gate))
        d_up = d_hidden * silu_gate
        d_gate_up = jnp.concatenate([d_gate, d_up], axis=-1).astype(jnp.bfloat16)
        grad_gate_up = pos_grad(ff_in, d_gate_up)
        d_ff_in = per_pos_back(d_gate_up, gate_up_full)
        grad_norm_ff = gain_grad(normed_two, d_ff_in)
        mid_grads.append(
            grad_part
            + norm_back(normed_two, inverse_two, d_ff_in * gains_ff.astype(jnp.float32)[None])
        )
        share_a, share_b, share_c = (
            lax.psum_scatter(grad_norm_ff, ("dp", "pair"), scatter_dimension=0, tiled=True),
            lax.psum_scatter(grad_gate_up, ("dp", "pair"), scatter_dimension=0, tiled=True),
            lax.psum_scatter(grad_down, ("dp", "pair"), scatter_dimension=0, tiled=True),
        )
        share_norm_ff_parts.append(jnp.transpose(share_a))
        share_gate_up_parts.append(back_layout(share_b))
        share_down_parts.append(back_layout(share_c))
    d_mid = jnp.concatenate(mid_grads, axis=1)
    gains_attn, qkv_full, out_full = (
        lax.all_gather(norm_attn, ("dp", "pair"), axis=1, tiled=True),
        lax.all_gather(w_qkv, ("dp", "pair"), axis=1, tiled=True),
        lax.all_gather(w_out, ("dp", "pair"), axis=1, tiled=True),
    )
    d_mid_low = d_mid.astype(jnp.bfloat16)
    grad_out_proj = pos_grad(context, d_mid_low)
    d_context = per_pos_back(d_mid_low, out_full).astype(jnp.bfloat16).reshape(head_shape)
    d_probs = jnp.einsum(
        "fphd,fqhd->fhpq", d_context, value_heads, preferred_element_type=jnp.float32
    )
    d_values = jnp.einsum(
        "fhpq,fphd->fqhd", probs_low, d_context, preferred_element_type=jnp.float32
    )
    d_scores = attn_probs * (d_probs - jnp.sum(attn_probs * d_probs, axis=-1, keepdims=True))
    d_scores = d_scores.astype(jnp.bfloat16)
    d_queries = (
        jnp.einsum("fhpq,fqhd->fphd", d_scores, key_heads, preferred_element_type=jnp.float32)
        * score_scale
    )
    d_keys = (
        jnp.einsum("fhpq,fphd->fqhd", d_scores, queries, preferred_element_type=jnp.float32)
        * score_scale
    )
    row_shape = (frame_count, positions, model_width)
    d_qkv = jnp.concatenate(
        [d_queries.reshape(row_shape), d_keys.reshape(row_shape), d_values.reshape(row_shape)],
        axis=-1,
    ).astype(jnp.bfloat16)
    grad_qkv = pos_grad(attn_in, d_qkv)
    d_attn_in = per_pos_back(d_qkv, qkv_full)
    grad_norm_attn = gain_grad(normed_one, d_attn_in)
    grad_tokens = d_mid + norm_back(
        normed_one, inverse_one, d_attn_in * gains_attn.astype(jnp.float32)[None]
    )
    share_norm_attn, share_qkv, share_out = (
        lax.psum_scatter(grad_norm_attn, ("dp", "pair"), scatter_dimension=0, tiled=True),
        lax.psum_scatter(grad_qkv, ("dp", "pair"), scatter_dimension=0, tiled=True),
        lax.psum_scatter(grad_out_proj, ("dp", "pair"), scatter_dimension=0, tiled=True),
    )
    share_norm_attn = jnp.transpose(share_norm_attn)
    share_qkv = back_layout(share_qkv)
    share_out = back_layout(share_out)
    share_norm_ff = jnp.concatenate(share_norm_ff_parts, axis=0)
    share_gate_up = jnp.concatenate(share_gate_up_parts, axis=0)
    share_down = jnp.concatenate(share_down_parts, axis=0)
    return (
        output,
        grad_tokens,
        share_norm_attn,
        share_qkv,
        share_out,
        share_norm_ff,
        share_gate_up,
        share_down,
    )


MESH_ID = pl.DeviceIdType.MESH
BF16 = jnp.bfloat16
F32 = jnp.float32


def here():
    dp = lax.axis_index("dp")
    core = lax.axis_index("pair")
    return lax.div(dp, 4), lax.rem(lax.div(dp, 2), 2), lax.rem(dp, 2), core


def flip(value, bit):
    return 1 - value if bit else value


def push(src, dst, send_sem, recv_sem, to):
    return pltpu.make_async_remote_copy(
        src_ref=src,
        dst_ref=dst,
        send_sem=send_sem,
        recv_sem=recv_sem,
        device_id=to,
        device_id_type=MESH_ID,
    )


def arrived(dst, recv_sem, to):
    push(dst, dst, recv_sem, recv_sem, to).wait_recv()


def greet_all(z, y, x, core):
    barrier = pltpu.get_barrier_semaphore()
    me = 2 * (z * 4 + y * 2 + x) + core

    def one(step, carry):
        other = lax.rem(me + step, 32)
        pl.semaphore_signal(
            barrier, inc=1, device_id=(lax.div(other, 2), lax.rem(other, 2)), device_id_type=MESH_ID
        )
        return carry

    lax.fori_loop(1, 32, one, 0)
    pl.semaphore_wait(barrier, 31)


def greet(peers):
    barrier = pltpu.get_barrier_semaphore()
    for to in peers:
        pl.semaphore_signal(barrier, inc=1, device_id=to, device_id_type=MESH_ID)
    pl.semaphore_wait(barrier, len(peers))


def maybe(condition, do):
    if condition is None:
        do()
    else:
        pl.when(condition)(do)


OFFSETS = [
    (dz, dy, dx) for dz in (0, -1, 1, -2, 2, -3, 3) for dy in (0, 1) for dx in (0, 1)
]
ORDERS = ("zxy", "zyx", "xyz", "yxz")


def hops(offset):
    return abs(offset[0]) + offset[1] + offset[2]


def arrival_axis(order, offset):
    part = dict(z=offset[0], y=offset[1], x=offset[2])
    last = None
    for axis in order:
        if part[axis] != 0:
            last = axis
    return last


def onward(order, offset):
    directions = []
    last = arrival_axis(order, offset)
    start = 0
    if last is not None:
        start = order.index(last) + 1
        if last == "z":
            directions.append("u" if offset[0] < 0 else "d")
    for axis in order[start:]:
        directions.extend(["u", "d"] if axis == "z" else [axis])
    return directions


def came_from(order, offset):
    last = arrival_axis(order, offset)
    if last == "z":
        return "d" if offset[0] < 0 else "u"
    return last


def offset_exists(offset, z):
    if offset[0] < 0:
        return z >= -offset[0]
    if offset[0] > 0:
        return z <= 3 - offset[0]
    return None


def direction_exists(direction, z):
    return {"u": z < 3, "d": z > 0}.get(direction)


DIRECTIONS = ("x", "y", "u", "d", "s")


def neighbour(direction, z, y, x, core):
    if direction == "x":
        return (z * 4 + y * 2 + 1 - x, core)
    if direction == "y":
        return (z * 4 + (1 - y) * 2 + x, core)
    if direction == "u":
        return (z * 4 + 4 + y * 2 + x, core)
    if direction == "d":
        return (z * 4 - 4 + y * 2 + x, core)
    return (z * 4 + y * 2 + x, 1 - core)


def chip_of(offset, z, y, x):
    return (z + offset[0]) * 4 + flip(y, offset[1]) * 2 + flip(x, offset[2])


RANK_STEPS = sorted(
    ((dl, dx, dc) for dl in (0, 1) for dx in (0, 1) for dc in (0, 1)), key=lambda step: (sum(step), step)
)


def group_place(z, y, x, core):
    zh, zl = lax.div(z, 2), lax.rem(z, 2)

    def member(step):
        return ((2 * zh + flip(zl, step[0])) * 4 + y * 2 + flip(x, step[1]), flip(core, step[2]))

    def rank(step):
        return 4 * flip(zl, step[0]) + 2 * flip(x, step[1]) + flip(core, step[2])

    def device(step, dzh=0, dy=0):
        return 16 * flip(zh, dzh) + 4 * flip(y, dy) + 8 * flip(zl, step[0]) + 2 * flip(x, step[1]) + flip(core, step[2])

    far = ((2 * (1 - zh) + zl) * 4 + y * 2 + x, core)
    across = (z * 4 + (1 - y) * 2 + x, core)
    return zh, zl, member, rank, device, far, across


def add_into(target, sources, rows=16, columns=1024):
    height, width = target.shape
    across = width // columns

    def one(step, carry):
        top = pl.multiple_of(lax.div(step, across) * rows, rows)
        left = pl.multiple_of(lax.rem(step, across) * columns, columns)
        spot = (pl.ds(top, rows), pl.ds(left, columns))
        total = sources[0][spot].astype(F32)
        for source in sources[1:]:
            total = total + source[spot].astype(F32)
        target[spot] = total.astype(target.dtype)
        return carry

    lax.fori_loop(0, (height // rows) * across, one, 0)


def row_loop(height, chunk, body):
    def one(step, carry):
        body(pl.ds(pl.multiple_of(step * chunk, chunk), chunk))
        return carry

    lax.fori_loop(0, height // chunk, one, 0)


def tile_loop(width, tile, body):
    def one(step, carry):
        body(pl.ds(pl.multiple_of(step * tile, tile), tile))
        return carry

    lax.fori_loop(0, width // tile, one, 0)


def dot(left, right):
    return jnp.dot(left, right, preferred_element_type=F32)


def dot_back(left, right):
    return lax.dot_general(left, right, (((1,), (1,)), ((), ())), preferred_element_type=F32)


def dot_grad(left, right):
    return lax.dot_general(left, right, (((0,), (0,)), ((), ())), preferred_element_type=F32)


def make_spread(spread):
    height, width = spread.shape
    head = lax.broadcasted_iota(jnp.int32, (height, width), 0) // HEAD_DIM
    spread[...] = jnp.where(
        head == lax.broadcasted_iota(jnp.int32, (height, width), 1), 1.0, 0.0
    ).astype(BF16)


def pairs_of(positions):
    return [(p, q) for p in range(positions) for q in range(p + 1)]


def split_product(product):
    high = product.astype(BF16)
    return high, (product - high.astype(F32)).astype(BF16)


def sums_over_heads(halves, spread, index):
    return dot(halves[2 * index], spread[...]) + dot(halves[2 * index + 1], spread[...])


def to_heads(values, spread):
    return dot_back(values, spread[...]).astype(BF16)


def attention_probs(qkv, halves, spread, model, position):
    height = qkv.shape[1]
    scale = 1.0 / math.sqrt(HEAD_DIM)

    def products(rows):
        for q in range(position + 1):
            product = qkv[position, rows, :model].astype(F32) * qkv[
                q, rows, model : 2 * model
            ].astype(F32)
            halves[2 * q, rows, :], halves[2 * q + 1, rows, :] = split_product(product)

    row_loop(height, 16, products)
    scores = [sums_over_heads(halves, spread, q) * scale for q in range(position + 1)]
    top = functools.reduce(jnp.maximum, scores)
    powers = [jnp.exp(score - top) for score in scores]
    total = functools.reduce(jnp.add, powers)
    return [power / total for power in powers]


def forward_kernel(
    gains_ref,
    tokens_ref,
    qkv_ref,
    out_ref,
    gate_up_ref,
    down_ref,
    grads_ref,
    gain_rows,
    qkv_rows,
    context,
    resid_mid,
    qkv_full,
    out_full,
    ff_out,
    ff_back,
    gate_up_grad,
    down_grad,
    qkv_buf,
    out_buf,
    gate_up_buf,
    down_buf,
    rows_buf,
    grads_buf,
    hidden,
    d_gate_up,
    out_stage,
    back_stage,
    gate_up_stage,
    down_stage,
    gains_all,
    attn_in,
    halves,
    spread,
    plane_sem,
    sibling_sem,
    send_sem,
    gains_send,
    gains_recv,
    rank_send,
    rank_recv,
    far_send,
    far_recv,
    across_send,
    across_recv,
    act_send,
    act_recv,
    local_sem,
    keep_sem,
    stage_sem,
):
    z, y, x, core = here()
    me = 2 * (z * 4 + y * 2 + x) + core
    zh, zl, member, rank, device, far, across = group_place(z, y, x, core)
    own_step = (0, 0, 0)
    positions, act_height, model = tokens_ref.shape
    height = gate_up_ref.shape[2]
    down_height = down_ref.shape[1]
    split = 4 * down_height
    sibling = neighbour("s", z, y, x, core)
    greet_all(z, y, x, core)
    part = qkv_ref.shape[2] // 2
    pieces = []
    for s in range(positions):
        pieces.append((qkv_ref, qkv_buf, s, pl.ds(0, part), "zxy"))
        pieces.append((qkv_ref, qkv_buf, s, pl.ds(part, part), "zyx"))
        pieces.append((out_ref, out_buf, s, pl.ds(0, model), ("xyz", "yxz")[s % 2]))

    def piece_rows(piece, number):
        _, full, index, columns, _ = pieces[piece]
        return full.at[index, pl.ds(pl.multiple_of(number * height, height), height), columns]

    def tree_send(piece, offset, direction):
        source, _, index, columns, _ = pieces[piece]
        chip = chip_of(offset, z, y, x)
        block = piece_rows(piece, 2 * chip + core)
        recv = sibling_sem if direction == "s" else plane_sem
        return push(
            source.at[index, :, columns] if hops(offset) == 0 else block,
            block,
            send_sem.at[piece, chip, DIRECTIONS.index(direction)],
            recv.at[piece, chip],
            neighbour(direction, z, y, x, core),
        )

    def tree_step(piece, offset, finish=False):
        order = pieces[piece][4]

        def go():
            chip = chip_of(offset, z, y, x)
            if hops(offset) > 0 and not finish:
                arrived(piece_rows(piece, 2 * chip + core), plane_sem.at[piece, chip], sibling)
            for direction in onward(order, offset) + ["s"]:
                copy = tree_send(piece, offset, direction)
                maybe(direction_exists(direction, z), copy.wait_send if finish else copy.start)

        maybe(offset_exists(offset, z), go)

    events = sorted(
        (
            (hops(offset), place, piece, offset)
            for piece in range(len(pieces))
            for place, offset in enumerate(OFFSETS)
        ),
        key=lambda event: event[:3],
    )

    def tree_steps(s, distance):
        for hop, _, piece, offset in events:
            if hop == distance and pieces[piece][2] == s:
                tree_step(piece, offset)

    def tree_end(s):
        mine = [piece for piece in range(len(pieces)) if pieces[piece][2] == s]

        def sibling_wait(chip, carry):
            for piece in mine:
                arrived(piece_rows(piece, 2 * chip + 1 - core), sibling_sem.at[piece, chip], sibling)
            return carry

        lax.fori_loop(0, 16, sibling_wait, 0)
        for piece in mine:
            tree_own[piece].wait()

    tree_own = [
        pltpu.make_async_copy(
            source.at[index, :, columns], piece_rows(piece, me), local_sem.at[piece]
        )
        for piece, (source, _, index, columns, _) in enumerate(pieces)
    ]

    def gains_copy(step):
        other = lax.rem(me + step, 32)
        return push(
            gains_ref,
            gains_all.at[me],
            gains_send.at[step],
            gains_recv.at[me],
            (lax.div(other, 2), lax.rem(other, 2)),
        )

    def gains_start(step, carry):
        gains_copy(step).start()
        return carry

    def gains_wait(step, carry):
        other = lax.rem(me + step, 32)
        gains_copy(step).wait_send()
        arrived(gains_all.at[other], gains_recv.at[other], sibling)
        return carry

    sends = []

    def start(copy):
        copy.start()
        sends.append(copy)

    def weight_rows(s, number):
        return gate_up_buf.at[s, pl.ds(pl.multiple_of(number * height, height), height), :]

    def down_rows(s, dzh, dy):
        number = 2 * flip(zh, dzh) + flip(y, dy)
        return down_buf.at[s, pl.ds(pl.multiple_of(number * down_height, down_height), down_height), :]

    def act_rows(which, s, step):
        full = (rows_buf, grads_buf)[which]
        return full.at[s, pl.ds(pl.multiple_of(rank(step) * act_height, act_height), act_height), :]

    def send_act(which, s, step, source, hop):
        landed = tuple(bit ^ (1 if axis == hop else 0) for axis, bit in enumerate(step))
        start(
            push(
                source,
                act_rows(which, s, step),
                act_send.at[which, s, 4 * step[0] + 2 * step[1] + step[2], hop],
                act_recv.at[which, s, 4 * landed[0] + 2 * landed[1] + landed[2]],
                member(tuple(1 if axis == hop else 0 for axis in range(3))),
            )
        )

    def wait_act(which, s, step):
        arrived(
            act_rows(which, s, step),
            act_recv.at[which, s, 4 * step[0] + 2 * step[1] + step[2]],
            sibling,
        )

    def act_own(which, s):
        source = act_rows(0, s, own_step) if which == 0 else grads_ref.at[s]
        for hop in (0, 1, 2):
            send_act(which, s, own_step, source, hop)

    def act_from_z(which, s):
        step = (1, 0, 0)
        wait_act(which, s, step)
        send_act(which, s, step, act_rows(which, s, step), 1)
        send_act(which, s, step, act_rows(which, s, step), 2)

    def act_from_x(which, s, steps=((0, 1, 0), (1, 1, 0))):
        for step in steps:
            wait_act(which, s, step)
            send_act(which, s, step, act_rows(which, s, step), 2)

    def act_from_core(which, s, steps=((0, 0, 1), (1, 0, 1), (0, 1, 1), (1, 1, 1))):
        for step in steps:
            wait_act(which, s, step)

    def mine(s):
        return gate_up_ref.at[rank(own_step), s]

    def ff_to_ranks(s):
        for slot, step in enumerate(RANK_STEPS):
            if step != own_step:
                start(
                    push(
                        gate_up_ref.at[rank(step), s],
                        weight_rows(s, device(own_step)),
                        rank_send.at[s, slot],
                        rank_recv.at[s, slot],
                        member(step),
                    )
                )

    def ff_own_far(s):
        start(push(mine(s), weight_rows(s, device(own_step)), far_send.at[s, 0], far_recv.at[s, 0], far))
        start(push(down_ref.at[s], down_rows(s, 0, 0), far_send.at[s, 8], far_recv.at[s, 8], far))

    def ff_own_across(s):
        for slot, source, target in (
            (0, mine(s), weight_rows(s, device(own_step))),
            (8, down_ref.at[s], down_rows(s, 0, 0)),
        ):
            start(push(source, target, across_send.at[s, 0, slot], across_recv.at[s, 0, slot], across))

    def ff_from_rank(s, slots):
        for slot in slots:
            block = weight_rows(s, device(RANK_STEPS[slot]))
            arrived(block, rank_recv.at[s, slot], sibling)
            start(push(block, block, far_send.at[s, slot], far_recv.at[s, slot], far))
            start(push(block, block, across_send.at[s, 0, slot], across_recv.at[s, 0, slot], across))

    def ff_from_far(s, slots):
        for slot in slots:
            block = down_rows(s, 1, 0) if slot == 8 else weight_rows(s, device(RANK_STEPS[slot], 1, 0))
            arrived(block, far_recv.at[s, slot], sibling)
            start(push(block, block, across_send.at[s, 1, slot], across_recv.at[s, 1, slot], across))

    def ff_end(s):
        for dzh in (0, 1):
            for slot, step in enumerate(RANK_STEPS):
                arrived(weight_rows(s, device(step, dzh, 1)), across_recv.at[s, dzh, slot], sibling)
            arrived(down_rows(s, dzh, 1), across_recv.at[s, dzh, 8], sibling)

    ff_local = []
    for s in range(positions):
        ff_local.append(
            [
                pltpu.make_async_copy(mine(s), weight_rows(s, device(own_step)), local_sem.at[7 + 3 * s]),
                pltpu.make_async_copy(down_ref.at[s], down_rows(s, 0, 0), local_sem.at[8 + 3 * s]),
                pltpu.make_async_copy(grads_ref.at[s], act_rows(1, s, own_step), local_sem.at[9 + 3 * s]),
            ]
        )
    gains_local = pltpu.make_async_copy(gains_ref, gains_all.at[me], local_sem.at[6])

    def take_gains():
        lax.fori_loop(1, 32, gains_wait, 0)
        gains_local.wait()
        for block in range(8):
            total = gains_all[4 * block].astype(F32)
            for extra in range(1, 4):
                total = total + gains_all[4 * block + extra].astype(F32)
            gain_rows[:, 128 * block : 128 * block + 128] = total

        def first_norm(rows):
            for p in range(positions):
                r, _ = normed(tokens_ref[p, rows, :].astype(F32))
                attn_in[p, rows, :] = (r * gain_rows[p : p + 1, :]).astype(BF16)

        row_loop(act_height, 16, first_norm)

    keep = []

    def attention(p):
        for source, target, slot in (
            (qkv_buf.at[p], qkv_full.at[p], 2 * p),
            (out_buf.at[p], out_full.at[p], 2 * p + 1),
        ):
            keep.append(pltpu.make_async_copy(source, target, keep_sem.at[slot]))
            keep[-1].start()

        def project(columns):
            qkv_rows[p, :, columns] = dot(attn_in[p], qkv_buf[p, :, columns]).astype(BF16)

        tile_loop(3 * model, 512, project)
        probs = attention_probs(qkv_rows, halves, spread, model, p)
        for q in range(p + 1):
            halves[2 * q] = to_heads(probs[q].astype(BF16), spread)

        def mix(rows):
            total = None
            for q in range(p + 1):
                term = halves[2 * q, rows, :].astype(F32) * qkv_rows[q, rows, 2 * model :].astype(F32)
                total = term if total is None else total + term
            context[p, rows, :] = total.astype(BF16)

        row_loop(act_height, 16, mix)

        def attend(columns):
            resid_mid[p, :, columns] = tokens_ref[p, :, columns].astype(F32) + dot(
                context[p], out_buf[p, :, columns]
            )

        tile_loop(model, 512, attend)

        def second_norm(step, carry):
            rows = pl.ds(pl.multiple_of(step * 16, 16), 16)
            r, _ = normed(resid_mid[p, rows, :])
            top = rank(own_step) * act_height + step * 16
            rows_buf[p, pl.ds(pl.multiple_of(top, 16), 16), :] = (
                r * gain_rows[positions + p : positions + p + 1, :]
            ).astype(BF16)
            return carry

        lax.fori_loop(0, act_height // 16, second_norm, 0)

    def ff_block(s, number):
        rows = pl.ds(pl.multiple_of(number * 2 * act_height, 2 * act_height), 2 * act_height)
        normed_rows = rows_buf[s, rows, :]
        grads = grads_buf[s, rows, :]
        for tile in range(split // 256):
            left, right = pl.ds(tile * 256, 256), pl.ds(split + tile * 256, 256)
            gate = dot(normed_rows, gate_up_buf[s, :, left])
            up = dot(normed_rows, gate_up_buf[s, :, right])
            d_hidden = dot_back(grads, down_buf[s, left, :])
            sigmoid_gate = jax.nn.sigmoid(gate)
            silu_gate = gate * sigmoid_gate
            hidden[rows, left] = (silu_gate * up).astype(BF16)
            d_gate_up[rows, left] = (
                d_hidden * up * sigmoid_gate * (1.0 + gate * (1.0 - sigmoid_gate))
            ).astype(BF16)
            d_gate_up[rows, right] = (d_hidden * silu_gate).astype(BF16)
        for tile in range(model // 512):
            columns = pl.ds(tile * 512, 512)
            out_stage[rows, columns] = dot(hidden[rows, :], down_buf[s, :, columns]).astype(BF16)
            back_stage[rows, columns] = dot_back(
                d_gate_up[rows, :], gate_up_buf[s, columns, :]
            ).astype(BF16)

    def ff_blocks(s):
        def one(number, carry):
            ff_block(s, number)
            return carry

        lax.fori_loop(0, 4, one, 0)

    stages = []

    def stage_out(s, first):
        chosen = (
            [(out_stage, ff_out, 0), (back_stage, ff_back, 1)]
            if first
            else [(gate_up_stage, gate_up_grad, 2), (down_stage, down_grad, 3)]
        )
        for source, target, slot in chosen:
            stages.append(pltpu.make_async_copy(source, target.at[s], stage_sem.at[s, slot]))
            stages[-1].start()

    def ff_grads(s):
        stage_out(s, True)

        def gate_up_tile(columns):
            gate_up_stage[:, columns] = dot_grad(rows_buf[s], d_gate_up[:, columns]).astype(BF16)

        def down_tile(columns):
            down_stage[:, columns] = dot_grad(hidden[...], grads_buf[s, :, columns]).astype(BF16)

        tile_loop(2 * split, 256, gate_up_tile)
        tile_loop(model, 256, down_tile)
        stage_out(s, False)

    def stages_end():
        while stages:
            stages.pop(0).wait()

    tree_steps(0, 0)
    lax.fori_loop(1, 32, gains_start, 0)
    ff_to_ranks(0)
    ff_own_far(0)
    ff_own_across(0)
    act_own(1, 0)
    for copy in tree_own + ff_local[0] + ff_local[1] + [gains_local]:
        copy.start()
    make_spread(spread)
    tree_steps(0, 1)
    ff_from_rank(0, (1, 2, 3, 4))
    take_gains()
    tree_steps(0, 2)
    ff_from_rank(0, (5, 6, 7))
    act_from_z(1, 0)
    tree_steps(1, 0)
    tree_steps(0, 3)
    ff_from_far(0, (0, 8, 1, 2))
    tree_steps(0, 4)
    tree_steps(0, 5)
    tree_steps(1, 1)
    ff_to_ranks(1)
    tree_end(0)
    attention(0)
    act_own(0, 0)
    ff_from_far(0, (3, 4, 5, 6, 7))
    act_from_x(1, 0)
    tree_steps(1, 2)
    act_from_z(0, 0)
    ff_own_far(1)
    ff_own_across(1)
    act_own(1, 1)
    tree_steps(1, 3)
    act_from_x(0, 0)
    ff_from_rank(1, (1, 2, 3, 4))
    tree_steps(1, 4)
    ff_from_rank(1, (5, 6, 7))
    tree_steps(1, 5)
    act_from_z(1, 1)
    tree_end(1)
    attention(1)
    act_own(0, 1)
    ff_from_far(1, (0, 8, 1, 2, 3))
    act_from_core(1, 0)
    act_from_core(0, 0)
    for copy in ff_local[0]:
        copy.wait()
    ff_end(0)
    ff_blocks(0)
    act_from_z(0, 1)
    ff_from_far(1, (4, 5, 6, 7))
    act_from_x(1, 1)
    act_from_x(0, 1, ((0, 1, 0),))
    ff_grads(0)
    act_from_x(0, 1, ((1, 1, 0),))
    for copy in ff_local[1]:
        copy.wait()
    act_from_core(1, 1)
    ff_end(1)
    stages_end()
    for step in ((0, 0, 1), (1, 0, 1), (0, 1, 1), (1, 1, 1)):
        act_from_core(0, 1, (step,))
        ff_block(1, 2 * flip(zl, step[0]) + flip(x, step[1]))
    ff_grads(1)
    for _, _, piece, offset in events:
        tree_step(piece, offset, finish=True)
    for copy in sends:
        copy.wait_send()
    for copy in keep:
        copy.wait()
    stages_end()


def forward_gather(gains, tokens, w_qkv, w_out, gate_up_parts, w_down, grads):
    positions, act_height, model = tokens.shape
    _, height, qkv_width = w_qkv.shape
    ranks, _, _, width = gate_up_parts.shape
    split = 4 * w_down.shape[1]
    group_rows = ranks * act_height
    dma = pltpu.SemaphoreType.DMA
    vmem = pl.BlockSpec(memory_space=pltpu.VMEM)
    anywhere = pl.BlockSpec(memory_space=pl.ANY)
    return pl.pallas_call(
        forward_kernel,
        out_shape=(
            jax.ShapeDtypeStruct((16, model), F32),
            jax.ShapeDtypeStruct((positions, act_height, 3 * model), BF16),
            jax.ShapeDtypeStruct((positions, act_height, model), BF16),
            jax.ShapeDtypeStruct((positions, act_height, model), F32),
            jax.ShapeDtypeStruct((positions, model, qkv_width), BF16),
            jax.ShapeDtypeStruct((positions, model, model), BF16),
            jax.ShapeDtypeStruct((positions, group_rows, model), BF16),
            jax.ShapeDtypeStruct((positions, group_rows, model), BF16),
            jax.ShapeDtypeStruct((positions, model, width), BF16),
            jax.ShapeDtypeStruct((positions, split, model), BF16),
        ),
        in_specs=[anywhere, vmem] + [anywhere] * 5,
        out_specs=(vmem,) * 4 + (anywhere,) * 6,
        scratch_shapes=[
            pltpu.VMEM((positions, model, qkv_width), BF16),
            pltpu.VMEM((positions, model, model), BF16),
            pltpu.VMEM((positions, model, width), BF16),
            pltpu.VMEM((positions, split, model), BF16),
            pltpu.VMEM((positions, group_rows, model), BF16),
            pltpu.VMEM((positions, group_rows, model), BF16),
            pltpu.VMEM((group_rows, split), BF16),
            pltpu.VMEM((group_rows, width), BF16),
            pltpu.VMEM((group_rows, model), BF16),
            pltpu.VMEM((group_rows, model), BF16),
            pltpu.VMEM((model, width), BF16),
            pltpu.VMEM((split, model), BF16),
            pltpu.VMEM((32, 16, 128), BF16),
            pltpu.VMEM((positions, act_height, model), BF16),
            pltpu.VMEM((2 * positions, act_height, model), BF16),
            pltpu.VMEM((model, 128), BF16),
            dma((6, 16)),
            dma((6, 16)),
            dma((6, 16, 5)),
            dma((32,)),
            dma((32,)),
            dma((2, 8)),
            dma((2, 8)),
            dma((2, 9)),
            dma((2, 9)),
            dma((2, 2, 9)),
            dma((2, 2, 9)),
            dma((2, 2, 8, 3)),
            dma((2, 2, 8)),
            dma((13,)),
            dma((4,)),
            dma((2, 4)),
        ],
        compiler_params=pltpu.CompilerParams(
            collective_id=4, has_side_effects=True, vmem_limit_bytes=62 * 2**20
        ),
        name="forward_gather",
    )(gains, tokens, w_qkv, w_out, gate_up_parts, w_down, grads)


def slot_index(order, direction, offset, z, y, x):
    axis = {"u": "z", "d": "z"}.get(direction, direction)
    index, count = 0, 1
    values = dict(z=z + offset[0], y=flip(y, offset[1]), x=flip(x, offset[2]))
    sizes = dict(z=4, y=2, x=2)
    for earlier in order[: order.index(axis)]:
        index = index * sizes[earlier] + values[earlier]
        count *= sizes[earlier]
    if axis == "z":
        index = index * 5 + (4 if direction == "d" and offset[0] == 0 else values["z"])
        count *= 5
    return index, count


def slot_base(order):
    base, total = {}, 0
    for axis, direction in (("x", "x"), ("y", "y"), ("z", "u")):
        base[axis] = total
        total += slot_index(order, direction, (0, 0, 0), 0, 0, 0)[1]
    base["u"] = base["d"] = base["z"]
    return base, total


def backward_kernel(
    tokens_ref,
    cot_ref,
    gain_rows,
    qkv_rows,
    context,
    resid_mid,
    qkv_full,
    out_full,
    out_ref,
    back_ref,
    gate_up_ref,
    down_ref,
    output,
    grad_tokens,
    gains_sum,
    qkv_sum,
    attn_out_sum,
    gate_up_sum,
    down_sum,
    act_own,
    core_buf,
    x_buf,
    z_buf,
    gate_own,
    down_own,
    across_gate,
    across_down,
    far_gate,
    far_down,
    qkv_grad,
    out_grad,
    slots_0,
    slots_1,
    slots_2,
    slots_3,
    qkv_tiles,
    out_tiles,
    turned,
    attn_turned,
    context_turned,
    d_qkv,
    d_mid_low,
    d_mid,
    d_context,
    d_rows,
    halves,
    probs_buf,
    spread,
    gain_acc,
    gains_part,
    gains_buf,
    core_send,
    core_recv,
    x_send,
    x_recv,
    z_send,
    z_recv,
    across_send,
    across_recv,
    far_send,
    far_recv,
    rank_send,
    rank_recv,
    swap_send,
    swap_recv,
    tree_send,
    tree_recv,
    gains_send,
    gains_recv,
    own_sem,
    part_sem,
    tile_sem,
):
    z, y, x, core = here()
    me = 2 * (z * 4 + y * 2 + x) + core
    zh, zl, member, rank, device, far, across = group_place(z, y, x, core)
    own_step = (0, 0, 0)
    positions, act_height, model = tokens_ref.shape
    sets = positions
    height = qkv_sum.shape[1]
    down_height = down_sum.shape[1]
    half = 16 * height
    sibling = member((0, 0, 1))
    scale = 1.0 / math.sqrt(HEAD_DIM)
    pairs = pairs_of(positions)
    greet_all(z, y, x, core)
    sends = []

    def start(copy):
        copy.start()
        sends.append(copy)

    def run_rows(dzh, dy, low):
        number = 16 * flip(zh, dzh) + 4 * flip(y, dy) + 8 * low
        return pl.ds(pl.multiple_of(number * height, 4 * height), 4 * height)

    def down_rows(dzh, dy):
        number = 2 * flip(zh, dzh) + flip(y, dy)
        return pl.ds(pl.multiple_of(number * down_height, down_height), down_height)

    def ff_across(turn):
        dzh = 1 - turn
        for s in range(sets):
            for low in (0, 1):
                start(
                    push(
                        gate_up_ref.at[s, run_rows(dzh, 1, low)],
                        across_gate.at[turn, s, low],
                        across_send.at[turn, s, low],
                        across_recv.at[turn, s, low],
                        across,
                    )
                )
            start(
                push(
                    down_ref.at[s, down_rows(dzh, 1)],
                    across_down.at[turn, s],
                    across_send.at[turn, s, 2],
                    across_recv.at[turn, s, 2],
                    across,
                )
            )

    part_copies = []
    for turn in (0, 1):
        for s in range(sets):
            for low in (0, 1):
                part_copies.append(
                    pltpu.make_async_copy(
                        gate_up_ref.at[s, run_rows(1 - turn, 0, low)],
                        gate_own.at[turn, s, low],
                        part_sem.at[turn, s, low],
                    )
                )
            part_copies.append(
                pltpu.make_async_copy(
                    down_ref.at[s, down_rows(1 - turn, 0)], down_own.at[turn, s], part_sem.at[turn, s, 2]
                )
            )

    def ff_first():
        for s in range(sets):
            for low in (0, 1):
                block = across_gate.at[0, s, low]
                arrived(block, across_recv.at[0, s, low], across)
                add_into(block, [block, gate_own.at[0, s, low]])
                start(push(block, far_gate.at[s, low], far_send.at[s, low], far_recv.at[s, low], far))
            block = across_down.at[0, s]
            arrived(block, across_recv.at[0, s, 2], across)
            add_into(block, [block, down_own.at[0, s]])
            start(push(block, far_down.at[s], far_send.at[s, 2], far_recv.at[s, 2], far))

    def share(step, s):
        number = 2 * flip(x, step[1]) + flip(core, step[2])
        return across_gate.at[
            1, s, flip(zl, step[0]), pl.ds(pl.multiple_of(number * height, height), height)
        ]

    def ff_second():
        for s in range(sets):
            for low in (0, 1):
                block = across_gate.at[1, s, low]
                arrived(block, across_recv.at[1, s, low], across)
                arrived(far_gate.at[s, low], far_recv.at[s, low], far)
                add_into(block, [block, far_gate.at[s, low], gate_own.at[1, s, low]])
            for slot, step in enumerate(RANK_STEPS):
                if step != own_step:
                    start(
                        push(
                            share(step, s),
                            gate_up_sum.at[rank(own_step), s],
                            rank_send.at[slot, s],
                            rank_recv.at[slot, s],
                            member(step),
                        )
                    )
            add_into(gate_up_sum.at[rank(own_step), s], [share(own_step, s)])
            arrived(across_down.at[1, s], across_recv.at[1, s, 2], across)
            arrived(far_down.at[s], far_recv.at[s, 2], far)
            add_into(down_sum.at[s], [across_down.at[1, s], far_down.at[s], down_own.at[1, s]])

    def ff_last():
        for slot, step in enumerate(RANK_STEPS):
            for s in range(sets):
                if step != own_step:
                    arrived(gate_up_sum.at[rank(step), s], rank_recv.at[slot, s], member(step))

    acts = [back_ref, out_ref]

    def act_rows(step):
        return pl.ds(pl.multiple_of(rank(step) * act_height, act_height), act_height)

    def act_core_sends(which):
        for dl, dx in ((1, 1), (0, 1), (1, 0), (0, 0)):
            start(
                push(
                    acts[which].at[:, act_rows((dl, dx, 1))],
                    core_buf.at[which, dl, dx],
                    core_send.at[which, dl, dx],
                    core_recv.at[which, dl, dx],
                    sibling,
                )
            )

    def act_load(which):
        return [
            pltpu.make_async_copy(
                acts[which].at[:, act_rows((dl, dx, 0))], act_own.at[dl, dx], own_sem.at[which, dl, dx]
            )
            for dl in (0, 1)
            for dx in (0, 1)
        ]

    def core_add(which, dl, dx):
        block = core_buf.at[which, dl, dx]
        arrived(block, core_recv.at[which, dl, dx], sibling)
        for s in range(sets):
            add_into(block.at[s], [block.at[s], act_own.at[dl, dx, s]])

    def act_first(which):
        for dl in (1, 0):
            core_add(which, dl, 1)
            start(
                push(
                    core_buf.at[which, dl, 1],
                    x_buf.at[which, dl],
                    x_send.at[which, dl],
                    x_recv.at[which, dl],
                    member((0, 1, 0)),
                )
            )
        core_add(which, 1, 0)
        core_add(which, 0, 0)

    def act_second(which):
        arrived(x_buf.at[which, 1], x_recv.at[which, 1], member((0, 1, 0)))
        for s in range(sets):
            block = x_buf.at[which, 1, s]
            add_into(block, [block, core_buf.at[which, 1, 0, s]])
        start(
            push(
                x_buf.at[which, 1], z_buf.at[which], z_send.at[which], z_recv.at[which], member((1, 0, 0))
            )
        )

    def act_third(which):
        arrived(x_buf.at[which, 0], x_recv.at[which, 0], member((0, 1, 0)))
        arrived(z_buf.at[which], z_recv.at[which], member((1, 0, 0)))

    pieces = [
        (qkv_grad, qkv_sum, 0, "zxy", slots_0),
        (qkv_grad, qkv_sum, 1, "zyx", slots_1),
        (out_grad, attn_out_sum, 0, "xyz", slots_2),
        (out_grad, attn_out_sum, 1, "yxz", slots_3),
    ]
    events = sorted(
        ((-hops(offset), place, piece, offset) for piece in range(4) for place, offset in enumerate(OFFSETS)),
        key=lambda event: event[:3],
    )

    def tree_block(piece, offset):
        source, _, index, _, _ = pieces[piece]
        chip = chip_of(offset, z, y, x)
        return source.at[index, pl.ds(pl.multiple_of(chip * height, height), height), :]

    def tree_copy(piece, offset):
        _, _, _, order, slots = pieces[piece]
        toward = came_from(order, offset)
        base, _ = slot_base(order)
        seen = {"x": "x", "y": "y", "u": "d", "d": "u"}[toward]
        nearer = offset
        if toward == "u":
            nearer = (offset[0] - 1, offset[1], offset[2])
        if toward == "d":
            nearer = (offset[0] + 1, offset[1], offset[2])
        there = {"u": z + 1, "d": z - 1}.get(toward, z)
        index_there, _ = slot_index(
            order, seen, nearer, there, y if toward != "y" else 1 - y, x if toward != "x" else 1 - x
        )
        if toward in "xy":
            index_there, _ = slot_index(order, seen, offset, z, y, x)
        place = base[seen] + index_there
        return push(
            tree_block(piece, offset),
            slots.at[place],
            tree_send.at[piece, chip_of(offset, z, y, x)],
            tree_recv.at[piece, place],
            neighbour(toward, z, y, x, core),
        )

    def tree_step(piece, offset):
        _, result, index, order, slots = pieces[piece]
        base, _ = slot_base(order)

        def go():
            block = tree_block(piece, offset)
            sure, unsure = [], []
            for direction in onward(order, offset):
                local, _ = slot_index(order, direction, offset, z, y, x)
                place = base[direction] + local
                (sure if direction in "xy" else unsure).append((direction, place))
            terms = [block]
            for _, place in sure:
                arrived(slots.at[place], tree_recv.at[piece, place], sibling)
                terms.append(slots.at[place])
            last = hops(offset) == 0
            target = result.at[index] if last else block
            if last or len(terms) > 1:
                add_into(target, terms)
            for direction, place in unsure:

                def more(place=place):
                    arrived(slots.at[place], tree_recv.at[piece, place], sibling)
                    add_into(target, [target, slots.at[place]])

                maybe(direction_exists(direction, z), more)
            if not last:
                tree_copy(piece, offset).start()

        maybe(offset_exists(offset, z), go)

    def tree_steps(which, distances):
        for hop, _, piece, offset in events:
            if piece in which and -hop in distances:
                tree_step(piece, offset)

    def gains_copy(step):
        other = lax.rem(me + step, 32)
        return push(
            gains_part.at[lax.div(other, 4)],
            gains_buf.at[me],
            gains_send.at[step],
            gains_recv.at[me],
            (lax.div(other, 2), lax.rem(other, 2)),
        )

    def gains_start(step, carry):
        gains_copy(step).start()
        return carry

    def gains_wait(step, carry):
        other = lax.rem(me + step, 32)
        gains_copy(step).wait_send()
        arrived(gains_buf.at[other], gains_recv.at[other], sibling)
        gains_sum[...] += gains_buf[other]
        return carry

    def swap_copy(index, source, target):
        return push(source, target, swap_send.at[index], swap_recv.at[index], sibling)

    def turn(source, target, slot):
        def one(block, p):
            flat = source(p, block)
            turned[slot, p, pl.ds(2 * block, 2)] = flat.T.astype(BF16).reshape(2, 2, height, act_height)

        for p in range(positions):
            for block in range(model // 128):
                one(block, p)
            target[p, :, :, :act_height] = turned[slot, p, :, core]

    qkv_tile = qkv_tiles.shape[1]
    tile_count = model // qkv_tile

    def qkv_load(number):
        p, tile = divmod(number, tile_count)
        return pltpu.make_async_copy(
            qkv_full.at[p, pl.ds(tile * qkv_tile, qkv_tile)],
            qkv_tiles.at[number % 2],
            tile_sem.at[number % 2],
        )

    out_loads = [
        pltpu.make_async_copy(out_full.at[p], out_tiles.at[p], tile_sem.at[2 + p]) for p in range(positions)
    ]

    act_core_sends(0)
    ff_across(0)
    ff_across(1)
    load_back = act_load(0)
    for copy in load_back + out_loads + part_copies:
        copy.start()
    act_core_sends(1)
    qkv_load(0).start()
    qkv_load(1).start()
    make_spread(spread)
    gain_acc[...] = jnp.zeros_like(gain_acc)
    for copy in load_back:
        copy.wait()
    act_first(0)
    load_out = act_load(1)
    for copy in load_out:
        copy.start()

    def context_block(p, block):
        return context[p, :, 128 * block : 128 * block + 128].astype(F32)

    def attn_norm(rows):
        for p in range(positions):
            r, _ = normed(tokens_ref[p, rows, :].astype(F32))
            d_rows[p, rows, :] = r * gain_rows[p : p + 1, :]

    row_loop(act_height, 16, attn_norm)
    turn(context_block, context_turned, 0)
    turn(
        lambda p, block: d_rows[p, :, 128 * block : 128 * block + 128], attn_turned, 1
    )
    swaps = []
    for p in range(positions):
        swaps.append(
            swap_copy(
                4 * p,
                turned.at[0, p, :, 1 - core],
                context_turned.at[p, :, :, pl.ds(act_height, act_height)],
            )
        )
        swaps.append(
            swap_copy(
                4 * p + 1,
                turned.at[1, p, :, 1 - core],
                attn_turned.at[p, :, :, pl.ds(act_height, act_height)],
            )
        )
        swaps[-1].start()
        swaps[-2].start()
    act_second(0)
    for copy in part_copies:
        copy.wait()
    ff_first()
    for p in range(positions):
        probs = attention_probs(qkv_rows, halves, spread, model, p)
        for q in range(p + 1):
            probs_buf[pairs.index((p, q))] = probs[q]
    act_third(0)

    def mid_back(rows):
        for p in range(positions):
            d_ff_in = (
                core_buf[0, 0, 0, p, rows, :].astype(F32)
                + x_buf[0, 0, p, rows, :].astype(F32)
                + z_buf[0, p, rows, :].astype(F32)
            )
            r, inverse = normed(resid_mid[p, rows, :])
            gain_acc[positions + p] += r * d_ff_in
            total = cot_ref[p, rows, :] + norm_back(
                r, inverse, d_ff_in * gain_rows[positions + p : positions + p + 1, :]
            )
            d_mid[p, rows, :] = total
            d_mid_low[p, rows, :] = total.astype(BF16)

    row_loop(act_height, 16, mid_back)
    for p in range(positions):
        swaps.append(
            swap_copy(
                4 * p + 2,
                d_mid_low.at[p, pl.ds(0, act_height)],
                d_mid_low.at[p, pl.ds(act_height, act_height)],
            )
        )
        swaps[-1].start()
    for copy in out_loads:
        copy.wait()
    for p in range(positions):

        def context_back(columns, p=p):
            d_context[p, :, columns] = lax.dot_general(
                d_mid_low[p, :act_height, :],
                out_tiles[p, columns, :],
                (((1,), (1,)), ((), ())),
                preferred_element_type=F32,
            ).astype(BF16)

        tile_loop(model, 256, context_back)

    def context_products(rows):
        for index, (p, q) in enumerate(pairs):
            product = d_context[p, rows, :].astype(F32) * qkv_rows[q, rows, 2 * model :].astype(F32)
            halves[2 * index, rows, :], halves[2 * index + 1, rows, :] = split_product(product)

    row_loop(act_height, 16, context_products)
    d_probs = [sums_over_heads(halves, spread, index) for index in range(len(pairs))]
    for p in range(positions):
        own = [index for index, pair in enumerate(pairs) if pair[0] == p]
        mean = functools.reduce(jnp.add, [probs_buf[index] * d_probs[index] for index in own])
        for index in own:
            d_score = (probs_buf[index] * (d_probs[index] - mean)).astype(BF16)
            halves[2 * index] = to_heads(d_score, spread)
            halves[2 * index + 1] = to_heads(probs_buf[index].astype(BF16), spread)

    def qkv_back(rows):
        d_keys = [None] * positions
        d_values = [None] * positions

        def plus(total, term):
            return term if total is None else total + term

        for p in range(positions):
            d_query = None
            d_own = d_context[p, rows, :].astype(F32)
            query = qkv_rows[p, rows, :model].astype(F32)
            for index, (own, q) in enumerate(pairs):
                if own == p:
                    d_score = halves[2 * index, rows, :].astype(F32)
                    key = qkv_rows[q, rows, model : 2 * model].astype(F32)
                    d_query = plus(d_query, d_score * key)
                    d_keys[q] = plus(d_keys[q], d_score * query)
                    d_values[q] = plus(d_values[q], halves[2 * index + 1, rows, :].astype(F32) * d_own)
            d_qkv[p, rows, :model] = (d_query * scale).astype(BF16)
        for p in range(positions):
            d_qkv[p, rows, model : 2 * model] = (d_keys[p] * scale).astype(BF16)
            d_qkv[p, rows, 2 * model :] = d_values[p].astype(BF16)

    row_loop(act_height, 16, qkv_back)
    for p in range(positions):
        swaps.append(
            swap_copy(
                4 * p + 3,
                d_qkv.at[p, pl.ds(0, act_height)],
                d_qkv.at[p, pl.ds(act_height, act_height)],
            )
        )
        swaps[-1].start()

    def swap_wait(index, target):
        arrived(target, swap_recv.at[index], sibling)

    for p in range(positions):
        swap_wait(4 * p, context_turned.at[p, :, :, pl.ds(act_height, act_height)])
        swap_wait(4 * p + 2, d_mid_low.at[p, pl.ds(act_height, act_height)])

        def out_weights(columns, p=p):
            out_grad[p, :, columns] = jnp.dot(
                context_turned[p].reshape(half, 2 * act_height),
                d_mid_low[p, :, columns],
                preferred_element_type=F32,
            ).astype(BF16)

        tile_loop(model, 256, out_weights)
    tree_steps((2, 3), (5,))
    for copy in load_out:
        copy.wait()
    act_first(1)
    for p in range(positions):
        swap_wait(4 * p + 1, attn_turned.at[p, :, :, pl.ds(act_height, act_height)])
        swap_wait(4 * p + 3, d_qkv.at[p, pl.ds(act_height, act_height)])

        def qkv_weights(columns, p=p):
            qkv_grad[p, :, columns] = jnp.dot(
                attn_turned[p].reshape(half, 2 * act_height),
                d_qkv[p, :, columns],
                preferred_element_type=F32,
            ).astype(BF16)

        tile_loop(3 * model, 256, qkv_weights)
        tree_steps((p,), (5,))
    tree_steps((0, 1, 2, 3), (4,))
    act_second(1)
    ff_second()
    for number in range(positions * tile_count):
        p, tile = divmod(number, tile_count)
        qkv_load(number).wait()
        d_rows[p, :, tile * qkv_tile : (tile + 1) * qkv_tile] = lax.dot_general(
            d_qkv[p, :act_height, :],
            qkv_tiles[number % 2],
            (((1,), (1,)), ((), ())),
            preferred_element_type=F32,
        )
        if number + 2 < positions * tile_count:
            qkv_load(number + 2).start()
    tree_steps((0, 1, 2, 3), (3,))

    def attn_back(rows):
        for p in range(positions):
            r, inverse = normed(tokens_ref[p, rows, :].astype(F32))
            d_attn_in = d_rows[p, rows, :]
            gain_acc[p] += r * d_attn_in
            grad_tokens[p, rows, :] = d_mid[p, rows, :] + norm_back(
                r, inverse, d_attn_in * gain_rows[p : p + 1, :]
            )

    row_loop(act_height, 16, attn_back)
    gains_part[...] = jnp.zeros_like(gains_part)
    for index in range(2 * positions):
        sums = jnp.sum(gain_acc[index], axis=0, keepdims=True)
        for block in range(8):
            gains_part[block, index : index + 1, :] = sums[:, 128 * block : 128 * block + 128]
    lax.fori_loop(1, 32, gains_start, 0)
    tree_steps((0, 1, 2, 3), (2,))
    act_third(1)

    def finish_output(rows):
        for p in range(positions):
            total = (
                core_buf[1, 0, 0, p, rows, :].astype(F32)
                + x_buf[1, 0, p, rows, :].astype(F32)
                + z_buf[1, p, rows, :].astype(F32)
            )
            output[p, rows, :] = (resid_mid[p, rows, :] + total).astype(BF16)

    row_loop(act_height, 16, finish_output)
    tree_steps((0, 1, 2, 3), (1,))
    tree_steps((0, 1, 2, 3), (0,))
    ff_last()
    gains_sum[...] = gains_part[lax.div(me, 4)]
    lax.fori_loop(1, 32, gains_wait, 0)
    for _, _, piece, offset in events:
        if hops(offset) > 0:
            maybe(offset_exists(offset, z), tree_copy(piece, offset).wait_send)
    for copy in sends + swaps:
        copy.wait_send()


def backward_scatter(
    tokens,
    grads,
    gain_rows,
    qkv_rows,
    context,
    resid_mid,
    qkv_full,
    out_full,
    out_part,
    back_part,
    gate_up_grad,
    down_grad,
):
    sets, act_height, model = tokens.shape
    width = gate_up_grad.shape[2]
    height = model // 32
    down_height = down_grad.shape[1] // 4
    dma = pltpu.SemaphoreType.DMA
    vmem = pl.BlockSpec(memory_space=pltpu.VMEM)
    anywhere = pl.BlockSpec(memory_space=pl.ANY)
    places = [slot_base(order)[1] for order in ORDERS]
    pair_count = len(pairs_of(sets))
    act = (sets, act_height, model)
    return pl.pallas_call(
        backward_kernel,
        out_shape=(
            jax.ShapeDtypeStruct(act, BF16),
            jax.ShapeDtypeStruct(act, F32),
            jax.ShapeDtypeStruct((8, 128), F32),
            jax.ShapeDtypeStruct((sets, height, 3 * model), F32),
            jax.ShapeDtypeStruct((sets, height, model), F32),
            jax.ShapeDtypeStruct((8, sets, height, width), BF16),
            jax.ShapeDtypeStruct((sets, down_height, model), F32),
        ),
        in_specs=[vmem] * 6 + [anywhere] * 6,
        out_specs=(vmem,) * 7,
        scratch_shapes=[
            pltpu.VMEM((2, 2) + act, BF16),
            pltpu.VMEM((2, 2, 2) + act, BF16),
            pltpu.VMEM((2, 2) + act, BF16),
            pltpu.VMEM((2,) + act, BF16),
            pltpu.VMEM((2, sets, 2, 4 * height, width), BF16),
            pltpu.VMEM((2, sets, down_height, model), BF16),
            pltpu.VMEM((2, sets, 2, 4 * height, width), BF16),
            pltpu.VMEM((2, sets, down_height, model), BF16),
            pltpu.VMEM((sets, 2, 4 * height, width), BF16),
            pltpu.VMEM((sets, down_height, model), BF16),
            pltpu.VMEM((sets, 16 * height, 3 * model), BF16),
            pltpu.VMEM((sets, 16 * height, model), BF16),
            pltpu.VMEM((places[0], height, 3 * model), BF16),
            pltpu.VMEM((places[1], height, 3 * model), BF16),
            pltpu.VMEM((places[2], height, model), BF16),
            pltpu.VMEM((places[3], height, model), BF16),
            pltpu.VMEM((2, 128, 3 * model), BF16),
            pltpu.VMEM((sets, model, model), BF16),
            pltpu.VMEM((2, sets, 16, 2, height, act_height), BF16),
            pltpu.VMEM((sets, 16, height, 2 * act_height), BF16),
            pltpu.VMEM((sets, 16, height, 2 * act_height), BF16),
            pltpu.VMEM((sets, 2 * act_height, 3 * model), BF16),
            pltpu.VMEM((sets, 2 * act_height, model), BF16),
            pltpu.VMEM(act, F32),
            pltpu.VMEM(act, BF16),
            pltpu.VMEM(act, F32),
            pltpu.VMEM((2 * pair_count, act_height, model), BF16),
            pltpu.VMEM((pair_count, act_height, 128), F32),
            pltpu.VMEM((model, 128), BF16),
            pltpu.VMEM((2 * sets, 16, model), F32),
            pltpu.VMEM((8, 8, 128), F32),
            pltpu.VMEM((32, 8, 128), F32),
            dma((2, 2, 2)),
            dma((2, 2, 2)),
            dma((2, 2)),
            dma((2, 2)),
            dma((2,)),
            dma((2,)),
            dma((2, sets, 3)),
            dma((2, sets, 3)),
            dma((sets, 3)),
            dma((sets, 3)),
            dma((8, sets)),
            dma((8, sets)),
            dma((4 * sets,)),
            dma((4 * sets,)),
            dma((4, 16)),
            dma((4, max(places))),
            dma((32,)),
            dma((32,)),
            dma((2, 2, 2)),
            dma((2, sets, 3)),
            dma((2 + sets,)),
        ],
        compiler_params=pltpu.CompilerParams(
            collective_id=5, has_side_effects=True, vmem_limit_bytes=63 * 2**20
        ),
        name="backward_scatter",
    )(
        tokens,
        grads,
        gain_rows,
        qkv_rows,
        context,
        resid_mid,
        qkv_full,
        out_full,
        out_part,
        back_part,
        gate_up_grad,
        down_grad,
    )


def local_fast(
    tokens,
    norm_attn,
    w_qkv,
    w_out,
    norm_ff,
    w_gate_up,
    w_down,
    cotangent,
    valid_frames,
    item_lengths,
):
    frame_count, positions, model = tokens.shape
    own_gain = norm_attn.shape[1]
    device_index = lax.axis_index(("dp", "pair"))
    local_ids = jnp.arange(frame_count, dtype=jnp.int32)
    frame_ids = device_index * frame_count + local_ids
    item_ends = jnp.cumsum(item_lengths)
    item_starts = item_ends - item_lengths
    in_item = (frame_ids[:, None] >= item_starts[None, :]) & (
        frame_ids[:, None] < item_ends[None, :]
    )
    item_share = 8 * frame_count / item_lengths.astype(F32)
    frame_weight = jnp.sum(jnp.where(in_item, item_share[None, :], 0.0), axis=1)
    frame_weight = jnp.where(local_ids < valid_frames[0], frame_weight, 0.0)
    grad_out = jnp.swapaxes(cotangent, 0, 1).astype(F32) * frame_weight[None, :, None]
    grad_low = grad_out.astype(BF16)

    unit_gains = jnp.concatenate([norm_attn, norm_ff], axis=0)
    lanes = jnp.arange(128, dtype=jnp.int32) // own_gain
    gains = jnp.where(lanes == lax.rem(device_index, 128 // own_gain), jnp.tile(unit_gains, (1, 128 // own_gain)), 0)
    gains = jnp.pad(gains, ((0, 16 - 2 * positions), (0, 0)))

    unit = w_down.shape[1]
    parts = w_gate_up.reshape(positions, -1, 2, 2, 2, 2, 2, 2, unit)
    parts = parts.transpose(4, 6, 7, 0, 1, 2, 3, 5, 8)
    parts = parts.reshape(8, positions, w_gate_up.shape[1], 8 * unit)
    tokens_low = jnp.swapaxes(tokens, 0, 1)
    (
        gains_rows,
        qkv,
        context,
        resid_mid,
        qkv_full,
        out_full,
        out_part,
        back_part,
        gate_up_grad,
        down_grad,
    ) = forward_gather(gains, tokens_low, w_qkv, w_out, parts, w_down, grad_low)
    output, grad_tokens, gains_sum, share_qkv, share_out, gate_up_sum, down_sum = backward_scatter(
        tokens_low,
        grad_out,
        gains_rows,
        qkv,
        context,
        resid_mid,
        qkv_full,
        out_full,
        out_part,
        back_part,
        gate_up_grad,
        down_grad,
    )
    output = jnp.swapaxes(output, 0, 1)
    grad_tokens = jnp.swapaxes(grad_tokens, 0, 1)
    share_gate_up = gate_up_sum.reshape(2, 2, 2, positions, -1, 2, 2, 2, unit)
    share_gate_up = share_gate_up.transpose(3, 4, 5, 6, 0, 7, 1, 2, 8)
    share_gate_up = share_gate_up.reshape(w_gate_up.shape).astype(F32)
    shift = lax.rem(device_index, 128 // own_gain) * own_gain
    gain_grads = lax.dynamic_slice(gains_sum, (0, shift), (2 * positions, own_gain))
    return (
        output,
        grad_tokens,
        gain_grads[:positions],
        share_qkv,
        share_out,
        gain_grads[positions:],
        share_gate_up,
        down_sum,
    )


def solution(mesh):
    in_specs = (
        P(("dp", "pair"), None, None),
        P(None, ("dp", "pair")),
        P(None, ("dp", "pair"), None),
        P(None, ("dp", "pair"), None),
        P(None, ("dp", "pair")),
        P(None, ("dp", "pair"), None),
        P(None, ("dp", "pair"), None),
        P(("dp", "pair"), None, None),
        P(("dp", "pair")),
        P(),
    )
    out_specs = (
        P(("dp", "pair"), None, None),
        P(("dp", "pair"), None, None),
        P(None, ("dp", "pair")),
        P(None, ("dp", "pair"), None),
        P(None, ("dp", "pair"), None),
        P(None, ("dp", "pair")),
        P(None, ("dp", "pair"), None),
        P(None, ("dp", "pair"), None),
    )
    body = local_fast if mesh.shape["dp"] == 16 and mesh.shape["pair"] == 2 else local
    return jax.shard_map(body, mesh=mesh, in_specs=in_specs, out_specs=out_specs, check_vma=False)
```

```python
import functools
import math

import jax
import jax.numpy as jnp
from jax import lax
from jax.experimental import pallas as pl
from jax.experimental.pallas import tpu as pltpu
from jax.sharding import PartitionSpec as P

HEAD_DIM = 64


def per_pos(activations, weight):
    return jnp.einsum("fgk,gke->fge", activations, weight, preferred_element_type=jnp.float32)


def per_pos_back(gradients, weight):
    return jnp.einsum("fge,gke->fgk", gradients, weight, preferred_element_type=jnp.float32)


def pos_grad(activations, gradients):
    return jnp.einsum("fgk,fge->kge", activations, gradients, preferred_element_type=jnp.float32)


def gain_grad(normed_rows, gradients):
    return jnp.transpose(jnp.sum(normed_rows * gradients, axis=0))


def back_layout(share):
    return jnp.swapaxes(share, 0, 1)


def normed(values):
    inverse = lax.rsqrt(jnp.mean(values * values, axis=-1, keepdims=True) + 1e-05)
    return (values * inverse, inverse)


def norm_back(normed_rows, inverse, gradients):
    return inverse * (
        gradients - normed_rows * jnp.mean(gradients * normed_rows, axis=-1, keepdims=True)
    )


def gather_ff_fwd(norm_ff, w_gate_up, w_down, start, group):
    return (
        lax.all_gather(norm_ff[start : start + group], ("dp", "pair"), axis=1, tiled=True),
        lax.all_gather(w_gate_up[start : start + group], ("dp", "pair"), axis=1, tiled=True),
        lax.all_gather(w_down[start : start + group], ("dp", "pair"), axis=1, tiled=True),
    )


def gather_ff_back(norm_ff, w_gate_up, w_down, start, group):
    return (
        lax.all_gather(norm_ff[start : start + group], ("dp", "pair"), axis=1, tiled=True),
        lax.all_gather(w_gate_up[start : start + group], ("dp", "pair"), axis=1, tiled=True),
        lax.all_gather(w_down[start : start + group], ("dp", "pair"), axis=1, tiled=True),
    )


def local(
    tokens,
    norm_attn,
    w_qkv,
    w_out,
    norm_ff,
    w_gate_up,
    w_down,
    cotangent,
    valid_frames,
    item_lengths,
):
    frame_count, positions, model_width = tokens.shape
    head_count = model_width // HEAD_DIM
    ff_units = w_gate_up.shape[2] // 2
    score_scale = 1.0 / math.sqrt(HEAD_DIM)
    causal = jnp.arange(positions)[:, None] >= jnp.arange(positions)[None, :]
    head_shape = (frame_count, positions, head_count, HEAD_DIM)
    group = 1
    gains_attn, qkv_full, out_full = (
        lax.all_gather(norm_attn, ("dp", "pair"), axis=1, tiled=True),
        lax.all_gather(w_qkv, ("dp", "pair"), axis=1, tiled=True),
        lax.all_gather(w_out, ("dp", "pair"), axis=1, tiled=True),
    )
    resid_in = tokens.astype(jnp.float32)
    normed_one, inverse_one = normed(resid_in)
    attn_in = (normed_one * gains_attn.astype(jnp.float32)[None]).astype(jnp.bfloat16)
    qkv_rows = per_pos(attn_in, qkv_full).astype(jnp.bfloat16)
    queries = qkv_rows[..., :model_width].reshape(head_shape)
    key_heads = qkv_rows[..., model_width : 2 * model_width].reshape(head_shape)
    value_heads = qkv_rows[..., 2 * model_width :].reshape(head_shape)
    scores = (
        jnp.einsum("fphd,fqhd->fhpq", queries, key_heads, preferred_element_type=jnp.float32)
        * score_scale
    )
    scores = jnp.where(causal, scores, -1e30)
    row_max = jnp.max(scores, axis=-1, keepdims=True)
    attn_probs = jnp.exp(scores - row_max)
    attn_probs = attn_probs / jnp.sum(attn_probs, axis=-1, keepdims=True)
    probs_low = attn_probs.astype(jnp.bfloat16)
    context = jnp.einsum(
        "fhpq,fqhd->fphd", probs_low, value_heads, preferred_element_type=jnp.float32
    )
    context = context.astype(jnp.bfloat16).reshape(frame_count, positions, model_width)
    resid_mid = resid_in + per_pos(context, out_full)
    kept_parts = []
    out_parts = []
    for start in range(0, positions, group):
        gains_ff, gate_up_full, down_full = gather_ff_fwd(norm_ff, w_gate_up, w_down, start, group)
        mid_part = resid_mid[:, start : start + group]
        normed_two, inverse_two = normed(mid_part)
        ff_in = (normed_two * gains_ff.astype(jnp.float32)[None]).astype(jnp.bfloat16)
        gate_up = per_pos(ff_in, gate_up_full)
        gate_part = gate_up[..., :ff_units]
        up_part = gate_up[..., ff_units:]
        sigmoid_gate = jax.nn.sigmoid(gate_part)
        silu_gate = gate_part * sigmoid_gate
        hidden = (silu_gate * up_part).astype(jnp.bfloat16)
        out_parts.append(mid_part + per_pos(hidden, down_full))
        kept_parts.append(
            (normed_two, inverse_two, ff_in, gate_part, up_part, sigmoid_gate, silu_gate, hidden)
        )
    output = jnp.concatenate(out_parts, axis=1).astype(jnp.bfloat16)
    device_index = lax.axis_index(("dp", "pair"))
    local_ids = jnp.arange(frame_count, dtype=jnp.int32)
    frame_ids = device_index * frame_count + local_ids
    item_ends = jnp.cumsum(item_lengths)
    item_starts = item_ends - item_lengths
    in_item = (frame_ids[:, None] >= item_starts[None, :]) & (
        frame_ids[:, None] < item_ends[None, :]
    )
    item_share = 8 * frame_count / item_lengths.astype(jnp.float32)
    frame_weight = jnp.sum(jnp.where(in_item, item_share[None, :], 0.0), axis=1)
    frame_weight = jnp.where(local_ids < valid_frames[0], frame_weight, 0.0)
    grad_out = cotangent.astype(jnp.float32) * frame_weight[:, None, None]
    mid_grads = []
    share_norm_ff_parts = []
    share_gate_up_parts = []
    share_down_parts = []
    for index, start in enumerate(range(0, positions, group)):
        normed_two, inverse_two, ff_in, gate_part, up_part, sigmoid_gate, silu_gate, hidden = (
            kept_parts[index]
        )
        gains_ff, gate_up_full, down_full = gather_ff_back(norm_ff, w_gate_up, w_down, start, group)
        grad_part = grad_out[:, start : start + group]
        grad_low = grad_part.astype(jnp.bfloat16)
        grad_down = pos_grad(hidden, grad_low)
        d_hidden = per_pos_back(grad_low, down_full)
        d_gate = d_hidden * up_part * sigmoid_gate * (1.0 + gate_part * (1.0 - sigmoid_gate))
        d_up = d_hidden * silu_gate
        d_gate_up = jnp.concatenate([d_gate, d_up], axis=-1).astype(jnp.bfloat16)
        grad_gate_up = pos_grad(ff_in, d_gate_up)
        d_ff_in = per_pos_back(d_gate_up, gate_up_full)
        grad_norm_ff = gain_grad(normed_two, d_ff_in)
        mid_grads.append(
            grad_part
            + norm_back(normed_two, inverse_two, d_ff_in * gains_ff.astype(jnp.float32)[None])
        )
        share_a, share_b, share_c = (
            lax.psum_scatter(grad_norm_ff, ("dp", "pair"), scatter_dimension=0, tiled=True),
            lax.psum_scatter(grad_gate_up, ("dp", "pair"), scatter_dimension=0, tiled=True),
            lax.psum_scatter(grad_down, ("dp", "pair"), scatter_dimension=0, tiled=True),
        )
        share_norm_ff_parts.append(jnp.transpose(share_a))
        share_gate_up_parts.append(back_layout(share_b))
        share_down_parts.append(back_layout(share_c))
    d_mid = jnp.concatenate(mid_grads, axis=1)
    gains_attn, qkv_full, out_full = (
        lax.all_gather(norm_attn, ("dp", "pair"), axis=1, tiled=True),
        lax.all_gather(w_qkv, ("dp", "pair"), axis=1, tiled=True),
        lax.all_gather(w_out, ("dp", "pair"), axis=1, tiled=True),
    )
    d_mid_low = d_mid.astype(jnp.bfloat16)
    grad_out_proj = pos_grad(context, d_mid_low)
    d_context = per_pos_back(d_mid_low, out_full).astype(jnp.bfloat16).reshape(head_shape)
    d_probs = jnp.einsum(
        "fphd,fqhd->fhpq", d_context, value_heads, preferred_element_type=jnp.float32
    )
    d_values = jnp.einsum(
        "fhpq,fphd->fqhd", probs_low, d_context, preferred_element_type=jnp.float32
    )
    d_scores = attn_probs * (d_probs - jnp.sum(attn_probs * d_probs, axis=-1, keepdims=True))
    d_scores = d_scores.astype(jnp.bfloat16)
    d_queries = (
        jnp.einsum("fhpq,fqhd->fphd", d_scores, key_heads, preferred_element_type=jnp.float32)
        * score_scale
    )
    d_keys = (
        jnp.einsum("fhpq,fphd->fqhd", d_scores, queries, preferred_element_type=jnp.float32)
        * score_scale
    )
    row_shape = (frame_count, positions, model_width)
    d_qkv = jnp.concatenate(
        [d_queries.reshape(row_shape), d_keys.reshape(row_shape), d_values.reshape(row_shape)],
        axis=-1,
    ).astype(jnp.bfloat16)
    grad_qkv = pos_grad(attn_in, d_qkv)
    d_attn_in = per_pos_back(d_qkv, qkv_full)
    grad_norm_attn = gain_grad(normed_one, d_attn_in)
    grad_tokens = d_mid + norm_back(
        normed_one, inverse_one, d_attn_in * gains_attn.astype(jnp.float32)[None]
    )
    share_norm_attn, share_qkv, share_out = (
        lax.psum_scatter(grad_norm_attn, ("dp", "pair"), scatter_dimension=0, tiled=True),
        lax.psum_scatter(grad_qkv, ("dp", "pair"), scatter_dimension=0, tiled=True),
        lax.psum_scatter(grad_out_proj, ("dp", "pair"), scatter_dimension=0, tiled=True),
    )
    share_norm_attn = jnp.transpose(share_norm_attn)
    share_qkv = back_layout(share_qkv)
    share_out = back_layout(share_out)
    share_norm_ff = jnp.concatenate(share_norm_ff_parts, axis=0)
    share_gate_up = jnp.concatenate(share_gate_up_parts, axis=0)
    share_down = jnp.concatenate(share_down_parts, axis=0)
    return (
        output,
        grad_tokens,
        share_norm_attn,
        share_qkv,
        share_out,
        share_norm_ff,
        share_gate_up,
        share_down,
    )


MESH_ID = pl.DeviceIdType.MESH
BF16 = jnp.bfloat16
F32 = jnp.float32


def here():
    dp = lax.axis_index("dp")
    core = lax.axis_index("pair")
    return lax.div(dp, 4), lax.rem(lax.div(dp, 2), 2), lax.rem(dp, 2), core


def flip(value, bit):
    return 1 - value if bit else value


def push(src, dst, send_sem, recv_sem, to):
    return pltpu.make_async_remote_copy(
        src_ref=src,
        dst_ref=dst,
        send_sem=send_sem,
        recv_sem=recv_sem,
        device_id=to,
        device_id_type=MESH_ID,
    )


def arrived(dst, recv_sem, to):
    push(dst, dst, recv_sem, recv_sem, to).wait_recv()


def greet_all(z, y, x, core):
    barrier = pltpu.get_barrier_semaphore()
    me = 2 * (z * 4 + y * 2 + x) + core

    def one(step, carry):
        other = lax.rem(me + step, 32)
        pl.semaphore_signal(
            barrier, inc=1, device_id=(lax.div(other, 2), lax.rem(other, 2)), device_id_type=MESH_ID
        )
        return carry

    lax.fori_loop(1, 32, one, 0)
    pl.semaphore_wait(barrier, 31)


def greet(peers):
    barrier = pltpu.get_barrier_semaphore()
    for to in peers:
        pl.semaphore_signal(barrier, inc=1, device_id=to, device_id_type=MESH_ID)
    pl.semaphore_wait(barrier, len(peers))


def maybe(condition, do):
    if condition is None:
        do()
    else:
        pl.when(condition)(do)


OFFSETS = [
    (dz, dy, dx) for dz in (0, -1, 1, -2, 2, -3, 3) for dy in (0, 1) for dx in (0, 1)
]
ORDERS = ("zxy", "zyx", "xyz", "yxz")


def hops(offset):
    return abs(offset[0]) + offset[1] + offset[2]


def arrival_axis(order, offset):
    part = dict(z=offset[0], y=offset[1], x=offset[2])
    last = None
    for axis in order:
        if part[axis] != 0:
            last = axis
    return last


def onward(order, offset):
    directions = []
    last = arrival_axis(order, offset)
    start = 0
    if last is not None:
        start = order.index(last) + 1
        if last == "z":
            directions.append("u" if offset[0] < 0 else "d")
    for axis in order[start:]:
        directions.extend(["u", "d"] if axis == "z" else [axis])
    return directions


def came_from(order, offset):
    last = arrival_axis(order, offset)
    if last == "z":
        return "d" if offset[0] < 0 else "u"
    return last


def offset_exists(offset, z):
    if offset[0] < 0:
        return z >= -offset[0]
    if offset[0] > 0:
        return z <= 3 - offset[0]
    return None


def direction_exists(direction, z):
    return {"u": z < 3, "d": z > 0}.get(direction)


DIRECTIONS = ("x", "y", "u", "d", "s")


def neighbour(direction, z, y, x, core):
    if direction == "x":
        return (z * 4 + y * 2 + 1 - x, core)
    if direction == "y":
        return (z * 4 + (1 - y) * 2 + x, core)
    if direction == "u":
        return (z * 4 + 4 + y * 2 + x, core)
    if direction == "d":
        return (z * 4 - 4 + y * 2 + x, core)
    return (z * 4 + y * 2 + x, 1 - core)


def chip_of(offset, z, y, x):
    return (z + offset[0]) * 4 + flip(y, offset[1]) * 2 + flip(x, offset[2])


RANK_STEPS = sorted(
    ((dl, dx, dc) for dl in (0, 1) for dx in (0, 1) for dc in (0, 1)), key=lambda step: (sum(step), step)
)


def group_place(z, y, x, core):
    zh, zl = lax.div(z, 2), lax.rem(z, 2)

    def member(step):
        return ((2 * zh + flip(zl, step[0])) * 4 + y * 2 + flip(x, step[1]), flip(core, step[2]))

    def rank(step):
        return 4 * flip(zl, step[0]) + 2 * flip(x, step[1]) + flip(core, step[2])

    def device(step, dzh=0, dy=0):
        return 16 * flip(zh, dzh) + 4 * flip(y, dy) + 8 * flip(zl, step[0]) + 2 * flip(x, step[1]) + flip(core, step[2])

    far = ((2 * (1 - zh) + zl) * 4 + y * 2 + x, core)
    across = (z * 4 + (1 - y) * 2 + x, core)
    return zh, zl, member, rank, device, far, across


def add_into(target, sources, rows=16, columns=1024):
    height, width = target.shape
    across = width // columns

    def one(step, carry):
        top = pl.multiple_of(lax.div(step, across) * rows, rows)
        left = pl.multiple_of(lax.rem(step, across) * columns, columns)
        spot = (pl.ds(top, rows), pl.ds(left, columns))
        total = sources[0][spot].astype(F32)
        for source in sources[1:]:
            total = total + source[spot].astype(F32)
        target[spot] = total.astype(target.dtype)
        return carry

    lax.fori_loop(0, (height // rows) * across, one, 0)


def row_loop(height, chunk, body):
    def one(step, carry):
        body(pl.ds(pl.multiple_of(step * chunk, chunk), chunk))
        return carry

    lax.fori_loop(0, height // chunk, one, 0)


def tile_loop(width, tile, body):
    def one(step, carry):
        body(pl.ds(pl.multiple_of(step * tile, tile), tile))
        return carry

    lax.fori_loop(0, width // tile, one, 0)


def dot(left, right):
    return jnp.dot(left, right, preferred_element_type=F32)


def dot_back(left, right):
    return lax.dot_general(left, right, (((1,), (1,)), ((), ())), preferred_element_type=F32)


def dot_grad(left, right):
    return lax.dot_general(left, right, (((0,), (0,)), ((), ())), preferred_element_type=F32)


def make_spread(spread):
    height, width = spread.shape
    head = lax.broadcasted_iota(jnp.int32, (height, width), 0) // HEAD_DIM
    spread[...] = jnp.where(
        head == lax.broadcasted_iota(jnp.int32, (height, width), 1), 1.0, 0.0
    ).astype(BF16)


def pairs_of(positions):
    return [(p, q) for p in range(positions) for q in range(p + 1)]


def split_product(product):
    high = product.astype(BF16)
    return high, (product - high.astype(F32)).astype(BF16)


def sums_over_heads(halves, spread, index):
    return dot(halves[2 * index], spread[...]) + dot(halves[2 * index + 1], spread[...])


def to_heads(values, spread):
    return dot_back(values, spread[...]).astype(BF16)


def attention_probs(qkv, halves, spread, model, position):
    height = qkv.shape[1]
    scale = 1.0 / math.sqrt(HEAD_DIM)

    def products(rows):
        for q in range(position + 1):
            product = qkv[position, rows, :model].astype(F32) * qkv[
                q, rows, model : 2 * model
            ].astype(F32)
            halves[2 * q, rows, :], halves[2 * q + 1, rows, :] = split_product(product)

    row_loop(height, 16, products)
    scores = [sums_over_heads(halves, spread, q) * scale for q in range(position + 1)]
    top = functools.reduce(jnp.maximum, scores)
    powers = [jnp.exp(score - top) for score in scores]
    total = functools.reduce(jnp.add, powers)
    return [power / total for power in powers]


FORWARD_STEPS = [
    ("tree", 3, 0, 0, 0), ("tree", 5, 0, 0, 0), ("tree", 0, 0, 0, 0), ("tree", 2, 0, 0, 0),
    ("tree", 5, 1, 0, 0), ("parts",), ("to_rank", 0, 7), ("tree", 0, -1, 0, 0), ("tree", 0, 0, 0, 1),
    ("to_rank", 0, 3), ("tree", 2, 0, 0, 1), ("tree", 1, 0, 0, 0), ("tree", 0, -2, 0, 0), ("cot",),
    ("rank_far", 0, 3), ("tree", 0, 0, 1, 0), ("tree", 4, 0, 0, 0), ("to_rank", 1, 4), ("tree", 1, -1, 0, 0),
    ("to_rank", 0, 2), ("to_rank", 1, 2), ("tree", 2, 0, 1, 1), ("tree", 0, 1, 0, 0), ("tree", 2, 0, 1, 0),
    ("own_across", 0, 0), ("tree", 1, 1, 0, 0), ("tree", 2, -1, 0, 0), ("tree", 0, -1, 0, 1),
    ("tree", 0, -3, 0, 0), ("to_rank", 0, 1), ("tree", 0, -2, 0, 1), ("tree", 1, 0, 1, 0),
    ("tree", 2, 1, 0, 1), ("tree", 0, 2, 0, 0), ("grads", 0), ("to_rank", 0, 6), ("rank_far", 0, 1),
    ("own_across", 1, 8), ("tree", 2, -2, 0, 0), ("own_across", 0, 8), ("tree", 2, -1, 1, 0),
    ("to_rank", 0, 5), ("rank_far", 0, 2), ("tree", 3, 0, 0, 1), ("own_far", 0, 8), ("tree", 1, -1, 1, 0),
    ("tree", 2, -1, 1, 1), ("far_across", 0, 2), ("rank_far", 0, 6), ("tree", 3, 0, 1, 1), ("gains",),
    ("tree", 2, 1, 0, 0), ("tree", 1, 2, 0, 0), ("rank_across", 0, 3), ("tree", 1, -2, 0, 0),
    ("tree", 0, 3, 0, 0), ("tree", 2, 1, 1, 1), ("tree", 5, 0, 0, 1), ("tree", 2, 2, 0, 0), ("to_rank", 0, 4),
    ("tree", 1, 2, 1, 0), ("tree", 3, -1, 0, 0), ("tree", 4, 1, 0, 0), ("tree", 0, -1, 1, 1),
    ("tree", 0, 2, 0, 1), ("rank_far", 0, 7), ("rank_far", 0, 4), ("far_across", 0, 3), ("tree", 2, 2, 1, 1),
    ("tree", 1, 3, 0, 0), ("tree", 1, 1, 1, 0), ("rank_across", 0, 1), ("to_rank", 1, 6),
    ("tree", 2, -3, 0, 0), ("tree", 0, -3, 0, 1), ("tree", 0, 0, 1, 1), ("tree", 1, 2, 0, 1),
    ("tree", 2, 1, 1, 0), ("tree", 2, -1, 0, 1), ("tree", 1, 0, 1, 1), ("tree", 2, -2, 1, 0),
    ("tree", 2, 3, 1, 1), ("far_across", 0, 6), ("own_far", 0, 0), ("tree", 1, -2, 0, 1),
    ("tree", 0, 2, 1, 1), ("tree", 4, 2, 0, 0), ("tree", 1, 3, 0, 1), ("tree", 3, 1, 0, 0),
    ("tree", 2, -2, 1, 1), ("rank_far", 0, 5), ("tree", 0, -2, 1, 1), ("tree", 0, 1, 1, 0),
    ("tree", 5, 0, 1, 0), ("far_across", 0, 1), ("tree", 1, -2, 1, 0), ("tree", 1, 2, 1, 1),
    ("tree", 2, 2, 1, 0), ("tree", 1, -3, 0, 0), ("to_rank", 1, 5), ("tree", 0, -1, 1, 0),
    ("tree", 3, -2, 0, 0), ("tree", 1, 3, 1, 0), ("act_z", 1, 0), ("tree", 0, 1, 0, 1), ("tree", 3, 1, 0, 1),
    ("tree", 2, 2, 0, 1), ("tree", 0, 3, 1, 0), ("tree", 4, -1, 0, 0), ("tree", 2, -2, 0, 1),
    ("tree", 2, -3, 1, 1), ("tree", 0, -3, 1, 1), ("far_across", 0, 7), ("tree", 0, -3, 1, 0),
    ("tree", 0, 2, 1, 0), ("tree", 3, 1, 1, 0), ("tree", 2, -3, 1, 0), ("tree", 1, -1, 0, 1),
    ("tree", 1, -3, 1, 0), ("rank_across", 0, 7), ("far_across", 0, 0), ("tree", 1, 3, 1, 1),
    ("tree", 3, 2, 0, 0), ("tree", 2, 3, 0, 0), ("rank_across", 0, 6), ("tree", 5, 1, 1, 0),
    ("tree", 0, 3, 0, 1), ("tree", 1, -3, 0, 1), ("tree", 3, -2, 0, 1), ("act_c", 1, 0, 0, 0),
    ("tree", 4, 0, 1, 0), ("tree", 5, 0, 1, 1), ("tree", 4, -2, 0, 0), ("far_across", 0, 4), ("grads", 1),
    ("tree", 2, -3, 0, 1), ("tree", 5, -1, 1, 0), ("tree", 1, -3, 1, 1), ("act_c", 1, 0, 1, 0),
    ("far_across", 0, 8), ("tree", 5, 1, 0, 1), ("far_across", 0, 5), ("tree", 1, -1, 1, 1),
    ("tree", 1, 0, 0, 1), ("rank_across", 0, 5), ("tree", 5, -1, 0, 0), ("tree", 3, -3, 0, 0),
    ("to_rank", 1, 1), ("act_x", 1, 0, 1), ("tree", 1, 1, 0, 1), ("tree", 5, 2, 1, 0), ("own_far", 1, 8),
    ("act_x", 1, 0, 0), ("tree", 5, -1, 0, 1), ("tree", 4, -3, 0, 0), ("tree", 0, 1, 1, 1),
    ("tree", 1, 1, 1, 1), ("tree", 2, 3, 0, 1), ("tree", 3, 1, 1, 1), ("tree", 3, -1, 0, 1),
    ("tree", 4, -1, 1, 0), ("tree", 3, -3, 0, 1), ("tree", 3, 2, 0, 1), ("own_across", 1, 0),
    ("tree", 1, -2, 1, 1), ("to_rank", 1, 3), ("tree", 3, 0, 1, 0), ("tree", 0, 3, 1, 1),
    ("tree", 0, -2, 1, 0), ("tree", 3, 2, 1, 0), ("tree", 2, 3, 1, 0), ("tree", 3, 3, 0, 0), ("tree_end", 0),
    ("tree", 4, -1, 1, 1), ("to_rank", 1, 7), ("attention", 0), ("tree", 4, 3, 0, 0), ("act_x", 0, 0, 0),
    ("tree", 4, 3, 1, 0), ("tree", 3, -3, 1, 0), ("tree", 4, 3, 0, 1), ("tree", 4, -2, 1, 0),
    ("tree", 3, 3, 0, 1), ("tree", 5, -1, 1, 1), ("rank_far", 1, 7), ("rank_across", 0, 2),
    ("tree", 4, 2, 1, 0), ("tree", 5, 1, 1, 1), ("tree", 5, 3, 1, 0), ("tree", 4, -3, 0, 1),
    ("rank_across", 0, 4), ("tree", 4, -3, 1, 0), ("own_far", 1, 0), ("rank_far", 1, 2), ("tree", 4, 3, 1, 1),
    ("rank_across", 1, 7), ("far_across", 1, 8), ("tree", 4, 1, 1, 0), ("act_z", 1, 1), ("tree", 5, -2, 0, 1),
    ("tree", 4, -3, 1, 1), ("tree", 3, 2, 1, 1), ("tree", 5, -2, 0, 0), ("act_z", 0, 0), ("tree", 4, 2, 1, 1),
    ("tree", 5, 2, 0, 0), ("rank_far", 1, 1), ("ff_end", 0), ("act_c", 0, 0, 1, 0), ("rank_across", 1, 2),
    ("tree", 4, 0, 0, 1), ("tree", 4, 1, 1, 1), ("rank_far", 1, 5), ("act_x", 1, 1, 0), ("tree", 3, -1, 1, 0),
    ("tree", 5, 2, 1, 1), ("tree", 5, 3, 0, 0), ("far_across", 1, 7), ("tree", 3, 3, 1, 1),
    ("tree", 3, -1, 1, 1), ("tree", 4, -2, 1, 1), ("act_c", 1, 0, 0, 1), ("act_c", 0, 0, 0, 0),
    ("tree", 4, 0, 1, 1), ("rank_far", 1, 3), ("act_c", 1, 0, 1, 1), ("tree", 3, -2, 1, 0),
    ("tree", 5, -2, 1, 0), ("rank_far", 1, 4), ("far_across", 1, 0), ("tree", 5, -3, 0, 0),
    ("tree", 4, 1, 0, 1), ("tree", 3, -2, 1, 1), ("act_c", 1, 1, 1, 0), ("rank_far", 1, 6),
    ("tree", 4, -1, 0, 1), ("tree", 5, 2, 0, 1), ("tree", 5, -3, 1, 0), ("act_c", 0, 0, 0, 1),
    ("far_across", 1, 2), ("act_c", 1, 1, 0, 0), ("tree", 5, -3, 0, 1), ("tree", 5, -2, 1, 1),
    ("tree", 3, 3, 1, 0), ("rank_across", 1, 6), ("rank_across", 1, 3), ("tree", 5, 3, 1, 1),
    ("rank_across", 1, 4), ("block", 0, 1), ("tree", 4, 2, 0, 1), ("tree", 5, 3, 0, 1), ("tree", 4, -2, 0, 1),
    ("tree", 3, -3, 1, 1), ("far_across", 1, 1), ("tree", 5, -3, 1, 1), ("block", 0, 0),
    ("rank_across", 1, 5), ("act_x", 1, 1, 1), ("tree_end", 1), ("attention", 1), ("far_across", 1, 3),
    ("rank_across", 1, 1), ("act_x", 0, 0, 1), ("block", 0, 2), ("far_across", 1, 5), ("act_c", 0, 0, 1, 1),
    ("block", 0, 3), ("down_grad", 0), ("act_c", 1, 1, 0, 1), ("far_across", 1, 6), ("act_x", 0, 1, 0),
    ("act_c", 1, 1, 1, 1), ("act_z", 0, 1), ("far_across", 1, 4), ("gate_grad", 0), ("act_c", 0, 1, 0, 1),
    ("act_c", 0, 1, 0, 0), ("ff_end", 1), ("act_c", 0, 1, 1, 0), ("block", 1, 1), ("block", 1, 2),
    ("act_x", 0, 1, 1), ("block", 1, 0), ("act_c", 0, 1, 1, 1), ("block", 1, 3), ("down_grad", 1),
    ("gate_grad", 1),
]


def forward_kernel(
    valid_ref,
    lengths_ref,
    norm_attn_ref,
    norm_ff_ref,
    tokens_ref,
    cot_ref,
    qkv_ref,
    out_ref,
    gate_up_ref,
    down_ref,
    gain_rows,
    cot_rows,
    qkv_rows,
    context,
    resid_mid,
    qkv_full,
    out_full,
    ff_out,
    ff_back,
    gate_up_grad,
    down_grad,
    qkv_buf,
    out_buf,
    gate_up_buf,
    down_buf,
    rows_buf,
    grads_buf,
    hidden,
    d_gate_up,
    out_stage,
    back_stage,
    gate_up_stage,
    down_stage,
    gains_own,
    gains_all,
    gate_up_raw,
    gate_up_parts,
    grads_own,
    attn_in,
    halves,
    spread,
    plane_sem,
    sibling_sem,
    send_sem,
    gains_send,
    gains_recv,
    rank_send,
    rank_recv,
    far_send,
    far_recv,
    across_send,
    across_recv,
    act_send,
    act_recv,
    local_sem,
    keep_sem,
    stage_sem,
):
    z, y, x, core = here()
    me = 2 * (z * 4 + y * 2 + x) + core
    zh, zl, member, rank, device, far, across = group_place(z, y, x, core)
    own_step = (0, 0, 0)
    act_height, positions, model = tokens_ref.shape
    height = gate_up_ref.shape[1]
    down_height = down_ref.shape[1]
    split = 4 * down_height
    sibling = neighbour("s", z, y, x, core)
    greet_all(z, y, x, core)
    part = qkv_ref.shape[2] // 2
    pieces = []
    for s in range(positions):
        pieces.append((qkv_ref, qkv_buf, s, pl.ds(0, part), "zxy"))
        pieces.append((qkv_ref, qkv_buf, s, pl.ds(part, part), "zyx"))
        pieces.append((out_ref, out_buf, s, pl.ds(0, model), ("xyz", "yxz")[s % 2]))

    def piece_rows(piece, number):
        _, full, index, columns, _ = pieces[piece]
        return full.at[index, pl.ds(pl.multiple_of(number * height, height), height), columns]

    def tree_send(piece, offset, direction):
        source, _, index, columns, _ = pieces[piece]
        chip = chip_of(offset, z, y, x)
        block = piece_rows(piece, 2 * chip + core)
        recv = sibling_sem if direction == "s" else plane_sem
        return push(
            source.at[index, :, columns] if hops(offset) == 0 else block,
            block,
            send_sem.at[piece, chip, DIRECTIONS.index(direction)],
            recv.at[piece, chip],
            neighbour(direction, z, y, x, core),
        )

    def tree_step(piece, offset, finish=False):
        order = pieces[piece][4]

        def go():
            chip = chip_of(offset, z, y, x)
            if hops(offset) > 0 and not finish:
                arrived(piece_rows(piece, 2 * chip + core), plane_sem.at[piece, chip], sibling)
            for direction in onward(order, offset) + ["s"]:
                copy = tree_send(piece, offset, direction)
                maybe(direction_exists(direction, z), copy.wait_send if finish else copy.start)

        maybe(offset_exists(offset, z), go)

    events = sorted(
        (
            (hops(offset), place, piece, offset)
            for piece in range(len(pieces))
            for place, offset in enumerate(OFFSETS)
        ),
        key=lambda event: event[:3],
    )

    def tree_steps(s, distance):
        for hop, _, piece, offset in events:
            if hop == distance and pieces[piece][2] == s:
                tree_step(piece, offset)

    def tree_end(s):
        mine = [piece for piece in range(len(pieces)) if pieces[piece][2] == s]

        def sibling_wait(chip, carry):
            for piece in mine:
                arrived(piece_rows(piece, 2 * chip + 1 - core), sibling_sem.at[piece, chip], sibling)
            return carry

        lax.fori_loop(0, 16, sibling_wait, 0)
        for piece in mine:
            tree_own[piece].wait()

    tree_own = [
        pltpu.make_async_copy(
            source.at[index, :, columns], piece_rows(piece, me), local_sem.at[piece]
        )
        for piece, (source, _, index, columns, _) in enumerate(pieces)
    ]

    def gains_copy(step):
        other = lax.rem(me + step, 32)
        return push(
            gains_own,
            gains_all.at[me],
            gains_send.at[step],
            gains_recv.at[me],
            (lax.div(other, 2), lax.rem(other, 2)),
        )

    def gains_start(step, carry):
        gains_copy(step).start()
        return carry

    def gains_wait(step, carry):
        other = lax.rem(me + step, 32)
        gains_copy(step).wait_send()
        arrived(gains_all.at[other], gains_recv.at[other], sibling)
        return carry

    sends = []

    def start(copy):
        copy.start()
        sends.append(copy)

    def weight_rows(s, number):
        return gate_up_buf.at[s, pl.ds(pl.multiple_of(number * height, height), height), :]

    def down_rows(s, dzh, dy):
        number = 2 * flip(zh, dzh) + flip(y, dy)
        return down_buf.at[s, pl.ds(pl.multiple_of(number * down_height, down_height), down_height), :]

    def act_rows(which, s, step):
        full = (rows_buf, grads_buf)[which]
        return full.at[s, pl.ds(pl.multiple_of(rank(step) * act_height, act_height), act_height), :]

    def send_act(which, s, step, source, hop):
        landed = tuple(bit ^ (1 if axis == hop else 0) for axis, bit in enumerate(step))
        start(
            push(
                source,
                act_rows(which, s, step),
                act_send.at[which, s, 4 * step[0] + 2 * step[1] + step[2], hop],
                act_recv.at[which, s, 4 * landed[0] + 2 * landed[1] + landed[2]],
                member(tuple(1 if axis == hop else 0 for axis in range(3))),
            )
        )

    def wait_act(which, s, step):
        arrived(
            act_rows(which, s, step),
            act_recv.at[which, s, 4 * step[0] + 2 * step[1] + step[2]],
            sibling,
        )

    def act_own(which, s):
        source = act_rows(0, s, own_step) if which == 0 else grads_own.at[s]
        for hop in (0, 1, 2):
            send_act(which, s, own_step, source, hop)

    def act_from_z(which, s):
        step = (1, 0, 0)
        wait_act(which, s, step)
        send_act(which, s, step, act_rows(which, s, step), 1)
        send_act(which, s, step, act_rows(which, s, step), 2)

    def act_from_x(which, s, dl):
        wait_act(which, s, (dl, 1, 0))
        send_act(which, s, (dl, 1, 0), act_rows(which, s, (dl, 1, 0)), 2)

    def act_from_core(which, s, dl, dx):
        wait_act(which, s, (dl, dx, 1))

    def mine(s):
        return gate_up_parts.at[rank(own_step), s]

    def ff_source(s, slot):
        return down_ref.at[s] if slot == 8 else mine(s)

    def ff_rows(s, slot, dzh):
        return down_rows(s, dzh, 0) if slot == 8 else weight_rows(s, device(RANK_STEPS[slot], dzh, 0))

    def to_rank(s, slot):
        step = RANK_STEPS[slot]
        start(
            push(
                gate_up_parts.at[rank(step), s],
                weight_rows(s, device(own_step)),
                rank_send.at[s, slot],
                rank_recv.at[s, slot],
                member(step),
            )
        )

    def send_far(s, slot, source):
        start(push(source, ff_rows(s, slot, 0), far_send.at[s, slot], far_recv.at[s, slot], far))

    def send_across(s, slot, source, dzh):
        start(
            push(
                source,
                ff_rows(s, slot, dzh),
                across_send.at[s, dzh, slot],
                across_recv.at[s, dzh, slot],
                across,
            )
        )

    def own_far(s, slot):
        send_far(s, slot, ff_source(s, slot))

    def own_across(s, slot):
        send_across(s, slot, ff_source(s, slot), 0)

    def rank_far(s, slot):
        arrived(ff_rows(s, slot, 0), rank_recv.at[s, slot], sibling)
        send_far(s, slot, ff_rows(s, slot, 0))

    def rank_across(s, slot):
        send_across(s, slot, ff_rows(s, slot, 0), 0)

    def far_across(s, slot):
        arrived(ff_rows(s, slot, 1), far_recv.at[s, slot], sibling)
        send_across(s, slot, ff_rows(s, slot, 1), 1)

    def ff_end(s):
        for copy in ff_local[s]:
            copy.wait()
        for dzh in (0, 1):
            for slot, step in enumerate(RANK_STEPS):
                arrived(weight_rows(s, device(step, dzh, 1)), across_recv.at[s, dzh, slot], sibling)
            arrived(down_rows(s, dzh, 1), across_recv.at[s, dzh, 8], sibling)

    ff_local = []
    for s in range(positions):
        ff_local.append(
            [
                pltpu.make_async_copy(mine(s), weight_rows(s, device(own_step)), local_sem.at[7 + 3 * s]),
                pltpu.make_async_copy(down_ref.at[s], down_rows(s, 0, 0), local_sem.at[8 + 3 * s]),
                pltpu.make_async_copy(grads_own.at[s], act_rows(1, s, own_step), local_sem.at[9 + 3 * s]),
            ]
        )
    gains_local = pltpu.make_async_copy(gains_own, gains_all.at[me], local_sem.at[6])

    def gains_begin():
        places = 128 // norm_attn_ref.shape[1]
        lane = lax.broadcasted_iota(jnp.int32, (positions, 128), 1) // norm_attn_ref.shape[1]
        gains_own[...] = jnp.zeros_like(gains_own)
        for index, source in enumerate((norm_attn_ref, norm_ff_ref)):
            tiled = jnp.concatenate([source[...].astype(F32)] * places, axis=1)
            gains_own[index * positions : (index + 1) * positions, :] = jnp.where(
                lane == lax.rem(me, places), tiled, 0.0
            ).astype(BF16)
        lax.fori_loop(1, 32, gains_start, 0)
        gains_local.start()

    raw_copy = pltpu.make_async_copy(gate_up_ref, gate_up_raw, local_sem.at[13])

    def part_units():
        raw_copy.wait()
        unit = down_height
        for number in range(8):
            low, rest = divmod(number, 4)
            for s in range(positions):
                for side in (0, 1):
                    for group in range(4):
                        zh_part, y_part = divmod(group, 2)
                        block = 32 * side + 16 * zh_part + 8 * low + 4 * y_part + rest
                        gate_up_parts[number, s, :, (4 * side + group) * unit : (4 * side + group + 1) * unit] = (
                            gate_up_raw[s, :, block * unit : (block + 1) * unit]
                        )
        for s in range(positions):
            ff_local[s][0].start()
            ff_local[s][1].start()

    def weigh():
        def one(rows):
            slot = lax.broadcasted_iota(jnp.int32, (16, 128), 0) + rows.start
            frame = me * act_height + slot
            weight = jnp.zeros((16, 128), F32)
            first = 0
            for item in range(lengths_ref.shape[0]):
                length = lengths_ref[item]
                inside = (frame >= first) & (frame < first + length)
                share = 8.0 * act_height / jnp.full((16, 128), length, jnp.int32).astype(F32)
                weight = weight + jnp.where(inside, share, 0.0)
                first = first + length
            weight = jnp.where(slot < valid_ref[0], weight, 0.0)[:, :1]
            values = cot_ref[rows].astype(F32)
            for p in range(positions):
                grads = values[:, p, :] * weight
                cot_rows[p, rows, :] = grads
                grads_own[p, rows, :] = grads.astype(BF16)

        row_loop(act_height, 16, one)
        for s in range(positions):
            ff_local[s][2].start()

    def take_gains():
        lax.fori_loop(1, 32, gains_wait, 0)
        gains_local.wait()
        for block in range(8):
            total = gains_all[4 * block].astype(F32)
            for extra in range(1, 4):
                total = total + gains_all[4 * block + extra].astype(F32)
            gain_rows[:, 128 * block : 128 * block + 128] = total

        def first_norm(rows):
            values = tokens_ref[rows].astype(F32)
            for p in range(positions):
                resid_mid[p, rows, :] = values[:, p, :]
                r, _ = normed(values[:, p, :])
                attn_in[p, rows, :] = (r * gain_rows[p : p + 1, :]).astype(BF16)

        row_loop(act_height, 16, first_norm)

    keep = []

    def attention(p):
        for source, target, slot in (
            (qkv_buf.at[p], qkv_full.at[p], 2 * p),
            (out_buf.at[p], out_full.at[p], 2 * p + 1),
        ):
            keep.append(pltpu.make_async_copy(source, target, keep_sem.at[slot]))
            keep[-1].start()

        def project(columns):
            qkv_rows[p, :, columns] = dot(attn_in[p], qkv_buf[p, :, columns]).astype(BF16)

        tile_loop(3 * model, 512, project)
        probs = attention_probs(qkv_rows, halves, spread, model, p)
        for q in range(p + 1):
            halves[2 * q] = to_heads(probs[q].astype(BF16), spread)

        def mix(rows):
            total = None
            for q in range(p + 1):
                term = halves[2 * q, rows, :].astype(F32) * qkv_rows[q, rows, 2 * model :].astype(F32)
                total = term if total is None else total + term
            context[p, rows, :] = total.astype(BF16)

        row_loop(act_height, 16, mix)

        def attend(columns):
            resid_mid[p, :, columns] += dot(context[p], out_buf[p, :, columns])

        tile_loop(model, 512, attend)

        def second_norm(step, carry):
            rows = pl.ds(pl.multiple_of(step * 16, 16), 16)
            r, _ = normed(resid_mid[p, rows, :])
            top = rank(own_step) * act_height + step * 16
            rows_buf[p, pl.ds(pl.multiple_of(top, 16), 16), :] = (
                r * gain_rows[positions + p : positions + p + 1, :]
            ).astype(BF16)
            return carry

        lax.fori_loop(0, act_height // 16, second_norm, 0)

    def ff_block(s, number):
        rows = pl.ds(pl.multiple_of(number * 2 * act_height, 2 * act_height), 2 * act_height)
        normed_rows = rows_buf[s, rows, :]
        grads = grads_buf[s, rows, :]
        for tile in range(split // 256):
            left, right = pl.ds(tile * 256, 256), pl.ds(split + tile * 256, 256)
            gate = dot(normed_rows, gate_up_buf[s, :, left])
            up = dot(normed_rows, gate_up_buf[s, :, right])
            d_hidden = dot_back(grads, down_buf[s, left, :])
            sigmoid_gate = jax.nn.sigmoid(gate)
            silu_gate = gate * sigmoid_gate
            hidden[rows, left] = (silu_gate * up).astype(BF16)
            d_gate_up[rows, left] = (
                d_hidden * up * sigmoid_gate * (1.0 + gate * (1.0 - sigmoid_gate))
            ).astype(BF16)
            d_gate_up[rows, right] = (d_hidden * silu_gate).astype(BF16)
        for tile in range(model // 512):
            columns = pl.ds(tile * 512, 512)
            out_stage[rows, columns] = dot(hidden[rows, :], down_buf[s, :, columns]).astype(BF16)
            back_stage[rows, columns] = dot_back(
                d_gate_up[rows, :], gate_up_buf[s, columns, :]
            ).astype(BF16)

    stages = []

    def stage_out(s, *slots):
        for slot in slots:
            source, target = (
                (out_stage, ff_out),
                (back_stage, ff_back),
                (gate_up_stage, gate_up_grad),
                (down_stage, down_grad),
            )[slot]
            stages.append(pltpu.make_async_copy(source, target.at[s], stage_sem.at[s, slot]))
            stages[-1].start()

    def gate_grad(s):
        stage_out(s, 0, 1)

        def gate_up_tile(columns):
            gate_up_stage[:, columns] = dot_grad(rows_buf[s], d_gate_up[:, columns]).astype(BF16)

        tile_loop(2 * split, 256, gate_up_tile)
        stage_out(s, 2)

    def down_weights_grad(s):
        def down_tile(columns):
            down_stage[:, columns] = dot_grad(hidden[...], grads_buf[s, :, columns]).astype(BF16)

        tile_loop(model, 256, down_tile)
        stage_out(s, 3)

    def stages_end():
        while stages:
            stages.pop(0).wait()

    for copy in tree_own:
        copy.start()
    raw_copy.start()
    gains_begin()
    make_spread(spread)
    chips = ((0, 0), (1, 0), (0, 1), (1, 1))

    def block(s, order):
        if s > 0 and order == chosen_first[0]:
            stages_end()
        ff_block(s, 2 * flip(zl, chips[order][0]) + flip(x, chips[order][1]))

    def attend_and_send(s):
        attention(s)
        act_own(0, s)

    chosen_first = [step[2] for step in FORWARD_STEPS if step[:2] == ("block", 1)]
    kinds = dict(
        tree=lambda piece, dz, dy, dx: tree_step(piece, (dz, dy, dx)),
        tree_end=tree_end,
        gains=take_gains,
        parts=part_units,
        cot=weigh,
        attention=attend_and_send,
        grads=lambda s: act_own(1, s),
        act_z=act_from_z,
        act_x=act_from_x,
        act_c=act_from_core,
        to_rank=to_rank,
        own_far=own_far,
        own_across=own_across,
        rank_far=rank_far,
        rank_across=rank_across,
        far_across=far_across,
        ff_end=ff_end,
        block=block,
        gate_grad=gate_grad,
        down_grad=down_weights_grad,
    )
    for kind, *numbers in FORWARD_STEPS:
        kinds[kind](*numbers)
    for _, _, piece, offset in events:
        tree_step(piece, offset, finish=True)
    for copy in sends:
        copy.wait_send()
    for copy in keep:
        copy.wait()
    stages_end()


def forward_gather(valid, lengths, norm_attn, norm_ff, tokens, cot, w_qkv, w_out, w_gate_up, w_down):
    act_height, positions, model = tokens.shape
    _, height, qkv_width = w_qkv.shape
    unit = w_down.shape[1]
    ranks, split, width = 8, 4 * unit, 8 * unit
    group_rows = ranks * act_height
    dma = pltpu.SemaphoreType.DMA
    vmem = pl.BlockSpec(memory_space=pltpu.VMEM)
    smem = pl.BlockSpec(memory_space=pltpu.SMEM)
    anywhere = pl.BlockSpec(memory_space=pl.ANY)
    return pl.pallas_call(
        forward_kernel,
        out_shape=(
            jax.ShapeDtypeStruct((16, model), F32),
            jax.ShapeDtypeStruct((positions, act_height, model), F32),
            jax.ShapeDtypeStruct((positions, act_height, 3 * model), BF16),
            jax.ShapeDtypeStruct((positions, act_height, model), BF16),
            jax.ShapeDtypeStruct((positions, act_height, model), F32),
            jax.ShapeDtypeStruct((positions, model, qkv_width), BF16),
            jax.ShapeDtypeStruct((positions, model, model), BF16),
            jax.ShapeDtypeStruct((positions, group_rows, model), BF16),
            jax.ShapeDtypeStruct((positions, group_rows, model), BF16),
            jax.ShapeDtypeStruct((positions, model, width), BF16),
            jax.ShapeDtypeStruct((positions, split, model), BF16),
        ),
        in_specs=[smem] * 2 + [vmem] * 4 + [anywhere] * 4,
        out_specs=(vmem,) * 5 + (anywhere,) * 6,
        scratch_shapes=[
            pltpu.VMEM((positions, model, qkv_width), BF16),
            pltpu.VMEM((positions, model, model), BF16),
            pltpu.VMEM((positions, model, width), BF16),
            pltpu.VMEM((positions, split, model), BF16),
            pltpu.VMEM((positions, group_rows, model), BF16),
            pltpu.VMEM((positions, group_rows, model), BF16),
            pltpu.VMEM((group_rows, split), BF16),
            pltpu.VMEM((group_rows, width), BF16),
            pltpu.VMEM((group_rows, model), BF16),
            pltpu.VMEM((group_rows, model), BF16),
            pltpu.VMEM((model, width), BF16),
            pltpu.VMEM((split, model), BF16),
            pltpu.VMEM((16, 128), BF16),
            pltpu.VMEM((32, 16, 128), BF16),
            pltpu.VMEM(w_gate_up.shape, BF16),
            pltpu.VMEM((ranks, positions, height, width), BF16),
            pltpu.VMEM((positions, act_height, model), BF16),
            pltpu.VMEM((positions, act_height, model), BF16),
            pltpu.VMEM((2 * positions, act_height, model), BF16),
            pltpu.VMEM((model, 128), BF16),
            dma((6, 16)),
            dma((6, 16)),
            dma((6, 16, 5)),
            dma((32,)),
            dma((32,)),
            dma((2, 8)),
            dma((2, 8)),
            dma((2, 9)),
            dma((2, 9)),
            dma((2, 2, 9)),
            dma((2, 2, 9)),
            dma((2, 2, 8, 3)),
            dma((2, 2, 8)),
            dma((14,)),
            dma((4,)),
            dma((2, 4)),
        ],
        compiler_params=pltpu.CompilerParams(
            collective_id=4, has_side_effects=True, vmem_limit_bytes=62 * 2**20
        ),
        name="forward_gather",
    )(valid, lengths, norm_attn, norm_ff, tokens, cot, w_qkv, w_out, w_gate_up, w_down)


def slot_index(order, direction, offset, z, y, x):
    axis = {"u": "z", "d": "z"}.get(direction, direction)
    index, count = 0, 1
    values = dict(z=z + offset[0], y=flip(y, offset[1]), x=flip(x, offset[2]))
    sizes = dict(z=4, y=2, x=2)
    for earlier in order[: order.index(axis)]:
        index = index * sizes[earlier] + values[earlier]
        count *= sizes[earlier]
    if axis == "z":
        index = index * 5 + (4 if direction == "d" and offset[0] == 0 else values["z"])
        count *= 5
    return index, count


def slot_base(order):
    base, total = {}, 0
    for axis, direction in (("x", "x"), ("y", "y"), ("z", "u")):
        base[axis] = total
        total += slot_index(order, direction, (0, 0, 0), 0, 0, 0)[1]
    base["u"] = base["d"] = base["z"]
    return base, total


def backward_kernel(
    tokens_ref,
    cot_ref,
    gain_rows,
    qkv_rows,
    context,
    resid_mid,
    qkv_full,
    out_full,
    out_ref,
    back_ref,
    gate_up_ref,
    down_ref,
    output,
    grad_tokens,
    norm_attn_sum,
    norm_ff_sum,
    qkv_sum,
    attn_out_sum,
    gate_up_total,
    down_sum,
    act_own,
    core_buf,
    x_buf,
    z_buf,
    gate_own,
    down_own,
    across_gate,
    across_down,
    far_gate,
    far_down,
    qkv_grad,
    out_grad,
    slots_0,
    slots_1,
    slots_2,
    slots_3,
    qkv_tiles,
    out_tiles,
    turned,
    attn_turned,
    context_turned,
    d_qkv,
    d_mid_low,
    d_mid,
    d_context,
    d_rows,
    halves,
    probs_buf,
    spread,
    gain_acc,
    gains_part,
    gains_buf,
    gains_sum,
    gate_up_sum,
    core_send,
    core_recv,
    x_send,
    x_recv,
    z_send,
    z_recv,
    across_send,
    across_recv,
    far_send,
    far_recv,
    rank_send,
    rank_recv,
    swap_send,
    swap_recv,
    tree_send,
    tree_recv,
    gains_send,
    gains_recv,
    own_sem,
    part_sem,
    tile_sem,
):
    z, y, x, core = here()
    me = 2 * (z * 4 + y * 2 + x) + core
    zh, zl, member, rank, device, far, across = group_place(z, y, x, core)
    own_step = (0, 0, 0)
    act_height, positions, model = tokens_ref.shape
    sets = positions
    height = qkv_sum.shape[1]
    down_height = down_sum.shape[1]
    half = 16 * height
    sibling = member((0, 0, 1))
    scale = 1.0 / math.sqrt(HEAD_DIM)
    pairs = pairs_of(positions)
    greet_all(z, y, x, core)
    sends = []

    def start(copy):
        copy.start()
        sends.append(copy)

    def run_rows(dzh, dy, low):
        number = 16 * flip(zh, dzh) + 4 * flip(y, dy) + 8 * low
        return pl.ds(pl.multiple_of(number * height, 4 * height), 4 * height)

    def down_rows(dzh, dy):
        number = 2 * flip(zh, dzh) + flip(y, dy)
        return pl.ds(pl.multiple_of(number * down_height, down_height), down_height)

    def ff_across(turn):
        dzh = 1 - turn
        for s in range(sets):
            for low in (0, 1):
                start(
                    push(
                        gate_up_ref.at[s, run_rows(dzh, 1, low)],
                        across_gate.at[turn, s, low],
                        across_send.at[turn, s, low],
                        across_recv.at[turn, s, low],
                        across,
                    )
                )
            start(
                push(
                    down_ref.at[s, down_rows(dzh, 1)],
                    across_down.at[turn, s],
                    across_send.at[turn, s, 2],
                    across_recv.at[turn, s, 2],
                    across,
                )
            )

    part_copies = []
    for turn in (0, 1):
        for s in range(sets):
            for low in (0, 1):
                part_copies.append(
                    pltpu.make_async_copy(
                        gate_up_ref.at[s, run_rows(1 - turn, 0, low)],
                        gate_own.at[turn, s, low],
                        part_sem.at[turn, s, low],
                    )
                )
            part_copies.append(
                pltpu.make_async_copy(
                    down_ref.at[s, down_rows(1 - turn, 0)], down_own.at[turn, s], part_sem.at[turn, s, 2]
                )
            )

    def ff_first():
        for s in range(sets):
            for low in (0, 1):
                block = across_gate.at[0, s, low]
                arrived(block, across_recv.at[0, s, low], across)
                add_into(block, [block, gate_own.at[0, s, low]])
                start(push(block, far_gate.at[s, low], far_send.at[s, low], far_recv.at[s, low], far))
            block = across_down.at[0, s]
            arrived(block, across_recv.at[0, s, 2], across)
            add_into(block, [block, down_own.at[0, s]])
            start(push(block, far_down.at[s], far_send.at[s, 2], far_recv.at[s, 2], far))

    def share(step, s):
        number = 2 * flip(x, step[1]) + flip(core, step[2])
        return across_gate.at[
            1, s, flip(zl, step[0]), pl.ds(pl.multiple_of(number * height, height), height)
        ]

    def place_units(step, s, source):
        unit = down_height
        for side in (0, 1):
            for group in range(4):
                zh_part, y_part = divmod(group, 2)
                number = 8 * flip(zl, step[0]) + 2 * flip(x, step[1]) + flip(core, step[2])
                left = (32 * side + 16 * zh_part + 4 * y_part + number) * unit
                gate_up_total[s, :, pl.ds(pl.multiple_of(left, unit), unit)] = source[
                    :, (4 * side + group) * unit : (4 * side + group + 1) * unit
                ].astype(F32)

    def ff_second():
        for s in range(sets):
            for low in (0, 1):
                block = across_gate.at[1, s, low]
                arrived(block, across_recv.at[1, s, low], across)
                arrived(far_gate.at[s, low], far_recv.at[s, low], far)
                add_into(block, [block, far_gate.at[s, low], gate_own.at[1, s, low]])
            for slot, step in enumerate(RANK_STEPS):
                if step != own_step:
                    start(
                        push(
                            share(step, s),
                            gate_up_sum.at[rank(own_step), s],
                            rank_send.at[slot, s],
                            rank_recv.at[slot, s],
                            member(step),
                        )
                    )
            place_units(own_step, s, share(own_step, s))
            arrived(across_down.at[1, s], across_recv.at[1, s, 2], across)
            arrived(far_down.at[s], far_recv.at[s, 2], far)
            add_into(down_sum.at[s], [across_down.at[1, s], far_down.at[s], down_own.at[1, s]])

    def ff_last():
        for slot, step in enumerate(RANK_STEPS):
            for s in range(sets):
                if step != own_step:
                    block = gate_up_sum.at[rank(step), s]
                    arrived(block, rank_recv.at[slot, s], member(step))
                    place_units(step, s, block)

    acts = [back_ref, out_ref]

    def act_rows(step):
        return pl.ds(pl.multiple_of(rank(step) * act_height, act_height), act_height)

    def act_core_sends(which):
        for dl, dx in ((1, 1), (0, 1), (1, 0), (0, 0)):
            start(
                push(
                    acts[which].at[:, act_rows((dl, dx, 1))],
                    core_buf.at[which, dl, dx],
                    core_send.at[which, dl, dx],
                    core_recv.at[which, dl, dx],
                    sibling,
                )
            )

    def act_load(which):
        return [
            pltpu.make_async_copy(
                acts[which].at[:, act_rows((dl, dx, 0))], act_own.at[dl, dx], own_sem.at[which, dl, dx]
            )
            for dl in (0, 1)
            for dx in (0, 1)
        ]

    def core_add(which, dl, dx):
        block = core_buf.at[which, dl, dx]
        arrived(block, core_recv.at[which, dl, dx], sibling)
        for s in range(sets):
            add_into(block.at[s], [block.at[s], act_own.at[dl, dx, s]])

    def act_first(which):
        for dl in (1, 0):
            core_add(which, dl, 1)
            start(
                push(
                    core_buf.at[which, dl, 1],
                    x_buf.at[which, dl],
                    x_send.at[which, dl],
                    x_recv.at[which, dl],
                    member((0, 1, 0)),
                )
            )
        core_add(which, 1, 0)
        core_add(which, 0, 0)

    def act_second(which):
        arrived(x_buf.at[which, 1], x_recv.at[which, 1], member((0, 1, 0)))
        for s in range(sets):
            block = x_buf.at[which, 1, s]
            add_into(block, [block, core_buf.at[which, 1, 0, s]])
        start(
            push(
                x_buf.at[which, 1], z_buf.at[which], z_send.at[which], z_recv.at[which], member((1, 0, 0))
            )
        )

    def act_third(which):
        arrived(x_buf.at[which, 0], x_recv.at[which, 0], member((0, 1, 0)))
        arrived(z_buf.at[which], z_recv.at[which], member((1, 0, 0)))

    pieces = [
        (qkv_grad, qkv_sum, 0, "zxy", slots_0),
        (qkv_grad, qkv_sum, 1, "zyx", slots_1),
        (out_grad, attn_out_sum, 0, "xyz", slots_2),
        (out_grad, attn_out_sum, 1, "yxz", slots_3),
    ]
    events = sorted(
        ((-hops(offset), place, piece, offset) for piece in range(4) for place, offset in enumerate(OFFSETS)),
        key=lambda event: event[:3],
    )

    def tree_block(piece, offset):
        source, _, index, _, _ = pieces[piece]
        chip = chip_of(offset, z, y, x)
        return source.at[index, pl.ds(pl.multiple_of(chip * height, height), height), :]

    def tree_copy(piece, offset):
        _, _, _, order, slots = pieces[piece]
        toward = came_from(order, offset)
        base, _ = slot_base(order)
        seen = {"x": "x", "y": "y", "u": "d", "d": "u"}[toward]
        nearer = offset
        if toward == "u":
            nearer = (offset[0] - 1, offset[1], offset[2])
        if toward == "d":
            nearer = (offset[0] + 1, offset[1], offset[2])
        there = {"u": z + 1, "d": z - 1}.get(toward, z)
        index_there, _ = slot_index(
            order, seen, nearer, there, y if toward != "y" else 1 - y, x if toward != "x" else 1 - x
        )
        if toward in "xy":
            index_there, _ = slot_index(order, seen, offset, z, y, x)
        place = base[seen] + index_there
        return push(
            tree_block(piece, offset),
            slots.at[place],
            tree_send.at[piece, chip_of(offset, z, y, x)],
            tree_recv.at[piece, place],
            neighbour(toward, z, y, x, core),
        )

    def tree_step(piece, offset):
        _, result, index, order, slots = pieces[piece]
        base, _ = slot_base(order)

        def go():
            block = tree_block(piece, offset)
            sure, unsure = [], []
            for direction in onward(order, offset):
                local, _ = slot_index(order, direction, offset, z, y, x)
                place = base[direction] + local
                (sure if direction in "xy" else unsure).append((direction, place))
            terms = [block]
            for _, place in sure:
                arrived(slots.at[place], tree_recv.at[piece, place], sibling)
                terms.append(slots.at[place])
            last = hops(offset) == 0
            target = result.at[index] if last else block
            if last or len(terms) > 1:
                add_into(target, terms)
            for direction, place in unsure:

                def more(place=place):
                    arrived(slots.at[place], tree_recv.at[piece, place], sibling)
                    add_into(target, [target, slots.at[place]])

                maybe(direction_exists(direction, z), more)
            if not last:
                tree_copy(piece, offset).start()

        maybe(offset_exists(offset, z), go)

    def tree_steps(which, distances):
        for hop, _, piece, offset in events:
            if piece in which and -hop in distances:
                tree_step(piece, offset)

    def gains_copy(step):
        other = lax.rem(me + step, 32)
        return push(
            gains_part.at[lax.div(other, 4)],
            gains_buf.at[me],
            gains_send.at[step],
            gains_recv.at[me],
            (lax.div(other, 2), lax.rem(other, 2)),
        )

    def gains_start(step, carry):
        gains_copy(step).start()
        return carry

    def gains_wait(step, carry):
        other = lax.rem(me + step, 32)
        gains_copy(step).wait_send()
        arrived(gains_buf.at[other], gains_recv.at[other], sibling)
        gains_sum[...] += gains_buf[other]
        return carry

    def swap_copy(index, source, target):
        return push(source, target, swap_send.at[index], swap_recv.at[index], sibling)

    def turn(source, target, slot):
        def one(block, p):
            flat = source(p, block)
            turned[slot, p, pl.ds(2 * block, 2)] = flat.T.astype(BF16).reshape(2, 2, height, act_height)

        for p in range(positions):
            for block in range(model // 128):
                one(block, p)
            target[p, :, :, :act_height] = turned[slot, p, :, core]

    qkv_tile = qkv_tiles.shape[1]
    tile_count = model // qkv_tile

    def qkv_load(number):
        p, tile = divmod(number, tile_count)
        return pltpu.make_async_copy(
            qkv_full.at[p, pl.ds(tile * qkv_tile, qkv_tile)],
            qkv_tiles.at[number % 2],
            tile_sem.at[number % 2],
        )

    out_loads = [
        pltpu.make_async_copy(out_full.at[p], out_tiles.at[p], tile_sem.at[2 + p]) for p in range(positions)
    ]

    act_core_sends(0)
    ff_across(0)
    ff_across(1)
    load_back = act_load(0)
    for copy in load_back + out_loads + part_copies:
        copy.start()
    act_core_sends(1)
    qkv_load(0).start()
    qkv_load(1).start()
    make_spread(spread)
    gain_acc[...] = jnp.zeros_like(gain_acc)
    for copy in load_back:
        copy.wait()
    act_first(0)
    load_out = act_load(1)
    for copy in load_out:
        copy.start()

    def context_block(p, block):
        return context[p, :, 128 * block : 128 * block + 128].astype(F32)

    def attn_norm(rows):
        values = tokens_ref[rows].astype(F32)
        for p in range(positions):
            r, _ = normed(values[:, p, :])
            d_rows[p, rows, :] = r * gain_rows[p : p + 1, :]

    row_loop(act_height, 16, attn_norm)
    turn(context_block, context_turned, 0)
    turn(
        lambda p, block: d_rows[p, :, 128 * block : 128 * block + 128], attn_turned, 1
    )
    swaps = []
    for p in range(positions):
        swaps.append(
            swap_copy(
                4 * p,
                turned.at[0, p, :, 1 - core],
                context_turned.at[p, :, :, pl.ds(act_height, act_height)],
            )
        )
        swaps.append(
            swap_copy(
                4 * p + 1,
                turned.at[1, p, :, 1 - core],
                attn_turned.at[p, :, :, pl.ds(act_height, act_height)],
            )
        )
        swaps[-1].start()
        swaps[-2].start()
    act_second(0)
    for copy in part_copies:
        copy.wait()
    ff_first()
    for p in range(positions):
        probs = attention_probs(qkv_rows, halves, spread, model, p)
        for q in range(p + 1):
            probs_buf[pairs.index((p, q))] = probs[q]
    act_third(0)

    def mid_back(rows):
        for p in range(positions):
            d_ff_in = (
                core_buf[0, 0, 0, p, rows, :].astype(F32)
                + x_buf[0, 0, p, rows, :].astype(F32)
                + z_buf[0, p, rows, :].astype(F32)
            )
            r, inverse = normed(resid_mid[p, rows, :])
            gain_acc[positions + p] += r * d_ff_in
            total = cot_ref[p, rows, :] + norm_back(
                r, inverse, d_ff_in * gain_rows[positions + p : positions + p + 1, :]
            )
            d_mid[p, rows, :] = total
            d_mid_low[p, rows, :] = total.astype(BF16)

    row_loop(act_height, 16, mid_back)
    for p in range(positions):
        swaps.append(
            swap_copy(
                4 * p + 2,
                d_mid_low.at[p, pl.ds(0, act_height)],
                d_mid_low.at[p, pl.ds(act_height, act_height)],
            )
        )
        swaps[-1].start()
    for copy in out_loads:
        copy.wait()
    for p in range(positions):

        def context_back(columns, p=p):
            d_context[p, :, columns] = lax.dot_general(
                d_mid_low[p, :act_height, :],
                out_tiles[p, columns, :],
                (((1,), (1,)), ((), ())),
                preferred_element_type=F32,
            ).astype(BF16)

        tile_loop(model, 256, context_back)

    def context_products(rows):
        for index, (p, q) in enumerate(pairs):
            product = d_context[p, rows, :].astype(F32) * qkv_rows[q, rows, 2 * model :].astype(F32)
            halves[2 * index, rows, :], halves[2 * index + 1, rows, :] = split_product(product)

    row_loop(act_height, 16, context_products)
    d_probs = [sums_over_heads(halves, spread, index) for index in range(len(pairs))]
    for p in range(positions):
        own = [index for index, pair in enumerate(pairs) if pair[0] == p]
        mean = functools.reduce(jnp.add, [probs_buf[index] * d_probs[index] for index in own])
        for index in own:
            d_score = (probs_buf[index] * (d_probs[index] - mean)).astype(BF16)
            halves[2 * index] = to_heads(d_score, spread)
            halves[2 * index + 1] = to_heads(probs_buf[index].astype(BF16), spread)

    def qkv_back(rows):
        d_keys = [None] * positions
        d_values = [None] * positions

        def plus(total, term):
            return term if total is None else total + term

        for p in range(positions):
            d_query = None
            d_own = d_context[p, rows, :].astype(F32)
            query = qkv_rows[p, rows, :model].astype(F32)
            for index, (own, q) in enumerate(pairs):
                if own == p:
                    d_score = halves[2 * index, rows, :].astype(F32)
                    key = qkv_rows[q, rows, model : 2 * model].astype(F32)
                    d_query = plus(d_query, d_score * key)
                    d_keys[q] = plus(d_keys[q], d_score * query)
                    d_values[q] = plus(d_values[q], halves[2 * index + 1, rows, :].astype(F32) * d_own)
            d_qkv[p, rows, :model] = (d_query * scale).astype(BF16)
        for p in range(positions):
            d_qkv[p, rows, model : 2 * model] = (d_keys[p] * scale).astype(BF16)
            d_qkv[p, rows, 2 * model :] = d_values[p].astype(BF16)

    row_loop(act_height, 16, qkv_back)
    for p in range(positions):
        swaps.append(
            swap_copy(
                4 * p + 3,
                d_qkv.at[p, pl.ds(0, act_height)],
                d_qkv.at[p, pl.ds(act_height, act_height)],
            )
        )
        swaps[-1].start()

    def swap_wait(index, target):
        arrived(target, swap_recv.at[index], sibling)

    for p in range(positions):
        swap_wait(4 * p, context_turned.at[p, :, :, pl.ds(act_height, act_height)])
        swap_wait(4 * p + 2, d_mid_low.at[p, pl.ds(act_height, act_height)])

        def out_weights(columns, p=p):
            out_grad[p, :, columns] = jnp.dot(
                context_turned[p].reshape(half, 2 * act_height),
                d_mid_low[p, :, columns],
                preferred_element_type=F32,
            ).astype(BF16)

        tile_loop(model, 256, out_weights)
    tree_steps((2, 3), (5,))
    for copy in load_out:
        copy.wait()
    act_first(1)
    for p in range(positions):
        swap_wait(4 * p + 1, attn_turned.at[p, :, :, pl.ds(act_height, act_height)])
        swap_wait(4 * p + 3, d_qkv.at[p, pl.ds(act_height, act_height)])

        def qkv_weights(columns, p=p):
            qkv_grad[p, :, columns] = jnp.dot(
                attn_turned[p].reshape(half, 2 * act_height),
                d_qkv[p, :, columns],
                preferred_element_type=F32,
            ).astype(BF16)

        tile_loop(3 * model, 256, qkv_weights)
        tree_steps((p,), (5,))
    tree_steps((0, 1, 2, 3), (4,))
    act_second(1)
    ff_second()
    for number in range(positions * tile_count):
        p, tile = divmod(number, tile_count)
        qkv_load(number).wait()
        d_rows[p, :, tile * qkv_tile : (tile + 1) * qkv_tile] = lax.dot_general(
            d_qkv[p, :act_height, :],
            qkv_tiles[number % 2],
            (((1,), (1,)), ((), ())),
            preferred_element_type=F32,
        )
        if number + 2 < positions * tile_count:
            qkv_load(number + 2).start()
    tree_steps((0, 1, 2, 3), (3,))

    def attn_back(rows):
        values = tokens_ref[rows].astype(F32)
        for p in range(positions):
            r, inverse = normed(values[:, p, :])
            d_attn_in = d_rows[p, rows, :]
            gain_acc[p] += r * d_attn_in
            grad_tokens[rows, p, :] = d_mid[p, rows, :] + norm_back(
                r, inverse, d_attn_in * gain_rows[p : p + 1, :]
            )

    row_loop(act_height, 16, attn_back)
    gains_part[...] = jnp.zeros_like(gains_part)
    for index in range(2 * positions):
        sums = jnp.sum(gain_acc[index], axis=0, keepdims=True)
        for block in range(8):
            gains_part[block, index : index + 1, :] = sums[:, 128 * block : 128 * block + 128]
    lax.fori_loop(1, 32, gains_start, 0)
    tree_steps((0, 1, 2, 3), (2,))
    act_third(1)

    def finish_output(rows):
        rounded = []
        for p in range(positions):
            total = (
                core_buf[1, 0, 0, p, rows, :].astype(F32)
                + x_buf[1, 0, p, rows, :].astype(F32)
                + z_buf[1, p, rows, :].astype(F32)
            )
            rounded.append(resid_mid[p, rows, :] + total)
        output[rows] = jnp.stack(rounded, axis=1).astype(BF16)

    row_loop(act_height, 16, finish_output)
    tree_steps((0, 1, 2, 3), (1,))
    tree_steps((0, 1, 2, 3), (0,))
    ff_last()
    gains_sum[...] = gains_part[lax.div(me, 4)]
    lax.fori_loop(1, 32, gains_wait, 0)
    own_gain = norm_attn_sum.shape[1]
    for index, target in enumerate((norm_attn_sum, norm_ff_sum)):
        picked = jnp.zeros(target.shape, F32)
        for place in range(128 // own_gain):
            picked = picked + jnp.where(
                lax.rem(me, 128 // own_gain) == place,
                gains_sum[
                    index * positions : (index + 1) * positions, place * own_gain : (place + 1) * own_gain
                ],
                0.0,
            )
        target[...] = picked
    for _, _, piece, offset in events:
        if hops(offset) > 0:
            maybe(offset_exists(offset, z), tree_copy(piece, offset).wait_send)
    for copy in sends + swaps:
        copy.wait_send()


def backward_scatter(
    tokens,
    grads,
    gain_rows,
    qkv_rows,
    context,
    resid_mid,
    qkv_full,
    out_full,
    out_part,
    back_part,
    gate_up_grad,
    down_grad,
):
    act_height, sets, model = tokens.shape
    width = gate_up_grad.shape[2]
    height = model // 32
    down_height = down_grad.shape[1] // 4
    dma = pltpu.SemaphoreType.DMA
    vmem = pl.BlockSpec(memory_space=pltpu.VMEM)
    anywhere = pl.BlockSpec(memory_space=pl.ANY)
    places = [slot_base(order)[1] for order in ORDERS]
    pair_count = len(pairs_of(sets))
    act = (sets, act_height, model)
    return pl.pallas_call(
        backward_kernel,
        out_shape=(
            jax.ShapeDtypeStruct(tokens.shape, BF16),
            jax.ShapeDtypeStruct(tokens.shape, F32),
            jax.ShapeDtypeStruct((sets, height), F32),
            jax.ShapeDtypeStruct((sets, height), F32),
            jax.ShapeDtypeStruct((sets, height, 3 * model), F32),
            jax.ShapeDtypeStruct((sets, height, model), F32),
            jax.ShapeDtypeStruct((sets, height, 8 * width), F32),
            jax.ShapeDtypeStruct((sets, down_height, model), F32),
        ),
        in_specs=[vmem] * 6 + [anywhere] * 6,
        out_specs=(vmem,) * 8,
        scratch_shapes=[
            pltpu.VMEM((2, 2) + act, BF16),
            pltpu.VMEM((2, 2, 2) + act, BF16),
            pltpu.VMEM((2, 2) + act, BF16),
            pltpu.VMEM((2,) + act, BF16),
            pltpu.VMEM((2, sets, 2, 4 * height, width), BF16),
            pltpu.VMEM((2, sets, down_height, model), BF16),
            pltpu.VMEM((2, sets, 2, 4 * height, width), BF16),
            pltpu.VMEM((2, sets, down_height, model), BF16),
            pltpu.VMEM((sets, 2, 4 * height, width), BF16),
            pltpu.VMEM((sets, down_height, model), BF16),
            pltpu.VMEM((sets, 16 * height, 3 * model), BF16),
            pltpu.VMEM((sets, 16 * height, model), BF16),
            pltpu.VMEM((places[0], height, 3 * model), BF16),
            pltpu.VMEM((places[1], height, 3 * model), BF16),
            pltpu.VMEM((places[2], height, model), BF16),
            pltpu.VMEM((places[3], height, model), BF16),
            pltpu.VMEM((2, 128, 3 * model), BF16),
            pltpu.VMEM((sets, model, model), BF16),
            pltpu.VMEM((2, sets, 16, 2, height, act_height), BF16),
            pltpu.VMEM((sets, 16, height, 2 * act_height), BF16),
            pltpu.VMEM((sets, 16, height, 2 * act_height), BF16),
            pltpu.VMEM((sets, 2 * act_height, 3 * model), BF16),
            pltpu.VMEM((sets, 2 * act_height, model), BF16),
            pltpu.VMEM(act, F32),
            pltpu.VMEM(act, BF16),
            pltpu.VMEM(act, F32),
            pltpu.VMEM((2 * pair_count, act_height, model), BF16),
            pltpu.VMEM((pair_count, act_height, 128), F32),
            pltpu.VMEM((model, 128), BF16),
            pltpu.VMEM((2 * sets, 16, model), F32),
            pltpu.VMEM((8, 8, 128), F32),
            pltpu.VMEM((32, 8, 128), F32),
            pltpu.VMEM((8, 128), F32),
            pltpu.VMEM((8, sets, height, width), BF16),
            dma((2, 2, 2)),
            dma((2, 2, 2)),
            dma((2, 2)),
            dma((2, 2)),
            dma((2,)),
            dma((2,)),
            dma((2, sets, 3)),
            dma((2, sets, 3)),
            dma((sets, 3)),
            dma((sets, 3)),
            dma((8, sets)),
            dma((8, sets)),
            dma((4 * sets,)),
            dma((4 * sets,)),
            dma((4, 16)),
            dma((4, max(places))),
            dma((32,)),
            dma((32,)),
            dma((2, 2, 2)),
            dma((2, sets, 3)),
            dma((2 + sets,)),
        ],
        compiler_params=pltpu.CompilerParams(
            collective_id=5, has_side_effects=True, vmem_limit_bytes=63 * 2**20
        ),
        name="backward_scatter",
    )(
        tokens,
        grads,
        gain_rows,
        qkv_rows,
        context,
        resid_mid,
        qkv_full,
        out_full,
        out_part,
        back_part,
        gate_up_grad,
        down_grad,
    )


def local_fast(
    tokens,
    norm_attn,
    w_qkv,
    w_out,
    norm_ff,
    w_gate_up,
    w_down,
    cotangent,
    valid_frames,
    item_lengths,
):
    (
        gain_rows,
        cot_rows,
        qkv_rows,
        context,
        resid_mid,
        qkv_full,
        out_full,
        out_part,
        back_part,
        gate_up_grad,
        down_grad,
    ) = forward_gather(
        valid_frames,
        item_lengths,
        norm_attn,
        norm_ff,
        tokens,
        cotangent,
        w_qkv,
        w_out,
        w_gate_up,
        w_down,
    )
    (
        output,
        grad_tokens,
        share_norm_attn,
        share_norm_ff,
        share_qkv,
        share_out,
        share_gate_up,
        share_down,
    ) = backward_scatter(
        tokens,
        cot_rows,
        gain_rows,
        qkv_rows,
        context,
        resid_mid,
        qkv_full,
        out_full,
        out_part,
        back_part,
        gate_up_grad,
        down_grad,
    )
    return (
        output,
        grad_tokens,
        share_norm_attn,
        share_qkv,
        share_out,
        share_norm_ff,
        share_gate_up,
        share_down,
    )


def solution(mesh):
    in_specs = (
        P(("dp", "pair"), None, None),
        P(None, ("dp", "pair")),
        P(None, ("dp", "pair"), None),
        P(None, ("dp", "pair"), None),
        P(None, ("dp", "pair")),
        P(None, ("dp", "pair"), None),
        P(None, ("dp", "pair"), None),
        P(("dp", "pair"), None, None),
        P(("dp", "pair")),
        P(),
    )
    out_specs = (
        P(("dp", "pair"), None, None),
        P(("dp", "pair"), None, None),
        P(None, ("dp", "pair")),
        P(None, ("dp", "pair"), None),
        P(None, ("dp", "pair"), None),
        P(None, ("dp", "pair")),
        P(None, ("dp", "pair"), None),
        P(None, ("dp", "pair"), None),
    )
    body = local_fast if mesh.shape["dp"] == 16 and mesh.shape["pair"] == 2 else local
    return jax.shard_map(body, mesh=mesh, in_specs=in_specs, out_specs=out_specs, check_vma=False)
```

```python
import functools
import math

import jax
import jax.numpy as jnp
from jax import lax
from jax.experimental import pallas as pl
from jax.experimental.pallas import tpu as pltpu
from jax.sharding import PartitionSpec as P

HEAD_DIM = 64


def per_pos(activations, weight):
    return jnp.einsum("fgk,gke->fge", activations, weight, preferred_element_type=jnp.float32)


def per_pos_back(gradients, weight):
    return jnp.einsum("fge,gke->fgk", gradients, weight, preferred_element_type=jnp.float32)


def pos_grad(activations, gradients):
    return jnp.einsum("fgk,fge->kge", activations, gradients, preferred_element_type=jnp.float32)


def gain_grad(normed_rows, gradients):
    return jnp.transpose(jnp.sum(normed_rows * gradients, axis=0))


def back_layout(share):
    return jnp.swapaxes(share, 0, 1)


def normed(values):
    inverse = lax.rsqrt(jnp.mean(values * values, axis=-1, keepdims=True) + 1e-05)
    return (values * inverse, inverse)


def norm_back(normed_rows, inverse, gradients):
    return inverse * (
        gradients - normed_rows * jnp.mean(gradients * normed_rows, axis=-1, keepdims=True)
    )


def gather_ff_fwd(norm_ff, w_gate_up, w_down, start, group):
    return (
        lax.all_gather(norm_ff[start : start + group], ("dp", "pair"), axis=1, tiled=True),
        lax.all_gather(w_gate_up[start : start + group], ("dp", "pair"), axis=1, tiled=True),
        lax.all_gather(w_down[start : start + group], ("dp", "pair"), axis=1, tiled=True),
    )


def gather_ff_back(norm_ff, w_gate_up, w_down, start, group):
    return (
        lax.all_gather(norm_ff[start : start + group], ("dp", "pair"), axis=1, tiled=True),
        lax.all_gather(w_gate_up[start : start + group], ("dp", "pair"), axis=1, tiled=True),
        lax.all_gather(w_down[start : start + group], ("dp", "pair"), axis=1, tiled=True),
    )


def local(
    tokens,
    norm_attn,
    w_qkv,
    w_out,
    norm_ff,
    w_gate_up,
    w_down,
    cotangent,
    valid_frames,
    item_lengths,
):
    frame_count, positions, model_width = tokens.shape
    head_count = model_width // HEAD_DIM
    ff_units = w_gate_up.shape[2] // 2
    score_scale = 1.0 / math.sqrt(HEAD_DIM)
    causal = jnp.arange(positions)[:, None] >= jnp.arange(positions)[None, :]
    head_shape = (frame_count, positions, head_count, HEAD_DIM)
    group = 1
    gains_attn, qkv_full, out_full = (
        lax.all_gather(norm_attn, ("dp", "pair"), axis=1, tiled=True),
        lax.all_gather(w_qkv, ("dp", "pair"), axis=1, tiled=True),
        lax.all_gather(w_out, ("dp", "pair"), axis=1, tiled=True),
    )
    resid_in = tokens.astype(jnp.float32)
    normed_one, inverse_one = normed(resid_in)
    attn_in = (normed_one * gains_attn.astype(jnp.float32)[None]).astype(jnp.bfloat16)
    qkv_rows = per_pos(attn_in, qkv_full).astype(jnp.bfloat16)
    queries = qkv_rows[..., :model_width].reshape(head_shape)
    key_heads = qkv_rows[..., model_width : 2 * model_width].reshape(head_shape)
    value_heads = qkv_rows[..., 2 * model_width :].reshape(head_shape)
    scores = (
        jnp.einsum("fphd,fqhd->fhpq", queries, key_heads, preferred_element_type=jnp.float32)
        * score_scale
    )
    scores = jnp.where(causal, scores, -1e30)
    row_max = jnp.max(scores, axis=-1, keepdims=True)
    attn_probs = jnp.exp(scores - row_max)
    attn_probs = attn_probs / jnp.sum(attn_probs, axis=-1, keepdims=True)
    probs_low = attn_probs.astype(jnp.bfloat16)
    context = jnp.einsum(
        "fhpq,fqhd->fphd", probs_low, value_heads, preferred_element_type=jnp.float32
    )
    context = context.astype(jnp.bfloat16).reshape(frame_count, positions, model_width)
    resid_mid = resid_in + per_pos(context, out_full)
    kept_parts = []
    out_parts = []
    for start in range(0, positions, group):
        gains_ff, gate_up_full, down_full = gather_ff_fwd(norm_ff, w_gate_up, w_down, start, group)
        mid_part = resid_mid[:, start : start + group]
        normed_two, inverse_two = normed(mid_part)
        ff_in = (normed_two * gains_ff.astype(jnp.float32)[None]).astype(jnp.bfloat16)
        gate_up = per_pos(ff_in, gate_up_full)
        gate_part = gate_up[..., :ff_units]
        up_part = gate_up[..., ff_units:]
        sigmoid_gate = jax.nn.sigmoid(gate_part)
        silu_gate = gate_part * sigmoid_gate
        hidden = (silu_gate * up_part).astype(jnp.bfloat16)
        out_parts.append(mid_part + per_pos(hidden, down_full))
        kept_parts.append(
            (normed_two, inverse_two, ff_in, gate_part, up_part, sigmoid_gate, silu_gate, hidden)
        )
    output = jnp.concatenate(out_parts, axis=1).astype(jnp.bfloat16)
    device_index = lax.axis_index(("dp", "pair"))
    local_ids = jnp.arange(frame_count, dtype=jnp.int32)
    frame_ids = device_index * frame_count + local_ids
    item_ends = jnp.cumsum(item_lengths)
    item_starts = item_ends - item_lengths
    in_item = (frame_ids[:, None] >= item_starts[None, :]) & (
        frame_ids[:, None] < item_ends[None, :]
    )
    item_share = 8 * frame_count / item_lengths.astype(jnp.float32)
    frame_weight = jnp.sum(jnp.where(in_item, item_share[None, :], 0.0), axis=1)
    frame_weight = jnp.where(local_ids < valid_frames[0], frame_weight, 0.0)
    grad_out = cotangent.astype(jnp.float32) * frame_weight[:, None, None]
    mid_grads = []
    share_norm_ff_parts = []
    share_gate_up_parts = []
    share_down_parts = []
    for index, start in enumerate(range(0, positions, group)):
        normed_two, inverse_two, ff_in, gate_part, up_part, sigmoid_gate, silu_gate, hidden = (
            kept_parts[index]
        )
        gains_ff, gate_up_full, down_full = gather_ff_back(norm_ff, w_gate_up, w_down, start, group)
        grad_part = grad_out[:, start : start + group]
        grad_low = grad_part.astype(jnp.bfloat16)
        grad_down = pos_grad(hidden, grad_low)
        d_hidden = per_pos_back(grad_low, down_full)
        d_gate = d_hidden * up_part * sigmoid_gate * (1.0 + gate_part * (1.0 - sigmoid_gate))
        d_up = d_hidden * silu_gate
        d_gate_up = jnp.concatenate([d_gate, d_up], axis=-1).astype(jnp.bfloat16)
        grad_gate_up = pos_grad(ff_in, d_gate_up)
        d_ff_in = per_pos_back(d_gate_up, gate_up_full)
        grad_norm_ff = gain_grad(normed_two, d_ff_in)
        mid_grads.append(
            grad_part
            + norm_back(normed_two, inverse_two, d_ff_in * gains_ff.astype(jnp.float32)[None])
        )
        share_a, share_b, share_c = (
            lax.psum_scatter(grad_norm_ff, ("dp", "pair"), scatter_dimension=0, tiled=True),
            lax.psum_scatter(grad_gate_up, ("dp", "pair"), scatter_dimension=0, tiled=True),
            lax.psum_scatter(grad_down, ("dp", "pair"), scatter_dimension=0, tiled=True),
        )
        share_norm_ff_parts.append(jnp.transpose(share_a))
        share_gate_up_parts.append(back_layout(share_b))
        share_down_parts.append(back_layout(share_c))
    d_mid = jnp.concatenate(mid_grads, axis=1)
    gains_attn, qkv_full, out_full = (
        lax.all_gather(norm_attn, ("dp", "pair"), axis=1, tiled=True),
        lax.all_gather(w_qkv, ("dp", "pair"), axis=1, tiled=True),
        lax.all_gather(w_out, ("dp", "pair"), axis=1, tiled=True),
    )
    d_mid_low = d_mid.astype(jnp.bfloat16)
    grad_out_proj = pos_grad(context, d_mid_low)
    d_context = per_pos_back(d_mid_low, out_full).astype(jnp.bfloat16).reshape(head_shape)
    d_probs = jnp.einsum(
        "fphd,fqhd->fhpq", d_context, value_heads, preferred_element_type=jnp.float32
    )
    d_values = jnp.einsum(
        "fhpq,fphd->fqhd", probs_low, d_context, preferred_element_type=jnp.float32
    )
    d_scores = attn_probs * (d_probs - jnp.sum(attn_probs * d_probs, axis=-1, keepdims=True))
    d_scores = d_scores.astype(jnp.bfloat16)
    d_queries = (
        jnp.einsum("fhpq,fqhd->fphd", d_scores, key_heads, preferred_element_type=jnp.float32)
        * score_scale
    )
    d_keys = (
        jnp.einsum("fhpq,fphd->fqhd", d_scores, queries, preferred_element_type=jnp.float32)
        * score_scale
    )
    row_shape = (frame_count, positions, model_width)
    d_qkv = jnp.concatenate(
        [d_queries.reshape(row_shape), d_keys.reshape(row_shape), d_values.reshape(row_shape)],
        axis=-1,
    ).astype(jnp.bfloat16)
    grad_qkv = pos_grad(attn_in, d_qkv)
    d_attn_in = per_pos_back(d_qkv, qkv_full)
    grad_norm_attn = gain_grad(normed_one, d_attn_in)
    grad_tokens = d_mid + norm_back(
        normed_one, inverse_one, d_attn_in * gains_attn.astype(jnp.float32)[None]
    )
    share_norm_attn, share_qkv, share_out = (
        lax.psum_scatter(grad_norm_attn, ("dp", "pair"), scatter_dimension=0, tiled=True),
        lax.psum_scatter(grad_qkv, ("dp", "pair"), scatter_dimension=0, tiled=True),
        lax.psum_scatter(grad_out_proj, ("dp", "pair"), scatter_dimension=0, tiled=True),
    )
    share_norm_attn = jnp.transpose(share_norm_attn)
    share_qkv = back_layout(share_qkv)
    share_out = back_layout(share_out)
    share_norm_ff = jnp.concatenate(share_norm_ff_parts, axis=0)
    share_gate_up = jnp.concatenate(share_gate_up_parts, axis=0)
    share_down = jnp.concatenate(share_down_parts, axis=0)
    return (
        output,
        grad_tokens,
        share_norm_attn,
        share_qkv,
        share_out,
        share_norm_ff,
        share_gate_up,
        share_down,
    )


MESH_ID = pl.DeviceIdType.MESH
BF16 = jnp.bfloat16
F32 = jnp.float32


def here():
    dp = lax.axis_index("dp")
    core = lax.axis_index("pair")
    return lax.div(dp, 4), lax.rem(lax.div(dp, 2), 2), lax.rem(dp, 2), core


def flip(value, bit):
    return 1 - value if bit else value


def push(src, dst, send_sem, recv_sem, to):
    return pltpu.make_async_remote_copy(
        src_ref=src,
        dst_ref=dst,
        send_sem=send_sem,
        recv_sem=recv_sem,
        device_id=to,
        device_id_type=MESH_ID,
    )


def arrived(dst, recv_sem, to):
    push(dst, dst, recv_sem, recv_sem, to).wait_recv()


def greet_all(z, y, x, core):
    barrier = pltpu.get_barrier_semaphore()
    me = 2 * (z * 4 + y * 2 + x) + core

    def one(step, carry):
        other = lax.rem(me + step, 32)
        pl.semaphore_signal(
            barrier, inc=1, device_id=(lax.div(other, 2), lax.rem(other, 2)), device_id_type=MESH_ID
        )
        return carry

    lax.fori_loop(1, 32, one, 0)
    pl.semaphore_wait(barrier, 31)


def greet(peers):
    barrier = pltpu.get_barrier_semaphore()
    for to in peers:
        pl.semaphore_signal(barrier, inc=1, device_id=to, device_id_type=MESH_ID)
    pl.semaphore_wait(barrier, len(peers))


def maybe(condition, do):
    if condition is None:
        do()
    else:
        pl.when(condition)(do)


OFFSETS = [
    (dz, dy, dx) for dz in (0, -1, 1, -2, 2, -3, 3) for dy in (0, 1) for dx in (0, 1)
]
ORDERS = ("zxy", "zyx", "xyz", "yxz")


def hops(offset):
    return abs(offset[0]) + offset[1] + offset[2]


def arrival_axis(order, offset):
    part = dict(z=offset[0], y=offset[1], x=offset[2])
    last = None
    for axis in order:
        if part[axis] != 0:
            last = axis
    return last


def onward(order, offset):
    directions = []
    last = arrival_axis(order, offset)
    start = 0
    if last is not None:
        start = order.index(last) + 1
        if last == "z":
            directions.append("u" if offset[0] < 0 else "d")
    for axis in order[start:]:
        directions.extend(["u", "d"] if axis == "z" else [axis])
    return directions


def came_from(order, offset):
    last = arrival_axis(order, offset)
    if last == "z":
        return "d" if offset[0] < 0 else "u"
    return last


def offset_exists(offset, z):
    if offset[0] < 0:
        return z >= -offset[0]
    if offset[0] > 0:
        return z <= 3 - offset[0]
    return None


def direction_exists(direction, z):
    return {"u": z < 3, "d": z > 0}.get(direction)


DIRECTIONS = ("x", "y", "u", "d", "s")


def neighbour(direction, z, y, x, core):
    if direction == "x":
        return (z * 4 + y * 2 + 1 - x, core)
    if direction == "y":
        return (z * 4 + (1 - y) * 2 + x, core)
    if direction == "u":
        return (z * 4 + 4 + y * 2 + x, core)
    if direction == "d":
        return (z * 4 - 4 + y * 2 + x, core)
    return (z * 4 + y * 2 + x, 1 - core)


def chip_of(offset, z, y, x):
    return (z + offset[0]) * 4 + flip(y, offset[1]) * 2 + flip(x, offset[2])


RANK_STEPS = sorted(
    ((dl, dx, dc) for dl in (0, 1) for dx in (0, 1) for dc in (0, 1)), key=lambda step: (sum(step), step)
)


def group_place(z, y, x, core):
    zh, zl = lax.div(z, 2), lax.rem(z, 2)

    def member(step):
        return ((2 * zh + flip(zl, step[0])) * 4 + y * 2 + flip(x, step[1]), flip(core, step[2]))

    def rank(step):
        return 4 * flip(zl, step[0]) + 2 * flip(x, step[1]) + flip(core, step[2])

    def device(step, dzh=0, dy=0):
        return 16 * flip(zh, dzh) + 4 * flip(y, dy) + 8 * flip(zl, step[0]) + 2 * flip(x, step[1]) + flip(core, step[2])

    far = ((2 * (1 - zh) + zl) * 4 + y * 2 + x, core)
    across = (z * 4 + (1 - y) * 2 + x, core)
    return zh, zl, member, rank, device, far, across


def add_into(target, sources, rows=16, columns=1024):
    height, width = target.shape
    across = width // columns

    def one(step, carry):
        top = pl.multiple_of(lax.div(step, across) * rows, rows)
        left = pl.multiple_of(lax.rem(step, across) * columns, columns)
        spot = (pl.ds(top, rows), pl.ds(left, columns))
        total = sources[0][spot].astype(F32)
        for source in sources[1:]:
            total = total + source[spot].astype(F32)
        target[spot] = total.astype(target.dtype)
        return carry

    lax.fori_loop(0, (height // rows) * across, one, 0)


def row_loop(height, chunk, body):
    def one(step, carry):
        body(pl.ds(pl.multiple_of(step * chunk, chunk), chunk))
        return carry

    lax.fori_loop(0, height // chunk, one, 0)


def tile_loop(width, tile, body):
    def one(step, carry):
        body(pl.ds(pl.multiple_of(step * tile, tile), tile))
        return carry

    lax.fori_loop(0, width // tile, one, 0)


def dot(left, right):
    return jnp.dot(left, right, preferred_element_type=F32)


def dot_back(left, right):
    return lax.dot_general(left, right, (((1,), (1,)), ((), ())), preferred_element_type=F32)


def dot_grad(left, right):
    return lax.dot_general(left, right, (((0,), (0,)), ((), ())), preferred_element_type=F32)


def make_spread(spread):
    height, width = spread.shape
    head = lax.broadcasted_iota(jnp.int32, (height, width), 0) // HEAD_DIM
    spread[...] = jnp.where(
        head == lax.broadcasted_iota(jnp.int32, (height, width), 1), 1.0, 0.0
    ).astype(BF16)


def pairs_of(positions):
    return [(p, q) for p in range(positions) for q in range(p + 1)]


def split_product(product):
    high = product.astype(BF16)
    return high, (product - high.astype(F32)).astype(BF16)


def sums_over_heads(halves, spread, index):
    return dot(halves[2 * index], spread[...]) + dot(halves[2 * index + 1], spread[...])


def to_heads(values, spread):
    return dot_back(values, spread[...]).astype(BF16)


def attention_probs(qkv, halves, spread, model, position):
    height = qkv.shape[1]
    scale = 1.0 / math.sqrt(HEAD_DIM)

    def products(rows):
        for q in range(position + 1):
            product = qkv[position, rows, :model].astype(F32) * qkv[
                q, rows, model : 2 * model
            ].astype(F32)
            halves[2 * q, rows, :], halves[2 * q + 1, rows, :] = split_product(product)

    row_loop(height, 16, products)
    scores = [sums_over_heads(halves, spread, q) * scale for q in range(position + 1)]
    top = functools.reduce(jnp.maximum, scores)
    powers = [jnp.exp(score - top) for score in scores]
    total = functools.reduce(jnp.add, powers)
    return [power / total for power in powers]


(
    F_TREE,
    F_TREE_END,
    F_GAINS,
    F_PARTS,
    F_COT,
    F_ATTENTION,
    F_GRADS,
    F_ACT_Z,
    F_ACT_X,
    F_ACT_C,
    F_TO_RANK,
    F_OWN_FAR,
    F_OWN_ACROSS,
    F_RANK_FAR,
    F_RANK_ACROSS,
    F_FAR_ACROSS,
    F_FF_END,
    F_BLOCK,
    F_GATE_GRAD,
    F_DOWN_GRAD,
) = range(20)
FORWARD_STEPS = [
    (F_TREE, 3, 0, 0, 0), (F_TREE, 5, 0, 0, 0), (F_TREE, 0, 0, 0, 0), (F_TREE, 2, 0, 0, 0),
    (F_TREE, 5, 1, 0, 0), (F_PARTS,), (F_TO_RANK, 0, 7), (F_TREE, 0, -1, 0, 0), (F_TREE, 0, 0, 0, 1),
    (F_TO_RANK, 0, 3), (F_TREE, 2, 0, 0, 1), (F_TREE, 1, 0, 0, 0), (F_TREE, 0, -2, 0, 0), (F_COT,),
    (F_RANK_FAR, 0, 3), (F_TREE, 0, 0, 1, 0), (F_TREE, 4, 0, 0, 0), (F_TO_RANK, 1, 4), (F_TREE, 1, -1, 0, 0),
    (F_TO_RANK, 0, 2), (F_TO_RANK, 1, 2), (F_TREE, 2, 0, 1, 1), (F_TREE, 0, 1, 0, 0), (F_TREE, 2, 0, 1, 0),
    (F_OWN_ACROSS, 0, 0), (F_TREE, 1, 1, 0, 0), (F_TREE, 2, -1, 0, 0), (F_TREE, 0, -1, 0, 1),
    (F_TREE, 0, -3, 0, 0), (F_TO_RANK, 0, 1), (F_TREE, 0, -2, 0, 1), (F_TREE, 1, 0, 1, 0), (F_TREE, 2, 1, 0, 1),
    (F_TREE, 0, 2, 0, 0), (F_GRADS, 0), (F_TO_RANK, 0, 6), (F_RANK_FAR, 0, 1), (F_OWN_ACROSS, 1, 8),
    (F_TREE, 2, -2, 0, 0), (F_OWN_ACROSS, 0, 8), (F_TREE, 2, -1, 1, 0), (F_TO_RANK, 0, 5), (F_RANK_FAR, 0, 2),
    (F_TREE, 3, 0, 0, 1), (F_OWN_FAR, 0, 8), (F_TREE, 1, -1, 1, 0), (F_TREE, 2, -1, 1, 1), (F_FAR_ACROSS, 0, 2),
    (F_RANK_FAR, 0, 6), (F_TREE, 3, 0, 1, 1), (F_GAINS,), (F_TREE, 2, 1, 0, 0), (F_TREE, 1, 2, 0, 0),
    (F_RANK_ACROSS, 0, 3), (F_TREE, 1, -2, 0, 0), (F_TREE, 0, 3, 0, 0), (F_TREE, 2, 1, 1, 1),
    (F_TREE, 5, 0, 0, 1), (F_TREE, 2, 2, 0, 0), (F_TO_RANK, 0, 4), (F_TREE, 1, 2, 1, 0), (F_TREE, 3, -1, 0, 0),
    (F_TREE, 4, 1, 0, 0), (F_TREE, 0, -1, 1, 1), (F_TREE, 0, 2, 0, 1), (F_RANK_FAR, 0, 7), (F_RANK_FAR, 0, 4),
    (F_FAR_ACROSS, 0, 3), (F_TREE, 2, 2, 1, 1), (F_TREE, 1, 3, 0, 0), (F_TREE, 1, 1, 1, 0),
    (F_RANK_ACROSS, 0, 1), (F_TO_RANK, 1, 6), (F_TREE, 2, -3, 0, 0), (F_TREE, 0, -3, 0, 1),
    (F_TREE, 0, 0, 1, 1), (F_TREE, 1, 2, 0, 1), (F_TREE, 2, 1, 1, 0), (F_TREE, 2, -1, 0, 1),
    (F_TREE, 1, 0, 1, 1), (F_TREE, 2, -2, 1, 0), (F_TREE, 2, 3, 1, 1), (F_FAR_ACROSS, 0, 6), (F_OWN_FAR, 0, 0),
    (F_TREE, 1, -2, 0, 1), (F_TREE, 0, 2, 1, 1), (F_TREE, 4, 2, 0, 0), (F_TREE, 1, 3, 0, 1),
    (F_TREE, 3, 1, 0, 0), (F_TREE, 2, -2, 1, 1), (F_RANK_FAR, 0, 5), (F_TREE, 0, -2, 1, 1),
    (F_TREE, 0, 1, 1, 0), (F_TREE, 5, 0, 1, 0), (F_FAR_ACROSS, 0, 1), (F_TREE, 1, -2, 1, 0),
    (F_TREE, 1, 2, 1, 1), (F_TREE, 2, 2, 1, 0), (F_TREE, 1, -3, 0, 0), (F_TO_RANK, 1, 5), (F_TREE, 0, -1, 1, 0),
    (F_TREE, 3, -2, 0, 0), (F_TREE, 1, 3, 1, 0), (F_ACT_Z, 1, 0), (F_TREE, 0, 1, 0, 1), (F_TREE, 3, 1, 0, 1),
    (F_TREE, 2, 2, 0, 1), (F_TREE, 0, 3, 1, 0), (F_TREE, 4, -1, 0, 0), (F_TREE, 2, -2, 0, 1),
    (F_TREE, 2, -3, 1, 1), (F_TREE, 0, -3, 1, 1), (F_FAR_ACROSS, 0, 7), (F_TREE, 0, -3, 1, 0),
    (F_TREE, 0, 2, 1, 0), (F_TREE, 3, 1, 1, 0), (F_TREE, 2, -3, 1, 0), (F_TREE, 1, -1, 0, 1),
    (F_TREE, 1, -3, 1, 0), (F_RANK_ACROSS, 0, 7), (F_FAR_ACROSS, 0, 0), (F_TREE, 1, 3, 1, 1),
    (F_TREE, 3, 2, 0, 0), (F_TREE, 2, 3, 0, 0), (F_RANK_ACROSS, 0, 6), (F_TREE, 5, 1, 1, 0),
    (F_TREE, 0, 3, 0, 1), (F_TREE, 1, -3, 0, 1), (F_TREE, 3, -2, 0, 1), (F_ACT_C, 1, 0, 0, 0),
    (F_TREE, 4, 0, 1, 0), (F_TREE, 5, 0, 1, 1), (F_TREE, 4, -2, 0, 0), (F_FAR_ACROSS, 0, 4), (F_GRADS, 1),
    (F_TREE, 2, -3, 0, 1), (F_TREE, 5, -1, 1, 0), (F_TREE, 1, -3, 1, 1), (F_ACT_C, 1, 0, 1, 0),
    (F_FAR_ACROSS, 0, 8), (F_TREE, 5, 1, 0, 1), (F_FAR_ACROSS, 0, 5), (F_TREE, 1, -1, 1, 1),
    (F_TREE, 1, 0, 0, 1), (F_RANK_ACROSS, 0, 5), (F_TREE, 5, -1, 0, 0), (F_TREE, 3, -3, 0, 0),
    (F_TO_RANK, 1, 1), (F_ACT_X, 1, 0, 1), (F_TREE, 1, 1, 0, 1), (F_TREE, 5, 2, 1, 0), (F_OWN_FAR, 1, 8),
    (F_ACT_X, 1, 0, 0), (F_TREE, 5, -1, 0, 1), (F_TREE, 4, -3, 0, 0), (F_TREE, 0, 1, 1, 1),
    (F_TREE, 1, 1, 1, 1), (F_TREE, 2, 3, 0, 1), (F_TREE, 3, 1, 1, 1), (F_TREE, 3, -1, 0, 1),
    (F_TREE, 4, -1, 1, 0), (F_TREE, 3, -3, 0, 1), (F_TREE, 3, 2, 0, 1), (F_OWN_ACROSS, 1, 0),
    (F_TREE, 1, -2, 1, 1), (F_TO_RANK, 1, 3), (F_TREE, 3, 0, 1, 0), (F_TREE, 0, 3, 1, 1), (F_TREE, 0, -2, 1, 0),
    (F_TREE, 3, 2, 1, 0), (F_TREE, 2, 3, 1, 0), (F_TREE, 3, 3, 0, 0), (F_TREE_END, 0), (F_TREE, 4, -1, 1, 1),
    (F_TO_RANK, 1, 7), (F_ATTENTION, 0), (F_TREE, 4, 3, 0, 0), (F_ACT_X, 0, 0, 0), (F_TREE, 4, 3, 1, 0),
    (F_TREE, 3, -3, 1, 0), (F_TREE, 4, 3, 0, 1), (F_TREE, 4, -2, 1, 0), (F_TREE, 3, 3, 0, 1),
    (F_TREE, 5, -1, 1, 1), (F_RANK_FAR, 1, 7), (F_RANK_ACROSS, 0, 2), (F_TREE, 4, 2, 1, 0),
    (F_TREE, 5, 1, 1, 1), (F_TREE, 5, 3, 1, 0), (F_TREE, 4, -3, 0, 1), (F_RANK_ACROSS, 0, 4),
    (F_TREE, 4, -3, 1, 0), (F_OWN_FAR, 1, 0), (F_RANK_FAR, 1, 2), (F_TREE, 4, 3, 1, 1), (F_RANK_ACROSS, 1, 7),
    (F_FAR_ACROSS, 1, 8), (F_TREE, 4, 1, 1, 0), (F_ACT_Z, 1, 1), (F_TREE, 5, -2, 0, 1), (F_TREE, 4, -3, 1, 1),
    (F_TREE, 3, 2, 1, 1), (F_TREE, 5, -2, 0, 0), (F_ACT_Z, 0, 0), (F_TREE, 4, 2, 1, 1), (F_TREE, 5, 2, 0, 0),
    (F_RANK_FAR, 1, 1), (F_FF_END, 0), (F_ACT_C, 0, 0, 1, 0), (F_RANK_ACROSS, 1, 2), (F_TREE, 4, 0, 0, 1),
    (F_TREE, 4, 1, 1, 1), (F_RANK_FAR, 1, 5), (F_ACT_X, 1, 1, 0), (F_TREE, 3, -1, 1, 0), (F_TREE, 5, 2, 1, 1),
    (F_TREE, 5, 3, 0, 0), (F_FAR_ACROSS, 1, 7), (F_TREE, 3, 3, 1, 1), (F_TREE, 3, -1, 1, 1),
    (F_TREE, 4, -2, 1, 1), (F_ACT_C, 1, 0, 0, 1), (F_ACT_C, 0, 0, 0, 0), (F_TREE, 4, 0, 1, 1),
    (F_RANK_FAR, 1, 3), (F_ACT_C, 1, 0, 1, 1), (F_TREE, 3, -2, 1, 0), (F_TREE, 5, -2, 1, 0), (F_RANK_FAR, 1, 4),
    (F_FAR_ACROSS, 1, 0), (F_TREE, 5, -3, 0, 0), (F_TREE, 4, 1, 0, 1), (F_TREE, 3, -2, 1, 1),
    (F_ACT_C, 1, 1, 1, 0), (F_RANK_FAR, 1, 6), (F_TREE, 4, -1, 0, 1), (F_TREE, 5, 2, 0, 1),
    (F_TREE, 5, -3, 1, 0), (F_ACT_C, 0, 0, 0, 1), (F_FAR_ACROSS, 1, 2), (F_ACT_C, 1, 1, 0, 0),
    (F_TREE, 5, -3, 0, 1), (F_TREE, 5, -2, 1, 1), (F_TREE, 3, 3, 1, 0), (F_RANK_ACROSS, 1, 6),
    (F_RANK_ACROSS, 1, 3), (F_TREE, 5, 3, 1, 1), (F_RANK_ACROSS, 1, 4), (F_BLOCK, 0, 1), (F_TREE, 4, 2, 0, 1),
    (F_TREE, 5, 3, 0, 1), (F_TREE, 4, -2, 0, 1), (F_TREE, 3, -3, 1, 1), (F_FAR_ACROSS, 1, 1),
    (F_TREE, 5, -3, 1, 1), (F_BLOCK, 0, 0), (F_RANK_ACROSS, 1, 5), (F_ACT_X, 1, 1, 1), (F_TREE_END, 1),
    (F_ATTENTION, 1), (F_FAR_ACROSS, 1, 3), (F_RANK_ACROSS, 1, 1), (F_ACT_X, 0, 0, 1), (F_BLOCK, 0, 2),
    (F_FAR_ACROSS, 1, 5), (F_ACT_C, 0, 0, 1, 1), (F_BLOCK, 0, 3), (F_DOWN_GRAD, 0), (F_ACT_C, 1, 1, 0, 1),
    (F_FAR_ACROSS, 1, 6), (F_ACT_X, 0, 1, 0), (F_ACT_C, 1, 1, 1, 1), (F_ACT_Z, 0, 1), (F_FAR_ACROSS, 1, 4),
    (F_GATE_GRAD, 0), (F_ACT_C, 0, 1, 0, 1), (F_ACT_C, 0, 1, 0, 0), (F_FF_END, 1), (F_ACT_C, 0, 1, 1, 0),
    (F_BLOCK, 1, 1), (F_BLOCK, 1, 2), (F_ACT_X, 0, 1, 1), (F_BLOCK, 1, 0), (F_ACT_C, 0, 1, 1, 1),
    (F_BLOCK, 1, 3), (F_DOWN_GRAD, 1), (F_GATE_GRAD, 1),
]


def forward_kernel(
    valid_ref,
    lengths_ref,
    norm_attn_ref,
    norm_ff_ref,
    tokens_ref,
    cot_ref,
    qkv_ref,
    out_ref,
    gate_up_ref,
    down_ref,
    gain_rows,
    cot_rows,
    qkv_rows,
    context,
    resid_mid,
    qkv_full,
    out_full,
    ff_out,
    ff_back,
    gate_up_grad,
    down_grad,
    qkv_buf,
    out_buf,
    gate_up_buf,
    down_buf,
    rows_buf,
    grads_buf,
    hidden,
    d_gate_up,
    out_stage,
    back_stage,
    gate_up_stage,
    down_stage,
    gains_own,
    gains_all,
    gate_up_raw,
    gate_up_parts,
    grads_own,
    attn_in,
    halves,
    spread,
    plane_sem,
    sibling_sem,
    send_sem,
    gains_send,
    gains_recv,
    rank_send,
    rank_recv,
    far_send,
    far_recv,
    across_send,
    across_recv,
    act_send,
    act_recv,
    local_sem,
    keep_sem,
    stage_sem,
):
    z, y, x, core = here()
    me = 2 * (z * 4 + y * 2 + x) + core
    zh, zl, member, rank, device, far, across = group_place(z, y, x, core)
    own_step = (0, 0, 0)
    act_height, positions, model = tokens_ref.shape
    height = gate_up_ref.shape[1]
    down_height = down_ref.shape[1]
    split = 4 * down_height
    sibling = neighbour("s", z, y, x, core)
    greet_all(z, y, x, core)
    part = qkv_ref.shape[2] // 2
    pieces = []
    for s in range(positions):
        pieces.append((qkv_ref, qkv_buf, s, pl.ds(0, part), "zxy"))
        pieces.append((qkv_ref, qkv_buf, s, pl.ds(part, part), "zyx"))
        pieces.append((out_ref, out_buf, s, pl.ds(0, model), ("xyz", "yxz")[s % 2]))

    def piece_rows(piece, number):
        _, full, index, columns, _ = pieces[piece]
        return full.at[index, pl.ds(pl.multiple_of(number * height, height), height), columns]

    def tree_send(piece, offset, direction):
        source, _, index, columns, _ = pieces[piece]
        chip = chip_of(offset, z, y, x)
        block = piece_rows(piece, 2 * chip + core)
        recv = sibling_sem if direction == "s" else plane_sem
        return push(
            source.at[index, :, columns] if hops(offset) == 0 else block,
            block,
            send_sem.at[piece, chip, DIRECTIONS.index(direction)],
            recv.at[piece, chip],
            neighbour(direction, z, y, x, core),
        )

    def tree_step(piece, offset, finish=False):
        order = pieces[piece][4]

        def go():
            chip = chip_of(offset, z, y, x)
            if hops(offset) > 0 and not finish:
                arrived(piece_rows(piece, 2 * chip + core), plane_sem.at[piece, chip], sibling)
            for direction in onward(order, offset) + ["s"]:
                copy = tree_send(piece, offset, direction)
                maybe(direction_exists(direction, z), copy.wait_send if finish else copy.start)

        maybe(offset_exists(offset, z), go)

    events = sorted(
        (
            (hops(offset), place, piece, offset)
            for piece in range(len(pieces))
            for place, offset in enumerate(OFFSETS)
        ),
        key=lambda event: event[:3],
    )

    def tree_steps(s, distance):
        for hop, _, piece, offset in events:
            if hop == distance and pieces[piece][2] == s:
                tree_step(piece, offset)

    def tree_end(s):
        mine = [piece for piece in range(len(pieces)) if pieces[piece][2] == s]

        def sibling_wait(chip, carry):
            for piece in mine:
                arrived(piece_rows(piece, 2 * chip + 1 - core), sibling_sem.at[piece, chip], sibling)
            return carry

        lax.fori_loop(0, 16, sibling_wait, 0)
        for piece in mine:
            tree_own[piece].wait()

    tree_own = [
        pltpu.make_async_copy(
            source.at[index, :, columns], piece_rows(piece, me), local_sem.at[piece]
        )
        for piece, (source, _, index, columns, _) in enumerate(pieces)
    ]

    def gains_copy(step):
        other = lax.rem(me + step, 32)
        return push(
            gains_own,
            gains_all.at[me],
            gains_send.at[step],
            gains_recv.at[me],
            (lax.div(other, 2), lax.rem(other, 2)),
        )

    def gains_start(step, carry):
        gains_copy(step).start()
        return carry

    def gains_wait(step, carry):
        other = lax.rem(me + step, 32)
        gains_copy(step).wait_send()
        arrived(gains_all.at[other], gains_recv.at[other], sibling)
        return carry

    sends = []

    def start(copy):
        copy.start()
        sends.append(copy)

    def weight_rows(s, number):
        return gate_up_buf.at[s, pl.ds(pl.multiple_of(number * height, height), height), :]

    def down_rows(s, dzh, dy):
        number = 2 * flip(zh, dzh) + flip(y, dy)
        return down_buf.at[s, pl.ds(pl.multiple_of(number * down_height, down_height), down_height), :]

    def act_rows(which, s, step):
        full = (rows_buf, grads_buf)[which]
        return full.at[s, pl.ds(pl.multiple_of(rank(step) * act_height, act_height), act_height), :]

    def send_act(which, s, step, source, hop):
        landed = tuple(bit ^ (1 if axis == hop else 0) for axis, bit in enumerate(step))
        start(
            push(
                source,
                act_rows(which, s, step),
                act_send.at[which, s, 4 * step[0] + 2 * step[1] + step[2], hop],
                act_recv.at[which, s, 4 * landed[0] + 2 * landed[1] + landed[2]],
                member(tuple(1 if axis == hop else 0 for axis in range(3))),
            )
        )

    def wait_act(which, s, step):
        arrived(
            act_rows(which, s, step),
            act_recv.at[which, s, 4 * step[0] + 2 * step[1] + step[2]],
            sibling,
        )

    def act_own(which, s):
        source = act_rows(0, s, own_step) if which == 0 else grads_own.at[s]
        for hop in (0, 1, 2):
            send_act(which, s, own_step, source, hop)

    def act_from_z(which, s):
        step = (1, 0, 0)
        wait_act(which, s, step)
        send_act(which, s, step, act_rows(which, s, step), 1)
        send_act(which, s, step, act_rows(which, s, step), 2)

    def act_from_x(which, s, dl):
        wait_act(which, s, (dl, 1, 0))
        send_act(which, s, (dl, 1, 0), act_rows(which, s, (dl, 1, 0)), 2)

    def act_from_core(which, s, dl, dx):
        wait_act(which, s, (dl, dx, 1))

    def mine(s):
        return gate_up_parts.at[rank(own_step), s]

    def ff_source(s, slot):
        return down_ref.at[s] if slot == 8 else mine(s)

    def ff_rows(s, slot, dzh):
        return down_rows(s, dzh, 0) if slot == 8 else weight_rows(s, device(RANK_STEPS[slot], dzh, 0))

    def to_rank(s, slot):
        step = RANK_STEPS[slot]
        start(
            push(
                gate_up_parts.at[rank(step), s],
                weight_rows(s, device(own_step)),
                rank_send.at[s, slot],
                rank_recv.at[s, slot],
                member(step),
            )
        )

    def send_far(s, slot, source):
        start(push(source, ff_rows(s, slot, 0), far_send.at[s, slot], far_recv.at[s, slot], far))

    def send_across(s, slot, source, dzh):
        start(
            push(
                source,
                ff_rows(s, slot, dzh),
                across_send.at[s, dzh, slot],
                across_recv.at[s, dzh, slot],
                across,
            )
        )

    def own_far(s, slot):
        send_far(s, slot, ff_source(s, slot))

    def own_across(s, slot):
        send_across(s, slot, ff_source(s, slot), 0)

    def rank_far(s, slot):
        arrived(ff_rows(s, slot, 0), rank_recv.at[s, slot], sibling)
        send_far(s, slot, ff_rows(s, slot, 0))

    def rank_across(s, slot):
        send_across(s, slot, ff_rows(s, slot, 0), 0)

    def far_across(s, slot):
        arrived(ff_rows(s, slot, 1), far_recv.at[s, slot], sibling)
        send_across(s, slot, ff_rows(s, slot, 1), 1)

    def ff_end(s):
        for copy in ff_local[s]:
            copy.wait()
        for dzh in (0, 1):
            for slot, step in enumerate(RANK_STEPS):
                arrived(weight_rows(s, device(step, dzh, 1)), across_recv.at[s, dzh, slot], sibling)
            arrived(down_rows(s, dzh, 1), across_recv.at[s, dzh, 8], sibling)

    ff_local = []
    for s in range(positions):
        ff_local.append(
            [
                pltpu.make_async_copy(mine(s), weight_rows(s, device(own_step)), local_sem.at[7 + 3 * s]),
                pltpu.make_async_copy(down_ref.at[s], down_rows(s, 0, 0), local_sem.at[8 + 3 * s]),
                pltpu.make_async_copy(grads_own.at[s], act_rows(1, s, own_step), local_sem.at[9 + 3 * s]),
            ]
        )
    gains_local = pltpu.make_async_copy(gains_own, gains_all.at[me], local_sem.at[6])

    def gains_begin():
        places = 128 // norm_attn_ref.shape[1]
        lane = lax.broadcasted_iota(jnp.int32, (positions, 128), 1) // norm_attn_ref.shape[1]
        gains_own[...] = jnp.zeros_like(gains_own)
        for index, source in enumerate((norm_attn_ref, norm_ff_ref)):
            tiled = jnp.concatenate([source[...].astype(F32)] * places, axis=1)
            gains_own[index * positions : (index + 1) * positions, :] = jnp.where(
                lane == lax.rem(me, places), tiled, 0.0
            ).astype(BF16)
        lax.fori_loop(1, 32, gains_start, 0)
        gains_local.start()

    raw_copy = pltpu.make_async_copy(gate_up_ref, gate_up_raw, local_sem.at[13])

    def part_units():
        raw_copy.wait()
        unit = down_height
        for number in range(8):
            low, rest = divmod(number, 4)
            for s in range(positions):
                for side in (0, 1):
                    for group in range(4):
                        zh_part, y_part = divmod(group, 2)
                        block = 32 * side + 16 * zh_part + 8 * low + 4 * y_part + rest
                        gate_up_parts[number, s, :, (4 * side + group) * unit : (4 * side + group + 1) * unit] = (
                            gate_up_raw[s, :, block * unit : (block + 1) * unit]
                        )
        for s in range(positions):
            ff_local[s][0].start()
            ff_local[s][1].start()

    def weigh():
        def one(rows):
            slot = lax.broadcasted_iota(jnp.int32, (16, 128), 0) + rows.start
            frame = me * act_height + slot
            weight = jnp.zeros((16, 128), F32)
            first = 0
            for item in range(lengths_ref.shape[0]):
                length = lengths_ref[item]
                inside = (frame >= first) & (frame < first + length)
                share = 8.0 * act_height / jnp.full((16, 128), length, jnp.int32).astype(F32)
                weight = weight + jnp.where(inside, share, 0.0)
                first = first + length
            weight = jnp.where(slot < valid_ref[0], weight, 0.0)[:, :1]
            values = cot_ref[rows].astype(F32)
            for p in range(positions):
                grads = values[:, p, :] * weight
                cot_rows[p, rows, :] = grads
                grads_own[p, rows, :] = grads.astype(BF16)

        row_loop(act_height, 16, one)
        for s in range(positions):
            ff_local[s][2].start()

    def take_gains():
        lax.fori_loop(1, 32, gains_wait, 0)
        gains_local.wait()
        for block in range(8):
            total = gains_all[4 * block].astype(F32)
            for extra in range(1, 4):
                total = total + gains_all[4 * block + extra].astype(F32)
            gain_rows[:, 128 * block : 128 * block + 128] = total

        def first_norm(rows):
            values = tokens_ref[rows].astype(F32)
            for p in range(positions):
                resid_mid[p, rows, :] = values[:, p, :]
                r, _ = normed(values[:, p, :])
                attn_in[p, rows, :] = (r * gain_rows[p : p + 1, :]).astype(BF16)

        row_loop(act_height, 16, first_norm)

    keep = []

    def attention(p):
        for source, target, slot in (
            (qkv_buf.at[p], qkv_full.at[p], 2 * p),
            (out_buf.at[p], out_full.at[p], 2 * p + 1),
        ):
            keep.append(pltpu.make_async_copy(source, target, keep_sem.at[slot]))
            keep[-1].start()

        def project(columns):
            qkv_rows[p, :, columns] = dot(attn_in[p], qkv_buf[p, :, columns]).astype(BF16)

        tile_loop(3 * model, 512, project)
        probs = attention_probs(qkv_rows, halves, spread, model, p)
        for q in range(p + 1):
            halves[2 * q] = to_heads(probs[q].astype(BF16), spread)

        def mix(rows):
            total = None
            for q in range(p + 1):
                term = halves[2 * q, rows, :].astype(F32) * qkv_rows[q, rows, 2 * model :].astype(F32)
                total = term if total is None else total + term
            context[p, rows, :] = total.astype(BF16)

        row_loop(act_height, 16, mix)

        def attend(columns):
            resid_mid[p, :, columns] += dot(context[p], out_buf[p, :, columns])

        tile_loop(model, 512, attend)

        def second_norm(step, carry):
            rows = pl.ds(pl.multiple_of(step * 16, 16), 16)
            r, _ = normed(resid_mid[p, rows, :])
            top = rank(own_step) * act_height + step * 16
            rows_buf[p, pl.ds(pl.multiple_of(top, 16), 16), :] = (
                r * gain_rows[positions + p : positions + p + 1, :]
            ).astype(BF16)
            return carry

        lax.fori_loop(0, act_height // 16, second_norm, 0)

    def ff_block(s, number):
        rows = pl.ds(pl.multiple_of(number * 2 * act_height, 2 * act_height), 2 * act_height)
        normed_rows = rows_buf[s, rows, :]
        grads = grads_buf[s, rows, :]
        for tile in range(split // 256):
            left, right = pl.ds(tile * 256, 256), pl.ds(split + tile * 256, 256)
            gate = dot(normed_rows, gate_up_buf[s, :, left])
            up = dot(normed_rows, gate_up_buf[s, :, right])
            d_hidden = dot_back(grads, down_buf[s, left, :])
            sigmoid_gate = jax.nn.sigmoid(gate)
            silu_gate = gate * sigmoid_gate
            hidden[rows, left] = (silu_gate * up).astype(BF16)
            d_gate_up[rows, left] = (
                d_hidden * up * sigmoid_gate * (1.0 + gate * (1.0 - sigmoid_gate))
            ).astype(BF16)
            d_gate_up[rows, right] = (d_hidden * silu_gate).astype(BF16)
        for tile in range(model // 512):
            columns = pl.ds(tile * 512, 512)
            out_stage[rows, columns] = dot(hidden[rows, :], down_buf[s, :, columns]).astype(BF16)
            back_stage[rows, columns] = dot_back(
                d_gate_up[rows, :], gate_up_buf[s, columns, :]
            ).astype(BF16)

    stages = []

    def stage_out(s, *slots):
        for slot in slots:
            source, target = (
                (out_stage, ff_out),
                (back_stage, ff_back),
                (gate_up_stage, gate_up_grad),
                (down_stage, down_grad),
            )[slot]
            stages.append(pltpu.make_async_copy(source, target.at[s], stage_sem.at[s, slot]))
            stages[-1].start()

    def gate_grad(s):
        stage_out(s, 0, 1)

        def gate_up_tile(columns):
            gate_up_stage[:, columns] = dot_grad(rows_buf[s], d_gate_up[:, columns]).astype(BF16)

        tile_loop(2 * split, 256, gate_up_tile)
        stage_out(s, 2)

    def down_weights_grad(s):
        def down_tile(columns):
            down_stage[:, columns] = dot_grad(hidden[...], grads_buf[s, :, columns]).astype(BF16)

        tile_loop(model, 256, down_tile)
        stage_out(s, 3)

    def stages_end():
        while stages:
            stages.pop(0).wait()

    for copy in tree_own:
        copy.start()
    raw_copy.start()
    gains_begin()
    make_spread(spread)
    chips = ((0, 0), (1, 0), (0, 1), (1, 1))

    def block(s, order):
        if s > 0 and order == chosen_first[0]:
            stages_end()
        ff_block(s, 2 * flip(zl, chips[order][0]) + flip(x, chips[order][1]))

    def attend_and_send(s):
        attention(s)
        act_own(0, s)

    chosen_first = [step[2] for step in FORWARD_STEPS if step[:2] == (F_BLOCK, 1)]
    kinds = {
        F_TREE: lambda piece, dz, dy, dx: tree_step(piece, (dz, dy, dx)),
        F_TREE_END: tree_end,
        F_GAINS: take_gains,
        F_PARTS: part_units,
        F_COT: weigh,
        F_ATTENTION: attend_and_send,
        F_GRADS: lambda s: act_own(1, s),
        F_ACT_Z: act_from_z,
        F_ACT_X: act_from_x,
        F_ACT_C: act_from_core,
        F_TO_RANK: to_rank,
        F_OWN_FAR: own_far,
        F_OWN_ACROSS: own_across,
        F_RANK_FAR: rank_far,
        F_RANK_ACROSS: rank_across,
        F_FAR_ACROSS: far_across,
        F_FF_END: ff_end,
        F_BLOCK: block,
        F_GATE_GRAD: gate_grad,
        F_DOWN_GRAD: down_weights_grad,
    }
    for kind, *numbers in FORWARD_STEPS:
        kinds[kind](*numbers)
    for _, _, piece, offset in events:
        tree_step(piece, offset, finish=True)
    for copy in sends:
        copy.wait_send()
    for copy in keep:
        copy.wait()
    stages_end()


def forward_gather(valid, lengths, norm_attn, norm_ff, tokens, cot, w_qkv, w_out, w_gate_up, w_down):
    act_height, positions, model = tokens.shape
    _, height, qkv_width = w_qkv.shape
    unit = w_down.shape[1]
    ranks, split, width = 8, 4 * unit, 8 * unit
    group_rows = ranks * act_height
    dma = pltpu.SemaphoreType.DMA
    vmem = pl.BlockSpec(memory_space=pltpu.VMEM)
    smem = pl.BlockSpec(memory_space=pltpu.SMEM)
    anywhere = pl.BlockSpec(memory_space=pl.ANY)
    return pl.pallas_call(
        forward_kernel,
        out_shape=(
            jax.ShapeDtypeStruct((16, model), F32),
            jax.ShapeDtypeStruct((positions, act_height, model), F32),
            jax.ShapeDtypeStruct((positions, act_height, 3 * model), BF16),
            jax.ShapeDtypeStruct((positions, act_height, model), BF16),
            jax.ShapeDtypeStruct((positions, act_height, model), F32),
            jax.ShapeDtypeStruct((positions, model, qkv_width), BF16),
            jax.ShapeDtypeStruct((positions, model, model), BF16),
            jax.ShapeDtypeStruct((positions, group_rows, model), BF16),
            jax.ShapeDtypeStruct((positions, group_rows, model), BF16),
            jax.ShapeDtypeStruct((positions, model, width), BF16),
            jax.ShapeDtypeStruct((positions, split, model), BF16),
        ),
        in_specs=[smem] * 2 + [vmem] * 4 + [anywhere] * 4,
        out_specs=(vmem,) * 5 + (anywhere,) * 6,
        scratch_shapes=[
            pltpu.VMEM((positions, model, qkv_width), BF16),
            pltpu.VMEM((positions, model, model), BF16),
            pltpu.VMEM((positions, model, width), BF16),
            pltpu.VMEM((positions, split, model), BF16),
            pltpu.VMEM((positions, group_rows, model), BF16),
            pltpu.VMEM((positions, group_rows, model), BF16),
            pltpu.VMEM((group_rows, split), BF16),
            pltpu.VMEM((group_rows, width), BF16),
            pltpu.VMEM((group_rows, model), BF16),
            pltpu.VMEM((group_rows, model), BF16),
            pltpu.VMEM((model, width), BF16),
            pltpu.VMEM((split, model), BF16),
            pltpu.VMEM((16, 128), BF16),
            pltpu.VMEM((32, 16, 128), BF16),
            pltpu.VMEM(w_gate_up.shape, BF16),
            pltpu.VMEM((ranks, positions, height, width), BF16),
            pltpu.VMEM((positions, act_height, model), BF16),
            pltpu.VMEM((positions, act_height, model), BF16),
            pltpu.VMEM((2 * positions, act_height, model), BF16),
            pltpu.VMEM((model, 128), BF16),
            dma((6, 16)),
            dma((6, 16)),
            dma((6, 16, 5)),
            dma((32,)),
            dma((32,)),
            dma((2, 8)),
            dma((2, 8)),
            dma((2, 9)),
            dma((2, 9)),
            dma((2, 2, 9)),
            dma((2, 2, 9)),
            dma((2, 2, 8, 3)),
            dma((2, 2, 8)),
            dma((14,)),
            dma((4,)),
            dma((2, 4)),
        ],
        compiler_params=pltpu.CompilerParams(
            collective_id=4, has_side_effects=True, vmem_limit_bytes=62 * 2**20
        ),
        name="forward_gather",
    )(valid, lengths, norm_attn, norm_ff, tokens, cot, w_qkv, w_out, w_gate_up, w_down)


def slot_index(order, direction, offset, z, y, x):
    axis = {"u": "z", "d": "z"}.get(direction, direction)
    index, count = 0, 1
    values = dict(z=z + offset[0], y=flip(y, offset[1]), x=flip(x, offset[2]))
    sizes = dict(z=4, y=2, x=2)
    for earlier in order[: order.index(axis)]:
        index = index * sizes[earlier] + values[earlier]
        count *= sizes[earlier]
    if axis == "z":
        index = index * 5 + (4 if direction == "d" and offset[0] == 0 else values["z"])
        count *= 5
    return index, count


def slot_base(order):
    base, total = {}, 0
    for axis, direction in (("x", "x"), ("y", "y"), ("z", "u")):
        base[axis] = total
        total += slot_index(order, direction, (0, 0, 0), 0, 0, 0)[1]
    base["u"] = base["d"] = base["z"]
    return base, total


(
    B_TREE,
    B_RS_ACROSS,
    B_RS_FIRST,
    B_RS_SECOND,
    B_RS_RANK,
    B_RS_LAST,
    B_ACT_CORE,
    B_ACT_LOAD,
    B_ACT_ADD_X,
    B_ACT_ADD_Z,
    B_ACT_SUM,
    B_NORM_TURN,
    B_SWAP_TURNED,
    B_PROBS,
    B_MID,
    B_SCORES_BACK,
    B_SWAP_QKV,
    B_OUT_W,
    B_QKV_W,
    B_ROWS_BACK,
    B_ATTN_BACK,
    B_FINISH_OUTPUT,
) = range(22)
BACKWARD_STEPS = [
    (B_RS_ACROSS, 0, 0, 0), (B_ACT_CORE, 0, 0), (B_ACT_ADD_X, 0, 0, 1), (B_NORM_TURN,), (B_RS_FIRST, 0, 0),
    (B_RS_ACROSS, 0, 0, 1), (B_ACT_CORE, 0, 1), (B_ACT_ADD_Z, 0, 0), (B_ACT_ADD_X, 0, 0, 0),
    (B_ACT_ADD_X, 0, 1, 1), (B_RS_ACROSS, 1, 1, 0), (B_SWAP_TURNED,), (B_RS_ACROSS, 0, 1, 0),
    (B_RS_ACROSS, 0, 0, 2), (B_ACT_ADD_X, 0, 1, 0), (B_RS_FIRST, 0, 1), (B_RS_ACROSS, 1, 0, 1),
    (B_RS_ACROSS, 0, 1, 1), (B_PROBS,), (B_RS_ACROSS, 1, 1, 1), (B_ACT_ADD_Z, 0, 1), (B_RS_FIRST, 0, 2),
    (B_ACT_CORE, 1, 0), (B_ACT_SUM, 0, 0), (B_ACT_SUM, 0, 1), (B_MID, 1), (B_MID, 0), (B_ACT_LOAD, 1),
    (B_OUT_W, 0), (B_OUT_W, 1), (B_ACT_CORE, 1, 1), (B_ACT_ADD_X, 1, 0, 1), (B_RS_FIRST, 1, 1),
    (B_TREE, 2, -3, 0, 0), (B_SCORES_BACK,), (B_TREE, 2, -3, 1, 1), (B_TREE, 3, 3, 0, 0),
    (B_RS_ACROSS, 1, 0, 2), (B_SWAP_QKV,), (B_ACT_ADD_X, 1, 0, 0), (B_TREE, 3, 3, 0, 1), (B_TREE, 2, 3, 1, 0),
    (B_TREE, 3, -3, 0, 1), (B_RS_SECOND, 0, 1), (B_TREE, 2, -3, 0, 1), (B_QKV_W, 0), (B_ACT_ADD_X, 1, 1, 1),
    (B_TREE, 2, 3, 1, 1), (B_RS_FIRST, 1, 2), (B_RS_ACROSS, 0, 1, 2), (B_TREE, 0, -1, 1, 1),
    (B_RS_ACROSS, 1, 0, 0), (B_QKV_W, 1), (B_TREE, 2, 2, 1, 1), (B_TREE, 1, 2, 1, 1), (B_TREE, 2, 3, 0, 0),
    (B_TREE, 2, 2, 1, 0), (B_TREE, 0, -3, 1, 1), (B_RS_SECOND, 0, 0), (B_RS_ACROSS, 1, 1, 2),
    (B_TREE, 1, 1, 1, 1), (B_TREE, 2, 3, 0, 1), (B_TREE, 0, 1, 1, 1), (B_TREE, 1, -3, 1, 1),
    (B_TREE, 1, -1, 0, 1), (B_TREE, 2, -2, 1, 1), (B_TREE, 0, 3, 1, 0), (B_TREE, 3, -3, 1, 0),
    (B_TREE, 1, 0, 1, 1), (B_RS_RANK, 0, 1), (B_TREE, 3, 2, 0, 1), (B_TREE, 2, -3, 1, 0), (B_TREE, 2, -1, 1, 1),
    (B_TREE, 3, 3, 1, 0), (B_TREE, 2, -2, 0, 0), (B_TREE, 3, -2, 0, 1), (B_TREE, 1, -3, 0, 1),
    (B_TREE, 3, 3, 1, 1), (B_TREE, 0, 3, 1, 1), (B_TREE, 3, -3, 1, 1), (B_RS_SECOND, 1, 1), (B_RS_RANK, 0, 3),
    (B_RS_FIRST, 1, 0), (B_TREE, 0, -2, 1, 1), (B_TREE, 2, 2, 0, 1), (B_TREE, 0, -3, 0, 1),
    (B_ACT_ADD_X, 1, 1, 0), (B_RS_RANK, 0, 4), (B_TREE, 3, -2, 1, 1), (B_TREE, 2, 1, 1, 0),
    (B_TREE, 0, 0, 1, 0), (B_TREE, 0, -3, 1, 0), (B_TREE, 3, -2, 1, 0), (B_ACT_ADD_Z, 1, 1),
    (B_TREE, 2, 2, 0, 0), (B_TREE, 1, -2, 1, 1), (B_TREE, 3, -1, 0, 1), (B_ROWS_BACK, 0), (B_TREE, 1, 3, 1, 1),
    (B_TREE, 0, -1, 1, 0), (B_TREE, 3, 2, 1, 0), (B_TREE, 2, -1, 0, 0), (B_TREE, 2, -2, 1, 0),
    (B_TREE, 2, -2, 0, 1), (B_TREE, 3, 2, 1, 1), (B_TREE, 0, 2, 1, 1), (B_TREE, 1, 3, 0, 1),
    (B_TREE, 0, 3, 0, 1), (B_RS_RANK, 0, 7), (B_TREE, 1, -3, 1, 0), (B_TREE, 1, 1, 0, 1), (B_TREE, 2, 1, 1, 1),
    (B_ACT_ADD_Z, 1, 0), (B_TREE, 3, 1, 0, 1), (B_TREE, 1, -2, 1, 0), (B_TREE, 0, -2, 1, 0),
    (B_TREE, 0, 0, 1, 1), (B_TREE, 1, -1, 1, 1), (B_RS_SECOND, 1, 0), (B_TREE, 2, 1, 0, 0),
    (B_TREE, 0, -2, 0, 1), (B_TREE, 3, -1, 1, 1), (B_RS_LAST, 0, 4), (B_TREE, 3, 2, 0, 0), (B_RS_RANK, 1, 2),
    (B_TREE, 3, -3, 0, 0), (B_ACT_SUM, 1, 0), (B_TREE, 1, -2, 0, 1), (B_TREE, 2, 1, 0, 1),
    (B_TREE, 0, -3, 0, 0), (B_TREE, 1, 3, 1, 0), (B_TREE, 0, 2, 0, 1), (B_RS_RANK, 1, 7), (B_TREE, 0, -1, 0, 1),
    (B_TREE, 2, -1, 1, 0), (B_TREE, 2, -1, 0, 1), (B_TREE, 1, -3, 0, 0), (B_TREE, 3, 1, 1, 1),
    (B_RS_RANK, 1, 5), (B_RS_RANK, 0, 6), (B_RS_LAST, 0, 7), (B_TREE, 0, 1, 1, 0), (B_TREE, 0, 2, 1, 0),
    (B_TREE, 3, 1, 1, 0), (B_TREE, 2, 0, 1, 1), (B_TREE, 0, 3, 0, 0), (B_RS_LAST, 1, 2), (B_TREE, 1, -1, 1, 0),
    (B_ACT_SUM, 1, 1), (B_FINISH_OUTPUT,), (B_TREE, 1, 3, 0, 0), (B_TREE, 0, -2, 0, 0), (B_TREE, 1, 2, 0, 1),
    (B_TREE, 1, 0, 1, 0), (B_TREE, 3, 1, 0, 0), (B_RS_RANK, 1, 6), (B_TREE, 3, -1, 1, 0), (B_RS_RANK, 0, 2),
    (B_RS_RANK, 1, 1), (B_TREE, 0, 2, 0, 0), (B_ROWS_BACK, 1), (B_RS_LAST, 1, 1), (B_TREE, 1, 0, 0, 1),
    (B_TREE, 0, 1, 0, 1), (B_TREE, 1, 2, 1, 0), (B_TREE, 3, -2, 0, 0), (B_RS_LAST, 0, 6), (B_RS_LAST, 1, 6),
    (B_TREE, 0, 0, 0, 1), (B_RS_RANK, 0, 5), (B_TREE, 2, 0, 1, 0), (B_TREE, 2, 0, 0, 1), (B_RS_LAST, 1, 5),
    (B_TREE, 1, 1, 1, 0), (B_TREE, 3, 0, 0, 1), (B_TREE, 1, -2, 0, 0), (B_TREE, 1, 2, 0, 0), (B_ATTN_BACK,),
    (B_TREE, 3, -1, 0, 0), (B_TREE, 0, -1, 0, 0), (B_TREE, 0, 1, 0, 0), (B_TREE, 1, -1, 0, 0),
    (B_RS_SECOND, 1, 2), (B_TREE, 1, 1, 0, 0), (B_TREE, 3, 0, 1, 1), (B_RS_SECOND, 0, 2), (B_RS_LAST, 0, 3),
    (B_RS_LAST, 0, 1), (B_RS_LAST, 0, 2), (B_TREE, 0, 0, 0, 0), (B_TREE, 2, 0, 0, 0), (B_RS_LAST, 0, 5),
    (B_TREE, 3, 0, 1, 0), (B_RS_LAST, 1, 7), (B_RS_RANK, 1, 4), (B_RS_RANK, 1, 3), (B_TREE, 1, 0, 0, 0),
    (B_RS_LAST, 1, 4), (B_TREE, 3, 0, 0, 0), (B_RS_LAST, 1, 3),
]


def backward_kernel(
    tokens_ref,
    cot_ref,
    gain_rows,
    qkv_rows,
    context,
    resid_mid,
    qkv_full,
    out_full,
    out_ref,
    back_ref,
    gate_up_ref,
    down_ref,
    output,
    grad_tokens,
    norm_attn_sum,
    norm_ff_sum,
    qkv_sum,
    attn_out_sum,
    gate_up_total,
    down_sum,
    act_own,
    core_buf,
    x_buf,
    z_buf,
    gate_own,
    down_own,
    across_gate,
    across_down,
    far_gate,
    far_down,
    qkv_grad,
    out_grad,
    slots_0,
    slots_1,
    slots_2,
    slots_3,
    qkv_tiles,
    out_tiles,
    turned,
    attn_turned,
    context_turned,
    d_qkv,
    d_mid_low,
    d_mid,
    d_context,
    d_rows,
    halves,
    probs_buf,
    spread,
    gain_acc,
    gains_part,
    gains_buf,
    gains_sum,
    gate_up_sum,
    core_send,
    core_recv,
    x_send,
    x_recv,
    z_send,
    z_recv,
    across_send,
    across_recv,
    far_send,
    far_recv,
    rank_send,
    rank_recv,
    swap_send,
    swap_recv,
    tree_send,
    tree_recv,
    gains_send,
    gains_recv,
    own_sem,
    part_sem,
    tile_sem,
):
    z, y, x, core = here()
    me = 2 * (z * 4 + y * 2 + x) + core
    zh, zl, member, rank, device, far, across = group_place(z, y, x, core)
    own_step = (0, 0, 0)
    act_height, positions, model = tokens_ref.shape
    sets = positions
    height = qkv_sum.shape[1]
    down_height = down_sum.shape[1]
    half = 16 * height
    sibling = member((0, 0, 1))
    scale = 1.0 / math.sqrt(HEAD_DIM)
    pairs = pairs_of(positions)
    greet_all(z, y, x, core)
    sends = []

    def start(copy):
        copy.start()
        sends.append(copy)

    def run_rows(dzh, dy, low):
        number = 16 * flip(zh, dzh) + 4 * flip(y, dy) + 8 * low
        return pl.ds(pl.multiple_of(number * height, 4 * height), 4 * height)

    def down_rows(dzh, dy):
        number = 2 * flip(zh, dzh) + flip(y, dy)
        return pl.ds(pl.multiple_of(number * down_height, down_height), down_height)

    def ff_from(s, dzh, dy, part):
        if part == 2:
            return down_ref.at[s, down_rows(dzh, dy)]
        return gate_up_ref.at[s, run_rows(dzh, dy, part)]

    def ff_across(s, turn, part):
        return across_down.at[turn, s] if part == 2 else across_gate.at[turn, s, part]

    def ff_own(s, turn, part):
        return down_own.at[turn, s] if part == 2 else gate_own.at[turn, s, part]

    def ff_far(s, part):
        return far_down.at[s] if part == 2 else far_gate.at[s, part]

    def part_copy(s, turn, part):
        return pltpu.make_async_copy(
            ff_from(s, 1 - turn, 0, part), ff_own(s, turn, part), part_sem.at[turn, s, part]
        )

    def rs_across(s, turn, part):
        start(
            push(
                ff_from(s, 1 - turn, 1, part),
                ff_across(s, turn, part),
                across_send.at[turn, s, part],
                across_recv.at[turn, s, part],
                across,
            )
        )

    def rs_first(s, part):
        block = ff_across(s, 0, part)
        part_copy(s, 0, part).wait()
        arrived(block, across_recv.at[0, s, part], across)
        add_into(block, [block, ff_own(s, 0, part)])
        start(push(block, ff_far(s, part), far_send.at[s, part], far_recv.at[s, part], far))

    def rs_second(s, part):
        block = ff_across(s, 1, part)
        part_copy(s, 1, part).wait()
        arrived(block, across_recv.at[1, s, part], across)
        arrived(ff_far(s, part), far_recv.at[s, part], far)
        target = down_sum.at[s] if part == 2 else block
        add_into(target, [block, ff_far(s, part), ff_own(s, 1, part)])

    def share(step, s):
        number = 2 * flip(x, step[1]) + flip(core, step[2])
        return across_gate.at[
            1, s, flip(zl, step[0]), pl.ds(pl.multiple_of(number * height, height), height)
        ]

    def place_units(step, s, source):
        unit = down_height
        number = 8 * flip(zl, step[0]) + 2 * flip(x, step[1]) + flip(core, step[2])
        for side in (0, 1):
            for group in range(4):
                zh_part, y_part = divmod(group, 2)
                left = (32 * side + 16 * zh_part + 4 * y_part + number) * unit
                gate_up_total[s, :, pl.ds(pl.multiple_of(left, unit), unit)] = source[
                    :, (4 * side + group) * unit : (4 * side + group + 1) * unit
                ].astype(F32)

    def rs_rank(s, slot):
        step = RANK_STEPS[slot]
        start(
            push(
                share(step, s),
                gate_up_sum.at[rank(own_step), s],
                rank_send.at[slot, s],
                rank_recv.at[slot, s],
                member(step),
            )
        )

    def rs_last(s, slot):
        step = RANK_STEPS[slot]
        block = gate_up_sum.at[rank(step), s]
        arrived(block, rank_recv.at[slot, s], member(step))
        place_units(step, s, block)

    acts = [back_ref, out_ref]

    def act_rows(step):
        return pl.ds(pl.multiple_of(rank(step) * act_height, act_height), act_height)

    def act_core(which, s):
        for dl, dx in ((1, 1), (0, 1), (1, 0), (0, 0)):
            start(
                push(
                    acts[which].at[s, act_rows((dl, dx, 1))],
                    core_buf.at[which, s, dl, dx],
                    core_send.at[which, s, dl, dx],
                    core_recv.at[which, s, dl, dx],
                    sibling,
                )
            )

    def act_copy(which, s, dl, dx):
        return pltpu.make_async_copy(
            acts[which].at[s, act_rows((dl, dx, 0))],
            act_own.at[s, dl, dx],
            own_sem.at[which, s, dl, dx],
        )

    def act_load(which):
        for s in range(sets):
            for dl in (0, 1):
                for dx in (0, 1):
                    act_copy(which, s, dl, dx).start()

    def act_ready(which, s, dl, dx):
        act_copy(which, s, dl, dx).wait()
        arrived(core_buf.at[which, s, dl, dx], core_recv.at[which, s, dl, dx], sibling)

    def act_add_x(which, s, dl):
        act_ready(which, s, dl, 1)
        block = core_buf.at[which, s, dl, 1]
        add_into(block, [block, act_own.at[s, dl, 1]])
        start(
            push(
                block,
                x_buf.at[which, s, dl],
                x_send.at[which, s, dl],
                x_recv.at[which, s, dl],
                member((0, 1, 0)),
            )
        )

    def act_add_z(which, s):
        act_ready(which, s, 1, 0)
        block = x_buf.at[which, s, 1]
        arrived(block, x_recv.at[which, s, 1], member((0, 1, 0)))
        add_into(block, [block, core_buf.at[which, s, 1, 0], act_own.at[s, 1, 0]])
        start(
            push(
                block, z_buf.at[which, s], z_send.at[which, s], z_recv.at[which, s], member((1, 0, 0))
            )
        )

    def act_sum(which, s):
        act_ready(which, s, 0, 0)
        arrived(x_buf.at[which, s, 0], x_recv.at[which, s, 0], member((0, 1, 0)))
        arrived(z_buf.at[which, s], z_recv.at[which, s], member((1, 0, 0)))

    def act_total(which, s, rows):
        return (
            act_own[s, 0, 0, rows, :].astype(F32)
            + core_buf[which, s, 0, 0, rows, :].astype(F32)
            + x_buf[which, s, 0, rows, :].astype(F32)
            + z_buf[which, s, rows, :].astype(F32)
        )

    pieces = [
        (qkv_grad, qkv_sum, 0, "zxy", slots_0),
        (qkv_grad, qkv_sum, 1, "zyx", slots_1),
        (out_grad, attn_out_sum, 0, "xyz", slots_2),
        (out_grad, attn_out_sum, 1, "yxz", slots_3),
    ]
    events = sorted(
        ((-hops(offset), place, piece, offset) for piece in range(4) for place, offset in enumerate(OFFSETS)),
        key=lambda event: event[:3],
    )

    def tree_block(piece, offset):
        source, _, index, _, _ = pieces[piece]
        chip = chip_of(offset, z, y, x)
        return source.at[index, pl.ds(pl.multiple_of(chip * height, height), height), :]

    def tree_copy(piece, offset):
        _, _, _, order, slots = pieces[piece]
        toward = came_from(order, offset)
        base, _ = slot_base(order)
        seen = {"x": "x", "y": "y", "u": "d", "d": "u"}[toward]
        nearer = offset
        if toward == "u":
            nearer = (offset[0] - 1, offset[1], offset[2])
        if toward == "d":
            nearer = (offset[0] + 1, offset[1], offset[2])
        there = {"u": z + 1, "d": z - 1}.get(toward, z)
        index_there, _ = slot_index(
            order, seen, nearer, there, y if toward != "y" else 1 - y, x if toward != "x" else 1 - x
        )
        if toward in "xy":
            index_there, _ = slot_index(order, seen, offset, z, y, x)
        place = base[seen] + index_there
        return push(
            tree_block(piece, offset),
            slots.at[place],
            tree_send.at[piece, chip_of(offset, z, y, x)],
            tree_recv.at[piece, place],
            neighbour(toward, z, y, x, core),
        )

    def tree_step(piece, offset):
        _, result, index, order, slots = pieces[piece]
        base, _ = slot_base(order)

        def go():
            block = tree_block(piece, offset)
            sure, unsure = [], []
            for direction in onward(order, offset):
                local, _ = slot_index(order, direction, offset, z, y, x)
                place = base[direction] + local
                (sure if direction in "xy" else unsure).append((direction, place))
            terms = [block]
            for _, place in sure:
                arrived(slots.at[place], tree_recv.at[piece, place], sibling)
                terms.append(slots.at[place])
            last = hops(offset) == 0
            target = result.at[index] if last else block
            if last or len(terms) > 1:
                add_into(target, terms)
            for direction, place in unsure:

                def more(place=place):
                    arrived(slots.at[place], tree_recv.at[piece, place], sibling)
                    add_into(target, [target, slots.at[place]])

                maybe(direction_exists(direction, z), more)
            if not last:
                tree_copy(piece, offset).start()

        maybe(offset_exists(offset, z), go)

    def gains_copy(step):
        other = lax.rem(me + step, 32)
        return push(
            gains_part.at[lax.div(other, 4)],
            gains_buf.at[me],
            gains_send.at[step],
            gains_recv.at[me],
            (lax.div(other, 2), lax.rem(other, 2)),
        )

    def gains_start(step, carry):
        gains_copy(step).start()
        return carry

    def gains_wait(step, carry):
        other = lax.rem(me + step, 32)
        gains_copy(step).wait_send()
        arrived(gains_buf.at[other], gains_recv.at[other], sibling)
        gains_sum[...] += gains_buf[other]
        return carry

    def turn(source, target, slot):
        def one(block, p):
            flat = source(p, block)
            turned[slot, p, pl.ds(2 * block, 2)] = flat.T.astype(BF16).reshape(2, 2, height, act_height)

        for p in range(positions):
            for block in range(model // 128):
                one(block, p)
            target[p, :, :, :act_height] = turned[slot, p, :, core]

    qkv_tile = qkv_tiles.shape[1]
    tile_count = model // qkv_tile

    def qkv_load(number):
        p, tile = divmod(number, tile_count)
        return pltpu.make_async_copy(
            qkv_full.at[p, pl.ds(tile * qkv_tile, qkv_tile)],
            qkv_tiles.at[number % 2],
            tile_sem.at[number % 2],
        )

    out_loads = [
        pltpu.make_async_copy(out_full.at[p], out_tiles.at[p], tile_sem.at[2 + p]) for p in range(positions)
    ]

    def context_block(p, block):
        return context[p, :, 128 * block : 128 * block + 128].astype(F32)

    def attn_block(p, block):
        return d_rows[p, :, 128 * block : 128 * block + 128]

    def norm_turn():
        def attn_norm(rows):
            values = tokens_ref[rows].astype(F32)
            for p in range(positions):
                r, _ = normed(values[:, p, :])
                d_rows[p, rows, :] = r * gain_rows[p : p + 1, :]

        row_loop(act_height, 16, attn_norm)
        turn(context_block, context_turned, 0)
        turn(attn_block, attn_turned, 1)

    def landing(kind, p):
        other = pl.ds(act_height, act_height)
        return (
            context_turned.at[p, :, :, other],
            attn_turned.at[p, :, :, other],
            d_mid_low.at[p, other],
            d_qkv.at[p, other],
        )[kind]

    def swap(kind, p, source):
        start(
            push(source, landing(kind, p), swap_send.at[4 * p + kind], swap_recv.at[4 * p + kind], sibling)
        )

    def swap_wait(kind, p):
        arrived(landing(kind, p), swap_recv.at[4 * p + kind], sibling)

    def swap_turned():
        for p in range(positions):
            swap(0, p, turned.at[0, p, :, 1 - core])
            swap(1, p, turned.at[1, p, :, 1 - core])

    def find_probs():
        for p in range(positions):
            probs = attention_probs(qkv_rows, halves, spread, model, p)
            for q in range(p + 1):
                probs_buf[pairs.index((p, q))] = probs[q]

    def mid(p):
        def mid_back(rows):
            d_ff_in = act_total(0, p, rows)
            r, inverse = normed(resid_mid[p, rows, :])
            gain_acc[positions + p] += r * d_ff_in
            total = cot_ref[p, rows, :] + norm_back(
                r, inverse, d_ff_in * gain_rows[positions + p : positions + p + 1, :]
            )
            d_mid[p, rows, :] = total
            d_mid_low[p, rows, :] = total.astype(BF16)

        row_loop(act_height, 16, mid_back)
        swap(2, p, d_mid_low.at[p, pl.ds(0, act_height)])
        out_loads[p].wait()

        def context_back(columns):
            d_context[p, :, columns] = dot_back(
                d_mid_low[p, :act_height, :], out_tiles[p, columns, :]
            ).astype(BF16)

        tile_loop(model, 256, context_back)

    def scores_back():
        def context_products(rows):
            for index, (p, q) in enumerate(pairs):
                product = d_context[p, rows, :].astype(F32) * qkv_rows[q, rows, 2 * model :].astype(F32)
                halves[2 * index, rows, :], halves[2 * index + 1, rows, :] = split_product(product)

        row_loop(act_height, 16, context_products)
        d_probs = [sums_over_heads(halves, spread, index) for index in range(len(pairs))]
        for p in range(positions):
            own = [index for index, pair in enumerate(pairs) if pair[0] == p]
            mean = functools.reduce(jnp.add, [probs_buf[index] * d_probs[index] for index in own])
            for index in own:
                d_score = (probs_buf[index] * (d_probs[index] - mean)).astype(BF16)
                halves[2 * index] = to_heads(d_score, spread)
                halves[2 * index + 1] = to_heads(probs_buf[index].astype(BF16), spread)

        def plus(total, term):
            return term if total is None else total + term

        def qkv_back(rows):
            d_keys = [None] * positions
            d_values = [None] * positions
            for p in range(positions):
                d_query = None
                d_own = d_context[p, rows, :].astype(F32)
                query = qkv_rows[p, rows, :model].astype(F32)
                for index, (own, q) in enumerate(pairs):
                    if own == p:
                        d_score = halves[2 * index, rows, :].astype(F32)
                        key = qkv_rows[q, rows, model : 2 * model].astype(F32)
                        d_query = plus(d_query, d_score * key)
                        d_keys[q] = plus(d_keys[q], d_score * query)
                        d_values[q] = plus(
                            d_values[q], halves[2 * index + 1, rows, :].astype(F32) * d_own
                        )
                d_qkv[p, rows, :model] = (d_query * scale).astype(BF16)
            for p in range(positions):
                d_qkv[p, rows, model : 2 * model] = (d_keys[p] * scale).astype(BF16)
                d_qkv[p, rows, 2 * model :] = d_values[p].astype(BF16)

        row_loop(act_height, 16, qkv_back)

    def swap_qkv():
        for p in range(positions):
            swap(3, p, d_qkv.at[p, pl.ds(0, act_height)])

    def out_weights(p):
        swap_wait(0, p)
        swap_wait(2, p)

        def tile(columns):
            out_grad[p, :, columns] = dot(
                context_turned[p].reshape(half, 2 * act_height), d_mid_low[p, :, columns]
            ).astype(BF16)

        tile_loop(model, 256, tile)

    def qkv_weights(p):
        swap_wait(1, p)
        swap_wait(3, p)

        def tile(columns):
            qkv_grad[p, :, columns] = dot(
                attn_turned[p].reshape(half, 2 * act_height), d_qkv[p, :, columns]
            ).astype(BF16)

        tile_loop(3 * model, 256, tile)

    def rows_back(p):
        for tile in range(tile_count):
            number = p * tile_count + tile
            qkv_load(number).wait()
            d_rows[p, :, tile * qkv_tile : (tile + 1) * qkv_tile] = dot_back(
                d_qkv[p, :act_height, :], qkv_tiles[number % 2]
            )
            if number + 2 < positions * tile_count:
                qkv_load(number + 2).start()

    def attn_back():
        def norm_one_back(rows):
            values = tokens_ref[rows].astype(F32)
            for p in range(positions):
                r, inverse = normed(values[:, p, :])
                d_attn_in = d_rows[p, rows, :]
                gain_acc[p] += r * d_attn_in
                grad_tokens[rows, p, :] = d_mid[p, rows, :] + norm_back(
                    r, inverse, d_attn_in * gain_rows[p : p + 1, :]
                )

        row_loop(act_height, 16, norm_one_back)
        gains_part[...] = jnp.zeros_like(gains_part)
        for index in range(2 * positions):
            sums = jnp.sum(gain_acc[index], axis=0, keepdims=True)
            for block in range(8):
                gains_part[block, index : index + 1, :] = sums[:, 128 * block : 128 * block + 128]
        lax.fori_loop(1, 32, gains_start, 0)

    def finish_output():
        def finish(rows):
            rounded = [resid_mid[p, rows, :] + act_total(1, p, rows) for p in range(positions)]
            output[rows] = jnp.stack(rounded, axis=1).astype(BF16)

        row_loop(act_height, 16, finish)

    for s in range(sets):
        for turn_number in (0, 1):
            for part in (0, 1, 2):
                part_copy(s, turn_number, part).start()
    for copy in out_loads:
        copy.start()
    act_load(0)
    qkv_load(0).start()
    qkv_load(1).start()
    make_spread(spread)
    gain_acc[...] = jnp.zeros_like(gain_acc)
    kinds = {
        B_TREE: lambda piece, dz, dy, dx: tree_step(piece, (dz, dy, dx)),
        B_RS_ACROSS: rs_across,
        B_RS_FIRST: rs_first,
        B_RS_SECOND: rs_second,
        B_RS_RANK: rs_rank,
        B_RS_LAST: rs_last,
        B_ACT_CORE: act_core,
        B_ACT_LOAD: act_load,
        B_ACT_ADD_X: act_add_x,
        B_ACT_ADD_Z: act_add_z,
        B_ACT_SUM: act_sum,
        B_NORM_TURN: norm_turn,
        B_SWAP_TURNED: swap_turned,
        B_PROBS: find_probs,
        B_MID: mid,
        B_SCORES_BACK: scores_back,
        B_SWAP_QKV: swap_qkv,
        B_OUT_W: out_weights,
        B_QKV_W: qkv_weights,
        B_ROWS_BACK: rows_back,
        B_ATTN_BACK: attn_back,
        B_FINISH_OUTPUT: finish_output,
    }
    for kind, *numbers in BACKWARD_STEPS:
        kinds[kind](*numbers)
    for s in range(sets):
        place_units(own_step, s, share(own_step, s))
    gains_sum[...] = gains_part[lax.div(me, 4)]
    lax.fori_loop(1, 32, gains_wait, 0)
    own_gain = norm_attn_sum.shape[1]
    for index, target in enumerate((norm_attn_sum, norm_ff_sum)):
        picked = jnp.zeros(target.shape, F32)
        for place in range(128 // own_gain):
            picked = picked + jnp.where(
                lax.rem(me, 128 // own_gain) == place,
                gains_sum[
                    index * positions : (index + 1) * positions, place * own_gain : (place + 1) * own_gain
                ],
                0.0,
            )
        target[...] = picked
    for _, _, piece, offset in events:
        if hops(offset) > 0:
            maybe(offset_exists(offset, z), tree_copy(piece, offset).wait_send)
    for copy in sends:
        copy.wait_send()


def backward_scatter(
    tokens,
    grads,
    gain_rows,
    qkv_rows,
    context,
    resid_mid,
    qkv_full,
    out_full,
    out_part,
    back_part,
    gate_up_grad,
    down_grad,
):
    act_height, sets, model = tokens.shape
    width = gate_up_grad.shape[2]
    height = model // 32
    down_height = down_grad.shape[1] // 4
    dma = pltpu.SemaphoreType.DMA
    vmem = pl.BlockSpec(memory_space=pltpu.VMEM)
    anywhere = pl.BlockSpec(memory_space=pl.ANY)
    places = [slot_base(order)[1] for order in ORDERS]
    pair_count = len(pairs_of(sets))
    act = (sets, act_height, model)
    return pl.pallas_call(
        backward_kernel,
        out_shape=(
            jax.ShapeDtypeStruct(tokens.shape, BF16),
            jax.ShapeDtypeStruct(tokens.shape, F32),
            jax.ShapeDtypeStruct((sets, height), F32),
            jax.ShapeDtypeStruct((sets, height), F32),
            jax.ShapeDtypeStruct((sets, height, 3 * model), F32),
            jax.ShapeDtypeStruct((sets, height, model), F32),
            jax.ShapeDtypeStruct((sets, height, 8 * width), F32),
            jax.ShapeDtypeStruct((sets, down_height, model), F32),
        ),
        in_specs=[vmem] * 6 + [anywhere] * 6,
        out_specs=(vmem,) * 8,
        scratch_shapes=[
            pltpu.VMEM((sets, 2, 2, act_height, model), BF16),
            pltpu.VMEM((2, sets, 2, 2, act_height, model), BF16),
            pltpu.VMEM((2, sets, 2, act_height, model), BF16),
            pltpu.VMEM((2, sets, act_height, model), BF16),
            pltpu.VMEM((2, sets, 2, 4 * height, width), BF16),
            pltpu.VMEM((2, sets, down_height, model), BF16),
            pltpu.VMEM((2, sets, 2, 4 * height, width), BF16),
            pltpu.VMEM((2, sets, down_height, model), BF16),
            pltpu.VMEM((sets, 2, 4 * height, width), BF16),
            pltpu.VMEM((sets, down_height, model), BF16),
            pltpu.VMEM((sets, 16 * height, 3 * model), BF16),
            pltpu.VMEM((sets, 16 * height, model), BF16),
            pltpu.VMEM((places[0], height, 3 * model), BF16),
            pltpu.VMEM((places[1], height, 3 * model), BF16),
            pltpu.VMEM((places[2], height, model), BF16),
            pltpu.VMEM((places[3], height, model), BF16),
            pltpu.VMEM((2, 128, 3 * model), BF16),
            pltpu.VMEM((sets, model, model), BF16),
            pltpu.VMEM((2, sets, 16, 2, height, act_height), BF16),
            pltpu.VMEM((sets, 16, height, 2 * act_height), BF16),
            pltpu.VMEM((sets, 16, height, 2 * act_height), BF16),
            pltpu.VMEM((sets, 2 * act_height, 3 * model), BF16),
            pltpu.VMEM((sets, 2 * act_height, model), BF16),
            pltpu.VMEM(act, F32),
            pltpu.VMEM(act, BF16),
            pltpu.VMEM(act, F32),
            pltpu.VMEM((2 * pair_count, act_height, model), BF16),
            pltpu.VMEM((pair_count, act_height, 128), F32),
            pltpu.VMEM((model, 128), BF16),
            pltpu.VMEM((2 * sets, 16, model), F32),
            pltpu.VMEM((8, 8, 128), F32),
            pltpu.VMEM((32, 8, 128), F32),
            pltpu.VMEM((8, 128), F32),
            pltpu.VMEM((8, sets, height, width), BF16),
            dma((2, sets, 2, 2)),
            dma((2, sets, 2, 2)),
            dma((2, sets, 2)),
            dma((2, sets, 2)),
            dma((2, sets)),
            dma((2, sets)),
            dma((2, sets, 3)),
            dma((2, sets, 3)),
            dma((sets, 3)),
            dma((sets, 3)),
            dma((8, sets)),
            dma((8, sets)),
            dma((4 * sets,)),
            dma((4 * sets,)),
            dma((4, 16)),
            dma((4, max(places))),
            dma((32,)),
            dma((32,)),
            dma((2, sets, 2, 2)),
            dma((2, sets, 3)),
            dma((2 + sets,)),
        ],
        compiler_params=pltpu.CompilerParams(
            collective_id=5, has_side_effects=True, vmem_limit_bytes=63 * 2**20
        ),
        name="backward_scatter",
    )(
        tokens,
        grads,
        gain_rows,
        qkv_rows,
        context,
        resid_mid,
        qkv_full,
        out_full,
        out_part,
        back_part,
        gate_up_grad,
        down_grad,
    )


def settle_kernel(*refs):
    count = len(refs) // 2
    sems = refs[-1]
    copies = [
        pltpu.make_async_copy(refs[index], refs[count + index], sems.at[index]) for index in range(count)
    ]
    for copy in copies:
        copy.start()
    for copy in copies:
        copy.wait()


def settle(arrays):
    anywhere = pl.BlockSpec(memory_space=pl.ANY)
    return pl.pallas_call(
        settle_kernel,
        out_shape=tuple(jax.ShapeDtypeStruct(array.shape, array.dtype) for array in arrays),
        in_specs=[anywhere] * len(arrays),
        out_specs=(anywhere,) * len(arrays),
        scratch_shapes=[pltpu.SemaphoreType.DMA((len(arrays),))],
        name="settle",
    )(*arrays)


def local_fast(
    tokens,
    norm_attn,
    w_qkv,
    w_out,
    norm_ff,
    w_gate_up,
    w_down,
    cotangent,
    valid_frames,
    item_lengths,
):
    (
        gain_rows,
        cot_rows,
        qkv_rows,
        context,
        resid_mid,
        qkv_full,
        out_full,
        out_part,
        back_part,
        gate_up_grad,
        down_grad,
    ) = forward_gather(
        valid_frames,
        item_lengths,
        norm_attn,
        norm_ff,
        tokens,
        cotangent,
        w_qkv,
        w_out,
        w_gate_up,
        w_down,
    )
    (
        output,
        grad_tokens,
        share_norm_attn,
        share_norm_ff,
        share_qkv,
        share_out,
        share_gate_up,
        share_down,
    ) = settle(backward_scatter(
        tokens,
        cot_rows,
        gain_rows,
        qkv_rows,
        context,
        resid_mid,
        qkv_full,
        out_full,
        out_part,
        back_part,
        gate_up_grad,
        down_grad,
    ))
    return (
        output,
        grad_tokens,
        share_norm_attn,
        share_qkv,
        share_out,
        share_norm_ff,
        share_gate_up,
        share_down,
    )


def solution(mesh):
    in_specs = (
        P(("dp", "pair"), None, None),
        P(None, ("dp", "pair")),
        P(None, ("dp", "pair"), None),
        P(None, ("dp", "pair"), None),
        P(None, ("dp", "pair")),
        P(None, ("dp", "pair"), None),
        P(None, ("dp", "pair"), None),
        P(("dp", "pair"), None, None),
        P(("dp", "pair")),
        P(),
    )
    out_specs = (
        P(("dp", "pair"), None, None),
        P(("dp", "pair"), None, None),
        P(None, ("dp", "pair")),
        P(None, ("dp", "pair"), None),
        P(None, ("dp", "pair"), None),
        P(None, ("dp", "pair")),
        P(None, ("dp", "pair"), None),
        P(None, ("dp", "pair"), None),
    )
    body = local_fast if mesh.shape["dp"] == 16 and mesh.shape["pair"] == 2 else local
    return jax.shard_map(body, mesh=mesh, in_specs=in_specs, out_specs=out_specs, check_vma=False)
```

```python
import functools
import math

import jax
import jax.numpy as jnp
from jax import lax
from jax.experimental import pallas as pl
from jax.experimental.pallas import tpu as pltpu
from jax.sharding import PartitionSpec as P

HEAD_DIM = 64


def per_pos(activations, weight):
    return jnp.einsum("fgk,gke->fge", activations, weight, preferred_element_type=jnp.float32)


def per_pos_back(gradients, weight):
    return jnp.einsum("fge,gke->fgk", gradients, weight, preferred_element_type=jnp.float32)


def pos_grad(activations, gradients):
    return jnp.einsum("fgk,fge->kge", activations, gradients, preferred_element_type=jnp.float32)


def gain_grad(normed_rows, gradients):
    return jnp.transpose(jnp.sum(normed_rows * gradients, axis=0))


def back_layout(share):
    return jnp.swapaxes(share, 0, 1)


def normed(values):
    inverse = lax.rsqrt(jnp.mean(values * values, axis=-1, keepdims=True) + 1e-05)
    return (values * inverse, inverse)


def norm_back(normed_rows, inverse, gradients):
    return inverse * (
        gradients - normed_rows * jnp.mean(gradients * normed_rows, axis=-1, keepdims=True)
    )


def gather_ff_fwd(norm_ff, w_gate_up, w_down, start, group):
    return (
        lax.all_gather(norm_ff[start : start + group], ("dp", "pair"), axis=1, tiled=True),
        lax.all_gather(w_gate_up[start : start + group], ("dp", "pair"), axis=1, tiled=True),
        lax.all_gather(w_down[start : start + group], ("dp", "pair"), axis=1, tiled=True),
    )


def gather_ff_back(norm_ff, w_gate_up, w_down, start, group):
    return (
        lax.all_gather(norm_ff[start : start + group], ("dp", "pair"), axis=1, tiled=True),
        lax.all_gather(w_gate_up[start : start + group], ("dp", "pair"), axis=1, tiled=True),
        lax.all_gather(w_down[start : start + group], ("dp", "pair"), axis=1, tiled=True),
    )


def local(
    tokens,
    norm_attn,
    w_qkv,
    w_out,
    norm_ff,
    w_gate_up,
    w_down,
    cotangent,
    valid_frames,
    item_lengths,
):
    frame_count, positions, model_width = tokens.shape
    head_count = model_width // HEAD_DIM
    ff_units = w_gate_up.shape[2] // 2
    score_scale = 1.0 / math.sqrt(HEAD_DIM)
    causal = jnp.arange(positions)[:, None] >= jnp.arange(positions)[None, :]
    head_shape = (frame_count, positions, head_count, HEAD_DIM)
    group = 1
    gains_attn, qkv_full, out_full = (
        lax.all_gather(norm_attn, ("dp", "pair"), axis=1, tiled=True),
        lax.all_gather(w_qkv, ("dp", "pair"), axis=1, tiled=True),
        lax.all_gather(w_out, ("dp", "pair"), axis=1, tiled=True),
    )
    resid_in = tokens.astype(jnp.float32)
    normed_one, inverse_one = normed(resid_in)
    attn_in = (normed_one * gains_attn.astype(jnp.float32)[None]).astype(jnp.bfloat16)
    qkv_rows = per_pos(attn_in, qkv_full).astype(jnp.bfloat16)
    queries = qkv_rows[..., :model_width].reshape(head_shape)
    key_heads = qkv_rows[..., model_width : 2 * model_width].reshape(head_shape)
    value_heads = qkv_rows[..., 2 * model_width :].reshape(head_shape)
    scores = (
        jnp.einsum("fphd,fqhd->fhpq", queries, key_heads, preferred_element_type=jnp.float32)
        * score_scale
    )
    scores = jnp.where(causal, scores, -1e30)
    row_max = jnp.max(scores, axis=-1, keepdims=True)
    attn_probs = jnp.exp(scores - row_max)
    attn_probs = attn_probs / jnp.sum(attn_probs, axis=-1, keepdims=True)
    probs_low = attn_probs.astype(jnp.bfloat16)
    context = jnp.einsum(
        "fhpq,fqhd->fphd", probs_low, value_heads, preferred_element_type=jnp.float32
    )
    context = context.astype(jnp.bfloat16).reshape(frame_count, positions, model_width)
    resid_mid = resid_in + per_pos(context, out_full)
    kept_parts = []
    out_parts = []
    for start in range(0, positions, group):
        gains_ff, gate_up_full, down_full = gather_ff_fwd(norm_ff, w_gate_up, w_down, start, group)
        mid_part = resid_mid[:, start : start + group]
        normed_two, inverse_two = normed(mid_part)
        ff_in = (normed_two * gains_ff.astype(jnp.float32)[None]).astype(jnp.bfloat16)
        gate_up = per_pos(ff_in, gate_up_full)
        gate_part = gate_up[..., :ff_units]
        up_part = gate_up[..., ff_units:]
        sigmoid_gate = jax.nn.sigmoid(gate_part)
        silu_gate = gate_part * sigmoid_gate
        hidden = (silu_gate * up_part).astype(jnp.bfloat16)
        out_parts.append(mid_part + per_pos(hidden, down_full))
        kept_parts.append(
            (normed_two, inverse_two, ff_in, gate_part, up_part, sigmoid_gate, silu_gate, hidden)
        )
    output = jnp.concatenate(out_parts, axis=1).astype(jnp.bfloat16)
    device_index = lax.axis_index(("dp", "pair"))
    local_ids = jnp.arange(frame_count, dtype=jnp.int32)
    frame_ids = device_index * frame_count + local_ids
    item_ends = jnp.cumsum(item_lengths)
    item_starts = item_ends - item_lengths
    in_item = (frame_ids[:, None] >= item_starts[None, :]) & (
        frame_ids[:, None] < item_ends[None, :]
    )
    item_share = 8 * frame_count / item_lengths.astype(jnp.float32)
    frame_weight = jnp.sum(jnp.where(in_item, item_share[None, :], 0.0), axis=1)
    frame_weight = jnp.where(local_ids < valid_frames[0], frame_weight, 0.0)
    grad_out = cotangent.astype(jnp.float32) * frame_weight[:, None, None]
    mid_grads = []
    share_norm_ff_parts = []
    share_gate_up_parts = []
    share_down_parts = []
    for index, start in enumerate(range(0, positions, group)):
        normed_two, inverse_two, ff_in, gate_part, up_part, sigmoid_gate, silu_gate, hidden = (
            kept_parts[index]
        )
        gains_ff, gate_up_full, down_full = gather_ff_back(norm_ff, w_gate_up, w_down, start, group)
        grad_part = grad_out[:, start : start + group]
        grad_low = grad_part.astype(jnp.bfloat16)
        grad_down = pos_grad(hidden, grad_low)
        d_hidden = per_pos_back(grad_low, down_full)
        d_gate = d_hidden * up_part * sigmoid_gate * (1.0 + gate_part * (1.0 - sigmoid_gate))
        d_up = d_hidden * silu_gate
        d_gate_up = jnp.concatenate([d_gate, d_up], axis=-1).astype(jnp.bfloat16)
        grad_gate_up = pos_grad(ff_in, d_gate_up)
        d_ff_in = per_pos_back(d_gate_up, gate_up_full)
        grad_norm_ff = gain_grad(normed_two, d_ff_in)
        mid_grads.append(
            grad_part
            + norm_back(normed_two, inverse_two, d_ff_in * gains_ff.astype(jnp.float32)[None])
        )
        share_a, share_b, share_c = (
            lax.psum_scatter(grad_norm_ff, ("dp", "pair"), scatter_dimension=0, tiled=True),
            lax.psum_scatter(grad_gate_up, ("dp", "pair"), scatter_dimension=0, tiled=True),
            lax.psum_scatter(grad_down, ("dp", "pair"), scatter_dimension=0, tiled=True),
        )
        share_norm_ff_parts.append(jnp.transpose(share_a))
        share_gate_up_parts.append(back_layout(share_b))
        share_down_parts.append(back_layout(share_c))
    d_mid = jnp.concatenate(mid_grads, axis=1)
    gains_attn, qkv_full, out_full = (
        lax.all_gather(norm_attn, ("dp", "pair"), axis=1, tiled=True),
        lax.all_gather(w_qkv, ("dp", "pair"), axis=1, tiled=True),
        lax.all_gather(w_out, ("dp", "pair"), axis=1, tiled=True),
    )
    d_mid_low = d_mid.astype(jnp.bfloat16)
    grad_out_proj = pos_grad(context, d_mid_low)
    d_context = per_pos_back(d_mid_low, out_full).astype(jnp.bfloat16).reshape(head_shape)
    d_probs = jnp.einsum(
        "fphd,fqhd->fhpq", d_context, value_heads, preferred_element_type=jnp.float32
    )
    d_values = jnp.einsum(
        "fhpq,fphd->fqhd", probs_low, d_context, preferred_element_type=jnp.float32
    )
    d_scores = attn_probs * (d_probs - jnp.sum(attn_probs * d_probs, axis=-1, keepdims=True))
    d_scores = d_scores.astype(jnp.bfloat16)
    d_queries = (
        jnp.einsum("fhpq,fqhd->fphd", d_scores, key_heads, preferred_element_type=jnp.float32)
        * score_scale
    )
    d_keys = (
        jnp.einsum("fhpq,fphd->fqhd", d_scores, queries, preferred_element_type=jnp.float32)
        * score_scale
    )
    row_shape = (frame_count, positions, model_width)
    d_qkv = jnp.concatenate(
        [d_queries.reshape(row_shape), d_keys.reshape(row_shape), d_values.reshape(row_shape)],
        axis=-1,
    ).astype(jnp.bfloat16)
    grad_qkv = pos_grad(attn_in, d_qkv)
    d_attn_in = per_pos_back(d_qkv, qkv_full)
    grad_norm_attn = gain_grad(normed_one, d_attn_in)
    grad_tokens = d_mid + norm_back(
        normed_one, inverse_one, d_attn_in * gains_attn.astype(jnp.float32)[None]
    )
    share_norm_attn, share_qkv, share_out = (
        lax.psum_scatter(grad_norm_attn, ("dp", "pair"), scatter_dimension=0, tiled=True),
        lax.psum_scatter(grad_qkv, ("dp", "pair"), scatter_dimension=0, tiled=True),
        lax.psum_scatter(grad_out_proj, ("dp", "pair"), scatter_dimension=0, tiled=True),
    )
    share_norm_attn = jnp.transpose(share_norm_attn)
    share_qkv = back_layout(share_qkv)
    share_out = back_layout(share_out)
    share_norm_ff = jnp.concatenate(share_norm_ff_parts, axis=0)
    share_gate_up = jnp.concatenate(share_gate_up_parts, axis=0)
    share_down = jnp.concatenate(share_down_parts, axis=0)
    return (
        output,
        grad_tokens,
        share_norm_attn,
        share_qkv,
        share_out,
        share_norm_ff,
        share_gate_up,
        share_down,
    )


MESH_ID = pl.DeviceIdType.MESH
BF16 = jnp.bfloat16
F32 = jnp.float32


def here():
    dp = lax.axis_index("dp")
    core = lax.axis_index("pair")
    return lax.div(dp, 4), lax.rem(lax.div(dp, 2), 2), lax.rem(dp, 2), core


def flip(value, bit):
    return 1 - value if bit else value


def push(src, dst, send_sem, recv_sem, to):
    return pltpu.make_async_remote_copy(
        src_ref=src,
        dst_ref=dst,
        send_sem=send_sem,
        recv_sem=recv_sem,
        device_id=to,
        device_id_type=MESH_ID,
    )


def arrived(dst, recv_sem, to):
    push(dst, dst, recv_sem, recv_sem, to).wait_recv()


def greet_all(z, y, x, core):
    barrier = pltpu.get_barrier_semaphore()
    me = 2 * (z * 4 + y * 2 + x) + core

    def one(step, carry):
        other = lax.rem(me + step, 32)
        pl.semaphore_signal(
            barrier, inc=1, device_id=(lax.div(other, 2), lax.rem(other, 2)), device_id_type=MESH_ID
        )
        return carry

    lax.fori_loop(1, 32, one, 0)
    pl.semaphore_wait(barrier, 31)


def greet(peers):
    barrier = pltpu.get_barrier_semaphore()
    for to in peers:
        pl.semaphore_signal(barrier, inc=1, device_id=to, device_id_type=MESH_ID)
    pl.semaphore_wait(barrier, len(peers))


def maybe(condition, do):
    if condition is None:
        do()
    else:
        pl.when(condition)(do)


OFFSETS = [
    (dz, dy, dx) for dz in (0, -1, 1, -2, 2, -3, 3) for dy in (0, 1) for dx in (0, 1)
]
ORDERS = ("zxy", "zyx", "xyz", "yxz")


def hops(offset):
    return abs(offset[0]) + offset[1] + offset[2]


def arrival_axis(order, offset):
    part = dict(z=offset[0], y=offset[1], x=offset[2])
    last = None
    for axis in order:
        if part[axis] != 0:
            last = axis
    return last


def onward(order, offset):
    directions = []
    last = arrival_axis(order, offset)
    start = 0
    if last is not None:
        start = order.index(last) + 1
        if last == "z":
            directions.append("u" if offset[0] < 0 else "d")
    for axis in order[start:]:
        directions.extend(["u", "d"] if axis == "z" else [axis])
    return directions


def came_from(order, offset):
    last = arrival_axis(order, offset)
    if last == "z":
        return "d" if offset[0] < 0 else "u"
    return last


def offset_exists(offset, z):
    if offset[0] < 0:
        return z >= -offset[0]
    if offset[0] > 0:
        return z <= 3 - offset[0]
    return None


def direction_exists(direction, z):
    return {"u": z < 3, "d": z > 0}.get(direction)


DIRECTIONS = ("x", "y", "u", "d", "s")


def neighbour(direction, z, y, x, core):
    if direction == "x":
        return (z * 4 + y * 2 + 1 - x, core)
    if direction == "y":
        return (z * 4 + (1 - y) * 2 + x, core)
    if direction == "u":
        return (z * 4 + 4 + y * 2 + x, core)
    if direction == "d":
        return (z * 4 - 4 + y * 2 + x, core)
    return (z * 4 + y * 2 + x, 1 - core)


def chip_of(offset, z, y, x):
    return (z + offset[0]) * 4 + flip(y, offset[1]) * 2 + flip(x, offset[2])


RANK_STEPS = sorted(
    ((dl, dx, dc) for dl in (0, 1) for dx in (0, 1) for dc in (0, 1)), key=lambda step: (sum(step), step)
)


def group_place(z, y, x, core):
    zh, zl = lax.div(z, 2), lax.rem(z, 2)

    def member(step):
        return ((2 * zh + flip(zl, step[0])) * 4 + y * 2 + flip(x, step[1]), flip(core, step[2]))

    def rank(step):
        return 4 * flip(zl, step[0]) + 2 * flip(x, step[1]) + flip(core, step[2])

    def device(step, dzh=0, dy=0):
        return 16 * flip(zh, dzh) + 4 * flip(y, dy) + 8 * flip(zl, step[0]) + 2 * flip(x, step[1]) + flip(core, step[2])

    far = ((2 * (1 - zh) + zl) * 4 + y * 2 + x, core)
    across = (z * 4 + (1 - y) * 2 + x, core)
    return zh, zl, member, rank, device, far, across


def add_into(target, sources, rows=16, columns=1024):
    height, width = target.shape
    across = width // columns

    def one(step, carry):
        top = pl.multiple_of(lax.div(step, across) * rows, rows)
        left = pl.multiple_of(lax.rem(step, across) * columns, columns)
        spot = (pl.ds(top, rows), pl.ds(left, columns))
        total = sources[0][spot].astype(F32)
        for source in sources[1:]:
            total = total + source[spot].astype(F32)
        target[spot] = total.astype(target.dtype)
        return carry

    lax.fori_loop(0, (height // rows) * across, one, 0)


def row_loop(height, chunk, body):
    def one(step, carry):
        body(pl.ds(pl.multiple_of(step * chunk, chunk), chunk))
        return carry

    lax.fori_loop(0, height // chunk, one, 0)


def tile_loop(width, tile, body):
    def one(step, carry):
        body(pl.ds(pl.multiple_of(step * tile, tile), tile))
        return carry

    lax.fori_loop(0, width // tile, one, 0)


def dot(left, right):
    return jnp.dot(left, right, preferred_element_type=F32)


def dot_back(left, right):
    return lax.dot_general(left, right, (((1,), (1,)), ((), ())), preferred_element_type=F32)


def dot_grad(left, right):
    return lax.dot_general(left, right, (((0,), (0,)), ((), ())), preferred_element_type=F32)


def make_spread(spread):
    height, width = spread.shape
    head = lax.broadcasted_iota(jnp.int32, (height, width), 0) // HEAD_DIM
    spread[...] = jnp.where(
        head == lax.broadcasted_iota(jnp.int32, (height, width), 1), 1.0, 0.0
    ).astype(BF16)


def pairs_of(positions):
    return [(p, q) for p in range(positions) for q in range(p + 1)]


def split_product(product):
    high = product.astype(BF16)
    return high, (product - high.astype(F32)).astype(BF16)


def sums_over_heads(halves, spread, index):
    return dot(halves[2 * index], spread[...]) + dot(halves[2 * index + 1], spread[...])


def to_heads(values, spread):
    return dot_back(values, spread[...]).astype(BF16)


def attention_probs(qkv, halves, spread, model, position):
    height = qkv.shape[1]
    scale = 1.0 / math.sqrt(HEAD_DIM)

    def products(rows):
        for q in range(position + 1):
            product = qkv[position, rows, :model].astype(F32) * qkv[
                q, rows, model : 2 * model
            ].astype(F32)
            halves[2 * q, rows, :], halves[2 * q + 1, rows, :] = split_product(product)

    row_loop(height, 16, products)
    scores = [sums_over_heads(halves, spread, q) * scale for q in range(position + 1)]
    top = functools.reduce(jnp.maximum, scores)
    powers = [jnp.exp(score - top) for score in scores]
    total = functools.reduce(jnp.add, powers)
    return [power / total for power in powers]


(
    F_TREE,
    F_TREE_END,
    F_GAINS,
    F_PARTS,
    F_COT,
    F_ATTENTION,
    F_GRADS,
    F_ACT_Z,
    F_ACT_X,
    F_ACT_C,
    F_TO_RANK,
    F_OWN_FAR,
    F_OWN_ACROSS,
    F_RANK_FAR,
    F_RANK_ACROSS,
    F_FAR_ACROSS,
    F_FF_END,
    F_BLOCK,
    F_GATE_GRAD,
    F_DOWN_GRAD,
) = range(20)
FORWARD_STEPS = [
    (F_TREE, 3, 0, 0, 0), (F_TREE, 5, 0, 0, 0), (F_TREE, 0, 0, 0, 0), (F_TREE, 2, 0, 0, 0),
    (F_TREE, 5, 1, 0, 0), (F_PARTS,), (F_TO_RANK, 0, 7), (F_TREE, 0, -1, 0, 0), (F_TREE, 0, 0, 0, 1),
    (F_TO_RANK, 0, 3), (F_TREE, 2, 0, 0, 1), (F_TREE, 1, 0, 0, 0), (F_TREE, 0, -2, 0, 0), (F_COT,),
    (F_RANK_FAR, 0, 3), (F_TREE, 0, 0, 1, 0), (F_TREE, 4, 0, 0, 0), (F_TO_RANK, 1, 4), (F_TREE, 1, -1, 0, 0),
    (F_TO_RANK, 0, 2), (F_TO_RANK, 1, 2), (F_TREE, 2, 0, 1, 1), (F_TREE, 0, 1, 0, 0), (F_TREE, 2, 0, 1, 0),
    (F_OWN_ACROSS, 0, 0), (F_TREE, 1, 1, 0, 0), (F_TREE, 2, -1, 0, 0), (F_TREE, 0, -1, 0, 1),
    (F_TREE, 0, -3, 0, 0), (F_TO_RANK, 0, 1), (F_TREE, 0, -2, 0, 1), (F_TREE, 1, 0, 1, 0), (F_TREE, 2, 1, 0, 1),
    (F_TREE, 0, 2, 0, 0), (F_GRADS, 0), (F_TO_RANK, 0, 6), (F_RANK_FAR, 0, 1), (F_OWN_ACROSS, 1, 8),
    (F_TREE, 2, -2, 0, 0), (F_OWN_ACROSS, 0, 8), (F_TREE, 2, -1, 1, 0), (F_TO_RANK, 0, 5), (F_RANK_FAR, 0, 2),
    (F_TREE, 3, 0, 0, 1), (F_OWN_FAR, 0, 8), (F_TREE, 1, -1, 1, 0), (F_TREE, 2, -1, 1, 1), (F_FAR_ACROSS, 0, 2),
    (F_RANK_FAR, 0, 6), (F_TREE, 3, 0, 1, 1), (F_GAINS,), (F_TREE, 2, 1, 0, 0), (F_TREE, 1, 2, 0, 0),
    (F_RANK_ACROSS, 0, 3), (F_TREE, 1, -2, 0, 0), (F_TREE, 0, 3, 0, 0), (F_TREE, 2, 1, 1, 1),
    (F_TREE, 5, 0, 0, 1), (F_TREE, 2, 2, 0, 0), (F_TO_RANK, 0, 4), (F_TREE, 1, 2, 1, 0), (F_TREE, 3, -1, 0, 0),
    (F_TREE, 4, 1, 0, 0), (F_TREE, 0, -1, 1, 1), (F_TREE, 0, 2, 0, 1), (F_RANK_FAR, 0, 7), (F_RANK_FAR, 0, 4),
    (F_FAR_ACROSS, 0, 3), (F_TREE, 2, 2, 1, 1), (F_TREE, 1, 3, 0, 0), (F_TREE, 1, 1, 1, 0),
    (F_RANK_ACROSS, 0, 1), (F_TO_RANK, 1, 6), (F_TREE, 2, -3, 0, 0), (F_TREE, 0, -3, 0, 1),
    (F_TREE, 0, 0, 1, 1), (F_TREE, 1, 2, 0, 1), (F_TREE, 2, 1, 1, 0), (F_TREE, 2, -1, 0, 1),
    (F_TREE, 1, 0, 1, 1), (F_TREE, 2, -2, 1, 0), (F_TREE, 2, 3, 1, 1), (F_FAR_ACROSS, 0, 6), (F_OWN_FAR, 0, 0),
    (F_TREE, 1, -2, 0, 1), (F_TREE, 0, 2, 1, 1), (F_TREE, 4, 2, 0, 0), (F_TREE, 1, 3, 0, 1),
    (F_TREE, 3, 1, 0, 0), (F_TREE, 2, -2, 1, 1), (F_RANK_FAR, 0, 5), (F_TREE, 0, -2, 1, 1),
    (F_TREE, 0, 1, 1, 0), (F_TREE, 5, 0, 1, 0), (F_FAR_ACROSS, 0, 1), (F_TREE, 1, -2, 1, 0),
    (F_TREE, 1, 2, 1, 1), (F_TREE, 2, 2, 1, 0), (F_TREE, 1, -3, 0, 0), (F_TO_RANK, 1, 5), (F_TREE, 0, -1, 1, 0),
    (F_TREE, 3, -2, 0, 0), (F_TREE, 1, 3, 1, 0), (F_ACT_Z, 1, 0), (F_TREE, 0, 1, 0, 1), (F_TREE, 3, 1, 0, 1),
    (F_TREE, 2, 2, 0, 1), (F_TREE, 0, 3, 1, 0), (F_TREE, 4, -1, 0, 0), (F_TREE, 2, -2, 0, 1),
    (F_TREE, 2, -3, 1, 1), (F_TREE, 0, -3, 1, 1), (F_FAR_ACROSS, 0, 7), (F_TREE, 0, -3, 1, 0),
    (F_TREE, 0, 2, 1, 0), (F_TREE, 3, 1, 1, 0), (F_TREE, 2, -3, 1, 0), (F_TREE, 1, -1, 0, 1),
    (F_TREE, 1, -3, 1, 0), (F_RANK_ACROSS, 0, 7), (F_FAR_ACROSS, 0, 0), (F_TREE, 1, 3, 1, 1),
    (F_TREE, 3, 2, 0, 0), (F_TREE, 2, 3, 0, 0), (F_RANK_ACROSS, 0, 6), (F_TREE, 5, 1, 1, 0),
    (F_TREE, 0, 3, 0, 1), (F_TREE, 1, -3, 0, 1), (F_TREE, 3, -2, 0, 1), (F_ACT_C, 1, 0, 0, 0),
    (F_TREE, 4, 0, 1, 0), (F_TREE, 5, 0, 1, 1), (F_TREE, 4, -2, 0, 0), (F_FAR_ACROSS, 0, 4), (F_GRADS, 1),
    (F_TREE, 2, -3, 0, 1), (F_TREE, 5, -1, 1, 0), (F_TREE, 1, -3, 1, 1), (F_ACT_C, 1, 0, 1, 0),
    (F_FAR_ACROSS, 0, 8), (F_TREE, 5, 1, 0, 1), (F_FAR_ACROSS, 0, 5), (F_TREE, 1, -1, 1, 1),
    (F_TREE, 1, 0, 0, 1), (F_RANK_ACROSS, 0, 5), (F_TREE, 5, -1, 0, 0), (F_TREE, 3, -3, 0, 0),
    (F_TO_RANK, 1, 1), (F_ACT_X, 1, 0, 1), (F_TREE, 1, 1, 0, 1), (F_TREE, 5, 2, 1, 0), (F_OWN_FAR, 1, 8),
    (F_ACT_X, 1, 0, 0), (F_TREE, 5, -1, 0, 1), (F_TREE, 4, -3, 0, 0), (F_TREE, 0, 1, 1, 1),
    (F_TREE, 1, 1, 1, 1), (F_TREE, 2, 3, 0, 1), (F_TREE, 3, 1, 1, 1), (F_TREE, 3, -1, 0, 1),
    (F_TREE, 4, -1, 1, 0), (F_TREE, 3, -3, 0, 1), (F_TREE, 3, 2, 0, 1), (F_OWN_ACROSS, 1, 0),
    (F_TREE, 1, -2, 1, 1), (F_TO_RANK, 1, 3), (F_TREE, 3, 0, 1, 0), (F_TREE, 0, 3, 1, 1), (F_TREE, 0, -2, 1, 0),
    (F_TREE, 3, 2, 1, 0), (F_TREE, 2, 3, 1, 0), (F_TREE, 3, 3, 0, 0), (F_TREE_END, 0), (F_TREE, 4, -1, 1, 1),
    (F_TO_RANK, 1, 7), (F_ATTENTION, 0), (F_TREE, 4, 3, 0, 0), (F_ACT_X, 0, 0, 0), (F_TREE, 4, 3, 1, 0),
    (F_TREE, 3, -3, 1, 0), (F_TREE, 4, 3, 0, 1), (F_TREE, 4, -2, 1, 0), (F_TREE, 3, 3, 0, 1),
    (F_TREE, 5, -1, 1, 1), (F_RANK_FAR, 1, 7), (F_RANK_ACROSS, 0, 2), (F_TREE, 4, 2, 1, 0),
    (F_TREE, 5, 1, 1, 1), (F_TREE, 5, 3, 1, 0), (F_TREE, 4, -3, 0, 1), (F_RANK_ACROSS, 0, 4),
    (F_TREE, 4, -3, 1, 0), (F_OWN_FAR, 1, 0), (F_RANK_FAR, 1, 2), (F_TREE, 4, 3, 1, 1), (F_RANK_ACROSS, 1, 7),
    (F_FAR_ACROSS, 1, 8), (F_TREE, 4, 1, 1, 0), (F_ACT_Z, 1, 1), (F_TREE, 5, -2, 0, 1), (F_TREE, 4, -3, 1, 1),
    (F_TREE, 3, 2, 1, 1), (F_TREE, 5, -2, 0, 0), (F_ACT_Z, 0, 0), (F_TREE, 4, 2, 1, 1), (F_TREE, 5, 2, 0, 0),
    (F_RANK_FAR, 1, 1), (F_FF_END, 0), (F_ACT_C, 0, 0, 1, 0), (F_RANK_ACROSS, 1, 2), (F_TREE, 4, 0, 0, 1),
    (F_TREE, 4, 1, 1, 1), (F_RANK_FAR, 1, 5), (F_ACT_X, 1, 1, 0), (F_TREE, 3, -1, 1, 0), (F_TREE, 5, 2, 1, 1),
    (F_TREE, 5, 3, 0, 0), (F_FAR_ACROSS, 1, 7), (F_TREE, 3, 3, 1, 1), (F_TREE, 3, -1, 1, 1),
    (F_TREE, 4, -2, 1, 1), (F_ACT_C, 1, 0, 0, 1), (F_ACT_C, 0, 0, 0, 0), (F_TREE, 4, 0, 1, 1),
    (F_RANK_FAR, 1, 3), (F_ACT_C, 1, 0, 1, 1), (F_TREE, 3, -2, 1, 0), (F_TREE, 5, -2, 1, 0), (F_RANK_FAR, 1, 4),
    (F_FAR_ACROSS, 1, 0), (F_TREE, 5, -3, 0, 0), (F_TREE, 4, 1, 0, 1), (F_TREE, 3, -2, 1, 1),
    (F_ACT_C, 1, 1, 1, 0), (F_RANK_FAR, 1, 6), (F_TREE, 4, -1, 0, 1), (F_TREE, 5, 2, 0, 1),
    (F_TREE, 5, -3, 1, 0), (F_ACT_C, 0, 0, 0, 1), (F_FAR_ACROSS, 1, 2), (F_ACT_C, 1, 1, 0, 0),
    (F_TREE, 5, -3, 0, 1), (F_TREE, 5, -2, 1, 1), (F_TREE, 3, 3, 1, 0), (F_RANK_ACROSS, 1, 6),
    (F_RANK_ACROSS, 1, 3), (F_TREE, 5, 3, 1, 1), (F_RANK_ACROSS, 1, 4), (F_BLOCK, 0, 1), (F_TREE, 4, 2, 0, 1),
    (F_TREE, 5, 3, 0, 1), (F_TREE, 4, -2, 0, 1), (F_TREE, 3, -3, 1, 1), (F_FAR_ACROSS, 1, 1),
    (F_TREE, 5, -3, 1, 1), (F_BLOCK, 0, 0), (F_RANK_ACROSS, 1, 5), (F_ACT_X, 1, 1, 1), (F_TREE_END, 1),
    (F_ATTENTION, 1), (F_FAR_ACROSS, 1, 3), (F_RANK_ACROSS, 1, 1), (F_ACT_X, 0, 0, 1), (F_BLOCK, 0, 2),
    (F_FAR_ACROSS, 1, 5), (F_ACT_C, 0, 0, 1, 1), (F_BLOCK, 0, 3), (F_DOWN_GRAD, 0), (F_ACT_C, 1, 1, 0, 1),
    (F_FAR_ACROSS, 1, 6), (F_ACT_X, 0, 1, 0), (F_ACT_C, 1, 1, 1, 1), (F_ACT_Z, 0, 1), (F_FAR_ACROSS, 1, 4),
    (F_GATE_GRAD, 0), (F_ACT_C, 0, 1, 0, 1), (F_ACT_C, 0, 1, 0, 0), (F_FF_END, 1), (F_ACT_C, 0, 1, 1, 0),
    (F_BLOCK, 1, 1), (F_BLOCK, 1, 2), (F_ACT_X, 0, 1, 1), (F_BLOCK, 1, 0), (F_ACT_C, 0, 1, 1, 1),
    (F_BLOCK, 1, 3), (F_DOWN_GRAD, 1), (F_GATE_GRAD, 1),
]


def forward_kernel(
    valid_ref,
    lengths_ref,
    norm_attn_ref,
    norm_ff_ref,
    tokens_ref,
    cot_ref,
    qkv_ref,
    out_ref,
    gate_up_ref,
    down_ref,
    gain_rows,
    cot_rows,
    qkv_rows,
    context,
    resid_mid,
    qkv_full,
    out_full,
    ff_out,
    ff_back,
    gate_up_grad,
    down_grad,
    qkv_buf,
    out_buf,
    gate_up_buf,
    down_buf,
    rows_buf,
    grads_buf,
    hidden,
    d_gate_up,
    out_stage,
    back_stage,
    gate_up_stage,
    down_stage,
    gains_own,
    gains_all,
    gate_up_raw,
    gate_up_parts,
    grads_own,
    attn_in,
    halves,
    spread,
    plane_sem,
    sibling_sem,
    send_sem,
    gains_send,
    gains_recv,
    rank_send,
    rank_recv,
    far_send,
    far_recv,
    across_send,
    across_recv,
    act_send,
    act_recv,
    local_sem,
    keep_sem,
    stage_sem,
):
    z, y, x, core = here()
    me = 2 * (z * 4 + y * 2 + x) + core
    zh, zl, member, rank, device, far, across = group_place(z, y, x, core)
    own_step = (0, 0, 0)
    act_height, positions, model = tokens_ref.shape
    height = gate_up_ref.shape[1]
    down_height = down_ref.shape[1]
    split = 4 * down_height
    sibling = neighbour("s", z, y, x, core)
    greet_all(z, y, x, core)
    part = qkv_ref.shape[2] // 2
    pieces = []
    for s in range(positions):
        pieces.append((qkv_ref, qkv_buf, s, pl.ds(0, part), "zxy"))
        pieces.append((qkv_ref, qkv_buf, s, pl.ds(part, part), "zyx"))
        pieces.append((out_ref, out_buf, s, pl.ds(0, model), ("xyz", "yxz")[s % 2]))

    def piece_rows(piece, number):
        _, full, index, columns, _ = pieces[piece]
        return full.at[index, pl.ds(pl.multiple_of(number * height, height), height), columns]

    def tree_send(piece, offset, direction):
        source, _, index, columns, _ = pieces[piece]
        chip = chip_of(offset, z, y, x)
        block = piece_rows(piece, 2 * chip + core)
        recv = sibling_sem if direction == "s" else plane_sem
        return push(
            source.at[index, :, columns] if hops(offset) == 0 else block,
            block,
            send_sem.at[piece, chip, DIRECTIONS.index(direction)],
            recv.at[piece, chip],
            neighbour(direction, z, y, x, core),
        )

    def tree_step(piece, offset, finish=False):
        order = pieces[piece][4]

        def go():
            chip = chip_of(offset, z, y, x)
            if hops(offset) > 0 and not finish:
                arrived(piece_rows(piece, 2 * chip + core), plane_sem.at[piece, chip], sibling)
            for direction in onward(order, offset) + ["s"]:
                copy = tree_send(piece, offset, direction)
                maybe(direction_exists(direction, z), copy.wait_send if finish else copy.start)

        maybe(offset_exists(offset, z), go)

    events = sorted(
        (
            (hops(offset), place, piece, offset)
            for piece in range(len(pieces))
            for place, offset in enumerate(OFFSETS)
        ),
        key=lambda event: event[:3],
    )

    def tree_steps(s, distance):
        for hop, _, piece, offset in events:
            if hop == distance and pieces[piece][2] == s:
                tree_step(piece, offset)

    def tree_end(s):
        mine = [piece for piece in range(len(pieces)) if pieces[piece][2] == s]

        def sibling_wait(chip, carry):
            for piece in mine:
                arrived(piece_rows(piece, 2 * chip + 1 - core), sibling_sem.at[piece, chip], sibling)
            return carry

        lax.fori_loop(0, 16, sibling_wait, 0)
        for piece in mine:
            tree_own[piece].wait()

    tree_own = [
        pltpu.make_async_copy(
            source.at[index, :, columns], piece_rows(piece, me), local_sem.at[piece]
        )
        for piece, (source, _, index, columns, _) in enumerate(pieces)
    ]

    def gains_copy(step):
        other = lax.rem(me + step, 32)
        return push(
            gains_own,
            gains_all.at[me],
            gains_send.at[step],
            gains_recv.at[me],
            (lax.div(other, 2), lax.rem(other, 2)),
        )

    def gains_start(step, carry):
        gains_copy(step).start()
        return carry

    def gains_wait(step, carry):
        other = lax.rem(me + step, 32)
        gains_copy(step).wait_send()
        arrived(gains_all.at[other], gains_recv.at[other], sibling)
        return carry

    sends = []

    def start(copy):
        copy.start()
        sends.append(copy)

    def weight_rows(s, number):
        return gate_up_buf.at[s, pl.ds(pl.multiple_of(number * height, height), height), :]

    def down_rows(s, dzh, dy):
        number = 2 * flip(zh, dzh) + flip(y, dy)
        return down_buf.at[s, pl.ds(pl.multiple_of(number * down_height, down_height), down_height), :]

    def act_rows(which, s, step):
        full = (rows_buf, grads_buf)[which]
        return full.at[s, pl.ds(pl.multiple_of(rank(step) * act_height, act_height), act_height), :]

    def send_act(which, s, step, source, hop):
        landed = tuple(bit ^ (1 if axis == hop else 0) for axis, bit in enumerate(step))
        start(
            push(
                source,
                act_rows(which, s, step),
                act_send.at[which, s, 4 * step[0] + 2 * step[1] + step[2], hop],
                act_recv.at[which, s, 4 * landed[0] + 2 * landed[1] + landed[2]],
                member(tuple(1 if axis == hop else 0 for axis in range(3))),
            )
        )

    def wait_act(which, s, step):
        arrived(
            act_rows(which, s, step),
            act_recv.at[which, s, 4 * step[0] + 2 * step[1] + step[2]],
            sibling,
        )

    def act_own(which, s):
        source = act_rows(0, s, own_step) if which == 0 else grads_own.at[s]
        for hop in (0, 1, 2):
            send_act(which, s, own_step, source, hop)

    def act_from_z(which, s):
        step = (1, 0, 0)
        wait_act(which, s, step)
        send_act(which, s, step, act_rows(which, s, step), 1)
        send_act(which, s, step, act_rows(which, s, step), 2)

    def act_from_x(which, s, dl):
        wait_act(which, s, (dl, 1, 0))
        send_act(which, s, (dl, 1, 0), act_rows(which, s, (dl, 1, 0)), 2)

    def act_from_core(which, s, dl, dx):
        wait_act(which, s, (dl, dx, 1))

    def mine(s):
        return gate_up_parts.at[rank(own_step), s]

    def ff_source(s, slot):
        return down_ref.at[s] if slot == 8 else mine(s)

    def ff_rows(s, slot, dzh):
        return down_rows(s, dzh, 0) if slot == 8 else weight_rows(s, device(RANK_STEPS[slot], dzh, 0))

    def to_rank(s, slot):
        step = RANK_STEPS[slot]
        start(
            push(
                gate_up_parts.at[rank(step), s],
                weight_rows(s, device(own_step)),
                rank_send.at[s, slot],
                rank_recv.at[s, slot],
                member(step),
            )
        )

    def send_far(s, slot, source):
        start(push(source, ff_rows(s, slot, 0), far_send.at[s, slot], far_recv.at[s, slot], far))

    def send_across(s, slot, source, dzh):
        start(
            push(
                source,
                ff_rows(s, slot, dzh),
                across_send.at[s, dzh, slot],
                across_recv.at[s, dzh, slot],
                across,
            )
        )

    def own_far(s, slot):
        send_far(s, slot, ff_source(s, slot))

    def own_across(s, slot):
        send_across(s, slot, ff_source(s, slot), 0)

    def rank_far(s, slot):
        arrived(ff_rows(s, slot, 0), rank_recv.at[s, slot], sibling)
        send_far(s, slot, ff_rows(s, slot, 0))

    def rank_across(s, slot):
        send_across(s, slot, ff_rows(s, slot, 0), 0)

    def far_across(s, slot):
        arrived(ff_rows(s, slot, 1), far_recv.at[s, slot], sibling)
        send_across(s, slot, ff_rows(s, slot, 1), 1)

    def ff_end(s):
        for copy in ff_local[s]:
            copy.wait()
        for dzh in (0, 1):
            for slot, step in enumerate(RANK_STEPS):
                arrived(weight_rows(s, device(step, dzh, 1)), across_recv.at[s, dzh, slot], sibling)
            arrived(down_rows(s, dzh, 1), across_recv.at[s, dzh, 8], sibling)

    ff_local = []
    for s in range(positions):
        ff_local.append(
            [
                pltpu.make_async_copy(mine(s), weight_rows(s, device(own_step)), local_sem.at[7 + 3 * s]),
                pltpu.make_async_copy(down_ref.at[s], down_rows(s, 0, 0), local_sem.at[8 + 3 * s]),
                pltpu.make_async_copy(grads_own.at[s], act_rows(1, s, own_step), local_sem.at[9 + 3 * s]),
            ]
        )
    gains_local = pltpu.make_async_copy(gains_own, gains_all.at[me], local_sem.at[6])

    def gains_begin():
        places = 128 // norm_attn_ref.shape[1]
        lane = lax.broadcasted_iota(jnp.int32, (positions, 128), 1) // norm_attn_ref.shape[1]
        gains_own[...] = jnp.zeros_like(gains_own)
        for index, source in enumerate((norm_attn_ref, norm_ff_ref)):
            tiled = jnp.concatenate([source[...].astype(F32)] * places, axis=1)
            gains_own[index * positions : (index + 1) * positions, :] = jnp.where(
                lane == lax.rem(me, places), tiled, 0.0
            ).astype(BF16)
        lax.fori_loop(1, 32, gains_start, 0)
        gains_local.start()

    raw_copy = pltpu.make_async_copy(gate_up_ref, gate_up_raw, local_sem.at[13])

    def part_units():
        raw_copy.wait()
        unit = down_height
        for number in range(8):
            low, rest = divmod(number, 4)
            for s in range(positions):
                for side in (0, 1):
                    for group in range(4):
                        zh_part, y_part = divmod(group, 2)
                        block = 32 * side + 16 * zh_part + 8 * low + 4 * y_part + rest
                        gate_up_parts[number, s, :, (4 * side + group) * unit : (4 * side + group + 1) * unit] = (
                            gate_up_raw[s, :, block * unit : (block + 1) * unit]
                        )
        for s in range(positions):
            ff_local[s][0].start()
            ff_local[s][1].start()

    def weigh():
        def one(rows):
            slot = lax.broadcasted_iota(jnp.int32, (16, 128), 0) + rows.start
            frame = me * act_height + slot
            weight = jnp.zeros((16, 128), F32)
            first = 0
            for item in range(lengths_ref.shape[0]):
                length = lengths_ref[item]
                inside = (frame >= first) & (frame < first + length)
                share = 8.0 * act_height / jnp.full((16, 128), length, jnp.int32).astype(F32)
                weight = weight + jnp.where(inside, share, 0.0)
                first = first + length
            weight = jnp.where(slot < valid_ref[0], weight, 0.0)[:, :1]
            values = cot_ref[rows].astype(F32)
            for p in range(positions):
                grads = values[:, p, :] * weight
                cot_rows[p, rows, :] = grads
                grads_own[p, rows, :] = grads.astype(BF16)

        row_loop(act_height, 16, one)
        for s in range(positions):
            ff_local[s][2].start()

    def take_gains():
        lax.fori_loop(1, 32, gains_wait, 0)
        gains_local.wait()
        for block in range(8):
            total = gains_all[4 * block].astype(F32)
            for extra in range(1, 4):
                total = total + gains_all[4 * block + extra].astype(F32)
            gain_rows[:, 128 * block : 128 * block + 128] = total

        def first_norm(rows):
            values = tokens_ref[rows].astype(F32)
            for p in range(positions):
                resid_mid[p, rows, :] = values[:, p, :]
                r, _ = normed(values[:, p, :])
                attn_in[p, rows, :] = (r * gain_rows[p : p + 1, :]).astype(BF16)

        row_loop(act_height, 16, first_norm)

    keep = []

    def attention(p):
        for source, target, slot in (
            (qkv_buf.at[p], qkv_full.at[p], 2 * p),
            (out_buf.at[p], out_full.at[p], 2 * p + 1),
        ):
            keep.append(pltpu.make_async_copy(source, target, keep_sem.at[slot]))
            keep[-1].start()

        def project(columns):
            qkv_rows[p, :, columns] = dot(attn_in[p], qkv_buf[p, :, columns]).astype(BF16)

        tile_loop(3 * model, 512, project)
        probs = attention_probs(qkv_rows, halves, spread, model, p)
        for q in range(p + 1):
            halves[2 * q] = to_heads(probs[q].astype(BF16), spread)

        def mix(rows):
            total = None
            for q in range(p + 1):
                term = halves[2 * q, rows, :].astype(F32) * qkv_rows[q, rows, 2 * model :].astype(F32)
                total = term if total is None else total + term
            context[p, rows, :] = total.astype(BF16)

        row_loop(act_height, 16, mix)

        def attend(columns):
            resid_mid[p, :, columns] += dot(context[p], out_buf[p, :, columns])

        tile_loop(model, 512, attend)

        def second_norm(step, carry):
            rows = pl.ds(pl.multiple_of(step * 16, 16), 16)
            r, _ = normed(resid_mid[p, rows, :])
            top = rank(own_step) * act_height + step * 16
            rows_buf[p, pl.ds(pl.multiple_of(top, 16), 16), :] = (
                r * gain_rows[positions + p : positions + p + 1, :]
            ).astype(BF16)
            return carry

        lax.fori_loop(0, act_height // 16, second_norm, 0)

    def ff_block(s, number):
        rows = pl.ds(pl.multiple_of(number * 2 * act_height, 2 * act_height), 2 * act_height)
        normed_rows = rows_buf[s, rows, :]
        grads = grads_buf[s, rows, :]
        for tile in range(split // 256):
            left, right = pl.ds(tile * 256, 256), pl.ds(split + tile * 256, 256)
            gate = dot(normed_rows, gate_up_buf[s, :, left])
            up = dot(normed_rows, gate_up_buf[s, :, right])
            d_hidden = dot_back(grads, down_buf[s, left, :])
            sigmoid_gate = jax.nn.sigmoid(gate)
            silu_gate = gate * sigmoid_gate
            hidden[rows, left] = (silu_gate * up).astype(BF16)
            d_gate_up[rows, left] = (
                d_hidden * up * sigmoid_gate * (1.0 + gate * (1.0 - sigmoid_gate))
            ).astype(BF16)
            d_gate_up[rows, right] = (d_hidden * silu_gate).astype(BF16)
        for tile in range(model // 512):
            columns = pl.ds(tile * 512, 512)
            out_stage[rows, columns] = dot(hidden[rows, :], down_buf[s, :, columns]).astype(BF16)
            back_stage[rows, columns] = dot_back(
                d_gate_up[rows, :], gate_up_buf[s, columns, :]
            ).astype(BF16)

    stages = []

    def stage_out(s, *slots):
        for slot in slots:
            source, target = (
                (out_stage, ff_out),
                (back_stage, ff_back),
                (gate_up_stage, gate_up_grad),
                (down_stage, down_grad),
            )[slot]
            stages.append(pltpu.make_async_copy(source, target.at[s], stage_sem.at[s, slot]))
            stages[-1].start()

    def gate_grad(s):
        stage_out(s, 0, 1)

        def gate_up_tile(columns):
            gate_up_stage[:, columns] = dot_grad(rows_buf[s], d_gate_up[:, columns]).astype(BF16)

        tile_loop(2 * split, 256, gate_up_tile)
        stage_out(s, 2)

    def down_weights_grad(s):
        def down_tile(columns):
            down_stage[:, columns] = dot_grad(hidden[...], grads_buf[s, :, columns]).astype(BF16)

        tile_loop(model, 256, down_tile)
        stage_out(s, 3)

    def stages_end():
        while stages:
            stages.pop(0).wait()

    for copy in tree_own:
        copy.start()
    raw_copy.start()
    gains_begin()
    make_spread(spread)
    chips = ((0, 0), (1, 0), (0, 1), (1, 1))

    def block(s, order):
        if s > 0 and order == chosen_first[0]:
            stages_end()
        ff_block(s, 2 * flip(zl, chips[order][0]) + flip(x, chips[order][1]))

    def attend_and_send(s):
        attention(s)
        act_own(0, s)

    chosen_first = [step[2] for step in FORWARD_STEPS if step[:2] == (F_BLOCK, 1)]
    kinds = {
        F_TREE: lambda piece, dz, dy, dx: tree_step(piece, (dz, dy, dx)),
        F_TREE_END: tree_end,
        F_GAINS: take_gains,
        F_PARTS: part_units,
        F_COT: weigh,
        F_ATTENTION: attend_and_send,
        F_GRADS: lambda s: act_own(1, s),
        F_ACT_Z: act_from_z,
        F_ACT_X: act_from_x,
        F_ACT_C: act_from_core,
        F_TO_RANK: to_rank,
        F_OWN_FAR: own_far,
        F_OWN_ACROSS: own_across,
        F_RANK_FAR: rank_far,
        F_RANK_ACROSS: rank_across,
        F_FAR_ACROSS: far_across,
        F_FF_END: ff_end,
        F_BLOCK: block,
        F_GATE_GRAD: gate_grad,
        F_DOWN_GRAD: down_weights_grad,
    }
    for kind, *numbers in FORWARD_STEPS:
        kinds[kind](*numbers)
    for _, _, piece, offset in events:
        tree_step(piece, offset, finish=True)
    for copy in sends:
        copy.wait_send()
    for copy in keep:
        copy.wait()
    stages_end()


def forward_gather(valid, lengths, norm_attn, norm_ff, tokens, cot, w_qkv, w_out, w_gate_up, w_down):
    act_height, positions, model = tokens.shape
    _, height, qkv_width = w_qkv.shape
    unit = w_down.shape[1]
    ranks, split, width = 8, 4 * unit, 8 * unit
    group_rows = ranks * act_height
    dma = pltpu.SemaphoreType.DMA
    vmem = pl.BlockSpec(memory_space=pltpu.VMEM)
    smem = pl.BlockSpec(memory_space=pltpu.SMEM)
    anywhere = pl.BlockSpec(memory_space=pl.ANY)
    return pl.pallas_call(
        forward_kernel,
        out_shape=(
            jax.ShapeDtypeStruct((16, model), F32),
            jax.ShapeDtypeStruct((positions, act_height, model), F32),
            jax.ShapeDtypeStruct((positions, act_height, 3 * model), BF16),
            jax.ShapeDtypeStruct((positions, act_height, model), BF16),
            jax.ShapeDtypeStruct((positions, act_height, model), F32),
            jax.ShapeDtypeStruct((positions, model, qkv_width), BF16),
            jax.ShapeDtypeStruct((positions, model, model), BF16),
            jax.ShapeDtypeStruct((positions, group_rows, model), BF16),
            jax.ShapeDtypeStruct((positions, group_rows, model), BF16),
            jax.ShapeDtypeStruct((positions, model, width), BF16),
            jax.ShapeDtypeStruct((positions, split, model), BF16),
        ),
        in_specs=[smem] * 2 + [vmem] * 4 + [anywhere] * 4,
        out_specs=(vmem,) * 5 + (anywhere,) * 6,
        scratch_shapes=[
            pltpu.VMEM((positions, model, qkv_width), BF16),
            pltpu.VMEM((positions, model, model), BF16),
            pltpu.VMEM((positions, model, width), BF16),
            pltpu.VMEM((positions, split, model), BF16),
            pltpu.VMEM((positions, group_rows, model), BF16),
            pltpu.VMEM((positions, group_rows, model), BF16),
            pltpu.VMEM((group_rows, split), BF16),
            pltpu.VMEM((group_rows, width), BF16),
            pltpu.VMEM((group_rows, model), BF16),
            pltpu.VMEM((group_rows, model), BF16),
            pltpu.VMEM((model, width), BF16),
            pltpu.VMEM((split, model), BF16),
            pltpu.VMEM((16, 128), BF16),
            pltpu.VMEM((32, 16, 128), BF16),
            pltpu.VMEM(w_gate_up.shape, BF16),
            pltpu.VMEM((ranks, positions, height, width), BF16),
            pltpu.VMEM((positions, act_height, model), BF16),
            pltpu.VMEM((positions, act_height, model), BF16),
            pltpu.VMEM((2 * positions, act_height, model), BF16),
            pltpu.VMEM((model, 128), BF16),
            dma((6, 16)),
            dma((6, 16)),
            dma((6, 16, 5)),
            dma((32,)),
            dma((32,)),
            dma((2, 8)),
            dma((2, 8)),
            dma((2, 9)),
            dma((2, 9)),
            dma((2, 2, 9)),
            dma((2, 2, 9)),
            dma((2, 2, 8, 3)),
            dma((2, 2, 8)),
            dma((14,)),
            dma((4,)),
            dma((2, 4)),
        ],
        compiler_params=pltpu.CompilerParams(
            collective_id=4, has_side_effects=True, vmem_limit_bytes=62 * 2**20
        ),
        name="forward_gather",
    )(valid, lengths, norm_attn, norm_ff, tokens, cot, w_qkv, w_out, w_gate_up, w_down)


def slot_index(order, direction, offset, z, y, x):
    axis = {"u": "z", "d": "z"}.get(direction, direction)
    index, count = 0, 1
    values = dict(z=z + offset[0], y=flip(y, offset[1]), x=flip(x, offset[2]))
    sizes = dict(z=4, y=2, x=2)
    for earlier in order[: order.index(axis)]:
        index = index * sizes[earlier] + values[earlier]
        count *= sizes[earlier]
    if axis == "z":
        index = index * 5 + (4 if direction == "d" and offset[0] == 0 else values["z"])
        count *= 5
    return index, count


def slot_base(order):
    base, total = {}, 0
    for axis, direction in (("x", "x"), ("y", "y"), ("z", "u")):
        base[axis] = total
        total += slot_index(order, direction, (0, 0, 0), 0, 0, 0)[1]
    base["u"] = base["d"] = base["z"]
    return base, total


(
    B_TREE,
    B_RS_ACROSS,
    B_RS_FIRST,
    B_RS_SECOND,
    B_RS_RANK,
    B_RS_LAST,
    B_ACT_CORE,
    B_ACT_LOAD,
    B_ACT_ADD_X,
    B_ACT_ADD_Z,
    B_ACT_SUM,
    B_NORM_TURN,
    B_SWAP_TURNED,
    B_PROBS,
    B_MID,
    B_SCORES_BACK,
    B_SWAP_QKV,
    B_OUT_W,
    B_QKV_W,
    B_ROWS_BACK,
    B_ATTN_BACK,
    B_FINISH_OUTPUT,
) = range(22)
BACKWARD_STEPS = [
    (B_RS_ACROSS, 0, 0, 0), (B_ACT_CORE, 0, 0), (B_ACT_ADD_X, 0, 0, 1), (B_NORM_TURN,), (B_RS_FIRST, 0, 0),
    (B_RS_ACROSS, 0, 0, 1), (B_ACT_CORE, 0, 1), (B_ACT_ADD_Z, 0, 0), (B_ACT_ADD_X, 0, 0, 0),
    (B_ACT_ADD_X, 0, 1, 1), (B_RS_ACROSS, 1, 1, 0), (B_SWAP_TURNED,), (B_RS_ACROSS, 0, 1, 0),
    (B_RS_ACROSS, 0, 0, 2), (B_ACT_ADD_X, 0, 1, 0), (B_RS_FIRST, 0, 1), (B_RS_ACROSS, 1, 0, 1),
    (B_RS_ACROSS, 0, 1, 1), (B_PROBS,), (B_RS_ACROSS, 1, 1, 1), (B_ACT_ADD_Z, 0, 1), (B_RS_FIRST, 0, 2),
    (B_ACT_CORE, 1, 0), (B_ACT_SUM, 0, 0), (B_ACT_SUM, 0, 1), (B_MID, 1), (B_MID, 0), (B_ACT_LOAD, 1),
    (B_OUT_W, 0), (B_OUT_W, 1), (B_ACT_CORE, 1, 1), (B_ACT_ADD_X, 1, 0, 1), (B_RS_FIRST, 1, 1),
    (B_TREE, 2, -3, 0, 0), (B_SCORES_BACK,), (B_TREE, 2, -3, 1, 1), (B_TREE, 3, 3, 0, 0),
    (B_RS_ACROSS, 1, 0, 2), (B_SWAP_QKV,), (B_ACT_ADD_X, 1, 0, 0), (B_TREE, 3, 3, 0, 1), (B_TREE, 2, 3, 1, 0),
    (B_TREE, 3, -3, 0, 1), (B_RS_SECOND, 0, 1), (B_TREE, 2, -3, 0, 1), (B_QKV_W, 0), (B_ACT_ADD_X, 1, 1, 1),
    (B_TREE, 2, 3, 1, 1), (B_RS_FIRST, 1, 2), (B_RS_ACROSS, 0, 1, 2), (B_TREE, 0, -1, 1, 1),
    (B_RS_ACROSS, 1, 0, 0), (B_QKV_W, 1), (B_TREE, 2, 2, 1, 1), (B_TREE, 1, 2, 1, 1), (B_TREE, 2, 3, 0, 0),
    (B_TREE, 2, 2, 1, 0), (B_TREE, 0, -3, 1, 1), (B_RS_SECOND, 0, 0), (B_RS_ACROSS, 1, 1, 2),
    (B_TREE, 1, 1, 1, 1), (B_TREE, 2, 3, 0, 1), (B_TREE, 0, 1, 1, 1), (B_TREE, 1, -3, 1, 1),
    (B_TREE, 1, -1, 0, 1), (B_TREE, 2, -2, 1, 1), (B_TREE, 0, 3, 1, 0), (B_TREE, 3, -3, 1, 0),
    (B_TREE, 1, 0, 1, 1), (B_RS_RANK, 0, 1), (B_TREE, 3, 2, 0, 1), (B_TREE, 2, -3, 1, 0), (B_TREE, 2, -1, 1, 1),
    (B_TREE, 3, 3, 1, 0), (B_TREE, 2, -2, 0, 0), (B_TREE, 3, -2, 0, 1), (B_TREE, 1, -3, 0, 1),
    (B_TREE, 3, 3, 1, 1), (B_TREE, 0, 3, 1, 1), (B_TREE, 3, -3, 1, 1), (B_RS_SECOND, 1, 1), (B_RS_RANK, 0, 3),
    (B_RS_FIRST, 1, 0), (B_TREE, 0, -2, 1, 1), (B_TREE, 2, 2, 0, 1), (B_TREE, 0, -3, 0, 1),
    (B_ACT_ADD_X, 1, 1, 0), (B_RS_RANK, 0, 4), (B_TREE, 3, -2, 1, 1), (B_TREE, 2, 1, 1, 0),
    (B_TREE, 0, 0, 1, 0), (B_TREE, 0, -3, 1, 0), (B_TREE, 3, -2, 1, 0), (B_ACT_ADD_Z, 1, 1),
    (B_TREE, 2, 2, 0, 0), (B_TREE, 1, -2, 1, 1), (B_TREE, 3, -1, 0, 1), (B_ROWS_BACK, 0), (B_TREE, 1, 3, 1, 1),
    (B_TREE, 0, -1, 1, 0), (B_TREE, 3, 2, 1, 0), (B_TREE, 2, -1, 0, 0), (B_TREE, 2, -2, 1, 0),
    (B_TREE, 2, -2, 0, 1), (B_TREE, 3, 2, 1, 1), (B_TREE, 0, 2, 1, 1), (B_TREE, 1, 3, 0, 1),
    (B_TREE, 0, 3, 0, 1), (B_RS_RANK, 0, 7), (B_TREE, 1, -3, 1, 0), (B_TREE, 1, 1, 0, 1), (B_TREE, 2, 1, 1, 1),
    (B_ACT_ADD_Z, 1, 0), (B_TREE, 3, 1, 0, 1), (B_TREE, 1, -2, 1, 0), (B_TREE, 0, -2, 1, 0),
    (B_TREE, 0, 0, 1, 1), (B_TREE, 1, -1, 1, 1), (B_RS_SECOND, 1, 0), (B_TREE, 2, 1, 0, 0),
    (B_TREE, 0, -2, 0, 1), (B_TREE, 3, -1, 1, 1), (B_RS_LAST, 0, 4), (B_TREE, 3, 2, 0, 0), (B_RS_RANK, 1, 2),
    (B_TREE, 3, -3, 0, 0), (B_ACT_SUM, 1, 0), (B_TREE, 1, -2, 0, 1), (B_TREE, 2, 1, 0, 1),
    (B_TREE, 0, -3, 0, 0), (B_TREE, 1, 3, 1, 0), (B_TREE, 0, 2, 0, 1), (B_RS_RANK, 1, 7), (B_TREE, 0, -1, 0, 1),
    (B_TREE, 2, -1, 1, 0), (B_TREE, 2, -1, 0, 1), (B_TREE, 1, -3, 0, 0), (B_TREE, 3, 1, 1, 1),
    (B_RS_RANK, 1, 5), (B_RS_RANK, 0, 6), (B_RS_LAST, 0, 7), (B_TREE, 0, 1, 1, 0), (B_TREE, 0, 2, 1, 0),
    (B_TREE, 3, 1, 1, 0), (B_TREE, 2, 0, 1, 1), (B_TREE, 0, 3, 0, 0), (B_RS_LAST, 1, 2), (B_TREE, 1, -1, 1, 0),
    (B_ACT_SUM, 1, 1), (B_FINISH_OUTPUT,), (B_TREE, 1, 3, 0, 0), (B_TREE, 0, -2, 0, 0), (B_TREE, 1, 2, 0, 1),
    (B_TREE, 1, 0, 1, 0), (B_TREE, 3, 1, 0, 0), (B_RS_RANK, 1, 6), (B_TREE, 3, -1, 1, 0), (B_RS_RANK, 0, 2),
    (B_RS_RANK, 1, 1), (B_TREE, 0, 2, 0, 0), (B_ROWS_BACK, 1), (B_RS_LAST, 1, 1), (B_TREE, 1, 0, 0, 1),
    (B_TREE, 0, 1, 0, 1), (B_TREE, 1, 2, 1, 0), (B_TREE, 3, -2, 0, 0), (B_RS_LAST, 0, 6), (B_RS_LAST, 1, 6),
    (B_TREE, 0, 0, 0, 1), (B_RS_RANK, 0, 5), (B_TREE, 2, 0, 1, 0), (B_TREE, 2, 0, 0, 1), (B_RS_LAST, 1, 5),
    (B_TREE, 1, 1, 1, 0), (B_TREE, 3, 0, 0, 1), (B_TREE, 1, -2, 0, 0), (B_TREE, 1, 2, 0, 0), (B_ATTN_BACK,),
    (B_TREE, 3, -1, 0, 0), (B_TREE, 0, -1, 0, 0), (B_TREE, 0, 1, 0, 0), (B_TREE, 1, -1, 0, 0),
    (B_RS_SECOND, 1, 2), (B_TREE, 1, 1, 0, 0), (B_TREE, 3, 0, 1, 1), (B_RS_SECOND, 0, 2), (B_RS_LAST, 0, 3),
    (B_RS_LAST, 0, 1), (B_RS_LAST, 0, 2), (B_TREE, 0, 0, 0, 0), (B_TREE, 2, 0, 0, 0), (B_RS_LAST, 0, 5),
    (B_TREE, 3, 0, 1, 0), (B_RS_LAST, 1, 7), (B_RS_RANK, 1, 4), (B_RS_RANK, 1, 3), (B_TREE, 1, 0, 0, 0),
    (B_RS_LAST, 1, 4), (B_TREE, 3, 0, 0, 0), (B_RS_LAST, 1, 3),
]


def backward_kernel(
    tokens_ref,
    cot_ref,
    gain_rows,
    qkv_rows,
    context,
    resid_mid,
    qkv_full,
    out_full,
    out_ref,
    back_ref,
    gate_up_ref,
    down_ref,
    output,
    grad_tokens,
    norm_attn_sum,
    norm_ff_sum,
    qkv_sum,
    attn_out_sum,
    gate_up_total,
    down_sum,
    act_own,
    core_buf,
    x_buf,
    z_buf,
    gate_own,
    down_own,
    across_gate,
    across_down,
    far_gate,
    far_down,
    qkv_grad,
    out_grad,
    slots_0,
    slots_1,
    slots_2,
    slots_3,
    qkv_tiles,
    out_tiles,
    turned,
    attn_turned,
    context_turned,
    d_qkv,
    d_mid_low,
    d_mid,
    d_context,
    d_rows,
    halves,
    probs_buf,
    spread,
    gain_acc,
    gains_part,
    gains_buf,
    gains_sum,
    gate_up_sum,
    core_send,
    core_recv,
    x_send,
    x_recv,
    z_send,
    z_recv,
    across_send,
    across_recv,
    far_send,
    far_recv,
    rank_send,
    rank_recv,
    swap_send,
    swap_recv,
    tree_send,
    tree_recv,
    gains_send,
    gains_recv,
    own_sem,
    part_sem,
    tile_sem,
):
    z, y, x, core = here()
    me = 2 * (z * 4 + y * 2 + x) + core
    zh, zl, member, rank, device, far, across = group_place(z, y, x, core)
    own_step = (0, 0, 0)
    act_height, positions, model = tokens_ref.shape
    sets = positions
    height = qkv_sum.shape[1]
    down_height = down_sum.shape[1]
    half = 16 * height
    sibling = member((0, 0, 1))
    scale = 1.0 / math.sqrt(HEAD_DIM)
    pairs = pairs_of(positions)
    greet_all(z, y, x, core)
    sends = []

    def start(copy):
        copy.start()
        sends.append(copy)

    def run_rows(dzh, dy, low):
        number = 16 * flip(zh, dzh) + 4 * flip(y, dy) + 8 * low
        return pl.ds(pl.multiple_of(number * height, 4 * height), 4 * height)

    def down_rows(dzh, dy):
        number = 2 * flip(zh, dzh) + flip(y, dy)
        return pl.ds(pl.multiple_of(number * down_height, down_height), down_height)

    def ff_from(s, dzh, dy, part):
        if part == 2:
            return down_ref.at[s, down_rows(dzh, dy)]
        return gate_up_ref.at[s, run_rows(dzh, dy, part)]

    def ff_across(s, turn, part):
        return across_down.at[turn, s] if part == 2 else across_gate.at[turn, s, part]

    def ff_own(s, turn, part):
        return down_own.at[turn, s] if part == 2 else gate_own.at[turn, s, part]

    def ff_far(s, part):
        return far_down.at[s] if part == 2 else far_gate.at[s, part]

    def part_copy(s, turn, part):
        return pltpu.make_async_copy(
            ff_from(s, 1 - turn, 0, part), ff_own(s, turn, part), part_sem.at[turn, s, part]
        )

    def rs_across(s, turn, part):
        start(
            push(
                ff_from(s, 1 - turn, 1, part),
                ff_across(s, turn, part),
                across_send.at[turn, s, part],
                across_recv.at[turn, s, part],
                across,
            )
        )

    def rs_first(s, part):
        block = ff_across(s, 0, part)
        part_copy(s, 0, part).wait()
        arrived(block, across_recv.at[0, s, part], across)
        add_into(block, [block, ff_own(s, 0, part)])
        start(push(block, ff_far(s, part), far_send.at[s, part], far_recv.at[s, part], far))

    def rs_second(s, part):
        block = ff_across(s, 1, part)
        part_copy(s, 1, part).wait()
        arrived(block, across_recv.at[1, s, part], across)
        arrived(ff_far(s, part), far_recv.at[s, part], far)
        target = down_sum.at[s] if part == 2 else block
        add_into(target, [block, ff_far(s, part), ff_own(s, 1, part)])

    def share(step, s):
        number = 2 * flip(x, step[1]) + flip(core, step[2])
        return across_gate.at[
            1, s, flip(zl, step[0]), pl.ds(pl.multiple_of(number * height, height), height)
        ]

    def place_units(step, s, source):
        unit = down_height
        number = 8 * flip(zl, step[0]) + 2 * flip(x, step[1]) + flip(core, step[2])
        for side in (0, 1):
            for group in range(4):
                zh_part, y_part = divmod(group, 2)
                left = (32 * side + 16 * zh_part + 4 * y_part + number) * unit
                gate_up_total[s, :, pl.ds(pl.multiple_of(left, unit), unit)] = source[
                    :, (4 * side + group) * unit : (4 * side + group + 1) * unit
                ].astype(F32)

    def rs_rank(s, slot):
        step = RANK_STEPS[slot]
        start(
            push(
                share(step, s),
                gate_up_sum.at[rank(own_step), s],
                rank_send.at[slot, s],
                rank_recv.at[slot, s],
                member(step),
            )
        )

    def rs_last(s, slot):
        step = RANK_STEPS[slot]
        block = gate_up_sum.at[rank(step), s]
        arrived(block, rank_recv.at[slot, s], member(step))
        place_units(step, s, block)

    acts = [back_ref, out_ref]

    def act_rows(step):
        return pl.ds(pl.multiple_of(rank(step) * act_height, act_height), act_height)

    def act_core(which, s):
        for dl, dx in ((1, 1), (0, 1), (1, 0), (0, 0)):
            start(
                push(
                    acts[which].at[s, act_rows((dl, dx, 1))],
                    core_buf.at[which, s, dl, dx],
                    core_send.at[which, s, dl, dx],
                    core_recv.at[which, s, dl, dx],
                    sibling,
                )
            )

    def act_copy(which, s, dl, dx):
        return pltpu.make_async_copy(
            acts[which].at[s, act_rows((dl, dx, 0))],
            act_own.at[s, dl, dx],
            own_sem.at[which, s, dl, dx],
        )

    def act_load(which):
        for s in range(sets):
            for dl in (0, 1):
                for dx in (0, 1):
                    act_copy(which, s, dl, dx).start()

    def act_ready(which, s, dl, dx):
        act_copy(which, s, dl, dx).wait()
        arrived(core_buf.at[which, s, dl, dx], core_recv.at[which, s, dl, dx], sibling)

    def act_add_x(which, s, dl):
        act_ready(which, s, dl, 1)
        block = core_buf.at[which, s, dl, 1]
        add_into(block, [block, act_own.at[s, dl, 1]])
        start(
            push(
                block,
                x_buf.at[which, s, dl],
                x_send.at[which, s, dl],
                x_recv.at[which, s, dl],
                member((0, 1, 0)),
            )
        )

    def act_add_z(which, s):
        act_ready(which, s, 1, 0)
        block = x_buf.at[which, s, 1]
        arrived(block, x_recv.at[which, s, 1], member((0, 1, 0)))
        add_into(block, [block, core_buf.at[which, s, 1, 0], act_own.at[s, 1, 0]])
        start(
            push(
                block, z_buf.at[which, s], z_send.at[which, s], z_recv.at[which, s], member((1, 0, 0))
            )
        )

    def act_sum(which, s):
        act_ready(which, s, 0, 0)
        arrived(x_buf.at[which, s, 0], x_recv.at[which, s, 0], member((0, 1, 0)))
        arrived(z_buf.at[which, s], z_recv.at[which, s], member((1, 0, 0)))

    def act_total(which, s, rows):
        return (
            act_own[s, 0, 0, rows, :].astype(F32)
            + core_buf[which, s, 0, 0, rows, :].astype(F32)
            + x_buf[which, s, 0, rows, :].astype(F32)
            + z_buf[which, s, rows, :].astype(F32)
        )

    pieces = [
        (qkv_grad, qkv_sum, 0, "zxy", slots_0),
        (qkv_grad, qkv_sum, 1, "zyx", slots_1),
        (out_grad, attn_out_sum, 0, "xyz", slots_2),
        (out_grad, attn_out_sum, 1, "yxz", slots_3),
    ]
    events = sorted(
        ((-hops(offset), place, piece, offset) for piece in range(4) for place, offset in enumerate(OFFSETS)),
        key=lambda event: event[:3],
    )

    def tree_block(piece, offset):
        source, _, index, _, _ = pieces[piece]
        chip = chip_of(offset, z, y, x)
        return source.at[index, pl.ds(pl.multiple_of(chip * height, height), height), :]

    def tree_copy(piece, offset):
        _, _, _, order, slots = pieces[piece]
        toward = came_from(order, offset)
        base, _ = slot_base(order)
        seen = {"x": "x", "y": "y", "u": "d", "d": "u"}[toward]
        nearer = offset
        if toward == "u":
            nearer = (offset[0] - 1, offset[1], offset[2])
        if toward == "d":
            nearer = (offset[0] + 1, offset[1], offset[2])
        there = {"u": z + 1, "d": z - 1}.get(toward, z)
        index_there, _ = slot_index(
            order, seen, nearer, there, y if toward != "y" else 1 - y, x if toward != "x" else 1 - x
        )
        if toward in "xy":
            index_there, _ = slot_index(order, seen, offset, z, y, x)
        place = base[seen] + index_there
        return push(
            tree_block(piece, offset),
            slots.at[place],
            tree_send.at[piece, chip_of(offset, z, y, x)],
            tree_recv.at[piece, place],
            neighbour(toward, z, y, x, core),
        )

    def tree_step(piece, offset):
        _, result, index, order, slots = pieces[piece]
        base, _ = slot_base(order)

        def go():
            block = tree_block(piece, offset)
            sure, unsure = [], []
            for direction in onward(order, offset):
                local, _ = slot_index(order, direction, offset, z, y, x)
                place = base[direction] + local
                (sure if direction in "xy" else unsure).append((direction, place))
            terms = [block]
            for _, place in sure:
                arrived(slots.at[place], tree_recv.at[piece, place], sibling)
                terms.append(slots.at[place])
            last = hops(offset) == 0
            target = result.at[index] if last else block
            if last or len(terms) > 1:
                add_into(target, terms)
            for direction, place in unsure:

                def more(place=place):
                    arrived(slots.at[place], tree_recv.at[piece, place], sibling)
                    add_into(target, [target, slots.at[place]])

                maybe(direction_exists(direction, z), more)
            if not last:
                tree_copy(piece, offset).start()

        maybe(offset_exists(offset, z), go)

    def gains_copy(step):
        other = lax.rem(me + step, 32)
        return push(
            gains_part.at[lax.div(other, 4)],
            gains_buf.at[me],
            gains_send.at[step],
            gains_recv.at[me],
            (lax.div(other, 2), lax.rem(other, 2)),
        )

    def gains_start(step, carry):
        gains_copy(step).start()
        return carry

    def gains_wait(step, carry):
        other = lax.rem(me + step, 32)
        gains_copy(step).wait_send()
        arrived(gains_buf.at[other], gains_recv.at[other], sibling)
        gains_sum[...] += gains_buf[other]
        return carry

    def turn(source, target, slot):
        def one(block, p):
            flat = source(p, block)
            turned[slot, p, pl.ds(2 * block, 2)] = flat.T.astype(BF16).reshape(2, 2, height, act_height)

        for p in range(positions):
            for block in range(model // 128):
                one(block, p)
            target[p, :, :, :act_height] = turned[slot, p, :, core]

    qkv_tile = qkv_tiles.shape[1]
    tile_count = model // qkv_tile

    def qkv_load(number):
        p, tile = divmod(number, tile_count)
        return pltpu.make_async_copy(
            qkv_full.at[p, pl.ds(tile * qkv_tile, qkv_tile)],
            qkv_tiles.at[number % 2],
            tile_sem.at[number % 2],
        )

    out_loads = [
        pltpu.make_async_copy(out_full.at[p], out_tiles.at[p], tile_sem.at[2 + p]) for p in range(positions)
    ]

    def context_block(p, block):
        return context[p, :, 128 * block : 128 * block + 128].astype(F32)

    def attn_block(p, block):
        return d_rows[p, :, 128 * block : 128 * block + 128]

    def norm_turn():
        def attn_norm(rows):
            values = tokens_ref[rows].astype(F32)
            for p in range(positions):
                r, _ = normed(values[:, p, :])
                d_rows[p, rows, :] = r * gain_rows[p : p + 1, :]

        row_loop(act_height, 16, attn_norm)
        turn(context_block, context_turned, 0)
        turn(attn_block, attn_turned, 1)

    def landing(kind, p):
        other = pl.ds(act_height, act_height)
        return (
            context_turned.at[p, :, :, other],
            attn_turned.at[p, :, :, other],
            d_mid_low.at[p, other],
            d_qkv.at[p, other],
        )[kind]

    def swap(kind, p, source):
        start(
            push(source, landing(kind, p), swap_send.at[4 * p + kind], swap_recv.at[4 * p + kind], sibling)
        )

    def swap_wait(kind, p):
        arrived(landing(kind, p), swap_recv.at[4 * p + kind], sibling)

    def swap_turned():
        for p in range(positions):
            swap(0, p, turned.at[0, p, :, 1 - core])
            swap(1, p, turned.at[1, p, :, 1 - core])

    def find_probs():
        for p in range(positions):
            probs = attention_probs(qkv_rows, halves, spread, model, p)
            for q in range(p + 1):
                probs_buf[pairs.index((p, q))] = probs[q]

    def mid(p):
        def mid_back(rows):
            d_ff_in = act_total(0, p, rows)
            r, inverse = normed(resid_mid[p, rows, :])
            gain_acc[positions + p] += r * d_ff_in
            total = cot_ref[p, rows, :] + norm_back(
                r, inverse, d_ff_in * gain_rows[positions + p : positions + p + 1, :]
            )
            d_mid[p, rows, :] = total
            d_mid_low[p, rows, :] = total.astype(BF16)

        row_loop(act_height, 16, mid_back)
        swap(2, p, d_mid_low.at[p, pl.ds(0, act_height)])
        out_loads[p].wait()

        def context_back(columns):
            d_context[p, :, columns] = dot_back(
                d_mid_low[p, :act_height, :], out_tiles[p, columns, :]
            ).astype(BF16)

        tile_loop(model, 256, context_back)

    def scores_back():
        def context_products(rows):
            for index, (p, q) in enumerate(pairs):
                product = d_context[p, rows, :].astype(F32) * qkv_rows[q, rows, 2 * model :].astype(F32)
                halves[2 * index, rows, :], halves[2 * index + 1, rows, :] = split_product(product)

        row_loop(act_height, 16, context_products)
        d_probs = [sums_over_heads(halves, spread, index) for index in range(len(pairs))]
        for p in range(positions):
            own = [index for index, pair in enumerate(pairs) if pair[0] == p]
            mean = functools.reduce(jnp.add, [probs_buf[index] * d_probs[index] for index in own])
            for index in own:
                d_score = (probs_buf[index] * (d_probs[index] - mean)).astype(BF16)
                halves[2 * index] = to_heads(d_score, spread)
                halves[2 * index + 1] = to_heads(probs_buf[index].astype(BF16), spread)

        def plus(total, term):
            return term if total is None else total + term

        def qkv_back(rows):
            d_keys = [None] * positions
            d_values = [None] * positions
            for p in range(positions):
                d_query = None
                d_own = d_context[p, rows, :].astype(F32)
                query = qkv_rows[p, rows, :model].astype(F32)
                for index, (own, q) in enumerate(pairs):
                    if own == p:
                        d_score = halves[2 * index, rows, :].astype(F32)
                        key = qkv_rows[q, rows, model : 2 * model].astype(F32)
                        d_query = plus(d_query, d_score * key)
                        d_keys[q] = plus(d_keys[q], d_score * query)
                        d_values[q] = plus(
                            d_values[q], halves[2 * index + 1, rows, :].astype(F32) * d_own
                        )
                d_qkv[p, rows, :model] = (d_query * scale).astype(BF16)
            for p in range(positions):
                d_qkv[p, rows, model : 2 * model] = (d_keys[p] * scale).astype(BF16)
                d_qkv[p, rows, 2 * model :] = d_values[p].astype(BF16)

        row_loop(act_height, 16, qkv_back)

    def swap_qkv():
        for p in range(positions):
            swap(3, p, d_qkv.at[p, pl.ds(0, act_height)])

    def out_weights(p):
        swap_wait(0, p)
        swap_wait(2, p)

        def tile(columns):
            out_grad[p, :, columns] = dot(
                context_turned[p].reshape(half, 2 * act_height), d_mid_low[p, :, columns]
            ).astype(BF16)

        tile_loop(model, 256, tile)

    def qkv_weights(p):
        swap_wait(1, p)
        swap_wait(3, p)

        def tile(columns):
            qkv_grad[p, :, columns] = dot(
                attn_turned[p].reshape(half, 2 * act_height), d_qkv[p, :, columns]
            ).astype(BF16)

        tile_loop(3 * model, 256, tile)

    def rows_back(p):
        for tile in range(tile_count):
            number = p * tile_count + tile
            qkv_load(number).wait()
            d_rows[p, :, tile * qkv_tile : (tile + 1) * qkv_tile] = dot_back(
                d_qkv[p, :act_height, :], qkv_tiles[number % 2]
            )
            if number + 2 < positions * tile_count:
                qkv_load(number + 2).start()

    def attn_back():
        def norm_one_back(rows):
            values = tokens_ref[rows].astype(F32)
            for p in range(positions):
                r, inverse = normed(values[:, p, :])
                d_attn_in = d_rows[p, rows, :]
                gain_acc[p] += r * d_attn_in
                grad_tokens[rows, p, :] = d_mid[p, rows, :] + norm_back(
                    r, inverse, d_attn_in * gain_rows[p : p + 1, :]
                )

        row_loop(act_height, 16, norm_one_back)
        gains_part[...] = jnp.zeros_like(gains_part)
        for index in range(2 * positions):
            sums = jnp.sum(gain_acc[index], axis=0, keepdims=True)
            for block in range(8):
                gains_part[block, index : index + 1, :] = sums[:, 128 * block : 128 * block + 128]
        lax.fori_loop(1, 32, gains_start, 0)

    def finish_output():
        def finish(rows):
            rounded = [resid_mid[p, rows, :] + act_total(1, p, rows) for p in range(positions)]
            output[rows] = jnp.stack(rounded, axis=1).astype(BF16)

        row_loop(act_height, 16, finish)

    for s in range(sets):
        for turn_number in (0, 1):
            for part in (0, 1, 2):
                part_copy(s, turn_number, part).start()
    for copy in out_loads:
        copy.start()
    act_load(0)
    qkv_load(0).start()
    qkv_load(1).start()
    make_spread(spread)
    gain_acc[...] = jnp.zeros_like(gain_acc)
    kinds = {
        B_TREE: lambda piece, dz, dy, dx: tree_step(piece, (dz, dy, dx)),
        B_RS_ACROSS: rs_across,
        B_RS_FIRST: rs_first,
        B_RS_SECOND: rs_second,
        B_RS_RANK: rs_rank,
        B_RS_LAST: rs_last,
        B_ACT_CORE: act_core,
        B_ACT_LOAD: act_load,
        B_ACT_ADD_X: act_add_x,
        B_ACT_ADD_Z: act_add_z,
        B_ACT_SUM: act_sum,
        B_NORM_TURN: norm_turn,
        B_SWAP_TURNED: swap_turned,
        B_PROBS: find_probs,
        B_MID: mid,
        B_SCORES_BACK: scores_back,
        B_SWAP_QKV: swap_qkv,
        B_OUT_W: out_weights,
        B_QKV_W: qkv_weights,
        B_ROWS_BACK: rows_back,
        B_ATTN_BACK: attn_back,
        B_FINISH_OUTPUT: finish_output,
    }
    for kind, *numbers in BACKWARD_STEPS:
        kinds[kind](*numbers)
    for s in range(sets):
        place_units(own_step, s, share(own_step, s))
    gains_sum[...] = gains_part[lax.div(me, 4)]
    lax.fori_loop(1, 32, gains_wait, 0)
    own_gain = norm_attn_sum.shape[1]
    for index, target in enumerate((norm_attn_sum, norm_ff_sum)):
        picked = jnp.zeros(target.shape, F32)
        for place in range(128 // own_gain):
            picked = picked + jnp.where(
                lax.rem(me, 128 // own_gain) == place,
                gains_sum[
                    index * positions : (index + 1) * positions, place * own_gain : (place + 1) * own_gain
                ],
                0.0,
            )
        target[...] = picked
    for _, _, piece, offset in events:
        if hops(offset) > 0:
            maybe(offset_exists(offset, z), tree_copy(piece, offset).wait_send)
    for copy in sends:
        copy.wait_send()


def backward_scatter(
    tokens,
    grads,
    gain_rows,
    qkv_rows,
    context,
    resid_mid,
    qkv_full,
    out_full,
    out_part,
    back_part,
    gate_up_grad,
    down_grad,
):
    act_height, sets, model = tokens.shape
    width = gate_up_grad.shape[2]
    height = model // 32
    down_height = down_grad.shape[1] // 4
    dma = pltpu.SemaphoreType.DMA
    vmem = pl.BlockSpec(memory_space=pltpu.VMEM)
    anywhere = pl.BlockSpec(memory_space=pl.ANY)
    places = [slot_base(order)[1] for order in ORDERS]
    pair_count = len(pairs_of(sets))
    act = (sets, act_height, model)
    return pl.pallas_call(
        backward_kernel,
        out_shape=(
            jax.ShapeDtypeStruct(tokens.shape, BF16),
            jax.ShapeDtypeStruct(tokens.shape, F32),
            jax.ShapeDtypeStruct((sets, height), F32),
            jax.ShapeDtypeStruct((sets, height), F32),
            jax.ShapeDtypeStruct((sets, height, 3 * model), F32),
            jax.ShapeDtypeStruct((sets, height, model), F32),
            jax.ShapeDtypeStruct((sets, height, 8 * width), F32),
            jax.ShapeDtypeStruct((sets, down_height, model), F32),
        ),
        in_specs=[vmem] * 6 + [anywhere] * 6,
        out_specs=(vmem,) * 8,
        scratch_shapes=[
            pltpu.VMEM((sets, 2, 2, act_height, model), BF16),
            pltpu.VMEM((2, sets, 2, 2, act_height, model), BF16),
            pltpu.VMEM((2, sets, 2, act_height, model), BF16),
            pltpu.VMEM((2, sets, act_height, model), BF16),
            pltpu.VMEM((2, sets, 2, 4 * height, width), BF16),
            pltpu.VMEM((2, sets, down_height, model), BF16),
            pltpu.VMEM((2, sets, 2, 4 * height, width), BF16),
            pltpu.VMEM((2, sets, down_height, model), BF16),
            pltpu.VMEM((sets, 2, 4 * height, width), BF16),
            pltpu.VMEM((sets, down_height, model), BF16),
            pltpu.VMEM((sets, 16 * height, 3 * model), BF16),
            pltpu.VMEM((sets, 16 * height, model), BF16),
            pltpu.VMEM((places[0], height, 3 * model), BF16),
            pltpu.VMEM((places[1], height, 3 * model), BF16),
            pltpu.VMEM((places[2], height, model), BF16),
            pltpu.VMEM((places[3], height, model), BF16),
            pltpu.VMEM((2, 128, 3 * model), BF16),
            pltpu.VMEM((sets, model, model), BF16),
            pltpu.VMEM((2, sets, 16, 2, height, act_height), BF16),
            pltpu.VMEM((sets, 16, height, 2 * act_height), BF16),
            pltpu.VMEM((sets, 16, height, 2 * act_height), BF16),
            pltpu.VMEM((sets, 2 * act_height, 3 * model), BF16),
            pltpu.VMEM((sets, 2 * act_height, model), BF16),
            pltpu.VMEM(act, F32),
            pltpu.VMEM(act, BF16),
            pltpu.VMEM(act, F32),
            pltpu.VMEM((2 * pair_count, act_height, model), BF16),
            pltpu.VMEM((pair_count, act_height, 128), F32),
            pltpu.VMEM((model, 128), BF16),
            pltpu.VMEM((2 * sets, 16, model), F32),
            pltpu.VMEM((8, 8, 128), F32),
            pltpu.VMEM((32, 8, 128), F32),
            pltpu.VMEM((8, 128), F32),
            pltpu.VMEM((8, sets, height, width), BF16),
            dma((2, sets, 2, 2)),
            dma((2, sets, 2, 2)),
            dma((2, sets, 2)),
            dma((2, sets, 2)),
            dma((2, sets)),
            dma((2, sets)),
            dma((2, sets, 3)),
            dma((2, sets, 3)),
            dma((sets, 3)),
            dma((sets, 3)),
            dma((8, sets)),
            dma((8, sets)),
            dma((4 * sets,)),
            dma((4 * sets,)),
            dma((4, 16)),
            dma((4, max(places))),
            dma((32,)),
            dma((32,)),
            dma((2, sets, 2, 2)),
            dma((2, sets, 3)),
            dma((2 + sets,)),
        ],
        compiler_params=pltpu.CompilerParams(
            collective_id=5, has_side_effects=True, vmem_limit_bytes=63 * 2**20
        ),
        name="backward_scatter",
    )(
        tokens,
        grads,
        gain_rows,
        qkv_rows,
        context,
        resid_mid,
        qkv_full,
        out_full,
        out_part,
        back_part,
        gate_up_grad,
        down_grad,
    )


def settle_kernel(*refs):
    count = len(refs) // 2
    sems = refs[-1]
    copies = [
        pltpu.make_async_copy(refs[index], refs[count + index], sems.at[index]) for index in range(count)
    ]
    for copy in copies:
        copy.start()
    for copy in copies:
        copy.wait()


def settle(arrays):
    anywhere = pl.BlockSpec(memory_space=pl.ANY)
    return pl.pallas_call(
        settle_kernel,
        out_shape=tuple(jax.ShapeDtypeStruct(array.shape, array.dtype) for array in arrays),
        in_specs=[pl.BlockSpec(memory_space=pltpu.VMEM)] * len(arrays),
        out_specs=(anywhere,) * len(arrays),
        scratch_shapes=[pltpu.SemaphoreType.DMA((len(arrays),))],
        name="settle",
    )(*arrays)


def local_fast(
    tokens,
    norm_attn,
    w_qkv,
    w_out,
    norm_ff,
    w_gate_up,
    w_down,
    cotangent,
    valid_frames,
    item_lengths,
):
    (
        gain_rows,
        cot_rows,
        qkv_rows,
        context,
        resid_mid,
        qkv_full,
        out_full,
        out_part,
        back_part,
        gate_up_grad,
        down_grad,
    ) = forward_gather(
        valid_frames,
        item_lengths,
        norm_attn,
        norm_ff,
        tokens,
        cotangent,
        w_qkv,
        w_out,
        w_gate_up,
        w_down,
    )
    (
        output,
        grad_tokens,
        share_norm_attn,
        share_norm_ff,
        share_qkv,
        share_out,
        share_gate_up,
        share_down,
    ) = settle(backward_scatter(
        tokens,
        cot_rows,
        gain_rows,
        qkv_rows,
        context,
        resid_mid,
        qkv_full,
        out_full,
        out_part,
        back_part,
        gate_up_grad,
        down_grad,
    ))
    return (
        output,
        grad_tokens,
        share_norm_attn,
        share_qkv,
        share_out,
        share_norm_ff,
        share_gate_up,
        share_down,
    )


def solution(mesh):
    in_specs = (
        P(("dp", "pair"), None, None),
        P(None, ("dp", "pair")),
        P(None, ("dp", "pair"), None),
        P(None, ("dp", "pair"), None),
        P(None, ("dp", "pair")),
        P(None, ("dp", "pair"), None),
        P(None, ("dp", "pair"), None),
        P(("dp", "pair"), None, None),
        P(("dp", "pair")),
        P(),
    )
    out_specs = (
        P(("dp", "pair"), None, None),
        P(("dp", "pair"), None, None),
        P(None, ("dp", "pair")),
        P(None, ("dp", "pair"), None),
        P(None, ("dp", "pair"), None),
        P(None, ("dp", "pair")),
        P(None, ("dp", "pair"), None),
        P(None, ("dp", "pair"), None),
    )
    body = local_fast if mesh.shape["dp"] == 16 and mesh.shape["pair"] == 2 else local
    return jax.shard_map(body, mesh=mesh, in_specs=in_specs, out_specs=out_specs, check_vma=False)
```

```python
import functools
import math

import jax
import jax.numpy as jnp
from jax import lax
from jax.experimental import pallas as pl
from jax.experimental.pallas import tpu as pltpu
from jax.sharding import PartitionSpec as P

HEAD_DIM = 64


def per_pos(activations, weight):
    return jnp.einsum("fgk,gke->fge", activations, weight, preferred_element_type=jnp.float32)


def per_pos_back(gradients, weight):
    return jnp.einsum("fge,gke->fgk", gradients, weight, preferred_element_type=jnp.float32)


def pos_grad(activations, gradients):
    return jnp.einsum("fgk,fge->kge", activations, gradients, preferred_element_type=jnp.float32)


def gain_grad(normed_rows, gradients):
    return jnp.transpose(jnp.sum(normed_rows * gradients, axis=0))


def back_layout(share):
    return jnp.swapaxes(share, 0, 1)


def normed(values):
    inverse = lax.rsqrt(jnp.mean(values * values, axis=-1, keepdims=True) + 1e-05)
    return (values * inverse, inverse)


def norm_back(normed_rows, inverse, gradients):
    return inverse * (
        gradients - normed_rows * jnp.mean(gradients * normed_rows, axis=-1, keepdims=True)
    )


def gather_ff_fwd(norm_ff, w_gate_up, w_down, start, group):
    return (
        lax.all_gather(norm_ff[start : start + group], ("dp", "pair"), axis=1, tiled=True),
        lax.all_gather(w_gate_up[start : start + group], ("dp", "pair"), axis=1, tiled=True),
        lax.all_gather(w_down[start : start + group], ("dp", "pair"), axis=1, tiled=True),
    )


def gather_ff_back(norm_ff, w_gate_up, w_down, start, group):
    return (
        lax.all_gather(norm_ff[start : start + group], ("dp", "pair"), axis=1, tiled=True),
        lax.all_gather(w_gate_up[start : start + group], ("dp", "pair"), axis=1, tiled=True),
        lax.all_gather(w_down[start : start + group], ("dp", "pair"), axis=1, tiled=True),
    )


def local(
    tokens,
    norm_attn,
    w_qkv,
    w_out,
    norm_ff,
    w_gate_up,
    w_down,
    cotangent,
    valid_frames,
    item_lengths,
):
    frame_count, positions, model_width = tokens.shape
    head_count = model_width // HEAD_DIM
    ff_units = w_gate_up.shape[2] // 2
    score_scale = 1.0 / math.sqrt(HEAD_DIM)
    causal = jnp.arange(positions)[:, None] >= jnp.arange(positions)[None, :]
    head_shape = (frame_count, positions, head_count, HEAD_DIM)
    group = 1
    gains_attn, qkv_full, out_full = (
        lax.all_gather(norm_attn, ("dp", "pair"), axis=1, tiled=True),
        lax.all_gather(w_qkv, ("dp", "pair"), axis=1, tiled=True),
        lax.all_gather(w_out, ("dp", "pair"), axis=1, tiled=True),
    )
    resid_in = tokens.astype(jnp.float32)
    normed_one, inverse_one = normed(resid_in)
    attn_in = (normed_one * gains_attn.astype(jnp.float32)[None]).astype(jnp.bfloat16)
    qkv_rows = per_pos(attn_in, qkv_full).astype(jnp.bfloat16)
    queries = qkv_rows[..., :model_width].reshape(head_shape)
    key_heads = qkv_rows[..., model_width : 2 * model_width].reshape(head_shape)
    value_heads = qkv_rows[..., 2 * model_width :].reshape(head_shape)
    scores = (
        jnp.einsum("fphd,fqhd->fhpq", queries, key_heads, preferred_element_type=jnp.float32)
        * score_scale
    )
    scores = jnp.where(causal, scores, -1e30)
    row_max = jnp.max(scores, axis=-1, keepdims=True)
    attn_probs = jnp.exp(scores - row_max)
    attn_probs = attn_probs / jnp.sum(attn_probs, axis=-1, keepdims=True)
    probs_low = attn_probs.astype(jnp.bfloat16)
    context = jnp.einsum(
        "fhpq,fqhd->fphd", probs_low, value_heads, preferred_element_type=jnp.float32
    )
    context = context.astype(jnp.bfloat16).reshape(frame_count, positions, model_width)
    resid_mid = resid_in + per_pos(context, out_full)
    kept_parts = []
    out_parts = []
    for start in range(0, positions, group):
        gains_ff, gate_up_full, down_full = gather_ff_fwd(norm_ff, w_gate_up, w_down, start, group)
        mid_part = resid_mid[:, start : start + group]
        normed_two, inverse_two = normed(mid_part)
        ff_in = (normed_two * gains_ff.astype(jnp.float32)[None]).astype(jnp.bfloat16)
        gate_up = per_pos(ff_in, gate_up_full)
        gate_part = gate_up[..., :ff_units]
        up_part = gate_up[..., ff_units:]
        sigmoid_gate = jax.nn.sigmoid(gate_part)
        silu_gate = gate_part * sigmoid_gate
        hidden = (silu_gate * up_part).astype(jnp.bfloat16)
        out_parts.append(mid_part + per_pos(hidden, down_full))
        kept_parts.append(
            (normed_two, inverse_two, ff_in, gate_part, up_part, sigmoid_gate, silu_gate, hidden)
        )
    output = jnp.concatenate(out_parts, axis=1).astype(jnp.bfloat16)
    device_index = lax.axis_index(("dp", "pair"))
    local_ids = jnp.arange(frame_count, dtype=jnp.int32)
    frame_ids = device_index * frame_count + local_ids
    item_ends = jnp.cumsum(item_lengths)
    item_starts = item_ends - item_lengths
    in_item = (frame_ids[:, None] >= item_starts[None, :]) & (
        frame_ids[:, None] < item_ends[None, :]
    )
    item_share = 8 * frame_count / item_lengths.astype(jnp.float32)
    frame_weight = jnp.sum(jnp.where(in_item, item_share[None, :], 0.0), axis=1)
    frame_weight = jnp.where(local_ids < valid_frames[0], frame_weight, 0.0)
    grad_out = cotangent.astype(jnp.float32) * frame_weight[:, None, None]
    mid_grads = []
    share_norm_ff_parts = []
    share_gate_up_parts = []
    share_down_parts = []
    for index, start in enumerate(range(0, positions, group)):
        normed_two, inverse_two, ff_in, gate_part, up_part, sigmoid_gate, silu_gate, hidden = (
            kept_parts[index]
        )
        gains_ff, gate_up_full, down_full = gather_ff_back(norm_ff, w_gate_up, w_down, start, group)
        grad_part = grad_out[:, start : start + group]
        grad_low = grad_part.astype(jnp.bfloat16)
        grad_down = pos_grad(hidden, grad_low)
        d_hidden = per_pos_back(grad_low, down_full)
        d_gate = d_hidden * up_part * sigmoid_gate * (1.0 + gate_part * (1.0 - sigmoid_gate))
        d_up = d_hidden * silu_gate
        d_gate_up = jnp.concatenate([d_gate, d_up], axis=-1).astype(jnp.bfloat16)
        grad_gate_up = pos_grad(ff_in, d_gate_up)
        d_ff_in = per_pos_back(d_gate_up, gate_up_full)
        grad_norm_ff = gain_grad(normed_two, d_ff_in)
        mid_grads.append(
            grad_part
            + norm_back(normed_two, inverse_two, d_ff_in * gains_ff.astype(jnp.float32)[None])
        )
        share_a, share_b, share_c = (
            lax.psum_scatter(grad_norm_ff, ("dp", "pair"), scatter_dimension=0, tiled=True),
            lax.psum_scatter(grad_gate_up, ("dp", "pair"), scatter_dimension=0, tiled=True),
            lax.psum_scatter(grad_down, ("dp", "pair"), scatter_dimension=0, tiled=True),
        )
        share_norm_ff_parts.append(jnp.transpose(share_a))
        share_gate_up_parts.append(back_layout(share_b))
        share_down_parts.append(back_layout(share_c))
    d_mid = jnp.concatenate(mid_grads, axis=1)
    gains_attn, qkv_full, out_full = (
        lax.all_gather(norm_attn, ("dp", "pair"), axis=1, tiled=True),
        lax.all_gather(w_qkv, ("dp", "pair"), axis=1, tiled=True),
        lax.all_gather(w_out, ("dp", "pair"), axis=1, tiled=True),
    )
    d_mid_low = d_mid.astype(jnp.bfloat16)
    grad_out_proj = pos_grad(context, d_mid_low)
    d_context = per_pos_back(d_mid_low, out_full).astype(jnp.bfloat16).reshape(head_shape)
    d_probs = jnp.einsum(
        "fphd,fqhd->fhpq", d_context, value_heads, preferred_element_type=jnp.float32
    )
    d_values = jnp.einsum(
        "fhpq,fphd->fqhd", probs_low, d_context, preferred_element_type=jnp.float32
    )
    d_scores = attn_probs * (d_probs - jnp.sum(attn_probs * d_probs, axis=-1, keepdims=True))
    d_scores = d_scores.astype(jnp.bfloat16)
    d_queries = (
        jnp.einsum("fhpq,fqhd->fphd", d_scores, key_heads, preferred_element_type=jnp.float32)
        * score_scale
    )
    d_keys = (
        jnp.einsum("fhpq,fphd->fqhd", d_scores, queries, preferred_element_type=jnp.float32)
        * score_scale
    )
    row_shape = (frame_count, positions, model_width)
    d_qkv = jnp.concatenate(
        [d_queries.reshape(row_shape), d_keys.reshape(row_shape), d_values.reshape(row_shape)],
        axis=-1,
    ).astype(jnp.bfloat16)
    grad_qkv = pos_grad(attn_in, d_qkv)
    d_attn_in = per_pos_back(d_qkv, qkv_full)
    grad_norm_attn = gain_grad(normed_one, d_attn_in)
    grad_tokens = d_mid + norm_back(
        normed_one, inverse_one, d_attn_in * gains_attn.astype(jnp.float32)[None]
    )
    share_norm_attn, share_qkv, share_out = (
        lax.psum_scatter(grad_norm_attn, ("dp", "pair"), scatter_dimension=0, tiled=True),
        lax.psum_scatter(grad_qkv, ("dp", "pair"), scatter_dimension=0, tiled=True),
        lax.psum_scatter(grad_out_proj, ("dp", "pair"), scatter_dimension=0, tiled=True),
    )
    share_norm_attn = jnp.transpose(share_norm_attn)
    share_qkv = back_layout(share_qkv)
    share_out = back_layout(share_out)
    share_norm_ff = jnp.concatenate(share_norm_ff_parts, axis=0)
    share_gate_up = jnp.concatenate(share_gate_up_parts, axis=0)
    share_down = jnp.concatenate(share_down_parts, axis=0)
    return (
        output,
        grad_tokens,
        share_norm_attn,
        share_qkv,
        share_out,
        share_norm_ff,
        share_gate_up,
        share_down,
    )


MESH_ID = pl.DeviceIdType.MESH
BF16 = jnp.bfloat16
F32 = jnp.float32


def here():
    dp = lax.axis_index("dp")
    core = lax.axis_index("pair")
    return lax.div(dp, 4), lax.rem(lax.div(dp, 2), 2), lax.rem(dp, 2), core


def flip(value, bit):
    return 1 - value if bit else value


def push(src, dst, send_sem, recv_sem, to):
    return pltpu.make_async_remote_copy(
        src_ref=src,
        dst_ref=dst,
        send_sem=send_sem,
        recv_sem=recv_sem,
        device_id=to,
        device_id_type=MESH_ID,
    )


def arrived(dst, recv_sem, to):
    push(dst, dst, recv_sem, recv_sem, to).wait_recv()


def greet_all(z, y, x, core):
    barrier = pltpu.get_barrier_semaphore()
    me = 2 * (z * 4 + y * 2 + x) + core

    def one(step, carry):
        other = lax.rem(me + step, 32)
        pl.semaphore_signal(
            barrier, inc=1, device_id=(lax.div(other, 2), lax.rem(other, 2)), device_id_type=MESH_ID
        )
        return carry

    lax.fori_loop(1, 32, one, 0)
    pl.semaphore_wait(barrier, 31)


def greet(peers):
    barrier = pltpu.get_barrier_semaphore()
    for to in peers:
        pl.semaphore_signal(barrier, inc=1, device_id=to, device_id_type=MESH_ID)
    pl.semaphore_wait(barrier, len(peers))


def maybe(condition, do):
    if condition is None:
        do()
    else:
        pl.when(condition)(do)


OFFSETS = [
    (dz, dy, dx) for dz in (0, -1, 1, -2, 2, -3, 3) for dy in (0, 1) for dx in (0, 1)
]
ORDERS = ("zxy", "zyx", "xyz", "yxz")


def hops(offset):
    return abs(offset[0]) + offset[1] + offset[2]


def arrival_axis(order, offset):
    part = dict(z=offset[0], y=offset[1], x=offset[2])
    last = None
    for axis in order:
        if part[axis] != 0:
            last = axis
    return last


def onward(order, offset):
    directions = []
    last = arrival_axis(order, offset)
    start = 0
    if last is not None:
        start = order.index(last) + 1
        if last == "z":
            directions.append("u" if offset[0] < 0 else "d")
    for axis in order[start:]:
        directions.extend(["u", "d"] if axis == "z" else [axis])
    return directions


def came_from(order, offset):
    last = arrival_axis(order, offset)
    if last == "z":
        return "d" if offset[0] < 0 else "u"
    return last


def offset_exists(offset, z):
    if offset[0] < 0:
        return z >= -offset[0]
    if offset[0] > 0:
        return z <= 3 - offset[0]
    return None


def direction_exists(direction, z):
    return {"u": z < 3, "d": z > 0}.get(direction)


def return_count(order, direction, level):
    return sum(
        hops(offset) > 0 and came_from(order, offset) == direction
        for offset in OFFSETS
        if 0 <= level + offset[0] <= 3
    )


def tree_count(order, direction, level):
    return sum(
        direction in onward(order, offset) for offset in OFFSETS if 0 <= level + offset[0] <= 3
    )


DIRECTIONS = ("x", "y", "u", "d", "s")


def neighbour(direction, z, y, x, core):
    if direction == "x":
        return (z * 4 + y * 2 + 1 - x, core)
    if direction == "y":
        return (z * 4 + (1 - y) * 2 + x, core)
    if direction == "u":
        return (z * 4 + 4 + y * 2 + x, core)
    if direction == "d":
        return (z * 4 - 4 + y * 2 + x, core)
    return (z * 4 + y * 2 + x, 1 - core)


def chip_of(offset, z, y, x):
    return (z + offset[0]) * 4 + flip(y, offset[1]) * 2 + flip(x, offset[2])


RANK_STEPS = sorted(
    ((dl, dx, dc) for dl in (0, 1) for dx in (0, 1) for dc in (0, 1)), key=lambda step: (sum(step), step)
)


def group_place(z, y, x, core):
    zh, zl = lax.div(z, 2), lax.rem(z, 2)

    def member(step):
        return ((2 * zh + flip(zl, step[0])) * 4 + y * 2 + flip(x, step[1]), flip(core, step[2]))

    def rank(step):
        return 4 * flip(zl, step[0]) + 2 * flip(x, step[1]) + flip(core, step[2])

    def device(step, dzh=0, dy=0):
        return 16 * flip(zh, dzh) + 4 * flip(y, dy) + 8 * flip(zl, step[0]) + 2 * flip(x, step[1]) + flip(core, step[2])

    far = ((2 * (1 - zh) + zl) * 4 + y * 2 + x, core)
    across = (z * 4 + (1 - y) * 2 + x, core)
    return zh, zl, member, rank, device, far, across


def add_into(target, sources, rows=16, columns=1024):
    height, width = target.shape
    across = width // columns

    def one(step, carry):
        top = pl.multiple_of(lax.div(step, across) * rows, rows)
        left = pl.multiple_of(lax.rem(step, across) * columns, columns)
        spot = (pl.ds(top, rows), pl.ds(left, columns))
        total = sources[0][spot].astype(F32)
        for source in sources[1:]:
            total = total + source[spot].astype(F32)
        target[spot] = total.astype(target.dtype)
        return carry

    lax.fori_loop(0, (height // rows) * across, one, 0)


def row_loop(height, chunk, body):
    def one(step, carry):
        body(pl.ds(pl.multiple_of(step * chunk, chunk), chunk))
        return carry

    lax.fori_loop(0, height // chunk, one, 0)


def tile_loop(width, tile, body):
    def one(step, carry):
        body(pl.ds(pl.multiple_of(step * tile, tile), tile))
        return carry

    lax.fori_loop(0, width // tile, one, 0)


def dot(left, right):
    return jnp.dot(left, right, preferred_element_type=F32)


def dot_back(left, right):
    return lax.dot_general(left, right, (((1,), (1,)), ((), ())), preferred_element_type=F32)


def dot_grad(left, right):
    return lax.dot_general(left, right, (((0,), (0,)), ((), ())), preferred_element_type=F32)


def make_spread(spread):
    height, width = spread.shape
    head = lax.broadcasted_iota(jnp.int32, (height, width), 0) // HEAD_DIM
    spread[...] = jnp.where(
        head == lax.broadcasted_iota(jnp.int32, (height, width), 1), 1.0, 0.0
    ).astype(BF16)


def pairs_of(positions):
    return [(p, q) for p in range(positions) for q in range(p + 1)]


def split_product(product):
    high = product.astype(BF16)
    return high, (product - high.astype(F32)).astype(BF16)


def sums_over_heads(halves, spread, index):
    return dot(halves[2 * index], spread[...]) + dot(halves[2 * index + 1], spread[...])


def to_heads(values, spread):
    return dot_back(values, spread[...]).astype(BF16)


def attention_probs(qkv, halves, spread, model, position):
    height = qkv.shape[1]
    scale = 1.0 / math.sqrt(HEAD_DIM)

    def products(rows):
        for q in range(position + 1):
            product = qkv[position, rows, :model].astype(F32) * qkv[
                q, rows, model : 2 * model
            ].astype(F32)
            halves[2 * q, rows, :], halves[2 * q + 1, rows, :] = split_product(product)

    row_loop(height, 16, products)
    scores = [sums_over_heads(halves, spread, q) * scale for q in range(position + 1)]
    top = functools.reduce(jnp.maximum, scores)
    powers = [jnp.exp(score - top) for score in scores]
    total = functools.reduce(jnp.add, powers)
    return [power / total for power in powers]


(
    F_TREE,
    F_TREE_END,
    F_GAINS,
    F_PARTS,
    F_COT,
    F_ATTENTION,
    F_GRADS,
    F_ACT_Z,
    F_ACT_X,
    F_ACT_C,
    F_TO_RANK,
    F_OWN_FAR,
    F_OWN_ACROSS,
    F_RANK_FAR,
    F_RANK_ACROSS,
    F_FAR_ACROSS,
    F_FF_END,
    F_BLOCK,
    F_GATE_GRAD,
    F_DOWN_GRAD,
) = range(20)
FORWARD_STEPS = [
    (F_TREE, 3, 0, 0, 0), (F_TREE, 5, 0, 0, 0), (F_TREE, 0, 0, 0, 0), (F_TREE, 2, 0, 0, 0),
    (F_TREE, 5, 1, 0, 0), (F_PARTS,), (F_TO_RANK, 0, 7), (F_TREE, 0, -1, 0, 0), (F_TREE, 0, 0, 0, 1),
    (F_TO_RANK, 0, 3), (F_TREE, 2, 0, 0, 1), (F_TREE, 1, 0, 0, 0), (F_TREE, 0, -2, 0, 0), (F_COT,),
    (F_RANK_FAR, 0, 3), (F_TREE, 0, 0, 1, 0), (F_TREE, 4, 0, 0, 0), (F_TO_RANK, 1, 4), (F_TREE, 1, -1, 0, 0),
    (F_TO_RANK, 0, 2), (F_TO_RANK, 1, 2), (F_TREE, 2, 0, 1, 1), (F_TREE, 0, 1, 0, 0), (F_TREE, 2, 0, 1, 0),
    (F_OWN_ACROSS, 0, 0), (F_TREE, 1, 1, 0, 0), (F_TREE, 2, -1, 0, 0), (F_TREE, 0, -1, 0, 1),
    (F_TREE, 0, -3, 0, 0), (F_TO_RANK, 0, 1), (F_TREE, 0, -2, 0, 1), (F_TREE, 1, 0, 1, 0), (F_TREE, 2, 1, 0, 1),
    (F_TREE, 0, 2, 0, 0), (F_GRADS, 0), (F_TO_RANK, 0, 6), (F_RANK_FAR, 0, 1), (F_OWN_ACROSS, 1, 8),
    (F_TREE, 2, -2, 0, 0), (F_OWN_ACROSS, 0, 8), (F_TREE, 2, -1, 1, 0), (F_TO_RANK, 0, 5), (F_RANK_FAR, 0, 2),
    (F_TREE, 3, 0, 0, 1), (F_OWN_FAR, 0, 8), (F_TREE, 1, -1, 1, 0), (F_TREE, 2, -1, 1, 1), (F_FAR_ACROSS, 0, 2),
    (F_RANK_FAR, 0, 6), (F_TREE, 3, 0, 1, 1), (F_GAINS,), (F_TREE, 2, 1, 0, 0), (F_TREE, 1, 2, 0, 0),
    (F_RANK_ACROSS, 0, 3), (F_TREE, 1, -2, 0, 0), (F_TREE, 0, 3, 0, 0), (F_TREE, 2, 1, 1, 1),
    (F_TREE, 5, 0, 0, 1), (F_TREE, 2, 2, 0, 0), (F_TO_RANK, 0, 4), (F_TREE, 1, 2, 1, 0), (F_TREE, 3, -1, 0, 0),
    (F_TREE, 4, 1, 0, 0), (F_TREE, 0, -1, 1, 1), (F_TREE, 0, 2, 0, 1), (F_RANK_FAR, 0, 7), (F_RANK_FAR, 0, 4),
    (F_FAR_ACROSS, 0, 3), (F_TREE, 2, 2, 1, 1), (F_TREE, 1, 3, 0, 0), (F_TREE, 1, 1, 1, 0),
    (F_RANK_ACROSS, 0, 1), (F_TO_RANK, 1, 6), (F_TREE, 2, -3, 0, 0), (F_TREE, 0, -3, 0, 1),
    (F_TREE, 0, 0, 1, 1), (F_TREE, 1, 2, 0, 1), (F_TREE, 2, 1, 1, 0), (F_TREE, 2, -1, 0, 1),
    (F_TREE, 1, 0, 1, 1), (F_TREE, 2, -2, 1, 0), (F_TREE, 2, 3, 1, 1), (F_FAR_ACROSS, 0, 6), (F_OWN_FAR, 0, 0),
    (F_TREE, 1, -2, 0, 1), (F_TREE, 0, 2, 1, 1), (F_TREE, 4, 2, 0, 0), (F_TREE, 1, 3, 0, 1),
    (F_TREE, 3, 1, 0, 0), (F_TREE, 2, -2, 1, 1), (F_RANK_FAR, 0, 5), (F_TREE, 0, -2, 1, 1),
    (F_TREE, 0, 1, 1, 0), (F_TREE, 5, 0, 1, 0), (F_FAR_ACROSS, 0, 1), (F_TREE, 1, -2, 1, 0),
    (F_TREE, 1, 2, 1, 1), (F_TREE, 2, 2, 1, 0), (F_TREE, 1, -3, 0, 0), (F_TO_RANK, 1, 5), (F_TREE, 0, -1, 1, 0),
    (F_TREE, 3, -2, 0, 0), (F_TREE, 1, 3, 1, 0), (F_ACT_Z, 1, 0), (F_TREE, 0, 1, 0, 1), (F_TREE, 3, 1, 0, 1),
    (F_TREE, 2, 2, 0, 1), (F_TREE, 0, 3, 1, 0), (F_TREE, 4, -1, 0, 0), (F_TREE, 2, -2, 0, 1),
    (F_TREE, 2, -3, 1, 1), (F_TREE, 0, -3, 1, 1), (F_FAR_ACROSS, 0, 7), (F_TREE, 0, -3, 1, 0),
    (F_TREE, 0, 2, 1, 0), (F_TREE, 3, 1, 1, 0), (F_TREE, 2, -3, 1, 0), (F_TREE, 1, -1, 0, 1),
    (F_TREE, 1, -3, 1, 0), (F_RANK_ACROSS, 0, 7), (F_FAR_ACROSS, 0, 0), (F_TREE, 1, 3, 1, 1),
    (F_TREE, 3, 2, 0, 0), (F_TREE, 2, 3, 0, 0), (F_RANK_ACROSS, 0, 6), (F_TREE, 5, 1, 1, 0),
    (F_TREE, 0, 3, 0, 1), (F_TREE, 1, -3, 0, 1), (F_TREE, 3, -2, 0, 1), (F_ACT_C, 1, 0, 0, 0),
    (F_TREE, 4, 0, 1, 0), (F_TREE, 5, 0, 1, 1), (F_TREE, 4, -2, 0, 0), (F_FAR_ACROSS, 0, 4), (F_GRADS, 1),
    (F_TREE, 2, -3, 0, 1), (F_TREE, 5, -1, 1, 0), (F_TREE, 1, -3, 1, 1), (F_ACT_C, 1, 0, 1, 0),
    (F_FAR_ACROSS, 0, 8), (F_TREE, 5, 1, 0, 1), (F_FAR_ACROSS, 0, 5), (F_TREE, 1, -1, 1, 1),
    (F_TREE, 1, 0, 0, 1), (F_RANK_ACROSS, 0, 5), (F_TREE, 5, -1, 0, 0), (F_TREE, 3, -3, 0, 0),
    (F_TO_RANK, 1, 1), (F_ACT_X, 1, 0, 1), (F_TREE, 1, 1, 0, 1), (F_TREE, 5, 2, 1, 0), (F_OWN_FAR, 1, 8),
    (F_ACT_X, 1, 0, 0), (F_TREE, 5, -1, 0, 1), (F_TREE, 4, -3, 0, 0), (F_TREE, 0, 1, 1, 1),
    (F_TREE, 1, 1, 1, 1), (F_TREE, 2, 3, 0, 1), (F_TREE, 3, 1, 1, 1), (F_TREE, 3, -1, 0, 1),
    (F_TREE, 4, -1, 1, 0), (F_TREE, 3, -3, 0, 1), (F_TREE, 3, 2, 0, 1), (F_OWN_ACROSS, 1, 0),
    (F_TREE, 1, -2, 1, 1), (F_TO_RANK, 1, 3), (F_TREE, 3, 0, 1, 0), (F_TREE, 0, 3, 1, 1), (F_TREE, 0, -2, 1, 0),
    (F_TREE, 3, 2, 1, 0), (F_TREE, 2, 3, 1, 0), (F_TREE, 3, 3, 0, 0), (F_TREE_END, 0), (F_TREE, 4, -1, 1, 1),
    (F_TO_RANK, 1, 7), (F_ATTENTION, 0), (F_TREE, 4, 3, 0, 0), (F_ACT_X, 0, 0, 0), (F_TREE, 4, 3, 1, 0),
    (F_TREE, 3, -3, 1, 0), (F_TREE, 4, 3, 0, 1), (F_TREE, 4, -2, 1, 0), (F_TREE, 3, 3, 0, 1),
    (F_TREE, 5, -1, 1, 1), (F_RANK_FAR, 1, 7), (F_RANK_ACROSS, 0, 2), (F_TREE, 4, 2, 1, 0),
    (F_TREE, 5, 1, 1, 1), (F_TREE, 5, 3, 1, 0), (F_TREE, 4, -3, 0, 1), (F_RANK_ACROSS, 0, 4),
    (F_TREE, 4, -3, 1, 0), (F_OWN_FAR, 1, 0), (F_RANK_FAR, 1, 2), (F_TREE, 4, 3, 1, 1), (F_RANK_ACROSS, 1, 7),
    (F_FAR_ACROSS, 1, 8), (F_TREE, 4, 1, 1, 0), (F_ACT_Z, 1, 1), (F_TREE, 5, -2, 0, 1), (F_TREE, 4, -3, 1, 1),
    (F_TREE, 3, 2, 1, 1), (F_TREE, 5, -2, 0, 0), (F_ACT_Z, 0, 0), (F_TREE, 4, 2, 1, 1), (F_TREE, 5, 2, 0, 0),
    (F_RANK_FAR, 1, 1), (F_FF_END, 0), (F_ACT_C, 0, 0, 1, 0), (F_RANK_ACROSS, 1, 2), (F_TREE, 4, 0, 0, 1),
    (F_TREE, 4, 1, 1, 1), (F_RANK_FAR, 1, 5), (F_ACT_X, 1, 1, 0), (F_TREE, 3, -1, 1, 0), (F_TREE, 5, 2, 1, 1),
    (F_TREE, 5, 3, 0, 0), (F_FAR_ACROSS, 1, 7), (F_TREE, 3, 3, 1, 1), (F_TREE, 3, -1, 1, 1),
    (F_TREE, 4, -2, 1, 1), (F_ACT_C, 1, 0, 0, 1), (F_ACT_C, 0, 0, 0, 0), (F_TREE, 4, 0, 1, 1),
    (F_RANK_FAR, 1, 3), (F_ACT_C, 1, 0, 1, 1), (F_TREE, 3, -2, 1, 0), (F_TREE, 5, -2, 1, 0), (F_RANK_FAR, 1, 4),
    (F_FAR_ACROSS, 1, 0), (F_TREE, 5, -3, 0, 0), (F_TREE, 4, 1, 0, 1), (F_TREE, 3, -2, 1, 1),
    (F_ACT_C, 1, 1, 1, 0), (F_RANK_FAR, 1, 6), (F_TREE, 4, -1, 0, 1), (F_TREE, 5, 2, 0, 1),
    (F_TREE, 5, -3, 1, 0), (F_ACT_C, 0, 0, 0, 1), (F_FAR_ACROSS, 1, 2), (F_ACT_C, 1, 1, 0, 0),
    (F_TREE, 5, -3, 0, 1), (F_TREE, 5, -2, 1, 1), (F_TREE, 3, 3, 1, 0), (F_RANK_ACROSS, 1, 6),
    (F_RANK_ACROSS, 1, 3), (F_TREE, 5, 3, 1, 1), (F_RANK_ACROSS, 1, 4), (F_BLOCK, 0, 1), (F_TREE, 4, 2, 0, 1),
    (F_TREE, 5, 3, 0, 1), (F_TREE, 4, -2, 0, 1), (F_TREE, 3, -3, 1, 1), (F_FAR_ACROSS, 1, 1),
    (F_TREE, 5, -3, 1, 1), (F_BLOCK, 0, 0), (F_RANK_ACROSS, 1, 5), (F_ACT_X, 1, 1, 1), (F_TREE_END, 1),
    (F_ATTENTION, 1), (F_FAR_ACROSS, 1, 3), (F_RANK_ACROSS, 1, 1), (F_ACT_X, 0, 0, 1), (F_BLOCK, 0, 2),
    (F_FAR_ACROSS, 1, 5), (F_ACT_C, 0, 0, 1, 1), (F_BLOCK, 0, 3), (F_DOWN_GRAD, 0), (F_ACT_C, 1, 1, 0, 1),
    (F_FAR_ACROSS, 1, 6), (F_ACT_X, 0, 1, 0), (F_ACT_C, 1, 1, 1, 1), (F_ACT_Z, 0, 1), (F_FAR_ACROSS, 1, 4),
    (F_GATE_GRAD, 0), (F_ACT_C, 0, 1, 0, 1), (F_ACT_C, 0, 1, 0, 0), (F_FF_END, 1), (F_ACT_C, 0, 1, 1, 0),
    (F_BLOCK, 1, 1), (F_BLOCK, 1, 2), (F_ACT_X, 0, 1, 1), (F_BLOCK, 1, 0), (F_ACT_C, 0, 1, 1, 1),
    (F_BLOCK, 1, 3), (F_DOWN_GRAD, 1), (F_GATE_GRAD, 1),
]


def forward_kernel(
    valid_ref,
    lengths_ref,
    norm_attn_ref,
    norm_ff_ref,
    tokens_ref,
    cot_ref,
    qkv_ref,
    out_ref,
    gate_up_ref,
    down_ref,
    gain_rows,
    cot_rows,
    qkv_rows,
    context,
    resid_mid,
    qkv_full,
    out_full,
    ff_out,
    ff_back,
    gate_up_grad,
    down_grad,
    qkv_buf,
    out_buf,
    gate_up_buf,
    down_buf,
    rows_buf,
    grads_buf,
    hidden,
    d_gate_up,
    out_stage,
    back_stage,
    gate_up_stage,
    down_stage,
    gains_own,
    gains_all,
    gate_up_raw,
    gate_up_parts,
    grads_own,
    attn_in,
    halves,
    spread,
    plane_sem,
    sibling_sem,
    send_sem,
    gains_send,
    gains_recv,
    rank_send,
    rank_recv,
    far_send,
    far_recv,
    across_send,
    across_recv,
    act_send,
    act_recv,
    local_sem,
    keep_sem,
    stage_sem,
):
    z, y, x, core = here()
    me = 2 * (z * 4 + y * 2 + x) + core
    zh, zl, member, rank, device, far, across = group_place(z, y, x, core)
    own_step = (0, 0, 0)
    act_height, positions, model = tokens_ref.shape
    height = gate_up_ref.shape[1]
    down_height = down_ref.shape[1]
    split = 4 * down_height
    sibling = neighbour("s", z, y, x, core)
    greet_all(z, y, x, core)
    part = qkv_ref.shape[2] // 2
    pieces = []
    for s in range(positions):
        pieces.append((qkv_ref, qkv_buf, s, pl.ds(0, part), "zxy"))
        pieces.append((qkv_ref, qkv_buf, s, pl.ds(part, part), "zyx"))
        pieces.append((out_ref, out_buf, s, pl.ds(0, model), ("xyz", "yxz")[s % 2]))

    def piece_rows(piece, number):
        _, full, index, columns, _ = pieces[piece]
        return full.at[index, pl.ds(pl.multiple_of(number * height, height), height), columns]

    def tree_send(piece, offset, direction):
        source, _, index, columns, _ = pieces[piece]
        chip = chip_of(offset, z, y, x)
        block = piece_rows(piece, 2 * chip + core)
        return push(
            source.at[index, :, columns] if hops(offset) == 0 else block,
            block,
            send_sem.at[piece, DIRECTIONS.index(direction)],
            sibling_sem.at[piece] if direction == "s" else plane_sem.at[piece, chip],
            neighbour(direction, z, y, x, core),
        )

    def tree_step(piece, offset):
        order = pieces[piece][4]

        def go():
            chip = chip_of(offset, z, y, x)
            if hops(offset) > 0:
                arrived(piece_rows(piece, 2 * chip + core), plane_sem.at[piece, chip], sibling)
            for direction in onward(order, offset) + ["s"]:
                copy = tree_send(piece, offset, direction)
                maybe(direction_exists(direction, z), copy.start)

        maybe(offset_exists(offset, z), go)

    def tree_bytes(piece, count):
        _, full, index, columns, _ = pieces[piece]
        return full.at[index, pl.ds(0, count * height), columns]

    def tree_sent(piece):
        order = pieces[piece][4]

        def sent(direction, count):
            block = tree_bytes(piece, count)
            push(block, block, send_sem.at[piece, DIRECTIONS.index(direction)], gains_recv, sibling).wait_send()

        sent("s", 16)
        for direction in "xy":
            sent(direction, tree_count(order, direction, 3))
        for direction in "ud":
            for level in range(4):
                if level != (3 if direction == "u" else 0):
                    pl.when(z == level)(
                        functools.partial(sent, direction, tree_count(order, direction, level))
                    )

    def tree_end(s):
        mine = [piece for piece in range(len(pieces)) if pieces[piece][2] == s]

        for piece in mine:
            arrived(tree_bytes(piece, 16), sibling_sem.at[piece], sibling)
        for piece in mine:
            tree_own[piece].wait()

    tree_own = [
        pltpu.make_async_copy(
            source.at[index, :, columns], piece_rows(piece, me), local_sem.at[piece]
        )
        for piece, (source, _, index, columns, _) in enumerate(pieces)
    ]

    def gains_copy(step):
        other = lax.rem(me + step, 32)
        return push(
            gains_own,
            gains_all.at[me],
            gains_send,
            gains_recv,
            (lax.div(other, 2), lax.rem(other, 2)),
        )

    def gains_start(step, carry):
        gains_copy(step).start()
        return carry

    def start(copy):
        copy.start()

    def weight_rows(s, number):
        return gate_up_buf.at[s, pl.ds(pl.multiple_of(number * height, height), height), :]

    def down_rows(s, dzh, dy):
        number = 2 * flip(zh, dzh) + flip(y, dy)
        return down_buf.at[s, pl.ds(pl.multiple_of(number * down_height, down_height), down_height), :]

    def act_rows(which, s, step):
        full = (rows_buf, grads_buf)[which]
        return full.at[s, pl.ds(pl.multiple_of(rank(step) * act_height, act_height), act_height), :]

    def send_act(which, s, step, source, hop):
        landed = tuple(bit ^ (1 if axis == hop else 0) for axis, bit in enumerate(step))
        start(
            push(
                source,
                act_rows(which, s, step),
                act_send.at[which, s, hop],
                act_recv.at[which, s, 4 * landed[0] + 2 * landed[1] + landed[2]],
                member(tuple(1 if axis == hop else 0 for axis in range(3))),
            )
        )

    def wait_act(which, s, step):
        arrived(
            act_rows(which, s, step),
            act_recv.at[which, s, 4 * step[0] + 2 * step[1] + step[2]],
            sibling,
        )

    def act_own(which, s):
        source = act_rows(0, s, own_step) if which == 0 else grads_own.at[s]
        for hop in (0, 1, 2):
            send_act(which, s, own_step, source, hop)

    def act_from_z(which, s):
        step = (1, 0, 0)
        wait_act(which, s, step)
        send_act(which, s, step, act_rows(which, s, step), 1)
        send_act(which, s, step, act_rows(which, s, step), 2)

    def act_from_x(which, s, dl):
        wait_act(which, s, (dl, 1, 0))
        send_act(which, s, (dl, 1, 0), act_rows(which, s, (dl, 1, 0)), 2)

    def act_from_core(which, s, dl, dx):
        wait_act(which, s, (dl, dx, 1))

    def mine(s):
        return gate_up_parts.at[rank(own_step), s]

    def ff_source(s, slot):
        return down_ref.at[s] if slot == 8 else mine(s)

    def ff_rows(s, slot, dzh):
        return down_rows(s, dzh, 0) if slot == 8 else weight_rows(s, device(RANK_STEPS[slot], dzh, 0))

    def to_rank(s, slot):
        step = RANK_STEPS[slot]
        start(
            push(
                gate_up_parts.at[rank(step), s],
                weight_rows(s, device(own_step)),
                rank_send.at[s],
                rank_recv.at[s, slot],
                member(step),
            )
        )

    def send_far(s, slot, source):
        start(push(source, ff_rows(s, slot, 0), far_send.at[s], far_recv.at[s, slot], far))

    def send_across(s, slot, source, dzh):
        start(
            push(
                source,
                ff_rows(s, slot, dzh),
                across_send.at[s],
                across_recv.at[s],
                across,
            )
        )

    def own_far(s, slot):
        send_far(s, slot, ff_source(s, slot))

    def own_across(s, slot):
        send_across(s, slot, ff_source(s, slot), 0)

    def rank_far(s, slot):
        arrived(ff_rows(s, slot, 0), rank_recv.at[s, slot], sibling)
        send_far(s, slot, ff_rows(s, slot, 0))

    def rank_across(s, slot):
        send_across(s, slot, ff_rows(s, slot, 0), 0)

    def far_across(s, slot):
        arrived(ff_rows(s, slot, 1), far_recv.at[s, slot], sibling)
        send_across(s, slot, ff_rows(s, slot, 1), 1)

    def ff_end(s):
        for copy in ff_local[s]:
            copy.wait()
        arrived(ff_bytes(s, 2 * share), across_recv.at[s], sibling)

    share = 8 * height + down_height * model // gate_up_buf.shape[2]

    def ff_bytes(s, rows):
        return gate_up_buf.at[s, pl.ds(0, rows), :]

    def ff_sent(s):
        for sem, rows in ((rank_send, 7 * height), (far_send, share), (across_send, 2 * share)):
            block = ff_bytes(s, rows)
            push(block, block, sem.at[s], gains_recv, sibling).wait_send()
        for which, full in enumerate((rows_buf, grads_buf)):
            for hop, count in enumerate((1, 2, 4)):
                block = full.at[s, pl.ds(0, count * act_height), :]
                push(block, block, act_send.at[which, s, hop], gains_recv, sibling).wait_send()

    ff_local = []
    for s in range(positions):
        ff_local.append(
            [
                pltpu.make_async_copy(mine(s), weight_rows(s, device(own_step)), local_sem.at[7 + 3 * s]),
                pltpu.make_async_copy(down_ref.at[s], down_rows(s, 0, 0), local_sem.at[8 + 3 * s]),
                pltpu.make_async_copy(grads_own.at[s], act_rows(1, s, own_step), local_sem.at[9 + 3 * s]),
            ]
        )
    gains_local = pltpu.make_async_copy(gains_own, gains_all.at[me], local_sem.at[6])

    def gains_begin():
        places = 128 // norm_attn_ref.shape[1]
        lane = lax.broadcasted_iota(jnp.int32, (positions, 128), 1) // norm_attn_ref.shape[1]
        gains_own[...] = jnp.zeros_like(gains_own)
        for index, source in enumerate((norm_attn_ref, norm_ff_ref)):
            tiled = jnp.concatenate([source[...].astype(F32)] * places, axis=1)
            gains_own[index * positions : (index + 1) * positions, :] = jnp.where(
                lane == lax.rem(me, places), tiled, 0.0
            ).astype(BF16)
        lax.fori_loop(1, 32, gains_start, 0)
        gains_local.start()

    raw_copy = pltpu.make_async_copy(gate_up_ref, gate_up_raw, local_sem.at[13])

    def part_units():
        raw_copy.wait()
        unit = down_height
        for number in range(8):
            low, rest = divmod(number, 4)
            for s in range(positions):
                for side in (0, 1):
                    for group in range(4):
                        zh_part, y_part = divmod(group, 2)
                        block = 32 * side + 16 * zh_part + 8 * low + 4 * y_part + rest
                        gate_up_parts[number, s, :, (4 * side + group) * unit : (4 * side + group + 1) * unit] = (
                            gate_up_raw[s, :, block * unit : (block + 1) * unit]
                        )
        for s in range(positions):
            ff_local[s][0].start()
            ff_local[s][1].start()

    def weigh():
        def one(rows):
            slot = lax.broadcasted_iota(jnp.int32, (16, 128), 0) + rows.start
            frame = me * act_height + slot
            weight = jnp.zeros((16, 128), F32)
            first = 0
            for item in range(lengths_ref.shape[0]):
                length = lengths_ref[item]
                inside = (frame >= first) & (frame < first + length)
                share = 8.0 * act_height / jnp.full((16, 128), length, jnp.int32).astype(F32)
                weight = weight + jnp.where(inside, share, 0.0)
                first = first + length
            weight = jnp.where(slot < valid_ref[0], weight, 0.0)[:, :1]
            values = cot_ref[rows].astype(F32)
            for p in range(positions):
                grads = values[:, p, :] * weight
                cot_rows[p, rows, :] = grads
                grads_own[p, rows, :] = grads.astype(BF16)

        row_loop(act_height, 16, one)
        for s in range(positions):
            ff_local[s][2].start()

    def take_gains():
        others = gains_all.at[pl.ds(0, 31)]
        arrived(others, gains_recv, sibling)
        push(others, others, gains_send, gains_recv, sibling).wait_send()
        gains_local.wait()
        for block in range(8):
            total = gains_all[4 * block].astype(F32)
            for extra in range(1, 4):
                total = total + gains_all[4 * block + extra].astype(F32)
            gain_rows[:, 128 * block : 128 * block + 128] = total

        def first_norm(rows):
            values = tokens_ref[rows].astype(F32)
            for p in range(positions):
                resid_mid[p, rows, :] = values[:, p, :]
                r, _ = normed(values[:, p, :])
                attn_in[p, rows, :] = (r * gain_rows[p : p + 1, :]).astype(BF16)

        row_loop(act_height, 16, first_norm)

    keep = []

    def attention(p):
        for source, target, slot in (
            (qkv_buf.at[p], qkv_full.at[p], 2 * p),
            (out_buf.at[p], out_full.at[p], 2 * p + 1),
        ):
            keep.append(pltpu.make_async_copy(source, target, keep_sem.at[slot]))
            keep[-1].start()

        def project(columns):
            qkv_rows[p, :, columns] = dot(attn_in[p], qkv_buf[p, :, columns]).astype(BF16)

        tile_loop(3 * model, 512, project)
        probs = attention_probs(qkv_rows, halves, spread, model, p)
        for q in range(p + 1):
            halves[2 * q] = to_heads(probs[q].astype(BF16), spread)

        def mix(rows):
            total = None
            for q in range(p + 1):
                term = halves[2 * q, rows, :].astype(F32) * qkv_rows[q, rows, 2 * model :].astype(F32)
                total = term if total is None else total + term
            context[p, rows, :] = total.astype(BF16)

        row_loop(act_height, 16, mix)

        def attend(columns):
            resid_mid[p, :, columns] += dot(context[p], out_buf[p, :, columns])

        tile_loop(model, 512, attend)

        def second_norm(step, carry):
            rows = pl.ds(pl.multiple_of(step * 16, 16), 16)
            r, _ = normed(resid_mid[p, rows, :])
            top = rank(own_step) * act_height + step * 16
            rows_buf[p, pl.ds(pl.multiple_of(top, 16), 16), :] = (
                r * gain_rows[positions + p : positions + p + 1, :]
            ).astype(BF16)
            return carry

        lax.fori_loop(0, act_height // 16, second_norm, 0)

    def ff_block(s, number):
        rows = pl.ds(pl.multiple_of(number * 2 * act_height, 2 * act_height), 2 * act_height)
        normed_rows = rows_buf[s, rows, :]
        grads = grads_buf[s, rows, :]
        for tile in range(split // 256):
            left, right = pl.ds(tile * 256, 256), pl.ds(split + tile * 256, 256)
            gate = dot(normed_rows, gate_up_buf[s, :, left])
            up = dot(normed_rows, gate_up_buf[s, :, right])
            d_hidden = dot_back(grads, down_buf[s, left, :])
            sigmoid_gate = jax.nn.sigmoid(gate)
            silu_gate = gate * sigmoid_gate
            hidden[rows, left] = (silu_gate * up).astype(BF16)
            d_gate_up[rows, left] = (
                d_hidden * up * sigmoid_gate * (1.0 + gate * (1.0 - sigmoid_gate))
            ).astype(BF16)
            d_gate_up[rows, right] = (d_hidden * silu_gate).astype(BF16)
        for tile in range(model // 512):
            columns = pl.ds(tile * 512, 512)
            out_stage[rows, columns] = dot(hidden[rows, :], down_buf[s, :, columns]).astype(BF16)
            back_stage[rows, columns] = dot_back(
                d_gate_up[rows, :], gate_up_buf[s, columns, :]
            ).astype(BF16)

    stages = []

    def stage_out(s, *slots):
        for slot in slots:
            source, target = (
                (out_stage, ff_out),
                (back_stage, ff_back),
                (gate_up_stage, gate_up_grad),
                (down_stage, down_grad),
            )[slot]
            stages.append(pltpu.make_async_copy(source, target.at[s], stage_sem.at[s, slot]))
            stages[-1].start()

    def gate_grad(s):
        stage_out(s, 0, 1)

        def gate_up_tile(columns):
            gate_up_stage[:, columns] = dot_grad(rows_buf[s], d_gate_up[:, columns]).astype(BF16)

        tile_loop(2 * split, 256, gate_up_tile)
        stage_out(s, 2)

    def down_weights_grad(s):
        def down_tile(columns):
            down_stage[:, columns] = dot_grad(hidden[...], grads_buf[s, :, columns]).astype(BF16)

        tile_loop(model, 256, down_tile)
        stage_out(s, 3)

    def stages_end():
        while stages:
            stages.pop(0).wait()

    for copy in tree_own:
        copy.start()
    raw_copy.start()
    gains_begin()
    make_spread(spread)
    chips = ((0, 0), (1, 0), (0, 1), (1, 1))

    def block(s, order):
        if s > 0 and order == chosen_first[0]:
            stages_end()
        ff_block(s, 2 * flip(zl, chips[order][0]) + flip(x, chips[order][1]))

    def attend_and_send(s):
        attention(s)
        act_own(0, s)

    chosen_first = [step[2] for step in FORWARD_STEPS if step[:2] == (F_BLOCK, 1)]
    kinds = {
        F_TREE: lambda piece, dz, dy, dx: tree_step(piece, (dz, dy, dx)),
        F_TREE_END: tree_end,
        F_GAINS: take_gains,
        F_PARTS: part_units,
        F_COT: weigh,
        F_ATTENTION: attend_and_send,
        F_GRADS: lambda s: act_own(1, s),
        F_ACT_Z: act_from_z,
        F_ACT_X: act_from_x,
        F_ACT_C: act_from_core,
        F_TO_RANK: to_rank,
        F_OWN_FAR: own_far,
        F_OWN_ACROSS: own_across,
        F_RANK_FAR: rank_far,
        F_RANK_ACROSS: rank_across,
        F_FAR_ACROSS: far_across,
        F_FF_END: ff_end,
        F_BLOCK: block,
        F_GATE_GRAD: gate_grad,
        F_DOWN_GRAD: down_weights_grad,
    }
    for kind, *numbers in FORWARD_STEPS:
        kinds[kind](*numbers)
    for piece in range(len(pieces)):
        tree_sent(piece)
    for s in range(positions):
        ff_sent(s)
    for copy in keep:
        copy.wait()
    stages_end()


def forward_gather(valid, lengths, norm_attn, norm_ff, tokens, cot, w_qkv, w_out, w_gate_up, w_down):
    act_height, positions, model = tokens.shape
    _, height, qkv_width = w_qkv.shape
    unit = w_down.shape[1]
    ranks, split, width = 8, 4 * unit, 8 * unit
    group_rows = ranks * act_height
    dma = pltpu.SemaphoreType.DMA
    vmem = pl.BlockSpec(memory_space=pltpu.VMEM)
    smem = pl.BlockSpec(memory_space=pltpu.SMEM)
    anywhere = pl.BlockSpec(memory_space=pl.ANY)
    return pl.pallas_call(
        forward_kernel,
        out_shape=(
            jax.ShapeDtypeStruct((16, model), F32),
            jax.ShapeDtypeStruct((positions, act_height, model), F32),
            jax.ShapeDtypeStruct((positions, act_height, 3 * model), BF16),
            jax.ShapeDtypeStruct((positions, act_height, model), BF16),
            jax.ShapeDtypeStruct((positions, act_height, model), F32),
            jax.ShapeDtypeStruct((positions, model, qkv_width), BF16),
            jax.ShapeDtypeStruct((positions, model, model), BF16),
            jax.ShapeDtypeStruct((positions, group_rows, model), BF16),
            jax.ShapeDtypeStruct((positions, group_rows, model), BF16),
            jax.ShapeDtypeStruct((positions, model, width), BF16),
            jax.ShapeDtypeStruct((positions, split, model), BF16),
        ),
        in_specs=[smem] * 2 + [vmem] * 4 + [anywhere] * 4,
        out_specs=(vmem,) * 5 + (anywhere,) * 6,
        scratch_shapes=[
            pltpu.VMEM((positions, model, qkv_width), BF16),
            pltpu.VMEM((positions, model, model), BF16),
            pltpu.VMEM((positions, model, width), BF16),
            pltpu.VMEM((positions, split, model), BF16),
            pltpu.VMEM((positions, group_rows, model), BF16),
            pltpu.VMEM((positions, group_rows, model), BF16),
            pltpu.VMEM((group_rows, split), BF16),
            pltpu.VMEM((group_rows, width), BF16),
            pltpu.VMEM((group_rows, model), BF16),
            pltpu.VMEM((group_rows, model), BF16),
            pltpu.VMEM((model, width), BF16),
            pltpu.VMEM((split, model), BF16),
            pltpu.VMEM((16, 128), BF16),
            pltpu.VMEM((32, 16, 128), BF16),
            pltpu.VMEM(w_gate_up.shape, BF16),
            pltpu.VMEM((ranks, positions, height, width), BF16),
            pltpu.VMEM((positions, act_height, model), BF16),
            pltpu.VMEM((positions, act_height, model), BF16),
            pltpu.VMEM((2 * positions, act_height, model), BF16),
            pltpu.VMEM((model, 128), BF16),
            dma((6, 16)),
            dma((6,)),
            dma((6, 5)),
            dma,
            dma,
            dma((2,)),
            dma((2, 8)),
            dma((2,)),
            dma((2, 9)),
            dma((2,)),
            dma((2,)),
            dma((2, 2, 3)),
            dma((2, 2, 8)),
            dma((14,)),
            dma((4,)),
            dma((2, 4)),
        ],
        compiler_params=pltpu.CompilerParams(
            collective_id=4, has_side_effects=True, vmem_limit_bytes=62 * 2**20
        ),
        name="forward_gather",
    )(valid, lengths, norm_attn, norm_ff, tokens, cot, w_qkv, w_out, w_gate_up, w_down)


def slot_index(order, direction, offset, z, y, x):
    axis = {"u": "z", "d": "z"}.get(direction, direction)
    index, count = 0, 1
    values = dict(z=z + offset[0], y=flip(y, offset[1]), x=flip(x, offset[2]))
    sizes = dict(z=4, y=2, x=2)
    for earlier in order[: order.index(axis)]:
        index = index * sizes[earlier] + values[earlier]
        count *= sizes[earlier]
    if axis == "z":
        index = index * 5 + (4 if direction == "d" and offset[0] == 0 else values["z"])
        count *= 5
    return index, count


def slot_base(order):
    base, total = {}, 0
    for axis, direction in (("x", "x"), ("y", "y"), ("z", "u")):
        base[axis] = total
        total += slot_index(order, direction, (0, 0, 0), 0, 0, 0)[1]
    base["u"] = base["d"] = base["z"]
    return base, total


(
    B_TREE,
    B_RS_ACROSS,
    B_RS_FIRST,
    B_RS_SECOND,
    B_RS_RANK,
    B_RS_LAST,
    B_ACT_CORE,
    B_ACT_LOAD,
    B_ACT_ADD_X,
    B_ACT_ADD_Z,
    B_ACT_SUM,
    B_NORM_TURN,
    B_SWAP_TURNED,
    B_PROBS,
    B_MID,
    B_SCORES_BACK,
    B_SWAP_QKV,
    B_OUT_W,
    B_QKV_W,
    B_ROWS_BACK,
    B_ATTN_BACK,
    B_FINISH_OUTPUT,
) = range(22)
BACKWARD_STEPS = [
    (B_RS_ACROSS, 0, 0, 0), (B_ACT_CORE, 0, 0), (B_RS_ACROSS, 0, 1, 0), (B_ACT_CORE, 1, 0),
    (B_RS_ACROSS, 0, 0, 1), (B_ACT_ADD_X, 0, 0, 1), (B_ACT_CORE, 0, 1), (B_RS_FIRST, 0, 0), (B_ACT_ADD_Z, 0, 0),
    (B_ACT_ADD_X, 0, 1, 1), (B_ACT_ADD_X, 0, 0, 0), (B_PROBS,), (B_ACT_ADD_X, 0, 1, 0), (B_NORM_TURN,),
    (B_RS_FIRST, 0, 1), (B_RS_ACROSS, 1, 1, 1), (B_ACT_ADD_Z, 0, 1), (B_RS_ACROSS, 0, 0, 2), (B_ACT_SUM, 0, 0),
    (B_RS_ACROSS, 0, 1, 1), (B_MID, 0), (B_RS_FIRST, 0, 2), (B_ACT_SUM, 0, 1), (B_MID, 1), (B_ACT_CORE, 1, 1),
    (B_RS_ACROSS, 1, 0, 1), (B_RS_ACROSS, 1, 0, 0), (B_SWAP_TURNED,), (B_ACT_LOAD, 1), (B_SCORES_BACK,),
    (B_SWAP_QKV,), (B_ACT_ADD_X, 1, 1, 1), (B_RS_ACROSS, 0, 1, 2), (B_RS_SECOND, 0, 1), (B_OUT_W, 0),
    (B_RS_FIRST, 1, 1), (B_ACT_ADD_X, 1, 1, 0), (B_OUT_W, 1), (B_RS_ACROSS, 1, 0, 2), (B_TREE, 3, 2, 0, 0),
    (B_TREE, 3, -3, 0, 0), (B_QKV_W, 1), (B_TREE, 1, -2, 1, 1), (B_ACT_ADD_X, 1, 0, 0), (B_TREE, 3, -3, 0, 1),
    (B_QKV_W, 0), (B_TREE, 1, -3, 0, 1), (B_TREE, 1, 0, 1, 1), (B_TREE, 3, -3, 1, 0), (B_TREE, 0, 1, 1, 0),
    (B_TREE, 0, -2, 1, 1), (B_TREE, 0, 1, 1, 1), (B_TREE, 3, 3, 0, 0), (B_TREE, 1, -1, 0, 1),
    (B_TREE, 0, 3, 1, 1), (B_TREE, 2, -3, 1, 1), (B_TREE, 3, 3, 1, 1), (B_TREE, 1, 2, 1, 1),
    (B_TREE, 3, 3, 0, 1), (B_TREE, 2, -2, 0, 0), (B_TREE, 2, 2, 0, 0), (B_ACT_ADD_X, 1, 0, 1),
    (B_TREE, 1, 3, 1, 1), (B_TREE, 2, -2, 1, 1), (B_TREE, 2, 3, 1, 0), (B_RS_SECOND, 0, 0),
    (B_TREE, 1, 1, 1, 1), (B_TREE, 1, 2, 0, 1), (B_RS_RANK, 0, 4), (B_RS_FIRST, 1, 0), (B_RS_FIRST, 1, 2),
    (B_TREE, 2, 3, 0, 0), (B_TREE, 2, 2, 1, 0), (B_TREE, 2, -3, 0, 0), (B_RS_ACROSS, 1, 1, 0),
    (B_TREE, 0, -3, 1, 1), (B_TREE, 0, 1, 0, 1), (B_TREE, 0, -2, 1, 0), (B_TREE, 0, -1, 1, 1),
    (B_TREE, 1, 3, 0, 1), (B_TREE, 0, 3, 1, 0), (B_TREE, 1, -3, 1, 1), (B_TREE, 3, 3, 1, 0),
    (B_TREE, 1, -1, 1, 1), (B_TREE, 3, 2, 1, 1), (B_ACT_ADD_Z, 1, 1), (B_TREE, 0, 2, 1, 1),
    (B_TREE, 2, -2, 1, 0), (B_TREE, 3, -2, 0, 1), (B_TREE, 2, -3, 1, 0), (B_TREE, 2, 3, 0, 1),
    (B_TREE, 0, -3, 0, 1), (B_TREE, 2, 2, 1, 1), (B_TREE, 3, -2, 0, 0), (B_TREE, 3, 2, 0, 1), (B_ROWS_BACK, 0),
    (B_TREE, 2, 3, 1, 1), (B_TREE, 0, -2, 0, 1), (B_TREE, 3, 2, 1, 0), (B_TREE, 2, -2, 0, 1),
    (B_TREE, 1, -2, 0, 1), (B_TREE, 2, 1, 0, 0), (B_TREE, 1, 1, 0, 1), (B_TREE, 0, 0, 1, 1),
    (B_TREE, 1, 3, 1, 0), (B_TREE, 2, 1, 1, 0), (B_RS_SECOND, 1, 1), (B_RS_RANK, 0, 1), (B_TREE, 0, 3, 0, 1),
    (B_ACT_ADD_Z, 1, 0), (B_TREE, 0, -1, 0, 1), (B_TREE, 0, 2, 0, 1), (B_TREE, 0, -3, 1, 0), (B_RS_RANK, 0, 2),
    (B_RS_ACROSS, 1, 1, 2), (B_TREE, 1, 3, 0, 0), (B_TREE, 2, -3, 0, 1), (B_TREE, 2, -1, 0, 0),
    (B_RS_SECOND, 1, 0), (B_RS_RANK, 1, 7), (B_TREE, 1, 2, 1, 0), (B_TREE, 1, -3, 1, 0), (B_RS_RANK, 1, 6),
    (B_TREE, 1, -2, 1, 0), (B_TREE, 3, -1, 0, 0), (B_RS_RANK, 1, 2), (B_TREE, 3, -2, 1, 0), (B_RS_RANK, 0, 6),
    (B_ACT_SUM, 1, 1), (B_RS_RANK, 1, 1), (B_TREE, 2, -1, 1, 0), (B_RS_RANK, 1, 4), (B_RS_RANK, 0, 3),
    (B_TREE, 3, 1, 0, 1), (B_TREE, 3, 1, 1, 1), (B_ROWS_BACK, 1), (B_RS_RANK, 0, 5), (B_TREE, 3, -2, 1, 1),
    (B_TREE, 3, 1, 1, 0), (B_TREE, 3, -1, 1, 0), (B_TREE, 0, 0, 1, 0), (B_TREE, 0, 2, 1, 0),
    (B_TREE, 0, 3, 0, 0), (B_TREE, 3, -3, 1, 1), (B_RS_LAST, 1, 1), (B_TREE, 3, -1, 0, 1),
    (B_TREE, 1, -3, 0, 0), (B_TREE, 0, -1, 1, 0), (B_ACT_SUM, 1, 0), (B_TREE, 2, 0, 1, 0),
    (B_TREE, 0, -3, 0, 0), (B_TREE, 1, 0, 1, 0), (B_RS_LAST, 0, 1), (B_TREE, 1, 2, 0, 0), (B_RS_RANK, 1, 5),
    (B_RS_RANK, 0, 7), (B_TREE, 1, 1, 1, 0), (B_TREE, 1, -1, 1, 0), (B_FINISH_OUTPUT,), (B_TREE, 0, 0, 0, 1),
    (B_TREE, 1, -2, 0, 0), (B_TREE, 0, -2, 0, 0), (B_TREE, 2, 2, 0, 1), (B_TREE, 3, 1, 0, 0), (B_RS_LAST, 0, 4),
    (B_TREE, 0, 2, 0, 0), (B_RS_LAST, 1, 7), (B_RS_SECOND, 1, 2), (B_RS_LAST, 0, 6), (B_TREE, 3, 0, 0, 1),
    (B_RS_LAST, 0, 7), (B_TREE, 2, -1, 1, 1), (B_RS_LAST, 1, 4), (B_TREE, 2, 1, 1, 1), (B_TREE, 2, 1, 0, 1),
    (B_TREE, 3, -1, 1, 1), (B_TREE, 1, 0, 0, 1), (B_RS_LAST, 0, 5), (B_TREE, 2, -1, 0, 1), (B_ATTN_BACK,),
    (B_RS_LAST, 1, 2), (B_TREE, 0, -1, 0, 0), (B_TREE, 0, 1, 0, 0), (B_RS_SECOND, 0, 2), (B_TREE, 2, 0, 1, 1),
    (B_TREE, 1, -1, 0, 0), (B_TREE, 1, 1, 0, 0), (B_RS_LAST, 1, 6), (B_TREE, 3, 0, 1, 1), (B_RS_LAST, 0, 2),
    (B_TREE, 2, 0, 0, 1), (B_RS_LAST, 0, 3), (B_RS_LAST, 1, 5), (B_RS_RANK, 1, 3), (B_TREE, 3, 0, 1, 0),
    (B_TREE, 3, 0, 0, 0), (B_TREE, 0, 0, 0, 0), (B_TREE, 2, 0, 0, 0), (B_TREE, 1, 0, 0, 0), (B_RS_LAST, 1, 3),
]


def backward_kernel(
    tokens_ref,
    cot_ref,
    gain_rows,
    qkv_rows,
    context,
    resid_mid,
    qkv_full,
    out_full,
    out_ref,
    back_ref,
    gate_up_ref,
    down_ref,
    output,
    grad_tokens,
    norm_attn_sum,
    norm_ff_sum,
    qkv_sum,
    attn_out_sum,
    gate_up_total,
    down_sum,
    act_own,
    core_buf,
    x_buf,
    z_buf,
    gate_own,
    down_own,
    across_gate,
    across_down,
    far_gate,
    far_down,
    qkv_grad,
    out_grad,
    slots_0,
    slots_1,
    slots_2,
    slots_3,
    qkv_tiles,
    out_tiles,
    turned,
    attn_turned,
    context_turned,
    d_qkv,
    d_mid_low,
    d_mid,
    d_context,
    d_rows,
    halves,
    probs_buf,
    spread,
    gain_acc,
    gains_part,
    gains_buf,
    gains_sum,
    gate_up_sum,
    core_send,
    core_recv,
    x_send,
    x_recv,
    z_send,
    z_recv,
    across_send,
    across_recv,
    far_send,
    far_recv,
    rank_send,
    rank_recv,
    swap_send,
    swap_recv,
    tree_send,
    tree_recv,
    gains_send,
    gains_recv,
    own_sem,
    part_sem,
    tile_sem,
):
    z, y, x, core = here()
    me = 2 * (z * 4 + y * 2 + x) + core
    zh, zl, member, rank, device, far, across = group_place(z, y, x, core)
    own_step = (0, 0, 0)
    act_height, positions, model = tokens_ref.shape
    sets = positions
    height = qkv_sum.shape[1]
    down_height = down_sum.shape[1]
    half = 16 * height
    sibling = member((0, 0, 1))
    scale = 1.0 / math.sqrt(HEAD_DIM)
    pairs = pairs_of(positions)
    greet_all(z, y, x, core)
    sends = []

    def start(copy):
        copy.start()
        sends.append(copy)

    def run_rows(dzh, dy, low):
        number = 16 * flip(zh, dzh) + 4 * flip(y, dy) + 8 * low
        return pl.ds(pl.multiple_of(number * height, 4 * height), 4 * height)

    def down_rows(dzh, dy):
        number = 2 * flip(zh, dzh) + flip(y, dy)
        return pl.ds(pl.multiple_of(number * down_height, down_height), down_height)

    def ff_from(s, dzh, dy, part):
        if part == 2:
            return down_ref.at[s, down_rows(dzh, dy)]
        return gate_up_ref.at[s, run_rows(dzh, dy, part)]

    def ff_across(s, turn, part):
        return across_down.at[turn, s] if part == 2 else across_gate.at[turn, s, part]

    def ff_own(s, turn, part):
        return down_own.at[turn, s] if part == 2 else gate_own.at[turn, s, part]

    def ff_far(s, part):
        return far_down.at[s] if part == 2 else far_gate.at[s, part]

    def part_copy(s, turn, part):
        return pltpu.make_async_copy(
            ff_from(s, 1 - turn, 0, part), ff_own(s, turn, part), part_sem.at[turn, s, part]
        )

    def rs_across(s, turn, part):
        start(
            push(
                ff_from(s, 1 - turn, 1, part),
                ff_across(s, turn, part),
                across_send.at[turn, s, part],
                across_recv.at[turn, s, part],
                across,
            )
        )

    def rs_first(s, part):
        block = ff_across(s, 0, part)
        part_copy(s, 0, part).wait()
        arrived(block, across_recv.at[0, s, part], across)
        add_into(block, [block, ff_own(s, 0, part)])
        start(push(block, ff_far(s, part), far_send.at[s, part], far_recv.at[s, part], far))

    def rs_second(s, part):
        block = ff_across(s, 1, part)
        part_copy(s, 1, part).wait()
        arrived(block, across_recv.at[1, s, part], across)
        arrived(ff_far(s, part), far_recv.at[s, part], far)
        target = down_sum.at[s] if part == 2 else block
        add_into(target, [block, ff_far(s, part), ff_own(s, 1, part)])

    def share(step, s):
        number = 2 * flip(x, step[1]) + flip(core, step[2])
        return across_gate.at[
            1, s, flip(zl, step[0]), pl.ds(pl.multiple_of(number * height, height), height)
        ]

    def place_units(step, s, source):
        unit = down_height
        number = 8 * flip(zl, step[0]) + 2 * flip(x, step[1]) + flip(core, step[2])
        for side in (0, 1):
            for group in range(4):
                zh_part, y_part = divmod(group, 2)
                left = (32 * side + 16 * zh_part + 4 * y_part + number) * unit
                gate_up_total[s, :, pl.ds(pl.multiple_of(left, unit), unit)] = source[
                    :, (4 * side + group) * unit : (4 * side + group + 1) * unit
                ].astype(F32)

    def rs_rank(s, slot):
        step = RANK_STEPS[slot]
        push(
                share(step, s),
                gate_up_sum.at[rank(own_step), s],
                rank_send.at[s],
                rank_recv.at[slot, s],
                member(step),
            ).start()

    def rs_last(s, slot):
        step = RANK_STEPS[slot]
        block = gate_up_sum.at[rank(step), s]
        arrived(block, rank_recv.at[slot, s], member(step))
        place_units(step, s, block)

    acts = [back_ref, out_ref]

    def act_rows(step):
        return pl.ds(pl.multiple_of(rank(step) * act_height, act_height), act_height)

    def act_core(which, s):
        for dl, dx in ((1, 1), (0, 1), (1, 0), (0, 0)):
            start(
                push(
                    acts[which].at[s, act_rows((dl, dx, 1))],
                    core_buf.at[which, s, dl, dx],
                    core_send.at[which, s, dl, dx],
                    core_recv.at[which, s, dl, dx],
                    sibling,
                )
            )

    def act_copy(which, s, dl, dx):
        return pltpu.make_async_copy(
            acts[which].at[s, act_rows((dl, dx, 0))],
            act_own.at[s, dl, dx],
            own_sem.at[which, s, dl, dx],
        )

    def act_load(which):
        for s in range(sets):
            for dl in (0, 1):
                for dx in (0, 1):
                    act_copy(which, s, dl, dx).start()

    def act_ready(which, s, dl, dx):
        act_copy(which, s, dl, dx).wait()
        arrived(core_buf.at[which, s, dl, dx], core_recv.at[which, s, dl, dx], sibling)

    def act_add_x(which, s, dl):
        act_ready(which, s, dl, 1)
        block = core_buf.at[which, s, dl, 1]
        add_into(block, [block, act_own.at[s, dl, 1]])
        start(
            push(
                block,
                x_buf.at[which, s, dl],
                x_send.at[which, s, dl],
                x_recv.at[which, s, dl],
                member((0, 1, 0)),
            )
        )

    def act_add_z(which, s):
        act_ready(which, s, 1, 0)
        block = x_buf.at[which, s, 1]
        arrived(block, x_recv.at[which, s, 1], member((0, 1, 0)))
        add_into(block, [block, core_buf.at[which, s, 1, 0], act_own.at[s, 1, 0]])
        start(
            push(
                block, z_buf.at[which, s], z_send.at[which, s], z_recv.at[which, s], member((1, 0, 0))
            )
        )

    def act_sum(which, s):
        act_ready(which, s, 0, 0)
        arrived(x_buf.at[which, s, 0], x_recv.at[which, s, 0], member((0, 1, 0)))
        arrived(z_buf.at[which, s], z_recv.at[which, s], member((1, 0, 0)))

    def act_total(which, s, rows):
        return (
            act_own[s, 0, 0, rows, :].astype(F32)
            + core_buf[which, s, 0, 0, rows, :].astype(F32)
            + x_buf[which, s, 0, rows, :].astype(F32)
            + z_buf[which, s, rows, :].astype(F32)
        )

    pieces = [
        (qkv_grad, qkv_sum, 0, "zxy", slots_0),
        (qkv_grad, qkv_sum, 1, "zyx", slots_1),
        (out_grad, attn_out_sum, 0, "xyz", slots_2),
        (out_grad, attn_out_sum, 1, "yxz", slots_3),
    ]
    events = sorted(
        ((-hops(offset), place, piece, offset) for piece in range(4) for place, offset in enumerate(OFFSETS)),
        key=lambda event: event[:3],
    )

    def tree_block(piece, offset):
        source, _, index, _, _ = pieces[piece]
        chip = chip_of(offset, z, y, x)
        return source.at[index, pl.ds(pl.multiple_of(chip * height, height), height), :]

    def tree_copy(piece, offset):
        _, _, _, order, slots = pieces[piece]
        toward = came_from(order, offset)
        base, _ = slot_base(order)
        seen = {"x": "x", "y": "y", "u": "d", "d": "u"}[toward]
        nearer = offset
        if toward == "u":
            nearer = (offset[0] - 1, offset[1], offset[2])
        if toward == "d":
            nearer = (offset[0] + 1, offset[1], offset[2])
        there = {"u": z + 1, "d": z - 1}.get(toward, z)
        index_there, _ = slot_index(
            order, seen, nearer, there, y if toward != "y" else 1 - y, x if toward != "x" else 1 - x
        )
        if toward in "xy":
            index_there, _ = slot_index(order, seen, offset, z, y, x)
        place = base[seen] + index_there
        return push(
            tree_block(piece, offset),
            slots.at[place],
            tree_send.at[piece, DIRECTIONS.index(toward)],
            tree_recv.at[piece, place],
            neighbour(toward, z, y, x, core),
        )

    def tree_step(piece, offset):
        _, result, index, order, slots = pieces[piece]
        base, _ = slot_base(order)

        def go():
            block = tree_block(piece, offset)
            sure, unsure = [], []
            for direction in onward(order, offset):
                local, _ = slot_index(order, direction, offset, z, y, x)
                place = base[direction] + local
                (sure if direction in "xy" else unsure).append((direction, place))
            terms = [block]
            for _, place in sure:
                arrived(slots.at[place], tree_recv.at[piece, place], sibling)
                terms.append(slots.at[place])
            last = hops(offset) == 0
            target = result.at[index] if last else block
            if last or len(terms) > 1:
                add_into(target, terms)
            for direction, place in unsure:

                def more(place=place):
                    arrived(slots.at[place], tree_recv.at[piece, place], sibling)
                    add_into(target, [target, slots.at[place]])

                maybe(direction_exists(direction, z), more)
            if not last:
                tree_copy(piece, offset).start()

        maybe(offset_exists(offset, z), go)

    def gains_copy(step):
        other = lax.rem(me + step, 32)
        return push(
            gains_part.at[lax.div(other, 4)],
            gains_buf.at[me],
            gains_send,
            gains_recv,
            (lax.div(other, 2), lax.rem(other, 2)),
        )

    def gains_start(step, carry):
        gains_copy(step).start()
        return carry

    def gains_add(step, carry):
        gains_sum[...] += gains_buf[lax.rem(me + step, 32)]
        return carry

    def turn(source, target, slot):
        def one(block, p):
            flat = source(p, block)
            turned[slot, p, pl.ds(2 * block, 2)] = flat.T.astype(BF16).reshape(2, 2, height, act_height)

        for p in range(positions):
            for block in range(model // 128):
                one(block, p)
            target[p, :, :, :act_height] = turned[slot, p, :, core]

    qkv_tile = qkv_tiles.shape[1]
    tile_count = model // qkv_tile

    def qkv_load(number):
        p, tile = divmod(number, tile_count)
        return pltpu.make_async_copy(
            qkv_full.at[p, pl.ds(tile * qkv_tile, qkv_tile)],
            qkv_tiles.at[number % 2],
            tile_sem.at[number % 2],
        )

    out_loads = [
        pltpu.make_async_copy(out_full.at[p], out_tiles.at[p], tile_sem.at[2 + p]) for p in range(positions)
    ]

    def context_block(p, block):
        return context[p, :, 128 * block : 128 * block + 128].astype(F32)

    def attn_block(p, block):
        return d_rows[p, :, 128 * block : 128 * block + 128]

    def norm_turn():
        def attn_norm(rows):
            values = tokens_ref[rows].astype(F32)
            for p in range(positions):
                r, _ = normed(values[:, p, :])
                d_rows[p, rows, :] = r * gain_rows[p : p + 1, :]

        row_loop(act_height, 16, attn_norm)
        turn(context_block, context_turned, 0)
        turn(attn_block, attn_turned, 1)

    def landing(kind, p):
        other = pl.ds(act_height, act_height)
        return (
            context_turned.at[p, :, :, other],
            attn_turned.at[p, :, :, other],
            d_mid_low.at[p, other],
            d_qkv.at[p, other],
        )[kind]

    def swap(kind, p, source):
        start(
            push(source, landing(kind, p), swap_send.at[4 * p + kind], swap_recv.at[4 * p + kind], sibling)
        )

    def swap_wait(kind, p):
        arrived(landing(kind, p), swap_recv.at[4 * p + kind], sibling)

    def swap_turned():
        for p in range(positions):
            swap(0, p, turned.at[0, p, :, 1 - core])
            swap(1, p, turned.at[1, p, :, 1 - core])

    def find_probs():
        for p in range(positions):
            probs = attention_probs(qkv_rows, halves, spread, model, p)
            for q in range(p + 1):
                probs_buf[pairs.index((p, q))] = probs[q]

    def mid(p):
        def mid_back(rows):
            d_ff_in = act_total(0, p, rows)
            r, inverse = normed(resid_mid[p, rows, :])
            gain_acc[positions + p] += r * d_ff_in
            total = cot_ref[p, rows, :] + norm_back(
                r, inverse, d_ff_in * gain_rows[positions + p : positions + p + 1, :]
            )
            d_mid[p, rows, :] = total
            d_mid_low[p, rows, :] = total.astype(BF16)

        row_loop(act_height, 16, mid_back)
        swap(2, p, d_mid_low.at[p, pl.ds(0, act_height)])
        out_loads[p].wait()

        def context_back(columns):
            d_context[p, :, columns] = dot_back(
                d_mid_low[p, :act_height, :], out_tiles[p, columns, :]
            ).astype(BF16)

        tile_loop(model, 256, context_back)

    def scores_back():
        def context_products(rows):
            for index, (p, q) in enumerate(pairs):
                product = d_context[p, rows, :].astype(F32) * qkv_rows[q, rows, 2 * model :].astype(F32)
                halves[2 * index, rows, :], halves[2 * index + 1, rows, :] = split_product(product)

        row_loop(act_height, 16, context_products)
        d_probs = [sums_over_heads(halves, spread, index) for index in range(len(pairs))]
        for p in range(positions):
            own = [index for index, pair in enumerate(pairs) if pair[0] == p]
            mean = functools.reduce(jnp.add, [probs_buf[index] * d_probs[index] for index in own])
            for index in own:
                d_score = (probs_buf[index] * (d_probs[index] - mean)).astype(BF16)
                halves[2 * index] = to_heads(d_score, spread)
                halves[2 * index + 1] = to_heads(probs_buf[index].astype(BF16), spread)

        def plus(total, term):
            return term if total is None else total + term

        def qkv_back(rows):
            d_keys = [None] * positions
            d_values = [None] * positions
            for p in range(positions):
                d_query = None
                d_own = d_context[p, rows, :].astype(F32)
                query = qkv_rows[p, rows, :model].astype(F32)
                for index, (own, q) in enumerate(pairs):
                    if own == p:
                        d_score = halves[2 * index, rows, :].astype(F32)
                        key = qkv_rows[q, rows, model : 2 * model].astype(F32)
                        d_query = plus(d_query, d_score * key)
                        d_keys[q] = plus(d_keys[q], d_score * query)
                        d_values[q] = plus(
                            d_values[q], halves[2 * index + 1, rows, :].astype(F32) * d_own
                        )
                d_qkv[p, rows, :model] = (d_query * scale).astype(BF16)
            for p in range(positions):
                d_qkv[p, rows, model : 2 * model] = (d_keys[p] * scale).astype(BF16)
                d_qkv[p, rows, 2 * model :] = d_values[p].astype(BF16)

        row_loop(act_height, 16, qkv_back)

    def swap_qkv():
        for p in range(positions):
            swap(3, p, d_qkv.at[p, pl.ds(0, act_height)])

    def out_weights(p):
        swap_wait(0, p)
        swap_wait(2, p)

        def tile(columns):
            out_grad[p, :, columns] = dot(
                context_turned[p].reshape(half, 2 * act_height), d_mid_low[p, :, columns]
            ).astype(BF16)

        tile_loop(model, 256, tile)

    def qkv_weights(p):
        swap_wait(1, p)
        swap_wait(3, p)

        def tile(columns):
            qkv_grad[p, :, columns] = dot(
                attn_turned[p].reshape(half, 2 * act_height), d_qkv[p, :, columns]
            ).astype(BF16)

        tile_loop(3 * model, 256, tile)

    def rows_back(p):
        for tile in range(tile_count):
            number = p * tile_count + tile
            qkv_load(number).wait()
            d_rows[p, :, tile * qkv_tile : (tile + 1) * qkv_tile] = dot_back(
                d_qkv[p, :act_height, :], qkv_tiles[number % 2]
            )
            if number + 2 < positions * tile_count:
                qkv_load(number + 2).start()

    def attn_back():
        def norm_one_back(rows):
            values = tokens_ref[rows].astype(F32)
            for p in range(positions):
                r, inverse = normed(values[:, p, :])
                d_attn_in = d_rows[p, rows, :]
                gain_acc[p] += r * d_attn_in
                grad_tokens[rows, p, :] = d_mid[p, rows, :] + norm_back(
                    r, inverse, d_attn_in * gain_rows[p : p + 1, :]
                )

        row_loop(act_height, 16, norm_one_back)
        gains_part[...] = jnp.zeros_like(gains_part)
        for index in range(2 * positions):
            sums = jnp.sum(gain_acc[index], axis=0, keepdims=True)
            for block in range(8):
                gains_part[block, index : index + 1, :] = sums[:, 128 * block : 128 * block + 128]
        lax.fori_loop(1, 32, gains_start, 0)

    def finish_output():
        def finish(rows):
            rounded = [resid_mid[p, rows, :] + act_total(1, p, rows) for p in range(positions)]
            output[rows] = jnp.stack(rounded, axis=1).astype(BF16)

        row_loop(act_height, 16, finish)

    for s in range(sets):
        for turn_number in (0, 1):
            for part in (0, 1, 2):
                part_copy(s, turn_number, part).start()
    for copy in out_loads:
        copy.start()
    act_load(0)
    qkv_load(0).start()
    qkv_load(1).start()
    make_spread(spread)
    gain_acc[...] = jnp.zeros_like(gain_acc)
    kinds = {
        B_TREE: lambda piece, dz, dy, dx: tree_step(piece, (dz, dy, dx)),
        B_RS_ACROSS: rs_across,
        B_RS_FIRST: rs_first,
        B_RS_SECOND: rs_second,
        B_RS_RANK: rs_rank,
        B_RS_LAST: rs_last,
        B_ACT_CORE: act_core,
        B_ACT_LOAD: act_load,
        B_ACT_ADD_X: act_add_x,
        B_ACT_ADD_Z: act_add_z,
        B_ACT_SUM: act_sum,
        B_NORM_TURN: norm_turn,
        B_SWAP_TURNED: swap_turned,
        B_PROBS: find_probs,
        B_MID: mid,
        B_SCORES_BACK: scores_back,
        B_SWAP_QKV: swap_qkv,
        B_OUT_W: out_weights,
        B_QKV_W: qkv_weights,
        B_ROWS_BACK: rows_back,
        B_ATTN_BACK: attn_back,
        B_FINISH_OUTPUT: finish_output,
    }
    for kind, *numbers in BACKWARD_STEPS:
        kinds[kind](*numbers)
    for s in range(sets):
        place_units(own_step, s, share(own_step, s))
    gains_sum[...] = gains_part[lax.div(me, 4)]
    others = gains_buf.at[pl.ds(0, 31)]
    arrived(others, gains_recv, sibling)
    push(others, others, gains_send, gains_recv, sibling).wait_send()
    lax.fori_loop(1, 32, gains_add, 0)
    own_gain = norm_attn_sum.shape[1]
    for index, target in enumerate((norm_attn_sum, norm_ff_sum)):
        picked = jnp.zeros(target.shape, F32)
        for place in range(128 // own_gain):
            picked = picked + jnp.where(
                lax.rem(me, 128 // own_gain) == place,
                gains_sum[
                    index * positions : (index + 1) * positions, place * own_gain : (place + 1) * own_gain
                ],
                0.0,
            )
        target[...] = picked
    def tree_sent(piece, direction, count):
        source, _, index, _, _ = pieces[piece]
        block = source.at[index, pl.ds(0, count * height), :]
        push(block, block, tree_send.at[piece, DIRECTIONS.index(direction)], gains_recv, sibling).wait_send()

    for piece in range(len(pieces)):
        order = pieces[piece][3]
        for direction in "xy":
            tree_sent(piece, direction, return_count(order, direction, 3))
        for direction in "ud":
            for level in range(4):
                if level != (3 if direction == "u" else 0):
                    pl.when(z == level)(
                        functools.partial(
                            tree_sent, piece, direction, return_count(order, direction, level)
                        )
                    )
    for s in range(sets):
        block = gate_up_sum.at[pl.ds(0, 7), s]
        push(block, block, rank_send.at[s], gains_recv, sibling).wait_send()
    for copy in sends:
        copy.wait_send()


def backward_scatter(
    tokens,
    grads,
    gain_rows,
    qkv_rows,
    context,
    resid_mid,
    qkv_full,
    out_full,
    out_part,
    back_part,
    gate_up_grad,
    down_grad,
):
    act_height, sets, model = tokens.shape
    width = gate_up_grad.shape[2]
    height = model // 32
    down_height = down_grad.shape[1] // 4
    dma = pltpu.SemaphoreType.DMA
    vmem = pl.BlockSpec(memory_space=pltpu.VMEM)
    anywhere = pl.BlockSpec(memory_space=pl.ANY)
    places = [slot_base(order)[1] for order in ORDERS]
    pair_count = len(pairs_of(sets))
    act = (sets, act_height, model)
    return pl.pallas_call(
        backward_kernel,
        out_shape=(
            jax.ShapeDtypeStruct(tokens.shape, BF16),
            jax.ShapeDtypeStruct(tokens.shape, F32),
            jax.ShapeDtypeStruct((sets, height), F32),
            jax.ShapeDtypeStruct((sets, height), F32),
            jax.ShapeDtypeStruct((sets, height, 3 * model), F32),
            jax.ShapeDtypeStruct((sets, height, model), F32),
            jax.ShapeDtypeStruct((sets, height, 8 * width), F32),
            jax.ShapeDtypeStruct((sets, down_height, model), F32),
        ),
        in_specs=[vmem] * 6 + [anywhere] * 6,
        out_specs=(vmem,) * 8,
        scratch_shapes=[
            pltpu.VMEM((sets, 2, 2, act_height, model), BF16),
            pltpu.VMEM((2, sets, 2, 2, act_height, model), BF16),
            pltpu.VMEM((2, sets, 2, act_height, model), BF16),
            pltpu.VMEM((2, sets, act_height, model), BF16),
            pltpu.VMEM((2, sets, 2, 4 * height, width), BF16),
            pltpu.VMEM((2, sets, down_height, model), BF16),
            pltpu.VMEM((2, sets, 2, 4 * height, width), BF16),
            pltpu.VMEM((2, sets, down_height, model), BF16),
            pltpu.VMEM((sets, 2, 4 * height, width), BF16),
            pltpu.VMEM((sets, down_height, model), BF16),
            pltpu.VMEM((sets, 16 * height, 3 * model), BF16),
            pltpu.VMEM((sets, 16 * height, model), BF16),
            pltpu.VMEM((places[0], height, 3 * model), BF16),
            pltpu.VMEM((places[1], height, 3 * model), BF16),
            pltpu.VMEM((places[2], height, model), BF16),
            pltpu.VMEM((places[3], height, model), BF16),
            pltpu.VMEM((2, 128, 3 * model), BF16),
            pltpu.VMEM((sets, model, model), BF16),
            pltpu.VMEM((2, sets, 16, 2, height, act_height), BF16),
            pltpu.VMEM((sets, 16, height, 2 * act_height), BF16),
            pltpu.VMEM((sets, 16, height, 2 * act_height), BF16),
            pltpu.VMEM((sets, 2 * act_height, 3 * model), BF16),
            pltpu.VMEM((sets, 2 * act_height, model), BF16),
            pltpu.VMEM(act, F32),
            pltpu.VMEM(act, BF16),
            pltpu.VMEM(act, F32),
            pltpu.VMEM((2 * pair_count, act_height, model), BF16),
            pltpu.VMEM((pair_count, act_height, 128), F32),
            pltpu.VMEM((model, 128), BF16),
            pltpu.VMEM((2 * sets, 16, model), F32),
            pltpu.VMEM((8, 8, 128), F32),
            pltpu.VMEM((32, 8, 128), F32),
            pltpu.VMEM((8, 128), F32),
            pltpu.VMEM((8, sets, height, width), BF16),
            dma((2, sets, 2, 2)),
            dma((2, sets, 2, 2)),
            dma((2, sets, 2)),
            dma((2, sets, 2)),
            dma((2, sets)),
            dma((2, sets)),
            dma((2, sets, 3)),
            dma((2, sets, 3)),
            dma((sets, 3)),
            dma((sets, 3)),
            dma((sets,)),
            dma((8, sets)),
            dma((4 * sets,)),
            dma((4 * sets,)),
            dma((4, 4)),
            dma((4, max(places))),
            dma,
            dma,
            dma((2, sets, 2, 2)),
            dma((2, sets, 3)),
            dma((2 + sets,)),
        ],
        compiler_params=pltpu.CompilerParams(
            collective_id=5, has_side_effects=True, vmem_limit_bytes=63 * 2**20
        ),
        name="backward_scatter",
    )(
        tokens,
        grads,
        gain_rows,
        qkv_rows,
        context,
        resid_mid,
        qkv_full,
        out_full,
        out_part,
        back_part,
        gate_up_grad,
        down_grad,
    )


def settle_kernel(*refs):
    count = len(refs) // 2
    sems = refs[-1]
    copies = [
        pltpu.make_async_copy(refs[index], refs[count + index], sems.at[index]) for index in range(count)
    ]
    for copy in copies:
        copy.start()
    for copy in copies:
        copy.wait()


def settle(arrays):
    anywhere = pl.BlockSpec(memory_space=pl.ANY)
    return pl.pallas_call(
        settle_kernel,
        out_shape=tuple(jax.ShapeDtypeStruct(array.shape, array.dtype) for array in arrays),
        in_specs=[pl.BlockSpec(memory_space=pltpu.VMEM)] * len(arrays),
        out_specs=(anywhere,) * len(arrays),
        scratch_shapes=[pltpu.SemaphoreType.DMA((len(arrays),))],
        name="settle",
    )(*arrays)


def local_fast(
    tokens,
    norm_attn,
    w_qkv,
    w_out,
    norm_ff,
    w_gate_up,
    w_down,
    cotangent,
    valid_frames,
    item_lengths,
):
    (
        gain_rows,
        cot_rows,
        qkv_rows,
        context,
        resid_mid,
        qkv_full,
        out_full,
        out_part,
        back_part,
        gate_up_grad,
        down_grad,
    ) = forward_gather(
        valid_frames,
        item_lengths,
        norm_attn,
        norm_ff,
        tokens,
        cotangent,
        w_qkv,
        w_out,
        w_gate_up,
        w_down,
    )
    (
        output,
        grad_tokens,
        share_norm_attn,
        share_norm_ff,
        share_qkv,
        share_out,
        share_gate_up,
        share_down,
    ) = settle(backward_scatter(
        tokens,
        cot_rows,
        gain_rows,
        qkv_rows,
        context,
        resid_mid,
        qkv_full,
        out_full,
        out_part,
        back_part,
        gate_up_grad,
        down_grad,
    ))
    return (
        output,
        grad_tokens,
        share_norm_attn,
        share_qkv,
        share_out,
        share_norm_ff,
        share_gate_up,
        share_down,
    )


def solution(mesh):
    in_specs = (
        P(("dp", "pair"), None, None),
        P(None, ("dp", "pair")),
        P(None, ("dp", "pair"), None),
        P(None, ("dp", "pair"), None),
        P(None, ("dp", "pair")),
        P(None, ("dp", "pair"), None),
        P(None, ("dp", "pair"), None),
        P(("dp", "pair"), None, None),
        P(("dp", "pair")),
        P(),
    )
    out_specs = (
        P(("dp", "pair"), None, None),
        P(("dp", "pair"), None, None),
        P(None, ("dp", "pair")),
        P(None, ("dp", "pair"), None),
        P(None, ("dp", "pair"), None),
        P(None, ("dp", "pair")),
        P(None, ("dp", "pair"), None),
        P(None, ("dp", "pair"), None),
    )
    body = local_fast if mesh.shape["dp"] == 16 and mesh.shape["pair"] == 2 else local
    return jax.shard_map(body, mesh=mesh, in_specs=in_specs, out_specs=out_specs, check_vma=False)
```

```python
import functools
import math

import jax
import jax.numpy as jnp
from jax import lax
from jax.experimental import pallas as pl
from jax.experimental.pallas import tpu as pltpu
from jax.sharding import PartitionSpec as P

HEAD_DIM = 64


def per_pos(activations, weight):
    return jnp.einsum("fgk,gke->fge", activations, weight, preferred_element_type=jnp.float32)


def per_pos_back(gradients, weight):
    return jnp.einsum("fge,gke->fgk", gradients, weight, preferred_element_type=jnp.float32)


def pos_grad(activations, gradients):
    return jnp.einsum("fgk,fge->kge", activations, gradients, preferred_element_type=jnp.float32)


def gain_grad(normed_rows, gradients):
    return jnp.transpose(jnp.sum(normed_rows * gradients, axis=0))


def back_layout(share):
    return jnp.swapaxes(share, 0, 1)


def normed(values):
    inverse = lax.rsqrt(jnp.mean(values * values, axis=-1, keepdims=True) + 1e-05)
    return (values * inverse, inverse)


def norm_back(normed_rows, inverse, gradients):
    return inverse * (
        gradients - normed_rows * jnp.mean(gradients * normed_rows, axis=-1, keepdims=True)
    )


def gather_ff_fwd(norm_ff, w_gate_up, w_down, start, group):
    return (
        lax.all_gather(norm_ff[start : start + group], ("dp", "pair"), axis=1, tiled=True),
        lax.all_gather(w_gate_up[start : start + group], ("dp", "pair"), axis=1, tiled=True),
        lax.all_gather(w_down[start : start + group], ("dp", "pair"), axis=1, tiled=True),
    )


def gather_ff_back(norm_ff, w_gate_up, w_down, start, group):
    return (
        lax.all_gather(norm_ff[start : start + group], ("dp", "pair"), axis=1, tiled=True),
        lax.all_gather(w_gate_up[start : start + group], ("dp", "pair"), axis=1, tiled=True),
        lax.all_gather(w_down[start : start + group], ("dp", "pair"), axis=1, tiled=True),
    )


def local(
    tokens,
    norm_attn,
    w_qkv,
    w_out,
    norm_ff,
    w_gate_up,
    w_down,
    cotangent,
    valid_frames,
    item_lengths,
):
    frame_count, positions, model_width = tokens.shape
    head_count = model_width // HEAD_DIM
    ff_units = w_gate_up.shape[2] // 2
    score_scale = 1.0 / math.sqrt(HEAD_DIM)
    causal = jnp.arange(positions)[:, None] >= jnp.arange(positions)[None, :]
    head_shape = (frame_count, positions, head_count, HEAD_DIM)
    group = 1
    gains_attn, qkv_full, out_full = (
        lax.all_gather(norm_attn, ("dp", "pair"), axis=1, tiled=True),
        lax.all_gather(w_qkv, ("dp", "pair"), axis=1, tiled=True),
        lax.all_gather(w_out, ("dp", "pair"), axis=1, tiled=True),
    )
    resid_in = tokens.astype(jnp.float32)
    normed_one, inverse_one = normed(resid_in)
    attn_in = (normed_one * gains_attn.astype(jnp.float32)[None]).astype(jnp.bfloat16)
    qkv_rows = per_pos(attn_in, qkv_full).astype(jnp.bfloat16)
    queries = qkv_rows[..., :model_width].reshape(head_shape)
    key_heads = qkv_rows[..., model_width : 2 * model_width].reshape(head_shape)
    value_heads = qkv_rows[..., 2 * model_width :].reshape(head_shape)
    scores = (
        jnp.einsum("fphd,fqhd->fhpq", queries, key_heads, preferred_element_type=jnp.float32)
        * score_scale
    )
    scores = jnp.where(causal, scores, -1e30)
    row_max = jnp.max(scores, axis=-1, keepdims=True)
    attn_probs = jnp.exp(scores - row_max)
    attn_probs = attn_probs / jnp.sum(attn_probs, axis=-1, keepdims=True)
    probs_low = attn_probs.astype(jnp.bfloat16)
    context = jnp.einsum(
        "fhpq,fqhd->fphd", probs_low, value_heads, preferred_element_type=jnp.float32
    )
    context = context.astype(jnp.bfloat16).reshape(frame_count, positions, model_width)
    resid_mid = resid_in + per_pos(context, out_full)
    kept_parts = []
    out_parts = []
    for start in range(0, positions, group):
        gains_ff, gate_up_full, down_full = gather_ff_fwd(norm_ff, w_gate_up, w_down, start, group)
        mid_part = resid_mid[:, start : start + group]
        normed_two, inverse_two = normed(mid_part)
        ff_in = (normed_two * gains_ff.astype(jnp.float32)[None]).astype(jnp.bfloat16)
        gate_up = per_pos(ff_in, gate_up_full)
        gate_part = gate_up[..., :ff_units]
        up_part = gate_up[..., ff_units:]
        sigmoid_gate = jax.nn.sigmoid(gate_part)
        silu_gate = gate_part * sigmoid_gate
        hidden = (silu_gate * up_part).astype(jnp.bfloat16)
        out_parts.append(mid_part + per_pos(hidden, down_full))
        kept_parts.append(
            (normed_two, inverse_two, ff_in, gate_part, up_part, sigmoid_gate, silu_gate, hidden)
        )
    output = jnp.concatenate(out_parts, axis=1).astype(jnp.bfloat16)
    device_index = lax.axis_index(("dp", "pair"))
    local_ids = jnp.arange(frame_count, dtype=jnp.int32)
    frame_ids = device_index * frame_count + local_ids
    item_ends = jnp.cumsum(item_lengths)
    item_starts = item_ends - item_lengths
    in_item = (frame_ids[:, None] >= item_starts[None, :]) & (
        frame_ids[:, None] < item_ends[None, :]
    )
    item_share = 8 * frame_count / item_lengths.astype(jnp.float32)
    frame_weight = jnp.sum(jnp.where(in_item, item_share[None, :], 0.0), axis=1)
    frame_weight = jnp.where(local_ids < valid_frames[0], frame_weight, 0.0)
    grad_out = cotangent.astype(jnp.float32) * frame_weight[:, None, None]
    mid_grads = []
    share_norm_ff_parts = []
    share_gate_up_parts = []
    share_down_parts = []
    for index, start in enumerate(range(0, positions, group)):
        normed_two, inverse_two, ff_in, gate_part, up_part, sigmoid_gate, silu_gate, hidden = (
            kept_parts[index]
        )
        gains_ff, gate_up_full, down_full = gather_ff_back(norm_ff, w_gate_up, w_down, start, group)
        grad_part = grad_out[:, start : start + group]
        grad_low = grad_part.astype(jnp.bfloat16)
        grad_down = pos_grad(hidden, grad_low)
        d_hidden = per_pos_back(grad_low, down_full)
        d_gate = d_hidden * up_part * sigmoid_gate * (1.0 + gate_part * (1.0 - sigmoid_gate))
        d_up = d_hidden * silu_gate
        d_gate_up = jnp.concatenate([d_gate, d_up], axis=-1).astype(jnp.bfloat16)
        grad_gate_up = pos_grad(ff_in, d_gate_up)
        d_ff_in = per_pos_back(d_gate_up, gate_up_full)
        grad_norm_ff = gain_grad(normed_two, d_ff_in)
        mid_grads.append(
            grad_part
            + norm_back(normed_two, inverse_two, d_ff_in * gains_ff.astype(jnp.float32)[None])
        )
        share_a, share_b, share_c = (
            lax.psum_scatter(grad_norm_ff, ("dp", "pair"), scatter_dimension=0, tiled=True),
            lax.psum_scatter(grad_gate_up, ("dp", "pair"), scatter_dimension=0, tiled=True),
            lax.psum_scatter(grad_down, ("dp", "pair"), scatter_dimension=0, tiled=True),
        )
        share_norm_ff_parts.append(jnp.transpose(share_a))
        share_gate_up_parts.append(back_layout(share_b))
        share_down_parts.append(back_layout(share_c))
    d_mid = jnp.concatenate(mid_grads, axis=1)
    gains_attn, qkv_full, out_full = (
        lax.all_gather(norm_attn, ("dp", "pair"), axis=1, tiled=True),
        lax.all_gather(w_qkv, ("dp", "pair"), axis=1, tiled=True),
        lax.all_gather(w_out, ("dp", "pair"), axis=1, tiled=True),
    )
    d_mid_low = d_mid.astype(jnp.bfloat16)
    grad_out_proj = pos_grad(context, d_mid_low)
    d_context = per_pos_back(d_mid_low, out_full).astype(jnp.bfloat16).reshape(head_shape)
    d_probs = jnp.einsum(
        "fphd,fqhd->fhpq", d_context, value_heads, preferred_element_type=jnp.float32
    )
    d_values = jnp.einsum(
        "fhpq,fphd->fqhd", probs_low, d_context, preferred_element_type=jnp.float32
    )
    d_scores = attn_probs * (d_probs - jnp.sum(attn_probs * d_probs, axis=-1, keepdims=True))
    d_scores = d_scores.astype(jnp.bfloat16)
    d_queries = (
        jnp.einsum("fhpq,fqhd->fphd", d_scores, key_heads, preferred_element_type=jnp.float32)
        * score_scale
    )
    d_keys = (
        jnp.einsum("fhpq,fphd->fqhd", d_scores, queries, preferred_element_type=jnp.float32)
        * score_scale
    )
    row_shape = (frame_count, positions, model_width)
    d_qkv = jnp.concatenate(
        [d_queries.reshape(row_shape), d_keys.reshape(row_shape), d_values.reshape(row_shape)],
        axis=-1,
    ).astype(jnp.bfloat16)
    grad_qkv = pos_grad(attn_in, d_qkv)
    d_attn_in = per_pos_back(d_qkv, qkv_full)
    grad_norm_attn = gain_grad(normed_one, d_attn_in)
    grad_tokens = d_mid + norm_back(
        normed_one, inverse_one, d_attn_in * gains_attn.astype(jnp.float32)[None]
    )
    share_norm_attn, share_qkv, share_out = (
        lax.psum_scatter(grad_norm_attn, ("dp", "pair"), scatter_dimension=0, tiled=True),
        lax.psum_scatter(grad_qkv, ("dp", "pair"), scatter_dimension=0, tiled=True),
        lax.psum_scatter(grad_out_proj, ("dp", "pair"), scatter_dimension=0, tiled=True),
    )
    share_norm_attn = jnp.transpose(share_norm_attn)
    share_qkv = back_layout(share_qkv)
    share_out = back_layout(share_out)
    share_norm_ff = jnp.concatenate(share_norm_ff_parts, axis=0)
    share_gate_up = jnp.concatenate(share_gate_up_parts, axis=0)
    share_down = jnp.concatenate(share_down_parts, axis=0)
    return (
        output,
        grad_tokens,
        share_norm_attn,
        share_qkv,
        share_out,
        share_norm_ff,
        share_gate_up,
        share_down,
    )


MESH_ID = pl.DeviceIdType.MESH
BF16 = jnp.bfloat16
F32 = jnp.float32


def here():
    dp = lax.axis_index("dp")
    core = lax.axis_index("pair")
    return lax.div(dp, 4), lax.rem(lax.div(dp, 2), 2), lax.rem(dp, 2), core


def flip(value, bit):
    return 1 - value if bit else value


def push(src, dst, send_sem, recv_sem, to):
    return pltpu.make_async_remote_copy(
        src_ref=src,
        dst_ref=dst,
        send_sem=send_sem,
        recv_sem=recv_sem,
        device_id=to,
        device_id_type=MESH_ID,
    )


def arrived(dst, recv_sem, to):
    push(dst, dst, recv_sem, recv_sem, to).wait_recv()


def greet_all(z, y, x, core):
    barrier = pltpu.get_barrier_semaphore()
    me = 2 * (z * 4 + y * 2 + x) + core

    def one(step, carry):
        other = lax.rem(me + step, 32)
        pl.semaphore_signal(
            barrier, inc=1, device_id=(lax.div(other, 2), lax.rem(other, 2)), device_id_type=MESH_ID
        )
        return carry

    lax.fori_loop(1, 32, one, 0)
    pl.semaphore_wait(barrier, 31)


def greet(peers):
    barrier = pltpu.get_barrier_semaphore()
    for to in peers:
        pl.semaphore_signal(barrier, inc=1, device_id=to, device_id_type=MESH_ID)
    pl.semaphore_wait(barrier, len(peers))


def maybe(condition, do):
    if condition is None:
        do()
    else:
        pl.when(condition)(do)


OFFSETS = [
    (dz, dy, dx) for dz in (0, -1, 1, -2, 2, -3, 3) for dy in (0, 1) for dx in (0, 1)
]
ORDERS = ("zxy", "zyx", "zyx", "yxz")


def hops(offset):
    return abs(offset[0]) + offset[1] + offset[2]


def arrival_axis(order, offset):
    part = dict(z=offset[0], y=offset[1], x=offset[2])
    last = None
    for axis in order:
        if part[axis] != 0:
            last = axis
    return last


def onward(order, offset):
    directions = []
    last = arrival_axis(order, offset)
    start = 0
    if last is not None:
        start = order.index(last) + 1
        if last == "z":
            directions.append("u" if offset[0] < 0 else "d")
    for axis in order[start:]:
        directions.extend(["u", "d"] if axis == "z" else [axis])
    return directions


def came_from(order, offset):
    last = arrival_axis(order, offset)
    if last == "z":
        return "d" if offset[0] < 0 else "u"
    return last


def offset_exists(offset, z):
    if offset[0] < 0:
        return z >= -offset[0]
    if offset[0] > 0:
        return z <= 3 - offset[0]
    return None


def direction_exists(direction, z):
    return {"u": z < 3, "d": z > 0}.get(direction)


def return_count(order, direction, level):
    return sum(
        hops(offset) > 0 and came_from(order, offset) == direction
        for offset in OFFSETS
        if 0 <= level + offset[0] <= 3
    )


def tree_count(order, direction, level):
    return sum(
        direction in onward(order, offset) for offset in OFFSETS if 0 <= level + offset[0] <= 3
    )


DIRECTIONS = ("x", "y", "u", "d", "s")


def neighbour(direction, z, y, x, core):
    if direction == "x":
        return (z * 4 + y * 2 + 1 - x, core)
    if direction == "y":
        return (z * 4 + (1 - y) * 2 + x, core)
    if direction == "u":
        return (z * 4 + 4 + y * 2 + x, core)
    if direction == "d":
        return (z * 4 - 4 + y * 2 + x, core)
    return (z * 4 + y * 2 + x, 1 - core)


def chip_of(offset, z, y, x):
    return (z + offset[0]) * 4 + flip(y, offset[1]) * 2 + flip(x, offset[2])


RANK_STEPS = sorted(
    ((dl, dx, dc) for dl in (0, 1) for dx in (0, 1) for dc in (0, 1)), key=lambda step: (sum(step), step)
)


def group_place(z, y, x, core):
    zh, zl = lax.div(z, 2), lax.rem(z, 2)

    def member(step):
        return ((2 * zh + flip(zl, step[0])) * 4 + y * 2 + flip(x, step[1]), flip(core, step[2]))

    def rank(step):
        return 4 * flip(zl, step[0]) + 2 * flip(x, step[1]) + flip(core, step[2])

    def device(step, dzh=0, dy=0):
        return 16 * flip(zh, dzh) + 4 * flip(y, dy) + 8 * flip(zl, step[0]) + 2 * flip(x, step[1]) + flip(core, step[2])

    far = ((2 * (1 - zh) + zl) * 4 + y * 2 + x, core)
    across = (z * 4 + (1 - y) * 2 + x, core)
    return zh, zl, member, rank, device, far, across


def add_into(target, sources, rows=16, columns=1024):
    height, width = target.shape
    across = width // columns

    def one(step, carry):
        top = pl.multiple_of(lax.div(step, across) * rows, rows)
        left = pl.multiple_of(lax.rem(step, across) * columns, columns)
        spot = (pl.ds(top, rows), pl.ds(left, columns))
        total = sources[0][spot].astype(F32)
        for source in sources[1:]:
            total = total + source[spot].astype(F32)
        target[spot] = total.astype(target.dtype)
        return carry

    lax.fori_loop(0, (height // rows) * across, one, 0)


def row_loop(height, chunk, body):
    def one(step, carry):
        body(pl.ds(pl.multiple_of(step * chunk, chunk), chunk))
        return carry

    lax.fori_loop(0, height // chunk, one, 0)


def tile_loop(width, tile, body):
    def one(step, carry):
        body(pl.ds(pl.multiple_of(step * tile, tile), tile))
        return carry

    lax.fori_loop(0, width // tile, one, 0)


def dot(left, right):
    return jnp.dot(left, right, preferred_element_type=F32)


def dot_back(left, right):
    return lax.dot_general(left, right, (((1,), (1,)), ((), ())), preferred_element_type=F32)


def dot_grad(left, right):
    return lax.dot_general(left, right, (((0,), (0,)), ((), ())), preferred_element_type=F32)


def make_spread(spread):
    height, width = spread.shape
    head = lax.broadcasted_iota(jnp.int32, (height, width), 0) // HEAD_DIM
    spread[...] = jnp.where(
        head == lax.broadcasted_iota(jnp.int32, (height, width), 1), 1.0, 0.0
    ).astype(BF16)


def pairs_of(positions):
    return [(p, q) for p in range(positions) for q in range(p + 1)]


def split_product(product):
    high = product.astype(BF16)
    return high, (product - high.astype(F32)).astype(BF16)


def sums_over_heads(halves, spread, index):
    return dot(halves[2 * index], spread[...]) + dot(halves[2 * index + 1], spread[...])


def to_heads(values, spread):
    return dot_back(values, spread[...]).astype(BF16)


def attention_probs(qkv, halves, spread, model, position):
    height = qkv.shape[1]
    scale = 1.0 / math.sqrt(HEAD_DIM)

    def products(rows):
        for q in range(position + 1):
            product = qkv[position, rows, :model].astype(F32) * qkv[
                q, rows, model : 2 * model
            ].astype(F32)
            halves[2 * q, rows, :], halves[2 * q + 1, rows, :] = split_product(product)

    row_loop(height, 16, products)
    scores = [sums_over_heads(halves, spread, q) * scale for q in range(position + 1)]
    top = functools.reduce(jnp.maximum, scores)
    powers = [jnp.exp(score - top) for score in scores]
    total = functools.reduce(jnp.add, powers)
    return [power / total for power in powers]


(
    F_TREE,
    F_TREE_END,
    F_GAINS,
    F_PARTS,
    F_COT,
    F_ATTENTION,
    F_GRADS,
    F_ACT_Z,
    F_ACT_X,
    F_ACT_C,
    F_TO_RANK,
    F_OWN_FAR,
    F_OWN_ACROSS,
    F_RANK_FAR,
    F_RANK_ACROSS,
    F_FAR_ACROSS,
    F_FF_END,
    F_BLOCK,
    F_GATE_GRAD,
    F_DOWN_GRAD,
) = range(20)
FORWARD_STEPS = [
    (F_TREE, 0, 0, 0, 0), (F_TREE, 2, 0, 0, 0), (F_COT,), (F_PARTS,), (F_TREE, 1, 0, 0, 0), (F_TO_RANK, 0, 3),
    (F_OWN_ACROSS, 0, 8), (F_TREE, 4, 0, 0, 0), (F_TREE, 3, 0, 0, 0), (F_TREE, 2, 0, 1, 0),
    (F_TREE, 0, -1, 0, 0), (F_TO_RANK, 0, 7), (F_TO_RANK, 1, 5), (F_TO_RANK, 0, 1), (F_TREE, 0, 0, 0, 1),
    (F_GAINS,), (F_TO_RANK, 0, 6), (F_RANK_FAR, 0, 3), (F_TO_RANK, 0, 2), (F_TREE, 1, 1, 0, 0),
    (F_TO_RANK, 0, 4), (F_TREE, 2, 1, 0, 0), (F_TREE, 2, -1, 0, 0), (F_TREE, 5, 0, 0, 0), (F_TREE, 2, 2, 0, 0),
    (F_TREE, 3, 0, 0, 1), (F_TREE, 1, -1, 0, 0), (F_TO_RANK, 1, 2), (F_TREE, 0, -2, 0, 0), (F_OWN_ACROSS, 1, 8),
    (F_TREE, 1, 0, 1, 0), (F_RANK_FAR, 0, 1), (F_TREE, 0, 1, 0, 0), (F_RANK_FAR, 0, 6), (F_TREE, 2, 1, 0, 1),
    (F_TREE, 2, -2, 0, 0), (F_RANK_FAR, 0, 7), (F_TREE, 0, 2, 0, 0), (F_TREE, 1, -2, 0, 0),
    (F_TREE, 0, -2, 0, 1), (F_OWN_FAR, 0, 8), (F_OWN_FAR, 0, 0), (F_TREE, 1, 2, 0, 0), (F_TREE, 0, -1, 0, 1),
    (F_GRADS, 0), (F_TO_RANK, 1, 4), (F_TREE, 3, -1, 0, 0), (F_TREE, 4, 1, 0, 0), (F_RANK_FAR, 0, 2),
    (F_TREE, 1, -2, 1, 0), (F_RANK_ACROSS, 0, 3), (F_TREE, 1, -3, 0, 0), (F_TREE, 2, 3, 0, 0),
    (F_TREE, 3, 1, 0, 0), (F_TREE, 2, 2, 1, 0), (F_TREE, 2, -2, 1, 0), (F_TREE, 2, -3, 0, 0),
    (F_TREE, 0, 0, 1, 1), (F_TREE, 5, 0, 1, 0), (F_TREE, 0, -1, 1, 1), (F_TREE, 0, 3, 0, 0),
    (F_TREE, 2, 0, 0, 1), (F_TREE, 0, -3, 0, 0), (F_TREE, 3, 0, 1, 1), (F_TREE, 2, 1, 1, 0),
    (F_TREE, 0, 2, 0, 1), (F_TREE, 1, 3, 0, 0), (F_TREE, 1, 2, 1, 0), (F_TREE, 0, 1, 1, 0), (F_ACT_X, 1, 0, 0),
    (F_TO_RANK, 0, 5), (F_TREE, 2, -1, 1, 0), (F_TREE, 2, -2, 0, 1), (F_RANK_ACROSS, 0, 1),
    (F_TREE, 0, 1, 0, 1), (F_RANK_FAR, 0, 4), (F_TREE, 5, 0, 0, 1), (F_TREE, 3, -2, 0, 0), (F_FAR_ACROSS, 0, 6),
    (F_TREE, 1, 2, 0, 1), (F_TREE, 4, -1, 0, 0), (F_FAR_ACROSS, 0, 7), (F_TREE, 1, 1, 1, 0),
    (F_TREE, 1, 3, 1, 0), (F_TREE, 4, 0, 1, 0), (F_TO_RANK, 1, 6), (F_TREE, 0, 1, 1, 1), (F_TREE, 2, -3, 0, 1),
    (F_FAR_ACROSS, 0, 3), (F_ACT_C, 1, 0, 0, 1), (F_RANK_FAR, 0, 5), (F_TO_RANK, 1, 1), (F_TREE, 1, -1, 0, 1),
    (F_TREE, 0, 3, 0, 1), (F_TREE, 2, -1, 0, 1), (F_RANK_ACROSS, 0, 5), (F_TREE, 3, 2, 0, 0),
    (F_TREE, 3, -1, 1, 0), (F_TREE, 3, 1, 0, 1), (F_RANK_ACROSS, 0, 6), (F_TREE, 0, -2, 1, 1),
    (F_TREE, 1, -3, 1, 0), (F_TREE, 5, 1, 0, 0), (F_TREE, 1, -1, 1, 0), (F_TREE, 1, -2, 1, 1),
    (F_TREE, 5, 0, 1, 1), (F_ACT_Z, 1, 0), (F_TREE, 2, 3, 1, 0), (F_TREE, 0, 3, 1, 0), (F_TREE, 3, 3, 0, 0),
    (F_FAR_ACROSS, 0, 4), (F_TREE, 4, -2, 0, 0), (F_TREE, 3, 0, 1, 0), (F_TREE, 0, -3, 0, 1),
    (F_TREE, 0, 2, 1, 0), (F_TREE, 5, -1, 0, 0), (F_TREE, 1, 3, 1, 1), (F_TREE, 4, 2, 0, 0),
    (F_TREE, 1, -3, 1, 1), (F_ACT_C, 1, 0, 1, 0), (F_TREE, 1, 0, 0, 1), (F_TREE, 0, -1, 1, 0),
    (F_FAR_ACROSS, 0, 2), (F_OWN_FAR, 1, 8), (F_TREE, 2, -2, 1, 1), (F_TREE, 0, 0, 1, 0), (F_TREE, 0, 3, 1, 1),
    (F_RANK_ACROSS, 0, 7), (F_TREE, 1, 0, 1, 1), (F_TREE, 4, 1, 0, 1), (F_RANK_FAR, 1, 4),
    (F_TREE, 2, -1, 1, 1), (F_FAR_ACROSS, 0, 8), (F_GRADS, 1), (F_TREE, 3, -2, 0, 1), (F_TREE, 3, 1, 1, 1),
    (F_TREE, 5, 1, 0, 1), (F_TREE, 3, 3, 1, 0), (F_TREE, 2, 1, 1, 1), (F_TREE, 2, -3, 1, 0),
    (F_TREE, 1, 1, 0, 1), (F_TREE, 4, 2, 1, 0), (F_TO_RANK, 1, 3), (F_TREE, 4, 3, 0, 0), (F_TREE, 5, 1, 1, 0),
    (F_TREE, 4, -3, 0, 0), (F_TREE, 5, -1, 0, 1), (F_TREE, 3, -2, 1, 0), (F_FAR_ACROSS, 0, 0),
    (F_TREE, 3, -3, 0, 0), (F_TREE, 4, -1, 1, 0), (F_FAR_ACROSS, 0, 1), (F_TREE, 1, 2, 1, 1),
    (F_TREE, 0, -2, 1, 0), (F_TREE, 2, 3, 1, 1), (F_FAR_ACROSS, 0, 5), (F_TREE, 1, 1, 1, 1),
    (F_TREE, 2, 2, 1, 1), (F_TREE, 4, -2, 1, 0), (F_TREE, 2, -3, 1, 1), (F_TREE, 2, 2, 0, 1),
    (F_TREE, 2, 3, 0, 1), (F_TREE, 2, 0, 1, 1), (F_TREE, 0, 2, 1, 1), (F_TREE, 4, -3, 1, 0),
    (F_TREE, 4, -3, 0, 1), (F_TREE, 0, -3, 1, 1), (F_FAR_ACROSS, 1, 8), (F_RANK_FAR, 1, 2),
    (F_TREE, 1, -1, 1, 1), (F_TREE, 0, -3, 1, 0), (F_TREE, 3, -1, 0, 1), (F_TREE, 1, -2, 0, 1),
    (F_TREE, 4, 0, 1, 1), (F_TO_RANK, 1, 7), (F_OWN_ACROSS, 1, 0), (F_TREE, 1, 3, 0, 1), (F_ACT_X, 1, 0, 1),
    (F_TREE, 3, 2, 0, 1), (F_TREE, 1, -3, 0, 1), (F_TREE_END, 0), (F_TREE, 4, -1, 0, 1), (F_TREE, 5, -1, 1, 0),
    (F_TREE, 4, 3, 1, 0), (F_ATTENTION, 0), (F_TREE, 5, 1, 1, 1), (F_TREE, 3, 2, 1, 0), (F_TREE, 5, -2, 1, 0),
    (F_TREE, 5, 2, 1, 0), (F_TREE, 5, -1, 1, 1), (F_TREE, 3, 3, 0, 1), (F_RANK_ACROSS, 0, 4),
    (F_TREE, 3, -3, 0, 1), (F_TREE, 4, -1, 1, 1), (F_TREE, 4, 2, 0, 1), (F_TREE, 5, -2, 0, 1),
    (F_TREE, 5, -2, 0, 0), (F_TREE, 4, 2, 1, 1), (F_TREE, 4, 1, 1, 0), (F_TREE, 4, -3, 1, 1), (F_ACT_Z, 0, 0),
    (F_FAR_ACROSS, 1, 2), (F_RANK_ACROSS, 0, 2), (F_TREE, 5, 2, 0, 1), (F_RANK_FAR, 1, 7), (F_TREE, 5, 2, 0, 0),
    (F_OWN_FAR, 1, 0), (F_OWN_ACROSS, 0, 0), (F_TREE, 5, -2, 1, 1), (F_RANK_ACROSS, 1, 4), (F_RANK_FAR, 1, 3),
    (F_ACT_X, 0, 0, 0), (F_TREE, 5, 3, 0, 1), (F_RANK_ACROSS, 1, 2), (F_ACT_Z, 1, 1), (F_TREE, 4, 0, 0, 1),
    (F_TREE, 3, 3, 1, 1), (F_TREE, 5, 2, 1, 1), (F_RANK_FAR, 1, 5), (F_TREE, 4, 3, 1, 1), (F_ACT_C, 1, 0, 1, 1),
    (F_RANK_ACROSS, 1, 5), (F_FAR_ACROSS, 1, 4), (F_TREE, 5, -3, 0, 1), (F_TREE, 5, 3, 1, 0),
    (F_TREE, 5, 3, 0, 0), (F_TREE, 3, -3, 1, 1), (F_RANK_FAR, 1, 6), (F_TREE, 4, -2, 1, 1), (F_RANK_FAR, 1, 1),
    (F_ACT_C, 1, 0, 0, 0), (F_TREE, 3, -1, 1, 1), (F_TREE, 3, -2, 1, 1), (F_TREE, 3, 2, 1, 1), (F_FF_END, 0),
    (F_ACT_C, 1, 1, 0, 0), (F_TREE, 4, 1, 1, 1), (F_TREE, 4, -2, 0, 1), (F_ACT_C, 0, 0, 1, 0),
    (F_ACT_C, 0, 0, 0, 1), (F_BLOCK, 0, 2), (F_FAR_ACROSS, 1, 7), (F_TREE, 4, 3, 0, 1), (F_RANK_ACROSS, 1, 1),
    (F_RANK_ACROSS, 1, 7), (F_TREE, 5, -3, 1, 0), (F_TREE, 3, -3, 1, 0), (F_TREE, 3, 1, 1, 0),
    (F_TREE, 5, -3, 0, 0), (F_TREE, 5, 3, 1, 1), (F_BLOCK, 0, 1), (F_ACT_C, 0, 0, 0, 0), (F_RANK_ACROSS, 1, 3),
    (F_TREE, 5, -3, 1, 1), (F_ACT_X, 1, 1, 0), (F_ACT_X, 0, 0, 1), (F_TREE_END, 1), (F_RANK_ACROSS, 1, 6),
    (F_ATTENTION, 1), (F_FAR_ACROSS, 1, 3), (F_ACT_C, 1, 1, 0, 1), (F_ACT_X, 1, 1, 1), (F_FAR_ACROSS, 1, 0),
    (F_BLOCK, 0, 0), (F_ACT_C, 0, 0, 1, 1), (F_BLOCK, 0, 3), (F_ACT_C, 1, 1, 1, 1), (F_FAR_ACROSS, 1, 1),
    (F_FAR_ACROSS, 1, 5), (F_DOWN_GRAD, 0), (F_ACT_Z, 0, 1), (F_ACT_C, 0, 1, 0, 0), (F_ACT_X, 0, 1, 0),
    (F_FAR_ACROSS, 1, 6), (F_GATE_GRAD, 0), (F_ACT_C, 1, 1, 1, 0), (F_ACT_C, 0, 1, 0, 1), (F_ACT_C, 0, 1, 1, 0),
    (F_FF_END, 1), (F_BLOCK, 1, 1), (F_BLOCK, 1, 2), (F_ACT_X, 0, 1, 1), (F_BLOCK, 1, 0), (F_ACT_C, 0, 1, 1, 1),
    (F_BLOCK, 1, 3), (F_DOWN_GRAD, 1), (F_GATE_GRAD, 1),
]


def forward_kernel(
    valid_ref,
    lengths_ref,
    norm_attn_ref,
    norm_ff_ref,
    tokens_ref,
    cot_ref,
    qkv_ref,
    out_ref,
    gate_up_ref,
    down_ref,
    gain_rows,
    cot_rows,
    qkv_rows,
    context,
    resid_mid,
    qkv_full,
    out_full,
    ff_out,
    ff_back,
    gate_up_grad,
    down_grad,
    qkv_buf,
    out_buf,
    gate_up_buf,
    down_buf,
    rows_buf,
    grads_buf,
    hidden,
    d_gate_up,
    out_stage,
    back_stage,
    gate_up_stage,
    down_stage,
    gains_own,
    gains_all,
    gate_up_raw,
    gate_up_parts,
    grads_own,
    attn_in,
    halves,
    spread,
    plane_sem,
    sibling_sem,
    send_sem,
    gains_send,
    gains_recv,
    rank_send,
    rank_recv,
    far_send,
    far_recv,
    across_send,
    across_recv,
    act_send,
    act_recv,
    local_sem,
    keep_sem,
    stage_sem,
):
    z, y, x, core = here()
    me = 2 * (z * 4 + y * 2 + x) + core
    zh, zl, member, rank, device, far, across = group_place(z, y, x, core)
    own_step = (0, 0, 0)
    act_height, positions, model = tokens_ref.shape
    height = gate_up_ref.shape[1]
    down_height = down_ref.shape[1]
    split = 4 * down_height
    sibling = neighbour("s", z, y, x, core)
    greet_all(z, y, x, core)
    part = qkv_ref.shape[2] * 12 // 24
    rest = qkv_ref.shape[2] - part
    pieces = []
    for s in range(positions):
        pieces.append((qkv_ref, qkv_buf, s, pl.ds(0, part), "zxy"))
        pieces.append((qkv_ref, qkv_buf, s, pl.ds(part, rest), "zyx"))
        pieces.append((out_ref, out_buf, s, pl.ds(0, model), ("zyx", "yxz")[s % 2]))

    def piece_rows(piece, number):
        _, full, index, columns, _ = pieces[piece]
        return full.at[index, pl.ds(pl.multiple_of(number * height, height), height), columns]

    def tree_send(piece, offset, direction):
        source, _, index, columns, _ = pieces[piece]
        chip = chip_of(offset, z, y, x)
        block = piece_rows(piece, 2 * chip + core)
        return push(
            source.at[index, :, columns] if hops(offset) == 0 else block,
            block,
            send_sem.at[piece, DIRECTIONS.index(direction)],
            sibling_sem.at[piece] if direction == "s" else plane_sem.at[piece, chip],
            neighbour(direction, z, y, x, core),
        )

    def tree_step(piece, offset):
        order = pieces[piece][4]

        def go():
            chip = chip_of(offset, z, y, x)
            if hops(offset) > 0:
                arrived(piece_rows(piece, 2 * chip + core), plane_sem.at[piece, chip], sibling)
            for direction in onward(order, offset) + ["s"]:
                copy = tree_send(piece, offset, direction)
                maybe(direction_exists(direction, z), copy.start)

        maybe(offset_exists(offset, z), go)

    def tree_bytes(piece, count):
        _, full, index, columns, _ = pieces[piece]
        return full.at[index, pl.ds(0, count * height), columns]

    def tree_sent(piece):
        order = pieces[piece][4]

        def sent(direction, count):
            block = tree_bytes(piece, count)
            push(block, block, send_sem.at[piece, DIRECTIONS.index(direction)], gains_recv, sibling).wait_send()

        sent("s", 16)
        for direction in "xy":
            sent(direction, tree_count(order, direction, 3))
        for direction in "ud":
            for level in range(4):
                if level != (3 if direction == "u" else 0):
                    pl.when(z == level)(
                        functools.partial(sent, direction, tree_count(order, direction, level))
                    )

    def tree_end(s):
        mine = [piece for piece in range(len(pieces)) if pieces[piece][2] == s]

        for piece in mine:
            arrived(tree_bytes(piece, 16), sibling_sem.at[piece], sibling)
        for piece in mine:
            tree_own[piece].wait()

    tree_own = [
        pltpu.make_async_copy(
            source.at[index, :, columns], piece_rows(piece, me), local_sem.at[piece]
        )
        for piece, (source, _, index, columns, _) in enumerate(pieces)
    ]

    def gains_copy(step):
        other = lax.rem(me + step, 32)
        return push(
            gains_own,
            gains_all.at[me],
            gains_send,
            gains_recv,
            (lax.div(other, 2), lax.rem(other, 2)),
        )

    def gains_start(step, carry):
        gains_copy(step).start()
        return carry

    def start(copy):
        copy.start()

    def weight_rows(s, number):
        return gate_up_buf.at[s, pl.ds(pl.multiple_of(number * height, height), height), :]

    def down_rows(s, dzh, dy):
        number = 2 * flip(zh, dzh) + flip(y, dy)
        return down_buf.at[s, pl.ds(pl.multiple_of(number * down_height, down_height), down_height), :]

    def act_rows(which, s, step):
        full = (rows_buf, grads_buf)[which]
        return full.at[s, pl.ds(pl.multiple_of(rank(step) * act_height, act_height), act_height), :]

    def send_act(which, s, step, source, hop):
        landed = tuple(bit ^ (1 if axis == hop else 0) for axis, bit in enumerate(step))
        start(
            push(
                source,
                act_rows(which, s, step),
                act_send.at[which, s, hop],
                act_recv.at[which, s, 4 * landed[0] + 2 * landed[1] + landed[2]],
                member(tuple(1 if axis == hop else 0 for axis in range(3))),
            )
        )

    def wait_act(which, s, step):
        arrived(
            act_rows(which, s, step),
            act_recv.at[which, s, 4 * step[0] + 2 * step[1] + step[2]],
            sibling,
        )

    def act_own(which, s):
        source = act_rows(0, s, own_step) if which == 0 else grads_own.at[s]
        for hop in (0, 1, 2):
            send_act(which, s, own_step, source, hop)

    def act_from_z(which, s):
        step = (1, 0, 0)
        wait_act(which, s, step)
        send_act(which, s, step, act_rows(which, s, step), 1)
        send_act(which, s, step, act_rows(which, s, step), 2)

    def act_from_x(which, s, dl):
        wait_act(which, s, (dl, 1, 0))
        send_act(which, s, (dl, 1, 0), act_rows(which, s, (dl, 1, 0)), 2)

    def act_from_core(which, s, dl, dx):
        wait_act(which, s, (dl, dx, 1))

    def mine(s):
        return gate_up_parts.at[rank(own_step), s]

    def ff_source(s, slot):
        return down_ref.at[s] if slot == 8 else mine(s)

    def ff_rows(s, slot, dzh):
        return down_rows(s, dzh, 0) if slot == 8 else weight_rows(s, device(RANK_STEPS[slot], dzh, 0))

    def to_rank(s, slot):
        step = RANK_STEPS[slot]
        start(
            push(
                gate_up_parts.at[rank(step), s],
                weight_rows(s, device(own_step)),
                rank_send.at[s],
                rank_recv.at[s, slot],
                member(step),
            )
        )

    def send_far(s, slot, source):
        start(push(source, ff_rows(s, slot, 0), far_send.at[s], far_recv.at[s, slot], far))

    def send_across(s, slot, source, dzh):
        start(
            push(
                source,
                ff_rows(s, slot, dzh),
                across_send.at[s],
                across_recv.at[s],
                across,
            )
        )

    def own_far(s, slot):
        send_far(s, slot, ff_source(s, slot))

    def own_across(s, slot):
        send_across(s, slot, ff_source(s, slot), 0)

    def rank_far(s, slot):
        arrived(ff_rows(s, slot, 0), rank_recv.at[s, slot], sibling)
        send_far(s, slot, ff_rows(s, slot, 0))

    def rank_across(s, slot):
        send_across(s, slot, ff_rows(s, slot, 0), 0)

    def far_across(s, slot):
        arrived(ff_rows(s, slot, 1), far_recv.at[s, slot], sibling)
        send_across(s, slot, ff_rows(s, slot, 1), 1)

    def ff_end(s):
        for copy in ff_local[s]:
            copy.wait()
        arrived(ff_bytes(s, 2 * share), across_recv.at[s], sibling)

    share = 8 * height + down_height * model // gate_up_buf.shape[2]

    def ff_bytes(s, rows):
        return gate_up_buf.at[s, pl.ds(0, rows), :]

    def ff_sent(s):
        for sem, rows in ((rank_send, 7 * height), (far_send, share), (across_send, 2 * share)):
            block = ff_bytes(s, rows)
            push(block, block, sem.at[s], gains_recv, sibling).wait_send()
        for which, full in enumerate((rows_buf, grads_buf)):
            for hop, count in enumerate((1, 2, 4)):
                block = full.at[s, pl.ds(0, count * act_height), :]
                push(block, block, act_send.at[which, s, hop], gains_recv, sibling).wait_send()

    ff_local = []
    for s in range(positions):
        ff_local.append(
            [
                pltpu.make_async_copy(mine(s), weight_rows(s, device(own_step)), local_sem.at[7 + 3 * s]),
                pltpu.make_async_copy(down_ref.at[s], down_rows(s, 0, 0), local_sem.at[8 + 3 * s]),
                pltpu.make_async_copy(grads_own.at[s], act_rows(1, s, own_step), local_sem.at[9 + 3 * s]),
            ]
        )
    gains_local = pltpu.make_async_copy(gains_own, gains_all.at[me], local_sem.at[6])

    def gains_begin():
        places = 128 // norm_attn_ref.shape[1]
        lane = lax.broadcasted_iota(jnp.int32, (positions, 128), 1) // norm_attn_ref.shape[1]
        gains_own[...] = jnp.zeros_like(gains_own)
        for index, source in enumerate((norm_attn_ref, norm_ff_ref)):
            tiled = jnp.concatenate([source[...].astype(F32)] * places, axis=1)
            gains_own[index * positions : (index + 1) * positions, :] = jnp.where(
                lane == lax.rem(me, places), tiled, 0.0
            ).astype(BF16)
        lax.fori_loop(1, 32, gains_start, 0)
        gains_local.start()

    raw_copy = pltpu.make_async_copy(gate_up_ref, gate_up_raw, local_sem.at[13])

    def part_units():
        raw_copy.wait()
        unit = down_height
        for number in range(8):
            low, rest = divmod(number, 4)
            for s in range(positions):
                for side in (0, 1):
                    for group in range(4):
                        zh_part, y_part = divmod(group, 2)
                        block = 32 * side + 16 * zh_part + 8 * low + 4 * y_part + rest
                        gate_up_parts[number, s, :, (4 * side + group) * unit : (4 * side + group + 1) * unit] = (
                            gate_up_raw[s, :, block * unit : (block + 1) * unit]
                        )
        for s in range(positions):
            ff_local[s][0].start()
            ff_local[s][1].start()

    def weigh():
        def one(rows):
            slot = lax.broadcasted_iota(jnp.int32, (16, 128), 0) + rows.start
            frame = me * act_height + slot
            weight = jnp.zeros((16, 128), F32)
            first = 0
            for item in range(lengths_ref.shape[0]):
                length = lengths_ref[item]
                inside = (frame >= first) & (frame < first + length)
                share = 8.0 * act_height / jnp.full((16, 128), length, jnp.int32).astype(F32)
                weight = weight + jnp.where(inside, share, 0.0)
                first = first + length
            weight = jnp.where(slot < valid_ref[0], weight, 0.0)[:, :1]
            values = cot_ref[rows].astype(F32)
            for p in range(positions):
                grads = values[:, p, :] * weight
                cot_rows[p, rows, :] = grads
                grads_own[p, rows, :] = grads.astype(BF16)

        row_loop(act_height, 16, one)
        for s in range(positions):
            ff_local[s][2].start()

    def take_gains():
        others = gains_all.at[pl.ds(0, 31)]
        arrived(others, gains_recv, sibling)
        push(others, others, gains_send, gains_recv, sibling).wait_send()
        gains_local.wait()
        for block in range(8):
            total = gains_all[4 * block].astype(F32)
            for extra in range(1, 4):
                total = total + gains_all[4 * block + extra].astype(F32)
            gain_rows[:, 128 * block : 128 * block + 128] = total

        def first_norm(rows):
            values = tokens_ref[rows].astype(F32)
            for p in range(positions):
                resid_mid[p, rows, :] = values[:, p, :]
                r, _ = normed(values[:, p, :])
                attn_in[p, rows, :] = (r * gain_rows[p : p + 1, :]).astype(BF16)

        row_loop(act_height, 16, first_norm)

    keep = []

    def attention(p):
        for source, target, slot in (
            (qkv_buf.at[p], qkv_full.at[p], 2 * p),
            (out_buf.at[p], out_full.at[p], 2 * p + 1),
        ):
            keep.append(pltpu.make_async_copy(source, target, keep_sem.at[slot]))
            keep[-1].start()

        def project(columns):
            qkv_rows[p, :, columns] = dot(attn_in[p], qkv_buf[p, :, columns]).astype(BF16)

        tile_loop(3 * model, 512, project)
        probs = attention_probs(qkv_rows, halves, spread, model, p)
        for q in range(p + 1):
            halves[2 * q] = to_heads(probs[q].astype(BF16), spread)

        def mix(rows):
            total = None
            for q in range(p + 1):
                term = halves[2 * q, rows, :].astype(F32) * qkv_rows[q, rows, 2 * model :].astype(F32)
                total = term if total is None else total + term
            context[p, rows, :] = total.astype(BF16)

        row_loop(act_height, 16, mix)

        def attend(columns):
            resid_mid[p, :, columns] += dot(context[p], out_buf[p, :, columns])

        tile_loop(model, 512, attend)

        def second_norm(step, carry):
            rows = pl.ds(pl.multiple_of(step * 16, 16), 16)
            r, _ = normed(resid_mid[p, rows, :])
            top = rank(own_step) * act_height + step * 16
            rows_buf[p, pl.ds(pl.multiple_of(top, 16), 16), :] = (
                r * gain_rows[positions + p : positions + p + 1, :]
            ).astype(BF16)
            return carry

        lax.fori_loop(0, act_height // 16, second_norm, 0)

    def ff_block(s, number):
        rows = pl.ds(pl.multiple_of(number * 2 * act_height, 2 * act_height), 2 * act_height)
        normed_rows = rows_buf[s, rows, :]
        grads = grads_buf[s, rows, :]
        for tile in range(split // 256):
            left, right = pl.ds(tile * 256, 256), pl.ds(split + tile * 256, 256)
            gate = dot(normed_rows, gate_up_buf[s, :, left])
            up = dot(normed_rows, gate_up_buf[s, :, right])
            d_hidden = dot_back(grads, down_buf[s, left, :])
            sigmoid_gate = jax.nn.sigmoid(gate)
            silu_gate = gate * sigmoid_gate
            hidden[rows, left] = (silu_gate * up).astype(BF16)
            d_gate_up[rows, left] = (
                d_hidden * up * sigmoid_gate * (1.0 + gate * (1.0 - sigmoid_gate))
            ).astype(BF16)
            d_gate_up[rows, right] = (d_hidden * silu_gate).astype(BF16)
        for tile in range(model // 512):
            columns = pl.ds(tile * 512, 512)
            out_stage[rows, columns] = dot(hidden[rows, :], down_buf[s, :, columns]).astype(BF16)
            back_stage[rows, columns] = dot_back(
                d_gate_up[rows, :], gate_up_buf[s, columns, :]
            ).astype(BF16)

    stages = []

    def stage_out(s, *slots):
        for slot in slots:
            source, target = (
                (out_stage, ff_out),
                (back_stage, ff_back),
                (gate_up_stage, gate_up_grad),
                (down_stage, down_grad),
            )[slot]
            stages.append(pltpu.make_async_copy(source, target.at[s], stage_sem.at[s, slot]))
            stages[-1].start()

    def gate_grad(s):
        stage_out(s, 0, 1)

        def gate_up_tile(columns):
            gate_up_stage[:, columns] = dot_grad(rows_buf[s], d_gate_up[:, columns]).astype(BF16)

        tile_loop(2 * split, 256, gate_up_tile)
        stage_out(s, 2)

    def down_weights_grad(s):
        def down_tile(columns):
            down_stage[:, columns] = dot_grad(hidden[...], grads_buf[s, :, columns]).astype(BF16)

        tile_loop(model, 256, down_tile)
        stage_out(s, 3)

    def stages_end():
        while stages:
            stages.pop(0).wait()

    for copy in tree_own:
        copy.start()
    raw_copy.start()
    gains_begin()
    make_spread(spread)
    chips = ((0, 0), (1, 0), (0, 1), (1, 1))

    def block(s, order):
        if s > 0 and order == chosen_first[0]:
            stages_end()
        ff_block(s, 2 * flip(zl, chips[order][0]) + flip(x, chips[order][1]))

    def attend_and_send(s):
        attention(s)
        act_own(0, s)

    chosen_first = [step[2] for step in FORWARD_STEPS if step[:2] == (F_BLOCK, 1)]
    kinds = {
        F_TREE: lambda piece, dz, dy, dx: tree_step(piece, (dz, dy, dx)),
        F_TREE_END: tree_end,
        F_GAINS: take_gains,
        F_PARTS: part_units,
        F_COT: weigh,
        F_ATTENTION: attend_and_send,
        F_GRADS: lambda s: act_own(1, s),
        F_ACT_Z: act_from_z,
        F_ACT_X: act_from_x,
        F_ACT_C: act_from_core,
        F_TO_RANK: to_rank,
        F_OWN_FAR: own_far,
        F_OWN_ACROSS: own_across,
        F_RANK_FAR: rank_far,
        F_RANK_ACROSS: rank_across,
        F_FAR_ACROSS: far_across,
        F_FF_END: ff_end,
        F_BLOCK: block,
        F_GATE_GRAD: gate_grad,
        F_DOWN_GRAD: down_weights_grad,
    }
    for kind, *numbers in FORWARD_STEPS:
        kinds[kind](*numbers)
    for piece in range(len(pieces)):
        tree_sent(piece)
    for s in range(positions):
        ff_sent(s)
    for copy in keep:
        copy.wait()
    stages_end()


def forward_gather(valid, lengths, norm_attn, norm_ff, tokens, cot, w_qkv, w_out, w_gate_up, w_down):
    act_height, positions, model = tokens.shape
    _, height, qkv_width = w_qkv.shape
    unit = w_down.shape[1]
    ranks, split, width = 8, 4 * unit, 8 * unit
    group_rows = ranks * act_height
    dma = pltpu.SemaphoreType.DMA
    vmem = pl.BlockSpec(memory_space=pltpu.VMEM)
    smem = pl.BlockSpec(memory_space=pltpu.SMEM)
    anywhere = pl.BlockSpec(memory_space=pl.ANY)
    return pl.pallas_call(
        forward_kernel,
        out_shape=(
            jax.ShapeDtypeStruct((16, model), F32),
            jax.ShapeDtypeStruct((positions, act_height, model), F32),
            jax.ShapeDtypeStruct((positions, act_height, 3 * model), BF16),
            jax.ShapeDtypeStruct((positions, act_height, model), BF16),
            jax.ShapeDtypeStruct((positions, act_height, model), F32),
            jax.ShapeDtypeStruct((positions, model, qkv_width), BF16),
            jax.ShapeDtypeStruct((positions, model, model), BF16),
            jax.ShapeDtypeStruct((positions, group_rows, model), BF16),
            jax.ShapeDtypeStruct((positions, group_rows, model), BF16),
            jax.ShapeDtypeStruct((positions, model, width), BF16),
            jax.ShapeDtypeStruct((positions, split, model), BF16),
        ),
        in_specs=[smem] * 2 + [vmem] * 4 + [anywhere] * 4,
        out_specs=(vmem,) * 5 + (anywhere,) * 6,
        scratch_shapes=[
            pltpu.VMEM((positions, model, qkv_width), BF16),
            pltpu.VMEM((positions, model, model), BF16),
            pltpu.VMEM((positions, model, width), BF16),
            pltpu.VMEM((positions, split, model), BF16),
            pltpu.VMEM((positions, group_rows, model), BF16),
            pltpu.VMEM((positions, group_rows, model), BF16),
            pltpu.VMEM((group_rows, split), BF16),
            pltpu.VMEM((group_rows, width), BF16),
            pltpu.VMEM((group_rows, model), BF16),
            pltpu.VMEM((group_rows, model), BF16),
            pltpu.VMEM((model, width), BF16),
            pltpu.VMEM((split, model), BF16),
            pltpu.VMEM((16, 128), BF16),
            pltpu.VMEM((32, 16, 128), BF16),
            pltpu.VMEM(w_gate_up.shape, BF16),
            pltpu.VMEM((ranks, positions, height, width), BF16),
            pltpu.VMEM((positions, act_height, model), BF16),
            pltpu.VMEM((positions, act_height, model), BF16),
            pltpu.VMEM((2 * positions, act_height, model), BF16),
            pltpu.VMEM((model, 128), BF16),
            dma((6, 16)),
            dma((6,)),
            dma((6, 5)),
            dma,
            dma,
            dma((2,)),
            dma((2, 8)),
            dma((2,)),
            dma((2, 9)),
            dma((2,)),
            dma((2,)),
            dma((2, 2, 3)),
            dma((2, 2, 8)),
            dma((14,)),
            dma((4,)),
            dma((2, 4)),
        ],
        compiler_params=pltpu.CompilerParams(
            collective_id=4, has_side_effects=True, vmem_limit_bytes=62 * 2**20
        ),
        name="forward_gather",
    )(valid, lengths, norm_attn, norm_ff, tokens, cot, w_qkv, w_out, w_gate_up, w_down)


def slot_index(order, direction, offset, z, y, x):
    axis = {"u": "z", "d": "z"}.get(direction, direction)
    index, count = 0, 1
    values = dict(z=z + offset[0], y=flip(y, offset[1]), x=flip(x, offset[2]))
    sizes = dict(z=4, y=2, x=2)
    for earlier in order[: order.index(axis)]:
        index = index * sizes[earlier] + values[earlier]
        count *= sizes[earlier]
    if axis == "z":
        index = index * 5 + (4 if direction == "d" and offset[0] == 0 else values["z"])
        count *= 5
    return index, count


def slot_base(order):
    base, total = {}, 0
    for axis, direction in (("x", "x"), ("y", "y"), ("z", "u")):
        base[axis] = total
        total += slot_index(order, direction, (0, 0, 0), 0, 0, 0)[1]
    base["u"] = base["d"] = base["z"]
    return base, total


(
    B_TREE,
    B_RS_ACROSS,
    B_RS_FIRST,
    B_RS_SECOND,
    B_RS_RANK,
    B_RS_LAST,
    B_ACT_CORE,
    B_ACT_LOAD,
    B_ACT_ADD_X,
    B_ACT_ADD_Z,
    B_ACT_SUM,
    B_NORM_TURN,
    B_SWAP_TURNED,
    B_PROBS,
    B_MID,
    B_SCORES_BACK,
    B_SWAP_QKV,
    B_OUT_W,
    B_QKV_W,
    B_ROWS_BACK,
    B_ATTN_BACK,
    B_FINISH_OUTPUT,
) = range(22)
BACKWARD_STEPS = [
    (B_ACT_CORE, 0, 0), (B_RS_ACROSS, 0, 0, 0), (B_RS_ACROSS, 0, 0, 1), (B_NORM_TURN,), (B_ACT_CORE, 0, 1),
    (B_ACT_ADD_X, 0, 0, 1), (B_RS_ACROSS, 0, 1, 0), (B_ACT_ADD_X, 0, 0, 0), (B_ACT_ADD_X, 0, 1, 1),
    (B_RS_ACROSS, 0, 0, 2), (B_RS_ACROSS, 1, 0, 1), (B_ACT_CORE, 1, 1), (B_SWAP_TURNED,), (B_RS_FIRST, 0, 0),
    (B_ACT_ADD_X, 0, 1, 0), (B_ACT_ADD_Z, 0, 0), (B_RS_FIRST, 0, 1), (B_ACT_ADD_Z, 0, 1),
    (B_RS_ACROSS, 1, 1, 1), (B_PROBS,), (B_ACT_SUM, 0, 0), (B_MID, 0), (B_OUT_W, 0), (B_RS_ACROSS, 1, 0, 0),
    (B_TREE, 2, -3, 1, 1), (B_RS_FIRST, 0, 2), (B_ACT_CORE, 1, 0), (B_TREE, 2, 1, 1, 1), (B_TREE, 2, 0, 0, 1),
    (B_RS_SECOND, 0, 0), (B_TREE, 2, 0, 1, 1), (B_RS_ACROSS, 0, 1, 1), (B_ACT_SUM, 0, 1), (B_TREE, 2, -1, 1, 1),
    (B_MID, 1), (B_ACT_LOAD, 1), (B_ACT_ADD_X, 1, 1, 0), (B_RS_ACROSS, 1, 1, 0), (B_SCORES_BACK,),
    (B_ACT_ADD_X, 1, 0, 0), (B_TREE, 2, 2, 1, 1), (B_OUT_W, 1), (B_SWAP_QKV,), (B_RS_FIRST, 1, 1),
    (B_ACT_ADD_X, 1, 1, 1), (B_RS_SECOND, 0, 1), (B_QKV_W, 0), (B_TREE, 2, 0, 1, 0), (B_TREE, 2, -1, 1, 0),
    (B_RS_RANK, 0, 4), (B_TREE, 3, -3, 1, 1), (B_QKV_W, 1), (B_TREE, 0, 1, 1, 1), (B_RS_ACROSS, 1, 0, 2),
    (B_TREE, 1, 2, 1, 1), (B_TREE, 0, -2, 1, 1), (B_TREE, 3, 3, 1, 0), (B_TREE, 0, -3, 1, 1),
    (B_TREE, 3, 3, 0, 1), (B_TREE, 3, -2, 0, 1), (B_TREE, 3, -3, 0, 1), (B_TREE, 1, -1, 1, 1),
    (B_TREE, 2, 3, 0, 1), (B_TREE, 3, 2, 1, 0), (B_TREE, 2, 3, 1, 1), (B_RS_RANK, 0, 7), (B_TREE, 3, -3, 1, 0),
    (B_RS_RANK, 0, 5), (B_ACT_ADD_X, 1, 0, 1), (B_RS_RANK, 0, 3), (B_TREE, 3, 3, 0, 0), (B_TREE, 1, 3, 0, 1),
    (B_TREE, 3, -2, 1, 0), (B_TREE, 0, 3, 1, 1), (B_TREE, 3, -3, 0, 0), (B_TREE, 3, 2, 0, 1),
    (B_TREE, 0, -3, 1, 0), (B_TREE, 1, 3, 1, 1), (B_TREE, 3, -2, 1, 1), (B_TREE, 0, 3, 1, 0),
    (B_TREE, 2, -3, 1, 0), (B_TREE, 3, 3, 1, 1), (B_TREE, 2, 1, 0, 1), (B_TREE, 2, 3, 1, 0),
    (B_TREE, 0, 2, 1, 1), (B_TREE, 2, -2, 1, 1), (B_TREE, 2, -2, 0, 1), (B_TREE, 2, 2, 0, 1),
    (B_TREE, 0, 0, 1, 1), (B_TREE, 2, -3, 0, 1), (B_TREE, 0, 1, 1, 0), (B_RS_FIRST, 1, 0), (B_TREE, 0, 3, 0, 1),
    (B_TREE, 3, 2, 1, 1), (B_TREE, 1, -3, 1, 1), (B_RS_SECOND, 1, 1), (B_TREE, 1, -3, 0, 1),
    (B_TREE, 1, 2, 1, 0), (B_TREE, 1, 2, 0, 1), (B_TREE, 2, 3, 0, 0), (B_RS_RANK, 0, 1), (B_TREE, 3, 1, 1, 1),
    (B_TREE, 1, -2, 0, 1), (B_RS_LAST, 0, 1), (B_ACT_ADD_Z, 1, 1), (B_RS_ACROSS, 1, 1, 2),
    (B_TREE, 0, -3, 0, 1), (B_RS_SECOND, 1, 0), (B_TREE, 3, -1, 0, 1), (B_RS_RANK, 1, 3), (B_TREE, 1, 3, 1, 0),
    (B_TREE, 2, 2, 1, 0), (B_RS_RANK, 0, 2), (B_TREE, 3, -1, 1, 0), (B_TREE, 0, 2, 1, 0), (B_TREE, 0, 2, 0, 1),
    (B_ACT_ADD_Z, 1, 0), (B_TREE, 1, 1, 1, 1), (B_TREE, 3, -1, 1, 1), (B_TREE, 1, -3, 1, 0),
    (B_TREE, 1, -3, 0, 0), (B_TREE, 3, 1, 1, 0), (B_TREE, 1, 0, 1, 1), (B_TREE, 1, -2, 1, 1),
    (B_RS_FIRST, 1, 2), (B_TREE, 0, -2, 0, 1), (B_TREE, 1, -1, 0, 1), (B_TREE, 0, -1, 1, 1), (B_RS_RANK, 1, 6),
    (B_RS_RANK, 1, 4), (B_ROWS_BACK, 0), (B_TREE, 0, 1, 0, 1), (B_TREE, 1, -1, 1, 0), (B_ROWS_BACK, 1),
    (B_TREE, 0, 3, 0, 0), (B_RS_LAST, 0, 3), (B_TREE, 1, 3, 0, 0), (B_TREE, 1, 1, 1, 0), (B_TREE, 2, 1, 1, 0),
    (B_ACT_SUM, 1, 1), (B_TREE, 1, 1, 0, 1), (B_TREE, 1, -2, 1, 0), (B_ACT_SUM, 1, 0), (B_RS_LAST, 0, 5),
    (B_RS_RANK, 1, 2), (B_RS_LAST, 0, 7), (B_TREE, 0, -3, 0, 0), (B_TREE, 0, 2, 0, 0), (B_TREE, 3, 1, 0, 1),
    (B_TREE, 1, 2, 0, 0), (B_TREE, 3, 0, 1, 1), (B_TREE, 2, -2, 1, 0), (B_TREE, 3, 2, 0, 0),
    (B_TREE, 2, -3, 0, 0), (B_FINISH_OUTPUT,), (B_RS_LAST, 1, 3), (B_TREE, 0, -2, 1, 0), (B_TREE, 1, -2, 0, 0),
    (B_TREE, 0, -1, 1, 0), (B_RS_LAST, 1, 6), (B_TREE, 0, -2, 0, 0), (B_TREE, 0, 0, 1, 0), (B_RS_RANK, 1, 1),
    (B_RS_ACROSS, 0, 1, 2), (B_TREE, 2, -1, 0, 1), (B_TREE, 0, 1, 0, 0), (B_TREE, 1, 0, 1, 0),
    (B_TREE, 0, -1, 0, 1), (B_RS_RANK, 0, 6), (B_TREE, 1, 0, 0, 1), (B_RS_LAST, 0, 4), (B_TREE, 3, -2, 0, 0),
    (B_TREE, 3, 0, 0, 1), (B_TREE, 2, -2, 0, 0), (B_RS_RANK, 1, 5), (B_TREE, 2, 2, 0, 0), (B_TREE, 1, -1, 0, 0),
    (B_TREE, 1, 1, 0, 0), (B_TREE, 0, 0, 0, 1), (B_RS_LAST, 0, 2), (B_TREE, 3, -1, 0, 0), (B_RS_LAST, 1, 1),
    (B_TREE, 0, -1, 0, 0), (B_TREE, 3, 0, 1, 0), (B_ATTN_BACK,), (B_TREE, 2, -1, 0, 0), (B_RS_RANK, 1, 7),
    (B_RS_LAST, 0, 6), (B_RS_SECOND, 1, 2), (B_RS_LAST, 1, 2), (B_TREE, 3, 1, 0, 0), (B_RS_SECOND, 0, 2),
    (B_TREE, 2, 1, 0, 0), (B_RS_LAST, 1, 5), (B_TREE, 3, 0, 0, 0), (B_RS_LAST, 1, 4), (B_TREE, 1, 0, 0, 0),
    (B_TREE, 0, 0, 0, 0), (B_TREE, 2, 0, 0, 0), (B_RS_LAST, 1, 7),
]


def backward_kernel(
    tokens_ref,
    cot_ref,
    gain_rows,
    qkv_rows,
    context,
    resid_mid,
    qkv_full,
    out_full,
    out_ref,
    back_ref,
    gate_up_ref,
    down_ref,
    output,
    grad_tokens,
    norm_attn_sum,
    norm_ff_sum,
    qkv_sum,
    attn_out_sum,
    gate_up_total,
    down_sum,
    act_own,
    core_buf,
    x_buf,
    z_buf,
    gate_own,
    down_own,
    across_gate,
    across_down,
    far_gate,
    far_down,
    qkv_grad,
    out_grad,
    slots_0,
    slots_1,
    slots_2,
    slots_3,
    qkv_tiles,
    out_tiles,
    turned,
    attn_turned,
    context_turned,
    d_qkv,
    d_mid_low,
    d_mid,
    d_context,
    d_rows,
    halves,
    probs_buf,
    spread,
    gain_acc,
    gains_part,
    gains_buf,
    gains_sum,
    gate_up_sum,
    core_send,
    core_recv,
    x_send,
    x_recv,
    z_send,
    z_recv,
    across_send,
    across_recv,
    far_send,
    far_recv,
    rank_send,
    rank_recv,
    swap_send,
    swap_recv,
    tree_send,
    tree_recv,
    gains_send,
    gains_recv,
    own_sem,
    part_sem,
    tile_sem,
):
    z, y, x, core = here()
    me = 2 * (z * 4 + y * 2 + x) + core
    zh, zl, member, rank, device, far, across = group_place(z, y, x, core)
    own_step = (0, 0, 0)
    act_height, positions, model = tokens_ref.shape
    sets = positions
    height = qkv_sum.shape[1]
    down_height = down_sum.shape[1]
    half = 16 * height
    sibling = member((0, 0, 1))
    scale = 1.0 / math.sqrt(HEAD_DIM)
    pairs = pairs_of(positions)
    greet_all(z, y, x, core)
    sends = []

    def start(copy):
        copy.start()
        sends.append(copy)

    def run_rows(dzh, dy, low):
        number = 16 * flip(zh, dzh) + 4 * flip(y, dy) + 8 * low
        return pl.ds(pl.multiple_of(number * height, 4 * height), 4 * height)

    def down_rows(dzh, dy):
        number = 2 * flip(zh, dzh) + flip(y, dy)
        return pl.ds(pl.multiple_of(number * down_height, down_height), down_height)

    def ff_from(s, dzh, dy, part):
        if part == 2:
            return down_ref.at[s, down_rows(dzh, dy)]
        return gate_up_ref.at[s, run_rows(dzh, dy, part)]

    def ff_across(s, turn, part):
        return across_down.at[turn, s] if part == 2 else across_gate.at[turn, s, part]

    def ff_own(s, turn, part):
        return down_own.at[turn, s] if part == 2 else gate_own.at[turn, s, part]

    def ff_far(s, part):
        return far_down.at[s] if part == 2 else far_gate.at[s, part]

    def part_copy(s, turn, part):
        return pltpu.make_async_copy(
            ff_from(s, 1 - turn, 0, part), ff_own(s, turn, part), part_sem.at[turn, s, part]
        )

    def rs_across(s, turn, part):
        start(
            push(
                ff_from(s, 1 - turn, 1, part),
                ff_across(s, turn, part),
                across_send.at[turn, s, part],
                across_recv.at[turn, s, part],
                across,
            )
        )

    def rs_first(s, part):
        block = ff_across(s, 0, part)
        part_copy(s, 0, part).wait()
        arrived(block, across_recv.at[0, s, part], across)
        add_into(block, [block, ff_own(s, 0, part)])
        start(push(block, ff_far(s, part), far_send.at[s, part], far_recv.at[s, part], far))

    def rs_second(s, part):
        block = ff_across(s, 1, part)
        part_copy(s, 1, part).wait()
        arrived(block, across_recv.at[1, s, part], across)
        arrived(ff_far(s, part), far_recv.at[s, part], far)
        target = down_sum.at[s] if part == 2 else block
        add_into(target, [block, ff_far(s, part), ff_own(s, 1, part)])

    def share(step, s):
        number = 2 * flip(x, step[1]) + flip(core, step[2])
        return across_gate.at[
            1, s, flip(zl, step[0]), pl.ds(pl.multiple_of(number * height, height), height)
        ]

    def place_units(step, s, source):
        unit = down_height
        number = 8 * flip(zl, step[0]) + 2 * flip(x, step[1]) + flip(core, step[2])
        for side in (0, 1):
            for group in range(4):
                zh_part, y_part = divmod(group, 2)
                left = (32 * side + 16 * zh_part + 4 * y_part + number) * unit
                gate_up_total[s, :, pl.ds(pl.multiple_of(left, unit), unit)] = source[
                    :, (4 * side + group) * unit : (4 * side + group + 1) * unit
                ].astype(F32)

    def rs_rank(s, slot):
        step = RANK_STEPS[slot]
        push(
                share(step, s),
                gate_up_sum.at[rank(own_step), s],
                rank_send.at[s],
                rank_recv.at[slot, s],
                member(step),
            ).start()

    def rs_last(s, slot):
        step = RANK_STEPS[slot]
        block = gate_up_sum.at[rank(step), s]
        arrived(block, rank_recv.at[slot, s], member(step))
        place_units(step, s, block)

    acts = [back_ref, out_ref]

    def act_rows(step):
        return pl.ds(pl.multiple_of(rank(step) * act_height, act_height), act_height)

    def act_core(which, s):
        for dl, dx in ((1, 1), (0, 1), (1, 0), (0, 0)):
            start(
                push(
                    acts[which].at[s, act_rows((dl, dx, 1))],
                    core_buf.at[which, s, dl, dx],
                    core_send.at[which, s, dl, dx],
                    core_recv.at[which, s, dl, dx],
                    sibling,
                )
            )

    def act_copy(which, s, dl, dx):
        return pltpu.make_async_copy(
            acts[which].at[s, act_rows((dl, dx, 0))],
            act_own.at[s, dl, dx],
            own_sem.at[which, s, dl, dx],
        )

    def act_load(which):
        for s in range(sets):
            for dl in (0, 1):
                for dx in (0, 1):
                    act_copy(which, s, dl, dx).start()

    def act_ready(which, s, dl, dx):
        act_copy(which, s, dl, dx).wait()
        arrived(core_buf.at[which, s, dl, dx], core_recv.at[which, s, dl, dx], sibling)

    def act_add_x(which, s, dl):
        act_ready(which, s, dl, 1)
        block = core_buf.at[which, s, dl, 1]
        add_into(block, [block, act_own.at[s, dl, 1]])
        start(
            push(
                block,
                x_buf.at[which, s, dl],
                x_send.at[which, s, dl],
                x_recv.at[which, s, dl],
                member((0, 1, 0)),
            )
        )

    def act_add_z(which, s):
        act_ready(which, s, 1, 0)
        block = x_buf.at[which, s, 1]
        arrived(block, x_recv.at[which, s, 1], member((0, 1, 0)))
        add_into(block, [block, core_buf.at[which, s, 1, 0], act_own.at[s, 1, 0]])
        start(
            push(
                block, z_buf.at[which, s], z_send.at[which, s], z_recv.at[which, s], member((1, 0, 0))
            )
        )

    def act_sum(which, s):
        act_ready(which, s, 0, 0)
        arrived(x_buf.at[which, s, 0], x_recv.at[which, s, 0], member((0, 1, 0)))
        arrived(z_buf.at[which, s], z_recv.at[which, s], member((1, 0, 0)))

    def act_total(which, s, rows):
        return (
            act_own[s, 0, 0, rows, :].astype(F32)
            + core_buf[which, s, 0, 0, rows, :].astype(F32)
            + x_buf[which, s, 0, rows, :].astype(F32)
            + z_buf[which, s, rows, :].astype(F32)
        )

    pieces = [
        (qkv_grad, qkv_sum, 0, "zxy", slots_0),
        (qkv_grad, qkv_sum, 1, "zyx", slots_1),
        (out_grad, attn_out_sum, 0, "zyx", slots_2),
        (out_grad, attn_out_sum, 1, "yxz", slots_3),
    ]
    events = sorted(
        ((-hops(offset), place, piece, offset) for piece in range(4) for place, offset in enumerate(OFFSETS)),
        key=lambda event: event[:3],
    )

    def tree_block(piece, offset):
        source, _, index, _, _ = pieces[piece]
        chip = chip_of(offset, z, y, x)
        return source.at[index, pl.ds(pl.multiple_of(chip * height, height), height), :]

    def tree_copy(piece, offset):
        _, _, _, order, slots = pieces[piece]
        toward = came_from(order, offset)
        base, _ = slot_base(order)
        seen = {"x": "x", "y": "y", "u": "d", "d": "u"}[toward]
        nearer = offset
        if toward == "u":
            nearer = (offset[0] - 1, offset[1], offset[2])
        if toward == "d":
            nearer = (offset[0] + 1, offset[1], offset[2])
        there = {"u": z + 1, "d": z - 1}.get(toward, z)
        index_there, _ = slot_index(
            order, seen, nearer, there, y if toward != "y" else 1 - y, x if toward != "x" else 1 - x
        )
        if toward in "xy":
            index_there, _ = slot_index(order, seen, offset, z, y, x)
        place = base[seen] + index_there
        return push(
            tree_block(piece, offset),
            slots.at[place],
            tree_send.at[piece, DIRECTIONS.index(toward)],
            tree_recv.at[piece, place],
            neighbour(toward, z, y, x, core),
        )

    def tree_step(piece, offset):
        _, result, index, order, slots = pieces[piece]
        base, _ = slot_base(order)

        def go():
            block = tree_block(piece, offset)
            sure, unsure = [], []
            for direction in onward(order, offset):
                local, _ = slot_index(order, direction, offset, z, y, x)
                place = base[direction] + local
                (sure if direction in "xy" else unsure).append((direction, place))
            terms = [block]
            for _, place in sure:
                arrived(slots.at[place], tree_recv.at[piece, place], sibling)
                terms.append(slots.at[place])
            last = hops(offset) == 0
            target = result.at[index] if last else block
            if last or len(terms) > 1:
                add_into(target, terms)
            for direction, place in unsure:

                def more(place=place):
                    arrived(slots.at[place], tree_recv.at[piece, place], sibling)
                    add_into(target, [target, slots.at[place]])

                maybe(direction_exists(direction, z), more)
            if not last:
                tree_copy(piece, offset).start()

        maybe(offset_exists(offset, z), go)

    def gains_copy(step):
        other = lax.rem(me + step, 32)
        return push(
            gains_part.at[lax.div(other, 4)],
            gains_buf.at[me],
            gains_send,
            gains_recv,
            (lax.div(other, 2), lax.rem(other, 2)),
        )

    def gains_start(step, carry):
        gains_copy(step).start()
        return carry

    def gains_add(step, carry):
        gains_sum[...] += gains_buf[lax.rem(me + step, 32)]
        return carry

    def turn(source, target, slot):
        def one(block, p):
            flat = source(p, block)
            turned[slot, p, pl.ds(2 * block, 2)] = flat.T.astype(BF16).reshape(2, 2, height, act_height)

        for p in range(positions):
            for block in range(model // 128):
                one(block, p)
            target[p, :, :, :act_height] = turned[slot, p, :, core]

    qkv_tile = qkv_tiles.shape[1]
    tile_count = model // qkv_tile

    def qkv_load(number):
        p, tile = divmod(number, tile_count)
        return pltpu.make_async_copy(
            qkv_full.at[p, pl.ds(tile * qkv_tile, qkv_tile)],
            qkv_tiles.at[number % 2],
            tile_sem.at[number % 2],
        )

    out_loads = [
        pltpu.make_async_copy(out_full.at[p], out_tiles.at[p], tile_sem.at[2 + p]) for p in range(positions)
    ]

    def context_block(p, block):
        return context[p, :, 128 * block : 128 * block + 128].astype(F32)

    def attn_block(p, block):
        return d_rows[p, :, 128 * block : 128 * block + 128]

    def norm_turn():
        def attn_norm(rows):
            values = tokens_ref[rows].astype(F32)
            for p in range(positions):
                r, _ = normed(values[:, p, :])
                d_rows[p, rows, :] = r * gain_rows[p : p + 1, :]

        row_loop(act_height, 16, attn_norm)
        turn(context_block, context_turned, 0)
        turn(attn_block, attn_turned, 1)

    def landing(kind, p):
        other = pl.ds(act_height, act_height)
        return (
            context_turned.at[p, :, :, other],
            attn_turned.at[p, :, :, other],
            d_mid_low.at[p, other],
            d_qkv.at[p, other],
        )[kind]

    def swap(kind, p, source):
        start(
            push(source, landing(kind, p), swap_send.at[4 * p + kind], swap_recv.at[4 * p + kind], sibling)
        )

    def swap_wait(kind, p):
        arrived(landing(kind, p), swap_recv.at[4 * p + kind], sibling)

    def swap_turned():
        for p in range(positions):
            swap(0, p, turned.at[0, p, :, 1 - core])
            swap(1, p, turned.at[1, p, :, 1 - core])

    def find_probs():
        for p in range(positions):
            probs = attention_probs(qkv_rows, halves, spread, model, p)
            for q in range(p + 1):
                probs_buf[pairs.index((p, q))] = probs[q]

    def mid(p):
        def mid_back(rows):
            d_ff_in = act_total(0, p, rows)
            r, inverse = normed(resid_mid[p, rows, :])
            gain_acc[positions + p] += r * d_ff_in
            total = cot_ref[p, rows, :] + norm_back(
                r, inverse, d_ff_in * gain_rows[positions + p : positions + p + 1, :]
            )
            d_mid[p, rows, :] = total
            d_mid_low[p, rows, :] = total.astype(BF16)

        row_loop(act_height, 16, mid_back)
        swap(2, p, d_mid_low.at[p, pl.ds(0, act_height)])
        out_loads[p].wait()

        def context_back(columns):
            d_context[p, :, columns] = dot_back(
                d_mid_low[p, :act_height, :], out_tiles[p, columns, :]
            ).astype(BF16)

        tile_loop(model, 256, context_back)

    def scores_back():
        def context_products(rows):
            for index, (p, q) in enumerate(pairs):
                product = d_context[p, rows, :].astype(F32) * qkv_rows[q, rows, 2 * model :].astype(F32)
                halves[2 * index, rows, :], halves[2 * index + 1, rows, :] = split_product(product)

        row_loop(act_height, 16, context_products)
        d_probs = [sums_over_heads(halves, spread, index) for index in range(len(pairs))]
        for p in range(positions):
            own = [index for index, pair in enumerate(pairs) if pair[0] == p]
            mean = functools.reduce(jnp.add, [probs_buf[index] * d_probs[index] for index in own])
            for index in own:
                d_score = (probs_buf[index] * (d_probs[index] - mean)).astype(BF16)
                halves[2 * index] = to_heads(d_score, spread)
                halves[2 * index + 1] = to_heads(probs_buf[index].astype(BF16), spread)

        def plus(total, term):
            return term if total is None else total + term

        def qkv_back(rows):
            d_keys = [None] * positions
            d_values = [None] * positions
            for p in range(positions):
                d_query = None
                d_own = d_context[p, rows, :].astype(F32)
                query = qkv_rows[p, rows, :model].astype(F32)
                for index, (own, q) in enumerate(pairs):
                    if own == p:
                        d_score = halves[2 * index, rows, :].astype(F32)
                        key = qkv_rows[q, rows, model : 2 * model].astype(F32)
                        d_query = plus(d_query, d_score * key)
                        d_keys[q] = plus(d_keys[q], d_score * query)
                        d_values[q] = plus(
                            d_values[q], halves[2 * index + 1, rows, :].astype(F32) * d_own
                        )
                d_qkv[p, rows, :model] = (d_query * scale).astype(BF16)
            for p in range(positions):
                d_qkv[p, rows, model : 2 * model] = (d_keys[p] * scale).astype(BF16)
                d_qkv[p, rows, 2 * model :] = d_values[p].astype(BF16)

        row_loop(act_height, 16, qkv_back)

    def swap_qkv():
        for p in range(positions):
            swap(3, p, d_qkv.at[p, pl.ds(0, act_height)])

    def out_weights(p):
        swap_wait(0, p)
        swap_wait(2, p)

        def tile(columns):
            out_grad[p, :, columns] = dot(
                context_turned[p].reshape(half, 2 * act_height), d_mid_low[p, :, columns]
            ).astype(BF16)

        tile_loop(model, 256, tile)

    def qkv_weights(p):
        swap_wait(1, p)
        swap_wait(3, p)

        def tile(columns):
            qkv_grad[p, :, columns] = dot(
                attn_turned[p].reshape(half, 2 * act_height), d_qkv[p, :, columns]
            ).astype(BF16)

        tile_loop(3 * model, 256, tile)

    def rows_back(p):
        for tile in range(tile_count):
            number = p * tile_count + tile
            qkv_load(number).wait()
            d_rows[p, :, tile * qkv_tile : (tile + 1) * qkv_tile] = dot_back(
                d_qkv[p, :act_height, :], qkv_tiles[number % 2]
            )
            if number + 2 < positions * tile_count:
                qkv_load(number + 2).start()

    def attn_back():
        def norm_one_back(rows):
            values = tokens_ref[rows].astype(F32)
            for p in range(positions):
                r, inverse = normed(values[:, p, :])
                d_attn_in = d_rows[p, rows, :]
                gain_acc[p] += r * d_attn_in
                grad_tokens[rows, p, :] = d_mid[p, rows, :] + norm_back(
                    r, inverse, d_attn_in * gain_rows[p : p + 1, :]
                )

        row_loop(act_height, 16, norm_one_back)
        gains_part[...] = jnp.zeros_like(gains_part)
        for index in range(2 * positions):
            sums = jnp.sum(gain_acc[index], axis=0, keepdims=True)
            for block in range(8):
                gains_part[block, index : index + 1, :] = sums[:, 128 * block : 128 * block + 128]
        lax.fori_loop(1, 32, gains_start, 0)

    def finish_output():
        def finish(rows):
            rounded = [resid_mid[p, rows, :] + act_total(1, p, rows) for p in range(positions)]
            output[rows] = jnp.stack(rounded, axis=1).astype(BF16)

        row_loop(act_height, 16, finish)

    for s in range(sets):
        for turn_number in (0, 1):
            for part in (0, 1, 2):
                part_copy(s, turn_number, part).start()
    for copy in out_loads:
        copy.start()
    act_load(0)
    qkv_load(0).start()
    qkv_load(1).start()
    make_spread(spread)
    gain_acc[...] = jnp.zeros_like(gain_acc)
    kinds = {
        B_TREE: lambda piece, dz, dy, dx: tree_step(piece, (dz, dy, dx)),
        B_RS_ACROSS: rs_across,
        B_RS_FIRST: rs_first,
        B_RS_SECOND: rs_second,
        B_RS_RANK: rs_rank,
        B_RS_LAST: rs_last,
        B_ACT_CORE: act_core,
        B_ACT_LOAD: act_load,
        B_ACT_ADD_X: act_add_x,
        B_ACT_ADD_Z: act_add_z,
        B_ACT_SUM: act_sum,
        B_NORM_TURN: norm_turn,
        B_SWAP_TURNED: swap_turned,
        B_PROBS: find_probs,
        B_MID: mid,
        B_SCORES_BACK: scores_back,
        B_SWAP_QKV: swap_qkv,
        B_OUT_W: out_weights,
        B_QKV_W: qkv_weights,
        B_ROWS_BACK: rows_back,
        B_ATTN_BACK: attn_back,
        B_FINISH_OUTPUT: finish_output,
    }
    for kind, *numbers in BACKWARD_STEPS:
        kinds[kind](*numbers)
    for s in range(sets):
        place_units(own_step, s, share(own_step, s))
    gains_sum[...] = gains_part[lax.div(me, 4)]
    others = gains_buf.at[pl.ds(0, 31)]
    arrived(others, gains_recv, sibling)
    push(others, others, gains_send, gains_recv, sibling).wait_send()
    lax.fori_loop(1, 32, gains_add, 0)
    own_gain = norm_attn_sum.shape[1]
    for index, target in enumerate((norm_attn_sum, norm_ff_sum)):
        picked = jnp.zeros(target.shape, F32)
        for place in range(128 // own_gain):
            picked = picked + jnp.where(
                lax.rem(me, 128 // own_gain) == place,
                gains_sum[
                    index * positions : (index + 1) * positions, place * own_gain : (place + 1) * own_gain
                ],
                0.0,
            )
        target[...] = picked
    def tree_sent(piece, direction, count):
        source, _, index, _, _ = pieces[piece]
        block = source.at[index, pl.ds(0, count * height), :]
        push(block, block, tree_send.at[piece, DIRECTIONS.index(direction)], gains_recv, sibling).wait_send()

    for piece in range(len(pieces)):
        order = pieces[piece][3]
        for direction in "xy":
            tree_sent(piece, direction, return_count(order, direction, 3))
        for direction in "ud":
            for level in range(4):
                if level != (3 if direction == "u" else 0):
                    pl.when(z == level)(
                        functools.partial(
                            tree_sent, piece, direction, return_count(order, direction, level)
                        )
                    )
    for s in range(sets):
        block = gate_up_sum.at[pl.ds(0, 7), s]
        push(block, block, rank_send.at[s], gains_recv, sibling).wait_send()
    for copy in sends:
        copy.wait_send()


def backward_scatter(
    tokens,
    grads,
    gain_rows,
    qkv_rows,
    context,
    resid_mid,
    qkv_full,
    out_full,
    out_part,
    back_part,
    gate_up_grad,
    down_grad,
):
    act_height, sets, model = tokens.shape
    width = gate_up_grad.shape[2]
    height = model // 32
    down_height = down_grad.shape[1] // 4
    dma = pltpu.SemaphoreType.DMA
    vmem = pl.BlockSpec(memory_space=pltpu.VMEM)
    anywhere = pl.BlockSpec(memory_space=pl.ANY)
    places = [slot_base(order)[1] for order in ORDERS]
    pair_count = len(pairs_of(sets))
    act = (sets, act_height, model)
    return pl.pallas_call(
        backward_kernel,
        out_shape=(
            jax.ShapeDtypeStruct(tokens.shape, BF16),
            jax.ShapeDtypeStruct(tokens.shape, F32),
            jax.ShapeDtypeStruct((sets, height), F32),
            jax.ShapeDtypeStruct((sets, height), F32),
            jax.ShapeDtypeStruct((sets, height, 3 * model), F32),
            jax.ShapeDtypeStruct((sets, height, model), F32),
            jax.ShapeDtypeStruct((sets, height, 8 * width), F32),
            jax.ShapeDtypeStruct((sets, down_height, model), F32),
        ),
        in_specs=[vmem] * 6 + [anywhere] * 6,
        out_specs=(vmem,) * 8,
        scratch_shapes=[
            pltpu.VMEM((sets, 2, 2, act_height, model), BF16),
            pltpu.VMEM((2, sets, 2, 2, act_height, model), BF16),
            pltpu.VMEM((2, sets, 2, act_height, model), BF16),
            pltpu.VMEM((2, sets, act_height, model), BF16),
            pltpu.VMEM((2, sets, 2, 4 * height, width), BF16),
            pltpu.VMEM((2, sets, down_height, model), BF16),
            pltpu.VMEM((2, sets, 2, 4 * height, width), BF16),
            pltpu.VMEM((2, sets, down_height, model), BF16),
            pltpu.VMEM((sets, 2, 4 * height, width), BF16),
            pltpu.VMEM((sets, down_height, model), BF16),
            pltpu.VMEM((sets, 16 * height, 3 * model), BF16),
            pltpu.VMEM((sets, 16 * height, model), BF16),
            pltpu.VMEM((places[0], height, 3 * model), BF16),
            pltpu.VMEM((places[1], height, 3 * model), BF16),
            pltpu.VMEM((places[2], height, model), BF16),
            pltpu.VMEM((places[3], height, model), BF16),
            pltpu.VMEM((2, 128, 3 * model), BF16),
            pltpu.VMEM((sets, model, model), BF16),
            pltpu.VMEM((2, sets, 16, 2, height, act_height), BF16),
            pltpu.VMEM((sets, 16, height, 2 * act_height), BF16),
            pltpu.VMEM((sets, 16, height, 2 * act_height), BF16),
            pltpu.VMEM((sets, 2 * act_height, 3 * model), BF16),
            pltpu.VMEM((sets, 2 * act_height, model), BF16),
            pltpu.VMEM(act, F32),
            pltpu.VMEM(act, BF16),
            pltpu.VMEM(act, F32),
            pltpu.VMEM((2 * pair_count, act_height, model), BF16),
            pltpu.VMEM((pair_count, act_height, 128), F32),
            pltpu.VMEM((model, 128), BF16),
            pltpu.VMEM((2 * sets, 16, model), F32),
            pltpu.VMEM((8, 8, 128), F32),
            pltpu.VMEM((32, 8, 128), F32),
            pltpu.VMEM((8, 128), F32),
            pltpu.VMEM((8, sets, height, width), BF16),
            dma((2, sets, 2, 2)),
            dma((2, sets, 2, 2)),
            dma((2, sets, 2)),
            dma((2, sets, 2)),
            dma((2, sets)),
            dma((2, sets)),
            dma((2, sets, 3)),
            dma((2, sets, 3)),
            dma((sets, 3)),
            dma((sets, 3)),
            dma((sets,)),
            dma((8, sets)),
            dma((4 * sets,)),
            dma((4 * sets,)),
            dma((4, 4)),
            dma((4, max(places))),
            dma,
            dma,
            dma((2, sets, 2, 2)),
            dma((2, sets, 3)),
            dma((2 + sets,)),
        ],
        compiler_params=pltpu.CompilerParams(
            collective_id=5, has_side_effects=True, vmem_limit_bytes=63 * 2**20
        ),
        name="backward_scatter",
    )(
        tokens,
        grads,
        gain_rows,
        qkv_rows,
        context,
        resid_mid,
        qkv_full,
        out_full,
        out_part,
        back_part,
        gate_up_grad,
        down_grad,
    )


def settle_kernel(*refs):
    count = (len(refs) - 1) // 3
    sems = refs[-1]
    stages = [
        (
            pltpu.make_async_copy(refs[index], refs[2 * count + index], sems.at[0, index]),
            pltpu.make_async_copy(refs[2 * count + index], refs[count + index], sems.at[1, index]),
        )
        for index in range(count)
    ]
    for read, _ in stages:
        read.start()
    for read, write in stages:
        read.wait()
        write.start()
    for _, write in stages:
        write.wait()


def settle(arrays):
    anywhere = pl.BlockSpec(memory_space=pl.ANY)
    return pl.pallas_call(
        settle_kernel,
        out_shape=tuple(jax.ShapeDtypeStruct(array.shape, array.dtype) for array in arrays),
        in_specs=[anywhere] * len(arrays),
        out_specs=(anywhere,) * len(arrays),
        scratch_shapes=[pltpu.VMEM(array.shape, array.dtype) for array in arrays]
        + [pltpu.SemaphoreType.DMA((2, len(arrays)))],
        name="settle",
    )(*arrays)


def local_fast(
    tokens,
    norm_attn,
    w_qkv,
    w_out,
    norm_ff,
    w_gate_up,
    w_down,
    cotangent,
    valid_frames,
    item_lengths,
):
    (
        gain_rows,
        cot_rows,
        qkv_rows,
        context,
        resid_mid,
        qkv_full,
        out_full,
        out_part,
        back_part,
        gate_up_grad,
        down_grad,
    ) = forward_gather(
        valid_frames,
        item_lengths,
        norm_attn,
        norm_ff,
        tokens,
        cotangent,
        w_qkv,
        w_out,
        w_gate_up,
        w_down,
    )
    (
        output,
        grad_tokens,
        share_norm_attn,
        share_norm_ff,
        share_qkv,
        share_out,
        share_gate_up,
        share_down,
    ) = settle(backward_scatter(
        tokens,
        cot_rows,
        gain_rows,
        qkv_rows,
        context,
        resid_mid,
        qkv_full,
        out_full,
        out_part,
        back_part,
        gate_up_grad,
        down_grad,
    ))
    return (
        output,
        grad_tokens,
        share_norm_attn,
        share_qkv,
        share_out,
        share_norm_ff,
        share_gate_up,
        share_down,
    )


def solution(mesh):
    in_specs = (
        P(("dp", "pair"), None, None),
        P(None, ("dp", "pair")),
        P(None, ("dp", "pair"), None),
        P(None, ("dp", "pair"), None),
        P(None, ("dp", "pair")),
        P(None, ("dp", "pair"), None),
        P(None, ("dp", "pair"), None),
        P(("dp", "pair"), None, None),
        P(("dp", "pair")),
        P(),
    )
    out_specs = (
        P(("dp", "pair"), None, None),
        P(("dp", "pair"), None, None),
        P(None, ("dp", "pair")),
        P(None, ("dp", "pair"), None),
        P(None, ("dp", "pair"), None),
        P(None, ("dp", "pair")),
        P(None, ("dp", "pair"), None),
        P(None, ("dp", "pair"), None),
    )
    body = local_fast if mesh.shape["dp"] == 16 and mesh.shape["pair"] == 2 else local
    return jax.shard_map(body, mesh=mesh, in_specs=in_specs, out_specs=out_specs, check_vma=False)
```

```python
import functools
import math

import jax
import jax.numpy as jnp
from jax import lax
from jax.experimental import pallas as pl
from jax.experimental.pallas import tpu as pltpu
from jax.sharding import PartitionSpec as P

HEAD_DIM = 64


def per_pos(activations, weight):
    return jnp.einsum("fgk,gke->fge", activations, weight, preferred_element_type=jnp.float32)


def per_pos_back(gradients, weight):
    return jnp.einsum("fge,gke->fgk", gradients, weight, preferred_element_type=jnp.float32)


def pos_grad(activations, gradients):
    return jnp.einsum("fgk,fge->kge", activations, gradients, preferred_element_type=jnp.float32)


def gain_grad(normed_rows, gradients):
    return jnp.transpose(jnp.sum(normed_rows * gradients, axis=0))


def back_layout(share):
    return jnp.swapaxes(share, 0, 1)


def normed(values):
    inverse = lax.rsqrt(jnp.mean(values * values, axis=-1, keepdims=True) + 1e-05)
    return (values * inverse, inverse)


def norm_back(normed_rows, inverse, gradients):
    return inverse * (
        gradients - normed_rows * jnp.mean(gradients * normed_rows, axis=-1, keepdims=True)
    )


def gather_ff_fwd(norm_ff, w_gate_up, w_down, start, group):
    return (
        lax.all_gather(norm_ff[start : start + group], ("dp", "pair"), axis=1, tiled=True),
        lax.all_gather(w_gate_up[start : start + group], ("dp", "pair"), axis=1, tiled=True),
        lax.all_gather(w_down[start : start + group], ("dp", "pair"), axis=1, tiled=True),
    )


def gather_ff_back(norm_ff, w_gate_up, w_down, start, group):
    return (
        lax.all_gather(norm_ff[start : start + group], ("dp", "pair"), axis=1, tiled=True),
        lax.all_gather(w_gate_up[start : start + group], ("dp", "pair"), axis=1, tiled=True),
        lax.all_gather(w_down[start : start + group], ("dp", "pair"), axis=1, tiled=True),
    )


def local(
    tokens,
    norm_attn,
    w_qkv,
    w_out,
    norm_ff,
    w_gate_up,
    w_down,
    cotangent,
    valid_frames,
    item_lengths,
):
    frame_count, positions, model_width = tokens.shape
    head_count = model_width // HEAD_DIM
    ff_units = w_gate_up.shape[2] // 2
    score_scale = 1.0 / math.sqrt(HEAD_DIM)
    causal = jnp.arange(positions)[:, None] >= jnp.arange(positions)[None, :]
    head_shape = (frame_count, positions, head_count, HEAD_DIM)
    group = 1
    gains_attn, qkv_full, out_full = (
        lax.all_gather(norm_attn, ("dp", "pair"), axis=1, tiled=True),
        lax.all_gather(w_qkv, ("dp", "pair"), axis=1, tiled=True),
        lax.all_gather(w_out, ("dp", "pair"), axis=1, tiled=True),
    )
    resid_in = tokens.astype(jnp.float32)
    normed_one, inverse_one = normed(resid_in)
    attn_in = (normed_one * gains_attn.astype(jnp.float32)[None]).astype(jnp.bfloat16)
    qkv_rows = per_pos(attn_in, qkv_full).astype(jnp.bfloat16)
    queries = qkv_rows[..., :model_width].reshape(head_shape)
    key_heads = qkv_rows[..., model_width : 2 * model_width].reshape(head_shape)
    value_heads = qkv_rows[..., 2 * model_width :].reshape(head_shape)
    scores = (
        jnp.einsum("fphd,fqhd->fhpq", queries, key_heads, preferred_element_type=jnp.float32)
        * score_scale
    )
    scores = jnp.where(causal, scores, -1e30)
    row_max = jnp.max(scores, axis=-1, keepdims=True)
    attn_probs = jnp.exp(scores - row_max)
    attn_probs = attn_probs / jnp.sum(attn_probs, axis=-1, keepdims=True)
    probs_low = attn_probs.astype(jnp.bfloat16)
    context = jnp.einsum(
        "fhpq,fqhd->fphd", probs_low, value_heads, preferred_element_type=jnp.float32
    )
    context = context.astype(jnp.bfloat16).reshape(frame_count, positions, model_width)
    resid_mid = resid_in + per_pos(context, out_full)
    kept_parts = []
    out_parts = []
    for start in range(0, positions, group):
        gains_ff, gate_up_full, down_full = gather_ff_fwd(norm_ff, w_gate_up, w_down, start, group)
        mid_part = resid_mid[:, start : start + group]
        normed_two, inverse_two = normed(mid_part)
        ff_in = (normed_two * gains_ff.astype(jnp.float32)[None]).astype(jnp.bfloat16)
        gate_up = per_pos(ff_in, gate_up_full)
        gate_part = gate_up[..., :ff_units]
        up_part = gate_up[..., ff_units:]
        sigmoid_gate = jax.nn.sigmoid(gate_part)
        silu_gate = gate_part * sigmoid_gate
        hidden = (silu_gate * up_part).astype(jnp.bfloat16)
        out_parts.append(mid_part + per_pos(hidden, down_full))
        kept_parts.append(
            (normed_two, inverse_two, ff_in, gate_part, up_part, sigmoid_gate, silu_gate, hidden)
        )
    output = jnp.concatenate(out_parts, axis=1).astype(jnp.bfloat16)
    device_index = lax.axis_index(("dp", "pair"))
    local_ids = jnp.arange(frame_count, dtype=jnp.int32)
    frame_ids = device_index * frame_count + local_ids
    item_ends = jnp.cumsum(item_lengths)
    item_starts = item_ends - item_lengths
    in_item = (frame_ids[:, None] >= item_starts[None, :]) & (
        frame_ids[:, None] < item_ends[None, :]
    )
    item_share = 8 * frame_count / item_lengths.astype(jnp.float32)
    frame_weight = jnp.sum(jnp.where(in_item, item_share[None, :], 0.0), axis=1)
    frame_weight = jnp.where(local_ids < valid_frames[0], frame_weight, 0.0)
    grad_out = cotangent.astype(jnp.float32) * frame_weight[:, None, None]
    mid_grads = []
    share_norm_ff_parts = []
    share_gate_up_parts = []
    share_down_parts = []
    for index, start in enumerate(range(0, positions, group)):
        normed_two, inverse_two, ff_in, gate_part, up_part, sigmoid_gate, silu_gate, hidden = (
            kept_parts[index]
        )
        gains_ff, gate_up_full, down_full = gather_ff_back(norm_ff, w_gate_up, w_down, start, group)
        grad_part = grad_out[:, start : start + group]
        grad_low = grad_part.astype(jnp.bfloat16)
        grad_down = pos_grad(hidden, grad_low)
        d_hidden = per_pos_back(grad_low, down_full)
        d_gate = d_hidden * up_part * sigmoid_gate * (1.0 + gate_part * (1.0 - sigmoid_gate))
        d_up = d_hidden * silu_gate
        d_gate_up = jnp.concatenate([d_gate, d_up], axis=-1).astype(jnp.bfloat16)
        grad_gate_up = pos_grad(ff_in, d_gate_up)
        d_ff_in = per_pos_back(d_gate_up, gate_up_full)
        grad_norm_ff = gain_grad(normed_two, d_ff_in)
        mid_grads.append(
            grad_part
            + norm_back(normed_two, inverse_two, d_ff_in * gains_ff.astype(jnp.float32)[None])
        )
        share_a, share_b, share_c = (
            lax.psum_scatter(grad_norm_ff, ("dp", "pair"), scatter_dimension=0, tiled=True),
            lax.psum_scatter(grad_gate_up, ("dp", "pair"), scatter_dimension=0, tiled=True),
            lax.psum_scatter(grad_down, ("dp", "pair"), scatter_dimension=0, tiled=True),
        )
        share_norm_ff_parts.append(jnp.transpose(share_a))
        share_gate_up_parts.append(back_layout(share_b))
        share_down_parts.append(back_layout(share_c))
    d_mid = jnp.concatenate(mid_grads, axis=1)
    gains_attn, qkv_full, out_full = (
        lax.all_gather(norm_attn, ("dp", "pair"), axis=1, tiled=True),
        lax.all_gather(w_qkv, ("dp", "pair"), axis=1, tiled=True),
        lax.all_gather(w_out, ("dp", "pair"), axis=1, tiled=True),
    )
    d_mid_low = d_mid.astype(jnp.bfloat16)
    grad_out_proj = pos_grad(context, d_mid_low)
    d_context = per_pos_back(d_mid_low, out_full).astype(jnp.bfloat16).reshape(head_shape)
    d_probs = jnp.einsum(
        "fphd,fqhd->fhpq", d_context, value_heads, preferred_element_type=jnp.float32
    )
    d_values = jnp.einsum(
        "fhpq,fphd->fqhd", probs_low, d_context, preferred_element_type=jnp.float32
    )
    d_scores = attn_probs * (d_probs - jnp.sum(attn_probs * d_probs, axis=-1, keepdims=True))
    d_scores = d_scores.astype(jnp.bfloat16)
    d_queries = (
        jnp.einsum("fhpq,fqhd->fphd", d_scores, key_heads, preferred_element_type=jnp.float32)
        * score_scale
    )
    d_keys = (
        jnp.einsum("fhpq,fphd->fqhd", d_scores, queries, preferred_element_type=jnp.float32)
        * score_scale
    )
    row_shape = (frame_count, positions, model_width)
    d_qkv = jnp.concatenate(
        [d_queries.reshape(row_shape), d_keys.reshape(row_shape), d_values.reshape(row_shape)],
        axis=-1,
    ).astype(jnp.bfloat16)
    grad_qkv = pos_grad(attn_in, d_qkv)
    d_attn_in = per_pos_back(d_qkv, qkv_full)
    grad_norm_attn = gain_grad(normed_one, d_attn_in)
    grad_tokens = d_mid + norm_back(
        normed_one, inverse_one, d_attn_in * gains_attn.astype(jnp.float32)[None]
    )
    share_norm_attn, share_qkv, share_out = (
        lax.psum_scatter(grad_norm_attn, ("dp", "pair"), scatter_dimension=0, tiled=True),
        lax.psum_scatter(grad_qkv, ("dp", "pair"), scatter_dimension=0, tiled=True),
        lax.psum_scatter(grad_out_proj, ("dp", "pair"), scatter_dimension=0, tiled=True),
    )
    share_norm_attn = jnp.transpose(share_norm_attn)
    share_qkv = back_layout(share_qkv)
    share_out = back_layout(share_out)
    share_norm_ff = jnp.concatenate(share_norm_ff_parts, axis=0)
    share_gate_up = jnp.concatenate(share_gate_up_parts, axis=0)
    share_down = jnp.concatenate(share_down_parts, axis=0)
    return (
        output,
        grad_tokens,
        share_norm_attn,
        share_qkv,
        share_out,
        share_norm_ff,
        share_gate_up,
        share_down,
    )


MESH_ID = pl.DeviceIdType.MESH
BF16 = jnp.bfloat16
F32 = jnp.float32


def here():
    dp = lax.axis_index("dp")
    core = lax.axis_index("pair")
    return lax.div(dp, 4), lax.rem(lax.div(dp, 2), 2), lax.rem(dp, 2), core


def flip(value, bit):
    return 1 - value if bit else value


def push(src, dst, send_sem, recv_sem, to):
    return pltpu.make_async_remote_copy(
        src_ref=src,
        dst_ref=dst,
        send_sem=send_sem,
        recv_sem=recv_sem,
        device_id=to,
        device_id_type=MESH_ID,
    )


def arrived(dst, recv_sem, to):
    push(dst, dst, recv_sem, recv_sem, to).wait_recv()


def greet_all(z, y, x, core):
    barrier = pltpu.get_barrier_semaphore()
    me = 2 * (z * 4 + y * 2 + x) + core

    def one(step, carry):
        other = lax.rem(me + step, 32)
        pl.semaphore_signal(
            barrier, inc=1, device_id=(lax.div(other, 2), lax.rem(other, 2)), device_id_type=MESH_ID
        )
        return carry

    lax.fori_loop(1, 32, one, 0)
    pl.semaphore_wait(barrier, 31)


def greet(peers):
    barrier = pltpu.get_barrier_semaphore()
    for to in peers:
        pl.semaphore_signal(barrier, inc=1, device_id=to, device_id_type=MESH_ID)
    pl.semaphore_wait(barrier, len(peers))


def maybe(condition, do):
    if condition is None:
        do()
    else:
        pl.when(condition)(do)


OFFSETS = [
    (dz, dy, dx) for dz in (0, -1, 1, -2, 2, -3, 3) for dy in (0, 1) for dx in (0, 1)
]
ORDERS = ("zxy", "zyx", "zyx", "yxz")


def hops(offset):
    return abs(offset[0]) + offset[1] + offset[2]


def arrival_axis(order, offset):
    part = dict(z=offset[0], y=offset[1], x=offset[2])
    last = None
    for axis in order:
        if part[axis] != 0:
            last = axis
    return last


def onward(order, offset):
    directions = []
    last = arrival_axis(order, offset)
    start = 0
    if last is not None:
        start = order.index(last) + 1
        if last == "z":
            directions.append("u" if offset[0] < 0 else "d")
    for axis in order[start:]:
        directions.extend(["u", "d"] if axis == "z" else [axis])
    return directions


def came_from(order, offset):
    last = arrival_axis(order, offset)
    if last == "z":
        return "d" if offset[0] < 0 else "u"
    return last


def offset_exists(offset, z):
    if offset[0] < 0:
        return z >= -offset[0]
    if offset[0] > 0:
        return z <= 3 - offset[0]
    return None


def direction_exists(direction, z):
    return {"u": z < 3, "d": z > 0}.get(direction)


def return_count(order, direction, level):
    return sum(
        hops(offset) > 0 and came_from(order, offset) == direction
        for offset in OFFSETS
        if 0 <= level + offset[0] <= 3
    )


def tree_count(order, direction, level):
    return sum(
        direction in onward(order, offset) for offset in OFFSETS if 0 <= level + offset[0] <= 3
    )


DIRECTIONS = ("x", "y", "u", "d", "s")


def neighbour(direction, z, y, x, core):
    if direction == "x":
        return (z * 4 + y * 2 + 1 - x, core)
    if direction == "y":
        return (z * 4 + (1 - y) * 2 + x, core)
    if direction == "u":
        return (z * 4 + 4 + y * 2 + x, core)
    if direction == "d":
        return (z * 4 - 4 + y * 2 + x, core)
    return (z * 4 + y * 2 + x, 1 - core)


def chip_of(offset, z, y, x):
    return (z + offset[0]) * 4 + flip(y, offset[1]) * 2 + flip(x, offset[2])


RANK_STEPS = sorted(
    ((dl, dx, dc) for dl in (0, 1) for dx in (0, 1) for dc in (0, 1)), key=lambda step: (sum(step), step)
)


def group_place(z, y, x, core):
    zh, zl = lax.div(z, 2), lax.rem(z, 2)

    def member(step):
        return ((2 * zh + flip(zl, step[0])) * 4 + y * 2 + flip(x, step[1]), flip(core, step[2]))

    def rank(step):
        return 4 * flip(zl, step[0]) + 2 * flip(x, step[1]) + flip(core, step[2])

    def device(step, dzh=0, dy=0):
        return 16 * flip(zh, dzh) + 4 * flip(y, dy) + 8 * flip(zl, step[0]) + 2 * flip(x, step[1]) + flip(core, step[2])

    far = ((2 * (1 - zh) + zl) * 4 + y * 2 + x, core)
    across = (z * 4 + (1 - y) * 2 + x, core)
    return zh, zl, member, rank, device, far, across


def add_into(target, sources, rows=16, columns=1024):
    height, width = target.shape
    across = width // columns

    def one(step, carry):
        top = pl.multiple_of(lax.div(step, across) * rows, rows)
        left = pl.multiple_of(lax.rem(step, across) * columns, columns)
        spot = (pl.ds(top, rows), pl.ds(left, columns))
        total = sources[0][spot].astype(F32)
        for source in sources[1:]:
            total = total + source[spot].astype(F32)
        target[spot] = total.astype(target.dtype)
        return carry

    lax.fori_loop(0, (height // rows) * across, one, 0)


def row_loop(height, chunk, body):
    def one(step, carry):
        body(pl.ds(pl.multiple_of(step * chunk, chunk), chunk))
        return carry

    lax.fori_loop(0, height // chunk, one, 0)


def tile_loop(width, tile, body):
    def one(step, carry):
        body(pl.ds(pl.multiple_of(step * tile, tile), tile))
        return carry

    lax.fori_loop(0, width // tile, one, 0)


def dot(left, right):
    return jnp.dot(left, right, preferred_element_type=F32)


def dot_back(left, right):
    return lax.dot_general(left, right, (((1,), (1,)), ((), ())), preferred_element_type=F32)


def dot_grad(left, right):
    return lax.dot_general(left, right, (((0,), (0,)), ((), ())), preferred_element_type=F32)


def make_spread(spread):
    height, width = spread.shape
    head = lax.broadcasted_iota(jnp.int32, (height, width), 0) // HEAD_DIM
    spread[...] = jnp.where(
        head == lax.broadcasted_iota(jnp.int32, (height, width), 1), 1.0, 0.0
    ).astype(BF16)


def pairs_of(positions):
    return [(p, q) for p in range(positions) for q in range(p + 1)]


def split_product(product):
    high = product.astype(BF16)
    return high, (product - high.astype(F32)).astype(BF16)


def sums_over_heads(halves, spread, index):
    return dot(halves[2 * index], spread[...]) + dot(halves[2 * index + 1], spread[...])


def to_heads(values, spread):
    return dot_back(values, spread[...]).astype(BF16)


def attention_probs(qkv, halves, spread, model, position):
    height = qkv.shape[1]
    scale = 1.0 / math.sqrt(HEAD_DIM)

    def products(rows):
        for q in range(position + 1):
            product = qkv[position, rows, :model].astype(F32) * qkv[
                q, rows, model : 2 * model
            ].astype(F32)
            halves[2 * q, rows, :], halves[2 * q + 1, rows, :] = split_product(product)

    row_loop(height, 16, products)
    scores = [sums_over_heads(halves, spread, q) * scale for q in range(position + 1)]
    top = functools.reduce(jnp.maximum, scores)
    powers = [jnp.exp(score - top) for score in scores]
    total = functools.reduce(jnp.add, powers)
    return [power / total for power in powers]


(
    F_TREE,
    F_TREE_END,
    F_GAINS,
    F_PARTS,
    F_COT,
    F_ATTENTION,
    F_GRADS,
    F_ACT_Z,
    F_ACT_X,
    F_ACT_C,
    F_TO_RANK,
    F_OWN_FAR,
    F_OWN_ACROSS,
    F_RANK_FAR,
    F_RANK_ACROSS,
    F_FAR_ACROSS,
    F_FF_END,
    F_BLOCK,
    F_GATE_GRAD,
    F_DOWN_GRAD,
) = range(20)
FORWARD_STEPS = [
    (F_TREE, 5, 0, 0, 0), (F_TREE, 4, 0, 0, 0), (F_TREE, 0, 0, 0, 0), (F_PARTS,), (F_TREE, 2, 0, 0, 0),
    (F_TREE, 1, 0, 0, 0), (F_TREE, 0, 1, 0, 0), (F_TREE, 5, 0, 0, 1), (F_TO_RANK, 0, 2), (F_TREE, 0, -1, 0, 0),
    (F_TO_RANK, 0, 7), (F_TREE, 0, 0, 0, 1), (F_TO_RANK, 0, 1), (F_TO_RANK, 0, 6), (F_TREE, 2, -1, 0, 0),
    (F_TREE, 2, 1, 0, 0), (F_TREE, 0, -1, 0, 1), (F_TO_RANK, 0, 3), (F_OWN_ACROSS, 0, 8), (F_TREE, 0, -2, 0, 0),
    (F_TREE, 4, -1, 0, 0), (F_TREE, 1, 1, 0, 0), (F_TREE, 2, 2, 0, 0), (F_TREE, 3, 0, 0, 0),
    (F_TREE, 1, 0, 1, 0), (F_TREE, 4, 0, 1, 0), (F_RANK_FAR, 0, 3), (F_RANK_FAR, 0, 1), (F_TREE, 1, -1, 0, 0),
    (F_TO_RANK, 1, 5), (F_OWN_ACROSS, 1, 8), (F_TREE, 1, 2, 0, 0), (F_TREE, 2, -2, 0, 0), (F_COT,),
    (F_TREE, 3, 1, 0, 0), (F_OWN_FAR, 0, 0), (F_TREE, 0, 2, 0, 0), (F_TREE, 0, -1, 1, 1), (F_TREE, 3, -1, 0, 0),
    (F_RANK_FAR, 0, 7), (F_GRADS, 0), (F_TREE, 1, -2, 0, 0), (F_TREE, 2, 2, 1, 0), (F_RANK_FAR, 0, 6),
    (F_TREE, 0, -2, 0, 1), (F_TO_RANK, 0, 4), (F_TO_RANK, 0, 5), (F_TREE, 1, 1, 1, 0), (F_TREE, 0, -3, 0, 0),
    (F_TREE, 2, 3, 0, 0), (F_OWN_FAR, 0, 8), (F_TREE, 5, 0, 1, 0), (F_TREE, 1, -2, 1, 0), (F_TREE, 2, -3, 0, 0),
    (F_TREE, 0, -2, 1, 0), (F_RANK_ACROSS, 0, 3), (F_TREE, 0, -3, 0, 1), (F_TREE, 2, -2, 1, 0),
    (F_TREE, 0, 2, 0, 1), (F_TREE, 0, 1, 1, 0), (F_TREE, 5, 1, 0, 1), (F_GAINS,), (F_RANK_ACROSS, 0, 6),
    (F_RANK_FAR, 0, 2), (F_TREE, 2, 0, 1, 0), (F_TREE, 0, 1, 0, 1), (F_TREE, 3, -2, 0, 0),
    (F_TREE, 1, -3, 0, 0), (F_TREE, 2, 1, 1, 0), (F_TREE, 1, 0, 1, 1), (F_TREE, 1, 3, 0, 0),
    (F_TREE, 3, 0, 0, 1), (F_TREE, 2, 1, 0, 1), (F_TREE, 3, 1, 1, 0), (F_TREE, 0, 3, 0, 0),
    (F_TREE, 3, 2, 0, 0), (F_RANK_FAR, 0, 4), (F_RANK_FAR, 0, 5), (F_FAR_ACROSS, 0, 0), (F_TREE, 2, 3, 0, 1),
    (F_FAR_ACROSS, 0, 8), (F_TO_RANK, 1, 4), (F_TREE, 5, 1, 0, 0), (F_TREE, 0, 2, 1, 1), (F_TREE, 1, 3, 1, 0),
    (F_TREE, 2, -3, 0, 1), (F_TREE, 1, 2, 1, 0), (F_TREE, 4, -2, 0, 0), (F_TREE, 5, 2, 0, 1),
    (F_FAR_ACROSS, 0, 2), (F_TREE, 1, -1, 1, 0), (F_RANK_ACROSS, 0, 4), (F_TREE, 1, -3, 1, 0),
    (F_TREE, 4, 1, 0, 0), (F_TREE, 1, 3, 1, 1), (F_TREE, 2, 0, 0, 1), (F_TO_RANK, 1, 6), (F_TREE, 0, 1, 1, 1),
    (F_TREE, 3, -1, 1, 0), (F_TO_RANK, 1, 2), (F_TREE, 2, 3, 1, 0), (F_TREE, 0, -2, 1, 1),
    (F_TREE, 2, -1, 1, 0), (F_TREE, 3, 0, 1, 1), (F_TREE, 4, -1, 1, 0), (F_TREE, 1, 2, 0, 1),
    (F_TREE, 1, -3, 0, 1), (F_OWN_FAR, 1, 8), (F_TREE, 5, 0, 1, 1), (F_ACT_C, 1, 0, 0, 0), (F_TREE, 0, 3, 0, 1),
    (F_TREE, 4, -3, 0, 0), (F_ACT_Z, 1, 0), (F_TREE, 5, 1, 1, 0), (F_TREE, 1, 2, 1, 1), (F_TREE, 5, 3, 0, 1),
    (F_TREE, 3, 3, 0, 0), (F_TREE, 0, -1, 1, 0), (F_TREE, 2, -3, 1, 0), (F_TREE, 2, -2, 1, 1),
    (F_TREE, 4, 0, 0, 1), (F_TREE, 1, 0, 0, 1), (F_TREE, 3, -1, 0, 1), (F_TO_RANK, 1, 1), (F_TREE, 4, 2, 0, 0),
    (F_TREE, 5, -1, 0, 1), (F_GRADS, 1), (F_TREE, 0, -3, 1, 1), (F_TREE, 0, 2, 1, 0), (F_RANK_ACROSS, 0, 1),
    (F_TREE, 4, 0, 1, 1), (F_TREE, 1, -1, 0, 1), (F_TREE, 5, 2, 0, 0), (F_TREE, 3, 2, 0, 1),
    (F_FAR_ACROSS, 0, 6), (F_TREE, 2, -2, 0, 1), (F_ACT_C, 1, 1, 0, 0), (F_TREE, 4, -3, 1, 0),
    (F_TREE, 1, 3, 0, 1), (F_TREE, 0, 0, 1, 0), (F_TREE, 3, -2, 1, 0), (F_RANK_ACROSS, 0, 5),
    (F_TREE, 0, 3, 1, 1), (F_TREE, 5, -1, 1, 0), (F_RANK_FAR, 1, 2), (F_FAR_ACROSS, 0, 1), (F_TREE, 3, 3, 1, 0),
    (F_FAR_ACROSS, 0, 3), (F_TREE, 2, 1, 1, 1), (F_TREE, 1, -2, 1, 1), (F_FAR_ACROSS, 0, 7),
    (F_ACT_C, 1, 0, 1, 0), (F_RANK_ACROSS, 1, 2), (F_TREE, 5, -1, 0, 0), (F_TREE, 1, 1, 1, 1),
    (F_TREE, 0, 0, 1, 1), (F_FAR_ACROSS, 0, 5), (F_TREE, 4, -3, 0, 1), (F_TO_RANK, 1, 3), (F_TREE, 2, 3, 1, 1),
    (F_TREE, 1, -1, 1, 1), (F_TREE, 3, -3, 0, 0), (F_TREE, 4, 1, 1, 0), (F_TREE, 1, 1, 0, 1),
    (F_TREE, 0, -3, 1, 0), (F_TREE, 4, -2, 1, 0), (F_TREE, 1, -3, 1, 1), (F_TREE, 0, 3, 1, 0),
    (F_TREE, 2, 0, 1, 1), (F_TREE, 2, -1, 0, 1), (F_TREE, 1, -2, 0, 1), (F_TREE, 2, 2, 0, 1),
    (F_TREE, 2, -3, 1, 1), (F_TREE, 4, 2, 1, 0), (F_TREE, 4, 3, 0, 0), (F_FAR_ACROSS, 1, 8),
    (F_TREE, 2, -1, 1, 1), (F_TO_RANK, 1, 7), (F_TREE, 2, 2, 1, 1), (F_TREE, 4, 3, 1, 0), (F_RANK_FAR, 1, 4),
    (F_RANK_ACROSS, 0, 7), (F_TREE, 5, -1, 1, 1), (F_RANK_ACROSS, 0, 2), (F_OWN_ACROSS, 1, 0),
    (F_TREE, 4, -1, 0, 1), (F_TREE, 3, -1, 1, 1), (F_FAR_ACROSS, 0, 4), (F_TREE_END, 0), (F_TREE, 3, 1, 0, 1),
    (F_TREE, 3, 0, 1, 0), (F_TREE, 3, -2, 0, 1), (F_ACT_X, 1, 0, 0), (F_ATTENTION, 0), (F_TREE, 5, 1, 1, 1),
    (F_TREE, 4, -2, 1, 1), (F_TREE, 3, -3, 0, 1), (F_ACT_X, 1, 0, 1), (F_RANK_FAR, 1, 3), (F_TREE, 3, 3, 0, 1),
    (F_TREE, 5, -2, 0, 0), (F_TREE, 4, 2, 1, 1), (F_TREE, 5, -2, 1, 1), (F_ACT_C, 1, 0, 0, 1),
    (F_TREE, 5, -3, 0, 0), (F_TREE, 4, -3, 1, 1), (F_ACT_Z, 0, 0), (F_TREE, 4, 2, 0, 1), (F_TREE, 3, -3, 1, 0),
    (F_TREE, 4, 1, 1, 1), (F_OWN_ACROSS, 0, 0), (F_ACT_X, 1, 1, 0), (F_TREE, 5, -2, 1, 0),
    (F_ACT_C, 1, 0, 1, 1), (F_TREE, 5, 2, 1, 0), (F_TREE, 5, -2, 0, 1), (F_FAR_ACROSS, 1, 3), (F_ACT_Z, 1, 1),
    (F_TREE, 5, 2, 1, 1), (F_FAR_ACROSS, 1, 2), (F_TREE, 5, -3, 1, 1), (F_RANK_FAR, 1, 1), (F_RANK_FAR, 1, 7),
    (F_TREE, 3, 2, 1, 1), (F_RANK_ACROSS, 1, 3), (F_TREE, 5, 3, 1, 0), (F_TREE, 4, 1, 0, 1), (F_ACT_X, 0, 0, 0),
    (F_TREE, 4, -1, 1, 1), (F_TREE, 4, -2, 0, 1), (F_RANK_FAR, 1, 6), (F_RANK_FAR, 1, 5), (F_TREE, 5, -3, 0, 1),
    (F_ACT_C, 0, 0, 0, 0), (F_TREE, 3, 2, 1, 0), (F_TREE, 4, 3, 0, 1), (F_ACT_C, 1, 1, 1, 0),
    (F_TREE, 3, -3, 1, 1), (F_TREE, 5, -3, 1, 0), (F_TREE, 3, 3, 1, 1), (F_ACT_C, 0, 0, 0, 1),
    (F_TREE, 3, 1, 1, 1), (F_RANK_ACROSS, 1, 6), (F_TREE, 4, 3, 1, 1), (F_TREE, 5, 3, 1, 1),
    (F_TREE, 3, -2, 1, 1), (F_FAR_ACROSS, 1, 4), (F_OWN_FAR, 1, 0), (F_FF_END, 0), (F_TREE, 5, 3, 0, 0),
    (F_RANK_ACROSS, 1, 1), (F_BLOCK, 0, 2), (F_TREE_END, 1), (F_RANK_ACROSS, 1, 7), (F_ACT_X, 0, 0, 1),
    (F_RANK_ACROSS, 1, 4), (F_ACT_C, 0, 0, 1, 0), (F_RANK_ACROSS, 1, 5), (F_ATTENTION, 1), (F_FAR_ACROSS, 1, 1),
    (F_BLOCK, 0, 1), (F_ACT_X, 1, 1, 1), (F_FAR_ACROSS, 1, 7), (F_FAR_ACROSS, 1, 6), (F_ACT_C, 0, 0, 1, 1),
    (F_BLOCK, 0, 3), (F_BLOCK, 0, 0), (F_FAR_ACROSS, 1, 5), (F_ACT_C, 1, 1, 0, 1), (F_FAR_ACROSS, 1, 0),
    (F_DOWN_GRAD, 0), (F_ACT_Z, 0, 1), (F_ACT_C, 1, 1, 1, 1), (F_ACT_X, 0, 1, 0), (F_GATE_GRAD, 0),
    (F_FF_END, 1), (F_ACT_C, 0, 1, 0, 1), (F_BLOCK, 1, 2), (F_ACT_C, 0, 1, 1, 0), (F_ACT_C, 0, 1, 0, 0),
    (F_BLOCK, 1, 1), (F_ACT_X, 0, 1, 1), (F_BLOCK, 1, 0), (F_ACT_C, 0, 1, 1, 1), (F_BLOCK, 1, 3),
    (F_DOWN_GRAD, 1), (F_GATE_GRAD, 1),
]


def forward_kernel(
    valid_ref,
    lengths_ref,
    norm_attn_ref,
    norm_ff_ref,
    tokens_ref,
    cot_ref,
    qkv_ref,
    out_ref,
    gate_up_ref,
    down_ref,
    gain_rows,
    cot_rows,
    qkv_rows,
    context,
    resid_mid,
    qkv_full,
    out_full,
    ff_out,
    ff_back,
    gate_up_grad,
    down_grad,
    qkv_buf,
    out_buf,
    gate_up_buf,
    down_buf,
    rows_buf,
    grads_buf,
    hidden,
    d_gate_up,
    out_stage,
    back_stage,
    gate_up_stage,
    down_stage,
    gains_own,
    gains_all,
    gate_up_raw,
    gate_up_parts,
    grads_own,
    attn_in,
    halves,
    spread,
    plane_sem,
    sibling_sem,
    send_sem,
    gains_send,
    gains_recv,
    rank_send,
    rank_recv,
    far_send,
    far_recv,
    across_send,
    across_recv,
    act_send,
    act_recv,
    local_sem,
    keep_sem,
    stage_sem,
):
    z, y, x, core = here()
    me = 2 * (z * 4 + y * 2 + x) + core
    zh, zl, member, rank, device, far, across = group_place(z, y, x, core)
    own_step = (0, 0, 0)
    act_height, positions, model = tokens_ref.shape
    height = gate_up_ref.shape[1]
    down_height = down_ref.shape[1]
    split = 4 * down_height
    sibling = neighbour("s", z, y, x, core)
    greet_all(z, y, x, core)
    part = qkv_ref.shape[2] * 12 // 24
    rest = qkv_ref.shape[2] - part
    pieces = []
    for s in range(positions):
        pieces.append((qkv_ref, qkv_buf, s, pl.ds(0, part), "zxy"))
        pieces.append((qkv_ref, qkv_buf, s, pl.ds(part, rest), "zyx"))
        pieces.append((out_ref, out_buf, s, pl.ds(0, model), ("zyx", "yxz")[s % 2]))

    def piece_rows(piece, number):
        _, full, index, columns, _ = pieces[piece]
        return full.at[index, pl.ds(pl.multiple_of(number * height, height), height), columns]

    def tree_send(piece, offset, direction):
        source, _, index, columns, _ = pieces[piece]
        chip = chip_of(offset, z, y, x)
        block = piece_rows(piece, 2 * chip + core)
        return push(
            source.at[index, :, columns] if hops(offset) == 0 else block,
            block,
            send_sem.at[piece, DIRECTIONS.index(direction)],
            sibling_sem.at[piece] if direction == "s" else plane_sem.at[piece, chip],
            neighbour(direction, z, y, x, core),
        )

    def tree_step(piece, offset):
        order = pieces[piece][4]

        def go():
            chip = chip_of(offset, z, y, x)
            if hops(offset) > 0:
                arrived(piece_rows(piece, 2 * chip + core), plane_sem.at[piece, chip], sibling)
            for direction in onward(order, offset) + ["s"]:
                copy = tree_send(piece, offset, direction)
                maybe(direction_exists(direction, z), copy.start)

        maybe(offset_exists(offset, z), go)

    def tree_bytes(piece, count):
        _, full, index, columns, _ = pieces[piece]
        return full.at[index, pl.ds(0, count * height), columns]

    def tree_sent(piece):
        order = pieces[piece][4]

        def sent(direction, count):
            block = tree_bytes(piece, count)
            push(block, block, send_sem.at[piece, DIRECTIONS.index(direction)], gains_recv, sibling).wait_send()

        sent("s", 16)
        for direction in "xy":
            sent(direction, tree_count(order, direction, 3))
        for direction in "ud":
            for level in range(4):
                if level != (3 if direction == "u" else 0):
                    pl.when(z == level)(
                        functools.partial(sent, direction, tree_count(order, direction, level))
                    )

    def tree_end(s):
        mine = [piece for piece in range(len(pieces)) if pieces[piece][2] == s]

        for piece in mine:
            arrived(tree_bytes(piece, 16), sibling_sem.at[piece], sibling)
        for piece in mine:
            tree_own[piece].wait()

    tree_own = [
        pltpu.make_async_copy(
            source.at[index, :, columns], piece_rows(piece, me), local_sem.at[piece]
        )
        for piece, (source, _, index, columns, _) in enumerate(pieces)
    ]

    def gains_copy(step):
        other = lax.rem(me + step, 32)
        return push(
            gains_own,
            gains_all.at[me],
            gains_send,
            gains_recv,
            (lax.div(other, 2), lax.rem(other, 2)),
        )

    def gains_start(step, carry):
        gains_copy(step).start()
        return carry

    def start(copy):
        copy.start()

    def weight_rows(s, number):
        return gate_up_buf.at[s, pl.ds(pl.multiple_of(number * height, height), height), :]

    def down_rows(s, dzh, dy):
        number = 2 * flip(zh, dzh) + flip(y, dy)
        return down_buf.at[s, pl.ds(pl.multiple_of(number * down_height, down_height), down_height), :]

    def act_rows(which, s, step):
        full = (rows_buf, grads_buf)[which]
        return full.at[s, pl.ds(pl.multiple_of(rank(step) * act_height, act_height), act_height), :]

    def send_act(which, s, step, source, hop):
        landed = tuple(bit ^ (1 if axis == hop else 0) for axis, bit in enumerate(step))
        start(
            push(
                source,
                act_rows(which, s, step),
                act_send.at[which, s, hop],
                act_recv.at[which, s, 4 * landed[0] + 2 * landed[1] + landed[2]],
                member(tuple(1 if axis == hop else 0 for axis in range(3))),
            )
        )

    def wait_act(which, s, step):
        arrived(
            act_rows(which, s, step),
            act_recv.at[which, s, 4 * step[0] + 2 * step[1] + step[2]],
            sibling,
        )

    def act_own(which, s):
        source = act_rows(0, s, own_step) if which == 0 else grads_own.at[s]
        for hop in (0, 1, 2):
            send_act(which, s, own_step, source, hop)

    def act_from_z(which, s):
        step = (1, 0, 0)
        wait_act(which, s, step)
        send_act(which, s, step, act_rows(which, s, step), 1)
        send_act(which, s, step, act_rows(which, s, step), 2)

    def act_from_x(which, s, dl):
        wait_act(which, s, (dl, 1, 0))
        send_act(which, s, (dl, 1, 0), act_rows(which, s, (dl, 1, 0)), 2)

    def act_from_core(which, s, dl, dx):
        wait_act(which, s, (dl, dx, 1))

    def mine(s):
        return gate_up_parts.at[rank(own_step), s]

    def ff_source(s, slot):
        return down_ref.at[s] if slot == 8 else mine(s)

    def ff_rows(s, slot, dzh):
        return down_rows(s, dzh, 0) if slot == 8 else weight_rows(s, device(RANK_STEPS[slot], dzh, 0))

    def to_rank(s, slot):
        step = RANK_STEPS[slot]
        start(
            push(
                gate_up_parts.at[rank(step), s],
                weight_rows(s, device(own_step)),
                rank_send.at[s],
                rank_recv.at[s, slot],
                member(step),
            )
        )

    def send_far(s, slot, source):
        start(push(source, ff_rows(s, slot, 0), far_send.at[s], far_recv.at[s, slot], far))

    def send_across(s, slot, source, dzh):
        start(
            push(
                source,
                ff_rows(s, slot, dzh),
                across_send.at[s],
                across_recv.at[s],
                across,
            )
        )

    def own_far(s, slot):
        send_far(s, slot, ff_source(s, slot))

    def own_across(s, slot):
        send_across(s, slot, ff_source(s, slot), 0)

    def rank_far(s, slot):
        arrived(ff_rows(s, slot, 0), rank_recv.at[s, slot], sibling)
        send_far(s, slot, ff_rows(s, slot, 0))

    def rank_across(s, slot):
        send_across(s, slot, ff_rows(s, slot, 0), 0)

    def far_across(s, slot):
        arrived(ff_rows(s, slot, 1), far_recv.at[s, slot], sibling)
        send_across(s, slot, ff_rows(s, slot, 1), 1)

    def ff_end(s):
        for copy in ff_local[s]:
            copy.wait()
        arrived(ff_bytes(s, 2 * share), across_recv.at[s], sibling)

    share = 8 * height + down_height * model // gate_up_buf.shape[2]

    def ff_bytes(s, rows):
        return gate_up_buf.at[s, pl.ds(0, rows), :]

    def ff_sent(s):
        for sem, rows in ((rank_send, 7 * height), (far_send, share), (across_send, 2 * share)):
            block = ff_bytes(s, rows)
            push(block, block, sem.at[s], gains_recv, sibling).wait_send()
        for which, full in enumerate((rows_buf, grads_buf)):
            for hop, count in enumerate((1, 2, 4)):
                block = full.at[s, pl.ds(0, count * act_height), :]
                push(block, block, act_send.at[which, s, hop], gains_recv, sibling).wait_send()

    ff_local = []
    for s in range(positions):
        ff_local.append(
            [
                pltpu.make_async_copy(mine(s), weight_rows(s, device(own_step)), local_sem.at[7 + 3 * s]),
                pltpu.make_async_copy(down_ref.at[s], down_rows(s, 0, 0), local_sem.at[8 + 3 * s]),
                pltpu.make_async_copy(grads_own.at[s], act_rows(1, s, own_step), local_sem.at[9 + 3 * s]),
            ]
        )
    gains_local = pltpu.make_async_copy(gains_own, gains_all.at[me], local_sem.at[6])

    def gains_begin():
        places = 128 // norm_attn_ref.shape[1]
        lane = lax.broadcasted_iota(jnp.int32, (positions, 128), 1) // norm_attn_ref.shape[1]
        gains_own[...] = jnp.zeros_like(gains_own)
        for index, source in enumerate((norm_attn_ref, norm_ff_ref)):
            tiled = jnp.concatenate([source[...].astype(F32)] * places, axis=1)
            gains_own[index * positions : (index + 1) * positions, :] = jnp.where(
                lane == lax.rem(me, places), tiled, 0.0
            ).astype(BF16)
        lax.fori_loop(1, 32, gains_start, 0)
        gains_local.start()

    raw_copy = pltpu.make_async_copy(gate_up_ref, gate_up_raw, local_sem.at[13])

    def part_units():
        raw_copy.wait()
        unit = down_height
        for number in range(8):
            low, rest = divmod(number, 4)
            for s in range(positions):
                for side in (0, 1):
                    for group in range(4):
                        zh_part, y_part = divmod(group, 2)
                        block = 32 * side + 16 * zh_part + 8 * low + 4 * y_part + rest
                        gate_up_parts[number, s, :, (4 * side + group) * unit : (4 * side + group + 1) * unit] = (
                            gate_up_raw[s, :, block * unit : (block + 1) * unit]
                        )
        for s in range(positions):
            ff_local[s][0].start()
            ff_local[s][1].start()

    def weigh():
        def one(rows):
            slot = lax.broadcasted_iota(jnp.int32, (16, 128), 0) + rows.start
            frame = me * act_height + slot
            weight = jnp.zeros((16, 128), F32)
            first = 0
            for item in range(lengths_ref.shape[0]):
                length = lengths_ref[item]
                inside = (frame >= first) & (frame < first + length)
                share = 8.0 * act_height / jnp.full((16, 128), length, jnp.int32).astype(F32)
                weight = weight + jnp.where(inside, share, 0.0)
                first = first + length
            weight = jnp.where(slot < valid_ref[0], weight, 0.0)[:, :1]
            values = cot_ref[rows].astype(F32)
            for p in range(positions):
                grads = values[:, p, :] * weight
                cot_rows[p, rows, :] = grads
                grads_own[p, rows, :] = grads.astype(BF16)

        row_loop(act_height, 16, one)
        for s in range(positions):
            ff_local[s][2].start()

    def take_gains():
        others = gains_all.at[pl.ds(0, 31)]
        arrived(others, gains_recv, sibling)
        push(others, others, gains_send, gains_recv, sibling).wait_send()
        gains_local.wait()
        for block in range(8):
            total = gains_all[4 * block].astype(F32)
            for extra in range(1, 4):
                total = total + gains_all[4 * block + extra].astype(F32)
            gain_rows[:, 128 * block : 128 * block + 128] = total

        def first_norm(rows):
            values = tokens_ref[rows].astype(F32)
            for p in range(positions):
                resid_mid[p, rows, :] = values[:, p, :]
                r, _ = normed(values[:, p, :])
                attn_in[p, rows, :] = (r * gain_rows[p : p + 1, :]).astype(BF16)

        row_loop(act_height, 16, first_norm)

    keep = []

    def attention(p):
        for source, target, slot in (
            (qkv_buf.at[p], qkv_full.at[p], 2 * p),
            (out_buf.at[p], out_full.at[p], 2 * p + 1),
        ):
            keep.append(pltpu.make_async_copy(source, target, keep_sem.at[slot]))
            keep[-1].start()

        def project(columns):
            qkv_rows[p, :, columns] = dot(attn_in[p], qkv_buf[p, :, columns]).astype(BF16)

        tile_loop(3 * model, 512, project)
        probs = attention_probs(qkv_rows, halves, spread, model, p)
        for q in range(p + 1):
            halves[2 * q] = to_heads(probs[q].astype(BF16), spread)

        def mix(rows):
            total = None
            for q in range(p + 1):
                term = halves[2 * q, rows, :].astype(F32) * qkv_rows[q, rows, 2 * model :].astype(F32)
                total = term if total is None else total + term
            context[p, rows, :] = total.astype(BF16)

        row_loop(act_height, 16, mix)

        def attend(columns):
            resid_mid[p, :, columns] += dot(context[p], out_buf[p, :, columns])

        tile_loop(model, 512, attend)

        def second_norm(step, carry):
            rows = pl.ds(pl.multiple_of(step * 16, 16), 16)
            r, _ = normed(resid_mid[p, rows, :])
            top = rank(own_step) * act_height + step * 16
            rows_buf[p, pl.ds(pl.multiple_of(top, 16), 16), :] = (
                r * gain_rows[positions + p : positions + p + 1, :]
            ).astype(BF16)
            return carry

        lax.fori_loop(0, act_height // 16, second_norm, 0)

    def ff_block(s, number):
        rows = pl.ds(pl.multiple_of(number * 2 * act_height, 2 * act_height), 2 * act_height)
        normed_rows = rows_buf[s, rows, :]
        grads = grads_buf[s, rows, :]
        for tile in range(split // 256):
            left, right = pl.ds(tile * 256, 256), pl.ds(split + tile * 256, 256)
            gate = dot(normed_rows, gate_up_buf[s, :, left])
            up = dot(normed_rows, gate_up_buf[s, :, right])
            d_hidden = dot_back(grads, down_buf[s, left, :])
            sigmoid_gate = jax.nn.sigmoid(gate)
            silu_gate = gate * sigmoid_gate
            hidden[rows, left] = (silu_gate * up).astype(BF16)
            d_gate_up[rows, left] = (
                d_hidden * up * sigmoid_gate * (1.0 + gate * (1.0 - sigmoid_gate))
            ).astype(BF16)
            d_gate_up[rows, right] = (d_hidden * silu_gate).astype(BF16)
        for tile in range(model // 512):
            columns = pl.ds(tile * 512, 512)
            out_stage[rows, columns] = dot(hidden[rows, :], down_buf[s, :, columns]).astype(BF16)
            back_stage[rows, columns] = dot_back(
                d_gate_up[rows, :], gate_up_buf[s, columns, :]
            ).astype(BF16)

    stages = []

    def stage_out(s, *slots):
        for slot in slots:
            source, target = (
                (out_stage, ff_out),
                (back_stage, ff_back),
                (gate_up_stage, gate_up_grad),
                (down_stage, down_grad),
            )[slot]
            stages.append(pltpu.make_async_copy(source, target.at[s], stage_sem.at[s, slot]))
            stages[-1].start()

    def gate_grad(s):
        stage_out(s, 0, 1)

        def gate_up_tile(columns):
            gate_up_stage[:, columns] = dot_grad(rows_buf[s], d_gate_up[:, columns]).astype(BF16)

        tile_loop(2 * split, 256, gate_up_tile)
        stage_out(s, 2)

    def down_weights_grad(s):
        def down_tile(columns):
            down_stage[:, columns] = dot_grad(hidden[...], grads_buf[s, :, columns]).astype(BF16)

        tile_loop(model, 256, down_tile)
        stage_out(s, 3)

    def stages_end():
        while stages:
            stages.pop(0).wait()

    for copy in tree_own:
        copy.start()
    raw_copy.start()
    gains_begin()
    make_spread(spread)
    chips = ((0, 0), (1, 0), (0, 1), (1, 1))

    def block(s, order):
        if s > 0 and order == chosen_first[0]:
            stages_end()
        ff_block(s, 2 * flip(zl, chips[order][0]) + flip(x, chips[order][1]))

    def attend_and_send(s):
        attention(s)
        act_own(0, s)

    chosen_first = [step[2] for step in FORWARD_STEPS if step[:2] == (F_BLOCK, 1)]
    kinds = {
        F_TREE: lambda piece, dz, dy, dx: tree_step(piece, (dz, dy, dx)),
        F_TREE_END: tree_end,
        F_GAINS: take_gains,
        F_PARTS: part_units,
        F_COT: weigh,
        F_ATTENTION: attend_and_send,
        F_GRADS: lambda s: act_own(1, s),
        F_ACT_Z: act_from_z,
        F_ACT_X: act_from_x,
        F_ACT_C: act_from_core,
        F_TO_RANK: to_rank,
        F_OWN_FAR: own_far,
        F_OWN_ACROSS: own_across,
        F_RANK_FAR: rank_far,
        F_RANK_ACROSS: rank_across,
        F_FAR_ACROSS: far_across,
        F_FF_END: ff_end,
        F_BLOCK: block,
        F_GATE_GRAD: gate_grad,
        F_DOWN_GRAD: down_weights_grad,
    }
    for kind, *numbers in FORWARD_STEPS:
        kinds[kind](*numbers)
    for piece in range(len(pieces)):
        tree_sent(piece)
    for s in range(positions):
        ff_sent(s)
    for copy in keep:
        copy.wait()
    stages_end()


def forward_gather(valid, lengths, norm_attn, norm_ff, tokens, cot, w_qkv, w_out, w_gate_up, w_down):
    act_height, positions, model = tokens.shape
    _, height, qkv_width = w_qkv.shape
    unit = w_down.shape[1]
    ranks, split, width = 8, 4 * unit, 8 * unit
    group_rows = ranks * act_height
    dma = pltpu.SemaphoreType.DMA
    vmem = pl.BlockSpec(memory_space=pltpu.VMEM)
    smem = pl.BlockSpec(memory_space=pltpu.SMEM)
    anywhere = pl.BlockSpec(memory_space=pl.ANY)
    return pl.pallas_call(
        forward_kernel,
        out_shape=(
            jax.ShapeDtypeStruct((16, model), F32),
            jax.ShapeDtypeStruct((positions, act_height, model), F32),
            jax.ShapeDtypeStruct((positions, act_height, 3 * model), BF16),
            jax.ShapeDtypeStruct((positions, act_height, model), BF16),
            jax.ShapeDtypeStruct((positions, act_height, model), F32),
            jax.ShapeDtypeStruct((positions, model, qkv_width), BF16),
            jax.ShapeDtypeStruct((positions, model, model), BF16),
            jax.ShapeDtypeStruct((positions, group_rows, model), BF16),
            jax.ShapeDtypeStruct((positions, group_rows, model), BF16),
            jax.ShapeDtypeStruct((positions, model, width), BF16),
            jax.ShapeDtypeStruct((positions, split, model), BF16),
        ),
        in_specs=[smem] * 2 + [vmem] * 4 + [anywhere] * 4,
        out_specs=(vmem,) * 5 + (anywhere,) * 6,
        scratch_shapes=[
            pltpu.VMEM((positions, model, qkv_width), BF16),
            pltpu.VMEM((positions, model, model), BF16),
            pltpu.VMEM((positions, model, width), BF16),
            pltpu.VMEM((positions, split, model), BF16),
            pltpu.VMEM((positions, group_rows, model), BF16),
            pltpu.VMEM((positions, group_rows, model), BF16),
            pltpu.VMEM((group_rows, split), BF16),
            pltpu.VMEM((group_rows, width), BF16),
            pltpu.VMEM((group_rows, model), BF16),
            pltpu.VMEM((group_rows, model), BF16),
            pltpu.VMEM((model, width), BF16),
            pltpu.VMEM((split, model), BF16),
            pltpu.VMEM((16, 128), BF16),
            pltpu.VMEM((32, 16, 128), BF16),
            pltpu.VMEM(w_gate_up.shape, BF16),
            pltpu.VMEM((ranks, positions, height, width), BF16),
            pltpu.VMEM((positions, act_height, model), BF16),
            pltpu.VMEM((positions, act_height, model), BF16),
            pltpu.VMEM((2 * positions, act_height, model), BF16),
            pltpu.VMEM((model, 128), BF16),
            dma((6, 16)),
            dma((6,)),
            dma((6, 5)),
            dma,
            dma,
            dma((2,)),
            dma((2, 8)),
            dma((2,)),
            dma((2, 9)),
            dma((2,)),
            dma((2,)),
            dma((2, 2, 3)),
            dma((2, 2, 8)),
            dma((14,)),
            dma((4,)),
            dma((2, 4)),
        ],
        compiler_params=pltpu.CompilerParams(
            collective_id=4, has_side_effects=True, vmem_limit_bytes=62 * 2**20
        ),
        name="forward_gather",
    )(valid, lengths, norm_attn, norm_ff, tokens, cot, w_qkv, w_out, w_gate_up, w_down)


def slot_index(order, direction, offset, z, y, x):
    axis = {"u": "z", "d": "z"}.get(direction, direction)
    index, count = 0, 1
    values = dict(z=z + offset[0], y=flip(y, offset[1]), x=flip(x, offset[2]))
    sizes = dict(z=4, y=2, x=2)
    for earlier in order[: order.index(axis)]:
        index = index * sizes[earlier] + values[earlier]
        count *= sizes[earlier]
    if axis == "z":
        index = index * 5 + (4 if direction == "d" and offset[0] == 0 else values["z"])
        count *= 5
    return index, count


def slot_base(order):
    base, total = {}, 0
    for axis, direction in (("x", "x"), ("y", "y"), ("z", "u")):
        base[axis] = total
        total += slot_index(order, direction, (0, 0, 0), 0, 0, 0)[1]
    base["u"] = base["d"] = base["z"]
    return base, total


(
    B_TREE,
    B_RS_ACROSS,
    B_RS_FIRST,
    B_RS_SECOND,
    B_RS_RANK,
    B_RS_LAST,
    B_ACT_CORE,
    B_ACT_LOAD,
    B_ACT_ADD_X,
    B_ACT_ADD_Z,
    B_ACT_SUM,
    B_NORM_TURN,
    B_SWAP_TURNED,
    B_PROBS,
    B_MID,
    B_SCORES_BACK,
    B_SWAP_QKV,
    B_OUT_W,
    B_QKV_W,
    B_ROWS_BACK,
    B_ATTN_BACK,
    B_FINISH_OUTPUT,
) = range(22)
BACKWARD_STEPS = [
    (B_ACT_CORE, 0, 0), (B_RS_ACROSS, 0, 0, 0), (B_ACT_ADD_X, 0, 0, 1), (B_RS_ACROSS, 0, 0, 1),
    (B_RS_ACROSS, 0, 1, 0), (B_ACT_CORE, 0, 1), (B_ACT_CORE, 1, 1), (B_NORM_TURN,), (B_ACT_ADD_X, 0, 0, 0),
    (B_ACT_ADD_X, 0, 1, 1), (B_RS_ACROSS, 0, 1, 1), (B_RS_FIRST, 0, 0), (B_ACT_ADD_Z, 0, 0), (B_RS_FIRST, 0, 1),
    (B_ACT_ADD_Z, 0, 1), (B_RS_ACROSS, 0, 0, 2), (B_PROBS,), (B_SWAP_TURNED,), (B_ACT_ADD_X, 0, 1, 0),
    (B_ACT_CORE, 1, 0), (B_ACT_SUM, 0, 0), (B_RS_ACROSS, 1, 0, 2), (B_MID, 0), (B_RS_ACROSS, 1, 0, 1),
    (B_OUT_W, 0), (B_TREE, 2, -1, 1, 1), (B_TREE, 2, -3, 1, 1), (B_TREE, 2, 2, 1, 1), (B_RS_FIRST, 0, 2),
    (B_TREE, 2, 3, 1, 1), (B_TREE, 2, 0, 0, 1), (B_TREE, 2, 1, 0, 1), (B_ACT_SUM, 0, 1), (B_TREE, 2, 3, 0, 1),
    (B_TREE, 2, 0, 1, 1), (B_TREE, 2, 1, 1, 1), (B_MID, 1), (B_ACT_LOAD, 1), (B_RS_ACROSS, 1, 0, 0),
    (B_ACT_ADD_X, 1, 1, 0), (B_ACT_ADD_X, 1, 0, 0), (B_SCORES_BACK,), (B_SWAP_QKV,), (B_OUT_W, 1),
    (B_RS_FIRST, 1, 1), (B_ACT_ADD_X, 1, 1, 1), (B_RS_ACROSS, 1, 1, 0), (B_QKV_W, 0), (B_TREE, 3, 2, 0, 1),
    (B_TREE, 0, -1, 1, 1), (B_RS_SECOND, 0, 1), (B_RS_SECOND, 0, 0), (B_ACT_ADD_X, 1, 0, 1), (B_QKV_W, 1),
    (B_RS_RANK, 0, 3), (B_TREE, 3, 3, 0, 1), (B_TREE, 2, -3, 1, 0), (B_RS_ACROSS, 1, 1, 1),
    (B_TREE, 2, 3, 1, 0), (B_ROWS_BACK, 0), (B_TREE, 1, -3, 1, 1), (B_TREE, 0, 2, 1, 1), (B_TREE, 1, 2, 1, 1),
    (B_TREE, 0, 3, 1, 1), (B_TREE, 2, -2, 1, 1), (B_RS_RANK, 0, 7), (B_TREE, 1, -2, 1, 1),
    (B_TREE, 3, -2, 1, 1), (B_TREE, 3, 3, 1, 0), (B_TREE, 0, -2, 1, 1), (B_TREE, 0, 0, 1, 1),
    (B_TREE, 3, 2, 1, 0), (B_RS_FIRST, 1, 0), (B_TREE, 1, -1, 0, 1), (B_TREE, 3, 3, 1, 1),
    (B_TREE, 3, -3, 1, 1), (B_TREE, 0, -3, 1, 1), (B_TREE, 3, -2, 1, 0), (B_TREE, 1, -3, 0, 1),
    (B_TREE, 3, 2, 1, 1), (B_TREE, 3, -3, 1, 0), (B_TREE, 3, -1, 1, 0), (B_TREE, 0, 2, 1, 0),
    (B_TREE, 3, -3, 0, 1), (B_RS_SECOND, 1, 1), (B_TREE, 3, -2, 0, 1), (B_TREE, 3, -3, 0, 0),
    (B_TREE, 0, 3, 0, 1), (B_TREE, 1, -1, 1, 1), (B_TREE, 1, 3, 1, 1), (B_TREE, 0, -1, 1, 0),
    (B_TREE, 0, 3, 1, 0), (B_TREE, 2, 3, 0, 0), (B_TREE, 1, 0, 1, 1), (B_TREE, 1, 1, 0, 1),
    (B_TREE, 2, 2, 1, 0), (B_ACT_ADD_Z, 1, 0), (B_ACT_ADD_Z, 1, 1), (B_TREE, 3, -1, 1, 1), (B_RS_LAST, 0, 7),
    (B_TREE, 2, -2, 1, 0), (B_TREE, 2, -2, 0, 1), (B_TREE, 0, 3, 0, 0), (B_TREE, 2, -1, 1, 0),
    (B_RS_SECOND, 1, 0), (B_TREE, 2, -3, 0, 1), (B_TREE, 1, 3, 0, 1), (B_RS_RANK, 1, 3), (B_TREE, 1, 3, 1, 0),
    (B_TREE, 3, 1, 1, 0), (B_RS_RANK, 1, 1), (B_TREE, 1, -3, 1, 0), (B_TREE, 1, 1, 1, 1), (B_RS_RANK, 1, 5),
    (B_TREE, 3, 1, 0, 1), (B_TREE, 0, -3, 0, 1), (B_TREE, 3, -2, 0, 0), (B_RS_FIRST, 1, 2),
    (B_TREE, 0, 1, 1, 1), (B_TREE, 1, -2, 0, 1), (B_TREE, 3, 1, 1, 1), (B_TREE, 0, -3, 1, 0), (B_RS_RANK, 1, 2),
    (B_TREE, 0, 2, 0, 1), (B_ROWS_BACK, 1), (B_RS_RANK, 0, 5), (B_TREE, 3, 3, 0, 0), (B_RS_ACROSS, 0, 1, 2),
    (B_TREE, 1, 3, 0, 0), (B_TREE, 0, 1, 1, 0), (B_RS_RANK, 0, 1), (B_RS_RANK, 0, 4), (B_RS_RANK, 1, 4),
    (B_TREE, 0, -2, 0, 1), (B_TREE, 2, 2, 0, 1), (B_TREE, 1, -2, 1, 0), (B_TREE, 3, -1, 0, 1),
    (B_TREE, 0, -2, 1, 0), (B_TREE, 2, -3, 0, 0), (B_TREE, 1, 2, 1, 0), (B_TREE, 3, 0, 1, 1), (B_ACT_SUM, 1, 0),
    (B_TREE, 1, 2, 0, 1), (B_RS_ACROSS, 1, 1, 2), (B_RS_RANK, 0, 6), (B_TREE, 0, -3, 0, 0),
    (B_TREE, 1, -3, 0, 0), (B_TREE, 0, 2, 0, 0), (B_RS_RANK, 0, 2), (B_RS_RANK, 1, 6), (B_ACT_SUM, 1, 1),
    (B_TREE, 1, -1, 1, 0), (B_TREE, 2, 1, 1, 0), (B_FINISH_OUTPUT,), (B_TREE, 2, 2, 0, 0), (B_RS_LAST, 0, 4),
    (B_RS_LAST, 0, 5), (B_TREE, 0, 1, 0, 1), (B_RS_LAST, 0, 3), (B_TREE, 0, -1, 0, 1), (B_TREE, 1, -2, 0, 0),
    (B_RS_LAST, 1, 1), (B_TREE, 0, -2, 0, 0), (B_TREE, 3, 2, 0, 0), (B_RS_SECOND, 0, 2), (B_RS_LAST, 1, 2),
    (B_TREE, 1, 1, 1, 0), (B_RS_LAST, 1, 3), (B_TREE, 2, -1, 0, 1), (B_TREE, 0, 0, 0, 1), (B_TREE, 1, 0, 0, 1),
    (B_TREE, 2, 0, 1, 0), (B_TREE, 2, -2, 0, 0), (B_RS_LAST, 1, 4), (B_RS_SECOND, 1, 2), (B_TREE, 1, 2, 0, 0),
    (B_RS_LAST, 0, 2), (B_TREE, 3, 1, 0, 0), (B_TREE, 3, -1, 0, 0), (B_TREE, 3, 0, 1, 0), (B_TREE, 1, -1, 0, 0),
    (B_TREE, 1, 1, 0, 0), (B_RS_RANK, 1, 7), (B_TREE, 1, 0, 1, 0), (B_RS_LAST, 0, 1), (B_TREE, 0, 1, 0, 0),
    (B_TREE, 3, 0, 0, 1), (B_TREE, 0, 0, 1, 0), (B_TREE, 0, -1, 0, 0), (B_RS_LAST, 1, 5), (B_TREE, 2, 1, 0, 0),
    (B_RS_LAST, 0, 6), (B_ATTN_BACK,), (B_RS_LAST, 1, 6), (B_TREE, 2, -1, 0, 0), (B_TREE, 1, 0, 0, 0),
    (B_RS_LAST, 1, 7), (B_TREE, 0, 0, 0, 0), (B_TREE, 2, 0, 0, 0), (B_TREE, 3, 0, 0, 0),
]


def backward_kernel(
    tokens_ref,
    cot_ref,
    gain_rows,
    qkv_rows,
    context,
    resid_mid,
    qkv_full,
    out_full,
    out_ref,
    back_ref,
    gate_up_ref,
    down_ref,
    output,
    grad_tokens,
    norm_attn_sum,
    norm_ff_sum,
    qkv_sum,
    attn_out_sum,
    gate_up_total,
    down_sum,
    act_own,
    core_buf,
    x_buf,
    z_buf,
    gate_own,
    down_own,
    across_gate,
    across_down,
    far_gate,
    far_down,
    qkv_grad,
    out_grad,
    slots_0,
    slots_1,
    slots_2,
    slots_3,
    qkv_tiles,
    out_tiles,
    turned,
    attn_turned,
    context_turned,
    d_qkv,
    d_mid_low,
    d_mid,
    d_context,
    d_rows,
    halves,
    probs_buf,
    spread,
    gain_acc,
    gains_part,
    gains_buf,
    gains_sum,
    gate_up_sum,
    core_send,
    core_recv,
    x_send,
    x_recv,
    z_send,
    z_recv,
    across_send,
    across_recv,
    far_send,
    far_recv,
    rank_send,
    rank_recv,
    swap_send,
    swap_recv,
    tree_send,
    tree_recv,
    gains_send,
    gains_recv,
    own_sem,
    part_sem,
    tile_sem,
):
    z, y, x, core = here()
    me = 2 * (z * 4 + y * 2 + x) + core
    zh, zl, member, rank, device, far, across = group_place(z, y, x, core)
    own_step = (0, 0, 0)
    act_height, positions, model = tokens_ref.shape
    sets = positions
    height = qkv_sum.shape[1]
    down_height = down_sum.shape[1]
    half = 16 * height
    sibling = member((0, 0, 1))
    scale = 1.0 / math.sqrt(HEAD_DIM)
    pairs = pairs_of(positions)
    greet_all(z, y, x, core)
    sends = []

    def start(copy):
        copy.start()
        sends.append(copy)

    def run_rows(dzh, dy, low):
        number = 16 * flip(zh, dzh) + 4 * flip(y, dy) + 8 * low
        return pl.ds(pl.multiple_of(number * height, 4 * height), 4 * height)

    def down_rows(dzh, dy):
        number = 2 * flip(zh, dzh) + flip(y, dy)
        return pl.ds(pl.multiple_of(number * down_height, down_height), down_height)

    def ff_from(s, dzh, dy, part):
        if part == 2:
            return down_ref.at[s, down_rows(dzh, dy)]
        return gate_up_ref.at[s, run_rows(dzh, dy, part)]

    def ff_across(s, turn, part):
        return across_down.at[turn, s] if part == 2 else across_gate.at[turn, s, part]

    def ff_own(s, turn, part):
        return down_own.at[turn, s] if part == 2 else gate_own.at[turn, s, part]

    def ff_far(s, part):
        return far_down.at[s] if part == 2 else far_gate.at[s, part]

    def part_copy(s, turn, part):
        return pltpu.make_async_copy(
            ff_from(s, 1 - turn, 0, part), ff_own(s, turn, part), part_sem.at[turn, s, part]
        )

    def rs_across(s, turn, part):
        start(
            push(
                ff_from(s, 1 - turn, 1, part),
                ff_across(s, turn, part),
                across_send.at[turn, s, part],
                across_recv.at[turn, s, part],
                across,
            )
        )

    def rs_first(s, part):
        block = ff_across(s, 0, part)
        part_copy(s, 0, part).wait()
        arrived(block, across_recv.at[0, s, part], across)
        add_into(block, [block, ff_own(s, 0, part)])
        start(push(block, ff_far(s, part), far_send.at[s, part], far_recv.at[s, part], far))

    def rs_second(s, part):
        block = ff_across(s, 1, part)
        part_copy(s, 1, part).wait()
        arrived(block, across_recv.at[1, s, part], across)
        arrived(ff_far(s, part), far_recv.at[s, part], far)
        target = down_sum.at[s] if part == 2 else block
        add_into(target, [block, ff_far(s, part), ff_own(s, 1, part)])

    def share(step, s):
        number = 2 * flip(x, step[1]) + flip(core, step[2])
        return across_gate.at[
            1, s, flip(zl, step[0]), pl.ds(pl.multiple_of(number * height, height), height)
        ]

    def place_units(step, s, source):
        unit = down_height
        number = 8 * flip(zl, step[0]) + 2 * flip(x, step[1]) + flip(core, step[2])
        for side in (0, 1):
            for group in range(4):
                zh_part, y_part = divmod(group, 2)
                left = (32 * side + 16 * zh_part + 4 * y_part + number) * unit
                gate_up_total[s, :, pl.ds(pl.multiple_of(left, unit), unit)] = source[
                    :, (4 * side + group) * unit : (4 * side + group + 1) * unit
                ].astype(F32)

    def rs_rank(s, slot):
        step = RANK_STEPS[slot]
        push(
                share(step, s),
                gate_up_sum.at[rank(own_step), s],
                rank_send.at[s],
                rank_recv.at[slot, s],
                member(step),
            ).start()

    def rs_last(s, slot):
        step = RANK_STEPS[slot]
        block = gate_up_sum.at[rank(step), s]
        arrived(block, rank_recv.at[slot, s], member(step))
        place_units(step, s, block)

    acts = [back_ref, out_ref]

    def act_rows(step):
        return pl.ds(pl.multiple_of(rank(step) * act_height, act_height), act_height)

    def act_core(which, s):
        for dl, dx in ((1, 1), (0, 1), (1, 0), (0, 0)):
            start(
                push(
                    acts[which].at[s, act_rows((dl, dx, 1))],
                    core_buf.at[which, s, dl, dx],
                    core_send.at[which, s, dl, dx],
                    core_recv.at[which, s, dl, dx],
                    sibling,
                )
            )

    def act_copy(which, s, dl, dx):
        return pltpu.make_async_copy(
            acts[which].at[s, act_rows((dl, dx, 0))],
            act_own.at[s, dl, dx],
            own_sem.at[which, s, dl, dx],
        )

    def act_load(which):
        for s in range(sets):
            for dl in (0, 1):
                for dx in (0, 1):
                    act_copy(which, s, dl, dx).start()

    def act_ready(which, s, dl, dx):
        act_copy(which, s, dl, dx).wait()
        arrived(core_buf.at[which, s, dl, dx], core_recv.at[which, s, dl, dx], sibling)

    def act_add_x(which, s, dl):
        act_ready(which, s, dl, 1)
        block = core_buf.at[which, s, dl, 1]
        add_into(block, [block, act_own.at[s, dl, 1]])
        start(
            push(
                block,
                x_buf.at[which, s, dl],
                x_send.at[which, s, dl],
                x_recv.at[which, s, dl],
                member((0, 1, 0)),
            )
        )

    def act_add_z(which, s):
        act_ready(which, s, 1, 0)
        block = x_buf.at[which, s, 1]
        arrived(block, x_recv.at[which, s, 1], member((0, 1, 0)))
        add_into(block, [block, core_buf.at[which, s, 1, 0], act_own.at[s, 1, 0]])
        start(
            push(
                block, z_buf.at[which, s], z_send.at[which, s], z_recv.at[which, s], member((1, 0, 0))
            )
        )

    def act_sum(which, s):
        act_ready(which, s, 0, 0)
        arrived(x_buf.at[which, s, 0], x_recv.at[which, s, 0], member((0, 1, 0)))
        arrived(z_buf.at[which, s], z_recv.at[which, s], member((1, 0, 0)))

    def act_total(which, s, rows):
        return (
            act_own[s, 0, 0, rows, :].astype(F32)
            + core_buf[which, s, 0, 0, rows, :].astype(F32)
            + x_buf[which, s, 0, rows, :].astype(F32)
            + z_buf[which, s, rows, :].astype(F32)
        )

    pieces = [
        (qkv_grad, qkv_sum, 0, "zxy", slots_0),
        (qkv_grad, qkv_sum, 1, "zyx", slots_1),
        (out_grad, attn_out_sum, 0, "zyx", slots_2),
        (out_grad, attn_out_sum, 1, "yxz", slots_3),
    ]
    events = sorted(
        ((-hops(offset), place, piece, offset) for piece in range(4) for place, offset in enumerate(OFFSETS)),
        key=lambda event: event[:3],
    )

    def tree_block(piece, offset):
        source, _, index, _, _ = pieces[piece]
        chip = chip_of(offset, z, y, x)
        return source.at[index, pl.ds(pl.multiple_of(chip * height, height), height), :]

    def tree_copy(piece, offset):
        _, _, _, order, slots = pieces[piece]
        toward = came_from(order, offset)
        base, _ = slot_base(order)
        seen = {"x": "x", "y": "y", "u": "d", "d": "u"}[toward]
        nearer = offset
        if toward == "u":
            nearer = (offset[0] - 1, offset[1], offset[2])
        if toward == "d":
            nearer = (offset[0] + 1, offset[1], offset[2])
        there = {"u": z + 1, "d": z - 1}.get(toward, z)
        index_there, _ = slot_index(
            order, seen, nearer, there, y if toward != "y" else 1 - y, x if toward != "x" else 1 - x
        )
        if toward in "xy":
            index_there, _ = slot_index(order, seen, offset, z, y, x)
        place = base[seen] + index_there
        return push(
            tree_block(piece, offset),
            slots.at[place],
            tree_send.at[piece, DIRECTIONS.index(toward)],
            tree_recv.at[piece, place],
            neighbour(toward, z, y, x, core),
        )

    def tree_step(piece, offset):
        _, result, index, order, slots = pieces[piece]
        base, _ = slot_base(order)

        def go():
            block = tree_block(piece, offset)
            sure, unsure = [], []
            for direction in onward(order, offset):
                local, _ = slot_index(order, direction, offset, z, y, x)
                place = base[direction] + local
                (sure if direction in "xy" else unsure).append((direction, place))
            terms = [block]
            for _, place in sure:
                arrived(slots.at[place], tree_recv.at[piece, place], sibling)
                terms.append(slots.at[place])
            last = hops(offset) == 0
            target = result.at[index] if last else block
            if last or len(terms) > 1:
                add_into(target, terms)
            for direction, place in unsure:

                def more(place=place):
                    arrived(slots.at[place], tree_recv.at[piece, place], sibling)
                    add_into(target, [target, slots.at[place]])

                maybe(direction_exists(direction, z), more)
            if not last:
                tree_copy(piece, offset).start()

        maybe(offset_exists(offset, z), go)

    def gains_copy(step):
        other = lax.rem(me + step, 32)
        return push(
            gains_part.at[lax.div(other, 4)],
            gains_buf.at[me],
            gains_send,
            gains_recv,
            (lax.div(other, 2), lax.rem(other, 2)),
        )

    def gains_start(step, carry):
        gains_copy(step).start()
        return carry

    def gains_add(step, carry):
        gains_sum[...] += gains_buf[lax.rem(me + step, 32)]
        return carry

    def turn(source, target, slot):
        def one(block, p):
            flat = source(p, block)
            turned[slot, p, pl.ds(2 * block, 2)] = flat.T.astype(BF16).reshape(2, 2, height, act_height)

        for p in range(positions):
            for block in range(model // 128):
                one(block, p)
            target[p, :, :, :act_height] = turned[slot, p, :, core]

    qkv_tile = qkv_tiles.shape[1]
    tile_count = model // qkv_tile

    def qkv_load(number):
        p, tile = divmod(number, tile_count)
        return pltpu.make_async_copy(
            qkv_full.at[p, pl.ds(tile * qkv_tile, qkv_tile)],
            qkv_tiles.at[number % 2],
            tile_sem.at[number % 2],
        )

    out_loads = [
        pltpu.make_async_copy(out_full.at[p], out_tiles.at[p], tile_sem.at[2 + p]) for p in range(positions)
    ]

    def context_block(p, block):
        return context[p, :, 128 * block : 128 * block + 128].astype(F32)

    def attn_block(p, block):
        return d_rows[p, :, 128 * block : 128 * block + 128]

    def norm_turn():
        def attn_norm(rows):
            values = tokens_ref[rows].astype(F32)
            for p in range(positions):
                r, _ = normed(values[:, p, :])
                d_rows[p, rows, :] = r * gain_rows[p : p + 1, :]

        row_loop(act_height, 16, attn_norm)
        turn(context_block, context_turned, 0)
        turn(attn_block, attn_turned, 1)

    def landing(kind, p):
        other = pl.ds(act_height, act_height)
        return (
            context_turned.at[p, :, :, other],
            attn_turned.at[p, :, :, other],
            d_mid_low.at[p, other],
            d_qkv.at[p, other],
        )[kind]

    def swap(kind, p, source):
        start(
            push(source, landing(kind, p), swap_send.at[4 * p + kind], swap_recv.at[4 * p + kind], sibling)
        )

    def swap_wait(kind, p):
        arrived(landing(kind, p), swap_recv.at[4 * p + kind], sibling)

    def swap_turned():
        for p in range(positions):
            swap(0, p, turned.at[0, p, :, 1 - core])
            swap(1, p, turned.at[1, p, :, 1 - core])

    def find_probs():
        for p in range(positions):
            probs = attention_probs(qkv_rows, halves, spread, model, p)
            for q in range(p + 1):
                probs_buf[pairs.index((p, q))] = probs[q]

    def mid(p):
        def mid_back(rows):
            d_ff_in = act_total(0, p, rows)
            r, inverse = normed(resid_mid[p, rows, :])
            gain_acc[positions + p] += r * d_ff_in
            total = cot_ref[p, rows, :] + norm_back(
                r, inverse, d_ff_in * gain_rows[positions + p : positions + p + 1, :]
            )
            d_mid[p, rows, :] = total
            d_mid_low[p, rows, :] = total.astype(BF16)

        row_loop(act_height, 16, mid_back)
        swap(2, p, d_mid_low.at[p, pl.ds(0, act_height)])
        out_loads[p].wait()

        def context_back(columns):
            d_context[p, :, columns] = dot_back(
                d_mid_low[p, :act_height, :], out_tiles[p, columns, :]
            ).astype(BF16)

        tile_loop(model, 256, context_back)

    def scores_back():
        def context_products(rows):
            for index, (p, q) in enumerate(pairs):
                product = d_context[p, rows, :].astype(F32) * qkv_rows[q, rows, 2 * model :].astype(F32)
                halves[2 * index, rows, :], halves[2 * index + 1, rows, :] = split_product(product)

        row_loop(act_height, 16, context_products)
        d_probs = [sums_over_heads(halves, spread, index) for index in range(len(pairs))]
        for p in range(positions):
            own = [index for index, pair in enumerate(pairs) if pair[0] == p]
            mean = functools.reduce(jnp.add, [probs_buf[index] * d_probs[index] for index in own])
            for index in own:
                d_score = (probs_buf[index] * (d_probs[index] - mean)).astype(BF16)
                halves[2 * index] = to_heads(d_score, spread)
                halves[2 * index + 1] = to_heads(probs_buf[index].astype(BF16), spread)

        def plus(total, term):
            return term if total is None else total + term

        def qkv_back(rows):
            d_keys = [None] * positions
            d_values = [None] * positions
            for p in range(positions):
                d_query = None
                d_own = d_context[p, rows, :].astype(F32)
                query = qkv_rows[p, rows, :model].astype(F32)
                for index, (own, q) in enumerate(pairs):
                    if own == p:
                        d_score = halves[2 * index, rows, :].astype(F32)
                        key = qkv_rows[q, rows, model : 2 * model].astype(F32)
                        d_query = plus(d_query, d_score * key)
                        d_keys[q] = plus(d_keys[q], d_score * query)
                        d_values[q] = plus(
                            d_values[q], halves[2 * index + 1, rows, :].astype(F32) * d_own
                        )
                d_qkv[p, rows, :model] = (d_query * scale).astype(BF16)
            for p in range(positions):
                d_qkv[p, rows, model : 2 * model] = (d_keys[p] * scale).astype(BF16)
                d_qkv[p, rows, 2 * model :] = d_values[p].astype(BF16)

        row_loop(act_height, 16, qkv_back)

    def swap_qkv():
        for p in range(positions):
            swap(3, p, d_qkv.at[p, pl.ds(0, act_height)])

    def out_weights(p):
        swap_wait(0, p)
        swap_wait(2, p)

        def tile(columns):
            out_grad[p, :, columns] = dot(
                context_turned[p].reshape(half, 2 * act_height), d_mid_low[p, :, columns]
            ).astype(BF16)

        tile_loop(model, 256, tile)

    def qkv_weights(p):
        swap_wait(1, p)
        swap_wait(3, p)

        def tile(columns):
            qkv_grad[p, :, columns] = dot(
                attn_turned[p].reshape(half, 2 * act_height), d_qkv[p, :, columns]
            ).astype(BF16)

        tile_loop(3 * model, 256, tile)

    def rows_back(p):
        for tile in range(tile_count):
            number = p * tile_count + tile
            qkv_load(number).wait()
            d_rows[p, :, tile * qkv_tile : (tile + 1) * qkv_tile] = dot_back(
                d_qkv[p, :act_height, :], qkv_tiles[number % 2]
            )
            if number + 2 < positions * tile_count:
                qkv_load(number + 2).start()

    def attn_back():
        def norm_one_back(rows):
            values = tokens_ref[rows].astype(F32)
            for p in range(positions):
                r, inverse = normed(values[:, p, :])
                d_attn_in = d_rows[p, rows, :]
                gain_acc[p] += r * d_attn_in
                grad_tokens[rows, p, :] = d_mid[p, rows, :] + norm_back(
                    r, inverse, d_attn_in * gain_rows[p : p + 1, :]
                )

        row_loop(act_height, 16, norm_one_back)
        gains_part[...] = jnp.zeros_like(gains_part)
        for index in range(2 * positions):
            sums = jnp.sum(gain_acc[index], axis=0, keepdims=True)
            for block in range(8):
                gains_part[block, index : index + 1, :] = sums[:, 128 * block : 128 * block + 128]
        lax.fori_loop(1, 32, gains_start, 0)

    def finish_output():
        def finish(rows):
            rounded = [resid_mid[p, rows, :] + act_total(1, p, rows) for p in range(positions)]
            output[rows] = jnp.stack(rounded, axis=1).astype(BF16)

        row_loop(act_height, 16, finish)

    for s in range(sets):
        for turn_number in (0, 1):
            for part in (0, 1, 2):
                part_copy(s, turn_number, part).start()
    for copy in out_loads:
        copy.start()
    act_load(0)
    qkv_load(0).start()
    qkv_load(1).start()
    make_spread(spread)
    gain_acc[...] = jnp.zeros_like(gain_acc)
    kinds = {
        B_TREE: lambda piece, dz, dy, dx: tree_step(piece, (dz, dy, dx)),
        B_RS_ACROSS: rs_across,
        B_RS_FIRST: rs_first,
        B_RS_SECOND: rs_second,
        B_RS_RANK: rs_rank,
        B_RS_LAST: rs_last,
        B_ACT_CORE: act_core,
        B_ACT_LOAD: act_load,
        B_ACT_ADD_X: act_add_x,
        B_ACT_ADD_Z: act_add_z,
        B_ACT_SUM: act_sum,
        B_NORM_TURN: norm_turn,
        B_SWAP_TURNED: swap_turned,
        B_PROBS: find_probs,
        B_MID: mid,
        B_SCORES_BACK: scores_back,
        B_SWAP_QKV: swap_qkv,
        B_OUT_W: out_weights,
        B_QKV_W: qkv_weights,
        B_ROWS_BACK: rows_back,
        B_ATTN_BACK: attn_back,
        B_FINISH_OUTPUT: finish_output,
    }
    for kind, *numbers in BACKWARD_STEPS:
        kinds[kind](*numbers)
    for s in range(sets):
        place_units(own_step, s, share(own_step, s))
    gains_sum[...] = gains_part[lax.div(me, 4)]
    others = gains_buf.at[pl.ds(0, 31)]
    arrived(others, gains_recv, sibling)
    push(others, others, gains_send, gains_recv, sibling).wait_send()
    lax.fori_loop(1, 32, gains_add, 0)
    own_gain = norm_attn_sum.shape[1]
    for index, target in enumerate((norm_attn_sum, norm_ff_sum)):
        picked = jnp.zeros(target.shape, F32)
        for place in range(128 // own_gain):
            picked = picked + jnp.where(
                lax.rem(me, 128 // own_gain) == place,
                gains_sum[
                    index * positions : (index + 1) * positions, place * own_gain : (place + 1) * own_gain
                ],
                0.0,
            )
        target[...] = picked
    def tree_sent(piece, direction, count):
        source, _, index, _, _ = pieces[piece]
        block = source.at[index, pl.ds(0, count * height), :]
        push(block, block, tree_send.at[piece, DIRECTIONS.index(direction)], gains_recv, sibling).wait_send()

    for piece in range(len(pieces)):
        order = pieces[piece][3]
        for direction in "xy":
            tree_sent(piece, direction, return_count(order, direction, 3))
        for direction in "ud":
            for level in range(4):
                if level != (3 if direction == "u" else 0):
                    pl.when(z == level)(
                        functools.partial(
                            tree_sent, piece, direction, return_count(order, direction, level)
                        )
                    )
    for s in range(sets):
        block = gate_up_sum.at[pl.ds(0, 7), s]
        push(block, block, rank_send.at[s], gains_recv, sibling).wait_send()
    for copy in sends:
        copy.wait_send()


def backward_scatter(
    tokens,
    grads,
    gain_rows,
    qkv_rows,
    context,
    resid_mid,
    qkv_full,
    out_full,
    out_part,
    back_part,
    gate_up_grad,
    down_grad,
):
    act_height, sets, model = tokens.shape
    width = gate_up_grad.shape[2]
    height = model // 32
    down_height = down_grad.shape[1] // 4
    dma = pltpu.SemaphoreType.DMA
    vmem = pl.BlockSpec(memory_space=pltpu.VMEM)
    anywhere = pl.BlockSpec(memory_space=pl.ANY)
    places = [slot_base(order)[1] for order in ORDERS]
    pair_count = len(pairs_of(sets))
    act = (sets, act_height, model)
    return pl.pallas_call(
        backward_kernel,
        out_shape=(
            jax.ShapeDtypeStruct(tokens.shape, BF16),
            jax.ShapeDtypeStruct(tokens.shape, F32),
            jax.ShapeDtypeStruct((sets, height), F32),
            jax.ShapeDtypeStruct((sets, height), F32),
            jax.ShapeDtypeStruct((sets, height, 3 * model), F32),
            jax.ShapeDtypeStruct((sets, height, model), F32),
            jax.ShapeDtypeStruct((sets, height, 8 * width), F32),
            jax.ShapeDtypeStruct((sets, down_height, model), F32),
        ),
        in_specs=[vmem] * 6 + [anywhere] * 6,
        out_specs=(vmem,) * 8,
        scratch_shapes=[
            pltpu.VMEM((sets, 2, 2, act_height, model), BF16),
            pltpu.VMEM((2, sets, 2, 2, act_height, model), BF16),
            pltpu.VMEM((2, sets, 2, act_height, model), BF16),
            pltpu.VMEM((2, sets, act_height, model), BF16),
            pltpu.VMEM((2, sets, 2, 4 * height, width), BF16),
            pltpu.VMEM((2, sets, down_height, model), BF16),
            pltpu.VMEM((2, sets, 2, 4 * height, width), BF16),
            pltpu.VMEM((2, sets, down_height, model), BF16),
            pltpu.VMEM((sets, 2, 4 * height, width), BF16),
            pltpu.VMEM((sets, down_height, model), BF16),
            pltpu.VMEM((sets, 16 * height, 3 * model), BF16),
            pltpu.VMEM((sets, 16 * height, model), BF16),
            pltpu.VMEM((places[0], height, 3 * model), BF16),
            pltpu.VMEM((places[1], height, 3 * model), BF16),
            pltpu.VMEM((places[2], height, model), BF16),
            pltpu.VMEM((places[3], height, model), BF16),
            pltpu.VMEM((2, 128, 3 * model), BF16),
            pltpu.VMEM((sets, model, model), BF16),
            pltpu.VMEM((2, sets, 16, 2, height, act_height), BF16),
            pltpu.VMEM((sets, 16, height, 2 * act_height), BF16),
            pltpu.VMEM((sets, 16, height, 2 * act_height), BF16),
            pltpu.VMEM((sets, 2 * act_height, 3 * model), BF16),
            pltpu.VMEM((sets, 2 * act_height, model), BF16),
            pltpu.VMEM(act, F32),
            pltpu.VMEM(act, BF16),
            pltpu.VMEM(act, F32),
            pltpu.VMEM((2 * pair_count, act_height, model), BF16),
            pltpu.VMEM((pair_count, act_height, 128), F32),
            pltpu.VMEM((model, 128), BF16),
            pltpu.VMEM((2 * sets, 16, model), F32),
            pltpu.VMEM((8, 8, 128), F32),
            pltpu.VMEM((32, 8, 128), F32),
            pltpu.VMEM((8, 128), F32),
            pltpu.VMEM((8, sets, height, width), BF16),
            dma((2, sets, 2, 2)),
            dma((2, sets, 2, 2)),
            dma((2, sets, 2)),
            dma((2, sets, 2)),
            dma((2, sets)),
            dma((2, sets)),
            dma((2, sets, 3)),
            dma((2, sets, 3)),
            dma((sets, 3)),
            dma((sets, 3)),
            dma((sets,)),
            dma((8, sets)),
            dma((4 * sets,)),
            dma((4 * sets,)),
            dma((4, 4)),
            dma((4, max(places))),
            dma,
            dma,
            dma((2, sets, 2, 2)),
            dma((2, sets, 3)),
            dma((2 + sets,)),
        ],
        compiler_params=pltpu.CompilerParams(
            collective_id=5, has_side_effects=True, vmem_limit_bytes=63 * 2**20
        ),
        name="backward_scatter",
    )(
        tokens,
        grads,
        gain_rows,
        qkv_rows,
        context,
        resid_mid,
        qkv_full,
        out_full,
        out_part,
        back_part,
        gate_up_grad,
        down_grad,
    )


def settle_kernel(*refs):
    count = (len(refs) - 1) // 3
    sems = refs[-1]
    stages = [
        (
            pltpu.make_async_copy(refs[index], refs[2 * count + index], sems.at[0, index]),
            pltpu.make_async_copy(refs[2 * count + index], refs[count + index], sems.at[1, index]),
        )
        for index in range(count)
    ]
    for read, _ in stages:
        read.start()
    for read, write in stages:
        read.wait()
        write.start()
    for _, write in stages:
        write.wait()


def settle(arrays):
    anywhere = pl.BlockSpec(memory_space=pl.ANY)
    return pl.pallas_call(
        settle_kernel,
        out_shape=tuple(jax.ShapeDtypeStruct(array.shape, array.dtype) for array in arrays),
        in_specs=[anywhere] * len(arrays),
        out_specs=(anywhere,) * len(arrays),
        scratch_shapes=[pltpu.VMEM(array.shape, array.dtype) for array in arrays]
        + [pltpu.SemaphoreType.DMA((2, len(arrays)))],
        name="settle",
    )(*arrays)


def local_fast(
    tokens,
    norm_attn,
    w_qkv,
    w_out,
    norm_ff,
    w_gate_up,
    w_down,
    cotangent,
    valid_frames,
    item_lengths,
):
    (
        gain_rows,
        cot_rows,
        qkv_rows,
        context,
        resid_mid,
        qkv_full,
        out_full,
        out_part,
        back_part,
        gate_up_grad,
        down_grad,
    ) = forward_gather(
        valid_frames,
        item_lengths,
        norm_attn,
        norm_ff,
        tokens,
        cotangent,
        w_qkv,
        w_out,
        w_gate_up,
        w_down,
    )
    (
        output,
        grad_tokens,
        share_norm_attn,
        share_norm_ff,
        share_qkv,
        share_out,
        share_gate_up,
        share_down,
    ) = settle(backward_scatter(
        tokens,
        cot_rows,
        gain_rows,
        qkv_rows,
        context,
        resid_mid,
        qkv_full,
        out_full,
        out_part,
        back_part,
        gate_up_grad,
        down_grad,
    ))
    return (
        output,
        grad_tokens,
        share_norm_attn,
        share_qkv,
        share_out,
        share_norm_ff,
        share_gate_up,
        share_down,
    )


def solution(mesh):
    in_specs = (
        P(("dp", "pair"), None, None),
        P(None, ("dp", "pair")),
        P(None, ("dp", "pair"), None),
        P(None, ("dp", "pair"), None),
        P(None, ("dp", "pair")),
        P(None, ("dp", "pair"), None),
        P(None, ("dp", "pair"), None),
        P(("dp", "pair"), None, None),
        P(("dp", "pair")),
        P(),
    )
    out_specs = (
        P(("dp", "pair"), None, None),
        P(("dp", "pair"), None, None),
        P(None, ("dp", "pair")),
        P(None, ("dp", "pair"), None),
        P(None, ("dp", "pair"), None),
        P(None, ("dp", "pair")),
        P(None, ("dp", "pair"), None),
        P(None, ("dp", "pair"), None),
    )
    body = local_fast if mesh.shape["dp"] == 16 and mesh.shape["pair"] == 2 else local
    return jax.shard_map(body, mesh=mesh, in_specs=in_specs, out_specs=out_specs, check_vma=False)
```

```python
import functools
import math

import jax
import jax.numpy as jnp
from jax import lax
from jax.experimental import pallas as pl
from jax.experimental.pallas import tpu as pltpu
from jax.sharding import PartitionSpec as P

HEAD_DIM = 64


def per_pos(activations, weight):
    return jnp.einsum("fgk,gke->fge", activations, weight, preferred_element_type=jnp.float32)


def per_pos_back(gradients, weight):
    return jnp.einsum("fge,gke->fgk", gradients, weight, preferred_element_type=jnp.float32)


def pos_grad(activations, gradients):
    return jnp.einsum("fgk,fge->kge", activations, gradients, preferred_element_type=jnp.float32)


def gain_grad(normed_rows, gradients):
    return jnp.transpose(jnp.sum(normed_rows * gradients, axis=0))


def back_layout(share):
    return jnp.swapaxes(share, 0, 1)


def normed(values):
    inverse = lax.rsqrt(jnp.mean(values * values, axis=-1, keepdims=True) + 1e-05)
    return (values * inverse, inverse)


def norm_back(normed_rows, inverse, gradients):
    return inverse * (
        gradients - normed_rows * jnp.mean(gradients * normed_rows, axis=-1, keepdims=True)
    )


def gather_ff_fwd(norm_ff, w_gate_up, w_down, start, group):
    return (
        lax.all_gather(norm_ff[start : start + group], ("dp", "pair"), axis=1, tiled=True),
        lax.all_gather(w_gate_up[start : start + group], ("dp", "pair"), axis=1, tiled=True),
        lax.all_gather(w_down[start : start + group], ("dp", "pair"), axis=1, tiled=True),
    )


def gather_ff_back(norm_ff, w_gate_up, w_down, start, group):
    return (
        lax.all_gather(norm_ff[start : start + group], ("dp", "pair"), axis=1, tiled=True),
        lax.all_gather(w_gate_up[start : start + group], ("dp", "pair"), axis=1, tiled=True),
        lax.all_gather(w_down[start : start + group], ("dp", "pair"), axis=1, tiled=True),
    )


def local(
    tokens,
    norm_attn,
    w_qkv,
    w_out,
    norm_ff,
    w_gate_up,
    w_down,
    cotangent,
    valid_frames,
    item_lengths,
):
    frame_count, positions, model_width = tokens.shape
    head_count = model_width // HEAD_DIM
    ff_units = w_gate_up.shape[2] // 2
    score_scale = 1.0 / math.sqrt(HEAD_DIM)
    causal = jnp.arange(positions)[:, None] >= jnp.arange(positions)[None, :]
    head_shape = (frame_count, positions, head_count, HEAD_DIM)
    group = 1
    gains_attn, qkv_full, out_full = (
        lax.all_gather(norm_attn, ("dp", "pair"), axis=1, tiled=True),
        lax.all_gather(w_qkv, ("dp", "pair"), axis=1, tiled=True),
        lax.all_gather(w_out, ("dp", "pair"), axis=1, tiled=True),
    )
    resid_in = tokens.astype(jnp.float32)
    normed_one, inverse_one = normed(resid_in)
    attn_in = (normed_one * gains_attn.astype(jnp.float32)[None]).astype(jnp.bfloat16)
    qkv_rows = per_pos(attn_in, qkv_full).astype(jnp.bfloat16)
    queries = qkv_rows[..., :model_width].reshape(head_shape)
    key_heads = qkv_rows[..., model_width : 2 * model_width].reshape(head_shape)
    value_heads = qkv_rows[..., 2 * model_width :].reshape(head_shape)
    scores = (
        jnp.einsum("fphd,fqhd->fhpq", queries, key_heads, preferred_element_type=jnp.float32)
        * score_scale
    )
    scores = jnp.where(causal, scores, -1e30)
    row_max = jnp.max(scores, axis=-1, keepdims=True)
    attn_probs = jnp.exp(scores - row_max)
    attn_probs = attn_probs / jnp.sum(attn_probs, axis=-1, keepdims=True)
    probs_low = attn_probs.astype(jnp.bfloat16)
    context = jnp.einsum(
        "fhpq,fqhd->fphd", probs_low, value_heads, preferred_element_type=jnp.float32
    )
    context = context.astype(jnp.bfloat16).reshape(frame_count, positions, model_width)
    resid_mid = resid_in + per_pos(context, out_full)
    kept_parts = []
    out_parts = []
    for start in range(0, positions, group):
        gains_ff, gate_up_full, down_full = gather_ff_fwd(norm_ff, w_gate_up, w_down, start, group)
        mid_part = resid_mid[:, start : start + group]
        normed_two, inverse_two = normed(mid_part)
        ff_in = (normed_two * gains_ff.astype(jnp.float32)[None]).astype(jnp.bfloat16)
        gate_up = per_pos(ff_in, gate_up_full)
        gate_part = gate_up[..., :ff_units]
        up_part = gate_up[..., ff_units:]
        sigmoid_gate = jax.nn.sigmoid(gate_part)
        silu_gate = gate_part * sigmoid_gate
        hidden = (silu_gate * up_part).astype(jnp.bfloat16)
        out_parts.append(mid_part + per_pos(hidden, down_full))
        kept_parts.append(
            (normed_two, inverse_two, ff_in, gate_part, up_part, sigmoid_gate, silu_gate, hidden)
        )
    output = jnp.concatenate(out_parts, axis=1).astype(jnp.bfloat16)
    device_index = lax.axis_index(("dp", "pair"))
    local_ids = jnp.arange(frame_count, dtype=jnp.int32)
    frame_ids = device_index * frame_count + local_ids
    item_ends = jnp.cumsum(item_lengths)
    item_starts = item_ends - item_lengths
    in_item = (frame_ids[:, None] >= item_starts[None, :]) & (
        frame_ids[:, None] < item_ends[None, :]
    )
    item_share = 8 * frame_count / item_lengths.astype(jnp.float32)
    frame_weight = jnp.sum(jnp.where(in_item, item_share[None, :], 0.0), axis=1)
    frame_weight = jnp.where(local_ids < valid_frames[0], frame_weight, 0.0)
    grad_out = cotangent.astype(jnp.float32) * frame_weight[:, None, None]
    mid_grads = []
    share_norm_ff_parts = []
    share_gate_up_parts = []
    share_down_parts = []
    for index, start in enumerate(range(0, positions, group)):
        normed_two, inverse_two, ff_in, gate_part, up_part, sigmoid_gate, silu_gate, hidden = (
            kept_parts[index]
        )
        gains_ff, gate_up_full, down_full = gather_ff_back(norm_ff, w_gate_up, w_down, start, group)
        grad_part = grad_out[:, start : start + group]
        grad_low = grad_part.astype(jnp.bfloat16)
        grad_down = pos_grad(hidden, grad_low)
        d_hidden = per_pos_back(grad_low, down_full)
        d_gate = d_hidden * up_part * sigmoid_gate * (1.0 + gate_part * (1.0 - sigmoid_gate))
        d_up = d_hidden * silu_gate
        d_gate_up = jnp.concatenate([d_gate, d_up], axis=-1).astype(jnp.bfloat16)
        grad_gate_up = pos_grad(ff_in, d_gate_up)
        d_ff_in = per_pos_back(d_gate_up, gate_up_full)
        grad_norm_ff = gain_grad(normed_two, d_ff_in)
        mid_grads.append(
            grad_part
            + norm_back(normed_two, inverse_two, d_ff_in * gains_ff.astype(jnp.float32)[None])
        )
        share_a, share_b, share_c = (
            lax.psum_scatter(grad_norm_ff, ("dp", "pair"), scatter_dimension=0, tiled=True),
            lax.psum_scatter(grad_gate_up, ("dp", "pair"), scatter_dimension=0, tiled=True),
            lax.psum_scatter(grad_down, ("dp", "pair"), scatter_dimension=0, tiled=True),
        )
        share_norm_ff_parts.append(jnp.transpose(share_a))
        share_gate_up_parts.append(back_layout(share_b))
        share_down_parts.append(back_layout(share_c))
    d_mid = jnp.concatenate(mid_grads, axis=1)
    gains_attn, qkv_full, out_full = (
        lax.all_gather(norm_attn, ("dp", "pair"), axis=1, tiled=True),
        lax.all_gather(w_qkv, ("dp", "pair"), axis=1, tiled=True),
        lax.all_gather(w_out, ("dp", "pair"), axis=1, tiled=True),
    )
    d_mid_low = d_mid.astype(jnp.bfloat16)
    grad_out_proj = pos_grad(context, d_mid_low)
    d_context = per_pos_back(d_mid_low, out_full).astype(jnp.bfloat16).reshape(head_shape)
    d_probs = jnp.einsum(
        "fphd,fqhd->fhpq", d_context, value_heads, preferred_element_type=jnp.float32
    )
    d_values = jnp.einsum(
        "fhpq,fphd->fqhd", probs_low, d_context, preferred_element_type=jnp.float32
    )
    d_scores = attn_probs * (d_probs - jnp.sum(attn_probs * d_probs, axis=-1, keepdims=True))
    d_scores = d_scores.astype(jnp.bfloat16)
    d_queries = (
        jnp.einsum("fhpq,fqhd->fphd", d_scores, key_heads, preferred_element_type=jnp.float32)
        * score_scale
    )
    d_keys = (
        jnp.einsum("fhpq,fphd->fqhd", d_scores, queries, preferred_element_type=jnp.float32)
        * score_scale
    )
    row_shape = (frame_count, positions, model_width)
    d_qkv = jnp.concatenate(
        [d_queries.reshape(row_shape), d_keys.reshape(row_shape), d_values.reshape(row_shape)],
        axis=-1,
    ).astype(jnp.bfloat16)
    grad_qkv = pos_grad(attn_in, d_qkv)
    d_attn_in = per_pos_back(d_qkv, qkv_full)
    grad_norm_attn = gain_grad(normed_one, d_attn_in)
    grad_tokens = d_mid + norm_back(
        normed_one, inverse_one, d_attn_in * gains_attn.astype(jnp.float32)[None]
    )
    share_norm_attn, share_qkv, share_out = (
        lax.psum_scatter(grad_norm_attn, ("dp", "pair"), scatter_dimension=0, tiled=True),
        lax.psum_scatter(grad_qkv, ("dp", "pair"), scatter_dimension=0, tiled=True),
        lax.psum_scatter(grad_out_proj, ("dp", "pair"), scatter_dimension=0, tiled=True),
    )
    share_norm_attn = jnp.transpose(share_norm_attn)
    share_qkv = back_layout(share_qkv)
    share_out = back_layout(share_out)
    share_norm_ff = jnp.concatenate(share_norm_ff_parts, axis=0)
    share_gate_up = jnp.concatenate(share_gate_up_parts, axis=0)
    share_down = jnp.concatenate(share_down_parts, axis=0)
    return (
        output,
        grad_tokens,
        share_norm_attn,
        share_qkv,
        share_out,
        share_norm_ff,
        share_gate_up,
        share_down,
    )


MESH_ID = pl.DeviceIdType.MESH
BF16 = jnp.bfloat16
F32 = jnp.float32


def here():
    dp = lax.axis_index("dp")
    core = lax.axis_index("pair")
    return lax.div(dp, 4), lax.rem(lax.div(dp, 2), 2), lax.rem(dp, 2), core


def flip(value, bit):
    return 1 - value if bit else value


def push(src, dst, send_sem, recv_sem, to):
    return pltpu.make_async_remote_copy(
        src_ref=src,
        dst_ref=dst,
        send_sem=send_sem,
        recv_sem=recv_sem,
        device_id=to,
        device_id_type=MESH_ID,
    )


def arrived(dst, recv_sem, to):
    push(dst, dst, recv_sem, recv_sem, to).wait_recv()


def greet_all(z, y, x, core):
    barrier = pltpu.get_barrier_semaphore()
    me = 2 * (z * 4 + y * 2 + x) + core

    def one(step, carry):
        other = lax.rem(me + step, 32)
        pl.semaphore_signal(
            barrier, inc=1, device_id=(lax.div(other, 2), lax.rem(other, 2)), device_id_type=MESH_ID
        )
        return carry

    lax.fori_loop(1, 32, one, 0)
    pl.semaphore_wait(barrier, 31)


def greet(peers):
    barrier = pltpu.get_barrier_semaphore()
    for to in peers:
        pl.semaphore_signal(barrier, inc=1, device_id=to, device_id_type=MESH_ID)
    pl.semaphore_wait(barrier, len(peers))


def maybe(condition, do):
    if condition is None:
        do()
    else:
        pl.when(condition)(do)


OFFSETS = [
    (dz, dy, dx) for dz in (0, -1, 1, -2, 2, -3, 3) for dy in (0, 1) for dx in (0, 1)
]
ORDERS = ("zxy", "zyx", "zyx", "yxz")


def hops(offset):
    return abs(offset[0]) + offset[1] + offset[2]


def arrival_axis(order, offset):
    part = dict(z=offset[0], y=offset[1], x=offset[2])
    last = None
    for axis in order:
        if part[axis] != 0:
            last = axis
    return last


def onward(order, offset):
    directions = []
    last = arrival_axis(order, offset)
    start = 0
    if last is not None:
        start = order.index(last) + 1
        if last == "z":
            directions.append("u" if offset[0] < 0 else "d")
    for axis in order[start:]:
        directions.extend(["u", "d"] if axis == "z" else [axis])
    return directions


def came_from(order, offset):
    last = arrival_axis(order, offset)
    if last == "z":
        return "d" if offset[0] < 0 else "u"
    return last


def offset_exists(offset, z):
    if offset[0] < 0:
        return z >= -offset[0]
    if offset[0] > 0:
        return z <= 3 - offset[0]
    return None


def direction_exists(direction, z):
    return {"u": z < 3, "d": z > 0}.get(direction)


def return_count(order, direction, level):
    return sum(
        hops(offset) > 0 and came_from(order, offset) == direction
        for offset in OFFSETS
        if 0 <= level + offset[0] <= 3
    )


def tree_count(order, direction, level):
    return sum(
        direction in onward(order, offset) for offset in OFFSETS if 0 <= level + offset[0] <= 3
    )


DIRECTIONS = ("x", "y", "u", "d", "s")


def neighbour(direction, z, y, x, core):
    if direction == "x":
        return (z * 4 + y * 2 + 1 - x, core)
    if direction == "y":
        return (z * 4 + (1 - y) * 2 + x, core)
    if direction == "u":
        return (z * 4 + 4 + y * 2 + x, core)
    if direction == "d":
        return (z * 4 - 4 + y * 2 + x, core)
    return (z * 4 + y * 2 + x, 1 - core)


def chip_of(offset, z, y, x):
    return (z + offset[0]) * 4 + flip(y, offset[1]) * 2 + flip(x, offset[2])


RANK_STEPS = sorted(
    ((dl, dx, dc) for dl in (0, 1) for dx in (0, 1) for dc in (0, 1)), key=lambda step: (sum(step), step)
)


def group_place(z, y, x, core):
    zh, zl = lax.div(z, 2), lax.rem(z, 2)

    def member(step):
        return ((2 * zh + flip(zl, step[0])) * 4 + y * 2 + flip(x, step[1]), flip(core, step[2]))

    def rank(step):
        return 4 * flip(zl, step[0]) + 2 * flip(x, step[1]) + flip(core, step[2])

    def device(step, dzh=0, dy=0):
        return 16 * flip(zh, dzh) + 4 * flip(y, dy) + 8 * flip(zl, step[0]) + 2 * flip(x, step[1]) + flip(core, step[2])

    far = ((2 * (1 - zh) + zl) * 4 + y * 2 + x, core)
    across = (z * 4 + (1 - y) * 2 + x, core)
    return zh, zl, member, rank, device, far, across


def add_into(target, sources, rows=16, columns=1024):
    height, width = target.shape
    across = width // columns

    def one(step, carry):
        top = pl.multiple_of(lax.div(step, across) * rows, rows)
        left = pl.multiple_of(lax.rem(step, across) * columns, columns)
        spot = (pl.ds(top, rows), pl.ds(left, columns))
        total = sources[0][spot].astype(F32)
        for source in sources[1:]:
            total = total + source[spot].astype(F32)
        target[spot] = total.astype(target.dtype)
        return carry

    lax.fori_loop(0, (height // rows) * across, one, 0)


def row_loop(height, chunk, body):
    def one(step, carry):
        body(pl.ds(pl.multiple_of(step * chunk, chunk), chunk))
        return carry

    lax.fori_loop(0, height // chunk, one, 0)


def tile_loop(width, tile, body):
    def one(step, carry):
        body(pl.ds(pl.multiple_of(step * tile, tile), tile))
        return carry

    lax.fori_loop(0, width // tile, one, 0)


def dot(left, right):
    return jnp.dot(left, right, preferred_element_type=F32)


def dot_back(left, right):
    return lax.dot_general(left, right, (((1,), (1,)), ((), ())), preferred_element_type=F32)


def dot_grad(left, right):
    return lax.dot_general(left, right, (((0,), (0,)), ((), ())), preferred_element_type=F32)


def make_spread(spread):
    height, width = spread.shape
    head = lax.broadcasted_iota(jnp.int32, (height, width), 0) // HEAD_DIM
    spread[...] = jnp.where(
        head == lax.broadcasted_iota(jnp.int32, (height, width), 1), 1.0, 0.0
    ).astype(BF16)


def pairs_of(positions):
    return [(p, q) for p in range(positions) for q in range(p + 1)]


def split_product(product):
    high = product.astype(BF16)
    return high, (product - high.astype(F32)).astype(BF16)


def sums_over_heads(halves, spread, index):
    return dot(halves[2 * index], spread[...]) + dot(halves[2 * index + 1], spread[...])


def to_heads(values, spread):
    return dot_back(values, spread[...]).astype(BF16)


def attention_probs(qkv, halves, spread, model, position):
    height = qkv.shape[1]
    scale = 1.0 / math.sqrt(HEAD_DIM)

    def products(rows):
        for q in range(position + 1):
            product = qkv[position, rows, :model].astype(F32) * qkv[
                q, rows, model : 2 * model
            ].astype(F32)
            halves[2 * q, rows, :], halves[2 * q + 1, rows, :] = split_product(product)

    row_loop(height, 16, products)
    scores = [sums_over_heads(halves, spread, q) * scale for q in range(position + 1)]
    top = functools.reduce(jnp.maximum, scores)
    powers = [jnp.exp(score - top) for score in scores]
    total = functools.reduce(jnp.add, powers)
    return [power / total for power in powers]


(
    F_TREE,
    F_TREE_END,
    F_GAINS,
    F_PARTS,
    F_COT,
    F_ATTENTION,
    F_GRADS,
    F_ACT_Z,
    F_ACT_X,
    F_ACT_C,
    F_TO_RANK,
    F_OWN_FAR,
    F_OWN_ACROSS,
    F_RANK_FAR,
    F_RANK_ACROSS,
    F_FAR_ACROSS,
    F_FF_END,
    F_BLOCK,
    F_GATE_GRAD,
    F_DOWN_GRAD,
) = range(20)
FORWARD_STEPS = [
    (F_TREE, 5, 0, 0, 0), (F_TREE, 4, 0, 0, 0), (F_TREE, 0, 0, 0, 0), (F_PARTS,), (F_TREE, 2, 0, 0, 0),
    (F_TREE, 1, 0, 0, 0), (F_TREE, 0, 1, 0, 0), (F_TREE, 5, 0, 0, 1), (F_TO_RANK, 0, 2), (F_TREE, 0, -1, 0, 0),
    (F_TO_RANK, 0, 7), (F_TREE, 0, 0, 0, 1), (F_TO_RANK, 0, 1), (F_TO_RANK, 0, 6), (F_TREE, 2, -1, 0, 0),
    (F_TREE, 2, 1, 0, 0), (F_TREE, 0, -1, 0, 1), (F_TO_RANK, 0, 3), (F_OWN_ACROSS, 0, 8), (F_TREE, 0, -2, 0, 0),
    (F_TREE, 4, -1, 0, 0), (F_TREE, 1, 1, 0, 0), (F_TREE, 2, 2, 0, 0), (F_TREE, 3, 0, 0, 0),
    (F_TREE, 1, 0, 1, 0), (F_TREE, 4, 0, 1, 0), (F_RANK_FAR, 0, 3), (F_RANK_FAR, 0, 1), (F_TREE, 1, -1, 0, 0),
    (F_TO_RANK, 1, 5), (F_OWN_ACROSS, 1, 8), (F_TREE, 1, 2, 0, 0), (F_TREE, 2, -2, 0, 0), (F_COT,),
    (F_TREE, 3, 1, 0, 0), (F_OWN_FAR, 0, 0), (F_TREE, 0, 2, 0, 0), (F_TREE, 0, -1, 1, 1), (F_TREE, 3, -1, 0, 0),
    (F_RANK_FAR, 0, 7), (F_GRADS, 0), (F_TREE, 1, -2, 0, 0), (F_TREE, 2, 2, 1, 0), (F_RANK_FAR, 0, 6),
    (F_TREE, 0, -2, 0, 1), (F_TO_RANK, 0, 4), (F_TO_RANK, 0, 5), (F_TREE, 1, 1, 1, 0), (F_TREE, 0, -3, 0, 0),
    (F_TREE, 2, 3, 0, 0), (F_OWN_FAR, 0, 8), (F_TREE, 5, 0, 1, 0), (F_TREE, 1, -2, 1, 0), (F_TREE, 2, -3, 0, 0),
    (F_TREE, 0, -2, 1, 0), (F_RANK_ACROSS, 0, 3), (F_TREE, 0, -3, 0, 1), (F_TREE, 2, -2, 1, 0),
    (F_TREE, 0, 2, 0, 1), (F_TREE, 0, 1, 1, 0), (F_TREE, 5, 1, 0, 1), (F_GAINS,), (F_RANK_ACROSS, 0, 6),
    (F_RANK_FAR, 0, 2), (F_TREE, 2, 0, 1, 0), (F_TREE, 0, 1, 0, 1), (F_TREE, 3, -2, 0, 0),
    (F_TREE, 1, -3, 0, 0), (F_TREE, 2, 1, 1, 0), (F_TREE, 1, 0, 1, 1), (F_TREE, 1, 3, 0, 0),
    (F_TREE, 3, 0, 0, 1), (F_TREE, 2, 1, 0, 1), (F_TREE, 3, 1, 1, 0), (F_TREE, 0, 3, 0, 0),
    (F_TREE, 3, 2, 0, 0), (F_RANK_FAR, 0, 4), (F_RANK_FAR, 0, 5), (F_FAR_ACROSS, 0, 0), (F_TREE, 2, 3, 0, 1),
    (F_FAR_ACROSS, 0, 8), (F_TO_RANK, 1, 4), (F_TREE, 5, 1, 0, 0), (F_TREE, 0, 2, 1, 1), (F_TREE, 1, 3, 1, 0),
    (F_TREE, 2, -3, 0, 1), (F_TREE, 1, 2, 1, 0), (F_TREE, 4, -2, 0, 0), (F_TREE, 5, 2, 0, 1),
    (F_FAR_ACROSS, 0, 2), (F_TREE, 1, -1, 1, 0), (F_RANK_ACROSS, 0, 4), (F_TREE, 1, -3, 1, 0),
    (F_TREE, 4, 1, 0, 0), (F_TREE, 1, 3, 1, 1), (F_TREE, 2, 0, 0, 1), (F_TO_RANK, 1, 6), (F_TREE, 0, 1, 1, 1),
    (F_TREE, 3, -1, 1, 0), (F_TO_RANK, 1, 2), (F_TREE, 2, 3, 1, 0), (F_TREE, 0, -2, 1, 1),
    (F_TREE, 2, -1, 1, 0), (F_TREE, 3, 0, 1, 1), (F_TREE, 4, -1, 1, 0), (F_TREE, 1, 2, 0, 1),
    (F_TREE, 1, -3, 0, 1), (F_OWN_FAR, 1, 8), (F_TREE, 5, 0, 1, 1), (F_ACT_C, 1, 0, 0, 0), (F_TREE, 0, 3, 0, 1),
    (F_TREE, 4, -3, 0, 0), (F_ACT_Z, 1, 0), (F_TREE, 5, 1, 1, 0), (F_TREE, 1, 2, 1, 1), (F_TREE, 5, 3, 0, 1),
    (F_TREE, 3, 3, 0, 0), (F_TREE, 0, -1, 1, 0), (F_TREE, 2, -3, 1, 0), (F_TREE, 2, -2, 1, 1),
    (F_TREE, 4, 0, 0, 1), (F_TREE, 1, 0, 0, 1), (F_TREE, 3, -1, 0, 1), (F_TO_RANK, 1, 1), (F_TREE, 4, 2, 0, 0),
    (F_TREE, 5, -1, 0, 1), (F_GRADS, 1), (F_TREE, 0, -3, 1, 1), (F_TREE, 0, 2, 1, 0), (F_RANK_ACROSS, 0, 1),
    (F_TREE, 4, 0, 1, 1), (F_TREE, 1, -1, 0, 1), (F_TREE, 5, 2, 0, 0), (F_TREE, 3, 2, 0, 1),
    (F_FAR_ACROSS, 0, 6), (F_TREE, 2, -2, 0, 1), (F_ACT_C, 1, 1, 0, 0), (F_TREE, 4, -3, 1, 0),
    (F_TREE, 1, 3, 0, 1), (F_TREE, 0, 0, 1, 0), (F_TREE, 3, -2, 1, 0), (F_RANK_ACROSS, 0, 5),
    (F_TREE, 0, 3, 1, 1), (F_TREE, 5, -1, 1, 0), (F_RANK_FAR, 1, 2), (F_FAR_ACROSS, 0, 1), (F_TREE, 3, 3, 1, 0),
    (F_FAR_ACROSS, 0, 3), (F_TREE, 2, 1, 1, 1), (F_TREE, 1, -2, 1, 1), (F_FAR_ACROSS, 0, 7),
    (F_ACT_C, 1, 0, 1, 0), (F_RANK_ACROSS, 1, 2), (F_TREE, 5, -1, 0, 0), (F_TREE, 1, 1, 1, 1),
    (F_TREE, 0, 0, 1, 1), (F_FAR_ACROSS, 0, 5), (F_TREE, 4, -3, 0, 1), (F_TO_RANK, 1, 3), (F_TREE, 2, 3, 1, 1),
    (F_TREE, 1, -1, 1, 1), (F_TREE, 3, -3, 0, 0), (F_TREE, 4, 1, 1, 0), (F_TREE, 1, 1, 0, 1),
    (F_TREE, 0, -3, 1, 0), (F_TREE, 4, -2, 1, 0), (F_TREE, 1, -3, 1, 1), (F_TREE, 0, 3, 1, 0),
    (F_TREE, 2, 0, 1, 1), (F_TREE, 2, -1, 0, 1), (F_TREE, 1, -2, 0, 1), (F_TREE, 2, 2, 0, 1),
    (F_TREE, 2, -3, 1, 1), (F_TREE, 4, 2, 1, 0), (F_TREE, 4, 3, 0, 0), (F_FAR_ACROSS, 1, 8),
    (F_TREE, 2, -1, 1, 1), (F_TO_RANK, 1, 7), (F_TREE, 2, 2, 1, 1), (F_TREE, 4, 3, 1, 0), (F_RANK_FAR, 1, 4),
    (F_RANK_ACROSS, 0, 7), (F_TREE, 5, -1, 1, 1), (F_RANK_ACROSS, 0, 2), (F_OWN_ACROSS, 1, 0),
    (F_TREE, 4, -1, 0, 1), (F_TREE, 3, -1, 1, 1), (F_FAR_ACROSS, 0, 4), (F_TREE_END, 0), (F_TREE, 3, 1, 0, 1),
    (F_TREE, 3, 0, 1, 0), (F_TREE, 3, -2, 0, 1), (F_ACT_X, 1, 0, 0), (F_ATTENTION, 0), (F_TREE, 5, 1, 1, 1),
    (F_TREE, 4, -2, 1, 1), (F_TREE, 3, -3, 0, 1), (F_ACT_X, 1, 0, 1), (F_RANK_FAR, 1, 3), (F_TREE, 3, 3, 0, 1),
    (F_TREE, 5, -2, 0, 0), (F_TREE, 4, 2, 1, 1), (F_TREE, 5, -2, 1, 1), (F_ACT_C, 1, 0, 0, 1),
    (F_TREE, 5, -3, 0, 0), (F_TREE, 4, -3, 1, 1), (F_ACT_Z, 0, 0), (F_TREE, 4, 2, 0, 1), (F_TREE, 3, -3, 1, 0),
    (F_TREE, 4, 1, 1, 1), (F_OWN_ACROSS, 0, 0), (F_ACT_X, 1, 1, 0), (F_TREE, 5, -2, 1, 0),
    (F_ACT_C, 1, 0, 1, 1), (F_TREE, 5, 2, 1, 0), (F_TREE, 5, -2, 0, 1), (F_FAR_ACROSS, 1, 3), (F_ACT_Z, 1, 1),
    (F_TREE, 5, 2, 1, 1), (F_FAR_ACROSS, 1, 2), (F_TREE, 5, -3, 1, 1), (F_RANK_FAR, 1, 1), (F_RANK_FAR, 1, 7),
    (F_TREE, 3, 2, 1, 1), (F_RANK_ACROSS, 1, 3), (F_TREE, 5, 3, 1, 0), (F_TREE, 4, 1, 0, 1), (F_ACT_X, 0, 0, 0),
    (F_TREE, 4, -1, 1, 1), (F_TREE, 4, -2, 0, 1), (F_RANK_FAR, 1, 6), (F_RANK_FAR, 1, 5), (F_TREE, 5, -3, 0, 1),
    (F_ACT_C, 0, 0, 0, 0), (F_TREE, 3, 2, 1, 0), (F_TREE, 4, 3, 0, 1), (F_ACT_C, 1, 1, 1, 0),
    (F_TREE, 3, -3, 1, 1), (F_TREE, 5, -3, 1, 0), (F_TREE, 3, 3, 1, 1), (F_ACT_C, 0, 0, 0, 1),
    (F_TREE, 3, 1, 1, 1), (F_RANK_ACROSS, 1, 6), (F_TREE, 4, 3, 1, 1), (F_TREE, 5, 3, 1, 1),
    (F_TREE, 3, -2, 1, 1), (F_FAR_ACROSS, 1, 4), (F_OWN_FAR, 1, 0), (F_FF_END, 0), (F_TREE, 5, 3, 0, 0),
    (F_RANK_ACROSS, 1, 1), (F_BLOCK, 0, 2), (F_TREE_END, 1), (F_RANK_ACROSS, 1, 7), (F_ACT_X, 0, 0, 1),
    (F_RANK_ACROSS, 1, 4), (F_ACT_C, 0, 0, 1, 0), (F_RANK_ACROSS, 1, 5), (F_ATTENTION, 1), (F_FAR_ACROSS, 1, 1),
    (F_BLOCK, 0, 1), (F_ACT_X, 1, 1, 1), (F_FAR_ACROSS, 1, 7), (F_FAR_ACROSS, 1, 6), (F_ACT_C, 0, 0, 1, 1),
    (F_BLOCK, 0, 3), (F_BLOCK, 0, 0), (F_FAR_ACROSS, 1, 5), (F_ACT_C, 1, 1, 0, 1), (F_FAR_ACROSS, 1, 0),
    (F_DOWN_GRAD, 0), (F_ACT_Z, 0, 1), (F_ACT_C, 1, 1, 1, 1), (F_ACT_X, 0, 1, 0), (F_GATE_GRAD, 0),
    (F_FF_END, 1), (F_ACT_C, 0, 1, 0, 1), (F_BLOCK, 1, 2), (F_ACT_C, 0, 1, 1, 0), (F_ACT_C, 0, 1, 0, 0),
    (F_BLOCK, 1, 1), (F_ACT_X, 0, 1, 1), (F_BLOCK, 1, 0), (F_ACT_C, 0, 1, 1, 1), (F_BLOCK, 1, 3),
    (F_DOWN_GRAD, 1), (F_GATE_GRAD, 1),
]


def forward_kernel(
    valid_ref,
    lengths_ref,
    norm_attn_ref,
    norm_ff_ref,
    tokens_ref,
    cot_ref,
    qkv_ref,
    out_ref,
    gate_up_ref,
    down_ref,
    gain_rows,
    cot_rows,
    qkv_rows,
    context,
    resid_mid,
    qkv_full,
    out_full,
    ff_out,
    ff_back,
    gate_up_grad,
    down_grad,
    qkv_buf,
    out_buf,
    gate_up_buf,
    down_buf,
    rows_buf,
    grads_buf,
    hidden,
    d_gate_up,
    out_stage,
    back_stage,
    gate_up_stage,
    down_stage,
    gains_own,
    gains_all,
    gate_up_raw,
    gate_up_parts,
    grads_own,
    attn_in,
    halves,
    spread,
    plane_sem,
    sibling_sem,
    send_sem,
    gains_send,
    gains_recv,
    rank_send,
    rank_recv,
    far_send,
    far_recv,
    across_send,
    across_recv,
    act_send,
    act_recv,
    local_sem,
    keep_sem,
    stage_sem,
):
    z, y, x, core = here()
    me = 2 * (z * 4 + y * 2 + x) + core
    zh, zl, member, rank, device, far, across = group_place(z, y, x, core)
    own_step = (0, 0, 0)
    act_height, positions, model = tokens_ref.shape
    height = gate_up_ref.shape[1]
    down_height = down_ref.shape[1]
    split = 4 * down_height
    sibling = neighbour("s", z, y, x, core)
    greet_all(z, y, x, core)
    part = qkv_ref.shape[2] * 12 // 24
    rest = qkv_ref.shape[2] - part
    pieces = []
    for s in range(positions):
        pieces.append((qkv_ref, qkv_buf, s, pl.ds(0, part), "zxy"))
        pieces.append((qkv_ref, qkv_buf, s, pl.ds(part, rest), "zyx"))
        pieces.append((out_ref, out_buf, s, pl.ds(0, model), ("zyx", "yxz")[s % 2]))

    def piece_rows(piece, number):
        _, full, index, columns, _ = pieces[piece]
        return full.at[index, pl.ds(pl.multiple_of(number * height, height), height), columns]

    def tree_send(piece, offset, direction):
        source, _, index, columns, _ = pieces[piece]
        chip = chip_of(offset, z, y, x)
        block = piece_rows(piece, 2 * chip + core)
        return push(
            source.at[index, :, columns] if hops(offset) == 0 else block,
            block,
            send_sem.at[piece, DIRECTIONS.index(direction)],
            sibling_sem.at[piece] if direction == "s" else plane_sem.at[piece, chip],
            neighbour(direction, z, y, x, core),
        )

    def tree_step(piece, offset):
        order = pieces[piece][4]

        def go():
            chip = chip_of(offset, z, y, x)
            if hops(offset) > 0:
                arrived(piece_rows(piece, 2 * chip + core), plane_sem.at[piece, chip], sibling)
            for direction in onward(order, offset) + ["s"]:
                copy = tree_send(piece, offset, direction)
                maybe(direction_exists(direction, z), copy.start)

        maybe(offset_exists(offset, z), go)

    def tree_bytes(piece, count):
        _, full, index, columns, _ = pieces[piece]
        return full.at[index, pl.ds(0, count * height), columns]

    def tree_sent(piece):
        order = pieces[piece][4]

        def sent(direction, count):
            block = tree_bytes(piece, count)
            push(block, block, send_sem.at[piece, DIRECTIONS.index(direction)], gains_recv, sibling).wait_send()

        sent("s", 16)
        for direction in "xy":
            sent(direction, tree_count(order, direction, 3))
        for direction in "ud":
            for level in range(4):
                if level != (3 if direction == "u" else 0):
                    pl.when(z == level)(
                        functools.partial(sent, direction, tree_count(order, direction, level))
                    )

    def tree_end(s):
        mine = [piece for piece in range(len(pieces)) if pieces[piece][2] == s]

        for piece in mine:
            arrived(tree_bytes(piece, 16), sibling_sem.at[piece], sibling)
        for piece in mine:
            tree_own[piece].wait()

    tree_own = [
        pltpu.make_async_copy(
            source.at[index, :, columns], piece_rows(piece, me), local_sem.at[piece]
        )
        for piece, (source, _, index, columns, _) in enumerate(pieces)
    ]

    def gains_copy(step):
        other = lax.rem(me + step, 32)
        return push(
            gains_own,
            gains_all.at[me],
            gains_send,
            gains_recv,
            (lax.div(other, 2), lax.rem(other, 2)),
        )

    def gains_start(step, carry):
        gains_copy(step).start()
        return carry

    def start(copy):
        copy.start()

    def weight_rows(s, number):
        return gate_up_buf.at[s, pl.ds(pl.multiple_of(number * height, height), height), :]

    def down_rows(s, dzh, dy):
        number = 2 * flip(zh, dzh) + flip(y, dy)
        return down_buf.at[s, pl.ds(pl.multiple_of(number * down_height, down_height), down_height), :]

    def act_rows(which, s, step):
        full = (rows_buf, grads_buf)[which]
        return full.at[s, pl.ds(pl.multiple_of(rank(step) * act_height, act_height), act_height), :]

    def send_act(which, s, step, source, hop):
        landed = tuple(bit ^ (1 if axis == hop else 0) for axis, bit in enumerate(step))
        start(
            push(
                source,
                act_rows(which, s, step),
                act_send.at[which, s, hop],
                act_recv.at[which, s, 4 * landed[0] + 2 * landed[1] + landed[2]],
                member(tuple(1 if axis == hop else 0 for axis in range(3))),
            )
        )

    def wait_act(which, s, step):
        arrived(
            act_rows(which, s, step),
            act_recv.at[which, s, 4 * step[0] + 2 * step[1] + step[2]],
            sibling,
        )

    def act_own(which, s):
        source = act_rows(0, s, own_step) if which == 0 else grads_own.at[s]
        for hop in (0, 1, 2):
            send_act(which, s, own_step, source, hop)

    def act_from_z(which, s):
        step = (1, 0, 0)
        wait_act(which, s, step)
        send_act(which, s, step, act_rows(which, s, step), 1)
        send_act(which, s, step, act_rows(which, s, step), 2)

    def act_from_x(which, s, dl):
        wait_act(which, s, (dl, 1, 0))
        send_act(which, s, (dl, 1, 0), act_rows(which, s, (dl, 1, 0)), 2)

    def act_from_core(which, s, dl, dx):
        wait_act(which, s, (dl, dx, 1))

    def mine(s):
        return gate_up_parts.at[rank(own_step), s]

    def ff_source(s, slot):
        return down_ref.at[s] if slot == 8 else mine(s)

    def ff_rows(s, slot, dzh):
        return down_rows(s, dzh, 0) if slot == 8 else weight_rows(s, device(RANK_STEPS[slot], dzh, 0))

    def to_rank(s, slot):
        step = RANK_STEPS[slot]
        start(
            push(
                gate_up_parts.at[rank(step), s],
                weight_rows(s, device(own_step)),
                rank_send.at[s],
                rank_recv.at[s, slot],
                member(step),
            )
        )

    def send_far(s, slot, source):
        start(push(source, ff_rows(s, slot, 0), far_send.at[s], far_recv.at[s, slot], far))

    def send_across(s, slot, source, dzh):
        start(
            push(
                source,
                ff_rows(s, slot, dzh),
                across_send.at[s],
                across_recv.at[s],
                across,
            )
        )

    def own_far(s, slot):
        send_far(s, slot, ff_source(s, slot))

    def own_across(s, slot):
        send_across(s, slot, ff_source(s, slot), 0)

    def rank_far(s, slot):
        arrived(ff_rows(s, slot, 0), rank_recv.at[s, slot], sibling)
        send_far(s, slot, ff_rows(s, slot, 0))

    def rank_across(s, slot):
        send_across(s, slot, ff_rows(s, slot, 0), 0)

    def far_across(s, slot):
        arrived(ff_rows(s, slot, 1), far_recv.at[s, slot], sibling)
        send_across(s, slot, ff_rows(s, slot, 1), 1)

    def ff_end(s):
        for copy in ff_local[s]:
            copy.wait()
        arrived(ff_bytes(s, 2 * share), across_recv.at[s], sibling)

    share = 8 * height + down_height * model // gate_up_buf.shape[2]

    def ff_bytes(s, rows):
        return gate_up_buf.at[s, pl.ds(0, rows), :]

    def ff_sent(s):
        for sem, rows in ((rank_send, 7 * height), (far_send, share), (across_send, 2 * share)):
            block = ff_bytes(s, rows)
            push(block, block, sem.at[s], gains_recv, sibling).wait_send()
        for which, full in enumerate((rows_buf, grads_buf)):
            for hop, count in enumerate((1, 2, 4)):
                block = full.at[s, pl.ds(0, count * act_height), :]
                push(block, block, act_send.at[which, s, hop], gains_recv, sibling).wait_send()

    ff_local = []
    for s in range(positions):
        ff_local.append(
            [
                pltpu.make_async_copy(mine(s), weight_rows(s, device(own_step)), local_sem.at[7 + 3 * s]),
                pltpu.make_async_copy(down_ref.at[s], down_rows(s, 0, 0), local_sem.at[8 + 3 * s]),
                pltpu.make_async_copy(grads_own.at[s], act_rows(1, s, own_step), local_sem.at[9 + 3 * s]),
            ]
        )
    gains_local = pltpu.make_async_copy(gains_own, gains_all.at[me], local_sem.at[6])

    def gains_begin():
        places = 128 // norm_attn_ref.shape[1]
        lane = lax.broadcasted_iota(jnp.int32, (positions, 128), 1) // norm_attn_ref.shape[1]
        gains_own[...] = jnp.zeros_like(gains_own)
        for index, source in enumerate((norm_attn_ref, norm_ff_ref)):
            tiled = jnp.concatenate([source[...].astype(F32)] * places, axis=1)
            gains_own[index * positions : (index + 1) * positions, :] = jnp.where(
                lane == lax.rem(me, places), tiled, 0.0
            ).astype(BF16)
        lax.fori_loop(1, 32, gains_start, 0)
        gains_local.start()

    raw_copy = pltpu.make_async_copy(gate_up_ref, gate_up_raw, local_sem.at[13])

    def part_units():
        raw_copy.wait()
        unit = down_height
        for number in range(8):
            low, rest = divmod(number, 4)
            for s in range(positions):
                for side in (0, 1):
                    for group in range(4):
                        zh_part, y_part = divmod(group, 2)
                        block = 32 * side + 16 * zh_part + 8 * low + 4 * y_part + rest
                        gate_up_parts[number, s, :, (4 * side + group) * unit : (4 * side + group + 1) * unit] = (
                            gate_up_raw[s, :, block * unit : (block + 1) * unit]
                        )
        for s in range(positions):
            ff_local[s][0].start()
            ff_local[s][1].start()

    def weigh():
        def one(rows):
            slot = lax.broadcasted_iota(jnp.int32, (16, 128), 0) + rows.start
            frame = me * act_height + slot
            weight = jnp.zeros((16, 128), F32)
            first = 0
            for item in range(lengths_ref.shape[0]):
                length = lengths_ref[item]
                inside = (frame >= first) & (frame < first + length)
                share = 8.0 * act_height / jnp.full((16, 128), length, jnp.int32).astype(F32)
                weight = weight + jnp.where(inside, share, 0.0)
                first = first + length
            weight = jnp.where(slot < valid_ref[0], weight, 0.0)[:, :1]
            values = cot_ref[rows].astype(F32)
            for p in range(positions):
                grads = values[:, p, :] * weight
                cot_rows[p, rows, :] = grads
                grads_own[p, rows, :] = grads.astype(BF16)

        row_loop(act_height, 16, one)
        for s in range(positions):
            ff_local[s][2].start()

    def take_gains():
        others = gains_all.at[pl.ds(0, 31)]
        arrived(others, gains_recv, sibling)
        push(others, others, gains_send, gains_recv, sibling).wait_send()
        gains_local.wait()
        for block in range(8):
            total = gains_all[4 * block].astype(F32)
            for extra in range(1, 4):
                total = total + gains_all[4 * block + extra].astype(F32)
            gain_rows[:, 128 * block : 128 * block + 128] = total

        def first_norm(rows):
            values = tokens_ref[rows].astype(F32)
            for p in range(positions):
                resid_mid[p, rows, :] = values[:, p, :]
                r, _ = normed(values[:, p, :])
                attn_in[p, rows, :] = (r * gain_rows[p : p + 1, :]).astype(BF16)

        row_loop(act_height, 16, first_norm)

    keep = []

    def attention(p):
        for source, target, slot in (
            (qkv_buf.at[p], qkv_full.at[p], 2 * p),
            (out_buf.at[p], out_full.at[p], 2 * p + 1),
        ):
            keep.append(pltpu.make_async_copy(source, target, keep_sem.at[slot]))
            keep[-1].start()

        def project(columns):
            qkv_rows[p, :, columns] = dot(attn_in[p], qkv_buf[p, :, columns]).astype(BF16)

        tile_loop(3 * model, 512, project)
        probs = attention_probs(qkv_rows, halves, spread, model, p)
        for q in range(p + 1):
            halves[2 * q] = to_heads(probs[q].astype(BF16), spread)

        def mix(rows):
            total = None
            for q in range(p + 1):
                term = halves[2 * q, rows, :].astype(F32) * qkv_rows[q, rows, 2 * model :].astype(F32)
                total = term if total is None else total + term
            context[p, rows, :] = total.astype(BF16)

        row_loop(act_height, 16, mix)

        def attend(columns):
            resid_mid[p, :, columns] += dot(context[p], out_buf[p, :, columns])

        tile_loop(model, 512, attend)

        def second_norm(step, carry):
            rows = pl.ds(pl.multiple_of(step * 16, 16), 16)
            r, _ = normed(resid_mid[p, rows, :])
            top = rank(own_step) * act_height + step * 16
            rows_buf[p, pl.ds(pl.multiple_of(top, 16), 16), :] = (
                r * gain_rows[positions + p : positions + p + 1, :]
            ).astype(BF16)
            return carry

        lax.fori_loop(0, act_height // 16, second_norm, 0)

    def ff_block(s, number):
        rows = pl.ds(pl.multiple_of(number * 2 * act_height, 2 * act_height), 2 * act_height)
        normed_rows = rows_buf[s, rows, :]
        grads = grads_buf[s, rows, :]
        for tile in range(split // 256):
            left, right = pl.ds(tile * 256, 256), pl.ds(split + tile * 256, 256)
            gate = dot(normed_rows, gate_up_buf[s, :, left])
            up = dot(normed_rows, gate_up_buf[s, :, right])
            d_hidden = dot_back(grads, down_buf[s, left, :])
            sigmoid_gate = jax.nn.sigmoid(gate)
            silu_gate = gate * sigmoid_gate
            hidden[rows, left] = (silu_gate * up).astype(BF16)
            d_gate_up[rows, left] = (
                d_hidden * up * sigmoid_gate * (1.0 + gate * (1.0 - sigmoid_gate))
            ).astype(BF16)
            d_gate_up[rows, right] = (d_hidden * silu_gate).astype(BF16)
        for tile in range(model // 512):
            columns = pl.ds(tile * 512, 512)
            out_stage[rows, columns] = dot(hidden[rows, :], down_buf[s, :, columns]).astype(BF16)
            back_stage[rows, columns] = dot_back(
                d_gate_up[rows, :], gate_up_buf[s, columns, :]
            ).astype(BF16)

    stages = []

    def stage_out(s, *slots):
        for slot in slots:
            source, target = (
                (out_stage, ff_out),
                (back_stage, ff_back),
                (gate_up_stage, gate_up_grad),
                (down_stage, down_grad),
            )[slot]
            stages.append(pltpu.make_async_copy(source, target.at[s], stage_sem.at[s, slot]))
            stages[-1].start()

    def gate_grad(s):
        stage_out(s, 0, 1)

        def gate_up_tile(columns):
            gate_up_stage[:, columns] = dot_grad(rows_buf[s], d_gate_up[:, columns]).astype(BF16)

        tile_loop(2 * split, 1024, gate_up_tile)
        stage_out(s, 2)

    def down_weights_grad(s):
        def down_tile(columns):
            down_stage[:, columns] = dot_grad(hidden[...], grads_buf[s, :, columns]).astype(BF16)

        tile_loop(model, 1024, down_tile)
        stage_out(s, 3)

    def stages_end():
        while stages:
            stages.pop(0).wait()

    for copy in tree_own:
        copy.start()
    raw_copy.start()
    gains_begin()
    make_spread(spread)
    chips = ((0, 0), (1, 0), (0, 1), (1, 1))

    def block(s, order):
        if s > 0 and order == chosen_first[0]:
            stages_end()
        ff_block(s, 2 * flip(zl, chips[order][0]) + flip(x, chips[order][1]))

    def attend_and_send(s):
        attention(s)
        act_own(0, s)

    chosen_first = [step[2] for step in FORWARD_STEPS if step[:2] == (F_BLOCK, 1)]
    kinds = {
        F_TREE: lambda piece, dz, dy, dx: tree_step(piece, (dz, dy, dx)),
        F_TREE_END: tree_end,
        F_GAINS: take_gains,
        F_PARTS: part_units,
        F_COT: weigh,
        F_ATTENTION: attend_and_send,
        F_GRADS: lambda s: act_own(1, s),
        F_ACT_Z: act_from_z,
        F_ACT_X: act_from_x,
        F_ACT_C: act_from_core,
        F_TO_RANK: to_rank,
        F_OWN_FAR: own_far,
        F_OWN_ACROSS: own_across,
        F_RANK_FAR: rank_far,
        F_RANK_ACROSS: rank_across,
        F_FAR_ACROSS: far_across,
        F_FF_END: ff_end,
        F_BLOCK: block,
        F_GATE_GRAD: gate_grad,
        F_DOWN_GRAD: down_weights_grad,
    }
    for kind, *numbers in FORWARD_STEPS:
        kinds[kind](*numbers)
    for piece in range(len(pieces)):
        tree_sent(piece)
    for s in range(positions):
        ff_sent(s)
    for copy in keep:
        copy.wait()
    stages_end()


def forward_gather(valid, lengths, norm_attn, norm_ff, tokens, cot, w_qkv, w_out, w_gate_up, w_down):
    act_height, positions, model = tokens.shape
    _, height, qkv_width = w_qkv.shape
    unit = w_down.shape[1]
    ranks, split, width = 8, 4 * unit, 8 * unit
    group_rows = ranks * act_height
    dma = pltpu.SemaphoreType.DMA
    vmem = pl.BlockSpec(memory_space=pltpu.VMEM)
    smem = pl.BlockSpec(memory_space=pltpu.SMEM)
    anywhere = pl.BlockSpec(memory_space=pl.ANY)
    return pl.pallas_call(
        forward_kernel,
        out_shape=(
            jax.ShapeDtypeStruct((16, model), F32),
            jax.ShapeDtypeStruct((positions, act_height, model), F32),
            jax.ShapeDtypeStruct((positions, act_height, 3 * model), BF16),
            jax.ShapeDtypeStruct((positions, act_height, model), BF16),
            jax.ShapeDtypeStruct((positions, act_height, model), F32),
            jax.ShapeDtypeStruct((positions, model, qkv_width), BF16),
            jax.ShapeDtypeStruct((positions, model, model), BF16),
            jax.ShapeDtypeStruct((positions, group_rows, model), BF16),
            jax.ShapeDtypeStruct((positions, group_rows, model), BF16),
            jax.ShapeDtypeStruct((positions, model, width), BF16),
            jax.ShapeDtypeStruct((positions, split, model), BF16),
        ),
        in_specs=[smem] * 2 + [vmem] * 4 + [anywhere] * 4,
        out_specs=(vmem,) * 5 + (anywhere,) * 6,
        scratch_shapes=[
            pltpu.VMEM((positions, model, qkv_width), BF16),
            pltpu.VMEM((positions, model, model), BF16),
            pltpu.VMEM((positions, model, width), BF16),
            pltpu.VMEM((positions, split, model), BF16),
            pltpu.VMEM((positions, group_rows, model), BF16),
            pltpu.VMEM((positions, group_rows, model), BF16),
            pltpu.VMEM((group_rows, split), BF16),
            pltpu.VMEM((group_rows, width), BF16),
            pltpu.VMEM((group_rows, model), BF16),
            pltpu.VMEM((group_rows, model), BF16),
            pltpu.VMEM((model, width), BF16),
            pltpu.VMEM((split, model), BF16),
            pltpu.VMEM((16, 128), BF16),
            pltpu.VMEM((32, 16, 128), BF16),
            pltpu.VMEM(w_gate_up.shape, BF16),
            pltpu.VMEM((ranks, positions, height, width), BF16),
            pltpu.VMEM((positions, act_height, model), BF16),
            pltpu.VMEM((positions, act_height, model), BF16),
            pltpu.VMEM((2 * positions, act_height, model), BF16),
            pltpu.VMEM((model, 128), BF16),
            dma((6, 16)),
            dma((6,)),
            dma((6, 5)),
            dma,
            dma,
            dma((2,)),
            dma((2, 8)),
            dma((2,)),
            dma((2, 9)),
            dma((2,)),
            dma((2,)),
            dma((2, 2, 3)),
            dma((2, 2, 8)),
            dma((14,)),
            dma((4,)),
            dma((2, 4)),
        ],
        compiler_params=pltpu.CompilerParams(
            collective_id=4, has_side_effects=True, vmem_limit_bytes=62 * 2**20
        ),
        name="forward_gather",
    )(valid, lengths, norm_attn, norm_ff, tokens, cot, w_qkv, w_out, w_gate_up, w_down)


def slot_index(order, direction, offset, z, y, x):
    axis = {"u": "z", "d": "z"}.get(direction, direction)
    index, count = 0, 1
    values = dict(z=z + offset[0], y=flip(y, offset[1]), x=flip(x, offset[2]))
    sizes = dict(z=4, y=2, x=2)
    for earlier in order[: order.index(axis)]:
        index = index * sizes[earlier] + values[earlier]
        count *= sizes[earlier]
    if axis == "z":
        index = index * 5 + (4 if direction == "d" and offset[0] == 0 else values["z"])
        count *= 5
    return index, count


def slot_base(order):
    base, total = {}, 0
    for axis, direction in (("x", "x"), ("y", "y"), ("z", "u")):
        base[axis] = total
        total += slot_index(order, direction, (0, 0, 0), 0, 0, 0)[1]
    base["u"] = base["d"] = base["z"]
    return base, total


(
    B_TREE,
    B_RS_ACROSS,
    B_RS_FIRST,
    B_RS_SECOND,
    B_RS_RANK,
    B_RS_LAST,
    B_ACT_CORE,
    B_ACT_LOAD,
    B_ACT_ADD_X,
    B_ACT_ADD_Z,
    B_ACT_SUM,
    B_NORM_TURN,
    B_SWAP_TURNED,
    B_PROBS,
    B_MID,
    B_SCORES_BACK,
    B_SWAP_QKV,
    B_OUT_W,
    B_QKV_W,
    B_ROWS_BACK,
    B_ATTN_BACK,
    B_FINISH_OUTPUT,
) = range(22)
BACKWARD_STEPS = [
    (B_ACT_CORE, 0, 0), (B_RS_ACROSS, 0, 0, 0), (B_ACT_ADD_X, 0, 0, 1), (B_RS_ACROSS, 0, 0, 1),
    (B_RS_ACROSS, 0, 1, 0), (B_ACT_CORE, 0, 1), (B_ACT_CORE, 1, 1), (B_NORM_TURN,), (B_ACT_ADD_X, 0, 0, 0),
    (B_ACT_ADD_X, 0, 1, 1), (B_RS_ACROSS, 0, 1, 1), (B_RS_FIRST, 0, 0), (B_ACT_ADD_Z, 0, 0), (B_RS_FIRST, 0, 1),
    (B_ACT_ADD_Z, 0, 1), (B_RS_ACROSS, 0, 0, 2), (B_PROBS,), (B_SWAP_TURNED,), (B_ACT_ADD_X, 0, 1, 0),
    (B_ACT_CORE, 1, 0), (B_ACT_SUM, 0, 0), (B_RS_ACROSS, 1, 0, 2), (B_MID, 0), (B_RS_ACROSS, 1, 0, 1),
    (B_OUT_W, 0), (B_TREE, 2, -1, 1, 1), (B_TREE, 2, -3, 1, 1), (B_TREE, 2, 2, 1, 1), (B_RS_FIRST, 0, 2),
    (B_TREE, 2, 3, 1, 1), (B_TREE, 2, 0, 0, 1), (B_TREE, 2, 1, 0, 1), (B_ACT_SUM, 0, 1), (B_TREE, 2, 3, 0, 1),
    (B_TREE, 2, 0, 1, 1), (B_TREE, 2, 1, 1, 1), (B_MID, 1), (B_ACT_LOAD, 1), (B_RS_ACROSS, 1, 0, 0),
    (B_ACT_ADD_X, 1, 1, 0), (B_ACT_ADD_X, 1, 0, 0), (B_SCORES_BACK,), (B_SWAP_QKV,), (B_OUT_W, 1),
    (B_RS_FIRST, 1, 1), (B_ACT_ADD_X, 1, 1, 1), (B_RS_ACROSS, 1, 1, 0), (B_QKV_W, 0), (B_TREE, 3, 2, 0, 1),
    (B_TREE, 0, -1, 1, 1), (B_RS_SECOND, 0, 1), (B_RS_SECOND, 0, 0), (B_ACT_ADD_X, 1, 0, 1), (B_QKV_W, 1),
    (B_RS_RANK, 0, 3), (B_TREE, 3, 3, 0, 1), (B_TREE, 2, -3, 1, 0), (B_RS_ACROSS, 1, 1, 1),
    (B_TREE, 2, 3, 1, 0), (B_ROWS_BACK, 0), (B_TREE, 1, -3, 1, 1), (B_TREE, 0, 2, 1, 1), (B_TREE, 1, 2, 1, 1),
    (B_TREE, 0, 3, 1, 1), (B_TREE, 2, -2, 1, 1), (B_RS_RANK, 0, 7), (B_TREE, 1, -2, 1, 1),
    (B_TREE, 3, -2, 1, 1), (B_TREE, 3, 3, 1, 0), (B_TREE, 0, -2, 1, 1), (B_TREE, 0, 0, 1, 1),
    (B_TREE, 3, 2, 1, 0), (B_RS_FIRST, 1, 0), (B_TREE, 1, -1, 0, 1), (B_TREE, 3, 3, 1, 1),
    (B_TREE, 3, -3, 1, 1), (B_TREE, 0, -3, 1, 1), (B_TREE, 3, -2, 1, 0), (B_TREE, 1, -3, 0, 1),
    (B_TREE, 3, 2, 1, 1), (B_TREE, 3, -3, 1, 0), (B_TREE, 3, -1, 1, 0), (B_TREE, 0, 2, 1, 0),
    (B_TREE, 3, -3, 0, 1), (B_RS_SECOND, 1, 1), (B_TREE, 3, -2, 0, 1), (B_TREE, 3, -3, 0, 0),
    (B_TREE, 0, 3, 0, 1), (B_TREE, 1, -1, 1, 1), (B_TREE, 1, 3, 1, 1), (B_TREE, 0, -1, 1, 0),
    (B_TREE, 0, 3, 1, 0), (B_TREE, 2, 3, 0, 0), (B_TREE, 1, 0, 1, 1), (B_TREE, 1, 1, 0, 1),
    (B_TREE, 2, 2, 1, 0), (B_ACT_ADD_Z, 1, 0), (B_ACT_ADD_Z, 1, 1), (B_TREE, 3, -1, 1, 1), (B_RS_LAST, 0, 7),
    (B_TREE, 2, -2, 1, 0), (B_TREE, 2, -2, 0, 1), (B_TREE, 0, 3, 0, 0), (B_TREE, 2, -1, 1, 0),
    (B_RS_SECOND, 1, 0), (B_TREE, 2, -3, 0, 1), (B_TREE, 1, 3, 0, 1), (B_RS_RANK, 1, 3), (B_TREE, 1, 3, 1, 0),
    (B_TREE, 3, 1, 1, 0), (B_RS_RANK, 1, 1), (B_TREE, 1, -3, 1, 0), (B_TREE, 1, 1, 1, 1), (B_RS_RANK, 1, 5),
    (B_TREE, 3, 1, 0, 1), (B_TREE, 0, -3, 0, 1), (B_TREE, 3, -2, 0, 0), (B_RS_FIRST, 1, 2),
    (B_TREE, 0, 1, 1, 1), (B_TREE, 1, -2, 0, 1), (B_TREE, 3, 1, 1, 1), (B_TREE, 0, -3, 1, 0), (B_RS_RANK, 1, 2),
    (B_TREE, 0, 2, 0, 1), (B_ROWS_BACK, 1), (B_RS_RANK, 0, 5), (B_TREE, 3, 3, 0, 0), (B_RS_ACROSS, 0, 1, 2),
    (B_TREE, 1, 3, 0, 0), (B_TREE, 0, 1, 1, 0), (B_RS_RANK, 0, 1), (B_RS_RANK, 0, 4), (B_RS_RANK, 1, 4),
    (B_TREE, 0, -2, 0, 1), (B_TREE, 2, 2, 0, 1), (B_TREE, 1, -2, 1, 0), (B_TREE, 3, -1, 0, 1),
    (B_TREE, 0, -2, 1, 0), (B_TREE, 2, -3, 0, 0), (B_TREE, 1, 2, 1, 0), (B_TREE, 3, 0, 1, 1), (B_ACT_SUM, 1, 0),
    (B_TREE, 1, 2, 0, 1), (B_RS_ACROSS, 1, 1, 2), (B_RS_RANK, 0, 6), (B_TREE, 0, -3, 0, 0),
    (B_TREE, 1, -3, 0, 0), (B_TREE, 0, 2, 0, 0), (B_RS_RANK, 0, 2), (B_RS_RANK, 1, 6), (B_ACT_SUM, 1, 1),
    (B_TREE, 1, -1, 1, 0), (B_TREE, 2, 1, 1, 0), (B_FINISH_OUTPUT,), (B_TREE, 2, 2, 0, 0), (B_RS_LAST, 0, 4),
    (B_RS_LAST, 0, 5), (B_TREE, 0, 1, 0, 1), (B_RS_LAST, 0, 3), (B_TREE, 0, -1, 0, 1), (B_TREE, 1, -2, 0, 0),
    (B_RS_LAST, 1, 1), (B_TREE, 0, -2, 0, 0), (B_TREE, 3, 2, 0, 0), (B_RS_SECOND, 0, 2), (B_RS_LAST, 1, 2),
    (B_TREE, 1, 1, 1, 0), (B_RS_LAST, 1, 3), (B_TREE, 2, -1, 0, 1), (B_TREE, 0, 0, 0, 1), (B_TREE, 1, 0, 0, 1),
    (B_TREE, 2, 0, 1, 0), (B_TREE, 2, -2, 0, 0), (B_RS_LAST, 1, 4), (B_RS_SECOND, 1, 2), (B_TREE, 1, 2, 0, 0),
    (B_RS_LAST, 0, 2), (B_TREE, 3, 1, 0, 0), (B_TREE, 3, -1, 0, 0), (B_TREE, 3, 0, 1, 0), (B_TREE, 1, -1, 0, 0),
    (B_TREE, 1, 1, 0, 0), (B_RS_RANK, 1, 7), (B_TREE, 1, 0, 1, 0), (B_RS_LAST, 0, 1), (B_TREE, 0, 1, 0, 0),
    (B_TREE, 3, 0, 0, 1), (B_TREE, 0, 0, 1, 0), (B_TREE, 0, -1, 0, 0), (B_RS_LAST, 1, 5), (B_TREE, 2, 1, 0, 0),
    (B_RS_LAST, 0, 6), (B_ATTN_BACK,), (B_RS_LAST, 1, 6), (B_TREE, 2, -1, 0, 0), (B_TREE, 1, 0, 0, 0),
    (B_RS_LAST, 1, 7), (B_TREE, 0, 0, 0, 0), (B_TREE, 2, 0, 0, 0), (B_TREE, 3, 0, 0, 0),
]


def backward_kernel(
    tokens_ref,
    cot_ref,
    gain_rows,
    qkv_rows,
    context,
    resid_mid,
    qkv_full,
    out_full,
    out_ref,
    back_ref,
    gate_up_ref,
    down_ref,
    output,
    grad_tokens,
    norm_attn_sum,
    norm_ff_sum,
    qkv_sum,
    attn_out_sum,
    gate_up_total,
    down_sum,
    act_own,
    core_buf,
    x_buf,
    z_buf,
    gate_own,
    down_own,
    across_gate,
    across_down,
    far_gate,
    far_down,
    qkv_grad,
    out_grad,
    slots_0,
    slots_1,
    slots_2,
    slots_3,
    qkv_tiles,
    out_tiles,
    turned,
    attn_turned,
    context_turned,
    d_qkv,
    d_mid_low,
    d_mid,
    d_context,
    d_rows,
    halves,
    probs_buf,
    spread,
    gain_acc,
    gains_part,
    gains_buf,
    gains_sum,
    gate_up_sum,
    core_send,
    core_recv,
    x_send,
    x_recv,
    z_send,
    z_recv,
    across_send,
    across_recv,
    far_send,
    far_recv,
    rank_send,
    rank_recv,
    swap_send,
    swap_recv,
    tree_send,
    tree_recv,
    gains_send,
    gains_recv,
    own_sem,
    part_sem,
    tile_sem,
):
    z, y, x, core = here()
    me = 2 * (z * 4 + y * 2 + x) + core
    zh, zl, member, rank, device, far, across = group_place(z, y, x, core)
    own_step = (0, 0, 0)
    act_height, positions, model = tokens_ref.shape
    sets = positions
    height = qkv_sum.shape[1]
    down_height = down_sum.shape[1]
    half = 16 * height
    sibling = member((0, 0, 1))
    scale = 1.0 / math.sqrt(HEAD_DIM)
    pairs = pairs_of(positions)
    greet_all(z, y, x, core)
    sends = []

    def start(copy):
        copy.start()
        sends.append(copy)

    def run_rows(dzh, dy, low):
        number = 16 * flip(zh, dzh) + 4 * flip(y, dy) + 8 * low
        return pl.ds(pl.multiple_of(number * height, 4 * height), 4 * height)

    def down_rows(dzh, dy):
        number = 2 * flip(zh, dzh) + flip(y, dy)
        return pl.ds(pl.multiple_of(number * down_height, down_height), down_height)

    def ff_from(s, dzh, dy, part):
        if part == 2:
            return down_ref.at[s, down_rows(dzh, dy)]
        return gate_up_ref.at[s, run_rows(dzh, dy, part)]

    def ff_across(s, turn, part):
        return across_down.at[turn, s] if part == 2 else across_gate.at[turn, s, part]

    def ff_own(s, turn, part):
        return down_own.at[turn, s] if part == 2 else gate_own.at[turn, s, part]

    def ff_far(s, part):
        return far_down.at[s] if part == 2 else far_gate.at[s, part]

    def part_copy(s, turn, part):
        return pltpu.make_async_copy(
            ff_from(s, 1 - turn, 0, part), ff_own(s, turn, part), part_sem.at[turn, s, part]
        )

    def rs_across(s, turn, part):
        start(
            push(
                ff_from(s, 1 - turn, 1, part),
                ff_across(s, turn, part),
                across_send.at[turn, s, part],
                across_recv.at[turn, s, part],
                across,
            )
        )

    def rs_first(s, part):
        block = ff_across(s, 0, part)
        part_copy(s, 0, part).wait()
        arrived(block, across_recv.at[0, s, part], across)
        add_into(block, [block, ff_own(s, 0, part)])
        start(push(block, ff_far(s, part), far_send.at[s, part], far_recv.at[s, part], far))

    def rs_second(s, part):
        block = ff_across(s, 1, part)
        part_copy(s, 1, part).wait()
        arrived(block, across_recv.at[1, s, part], across)
        arrived(ff_far(s, part), far_recv.at[s, part], far)
        target = down_sum.at[s] if part == 2 else block
        add_into(target, [block, ff_far(s, part), ff_own(s, 1, part)])

    def share(step, s):
        number = 2 * flip(x, step[1]) + flip(core, step[2])
        return across_gate.at[
            1, s, flip(zl, step[0]), pl.ds(pl.multiple_of(number * height, height), height)
        ]

    def place_units(step, s, source):
        unit = down_height
        number = 8 * flip(zl, step[0]) + 2 * flip(x, step[1]) + flip(core, step[2])
        for side in (0, 1):
            for group in range(4):
                zh_part, y_part = divmod(group, 2)
                left = (32 * side + 16 * zh_part + 4 * y_part + number) * unit
                gate_up_total[s, :, pl.ds(pl.multiple_of(left, unit), unit)] = source[
                    :, (4 * side + group) * unit : (4 * side + group + 1) * unit
                ].astype(F32)

    def rs_rank(s, slot):
        step = RANK_STEPS[slot]
        push(
                share(step, s),
                gate_up_sum.at[rank(own_step), s],
                rank_send.at[s],
                rank_recv.at[slot, s],
                member(step),
            ).start()

    def rs_last(s, slot):
        step = RANK_STEPS[slot]
        block = gate_up_sum.at[rank(step), s]
        arrived(block, rank_recv.at[slot, s], member(step))
        place_units(step, s, block)

    acts = [back_ref, out_ref]

    def act_rows(step):
        return pl.ds(pl.multiple_of(rank(step) * act_height, act_height), act_height)

    def act_core(which, s):
        for dl, dx in ((1, 1), (0, 1), (1, 0), (0, 0)):
            start(
                push(
                    acts[which].at[s, act_rows((dl, dx, 1))],
                    core_buf.at[which, s, dl, dx],
                    core_send.at[which, s, dl, dx],
                    core_recv.at[which, s, dl, dx],
                    sibling,
                )
            )

    def act_copy(which, s, dl, dx):
        return pltpu.make_async_copy(
            acts[which].at[s, act_rows((dl, dx, 0))],
            act_own.at[s, dl, dx],
            own_sem.at[which, s, dl, dx],
        )

    def act_load(which):
        for s in range(sets):
            for dl in (0, 1):
                for dx in (0, 1):
                    act_copy(which, s, dl, dx).start()

    def act_ready(which, s, dl, dx):
        act_copy(which, s, dl, dx).wait()
        arrived(core_buf.at[which, s, dl, dx], core_recv.at[which, s, dl, dx], sibling)

    def act_add_x(which, s, dl):
        act_ready(which, s, dl, 1)
        block = core_buf.at[which, s, dl, 1]
        add_into(block, [block, act_own.at[s, dl, 1]])
        start(
            push(
                block,
                x_buf.at[which, s, dl],
                x_send.at[which, s, dl],
                x_recv.at[which, s, dl],
                member((0, 1, 0)),
            )
        )

    def act_add_z(which, s):
        act_ready(which, s, 1, 0)
        block = x_buf.at[which, s, 1]
        arrived(block, x_recv.at[which, s, 1], member((0, 1, 0)))
        add_into(block, [block, core_buf.at[which, s, 1, 0], act_own.at[s, 1, 0]])
        start(
            push(
                block, z_buf.at[which, s], z_send.at[which, s], z_recv.at[which, s], member((1, 0, 0))
            )
        )

    def act_sum(which, s):
        act_ready(which, s, 0, 0)
        arrived(x_buf.at[which, s, 0], x_recv.at[which, s, 0], member((0, 1, 0)))
        arrived(z_buf.at[which, s], z_recv.at[which, s], member((1, 0, 0)))

    def act_total(which, s, rows):
        return (
            act_own[s, 0, 0, rows, :].astype(F32)
            + core_buf[which, s, 0, 0, rows, :].astype(F32)
            + x_buf[which, s, 0, rows, :].astype(F32)
            + z_buf[which, s, rows, :].astype(F32)
        )

    pieces = [
        (qkv_grad, qkv_sum, 0, "zxy", slots_0),
        (qkv_grad, qkv_sum, 1, "zyx", slots_1),
        (out_grad, attn_out_sum, 0, "zyx", slots_2),
        (out_grad, attn_out_sum, 1, "yxz", slots_3),
    ]
    events = sorted(
        ((-hops(offset), place, piece, offset) for piece in range(4) for place, offset in enumerate(OFFSETS)),
        key=lambda event: event[:3],
    )

    def tree_block(piece, offset):
        source, _, index, _, _ = pieces[piece]
        chip = chip_of(offset, z, y, x)
        return source.at[index, pl.ds(pl.multiple_of(chip * height, height), height), :]

    def tree_copy(piece, offset):
        _, _, _, order, slots = pieces[piece]
        toward = came_from(order, offset)
        base, _ = slot_base(order)
        seen = {"x": "x", "y": "y", "u": "d", "d": "u"}[toward]
        nearer = offset
        if toward == "u":
            nearer = (offset[0] - 1, offset[1], offset[2])
        if toward == "d":
            nearer = (offset[0] + 1, offset[1], offset[2])
        there = {"u": z + 1, "d": z - 1}.get(toward, z)
        index_there, _ = slot_index(
            order, seen, nearer, there, y if toward != "y" else 1 - y, x if toward != "x" else 1 - x
        )
        if toward in "xy":
            index_there, _ = slot_index(order, seen, offset, z, y, x)
        place = base[seen] + index_there
        return push(
            tree_block(piece, offset),
            slots.at[place],
            tree_send.at[piece, DIRECTIONS.index(toward)],
            tree_recv.at[piece, place],
            neighbour(toward, z, y, x, core),
        )

    def tree_step(piece, offset):
        _, result, index, order, slots = pieces[piece]
        base, _ = slot_base(order)

        def go():
            block = tree_block(piece, offset)
            sure, unsure = [], []
            for direction in onward(order, offset):
                local, _ = slot_index(order, direction, offset, z, y, x)
                place = base[direction] + local
                (sure if direction in "xy" else unsure).append((direction, place))
            terms = [block]
            for _, place in sure:
                arrived(slots.at[place], tree_recv.at[piece, place], sibling)
                terms.append(slots.at[place])
            last = hops(offset) == 0
            target = result.at[index] if last else block
            if last or len(terms) > 1:
                add_into(target, terms)
            for direction, place in unsure:

                def more(place=place):
                    arrived(slots.at[place], tree_recv.at[piece, place], sibling)
                    add_into(target, [target, slots.at[place]])

                maybe(direction_exists(direction, z), more)
            if not last:
                tree_copy(piece, offset).start()

        maybe(offset_exists(offset, z), go)

    def gains_copy(step):
        other = lax.rem(me + step, 32)
        return push(
            gains_part.at[lax.div(other, 4)],
            gains_buf.at[me],
            gains_send,
            gains_recv,
            (lax.div(other, 2), lax.rem(other, 2)),
        )

    def gains_start(step, carry):
        gains_copy(step).start()
        return carry

    def gains_add(step, carry):
        gains_sum[...] += gains_buf[lax.rem(me + step, 32)]
        return carry

    def turn(source, target, slot):
        def one(block, p):
            flat = source(p, block)
            turned[slot, p, pl.ds(2 * block, 2)] = flat.T.astype(BF16).reshape(2, 2, height, act_height)

        for p in range(positions):
            for block in range(model // 128):
                one(block, p)
            target[p, :, :, :act_height] = turned[slot, p, :, core]

    qkv_tile = qkv_tiles.shape[1]
    tile_count = model // qkv_tile

    def qkv_load(number):
        p, tile = divmod(number, tile_count)
        return pltpu.make_async_copy(
            qkv_full.at[p, pl.ds(tile * qkv_tile, qkv_tile)],
            qkv_tiles.at[number % 2],
            tile_sem.at[number % 2],
        )

    out_loads = [
        pltpu.make_async_copy(out_full.at[p], out_tiles.at[p], tile_sem.at[2 + p]) for p in range(positions)
    ]

    def context_block(p, block):
        return context[p, :, 128 * block : 128 * block + 128].astype(F32)

    def attn_block(p, block):
        return d_rows[p, :, 128 * block : 128 * block + 128]

    def norm_turn():
        def attn_norm(rows):
            values = tokens_ref[rows].astype(F32)
            for p in range(positions):
                r, _ = normed(values[:, p, :])
                d_rows[p, rows, :] = r * gain_rows[p : p + 1, :]

        row_loop(act_height, 16, attn_norm)
        turn(context_block, context_turned, 0)
        turn(attn_block, attn_turned, 1)

    def landing(kind, p):
        other = pl.ds(act_height, act_height)
        return (
            context_turned.at[p, :, :, other],
            attn_turned.at[p, :, :, other],
            d_mid_low.at[p, other],
            d_qkv.at[p, other],
        )[kind]

    def swap(kind, p, source):
        start(
            push(source, landing(kind, p), swap_send.at[4 * p + kind], swap_recv.at[4 * p + kind], sibling)
        )

    def swap_wait(kind, p):
        arrived(landing(kind, p), swap_recv.at[4 * p + kind], sibling)

    def swap_turned():
        for p in range(positions):
            swap(0, p, turned.at[0, p, :, 1 - core])
            swap(1, p, turned.at[1, p, :, 1 - core])

    def find_probs():
        for p in range(positions):
            probs = attention_probs(qkv_rows, halves, spread, model, p)
            for q in range(p + 1):
                probs_buf[pairs.index((p, q))] = probs[q]

    def mid(p):
        def mid_back(rows):
            d_ff_in = act_total(0, p, rows)
            r, inverse = normed(resid_mid[p, rows, :])
            gain_acc[positions + p] += r * d_ff_in
            total = cot_ref[p, rows, :] + norm_back(
                r, inverse, d_ff_in * gain_rows[positions + p : positions + p + 1, :]
            )
            d_mid[p, rows, :] = total
            d_mid_low[p, rows, :] = total.astype(BF16)

        row_loop(act_height, 16, mid_back)
        swap(2, p, d_mid_low.at[p, pl.ds(0, act_height)])
        out_loads[p].wait()

        def context_back(columns):
            d_context[p, :, columns] = dot_back(
                d_mid_low[p, :act_height, :], out_tiles[p, columns, :]
            ).astype(BF16)

        tile_loop(model, 256, context_back)

    def scores_back():
        def context_products(rows):
            for index, (p, q) in enumerate(pairs):
                product = d_context[p, rows, :].astype(F32) * qkv_rows[q, rows, 2 * model :].astype(F32)
                halves[2 * index, rows, :], halves[2 * index + 1, rows, :] = split_product(product)

        row_loop(act_height, 16, context_products)
        d_probs = [sums_over_heads(halves, spread, index) for index in range(len(pairs))]
        for p in range(positions):
            own = [index for index, pair in enumerate(pairs) if pair[0] == p]
            mean = functools.reduce(jnp.add, [probs_buf[index] * d_probs[index] for index in own])
            for index in own:
                d_score = (probs_buf[index] * (d_probs[index] - mean)).astype(BF16)
                halves[2 * index] = to_heads(d_score, spread)
                halves[2 * index + 1] = to_heads(probs_buf[index].astype(BF16), spread)

        def plus(total, term):
            return term if total is None else total + term

        def qkv_back(rows):
            d_keys = [None] * positions
            d_values = [None] * positions
            for p in range(positions):
                d_query = None
                d_own = d_context[p, rows, :].astype(F32)
                query = qkv_rows[p, rows, :model].astype(F32)
                for index, (own, q) in enumerate(pairs):
                    if own == p:
                        d_score = halves[2 * index, rows, :].astype(F32)
                        key = qkv_rows[q, rows, model : 2 * model].astype(F32)
                        d_query = plus(d_query, d_score * key)
                        d_keys[q] = plus(d_keys[q], d_score * query)
                        d_values[q] = plus(
                            d_values[q], halves[2 * index + 1, rows, :].astype(F32) * d_own
                        )
                d_qkv[p, rows, :model] = (d_query * scale).astype(BF16)
            for p in range(positions):
                d_qkv[p, rows, model : 2 * model] = (d_keys[p] * scale).astype(BF16)
                d_qkv[p, rows, 2 * model :] = d_values[p].astype(BF16)

        row_loop(act_height, 16, qkv_back)

    def swap_qkv():
        for p in range(positions):
            swap(3, p, d_qkv.at[p, pl.ds(0, act_height)])

    def out_weights(p):
        swap_wait(0, p)
        swap_wait(2, p)

        def tile(columns):
            out_grad[p, :, columns] = dot(
                context_turned[p].reshape(half, 2 * act_height), d_mid_low[p, :, columns]
            ).astype(BF16)

        tile_loop(model, 256, tile)

    def qkv_weights(p):
        swap_wait(1, p)
        swap_wait(3, p)

        def tile(columns):
            qkv_grad[p, :, columns] = dot(
                attn_turned[p].reshape(half, 2 * act_height), d_qkv[p, :, columns]
            ).astype(BF16)

        tile_loop(3 * model, 512, tile)

    def rows_back(p):
        for tile in range(tile_count):
            number = p * tile_count + tile
            qkv_load(number).wait()
            d_rows[p, :, tile * qkv_tile : (tile + 1) * qkv_tile] = dot_back(
                d_qkv[p, :act_height, :], qkv_tiles[number % 2]
            )
            if number + 2 < positions * tile_count:
                qkv_load(number + 2).start()

    def attn_back():
        def norm_one_back(rows):
            values = tokens_ref[rows].astype(F32)
            for p in range(positions):
                r, inverse = normed(values[:, p, :])
                d_attn_in = d_rows[p, rows, :]
                gain_acc[p] += r * d_attn_in
                grad_tokens[rows, p, :] = d_mid[p, rows, :] + norm_back(
                    r, inverse, d_attn_in * gain_rows[p : p + 1, :]
                )

        row_loop(act_height, 16, norm_one_back)
        gains_part[...] = jnp.zeros_like(gains_part)
        for index in range(2 * positions):
            sums = jnp.sum(gain_acc[index], axis=0, keepdims=True)
            for block in range(8):
                gains_part[block, index : index + 1, :] = sums[:, 128 * block : 128 * block + 128]
        lax.fori_loop(1, 32, gains_start, 0)

    def finish_output():
        def finish(rows):
            rounded = [resid_mid[p, rows, :] + act_total(1, p, rows) for p in range(positions)]
            output[rows] = jnp.stack(rounded, axis=1).astype(BF16)

        row_loop(act_height, 16, finish)

    for s in range(sets):
        for turn_number in (0, 1):
            for part in (0, 1, 2):
                part_copy(s, turn_number, part).start()
    for copy in out_loads:
        copy.start()
    act_load(0)
    qkv_load(0).start()
    qkv_load(1).start()
    make_spread(spread)
    gain_acc[...] = jnp.zeros_like(gain_acc)
    kinds = {
        B_TREE: lambda piece, dz, dy, dx: tree_step(piece, (dz, dy, dx)),
        B_RS_ACROSS: rs_across,
        B_RS_FIRST: rs_first,
        B_RS_SECOND: rs_second,
        B_RS_RANK: rs_rank,
        B_RS_LAST: rs_last,
        B_ACT_CORE: act_core,
        B_ACT_LOAD: act_load,
        B_ACT_ADD_X: act_add_x,
        B_ACT_ADD_Z: act_add_z,
        B_ACT_SUM: act_sum,
        B_NORM_TURN: norm_turn,
        B_SWAP_TURNED: swap_turned,
        B_PROBS: find_probs,
        B_MID: mid,
        B_SCORES_BACK: scores_back,
        B_SWAP_QKV: swap_qkv,
        B_OUT_W: out_weights,
        B_QKV_W: qkv_weights,
        B_ROWS_BACK: rows_back,
        B_ATTN_BACK: attn_back,
        B_FINISH_OUTPUT: finish_output,
    }
    for kind, *numbers in BACKWARD_STEPS:
        kinds[kind](*numbers)
    for s in range(sets):
        place_units(own_step, s, share(own_step, s))
    gains_sum[...] = gains_part[lax.div(me, 4)]
    others = gains_buf.at[pl.ds(0, 31)]
    arrived(others, gains_recv, sibling)
    push(others, others, gains_send, gains_recv, sibling).wait_send()
    lax.fori_loop(1, 32, gains_add, 0)
    own_gain = norm_attn_sum.shape[1]
    for index, target in enumerate((norm_attn_sum, norm_ff_sum)):
        picked = jnp.zeros(target.shape, F32)
        for place in range(128 // own_gain):
            picked = picked + jnp.where(
                lax.rem(me, 128 // own_gain) == place,
                gains_sum[
                    index * positions : (index + 1) * positions, place * own_gain : (place + 1) * own_gain
                ],
                0.0,
            )
        target[...] = picked
    def tree_sent(piece, direction, count):
        source, _, index, _, _ = pieces[piece]
        block = source.at[index, pl.ds(0, count * height), :]
        push(block, block, tree_send.at[piece, DIRECTIONS.index(direction)], gains_recv, sibling).wait_send()

    for piece in range(len(pieces)):
        order = pieces[piece][3]
        for direction in "xy":
            tree_sent(piece, direction, return_count(order, direction, 3))
        for direction in "ud":
            for level in range(4):
                if level != (3 if direction == "u" else 0):
                    pl.when(z == level)(
                        functools.partial(
                            tree_sent, piece, direction, return_count(order, direction, level)
                        )
                    )
    for s in range(sets):
        block = gate_up_sum.at[pl.ds(0, 7), s]
        push(block, block, rank_send.at[s], gains_recv, sibling).wait_send()
    for copy in sends:
        copy.wait_send()


def backward_scatter(
    tokens,
    grads,
    gain_rows,
    qkv_rows,
    context,
    resid_mid,
    qkv_full,
    out_full,
    out_part,
    back_part,
    gate_up_grad,
    down_grad,
):
    act_height, sets, model = tokens.shape
    width = gate_up_grad.shape[2]
    height = model // 32
    down_height = down_grad.shape[1] // 4
    dma = pltpu.SemaphoreType.DMA
    vmem = pl.BlockSpec(memory_space=pltpu.VMEM)
    anywhere = pl.BlockSpec(memory_space=pl.ANY)
    places = [slot_base(order)[1] for order in ORDERS]
    pair_count = len(pairs_of(sets))
    act = (sets, act_height, model)
    return pl.pallas_call(
        backward_kernel,
        out_shape=(
            jax.ShapeDtypeStruct(tokens.shape, BF16),
            jax.ShapeDtypeStruct(tokens.shape, F32),
            jax.ShapeDtypeStruct((sets, height), F32),
            jax.ShapeDtypeStruct((sets, height), F32),
            jax.ShapeDtypeStruct((sets, height, 3 * model), F32),
            jax.ShapeDtypeStruct((sets, height, model), F32),
            jax.ShapeDtypeStruct((sets, height, 8 * width), F32),
            jax.ShapeDtypeStruct((sets, down_height, model), F32),
        ),
        in_specs=[vmem] * 6 + [anywhere] * 6,
        out_specs=(vmem,) * 8,
        scratch_shapes=[
            pltpu.VMEM((sets, 2, 2, act_height, model), BF16),
            pltpu.VMEM((2, sets, 2, 2, act_height, model), BF16),
            pltpu.VMEM((2, sets, 2, act_height, model), BF16),
            pltpu.VMEM((2, sets, act_height, model), BF16),
            pltpu.VMEM((2, sets, 2, 4 * height, width), BF16),
            pltpu.VMEM((2, sets, down_height, model), BF16),
            pltpu.VMEM((2, sets, 2, 4 * height, width), BF16),
            pltpu.VMEM((2, sets, down_height, model), BF16),
            pltpu.VMEM((sets, 2, 4 * height, width), BF16),
            pltpu.VMEM((sets, down_height, model), BF16),
            pltpu.VMEM((sets, 16 * height, 3 * model), BF16),
            pltpu.VMEM((sets, 16 * height, model), BF16),
            pltpu.VMEM((places[0], height, 3 * model), BF16),
            pltpu.VMEM((places[1], height, 3 * model), BF16),
            pltpu.VMEM((places[2], height, model), BF16),
            pltpu.VMEM((places[3], height, model), BF16),
            pltpu.VMEM((2, 128, 3 * model), BF16),
            pltpu.VMEM((sets, model, model), BF16),
            pltpu.VMEM((2, sets, 16, 2, height, act_height), BF16),
            pltpu.VMEM((sets, 16, height, 2 * act_height), BF16),
            pltpu.VMEM((sets, 16, height, 2 * act_height), BF16),
            pltpu.VMEM((sets, 2 * act_height, 3 * model), BF16),
            pltpu.VMEM((sets, 2 * act_height, model), BF16),
            pltpu.VMEM(act, F32),
            pltpu.VMEM(act, BF16),
            pltpu.VMEM(act, F32),
            pltpu.VMEM((2 * pair_count, act_height, model), BF16),
            pltpu.VMEM((pair_count, act_height, 128), F32),
            pltpu.VMEM((model, 128), BF16),
            pltpu.VMEM((2 * sets, 16, model), F32),
            pltpu.VMEM((8, 8, 128), F32),
            pltpu.VMEM((32, 8, 128), F32),
            pltpu.VMEM((8, 128), F32),
            pltpu.VMEM((8, sets, height, width), BF16),
            dma((2, sets, 2, 2)),
            dma((2, sets, 2, 2)),
            dma((2, sets, 2)),
            dma((2, sets, 2)),
            dma((2, sets)),
            dma((2, sets)),
            dma((2, sets, 3)),
            dma((2, sets, 3)),
            dma((sets, 3)),
            dma((sets, 3)),
            dma((sets,)),
            dma((8, sets)),
            dma((4 * sets,)),
            dma((4 * sets,)),
            dma((4, 4)),
            dma((4, max(places))),
            dma,
            dma,
            dma((2, sets, 2, 2)),
            dma((2, sets, 3)),
            dma((2 + sets,)),
        ],
        compiler_params=pltpu.CompilerParams(
            collective_id=5, has_side_effects=True, vmem_limit_bytes=63 * 2**20
        ),
        name="backward_scatter",
    )(
        tokens,
        grads,
        gain_rows,
        qkv_rows,
        context,
        resid_mid,
        qkv_full,
        out_full,
        out_part,
        back_part,
        gate_up_grad,
        down_grad,
    )


def settle_kernel(*refs):
    count = (len(refs) - 1) // 3
    sems = refs[-1]
    stages = [
        (
            pltpu.make_async_copy(refs[index], refs[2 * count + index], sems.at[0, index]),
            pltpu.make_async_copy(refs[2 * count + index], refs[count + index], sems.at[1, index]),
        )
        for index in range(count)
    ]
    for read, _ in stages:
        read.start()
    for read, write in stages:
        read.wait()
        write.start()
    for _, write in stages:
        write.wait()


def settle(arrays):
    anywhere = pl.BlockSpec(memory_space=pl.ANY)
    return pl.pallas_call(
        settle_kernel,
        out_shape=tuple(jax.ShapeDtypeStruct(array.shape, array.dtype) for array in arrays),
        in_specs=[anywhere] * len(arrays),
        out_specs=(anywhere,) * len(arrays),
        scratch_shapes=[pltpu.VMEM(array.shape, array.dtype) for array in arrays]
        + [pltpu.SemaphoreType.DMA((2, len(arrays)))],
        name="settle",
    )(*arrays)


def local_fast(
    tokens,
    norm_attn,
    w_qkv,
    w_out,
    norm_ff,
    w_gate_up,
    w_down,
    cotangent,
    valid_frames,
    item_lengths,
):
    (
        gain_rows,
        cot_rows,
        qkv_rows,
        context,
        resid_mid,
        qkv_full,
        out_full,
        out_part,
        back_part,
        gate_up_grad,
        down_grad,
    ) = forward_gather(
        valid_frames,
        item_lengths,
        norm_attn,
        norm_ff,
        tokens,
        cotangent,
        w_qkv,
        w_out,
        w_gate_up,
        w_down,
    )
    (
        output,
        grad_tokens,
        share_norm_attn,
        share_norm_ff,
        share_qkv,
        share_out,
        share_gate_up,
        share_down,
    ) = settle(backward_scatter(
        tokens,
        cot_rows,
        gain_rows,
        qkv_rows,
        context,
        resid_mid,
        qkv_full,
        out_full,
        out_part,
        back_part,
        gate_up_grad,
        down_grad,
    ))
    return (
        output,
        grad_tokens,
        share_norm_attn,
        share_qkv,
        share_out,
        share_norm_ff,
        share_gate_up,
        share_down,
    )


def solution(mesh):
    in_specs = (
        P(("dp", "pair"), None, None),
        P(None, ("dp", "pair")),
        P(None, ("dp", "pair"), None),
        P(None, ("dp", "pair"), None),
        P(None, ("dp", "pair")),
        P(None, ("dp", "pair"), None),
        P(None, ("dp", "pair"), None),
        P(("dp", "pair"), None, None),
        P(("dp", "pair")),
        P(),
    )
    out_specs = (
        P(("dp", "pair"), None, None),
        P(("dp", "pair"), None, None),
        P(None, ("dp", "pair")),
        P(None, ("dp", "pair"), None),
        P(None, ("dp", "pair"), None),
        P(None, ("dp", "pair")),
        P(None, ("dp", "pair"), None),
        P(None, ("dp", "pair"), None),
    )
    body = local_fast if mesh.shape["dp"] == 16 and mesh.shape["pair"] == 2 else local
    return jax.shard_map(body, mesh=mesh, in_specs=in_specs, out_specs=out_specs, check_vma=False)
```
